32 devices in a mesh: dp: 4 (over y, core), ctx: 2 (over x), tp: 4 (over z).
Axes of the slice: x: 2, y: 2, z: 4, core: 2. Of those that a mesh axis runs over, the one named last changes fastest.
Arguments:
- tokens: bfloat16 [8, 256, 2048], P('dp', 'ctx'), may hold values from -6 to 6
- mixgain: bfloat16 [2048], replicated, may hold values from 0.5 to 1.5
- inproj: bfloat16 [2, 2048, 4096], P(None, ('dp', 'ctx'), 'tp'), may hold values from -0.125 to 0.125
- convkern: bfloat16 [4, 4096], P(None, 'tp'), may hold values from -3 to 3
- convbias: bfloat16 [4096], P('tp'), may hold values from -0.5 to 0.5
- selproj: bfloat16 [4096, 160], P('tp'), may hold values from -0.09375 to 0.09375
- stepproj: bfloat16 [128, 4096], P(None, 'tp'), may hold values from -0.5 to 0.5
- stepbias: bfloat16 [4096], P('tp'), may hold values from -6.875 to -2.296875
- decaylog: bfloat16 [4096, 16], P('tp'), may hold values from -4 to 2.6875
- skipgain: bfloat16 [4096], P('tp'), may hold values from 0.5 to 1.5
- outproj: bfloat16 [4096, 2048], P('tp', ('dp', 'ctx')), may hold values from -0.375 to 0.375
- ffngain: bfloat16 [2048], replicated, may hold values from 0.5 to 1.5
- gateup: bfloat16 [2, 2048, 8192], P(None, ('dp', 'ctx'), 'tp'), may hold values from -0.125 to 0.125
- downproj: bfloat16 [8192, 2048], P('tp', ('dp', 'ctx')), may hold values from -0.0625 to 0.0625
- cotangent: bfloat16 [8, 256, 2048], P('dp', 'ctx'), may hold values from -6 to 6
Outputs:
- layer_out: bfloat16 [8, 256, 2048], P('dp', 'ctx')
- tokens_grad: bfloat16 [8, 256, 2048], P('dp', 'ctx')
- mixgain_grad: float32 [2048], replicated
- inproj_grad: float32 [2, 2048, 4096], P(None, ('dp', 'ctx'), 'tp')
- convkern_grad: float32 [4, 4096], P(None, 'tp')
- convbias_grad: float32 [4096], P('tp')
- selproj_grad: float32 [4096, 160], P('tp')
- stepproj_grad: float32 [128, 4096], P(None, 'tp')
- stepbias_grad: float32 [4096], P('tp')
- decaylog_grad: float32 [4096, 16], P('tp')
- skipgain_grad: float32 [4096], P('tp')
- outproj_grad: float32 [4096, 2048], P('tp', ('dp', 'ctx'))
- ffngain_grad: float32 [2048], replicated
- gateup_grad: float32 [2, 2048, 8192], P(None, ('dp', 'ctx'), 'tp')
- downproj_grad: float32 [8192, 2048], P('tp', ('dp', 'ctx'))
The draws below stay inside these ranges and needn't reach their ends.
All inputs are finite; a program needn't handle non-finite values.
Results may differ from the reference program's by a relative error of at most 0.012.
The reference program's roundings to bfloat16 on the way count: a program that leaves them out, or rounds other values in their place, can miss the bound.
Values may be sent and summed in bfloat16 or wider, within the bound.
A program may use at most 320 MiB of HBM per device.

```python
import math
import jax
import jax.numpy as jnp
from jax import lax

D = 2048
E = 4096
FF = 8192
N_STATE = 16
R = 128
CONV = 4
LENGTH = 256
SEQS = 8
PROJ = 160


def block_scale(own_key, shape, split, smallest, high):
    def one(axis_at, parts):
        draws = jax.random.uniform(jax.random.fold_in(jax.random.fold_in(own_key, 6), axis_at), (parts,), jnp.float32, smallest / len(split), high / len(split))
        return jnp.repeat(jnp.exp(draws), shape[axis_at] // parts).reshape((-1,) + (1,) * (len(shape) - axis_at - 1))

    level = one(*split[0])
    for cut in split[1:]:
        level = level * one(*cut)
    return level


def scatter_about(own_key, shape, scale, most, shards=(), held_as=jnp.bfloat16):
    entries = scale * jax.random.normal(own_key, shape, jnp.float32)
    if shards:
        entries = entries * block_scale(own_key, shape, shards, -0.22, 0.18)
    return jnp.clip(entries, -most, most).astype(held_as)


def setup_inputs(seed: int = 0) -> dict:
    keys = jax.random.split(jax.random.key(seed), 16)
    return {
        "tokens": scatter_about(keys[0], (SEQS, LENGTH, D), 1.0, 6.0, ((0, 4), (1, 2))),
        "mixgain": jnp.clip(1.0 + 0.1 * jax.random.normal(keys[1], (D,), jnp.float32), 0.5, 1.5).astype(jnp.bfloat16),
        "inproj": scatter_about(keys[2], (2, D, E), D ** -0.5, 0.125, ((1, 8), (2, 4))),
        "convkern": scatter_about(keys[3], (CONV, E), 0.5, 3.0, ((1, 4),)),
        "convbias": jnp.clip(jax.random.uniform(keys[4], (E,), jnp.float32, -0.5, 0.5) * block_scale(keys[4], (E,), ((0, 4),), -0.4, 0.0), -0.5, 0.5).astype(jnp.bfloat16),
        "selproj": scatter_about(keys[5], (E, PROJ), E ** -0.5, 0.09375, ((0, 4),)),
        "stepproj": scatter_about(keys[6], (R, E), R ** -0.5, 0.5, ((1, 4),)),
        "stepbias": jnp.clip(-6.875 + 4.578125 * jax.random.uniform(keys[7], (E,), jnp.float32) ** block_scale(keys[7], (E,), ((0, 4),), -0.2, 0.2), -6.875, -2.296875).astype(jnp.bfloat16),
        "decaylog": jnp.clip(-4.0 + 6.6875 * jax.random.uniform(keys[8], (E, N_STATE), jnp.float32) ** block_scale(keys[8], (E, N_STATE), ((0, 4),), -0.2, 0.2), -4.0, 2.6875).astype(jnp.bfloat16),
        "skipgain": jnp.clip(0.5 + 1.0 * jax.random.uniform(keys[9], (E,), jnp.float32) ** block_scale(keys[9], (E,), ((0, 4),), -0.2, 0.2), 0.5, 1.5).astype(jnp.bfloat16),
        "outproj": scatter_about(keys[10], (E, D), (E // 16) ** -0.5, 0.375, ((0, 4), (1, 8))),
        "ffngain": jnp.clip(1.0 + 0.1 * jax.random.normal(keys[11], (D,), jnp.float32), 0.5, 1.5).astype(jnp.bfloat16),
        "gateup": scatter_about(keys[12], (2, D, FF), D ** -0.5, 0.125, ((1, 8), (2, 4))),
        "downproj": scatter_about(keys[13], (FF, D), FF ** -0.5, 0.0625, ((0, 4), (1, 8))),
        "cotangent": scatter_about(keys[14], (SEQS, LENGTH, D), 1.0, 6.0, ((0, 4), (1, 2))),
    }


EPSILON = 1e-05
HIGHEST = lax.Precision.HIGHEST

@jax.custom_vjp
def low(v):
    return lax.optimization_barrier(v.astype(jnp.bfloat16)).astype(jnp.float32)

@jax.custom_vjp
def low_back(v):
    return v

def low_keep(v):
    return (low(v), None)

def low_pass(kept, grad):
    return (grad,)

def back_keep(v):
    return (v, None)

def back_low(kept, grad):
    return (low(grad),)
low.defvjp(low_keep, low_pass)
low_back.defvjp(back_keep, back_low)

def product(left, right):
    return jnp.dot(left, right, precision=HIGHEST, preferred_element_type=jnp.float32)

def selective(step_size, inputs, b_rows, c_rows, decay_rate):
    length_now = step_size.shape[0]
    block_len = math.gcd(length_now, 64)
    blocks = length_now // block_len

    def one_step(carried, pieces):
        step_now, input_now, brow_now, crow_now = pieces
        carried = jnp.exp(step_now[:, None] * decay_rate) * carried + (step_now * input_now)[:, None] * brow_now[None, :]
        return (carried, lax.optimization_barrier(jnp.sum(carried * crow_now[None, :], -1)))

    def run_block(carried, pieces):
        return lax.scan(one_step, carried, pieces)
    shaped = (step_size.reshape(blocks, block_len, -1), inputs.reshape(blocks, block_len, -1), b_rows.reshape(blocks, block_len, -1), c_rows.reshape(blocks, block_len, -1))
    _, outputs = lax.scan(jax.checkpoint(run_block), jnp.zeros(decay_rate.shape, jnp.float32), shaped)
    return outputs.reshape(step_size.shape)

def layer_forward(hidden_in, mixgain, inproj, convkern, convbias, selproj, stepproj, stepbias, decaylog, skipgain, outproj, ffngain, gateup, downproj):
    length_now = hidden_in.shape[0]
    scale_one = lax.rsqrt(lax.optimization_barrier(jnp.mean(hidden_in * hidden_in, -1, keepdims=True)) + EPSILON)
    normed_one = low(hidden_in * scale_one * mixgain)
    conv_in = low_back(low(product(normed_one, inproj[0])))
    gate_mix = low_back(product(normed_one, inproj[1]))
    padded_in = jnp.concatenate([jnp.zeros((CONV - 1, conv_in.shape[1]), jnp.float32), conv_in], 0)
    conv_out = convbias[None]
    for offset in range(CONV):
        conv_out = conv_out + convkern[offset][None] * padded_in[offset:offset + length_now]
    scan_in = low(jax.nn.silu(conv_out))
    select_cols = low_back(product(scan_in, selproj))
    step_low = low(select_cols[:, :R])
    b_rows = select_cols[:, R:R + N_STATE]
    c_rows = select_cols[:, R + N_STATE:]
    step_pre = low_back(product(step_low, stepproj))
    step_size = jax.nn.softplus(step_pre + stepbias)
    decay_rate = -jnp.exp(decaylog)
    mixer_core = selective(step_size, scan_in, b_rows, c_rows, decay_rate) + skipgain * scan_in
    gated = low(mixer_core * jax.nn.silu(gate_mix))
    middle = hidden_in + low_back(product(gated, outproj))
    scale_two = lax.rsqrt(lax.optimization_barrier(jnp.mean(middle * middle, -1, keepdims=True)) + EPSILON)
    normed_two = low(middle * scale_two * ffngain)
    gate_ffn = low_back(product(normed_two, gateup[0]))
    up_ffn = low_back(product(normed_two, gateup[1]))
    activated = low(jax.nn.silu(gate_ffn) * up_ffn)
    return middle + product(activated, downproj)

def reference(tokens, mixgain, inproj, convkern, convbias, selproj, stepproj, stepbias, decaylog, skipgain, outproj, ffngain, gateup, downproj, cotangent):
    weights = tuple((array_in.astype(jnp.float32) for array_in in (mixgain, inproj, convkern, convbias, selproj, stepproj, stepbias, decaylog, skipgain, outproj, ffngain, gateup, downproj)))

    def per_sequence(running, pieces):
        seq_tokens, seq_cotangent = pieces
        value, pull = jax.vjp(layer_forward, seq_tokens.astype(jnp.float32), *weights)
        grads = pull(seq_cotangent.astype(jnp.float32))
        running = tuple((summed + update for summed, update in zip(running, grads[1:])))
        return (running, (value.astype(jnp.bfloat16), grads[0].astype(jnp.bfloat16)))
    start = tuple((jnp.zeros(array_in.shape, jnp.float32) for array_in in weights))
    totals, outputs = lax.scan(per_sequence, start, (tokens, cotangent))
    return (outputs[0], outputs[1], totals[0], totals[1], totals[2], totals[3], totals[4], totals[5], totals[6], totals[7], totals[8], totals[9], totals[10], totals[11], totals[12])
```

```python
import functools
import math

import jax
import jax.numpy as jnp
from jax import lax
from jax.experimental import pallas as pl
from jax.experimental.pallas import tpu as pltpu
from jax.sharding import PartitionSpec as P

EPSILON = 1e-05
LOG2E = math.log2(math.e)
LN2 = math.log(2.0)
SUB = 8
LANE = 128
PLANE = ("dp", "ctx")


def passed_along(value, axis, steps):
    count = lax.axis_size(axis)
    first, last = (max(0, -steps), min(count, count - steps))
    return lax.ppermute(value, axis, [(source, source + steps) for source in range(first, last)])


def matmul(left, right):
    return jnp.dot(left, right, preferred_element_type=jnp.float32)


def matmul_nt(left, right):
    return lax.dot_general(
        left, right, (((1,), (1,)), ((), ())), preferred_element_type=jnp.float32
    )


def matmul_tn(left, right):
    return lax.dot_general(
        left, right, (((0,), (0,)), ((), ())), preferred_element_type=jnp.float32
    )


def inverse_rms(values):
    return lax.rsqrt(jnp.mean(values * values, -1, keepdims=True) + EPSILON)


def silu_slope(values):
    logistic = jax.nn.sigmoid(values)
    return logistic * (1.0 + values * (1.0 - logistic))


def norm_back(grad_norm, values, scale, gain):
    scaled_grad = grad_norm * gain
    unit_rows = values * scale
    return scale * (scaled_grad - unit_rows * jnp.mean(scaled_grad * unit_rows, -1, keepdims=True))


def to_tiles(rows):
    count, width = rows.shape
    tiles = width // LANE
    return (
        rows.reshape(count // SUB, SUB, tiles, LANE)
        .transpose(0, 2, 1, 3)
        .reshape(count // SUB, tiles * SUB, LANE)
    )


def from_tiles(tiled):
    groups, rows, _ = tiled.shape
    tiles = rows // SUB
    return (
        tiled.reshape(groups, tiles, SUB, LANE)
        .transpose(0, 2, 1, 3)
        .reshape(groups * SUB, tiles * LANE)
    )


def token_row(ref, group, at, tiles):
    return ref[group, pl.ds(at, tiles, stride=SUB), :]


def ends_kernel(n_state, tiles, groups, reverse, step_ref, drive_ref, rows_ref, rate_ref, end_ref):
    base = pl.program_id(0) * groups * SUB * n_state
    rates = [rate_ref[n] for n in range(n_state)]

    def one(turn, states):
        group = groups - 1 - turn if reverse else turn
        order = range(SUB - 1, -1, -1) if reverse else range(SUB)
        states = list(states)
        for at in order:
            step = token_row(step_ref, group, at, tiles)
            drive = token_row(drive_ref, group, at, tiles)
            if not reverse:
                drive = drive * step
            for n in range(n_state):
                row = rows_ref[base + (group * SUB + at) * n_state + n]
                decay = jnp.exp2(step * rates[n])
                if reverse:
                    states[n] = decay * (states[n] + drive * row)
                else:
                    states[n] = decay * states[n] + drive * row
        return tuple(states)

    zero = jnp.zeros((tiles, LANE), jnp.float32)
    states = lax.fori_loop(0, groups, one, (zero,) * n_state)
    for n in range(n_state):
        end_ref[0, n] = states[n]


def scan_ends(step, drive, rows, rate, seqs, reverse):
    n_state, tiles, _ = rate.shape
    groups = step.shape[0] // seqs
    tile_spec = pl.BlockSpec((groups, tiles * SUB, LANE), lambda s: (s, 0, 0))
    return pl.pallas_call(
        functools.partial(ends_kernel, n_state, tiles, groups, reverse),
        grid=(seqs,),
        in_specs=[
            tile_spec,
            tile_spec,
            pl.BlockSpec(memory_space=pltpu.SMEM),
            pl.BlockSpec((n_state, tiles, LANE), lambda s: (0, 0, 0)),
        ],
        out_specs=pl.BlockSpec((1, n_state, tiles, LANE), lambda s: (s, 0, 0, 0)),
        out_shape=jax.ShapeDtypeStruct((seqs, n_state, tiles, LANE), jnp.float32),
        compiler_params=pltpu.CompilerParams(vmem_limit_bytes=32 * 2**20),
    )(step, drive, rows, rate)


def forward_kernel(
    n_state,
    tiles,
    groups,
    blocks,
    start_ref,
    step_ref,
    input_ref,
    brow_ref,
    crow_ref,
    rate_ref,
    prior_ref,
    mixed_ref,
    carried,
):
    base = (pl.program_id(0) * blocks + pl.program_id(1)) * groups * SUB * n_state

    @pl.when(pl.program_id(1) == 0)
    def _():
        carried[...] = start_ref[0]

    def one(group, states):
        states = list(states)
        for at in range(SUB):
            step = token_row(step_ref, group, at, tiles)
            drive = step * token_row(input_ref, group, at, tiles)
            mixed = [None] * 2
            for n in range(n_state):
                where = base + (group * SUB + at) * n_state + n
                prior_ref[group * SUB + at, n] = states[n]
                decay = jnp.exp2(step * rate_ref[n])
                states[n] = decay * states[n] + drive * brow_ref[where]
                term = states[n] * crow_ref[where]
                mixed[n % 2] = term if mixed[n % 2] is None else mixed[n % 2] + term
            mixed_ref[group, pl.ds(at, tiles, stride=SUB), :] = mixed[0] + mixed[1]
        return tuple(states)

    states = lax.fori_loop(0, groups, one, tuple(carried[n] for n in range(n_state)))
    for n in range(n_state):
        carried[n] = states[n]


def scan_forward(start, step, inputs, b_rows, c_rows, rate, seqs):
    n_state, tiles, _ = rate.shape
    all_groups = step.shape[0]
    groups = math.gcd(all_groups // seqs, 4)
    blocks = all_groups // seqs // groups
    tile_spec = pl.BlockSpec((groups, tiles * SUB, LANE), lambda s, b: (s * blocks + b, 0, 0))
    smem = pl.BlockSpec(memory_space=pltpu.SMEM)
    tokens = all_groups * SUB
    return pl.pallas_call(
        functools.partial(forward_kernel, n_state, tiles, groups, blocks),
        grid=(seqs, blocks),
        in_specs=[
            pl.BlockSpec((1, n_state, tiles, LANE), lambda s, b: (s, 0, 0, 0)),
            tile_spec,
            tile_spec,
            smem,
            smem,
            pl.BlockSpec((n_state, tiles, LANE), lambda s, b: (0, 0, 0)),
        ],
        out_specs=[
            pl.BlockSpec(
                (groups * SUB, n_state, tiles, LANE), lambda s, b: (s * blocks + b, 0, 0, 0)
            ),
            tile_spec,
        ],
        out_shape=[
            jax.ShapeDtypeStruct((tokens, n_state, tiles, LANE), jnp.float32),
            jax.ShapeDtypeStruct(step.shape, jnp.float32),
        ],
        scratch_shapes=[pltpu.VMEM((n_state, tiles, LANE), jnp.float32)],
        compiler_params=pltpu.CompilerParams(vmem_limit_bytes=32 * 2**20),
    )(start, step, inputs, b_rows, c_rows, rate)


def backward_kernel(
    n_state,
    tiles,
    groups,
    blocks,
    end_ref,
    prior_ref,
    step_ref,
    input_ref,
    ograd_ref,
    brow_ref,
    crow_ref,
    rate_ref,
    picks_ref,
    step_grad_ref,
    input_grad_ref,
    rate_grad_ref,
    part_ref,
    carried,
):
    block = blocks - 1 - pl.program_id(1)
    base = (pl.program_id(0) * blocks + block) * groups * SUB * n_state

    @pl.when(pl.program_id(1) == 0)
    def _():
        carried[...] = end_ref[0]

    @pl.when((pl.program_id(0) == 0) & (pl.program_id(1) == 0))
    def _():
        rate_grad_ref[...] = jnp.zeros_like(rate_grad_ref)

    def one(turn, grads):
        group = groups - 1 - turn
        grads = list(grads)
        for at in range(SUB - 1, -1, -1):
            step = token_row(step_ref, group, at, tiles)
            value = token_row(input_ref, group, at, tiles)
            ograd = token_row(ograd_ref, group, at, tiles)
            drive = step * value
            along_b = None
            along_rate = None
            brow_parts, crow_parts = [], []
            for n in range(n_state):
                where = base + (group * SUB + at) * n_state + n
                brow, crow = brow_ref[where], crow_ref[where]
                rate = rate_ref[n]
                decay = jnp.exp2(step * rate)
                grad = ograd * crow + grads[n]
                kept = decay * prior_ref[group * SUB + at, n]
                state = kept + drive * brow
                decay_term = grad * kept
                grads[n] = decay * grad
                rate_grad_ref[n] += decay_term * step
                by_rate, by_brow = decay_term * rate, grad * brow
                along_rate = by_rate if along_rate is None else along_rate + by_rate
                along_b = by_brow if along_b is None else along_b + by_brow
                brow_parts.append(grad * drive)
                crow_parts.append(ograd * state)
            step_grad_ref[group, pl.ds(at, tiles, stride=SUB), :] = (
                along_rate * LN2 + along_b * value
            )
            input_grad_ref[group, pl.ds(at, tiles, stride=SUB), :] = along_b * step
            parts = jnp.concatenate(brow_parts + crow_parts, 0).astype(jnp.bfloat16)
            part_ref[group * SUB + at] = jnp.dot(
                picks_ref[...], parts, preferred_element_type=jnp.float32
            )
        return tuple(grads)

    grads = lax.fori_loop(0, groups, one, tuple(carried[n] for n in range(n_state)))
    for n in range(n_state):
        carried[n] = grads[n]


def scan_backward(end_grad, prior, step, inputs, ograd, b_rows, c_rows, rate, seqs):
    n_state, tiles, _ = rate.shape
    all_groups = step.shape[0]
    groups = math.gcd(all_groups // seqs, 4)
    blocks = all_groups // seqs // groups

    def at(s, b):
        return s * blocks + blocks - 1 - b

    tile_spec = pl.BlockSpec((groups, tiles * SUB, LANE), lambda s, b: (at(s, b), 0, 0))
    smem = pl.BlockSpec(memory_space=pltpu.SMEM)
    tokens = all_groups * SUB
    picks = jnp.repeat(jnp.eye(2 * n_state, dtype=jnp.bfloat16), tiles, 1)
    return pl.pallas_call(
        functools.partial(backward_kernel, n_state, tiles, groups, blocks),
        grid=(seqs, blocks),
        in_specs=[
            pl.BlockSpec((1, n_state, tiles, LANE), lambda s, b: (s, 0, 0, 0)),
            pl.BlockSpec((groups * SUB, n_state, tiles, LANE), lambda s, b: (at(s, b), 0, 0, 0)),
            tile_spec,
            tile_spec,
            tile_spec,
            smem,
            smem,
            pl.BlockSpec((n_state, tiles, LANE), lambda s, b: (0, 0, 0)),
            pl.BlockSpec(picks.shape, lambda s, b: (0, 0)),
        ],
        out_specs=[
            tile_spec,
            tile_spec,
            pl.BlockSpec((n_state, tiles, LANE), lambda s, b: (0, 0, 0)),
            pl.BlockSpec((groups * SUB, 2 * n_state, LANE), lambda s, b: (at(s, b), 0, 0)),
        ],
        out_shape=[
            jax.ShapeDtypeStruct(step.shape, jnp.float32),
            jax.ShapeDtypeStruct(step.shape, jnp.float32),
            jax.ShapeDtypeStruct(rate.shape, jnp.float32),
            jax.ShapeDtypeStruct((tokens, 2 * n_state, LANE), jnp.float32),
        ],
        scratch_shapes=[pltpu.VMEM((n_state, tiles, LANE), jnp.float32)],
        compiler_params=pltpu.CompilerParams(vmem_limit_bytes=32 * 2**20),
    )(end_grad, prior, step, inputs, ograd, b_rows, c_rows, rate, picks)


def from_earlier(ends, decay, steps):
    count = lax.axis_size("ctx")
    if count == 1:
        return jnp.zeros_like(ends)
    if count == 2:
        return passed_along(ends, "ctx", steps)
    index = lax.axis_index("ctx")
    all_ends = lax.all_gather(ends, "ctx")
    all_decays = lax.all_gather(decay, "ctx")

    def one(turn, state):
        at = turn if steps > 0 else count - 1 - turn
        reached = at < index if steps > 0 else at > index
        return jnp.where(reached, all_decays[at] * state + all_ends[at], state)

    return lax.fori_loop(0, count, one, jnp.zeros_like(ends))


def gathered_rows(rows):
    return lax.all_gather(rows, PLANE, axis=0, tiled=True)


def swapped_columns(rows):
    return lax.all_to_all(rows, PLANE, split_axis=1, concat_axis=0, tiled=True)


def per_device(
    tokens,
    mixgain,
    inproj,
    convkern,
    convbias,
    selproj,
    stepproj,
    stepbias,
    decaylog,
    skipgain,
    outproj,
    ffngain,
    gateup,
    downproj,
    cotangent,
):
    seqs, span, width = tokens.shape
    rows = seqs * span
    taps, inner = convkern.shape
    rank = stepproj.shape[0]
    n_state = decaylog.shape[1]
    tiles = inner // LANE
    gain_mix = mixgain.astype(jnp.float32)
    gain_ffn = ffngain.astype(jnp.float32)
    kernel = convkern.astype(jnp.float32)
    kernel_bias = convbias.astype(jnp.float32)
    step_bias = stepbias.astype(jnp.float32)
    skip_weight = skipgain.astype(jnp.float32)
    decay_rate = -jnp.exp(jnp.transpose(decaylog.astype(jnp.float32)))
    rate = (decay_rate * LOG2E).reshape(n_state, tiles, LANE)

    in_full = lax.all_gather(inproj, PLANE, axis=1, tiled=True)
    out_full = lax.all_gather(outproj, PLANE, axis=1, tiled=True)
    gu_full = lax.all_gather(gateup, PLANE, axis=1, tiled=True)
    down_full = lax.all_gather(downproj, PLANE, axis=1, tiled=True)

    hidden_in = tokens.reshape(rows, width).astype(jnp.float32)
    scale_one = inverse_rms(hidden_in)
    normed_one = (hidden_in * scale_one * gain_mix).astype(jnp.bfloat16)
    normed_one_cols = swapped_columns(normed_one)
    conv_in = matmul(normed_one, in_full[0]).astype(jnp.bfloat16)
    gate_mix = matmul(normed_one, in_full[1])
    conv_seqs = conv_in.reshape(seqs, span, inner)
    rim_rows = passed_along(conv_seqs[:, span - (taps - 1) :], "ctx", 1)
    padded_in = jnp.concatenate([rim_rows, conv_seqs], 1).astype(jnp.float32)
    conv_out = kernel_bias[None, None]
    for offset in range(taps):
        conv_out = conv_out + kernel[offset][None, None] * padded_in[:, offset : offset + span]
    conv_out = conv_out.reshape(rows, inner)
    scan_in = jax.nn.silu(conv_out).astype(jnp.bfloat16)
    scan_float = scan_in.astype(jnp.float32)
    select_cols = lax.psum(matmul(scan_in, selproj), "tp")
    step_low = select_cols[:, :rank].astype(jnp.bfloat16)
    b_rows = select_cols[:, rank : rank + n_state].reshape(-1)
    c_rows = select_cols[:, rank + n_state :].reshape(-1)
    step_pre = matmul(step_low, stepproj) + step_bias[None]
    step_size = jax.nn.softplus(step_pre)
    span_decay = jnp.exp(
        decay_rate[None] * jnp.sum(step_size.reshape(seqs, span, inner), 1)[:, None]
    ).reshape(seqs, n_state, tiles, LANE)
    step_tiles, input_tiles = to_tiles(step_size), to_tiles(scan_float)
    ends = scan_ends(step_tiles, input_tiles, b_rows, rate, seqs, False)
    start = from_earlier(ends, span_decay, 1)
    prior, mixed_tiles = scan_forward(start, step_tiles, input_tiles, b_rows, c_rows, rate, seqs)
    mixer_core = from_tiles(mixed_tiles) + skip_weight[None] * scan_float
    gate_sig = jax.nn.silu(gate_mix)
    gated = (mixer_core * gate_sig).astype(jnp.bfloat16)
    mixed = lax.psum(matmul(gated, out_full).astype(jnp.bfloat16), "tp").astype(jnp.float32)
    middle = hidden_in + mixed
    scale_two = inverse_rms(middle)
    normed_two = (middle * scale_two * gain_ffn).astype(jnp.bfloat16)
    normed_two_cols = swapped_columns(normed_two)
    gate_ffn = matmul(normed_two, gu_full[0])
    up_ffn = matmul(normed_two, gu_full[1])
    activated = (jax.nn.silu(gate_ffn) * up_ffn).astype(jnp.bfloat16)
    ct_low = cotangent.reshape(rows, width)
    ct_cols = swapped_columns(ct_low)
    act_grad = matmul_nt(ct_low, down_full)
    gate_grad = (act_grad * up_ffn * silu_slope(gate_ffn)).astype(jnp.bfloat16)
    up_grad = (act_grad * jax.nn.silu(gate_ffn)).astype(jnp.bfloat16)
    normed_two_part = matmul_nt(gate_grad, gu_full[0]) + matmul_nt(up_grad, gu_full[1])
    normed_two_grad = lax.psum(normed_two_part.astype(jnp.bfloat16), "tp").astype(jnp.float32)
    activated_all = gathered_rows(activated)
    gate_grad_all = gathered_rows(gate_grad)
    up_grad_all = gathered_rows(up_grad)
    gated_all = gathered_rows(gated)
    ffn_out = lax.psum(matmul(activated, down_full).astype(jnp.bfloat16), "tp")
    layer_out = (middle + ffn_out.astype(jnp.float32)).astype(jnp.bfloat16)
    grad_downproj = matmul_tn(activated_all, ct_cols)
    grad_gateup = jnp.stack(
        [matmul_tn(normed_two_cols, gate_grad_all), matmul_tn(normed_two_cols, up_grad_all)]
    )
    grad_ffngain = jnp.sum(normed_two_grad * middle * scale_two, 0)
    middle_grad = ct_low.astype(jnp.float32) + norm_back(
        normed_two_grad, middle, scale_two, gain_ffn
    )
    middle_low = middle_grad.astype(jnp.bfloat16)
    middle_cols = swapped_columns(middle_low)
    grad_outproj = matmul_tn(gated_all, middle_cols)
    gated_grad = matmul_nt(middle_low, out_full)
    core_grad = gated_grad * gate_sig
    gate_mix_grad = (gated_grad * mixer_core * silu_slope(gate_mix)).astype(jnp.bfloat16)
    gate_mix_grad_all = gathered_rows(gate_mix_grad)
    grad_skipgain = jnp.sum(core_grad * scan_float, 0)
    ograd_tiles = to_tiles(core_grad)
    back_ends = scan_ends(step_tiles, ograd_tiles, c_rows, rate, seqs, True)
    end_grad = from_earlier(back_ends, span_decay, -1)
    step_grad_tiles, input_grad_tiles, rate_grad, parts = scan_backward(
        end_grad, prior, step_tiles, input_tiles, ograd_tiles, b_rows, c_rows, rate, seqs
    )
    grad_decaylog = rate_grad.reshape(n_state, inner) * decay_rate
    pre_grad = from_tiles(step_grad_tiles) * jax.nn.sigmoid(step_pre)
    grad_stepbias = jnp.sum(pre_grad, 0)
    pre_low = pre_grad.astype(jnp.bfloat16)
    grad_stepproj = matmul_tn(step_low, pre_low)
    select_grad = lax.psum(
        jnp.concatenate([matmul_nt(pre_low, stepproj), jnp.sum(parts, -1)], 1), "tp"
    )
    select_low = select_grad.astype(jnp.bfloat16)
    grad_selproj = matmul_tn(scan_in, select_low)
    scan_in_grad = (
        core_grad * skip_weight[None] + from_tiles(input_grad_tiles) + matmul_nt(select_low, selproj)
    )
    conv_grad = scan_in_grad * silu_slope(conv_out)
    grad_convbias = jnp.sum(conv_grad, 0)
    conv_grad_seqs = conv_grad.reshape(seqs, span, inner)
    padded_grad = jnp.zeros(padded_in.shape, jnp.float32)
    kernel_rows = []
    for offset in range(taps):
        kernel_rows.append(jnp.sum(conv_grad_seqs * padded_in[:, offset : offset + span], (0, 1)))
        padded_grad = padded_grad + jnp.pad(
            kernel[offset][None, None] * conv_grad_seqs,
            ((0, 0), (offset, taps - 1 - offset), (0, 0)),
        )
    grad_convkern = jnp.stack(kernel_rows)
    returned = passed_along(padded_grad[:, : taps - 1], "ctx", -1)
    conv_in_grad = (
        (padded_grad[:, taps - 1 :] + jnp.pad(returned, ((0, 0), (span - taps + 1, 0), (0, 0))))
        .astype(jnp.bfloat16)
        .reshape(rows, inner)
    )
    conv_in_grad_all = gathered_rows(conv_in_grad)
    normed_one_part = matmul_nt(conv_in_grad, in_full[0]) + matmul_nt(gate_mix_grad, in_full[1])
    normed_one_grad = lax.psum(normed_one_part.astype(jnp.bfloat16), "tp").astype(jnp.float32)
    grad_inproj = jnp.stack(
        [
            matmul_tn(normed_one_cols, conv_in_grad_all),
            matmul_tn(normed_one_cols, gate_mix_grad_all),
        ]
    )
    grad_mixgain = jnp.sum(normed_one_grad * hidden_in * scale_one, 0)
    tokens_grad = (middle_grad + norm_back(normed_one_grad, hidden_in, scale_one, gain_mix)).astype(
        jnp.bfloat16
    )
    smalls = lax.psum(
        (
            grad_mixgain,
            grad_convkern,
            grad_convbias,
            grad_selproj,
            grad_stepproj,
            grad_stepbias,
            grad_decaylog,
            grad_skipgain,
            grad_ffngain,
        ),
        PLANE,
    )
    return (
        layer_out.reshape(tokens.shape),
        tokens_grad.reshape(tokens.shape),
        smalls[0],
        grad_inproj,
        smalls[1],
        smalls[2],
        smalls[3],
        smalls[4],
        smalls[5],
        jnp.transpose(smalls[6]),
        smalls[7],
        grad_outproj,
        smalls[8],
        grad_gateup,
        grad_downproj,
    )


def solution(mesh):
    in_specs = (
        P("dp", "ctx", None),
        P(),
        P(None, ("dp", "ctx"), "tp"),
        P(None, "tp"),
        P("tp"),
        P("tp", None),
        P(None, "tp"),
        P("tp"),
        P("tp", None),
        P("tp"),
        P("tp", ("dp", "ctx")),
        P(),
        P(None, ("dp", "ctx"), "tp"),
        P("tp", ("dp", "ctx")),
        P("dp", "ctx", None),
    )
    out_specs = (
        P("dp", "ctx", None),
        P("dp", "ctx", None),
        P(),
        P(None, ("dp", "ctx"), "tp"),
        P(None, "tp"),
        P("tp"),
        P("tp", None),
        P(None, "tp"),
        P("tp"),
        P("tp", None),
        P("tp"),
        P("tp", ("dp", "ctx")),
        P(),
        P(None, ("dp", "ctx"), "tp"),
        P("tp", ("dp", "ctx")),
    )
    return jax.shard_map(
        per_device, mesh=mesh, in_specs=in_specs, out_specs=out_specs, check_vma=False
    )
```

```python
import functools
import math

import jax
import jax.numpy as jnp
from jax import lax
from jax.experimental import pallas as pl
from jax.experimental.pallas import tpu as pltpu
from jax.sharding import PartitionSpec as P

EPSILON = 1e-05
LOG2E = math.log2(math.e)
LN2 = math.log(2.0)
SUB = 8
LANE = 128
PLANE = ("dp", "ctx")


def passed_along(value, axis, steps):
    count = lax.axis_size(axis)
    first, last = (max(0, -steps), min(count, count - steps))
    return lax.ppermute(value, axis, [(source, source + steps) for source in range(first, last)])


def matmul(left, right):
    return jnp.dot(left, right, preferred_element_type=jnp.float32)


def matmul_nt(left, right):
    return lax.dot_general(
        left, right, (((1,), (1,)), ((), ())), preferred_element_type=jnp.float32
    )


def matmul_tn(left, right):
    return lax.dot_general(
        left, right, (((0,), (0,)), ((), ())), preferred_element_type=jnp.float32
    )


def inverse_rms(values):
    return lax.rsqrt(jnp.mean(values * values, -1, keepdims=True) + EPSILON)


def silu_slope(values):
    logistic = jax.nn.sigmoid(values)
    return logistic * (1.0 + values * (1.0 - logistic))


def norm_back(grad_norm, values, scale, gain):
    scaled_grad = grad_norm * gain
    unit_rows = values * scale
    return scale * (scaled_grad - unit_rows * jnp.mean(scaled_grad * unit_rows, -1, keepdims=True))


def to_tiles(rows):
    count, width = rows.shape
    tiles = width // LANE
    return (
        rows.reshape(count // SUB, SUB, tiles, LANE)
        .transpose(0, 2, 1, 3)
        .reshape(count // SUB, tiles * SUB, LANE)
    )


def from_tiles(tiled):
    groups, rows, _ = tiled.shape
    tiles = rows // SUB
    return (
        tiled.reshape(groups, tiles, SUB, LANE)
        .transpose(0, 2, 1, 3)
        .reshape(groups * SUB, tiles * LANE)
    )


def token_row(ref, group, at, tiles):
    return ref[group, pl.ds(at, tiles, stride=SUB), :]


def ends_kernel(n_state, tiles, groups, reverse, step_ref, drive_ref, rows_ref, rate_ref, end_ref):
    base = pl.program_id(0) * groups * SUB * n_state
    rates = [rate_ref[n] for n in range(n_state)]

    def one(turn, states):
        group = groups - 1 - turn if reverse else turn
        order = range(SUB - 1, -1, -1) if reverse else range(SUB)
        states = list(states)
        for at in order:
            step = token_row(step_ref, group, at, tiles)
            drive = token_row(drive_ref, group, at, tiles)
            if not reverse:
                drive = drive * step
            for n in range(n_state):
                row = rows_ref[base + (group * SUB + at) * n_state + n]
                decay = jnp.exp2(step * rates[n])
                if reverse:
                    states[n] = decay * (states[n] + drive * row)
                else:
                    states[n] = decay * states[n] + drive * row
        return tuple(states)

    zero = jnp.zeros((tiles, LANE), jnp.float32)
    states = lax.fori_loop(0, groups, one, (zero,) * n_state)
    for n in range(n_state):
        end_ref[0, n] = states[n]


def scan_ends(step, drive, rows, rate, seqs, reverse):
    n_state, tiles, _ = rate.shape
    groups = step.shape[0] // seqs
    tile_spec = pl.BlockSpec((groups, tiles * SUB, LANE), lambda s: (s, 0, 0))
    return pl.pallas_call(
        functools.partial(ends_kernel, n_state, tiles, groups, reverse),
        grid=(seqs,),
        in_specs=[
            tile_spec,
            tile_spec,
            pl.BlockSpec(memory_space=pltpu.SMEM),
            pl.BlockSpec((n_state, tiles, LANE), lambda s: (0, 0, 0)),
        ],
        out_specs=pl.BlockSpec((1, n_state, tiles, LANE), lambda s: (s, 0, 0, 0)),
        out_shape=jax.ShapeDtypeStruct((seqs, n_state, tiles, LANE), jnp.float32),
        compiler_params=pltpu.CompilerParams(vmem_limit_bytes=32 * 2**20),
    )(step, drive, rows, rate)


def forward_kernel(
    n_state,
    tiles,
    groups,
    blocks,
    start_ref,
    step_ref,
    input_ref,
    brow_ref,
    crow_ref,
    rate_ref,
    prior_ref,
    mixed_ref,
    carried,
):
    base = (pl.program_id(0) * blocks + pl.program_id(1)) * groups * SUB * n_state

    @pl.when(pl.program_id(1) == 0)
    def _():
        carried[...] = start_ref[0]

    def one(group, states):
        states = list(states)
        for at in range(SUB):
            step = token_row(step_ref, group, at, tiles)
            drive = step * token_row(input_ref, group, at, tiles)
            mixed = [None] * 2
            for n in range(n_state):
                where = base + (group * SUB + at) * n_state + n
                prior_ref[group * SUB + at, n] = states[n]
                decay = jnp.exp2(step * rate_ref[n])
                states[n] = decay * states[n] + drive * brow_ref[where]
                term = states[n] * crow_ref[where]
                mixed[n % 2] = term if mixed[n % 2] is None else mixed[n % 2] + term
            mixed_ref[group, pl.ds(at, tiles, stride=SUB), :] = mixed[0] + mixed[1]
        return tuple(states)

    states = lax.fori_loop(0, groups, one, tuple(carried[n] for n in range(n_state)))
    for n in range(n_state):
        carried[n] = states[n]


def scan_forward(start, step, inputs, b_rows, c_rows, rate, seqs):
    n_state, tiles, _ = rate.shape
    all_groups = step.shape[0]
    groups = math.gcd(all_groups // seqs, 4)
    blocks = all_groups // seqs // groups
    tile_spec = pl.BlockSpec((groups, tiles * SUB, LANE), lambda s, b: (s * blocks + b, 0, 0))
    smem = pl.BlockSpec(memory_space=pltpu.SMEM)
    tokens = all_groups * SUB
    return pl.pallas_call(
        functools.partial(forward_kernel, n_state, tiles, groups, blocks),
        grid=(seqs, blocks),
        in_specs=[
            pl.BlockSpec((1, n_state, tiles, LANE), lambda s, b: (s, 0, 0, 0)),
            tile_spec,
            tile_spec,
            smem,
            smem,
            pl.BlockSpec((n_state, tiles, LANE), lambda s, b: (0, 0, 0)),
        ],
        out_specs=[
            pl.BlockSpec(
                (groups * SUB, n_state, tiles, LANE), lambda s, b: (s * blocks + b, 0, 0, 0)
            ),
            tile_spec,
        ],
        out_shape=[
            jax.ShapeDtypeStruct((tokens, n_state, tiles, LANE), jnp.float32),
            jax.ShapeDtypeStruct(step.shape, jnp.float32),
        ],
        scratch_shapes=[pltpu.VMEM((n_state, tiles, LANE), jnp.float32)],
        compiler_params=pltpu.CompilerParams(vmem_limit_bytes=32 * 2**20),
    )(start, step, inputs, b_rows, c_rows, rate)


def backward_kernel(
    n_state,
    tiles,
    groups,
    blocks,
    end_ref,
    prior_ref,
    step_ref,
    input_ref,
    ograd_ref,
    brow_ref,
    crow_ref,
    rate_ref,
    picks_ref,
    step_grad_ref,
    input_grad_ref,
    rate_grad_ref,
    part_ref,
    carried,
):
    block = blocks - 1 - pl.program_id(1)
    base = (pl.program_id(0) * blocks + block) * groups * SUB * n_state

    @pl.when(pl.program_id(1) == 0)
    def _():
        carried[...] = end_ref[0]

    @pl.when((pl.program_id(0) == 0) & (pl.program_id(1) == 0))
    def _():
        rate_grad_ref[...] = jnp.zeros_like(rate_grad_ref)

    def one(turn, grads):
        group = groups - 1 - turn
        grads = list(grads)
        for at in range(SUB - 1, -1, -1):
            step = token_row(step_ref, group, at, tiles)
            value = token_row(input_ref, group, at, tiles)
            ograd = token_row(ograd_ref, group, at, tiles)
            drive = step * value
            along_b = None
            along_rate = None
            brow_parts, crow_parts = [], []
            for n in range(n_state):
                where = base + (group * SUB + at) * n_state + n
                brow, crow = brow_ref[where], crow_ref[where]
                rate = rate_ref[n]
                decay = jnp.exp2(step * rate)
                grad = ograd * crow + grads[n]
                kept = decay * prior_ref[group * SUB + at, n]
                state = kept + drive * brow
                decay_term = grad * kept
                grads[n] = decay * grad
                rate_grad_ref[n] += decay_term * step
                by_rate, by_brow = decay_term * rate, grad * brow
                along_rate = by_rate if along_rate is None else along_rate + by_rate
                along_b = by_brow if along_b is None else along_b + by_brow
                brow_parts.append(grad * drive)
                crow_parts.append(ograd * state)
            step_grad_ref[group, pl.ds(at, tiles, stride=SUB), :] = (
                along_rate * LN2 + along_b * value
            )
            input_grad_ref[group, pl.ds(at, tiles, stride=SUB), :] = along_b * step
            parts = jnp.concatenate(brow_parts + crow_parts, 0).astype(jnp.bfloat16)
            part_ref[group * SUB + at] = jnp.dot(
                picks_ref[...], parts, preferred_element_type=jnp.float32
            )
        return tuple(grads)

    grads = lax.fori_loop(0, groups, one, tuple(carried[n] for n in range(n_state)))
    for n in range(n_state):
        carried[n] = grads[n]


def scan_backward(end_grad, prior, step, inputs, ograd, b_rows, c_rows, rate, seqs):
    n_state, tiles, _ = rate.shape
    all_groups = step.shape[0]
    groups = math.gcd(all_groups // seqs, 4)
    blocks = all_groups // seqs // groups

    def at(s, b):
        return s * blocks + blocks - 1 - b

    tile_spec = pl.BlockSpec((groups, tiles * SUB, LANE), lambda s, b: (at(s, b), 0, 0))
    smem = pl.BlockSpec(memory_space=pltpu.SMEM)
    tokens = all_groups * SUB
    picks = jnp.repeat(jnp.eye(2 * n_state, dtype=jnp.bfloat16), tiles, 1)
    return pl.pallas_call(
        functools.partial(backward_kernel, n_state, tiles, groups, blocks),
        grid=(seqs, blocks),
        in_specs=[
            pl.BlockSpec((1, n_state, tiles, LANE), lambda s, b: (s, 0, 0, 0)),
            pl.BlockSpec((groups * SUB, n_state, tiles, LANE), lambda s, b: (at(s, b), 0, 0, 0)),
            tile_spec,
            tile_spec,
            tile_spec,
            smem,
            smem,
            pl.BlockSpec((n_state, tiles, LANE), lambda s, b: (0, 0, 0)),
            pl.BlockSpec(picks.shape, lambda s, b: (0, 0)),
        ],
        out_specs=[
            tile_spec,
            tile_spec,
            pl.BlockSpec((n_state, tiles, LANE), lambda s, b: (0, 0, 0)),
            pl.BlockSpec((groups * SUB, 2 * n_state, LANE), lambda s, b: (at(s, b), 0, 0)),
        ],
        out_shape=[
            jax.ShapeDtypeStruct(step.shape, jnp.float32),
            jax.ShapeDtypeStruct(step.shape, jnp.float32),
            jax.ShapeDtypeStruct(rate.shape, jnp.float32),
            jax.ShapeDtypeStruct((tokens, 2 * n_state, LANE), jnp.float32),
        ],
        scratch_shapes=[pltpu.VMEM((n_state, tiles, LANE), jnp.float32)],
        compiler_params=pltpu.CompilerParams(vmem_limit_bytes=32 * 2**20),
    )(end_grad, prior, step, inputs, ograd, b_rows, c_rows, rate, picks)


def from_earlier(ends, decay, steps):
    count = lax.axis_size("ctx")
    if count == 1:
        return jnp.zeros_like(ends)
    if count == 2:
        return passed_along(ends, "ctx", steps)
    index = lax.axis_index("ctx")
    all_ends = lax.all_gather(ends, "ctx")
    all_decays = lax.all_gather(decay, "ctx")

    def one(turn, state):
        at = turn if steps > 0 else count - 1 - turn
        reached = at < index if steps > 0 else at > index
        return jnp.where(reached, all_decays[at] * state + all_ends[at], state)

    return lax.fori_loop(0, count, one, jnp.zeros_like(ends))


def gathered_rows(rows):
    return lax.all_gather(rows, PLANE, axis=0, tiled=True)


def swapped_columns(rows):
    return lax.all_to_all(rows, PLANE, split_axis=1, concat_axis=0, tiled=True)


def place_in(axes):
    index = 0
    for axis in axes:
        index = index * lax.axis_size(axis) + lax.axis_index(axis)
    return index


def device_at(axes, index):
    where = {}
    for axis in reversed(axes):
        size = lax.axis_size(axis)
        where[axis] = lax.rem(index, size)
        index = lax.div(index, size)
    return where


def exchange_kernel(axes, count, counts, kinds, middle, *refs):
    n_parts, n_whole, n_own = counts
    parts, refs = refs[:n_parts], refs[n_parts:]
    whole, refs = refs[:n_whole], refs[n_whole:]
    own, refs = refs[:n_own], refs[n_own:]
    outs, refs = refs[: len(kinds)], refs[len(kinds) :]
    slots, refs = refs[:n_parts], refs[n_parts:]
    send_sem, recv_sem = refs
    me = place_in(axes)
    peers = [lax.rem(me + hop, count) for hop in range(1, count)]

    barrier = pltpu.get_barrier_semaphore()
    for peer in peers:
        pl.semaphore_signal(
            barrier,
            inc=1,
            device_id=device_at(axes, peer),
            device_id_type=pl.DeviceIdType.MESH,
        )
    pl.semaphore_wait(barrier, count - 1)

    def rows_of(ref, index):
        rows = ref.shape[0] // count
        return ref.at[pl.ds(pl.multiple_of(index * rows, rows), rows), :]

    def send(source, target, which, hop, peer):
        copy = pltpu.make_async_remote_copy(
            src_ref=source,
            dst_ref=target,
            send_sem=send_sem.at[which, hop],
            recv_sem=recv_sem.at[which, hop],
            device_id=device_at(axes, peer),
            device_id_type=pl.DeviceIdType.MESH,
        )
        copy.start()
        return copy

    copies = []
    for which, (part, slot) in enumerate(zip(parts, slots)):
        for hop, peer in enumerate(peers):
            copies.append(send(rows_of(part, peer), slot.at[hop], which, hop, peer))
    for copy in copies:
        copy.wait()
    sums = []
    for part, slot in zip(parts, slots):
        total = rows_of(part, me)[...].astype(jnp.float32)
        for hop in range(count - 1):
            total = total + slot[hop].astype(jnp.float32)
        sums.append(total)
    results = middle(sums, [rows_of(ref, me)[...] for ref in whole], [ref[...] for ref in own])
    copies = []
    for which, (ref, kind, value) in enumerate(zip(outs, kinds, results)):
        if kind == "rows":
            ref[...] = value.astype(ref.dtype)
        else:
            rows_of(ref, me)[...] = value.astype(ref.dtype)
            for hop, peer in enumerate(peers):
                copies.append(
                    send(rows_of(ref, me), rows_of(ref, me), n_parts + which, hop, peer)
                )
    for copy in copies:
        copy.wait()


def exchange(axes, call_id, parts, whole, own, middle, outs):
    count = math.prod(lax.axis_size(axis) for axis in axes)
    vmem = pl.BlockSpec(memory_space=pltpu.VMEM)
    scratch = [
        pltpu.VMEM((count - 1, part.shape[0] // count) + part.shape[1:], part.dtype)
        for part in parts
    ]
    sems = (len(parts) + len(outs), count - 1)
    return pl.pallas_call(
        functools.partial(
            exchange_kernel,
            axes,
            count,
            (len(parts), len(whole), len(own)),
            [kind for kind, _, _ in outs],
            middle,
        ),
        in_specs=[vmem] * (len(parts) + len(whole) + len(own)),
        out_specs=[vmem] * len(outs),
        out_shape=[jax.ShapeDtypeStruct(shape, dtype) for _, shape, dtype in outs],
        scratch_shapes=scratch
        + [pltpu.SemaphoreType.DMA(sems), pltpu.SemaphoreType.DMA(sems)],
        compiler_params=pltpu.CompilerParams(
            collective_id=call_id, has_side_effects=True, vmem_limit_bytes=40 * 2**20
        ),
    )(*parts, *whole, *own)


def after_mixer(sums, whole, own):
    (mixed,), (tokens_in,), (gain,) = sums, whole, own
    middle = tokens_in.astype(jnp.float32) + mixed
    return middle * inverse_rms(middle) * gain.astype(jnp.float32), middle


def after_ffn_back(sums, whole, own):
    (normed_grad,), (ct,), (middle, gain) = sums, whole, own
    scale = inverse_rms(middle)
    gain_grad = jnp.sum(normed_grad * middle * scale, 0, keepdims=True)
    middle_grad = ct.astype(jnp.float32) + norm_back(
        normed_grad, middle, scale, gain.astype(jnp.float32)
    )
    return middle_grad, middle_grad, gain_grad


def after_mixer_back(sums, whole, own):
    (normed_grad, ffn_out), (tokens_in,), (middle, middle_grad, gain) = sums, whole, own
    hidden_in = tokens_in.astype(jnp.float32)
    scale = inverse_rms(hidden_in)
    gain_grad = jnp.sum(normed_grad * hidden_in * scale, 0, keepdims=True)
    tokens_grad = middle_grad + norm_back(normed_grad, hidden_in, scale, gain.astype(jnp.float32))
    return tokens_grad, middle + ffn_out, gain_grad


def as_they_are(sums, whole, own):
    return sums


def per_device(
    tokens,
    mixgain,
    inproj,
    convkern,
    convbias,
    selproj,
    stepproj,
    stepbias,
    decaylog,
    skipgain,
    outproj,
    ffngain,
    gateup,
    downproj,
    cotangent,
):
    seqs, span, width = tokens.shape
    rows = seqs * span
    taps, inner = convkern.shape
    rank = stepproj.shape[0]
    n_state = decaylog.shape[1]
    tiles = inner // LANE
    gain_mix = mixgain.astype(jnp.float32)
    kernel = convkern.astype(jnp.float32)
    kernel_bias = convbias.astype(jnp.float32)
    step_bias = stepbias.astype(jnp.float32)
    skip_weight = skipgain.astype(jnp.float32)
    decay_rate = -jnp.exp(jnp.transpose(decaylog.astype(jnp.float32)))
    rate = (decay_rate * LOG2E).reshape(n_state, tiles, LANE)

    gain_mix_row, gain_ffn_row = mixgain.reshape(1, width), ffngain.reshape(1, width)
    own_rows = rows // lax.axis_size("tp")
    hidden = gateup.shape[2]
    low = jnp.bfloat16

    mix_pack = gathered_rows(
        jnp.concatenate([inproj[0], inproj[1], jnp.transpose(outproj)], 1)
    )
    ffn_pack = gathered_rows(
        jnp.concatenate([gateup[0], gateup[1], jnp.transpose(downproj)], 1)
    )

    tokens_rows = tokens.reshape(rows, width)
    hidden_in = tokens_rows.astype(jnp.float32)
    scale_one = inverse_rms(hidden_in)
    normed_one = (hidden_in * scale_one * gain_mix).astype(low)
    normed_one_cols = swapped_columns(normed_one)
    ct_low = cotangent.reshape(rows, width)
    ct_cols = swapped_columns(ct_low)
    conv_in = matmul(normed_one, mix_pack[:, :inner]).astype(low)
    gate_mix = matmul(normed_one, mix_pack[:, inner : 2 * inner])
    conv_seqs = conv_in.reshape(seqs, span, inner)
    rim_rows = passed_along(conv_seqs[:, span - (taps - 1) :], "ctx", 1)
    padded_in = jnp.concatenate([rim_rows, conv_seqs], 1).astype(jnp.float32)
    conv_out = kernel_bias[None, None]
    for offset in range(taps):
        conv_out = conv_out + kernel[offset][None, None] * padded_in[:, offset : offset + span]
    conv_out = conv_out.reshape(rows, inner)
    scan_in = jax.nn.silu(conv_out).astype(low)
    scan_float = scan_in.astype(jnp.float32)
    columns = selproj.shape[1]
    select_width = -(-columns // LANE) * LANE
    select_weights = jnp.pad(selproj, ((0, 0), (0, select_width - columns)))
    (select_cols,) = exchange(
        ("tp",),
        0,
        [matmul(scan_in, select_weights)],
        [],
        [],
        as_they_are,
        [("all", (rows, select_width), jnp.float32)],
    )
    step_low = select_cols[:, :rank].astype(low)
    b_rows = select_cols[:, rank : rank + n_state].reshape(-1)
    c_rows = select_cols[:, rank + n_state : columns].reshape(-1)
    step_pre = matmul(step_low, stepproj) + step_bias[None]
    step_size = jax.nn.softplus(step_pre)
    span_decay = jnp.exp(
        decay_rate[None] * jnp.sum(step_size.reshape(seqs, span, inner), 1)[:, None]
    ).reshape(seqs, n_state, tiles, LANE)
    step_tiles, input_tiles = to_tiles(step_size), to_tiles(scan_float)
    ends = scan_ends(step_tiles, input_tiles, b_rows, rate, seqs, False)
    start = from_earlier(ends, span_decay, 1)
    prior, mixed_tiles = scan_forward(start, step_tiles, input_tiles, b_rows, c_rows, rate, seqs)
    mixer_core = from_tiles(mixed_tiles) + skip_weight[None] * scan_float
    gate_sig = jax.nn.silu(gate_mix)
    gated = (mixer_core * gate_sig).astype(low)
    out_weights = mix_pack[:, 2 * inner :]
    normed_two, middle = exchange(
        ("tp",),
        1,
        [matmul_nt(gated, out_weights).astype(low)],
        [tokens_rows],
        [gain_ffn_row],
        after_mixer,
        [("all", (rows, width), low), ("rows", (own_rows, width), jnp.float32)],
    )
    normed_two_cols = swapped_columns(normed_two)
    gate_up = ffn_pack[:, : 2 * hidden]
    down_weights = ffn_pack[:, 2 * hidden :]
    both_ffn = matmul(normed_two, gate_up)
    gate_ffn, up_ffn = both_ffn[:, :hidden], both_ffn[:, hidden:]
    activated = (jax.nn.silu(gate_ffn) * up_ffn).astype(low)
    act_grad = matmul(ct_low, down_weights)
    gate_grad = (act_grad * up_ffn * silu_slope(gate_ffn)).astype(low)
    up_grad = (act_grad * jax.nn.silu(gate_ffn)).astype(low)
    ffn_grads = jnp.concatenate([gate_grad, up_grad], 1)
    ffn_all = gathered_rows(jnp.concatenate([activated, ffn_grads, gated], 1))
    normed_two_part = matmul_nt(ffn_grads, gate_up).astype(low)
    ffn_part = matmul_nt(activated, down_weights).astype(low)
    middle_low, middle_grad, ffngain_part = exchange(
        ("tp",),
        2,
        [normed_two_part],
        [ct_low],
        [middle, gain_ffn_row],
        after_ffn_back,
        [
            ("all", (rows, width), low),
            ("rows", (own_rows, width), jnp.float32),
            ("rows", (1, width), jnp.float32),
        ],
    )
    middle_cols = swapped_columns(middle_low)
    gated_grad = matmul(middle_low, out_weights)
    core_grad = gated_grad * gate_sig
    gate_mix_grad = (gated_grad * mixer_core * silu_slope(gate_mix)).astype(low)
    grad_skipgain = jnp.sum(core_grad * scan_float, 0)
    ograd_tiles = to_tiles(core_grad)
    back_ends = scan_ends(step_tiles, ograd_tiles, c_rows, rate, seqs, True)
    end_grad = from_earlier(back_ends, span_decay, -1)
    step_grad_tiles, input_grad_tiles, rate_grad, parts = scan_backward(
        end_grad, prior, step_tiles, input_tiles, ograd_tiles, b_rows, c_rows, rate, seqs
    )
    grad_decaylog = rate_grad.reshape(n_state, inner) * decay_rate
    pre_grad = from_tiles(step_grad_tiles) * jax.nn.sigmoid(step_pre)
    grad_stepbias = jnp.sum(pre_grad, 0)
    pre_low = pre_grad.astype(low)
    grad_stepproj = matmul_tn(step_low, pre_low)
    select_part = jnp.concatenate(
        [
            matmul_nt(pre_low, stepproj),
            jnp.sum(parts, -1),
            jnp.zeros((rows, select_width - columns), jnp.float32),
        ],
        1,
    ).astype(low)
    (select_low,) = exchange(
        ("tp",),
        3,
        [select_part],
        [],
        [],
        as_they_are,
        [("all", (rows, select_width), low)],
    )
    grad_selproj = matmul_tn(select_low, scan_in)
    scan_in_grad = (
        core_grad * skip_weight[None]
        + from_tiles(input_grad_tiles)
        + matmul_nt(select_low, select_weights)
    )
    conv_grad = scan_in_grad * silu_slope(conv_out)
    grad_convbias = jnp.sum(conv_grad, 0)
    conv_grad_seqs = conv_grad.reshape(seqs, span, inner)
    padded_grad = jnp.zeros(padded_in.shape, jnp.float32)
    kernel_rows = []
    for offset in range(taps):
        kernel_rows.append(jnp.sum(conv_grad_seqs * padded_in[:, offset : offset + span], (0, 1)))
        padded_grad = padded_grad + jnp.pad(
            kernel[offset][None, None] * conv_grad_seqs,
            ((0, 0), (offset, taps - 1 - offset), (0, 0)),
        )
    grad_convkern = jnp.stack(kernel_rows)
    returned = passed_along(padded_grad[:, : taps - 1], "ctx", -1)
    conv_in_grad = (
        (padded_grad[:, taps - 1 :] + jnp.pad(returned, ((0, 0), (span - taps + 1, 0), (0, 0))))
        .astype(low)
        .reshape(rows, inner)
    )
    mix_grads = jnp.concatenate([conv_in_grad, gate_mix_grad], 1)
    mix_all = gathered_rows(mix_grads)
    normed_one_part = matmul_nt(mix_grads, mix_pack[:, : 2 * inner]).astype(low)
    ffn_part, _ = lax.optimization_barrier((ffn_part, normed_one_part))
    tokens_grad, layer_out, mixgain_part = exchange(
        ("tp",),
        4,
        [normed_one_part, ffn_part],
        [tokens_rows],
        [middle, middle_grad, gain_mix_row],
        after_mixer_back,
        [
            ("all", (rows, width), low),
            ("all", (rows, width), low),
            ("rows", (1, width), jnp.float32),
        ],
    )
    grad_downproj = matmul_tn(ffn_all[:, :hidden], ct_cols)
    grad_gateup = jnp.stack(
        [
            matmul_tn(normed_two_cols, ffn_all[:, hidden : 2 * hidden]),
            matmul_tn(normed_two_cols, ffn_all[:, 2 * hidden : 3 * hidden]),
        ]
    )
    grad_outproj = matmul_tn(ffn_all[:, 3 * hidden :], middle_cols)
    grad_inproj = jnp.stack(
        [
            matmul_tn(normed_one_cols, mix_all[:, :inner]),
            matmul_tn(normed_one_cols, mix_all[:, inner:]),
        ]
    )
    small = [
        grad_convkern,
        grad_convbias[None],
        grad_stepbias[None],
        grad_decaylog,
        grad_skipgain[None],
        grad_stepproj,
        grad_selproj[:columns],
    ]
    sizes = [part.shape[0] for part in small]
    share = 16 * math.prod(lax.axis_size(axis) for axis in PLANE)
    small.append(jnp.zeros((-sum(sizes) % share, inner), jnp.float32))
    small = jnp.concatenate(small, 0).astype(low)
    (small,) = exchange(
        PLANE, 5, [small], [], [], as_they_are, [("all", small.shape, low)]
    )
    small = small.astype(jnp.float32)
    smalls, at = [], 0
    for size in sizes:
        smalls.append(small[at : at + size])
        at += size
    gains = lax.psum(jnp.concatenate([mixgain_part, ffngain_part], 0), PLANE + ("tp",))
    return (
        layer_out.reshape(tokens.shape),
        tokens_grad.reshape(tokens.shape),
        gains[0],
        grad_inproj,
        smalls[0],
        smalls[1][0],
        jnp.transpose(smalls[6]),
        smalls[5],
        smalls[2][0],
        jnp.transpose(smalls[3]),
        smalls[4][0],
        grad_outproj,
        gains[1],
        grad_gateup,
        grad_downproj,
    )


def solution(mesh):
    in_specs = (
        P("dp", "ctx", None),
        P(),
        P(None, ("dp", "ctx"), "tp"),
        P(None, "tp"),
        P("tp"),
        P("tp", None),
        P(None, "tp"),
        P("tp"),
        P("tp", None),
        P("tp"),
        P("tp", ("dp", "ctx")),
        P(),
        P(None, ("dp", "ctx"), "tp"),
        P("tp", ("dp", "ctx")),
        P("dp", "ctx", None),
    )
    out_specs = (
        P("dp", "ctx", None),
        P("dp", "ctx", None),
        P(),
        P(None, ("dp", "ctx"), "tp"),
        P(None, "tp"),
        P("tp"),
        P("tp", None),
        P(None, "tp"),
        P("tp"),
        P("tp", None),
        P("tp"),
        P("tp", ("dp", "ctx")),
        P(),
        P(None, ("dp", "ctx"), "tp"),
        P("tp", ("dp", "ctx")),
    )
    return jax.shard_map(
        per_device, mesh=mesh, in_specs=in_specs, out_specs=out_specs, check_vma=False
    )
```

```python
import functools
import math

import jax
import jax.numpy as jnp
from jax import lax
from jax.experimental import pallas as pl
from jax.experimental.pallas import tpu as pltpu
from jax.sharding import PartitionSpec as P

EPSILON = 1e-05
LOG2E = math.log2(math.e)
LN2 = math.log(2.0)
SUB = 8
LANE = 128
PLANE = ("dp", "ctx")


def passed_along(value, axis, steps):
    count = lax.axis_size(axis)
    first, last = (max(0, -steps), min(count, count - steps))
    return lax.ppermute(value, axis, [(source, source + steps) for source in range(first, last)])


def matmul(left, right):
    return jnp.dot(left, right, preferred_element_type=jnp.float32)


def matmul_nt(left, right):
    return lax.dot_general(
        left, right, (((1,), (1,)), ((), ())), preferred_element_type=jnp.float32
    )


def matmul_tn(left, right):
    return lax.dot_general(
        left, right, (((0,), (0,)), ((), ())), preferred_element_type=jnp.float32
    )


def inverse_rms(values):
    return lax.rsqrt(jnp.mean(values * values, -1, keepdims=True) + EPSILON)


def silu_slope(values):
    logistic = jax.nn.sigmoid(values)
    return logistic * (1.0 + values * (1.0 - logistic))


def norm_back(grad_norm, values, scale, gain):
    scaled_grad = grad_norm * gain
    unit_rows = values * scale
    return scale * (scaled_grad - unit_rows * jnp.mean(scaled_grad * unit_rows, -1, keepdims=True))


def stage_in(ref, group, held):
    for tile in range(held.shape[0] // SUB):
        held[pl.ds(tile * SUB, SUB), :] = ref[
            pl.ds(pl.multiple_of(group * SUB, SUB), SUB), pl.ds(tile * LANE, LANE)
        ]


def stage_out(held, ref, group):
    for tile in range(held.shape[0] // SUB):
        ref[pl.ds(pl.multiple_of(group * SUB, SUB), SUB), pl.ds(tile * LANE, LANE)] = held[
            pl.ds(tile * SUB, SUB), :
        ]


def token_row(held, at, tiles):
    return held[pl.ds(at, tiles, stride=SUB), :]


def ends_kernel(
    n_state,
    tiles,
    groups,
    reverse,
    step_ref,
    drive_ref,
    rows_ref,
    rate_ref,
    end_ref,
    step_held,
    drive_held,
):
    base = pl.program_id(0) * groups * SUB * n_state
    rates = [rate_ref[n] for n in range(n_state)]

    def one(turn, states):
        group = groups - 1 - turn if reverse else turn
        order = range(SUB - 1, -1, -1) if reverse else range(SUB)
        states = list(states)
        stage_in(step_ref, group, step_held)
        stage_in(drive_ref, group, drive_held)
        for at in order:
            step = token_row(step_held, at, tiles)
            drive = token_row(drive_held, at, tiles)
            if not reverse:
                drive = drive * step
            for n in range(n_state):
                row = rows_ref[base + (group * SUB + at) * n_state + n]
                decay = jnp.exp2(step * rates[n])
                if reverse:
                    states[n] = decay * (states[n] + drive * row)
                else:
                    states[n] = decay * states[n] + drive * row
        return tuple(states)

    zero = jnp.zeros((tiles, LANE), jnp.float32)
    states = lax.fori_loop(0, groups, one, (zero,) * n_state)
    for n in range(n_state):
        end_ref[0, n] = states[n]


def scan_ends(step, drive, rows, rate, seqs, reverse):
    n_state, tiles, _ = rate.shape
    groups = step.shape[0] // seqs // SUB
    rows_spec = pl.BlockSpec((groups * SUB, tiles * LANE), lambda s: (s, 0))
    held = pltpu.VMEM((tiles * SUB, LANE), jnp.float32)
    return pl.pallas_call(
        functools.partial(ends_kernel, n_state, tiles, groups, reverse),
        grid=(seqs,),
        in_specs=[
            rows_spec,
            rows_spec,
            pl.BlockSpec(memory_space=pltpu.SMEM),
            pl.BlockSpec((n_state, tiles, LANE), lambda s: (0, 0, 0)),
        ],
        out_specs=pl.BlockSpec((1, n_state, tiles, LANE), lambda s: (s, 0, 0, 0)),
        out_shape=jax.ShapeDtypeStruct((seqs, n_state, tiles, LANE), jnp.float32),
        scratch_shapes=[held, held],
        compiler_params=pltpu.CompilerParams(vmem_limit_bytes=32 * 2**20),
    )(step, drive, rows, rate)


def forward_kernel(
    n_state,
    tiles,
    groups,
    blocks,
    start_ref,
    step_ref,
    input_ref,
    brow_ref,
    crow_ref,
    rate_ref,
    prior_ref,
    mixed_ref,
    carried,
    step_held,
    input_held,
    mixed_held,
):
    base = (pl.program_id(0) * blocks + pl.program_id(1)) * groups * SUB * n_state

    @pl.when(pl.program_id(1) == 0)
    def _():
        carried[...] = start_ref[0]

    def one(group, states):
        states = list(states)
        stage_in(step_ref, group, step_held)
        stage_in(input_ref, group, input_held)
        for at in range(SUB):
            step = token_row(step_held, at, tiles)
            drive = step * token_row(input_held, at, tiles)
            mixed = [None] * 2
            for n in range(n_state):
                where = base + (group * SUB + at) * n_state + n
                prior_ref[group * SUB + at, n] = states[n]
                decay = jnp.exp2(step * rate_ref[n])
                states[n] = decay * states[n] + drive * brow_ref[where]
                term = states[n] * crow_ref[where]
                mixed[n % 2] = term if mixed[n % 2] is None else mixed[n % 2] + term
            mixed_held[pl.ds(at, tiles, stride=SUB), :] = mixed[0] + mixed[1]
        stage_out(mixed_held, mixed_ref, group)
        return tuple(states)

    states = lax.fori_loop(0, groups, one, tuple(carried[n] for n in range(n_state)))
    for n in range(n_state):
        carried[n] = states[n]


def scan_forward(start, step, inputs, b_rows, c_rows, rate, seqs):
    n_state, tiles, _ = rate.shape
    all_groups = step.shape[0] // SUB
    groups = math.gcd(all_groups // seqs, 4)
    blocks = all_groups // seqs // groups
    rows_spec = pl.BlockSpec((groups * SUB, tiles * LANE), lambda s, b: (s * blocks + b, 0))
    held = pltpu.VMEM((tiles * SUB, LANE), jnp.float32)
    smem = pl.BlockSpec(memory_space=pltpu.SMEM)
    tokens = all_groups * SUB
    return pl.pallas_call(
        functools.partial(forward_kernel, n_state, tiles, groups, blocks),
        grid=(seqs, blocks),
        in_specs=[
            pl.BlockSpec((1, n_state, tiles, LANE), lambda s, b: (s, 0, 0, 0)),
            rows_spec,
            rows_spec,
            smem,
            smem,
            pl.BlockSpec((n_state, tiles, LANE), lambda s, b: (0, 0, 0)),
        ],
        out_specs=[
            pl.BlockSpec(
                (groups * SUB, n_state, tiles, LANE), lambda s, b: (s * blocks + b, 0, 0, 0)
            ),
            rows_spec,
        ],
        out_shape=[
            jax.ShapeDtypeStruct((tokens, n_state, tiles, LANE), jnp.float32),
            jax.ShapeDtypeStruct(step.shape, jnp.float32),
        ],
        scratch_shapes=[pltpu.VMEM((n_state, tiles, LANE), jnp.float32)] + [held] * 3,
        compiler_params=pltpu.CompilerParams(vmem_limit_bytes=32 * 2**20),
    )(start, step, inputs, b_rows, c_rows, rate)


def backward_kernel(
    n_state,
    tiles,
    groups,
    blocks,
    end_ref,
    prior_ref,
    step_ref,
    input_ref,
    ograd_ref,
    brow_ref,
    crow_ref,
    rate_ref,
    picks_ref,
    step_grad_ref,
    input_grad_ref,
    rate_grad_ref,
    part_ref,
    carried,
    step_held,
    input_held,
    ograd_held,
    step_grad_held,
    input_grad_held,
):
    block = blocks - 1 - pl.program_id(1)
    base = (pl.program_id(0) * blocks + block) * groups * SUB * n_state

    @pl.when(pl.program_id(1) == 0)
    def _():
        carried[...] = end_ref[0]

    @pl.when((pl.program_id(0) == 0) & (pl.program_id(1) == 0))
    def _():
        rate_grad_ref[...] = jnp.zeros_like(rate_grad_ref)

    def one(turn, grads):
        group = groups - 1 - turn
        grads = list(grads)
        stage_in(step_ref, group, step_held)
        stage_in(input_ref, group, input_held)
        stage_in(ograd_ref, group, ograd_held)
        for at in range(SUB - 1, -1, -1):
            step = token_row(step_held, at, tiles)
            value = token_row(input_held, at, tiles)
            ograd = token_row(ograd_held, at, tiles)
            drive = step * value
            along_b = None
            along_rate = None
            brow_parts, crow_parts = [], []
            for n in range(n_state):
                where = base + (group * SUB + at) * n_state + n
                brow, crow = brow_ref[where], crow_ref[where]
                rate = rate_ref[n]
                decay = jnp.exp2(step * rate)
                grad = ograd * crow + grads[n]
                kept = decay * prior_ref[group * SUB + at, n]
                state = kept + drive * brow
                decay_term = grad * kept
                grads[n] = decay * grad
                rate_grad_ref[n] += decay_term * step
                by_rate, by_brow = decay_term * rate, grad * brow
                along_rate = by_rate if along_rate is None else along_rate + by_rate
                along_b = by_brow if along_b is None else along_b + by_brow
                brow_parts.append(grad * drive)
                crow_parts.append(ograd * state)
            step_grad_held[pl.ds(at, tiles, stride=SUB), :] = along_rate * LN2 + along_b * value
            input_grad_held[pl.ds(at, tiles, stride=SUB), :] = along_b * step
            parts = jnp.concatenate(brow_parts + crow_parts, 0).astype(jnp.bfloat16)
            part_ref[group * SUB + at] = jnp.dot(
                picks_ref[...], parts, preferred_element_type=jnp.float32
            )
        stage_out(step_grad_held, step_grad_ref, group)
        stage_out(input_grad_held, input_grad_ref, group)
        return tuple(grads)

    grads = lax.fori_loop(0, groups, one, tuple(carried[n] for n in range(n_state)))
    for n in range(n_state):
        carried[n] = grads[n]


def scan_backward(end_grad, prior, step, inputs, ograd, b_rows, c_rows, rate, seqs):
    n_state, tiles, _ = rate.shape
    all_groups = step.shape[0] // SUB
    groups = math.gcd(all_groups // seqs, 4)
    blocks = all_groups // seqs // groups

    def at(s, b):
        return s * blocks + blocks - 1 - b

    rows_spec = pl.BlockSpec((groups * SUB, tiles * LANE), lambda s, b: (at(s, b), 0))
    held = pltpu.VMEM((tiles * SUB, LANE), jnp.float32)
    smem = pl.BlockSpec(memory_space=pltpu.SMEM)
    tokens = all_groups * SUB
    picks = jnp.repeat(jnp.eye(2 * n_state, dtype=jnp.bfloat16), tiles, 1)
    return pl.pallas_call(
        functools.partial(backward_kernel, n_state, tiles, groups, blocks),
        grid=(seqs, blocks),
        in_specs=[
            pl.BlockSpec((1, n_state, tiles, LANE), lambda s, b: (s, 0, 0, 0)),
            pl.BlockSpec((groups * SUB, n_state, tiles, LANE), lambda s, b: (at(s, b), 0, 0, 0)),
            rows_spec,
            rows_spec,
            rows_spec,
            smem,
            smem,
            pl.BlockSpec((n_state, tiles, LANE), lambda s, b: (0, 0, 0)),
            pl.BlockSpec(picks.shape, lambda s, b: (0, 0)),
        ],
        out_specs=[
            rows_spec,
            rows_spec,
            pl.BlockSpec((n_state, tiles, LANE), lambda s, b: (0, 0, 0)),
            pl.BlockSpec((groups * SUB, 2 * n_state, LANE), lambda s, b: (at(s, b), 0, 0)),
        ],
        out_shape=[
            jax.ShapeDtypeStruct(step.shape, jnp.float32),
            jax.ShapeDtypeStruct(step.shape, jnp.float32),
            jax.ShapeDtypeStruct(rate.shape, jnp.float32),
            jax.ShapeDtypeStruct((tokens, 2 * n_state, LANE), jnp.float32),
        ],
        scratch_shapes=[pltpu.VMEM((n_state, tiles, LANE), jnp.float32)] + [held] * 5,
        compiler_params=pltpu.CompilerParams(vmem_limit_bytes=32 * 2**20),
    )(end_grad, prior, step, inputs, ograd, b_rows, c_rows, rate, picks)


def from_earlier(ends, decay, steps):
    count = lax.axis_size("ctx")
    if count == 1:
        return jnp.zeros_like(ends)
    if count == 2:
        return passed_along(ends, "ctx", steps)
    index = lax.axis_index("ctx")
    all_ends = lax.all_gather(ends, "ctx")
    all_decays = lax.all_gather(decay, "ctx")

    def one(turn, state):
        at = turn if steps > 0 else count - 1 - turn
        reached = at < index if steps > 0 else at > index
        return jnp.where(reached, all_decays[at] * state + all_ends[at], state)

    return lax.fori_loop(0, count, one, jnp.zeros_like(ends))


def gathered_rows(rows):
    return lax.all_gather(rows, PLANE, axis=0, tiled=True)


def swapped_columns(rows):
    return lax.all_to_all(rows, PLANE, split_axis=1, concat_axis=0, tiled=True)


def place_in(axes):
    index = 0
    for axis in axes:
        index = index * lax.axis_size(axis) + lax.axis_index(axis)
    return index


def device_at(axes, index):
    where = {}
    for axis in reversed(axes):
        size = lax.axis_size(axis)
        where[axis] = lax.rem(index, size)
        index = lax.div(index, size)
    return where


def exchange_kernel(axes, count, counts, kinds, middle, *refs):
    n_parts, n_whole, n_own = counts
    parts, refs = refs[:n_parts], refs[n_parts:]
    whole, refs = refs[:n_whole], refs[n_whole:]
    own, refs = refs[:n_own], refs[n_own:]
    outs, refs = refs[: len(kinds)], refs[len(kinds) :]
    slots, refs = refs[:n_parts], refs[n_parts:]
    send_sem, recv_sem = refs
    me = place_in(axes)
    peers = [lax.rem(me + hop, count) for hop in range(1, count)]

    barrier = pltpu.get_barrier_semaphore()
    for peer in peers:
        pl.semaphore_signal(
            barrier,
            inc=1,
            device_id=device_at(axes, peer),
            device_id_type=pl.DeviceIdType.MESH,
        )
    pl.semaphore_wait(barrier, count - 1)

    def rows_of(ref, index):
        rows = ref.shape[0] // count
        return ref.at[pl.ds(pl.multiple_of(index * rows, rows), rows), :]

    def send(source, target, which, hop, peer):
        copy = pltpu.make_async_remote_copy(
            src_ref=source,
            dst_ref=target,
            send_sem=send_sem.at[which, hop],
            recv_sem=recv_sem.at[which, hop],
            device_id=device_at(axes, peer),
            device_id_type=pl.DeviceIdType.MESH,
        )
        copy.start()
        return copy

    copies = []
    for which, (part, slot) in enumerate(zip(parts, slots)):
        for hop, peer in enumerate(peers):
            copies.append(send(rows_of(part, peer), slot.at[hop], which, hop, peer))
    for copy in copies:
        copy.wait()
    sums = []
    for part, slot in zip(parts, slots):
        total = rows_of(part, me)[...].astype(jnp.float32)
        for hop in range(count - 1):
            total = total + slot[hop].astype(jnp.float32)
        sums.append(total)
    results = middle(sums, [rows_of(ref, me)[...] for ref in whole], [ref[...] for ref in own])
    copies = []
    for which, (ref, kind, value) in enumerate(zip(outs, kinds, results)):
        if kind == "rows":
            ref[...] = value.astype(ref.dtype)
        else:
            rows_of(ref, me)[...] = value.astype(ref.dtype)
            for hop, peer in enumerate(peers):
                copies.append(
                    send(rows_of(ref, me), rows_of(ref, me), n_parts + which, hop, peer)
                )
    for copy in copies:
        copy.wait()


def exchange(axes, call_id, parts, whole, own, middle, outs):
    count = math.prod(lax.axis_size(axis) for axis in axes)
    vmem = pl.BlockSpec(memory_space=pltpu.VMEM)
    scratch = [
        pltpu.VMEM((count - 1, part.shape[0] // count) + part.shape[1:], part.dtype)
        for part in parts
    ]
    sems = (len(parts) + len(outs), count - 1)
    return pl.pallas_call(
        functools.partial(
            exchange_kernel,
            axes,
            count,
            (len(parts), len(whole), len(own)),
            [kind for kind, _, _ in outs],
            middle,
        ),
        in_specs=[vmem] * (len(parts) + len(whole) + len(own)),
        out_specs=[vmem] * len(outs),
        out_shape=[jax.ShapeDtypeStruct(shape, dtype) for _, shape, dtype in outs],
        scratch_shapes=scratch
        + [pltpu.SemaphoreType.DMA(sems), pltpu.SemaphoreType.DMA(sems)],
        compiler_params=pltpu.CompilerParams(
            collective_id=call_id, has_side_effects=True, vmem_limit_bytes=40 * 2**20
        ),
    )(*parts, *whole, *own)


def after_mixer(sums, whole, own):
    (mixed,), (tokens_in,), (gain,) = sums, whole, own
    middle = tokens_in.astype(jnp.float32) + mixed
    return middle * inverse_rms(middle) * gain.astype(jnp.float32), middle


def after_ffn_back(sums, whole, own):
    (normed_grad,), (ct,), (middle, gain) = sums, whole, own
    scale = inverse_rms(middle)
    gain_grad = jnp.sum(normed_grad * middle * scale, 0, keepdims=True)
    middle_grad = ct.astype(jnp.float32) + norm_back(
        normed_grad, middle, scale, gain.astype(jnp.float32)
    )
    return middle_grad, middle_grad, gain_grad


def after_mixer_back(sums, whole, own):
    (normed_grad, ffn_out, gains), (tokens_in,), (middle, middle_grad, gain) = sums, whole, own
    hidden_in = tokens_in.astype(jnp.float32)
    scale = inverse_rms(hidden_in)
    tokens_grad = middle_grad + norm_back(normed_grad, hidden_in, scale, gain.astype(jnp.float32))
    return tokens_grad, middle + ffn_out, gains


def as_they_are(sums, whole, own):
    return sums


def per_device(
    tokens,
    mixgain,
    inproj,
    convkern,
    convbias,
    selproj,
    stepproj,
    stepbias,
    decaylog,
    skipgain,
    outproj,
    ffngain,
    gateup,
    downproj,
    cotangent,
):
    seqs, span, width = tokens.shape
    rows = seqs * span
    taps, inner = convkern.shape
    rank = stepproj.shape[0]
    n_state = decaylog.shape[1]
    tiles = inner // LANE
    gain_mix = mixgain.astype(jnp.float32)
    kernel = convkern.astype(jnp.float32)
    kernel_bias = convbias.astype(jnp.float32)
    step_bias = stepbias.astype(jnp.float32)
    skip_weight = skipgain.astype(jnp.float32)
    decay_rate = -jnp.exp(jnp.transpose(decaylog.astype(jnp.float32)))
    rate = (decay_rate * LOG2E).reshape(n_state, tiles, LANE)

    gain_mix_row, gain_ffn_row = mixgain.reshape(1, width), ffngain.reshape(1, width)
    own_rows = rows // lax.axis_size("tp")
    hidden = gateup.shape[2]
    low = jnp.bfloat16

    mix_pack = gathered_rows(
        jnp.concatenate([inproj[0], inproj[1], jnp.transpose(outproj)], 1)
    )
    ffn_pack = gathered_rows(
        jnp.concatenate([gateup[0], gateup[1], jnp.transpose(downproj)], 1)
    )

    tokens_rows = tokens.reshape(rows, width)
    hidden_in = tokens_rows.astype(jnp.float32)
    scale_one = inverse_rms(hidden_in)
    normed_one = (hidden_in * scale_one * gain_mix).astype(low)
    ct_low = cotangent.reshape(rows, width)
    normed_one_cols, ct_cols = swapped_columns(normed_one), swapped_columns(ct_low)
    normed_one, normed_one_cols, ct_cols = lax.optimization_barrier(
        (normed_one, normed_one_cols, ct_cols)
    )
    conv_in = matmul(normed_one, mix_pack[:, :inner]).astype(low)
    gate_mix = matmul(normed_one, mix_pack[:, inner : 2 * inner])
    conv_seqs = conv_in.reshape(seqs, span, inner)
    rim_rows = passed_along(conv_seqs[:, span - (taps - 1) :], "ctx", 1)
    padded_in = jnp.concatenate([rim_rows, conv_seqs], 1).astype(jnp.float32)
    conv_out = kernel_bias[None, None]
    for offset in range(taps):
        conv_out = conv_out + kernel[offset][None, None] * padded_in[:, offset : offset + span]
    conv_out = conv_out.reshape(rows, inner)
    scan_in = jax.nn.silu(conv_out).astype(low)
    scan_float = scan_in.astype(jnp.float32)
    columns = selproj.shape[1]
    select_width = -(-columns // LANE) * LANE
    select_weights = jnp.pad(selproj, ((0, 0), (0, select_width - columns)))
    (select_cols,) = exchange(
        ("tp",),
        0,
        [matmul(scan_in, select_weights)],
        [],
        [],
        as_they_are,
        [("all", (rows, select_width), jnp.float32)],
    )
    step_low = select_cols[:, :rank].astype(low)
    b_rows = select_cols[:, rank : rank + n_state].reshape(-1)
    c_rows = select_cols[:, rank + n_state : columns].reshape(-1)
    step_pre = matmul(step_low, stepproj) + step_bias[None]
    step_size = jax.nn.softplus(step_pre)
    span_decay = jnp.exp(
        decay_rate[None] * jnp.sum(step_size.reshape(seqs, span, inner), 1)[:, None]
    ).reshape(seqs, n_state, tiles, LANE)
    ends = scan_ends(step_size, scan_float, b_rows, rate, seqs, False)
    start = from_earlier(ends, span_decay, 1)
    prior, scan_out = scan_forward(start, step_size, scan_float, b_rows, c_rows, rate, seqs)
    mixer_core = scan_out + skip_weight[None] * scan_float
    gate_sig = jax.nn.silu(gate_mix)
    gated = (mixer_core * gate_sig).astype(low)
    out_weights = mix_pack[:, 2 * inner :]
    normed_two, middle = exchange(
        ("tp",),
        1,
        [matmul_nt(gated, out_weights).astype(low)],
        [tokens_rows],
        [gain_ffn_row],
        after_mixer,
        [("all", (rows, width), low), ("rows", (own_rows, width), jnp.float32)],
    )
    normed_two_cols = swapped_columns(normed_two)
    gate_up = ffn_pack[:, : 2 * hidden]
    down_weights = ffn_pack[:, 2 * hidden :]
    both_ffn = matmul(normed_two, gate_up)
    gate_ffn, up_ffn = both_ffn[:, :hidden], both_ffn[:, hidden:]
    activated = (jax.nn.silu(gate_ffn) * up_ffn).astype(low)
    act_grad = matmul(ct_low, down_weights)
    gate_grad = (act_grad * up_ffn * silu_slope(gate_ffn)).astype(low)
    up_grad = (act_grad * jax.nn.silu(gate_ffn)).astype(low)
    ffn_grads = jnp.concatenate([gate_grad, up_grad], 1)
    ffn_sent, ffn_grads = lax.optimization_barrier(
        (jnp.concatenate([activated, ffn_grads, gated], 1), ffn_grads)
    )
    ffn_all = gathered_rows(ffn_sent)
    normed_two_part = matmul_nt(ffn_grads, gate_up).astype(low)
    normed_two_part, normed_two_cols = lax.optimization_barrier((normed_two_part, normed_two_cols))
    ffn_part = matmul_nt(activated, down_weights).astype(low)
    middle_low, middle_grad, ffngain_part = exchange(
        ("tp",),
        2,
        [normed_two_part],
        [ct_low],
        [middle, gain_ffn_row],
        after_ffn_back,
        [
            ("all", (rows, width), low),
            ("rows", (own_rows, width), jnp.float32),
            ("rows", (1, width), jnp.float32),
        ],
    )
    middle_cols = swapped_columns(middle_low)
    gated_grad = matmul(middle_low, out_weights)
    core_grad = gated_grad * gate_sig
    gate_mix_grad = (gated_grad * mixer_core * silu_slope(gate_mix)).astype(low)
    grad_skipgain = jnp.sum(core_grad * scan_float, 0)
    back_ends = scan_ends(step_size, core_grad, c_rows, rate, seqs, True)
    end_grad = from_earlier(back_ends, span_decay, -1)
    end_grad, middle_cols = lax.optimization_barrier((end_grad, middle_cols))
    step_grad, input_grad, rate_grad, parts = scan_backward(
        end_grad, prior, step_size, scan_float, core_grad, b_rows, c_rows, rate, seqs
    )
    grad_decaylog = rate_grad.reshape(n_state, inner) * decay_rate
    pre_grad = step_grad * jax.nn.sigmoid(step_pre)
    grad_stepbias = jnp.sum(pre_grad, 0)
    pre_low = pre_grad.astype(low)
    grad_stepproj = matmul_tn(step_low, pre_low)
    select_part = jnp.concatenate(
        [
            matmul_nt(pre_low, stepproj),
            jnp.sum(parts, -1),
            jnp.zeros((rows, select_width - columns), jnp.float32),
        ],
        1,
    ).astype(low)
    (select_low,) = exchange(
        ("tp",),
        3,
        [select_part],
        [],
        [],
        as_they_are,
        [("all", (rows, select_width), low)],
    )
    grad_selproj = matmul_tn(select_low, scan_in)
    scan_in_grad = (
        core_grad * skip_weight[None]
        + input_grad
        + matmul_nt(select_low, select_weights)
    )
    conv_grad = scan_in_grad * silu_slope(conv_out)
    grad_convbias = jnp.sum(conv_grad, 0)
    conv_grad_seqs = conv_grad.reshape(seqs, span, inner)
    padded_grad = jnp.zeros(padded_in.shape, jnp.float32)
    kernel_rows = []
    for offset in range(taps):
        kernel_rows.append(jnp.sum(conv_grad_seqs * padded_in[:, offset : offset + span], (0, 1)))
        padded_grad = padded_grad + jnp.pad(
            kernel[offset][None, None] * conv_grad_seqs,
            ((0, 0), (offset, taps - 1 - offset), (0, 0)),
        )
    grad_convkern = jnp.stack(kernel_rows)
    returned = passed_along(padded_grad[:, : taps - 1], "ctx", -1)
    conv_in_grad = (
        (padded_grad[:, taps - 1 :] + jnp.pad(returned, ((0, 0), (span - taps + 1, 0), (0, 0))))
        .astype(low)
        .reshape(rows, inner)
    )
    mix_grads = jnp.concatenate([conv_in_grad, gate_mix_grad], 1)
    mix_sent, ffn_all = lax.optimization_barrier((mix_grads, ffn_all))
    mix_all = gathered_rows(mix_sent)
    normed_one_part = matmul_nt(mix_grads, mix_pack[:, : 2 * inner])
    mixgain_part = jnp.sum(normed_one_part * hidden_in * scale_one, 0)
    normed_one_part = normed_one_part.astype(low)
    small = [
        grad_convkern,
        grad_convbias[None],
        grad_stepbias[None],
        grad_decaylog,
        grad_skipgain[None],
        grad_stepproj,
        grad_selproj[:columns],
        mixgain_part.reshape(-1, inner),
        ffngain_part.reshape(-1, inner),
    ]
    sizes = [part.shape[0] for part in small]
    share = 16 * math.prod(lax.axis_size(axis) for axis in PLANE)
    small.append(jnp.zeros((-sum(sizes) % share, inner), jnp.float32))
    small = jnp.concatenate(small, 0).astype(low)
    (small,) = exchange(
        PLANE, 5, [small], [], [], as_they_are, [("all", small.shape, low)]
    )
    small = small.astype(jnp.float32)
    smalls, at = [], 0
    for size in sizes:
        smalls.append(small[at : at + size])
        at += size
    gain_rows = jnp.concatenate(smalls[7:9], 0).reshape(-1, LANE)
    tokens_grad, layer_out, gains = exchange(
        ("tp",),
        4,
        [normed_one_part, ffn_part, gain_rows],
        [tokens_rows],
        [middle, middle_grad, gain_mix_row],
        after_mixer_back,
        [
            ("all", (rows, width), low),
            ("all", (rows, width), low),
            ("all", gain_rows.shape, jnp.float32),
        ],
    )
    gains = gains.reshape(2, width)
    grad_downproj = matmul_tn(ffn_all[:, :hidden], ct_cols)
    grad_gateup = jnp.stack(
        [
            matmul_tn(normed_two_cols, ffn_all[:, hidden : 2 * hidden]),
            matmul_tn(normed_two_cols, ffn_all[:, 2 * hidden : 3 * hidden]),
        ]
    )
    grad_outproj = matmul_tn(ffn_all[:, 3 * hidden :], middle_cols)
    grad_inproj = jnp.stack(
        [
            matmul_tn(normed_one_cols, mix_all[:, :inner]),
            matmul_tn(normed_one_cols, mix_all[:, inner:]),
        ]
    )
    return (
        layer_out.reshape(tokens.shape),
        tokens_grad.reshape(tokens.shape),
        gains[0],
        grad_inproj,
        smalls[0],
        smalls[1][0],
        jnp.transpose(smalls[6]),
        smalls[5],
        smalls[2][0],
        jnp.transpose(smalls[3]),
        smalls[4][0],
        grad_outproj,
        gains[1],
        grad_gateup,
        grad_downproj,
    )


def solution(mesh):
    in_specs = (
        P("dp", "ctx", None),
        P(),
        P(None, ("dp", "ctx"), "tp"),
        P(None, "tp"),
        P("tp"),
        P("tp", None),
        P(None, "tp"),
        P("tp"),
        P("tp", None),
        P("tp"),
        P("tp", ("dp", "ctx")),
        P(),
        P(None, ("dp", "ctx"), "tp"),
        P("tp", ("dp", "ctx")),
        P("dp", "ctx", None),
    )
    out_specs = (
        P("dp", "ctx", None),
        P("dp", "ctx", None),
        P(),
        P(None, ("dp", "ctx"), "tp"),
        P(None, "tp"),
        P("tp"),
        P("tp", None),
        P(None, "tp"),
        P("tp"),
        P("tp", None),
        P("tp"),
        P("tp", ("dp", "ctx")),
        P(),
        P(None, ("dp", "ctx"), "tp"),
        P("tp", ("dp", "ctx")),
    )
    return jax.shard_map(
        per_device, mesh=mesh, in_specs=in_specs, out_specs=out_specs, check_vma=False
    )
```

```python
import functools
import math

import jax
import jax.numpy as jnp
from jax import lax
from jax.experimental import pallas as pl
from jax.experimental.pallas import tpu as pltpu
from jax.sharding import PartitionSpec as P

EPSILON = 1e-05
LOG2E = math.log2(math.e)
LN2 = math.log(2.0)
SUB = 8
LANE = 128
PLANE = ("dp", "ctx")


def passed_along(value, axis, steps):
    count = lax.axis_size(axis)
    first, last = (max(0, -steps), min(count, count - steps))
    return lax.ppermute(value, axis, [(source, source + steps) for source in range(first, last)])


def matmul(left, right):
    return jnp.dot(left, right, preferred_element_type=jnp.float32)


def matmul_nt(left, right):
    return lax.dot_general(
        left, right, (((1,), (1,)), ((), ())), preferred_element_type=jnp.float32
    )


def matmul_tn(left, right):
    return lax.dot_general(
        left, right, (((0,), (0,)), ((), ())), preferred_element_type=jnp.float32
    )


def inverse_rms(values):
    return lax.rsqrt(jnp.mean(values * values, -1, keepdims=True) + EPSILON)


def silu_slope(values):
    logistic = jax.nn.sigmoid(values)
    return logistic * (1.0 + values * (1.0 - logistic))


def norm_back(grad_norm, values, scale, gain):
    scaled_grad = grad_norm * gain
    unit_rows = values * scale
    return scale * (scaled_grad - unit_rows * jnp.mean(scaled_grad * unit_rows, -1, keepdims=True))


def stage_in(ref, group, held):
    for tile in range(held.shape[0] // SUB):
        held[pl.ds(tile * SUB, SUB), :] = ref[
            pl.ds(pl.multiple_of(group * SUB, SUB), SUB), pl.ds(tile * LANE, LANE)
        ]


def stage_out(held, ref, group):
    for tile in range(held.shape[0] // SUB):
        ref[pl.ds(pl.multiple_of(group * SUB, SUB), SUB), pl.ds(tile * LANE, LANE)] = held[
            pl.ds(tile * SUB, SUB), :
        ]


def token_row(held, at, tiles):
    return held[pl.ds(at, tiles, stride=SUB), :]


def ends_kernel(
    n_state,
    tiles,
    groups,
    reverse,
    step_ref,
    drive_ref,
    rows_ref,
    rate_ref,
    end_ref,
    step_held,
    drive_held,
):
    base = pl.program_id(0) * groups * SUB * n_state
    rates = [rate_ref[n] for n in range(n_state)]

    def one(turn, states):
        group = groups - 1 - turn if reverse else turn
        order = range(SUB - 1, -1, -1) if reverse else range(SUB)
        states = list(states)
        stage_in(step_ref, group, step_held)
        stage_in(drive_ref, group, drive_held)
        for at in order:
            step = token_row(step_held, at, tiles)
            drive = token_row(drive_held, at, tiles)
            if not reverse:
                drive = drive * step
            for n in range(n_state):
                row = rows_ref[base + (group * SUB + at) * n_state + n]
                decay = jnp.exp2(step * rates[n])
                if reverse:
                    states[n] = decay * (states[n] + drive * row)
                else:
                    states[n] = decay * states[n] + drive * row
        return tuple(states)

    zero = jnp.zeros((tiles, LANE), jnp.float32)
    states = lax.fori_loop(0, groups, one, (zero,) * n_state)
    for n in range(n_state):
        end_ref[0, n] = states[n]


def scan_ends(step, drive, rows, rate, seqs, reverse):
    n_state, tiles, _ = rate.shape
    groups = step.shape[0] // seqs // SUB
    rows_spec = pl.BlockSpec((groups * SUB, tiles * LANE), lambda s: (s, 0))
    held = pltpu.VMEM((tiles * SUB, LANE), jnp.float32)
    return pl.pallas_call(
        functools.partial(ends_kernel, n_state, tiles, groups, reverse),
        grid=(seqs,),
        in_specs=[
            rows_spec,
            rows_spec,
            pl.BlockSpec(memory_space=pltpu.SMEM),
            pl.BlockSpec((n_state, tiles, LANE), lambda s: (0, 0, 0)),
        ],
        out_specs=pl.BlockSpec((1, n_state, tiles, LANE), lambda s: (s, 0, 0, 0)),
        out_shape=jax.ShapeDtypeStruct((seqs, n_state, tiles, LANE), jnp.float32),
        scratch_shapes=[held, held],
        compiler_params=pltpu.CompilerParams(vmem_limit_bytes=32 * 2**20),
    )(step, drive, rows, rate)


def forward_kernel(
    n_state,
    tiles,
    groups,
    blocks,
    start_ref,
    step_ref,
    input_ref,
    brow_ref,
    crow_ref,
    rate_ref,
    prior_ref,
    mixed_ref,
    carried,
    step_held,
    input_held,
    mixed_held,
):
    base = (pl.program_id(0) * blocks + pl.program_id(1)) * groups * SUB * n_state

    @pl.when(pl.program_id(1) == 0)
    def _():
        carried[...] = start_ref[0]

    def one(group, states):
        states = list(states)
        stage_in(step_ref, group, step_held)
        stage_in(input_ref, group, input_held)
        for at in range(SUB):
            step = token_row(step_held, at, tiles)
            drive = step * token_row(input_held, at, tiles)
            mixed = [None] * 2
            for n in range(n_state):
                where = base + (group * SUB + at) * n_state + n
                prior_ref[group * SUB + at, n] = states[n]
                decay = jnp.exp2(step * rate_ref[n])
                states[n] = decay * states[n] + drive * brow_ref[where]
                term = states[n] * crow_ref[where]
                mixed[n % 2] = term if mixed[n % 2] is None else mixed[n % 2] + term
            mixed_held[pl.ds(at, tiles, stride=SUB), :] = mixed[0] + mixed[1]
        stage_out(mixed_held, mixed_ref, group)
        return tuple(states)

    states = lax.fori_loop(0, groups, one, tuple(carried[n] for n in range(n_state)))
    for n in range(n_state):
        carried[n] = states[n]


def scan_forward(start, step, inputs, b_rows, c_rows, rate, seqs):
    n_state, tiles, _ = rate.shape
    all_groups = step.shape[0] // SUB
    groups = math.gcd(all_groups // seqs, 4)
    blocks = all_groups // seqs // groups
    rows_spec = pl.BlockSpec((groups * SUB, tiles * LANE), lambda s, b: (s * blocks + b, 0))
    held = pltpu.VMEM((tiles * SUB, LANE), jnp.float32)
    smem = pl.BlockSpec(memory_space=pltpu.SMEM)
    tokens = all_groups * SUB
    return pl.pallas_call(
        functools.partial(forward_kernel, n_state, tiles, groups, blocks),
        grid=(seqs, blocks),
        in_specs=[
            pl.BlockSpec((1, n_state, tiles, LANE), lambda s, b: (s, 0, 0, 0)),
            rows_spec,
            rows_spec,
            smem,
            smem,
            pl.BlockSpec((n_state, tiles, LANE), lambda s, b: (0, 0, 0)),
        ],
        out_specs=[
            pl.BlockSpec(
                (groups * SUB, n_state, tiles, LANE), lambda s, b: (s * blocks + b, 0, 0, 0)
            ),
            rows_spec,
        ],
        out_shape=[
            jax.ShapeDtypeStruct((tokens, n_state, tiles, LANE), jnp.float32),
            jax.ShapeDtypeStruct(step.shape, jnp.float32),
        ],
        scratch_shapes=[pltpu.VMEM((n_state, tiles, LANE), jnp.float32)] + [held] * 3,
        compiler_params=pltpu.CompilerParams(vmem_limit_bytes=32 * 2**20),
    )(start, step, inputs, b_rows, c_rows, rate)


def backward_kernel(
    n_state,
    tiles,
    groups,
    blocks,
    end_ref,
    prior_ref,
    step_ref,
    input_ref,
    ograd_ref,
    brow_ref,
    crow_ref,
    rate_ref,
    picks_ref,
    step_grad_ref,
    input_grad_ref,
    rate_grad_ref,
    part_ref,
    carried,
    step_held,
    input_held,
    ograd_held,
    step_grad_held,
    input_grad_held,
):
    block = blocks - 1 - pl.program_id(1)
    base = (pl.program_id(0) * blocks + block) * groups * SUB * n_state

    @pl.when(pl.program_id(1) == 0)
    def _():
        carried[...] = end_ref[0]

    @pl.when((pl.program_id(0) == 0) & (pl.program_id(1) == 0))
    def _():
        rate_grad_ref[...] = jnp.zeros_like(rate_grad_ref)

    def one(turn, grads):
        group = groups - 1 - turn
        grads = list(grads)
        stage_in(step_ref, group, step_held)
        stage_in(input_ref, group, input_held)
        stage_in(ograd_ref, group, ograd_held)
        for at in range(SUB - 1, -1, -1):
            step = token_row(step_held, at, tiles)
            value = token_row(input_held, at, tiles)
            ograd = token_row(ograd_held, at, tiles)
            drive = step * value
            along_b = None
            along_rate = None
            brow_parts, crow_parts = [], []
            for n in range(n_state):
                where = base + (group * SUB + at) * n_state + n
                brow, crow = brow_ref[where], crow_ref[where]
                rate = rate_ref[n]
                decay = jnp.exp2(step * rate)
                grad = ograd * crow + grads[n]
                kept = decay * prior_ref[group * SUB + at, n]
                state = kept + drive * brow
                decay_term = grad * kept
                grads[n] = decay * grad
                rate_grad_ref[n] += decay_term * step
                by_rate, by_brow = decay_term * rate, grad * brow
                along_rate = by_rate if along_rate is None else along_rate + by_rate
                along_b = by_brow if along_b is None else along_b + by_brow
                brow_parts.append(grad * drive)
                crow_parts.append(ograd * state)
            step_grad_held[pl.ds(at, tiles, stride=SUB), :] = along_rate * LN2 + along_b * value
            input_grad_held[pl.ds(at, tiles, stride=SUB), :] = along_b * step
            parts = jnp.concatenate(brow_parts + crow_parts, 0).astype(jnp.bfloat16)
            part_ref[group * SUB + at] = jnp.dot(
                picks_ref[...], parts, preferred_element_type=jnp.float32
            )
        stage_out(step_grad_held, step_grad_ref, group)
        stage_out(input_grad_held, input_grad_ref, group)
        return tuple(grads)

    grads = lax.fori_loop(0, groups, one, tuple(carried[n] for n in range(n_state)))
    for n in range(n_state):
        carried[n] = grads[n]


def scan_backward(end_grad, prior, step, inputs, ograd, b_rows, c_rows, rate, seqs):
    n_state, tiles, _ = rate.shape
    all_groups = step.shape[0] // SUB
    groups = math.gcd(all_groups // seqs, 4)
    blocks = all_groups // seqs // groups

    def at(s, b):
        return s * blocks + blocks - 1 - b

    rows_spec = pl.BlockSpec((groups * SUB, tiles * LANE), lambda s, b: (at(s, b), 0))
    held = pltpu.VMEM((tiles * SUB, LANE), jnp.float32)
    smem = pl.BlockSpec(memory_space=pltpu.SMEM)
    tokens = all_groups * SUB
    picks = jnp.repeat(jnp.eye(2 * n_state, dtype=jnp.bfloat16), tiles, 1)
    return pl.pallas_call(
        functools.partial(backward_kernel, n_state, tiles, groups, blocks),
        grid=(seqs, blocks),
        in_specs=[
            pl.BlockSpec((1, n_state, tiles, LANE), lambda s, b: (s, 0, 0, 0)),
            pl.BlockSpec((groups * SUB, n_state, tiles, LANE), lambda s, b: (at(s, b), 0, 0, 0)),
            rows_spec,
            rows_spec,
            rows_spec,
            smem,
            smem,
            pl.BlockSpec((n_state, tiles, LANE), lambda s, b: (0, 0, 0)),
            pl.BlockSpec(picks.shape, lambda s, b: (0, 0)),
        ],
        out_specs=[
            rows_spec,
            rows_spec,
            pl.BlockSpec((n_state, tiles, LANE), lambda s, b: (0, 0, 0)),
            pl.BlockSpec((groups * SUB, 2 * n_state, LANE), lambda s, b: (at(s, b), 0, 0)),
        ],
        out_shape=[
            jax.ShapeDtypeStruct(step.shape, jnp.float32),
            jax.ShapeDtypeStruct(step.shape, jnp.float32),
            jax.ShapeDtypeStruct(rate.shape, jnp.float32),
            jax.ShapeDtypeStruct((tokens, 2 * n_state, LANE), jnp.float32),
        ],
        scratch_shapes=[pltpu.VMEM((n_state, tiles, LANE), jnp.float32)] + [held] * 5,
        compiler_params=pltpu.CompilerParams(vmem_limit_bytes=32 * 2**20),
    )(end_grad, prior, step, inputs, ograd, b_rows, c_rows, rate, picks)


def from_earlier(ends, decay, steps):
    count = lax.axis_size("ctx")
    if count == 1:
        return jnp.zeros_like(ends)
    if count == 2:
        return passed_along(ends, "ctx", steps)
    index = lax.axis_index("ctx")
    all_ends = lax.all_gather(ends, "ctx")
    all_decays = lax.all_gather(decay, "ctx")

    def one(turn, state):
        at = turn if steps > 0 else count - 1 - turn
        reached = at < index if steps > 0 else at > index
        return jnp.where(reached, all_decays[at] * state + all_ends[at], state)

    return lax.fori_loop(0, count, one, jnp.zeros_like(ends))


def gathered_rows(rows):
    return lax.all_gather(rows, PLANE, axis=0, tiled=True)


def swapped_columns(rows):
    return lax.all_to_all(rows, PLANE, split_axis=1, concat_axis=0, tiled=True)


def place_in(axes):
    index = 0
    for axis in axes:
        index = index * lax.axis_size(axis) + lax.axis_index(axis)
    return index


def device_at(axes, index):
    where = {}
    for axis in reversed(axes):
        size = lax.axis_size(axis)
        where[axis] = lax.rem(index, size)
        index = lax.div(index, size)
    return where


def greet(groups):
    barrier = pltpu.get_barrier_semaphore()
    total = 0
    for axes, others in groups:
        for other in others:
            pl.semaphore_signal(
                barrier,
                inc=1,
                device_id=device_at(axes, other),
                device_id_type=pl.DeviceIdType.MESH,
            )
            total += 1
    pl.semaphore_wait(barrier, total)


def sent(source, target, send_sem, recv_sem, where):
    copy = pltpu.make_async_remote_copy(
        src_ref=source,
        dst_ref=target,
        send_sem=send_sem,
        recv_sem=recv_sem,
        device_id=where,
        device_id_type=pl.DeviceIdType.MESH,
    )
    copy.start()
    return copy


def finish(copies):
    for copy in copies:
        copy.wait()


def rows_of(ref, index, count):
    rows = ref.shape[0] // count
    return ref.at[pl.ds(pl.multiple_of(index * rows, rows), rows), :]


class Group:
    def __init__(self, axes, send_sem, recv_sem):
        self.axes = axes
        self.count = math.prod(lax.axis_size(axis) for axis in axes)
        self.me = place_in(axes)
        self.others = [lax.rem(self.me + hop, self.count) for hop in range(1, self.count)]
        self.send_sem, self.recv_sem = send_sem, recv_sem

    def own(self, ref):
        return rows_of(ref, self.me, self.count)

    def one(self, source, target, which, hop):
        return sent(
            source,
            target,
            self.send_sem.at[which, hop],
            self.recv_sem.at[which, hop],
            device_at(self.axes, self.others[hop]),
        )

    def scatter(self, part, slot, which):
        return [
            self.one(rows_of(part, other, self.count), slot.at[hop], which, hop)
            for hop, other in enumerate(self.others)
        ]

    def total(self, part, slot):
        total = self.own(part)[...].astype(jnp.float32)
        for hop in range(self.count - 1):
            total = total + slot[hop].astype(jnp.float32)
        return total

    def spread(self, ref, which):
        return [self.one(self.own(ref), self.own(ref), which, hop) for hop in range(self.count - 1)]


def exchange_kernel(axes, counts, kinds, middle, *refs):
    n_parts, n_whole, n_own = counts
    parts, refs = refs[:n_parts], refs[n_parts:]
    whole, refs = refs[:n_whole], refs[n_whole:]
    own, refs = refs[:n_own], refs[n_own:]
    outs, refs = refs[: len(kinds)], refs[len(kinds) :]
    slots, refs = refs[:n_parts], refs[n_parts:]
    group = Group(axes, *refs)
    greet([(axes, group.others)])
    copies = []
    for which, (part, slot) in enumerate(zip(parts, slots)):
        copies += group.scatter(part, slot, which)
    finish(copies)
    sums = [group.total(part, slot) for part, slot in zip(parts, slots)]
    results = middle(sums, [group.own(ref)[...] for ref in whole], [ref[...] for ref in own])
    copies = []
    for which, (ref, kind, value) in enumerate(zip(outs, kinds, results)):
        if kind == "rows":
            ref[...] = value.astype(ref.dtype)
        else:
            group.own(ref)[...] = value.astype(ref.dtype)
            copies += group.spread(ref, n_parts + which)
    finish(copies)


def slots_for(part, count):
    return pltpu.VMEM((count - 1, part.shape[0] // count) + part.shape[1:], part.dtype)


def group_size(axes):
    return math.prod(lax.axis_size(axis) for axis in axes)


def exchange(axes, call_id, parts, whole, own, middle, outs):
    count = group_size(axes)
    vmem = pl.BlockSpec(memory_space=pltpu.VMEM)
    sems = pltpu.SemaphoreType.DMA((len(parts) + len(outs), count - 1))
    return pl.pallas_call(
        functools.partial(
            exchange_kernel,
            axes,
            (len(parts), len(whole), len(own)),
            [kind for kind, _, _ in outs],
            middle,
        ),
        in_specs=[vmem] * (len(parts) + len(whole) + len(own)),
        out_specs=[vmem] * len(outs),
        out_shape=[jax.ShapeDtypeStruct(shape, dtype) for _, shape, dtype in outs],
        scratch_shapes=[slots_for(part, count) for part in parts] + [sems, sems],
        compiler_params=pltpu.CompilerParams(
            collective_id=call_id, has_side_effects=True, vmem_limit_bytes=40 * 2**20
        ),
    )(*parts, *whole, *own)


class PlaneGather:
    def __init__(self, own, gathered, send_sem, recv_sem):
        self.own, self.gathered = own, gathered
        self.send_sem, self.recv_sem = send_sem, recv_sem
        self.dp, self.ctx = lax.axis_index("dp"), lax.axis_index("ctx")
        self.n_dp, self.n_ctx = lax.axis_size("dp"), lax.axis_size("ctx")
        self.hands_on = relayed()
        self.count = self.n_dp * self.n_ctx
        self.me = self.dp * self.n_ctx + self.ctx
        self.others = [lax.rem(self.me + hop, self.count) for hop in range(1, self.count)]
        self.copies = {}
        if self.hands_on:
            core = lax.rem(self.dp, 2)
            over_core = self.dp + 1 - 2 * core
            over_y = lax.rem(self.dp + 2, 4)
            over_x = 1 - self.ctx
            self.core = {"dp": over_core, "ctx": self.ctx}
            self.at_x = {"dp": self.dp, "ctx": over_x}
            self.at_y = {"dp": over_y, "ctx": self.ctx}
            self.from_x = self.dp * 2 + over_x
            self.from_y = over_y * 2 + self.ctx
            self.across = over_y * 2 + over_x

    def part(self, owner, half):
        rows = self.gathered.shape[0] // self.count
        start, size = owner * rows, rows
        if half is not None:
            size = rows // 2
            start = start + half * size
        return self.gathered.at[pl.ds(pl.multiple_of(start, size), size), :]

    def send(self, which, owner, half, where):
        target = self.part(owner, half)
        source = target
        if owner is self.me:
            rows = self.own.shape[0]
            source = self.own
            if half is not None:
                source = self.own.at[pl.ds(half * (rows // 2), rows // 2), :]
        self.copies[which] = sent(
            source, target, self.send_sem.at[which], self.recv_sem.at[which], where
        )

    def arrived(self, *which):
        for one in which:
            self.copies[one].wait_recv()

    def begin(self, local_sem):
        self.local = pltpu.make_async_copy(self.own, self.part(self.me, None), local_sem)
        self.local.start()
        if not self.hands_on:
            for hop, other in enumerate(self.others):
                self.send(hop, self.me, None, device_at(PLANE, other))
            return
        self.send(0, self.me, 1, self.at_x)
        self.send(1, self.me, 0, self.at_y)
        self.send(2, self.me, None, self.core)
        self.send(3, self.me, 0, self.at_x)
        self.send(4, self.me, 1, self.at_y)

    def relay(self):
        if not self.hands_on:
            return
        self.arrived(0, 1)
        self.send(5, self.from_x, 1, self.at_y)
        self.send(6, self.from_y, 0, self.at_x)
        self.send(7, self.from_x, 1, self.core)
        self.send(8, self.from_y, 0, self.core)

    def hand_over(self):
        if not self.hands_on:
            return
        self.arrived(3, 4)
        self.send(9, self.from_x, 0, self.core)
        self.send(10, self.from_y, 1, self.core)

    def hand_over_last(self):
        if not self.hands_on:
            return
        self.arrived(5, 6)
        self.send(11, self.across, 1, self.core)
        self.send(12, self.across, 0, self.core)

    def end(self):
        if self.hands_on:
            self.arrived(2, 7, 8, 9, 10, 11, 12)
        else:
            self.arrived(*range(self.count - 1))
        for copy in self.copies.values():
            copy.wait_send()
        self.local.wait()


def relayed():
    return lax.axis_size("dp") == 4 and lax.axis_size("ctx") == 2


def gather_sems():
    count = 13 if relayed() else group_size(PLANE) - 1
    return pltpu.SemaphoreType.DMA((count,))


WIDE = 512


def products(source, first, last, dot, target, block_buf, block_sem, out_buf, out_sem):
    def fetch(j, slot):
        columns = pl.ds(pl.multiple_of(j * WIDE, WIDE), WIDE)
        return pltpu.make_async_copy(
            source.at[:, columns], block_buf.at[slot], block_sem.at[slot]
        )

    def store(j, slot):
        return pltpu.make_async_copy(out_buf.at[slot], target(j), out_sem.at[slot])

    fetch(first, first % 2).start()

    @pl.loop(first, last)
    def _(j):
        slot = lax.rem(j, 2)

        @pl.when(j + 1 < last)
        def _():
            fetch(j + 1, 1 - slot).start()

        fetch(j, slot).wait()

        @pl.when(j >= first + 2)
        def _():
            store(j - 2, slot).wait()

        out_buf[slot] = dot(block_buf[slot])
        store(j, slot).start()

    for j in range(max(first, last - 2), last):
        store(j, j % 2).wait()


def tail_kernel(
    sizes,
    mix_grads,
    normed_part,
    ffn_part,
    small,
    tokens,
    middle_rows,
    middle_grad,
    gain_row,
    one_cols,
    two_cols,
    ct_cols,
    middle_cols,
    ffn_all,
    tokens_grad,
    layer_out,
    small_sum,
    gains,
    mix_all,
    grad_inproj,
    grad_outproj,
    grad_gateup,
    grad_downproj,
    normed_slots,
    ffn_slots,
    small_slots,
    gain_slots,
    gain_own,
    block_buf,
    wide_buf,
    tall_buf,
    block_sem,
    wide_sem,
    tall_sem,
    tp_send,
    tp_recv,
    plane_send,
    plane_recv,
    gather_send,
    gather_recv,
    local_sem,
):
    inner, hidden, gain_at = sizes
    tp = Group(("tp",), tp_send, tp_recv)
    plane = Group(PLANE, plane_send, plane_recv)
    gather = PlaneGather(mix_grads, mix_all, gather_send, gather_recv)
    greet([(("tp",), tp.others), (PLANE, plane.others)])

    def flat(lhs):
        return lambda block: lax.dot_general(
            lhs[...], block, (((0,), (0,)), ((), ())), preferred_element_type=jnp.float32
        )

    def tall(rhs):
        return lambda block: lax.dot_general(
            block, rhs[...], (((0,), (0,)), ((), ())), preferred_element_type=jnp.float32
        )

    def side_by_side(ref, first):
        per = ref.shape[2] // WIDE

        def target(j):
            at = j - first
            columns = pl.ds(pl.multiple_of(lax.rem(at, per) * WIDE, WIDE), WIDE)
            return ref.at[lax.div(at, per), :, columns]

        return target

    def one_above_other(ref, first):
        return lambda j: ref.at[pl.ds(pl.multiple_of((j - first) * WIDE, WIDE), WIDE), :]

    wide = (block_buf, block_sem, wide_buf, wide_sem)
    high = (block_buf, block_sem, tall_buf, tall_sem)
    down_end = hidden // WIDE
    gu_end = 3 * hidden // WIDE
    out_end = gu_end + inner // WIDE

    normed_sent = tp.scatter(normed_part, normed_slots, 0)
    gather.begin(local_sem)
    ffn_sent = tp.scatter(ffn_part, ffn_slots, 1)
    small_sent = plane.scatter(small, small_slots, 0)
    products(
        ffn_all, down_end, gu_end, flat(two_cols), side_by_side(grad_gateup, down_end), *wide
    )
    gather.relay()
    products(ffn_all, 0, down_end, tall(ct_cols), one_above_other(grad_downproj, 0), *high)
    gather.hand_over()
    finish(normed_sent)
    hidden_in = tp.own(tokens)[...].astype(jnp.float32)
    tp.own(tokens_grad)[...] = (
        middle_grad[...]
        + norm_back(
            tp.total(normed_part, normed_slots),
            hidden_in,
            inverse_rms(hidden_in),
            gain_row[...].astype(jnp.float32),
        )
    ).astype(tokens_grad.dtype)
    tokens_sent = tp.spread(tokens_grad, 2)
    finish(small_sent)
    plane.own(small_sum)[...] = plane.total(small, small_slots).astype(small_sum.dtype)
    small_sent = plane.spread(small_sum, 1)
    products(
        ffn_all, gu_end, out_end, tall(middle_cols), one_above_other(grad_outproj, gu_end), *high
    )
    gather.hand_over_last()
    finish(ffn_sent)
    tp.own(layer_out)[...] = (middle_rows[...] + tp.total(ffn_part, ffn_slots)).astype(
        layer_out.dtype
    )
    layer_sent = tp.spread(layer_out, 3)
    finish(small_sent)
    gain_own[...] = small_sum[pl.ds(gain_at, gain_own.shape[0]), :].astype(jnp.float32)
    gain_sent = [tp.one(gain_own, gain_slots.at[hop], 4, hop) for hop in range(tp.count - 1)]
    gather.end()
    products(
        mix_all, 0, 2 * inner // WIDE, flat(one_cols), side_by_side(grad_inproj, 0), *wide
    )
    finish(gain_sent)
    total = gain_own[...]
    for hop in range(tp.count - 1):
        total = total + gain_slots[hop]
    gains[...] = total
    finish(tokens_sent)
    finish(layer_sent)


def run_tail(
    call_id,
    gain_at,
    mix_grads,
    normed_part,
    ffn_part,
    small,
    tokens,
    middle_rows,
    middle_grad,
    gain_row,
    one_cols,
    two_cols,
    ct_cols,
    middle_cols,
    ffn_all,
):
    inner = mix_grads.shape[1] // 2
    hidden = (ffn_all.shape[1] - inner) // 3
    share = one_cols.shape[1]
    all_rows = ffn_all.shape[0]
    tp_count, plane_count = group_size(("tp",)), group_size(PLANE)
    low, full = jnp.bfloat16, jnp.float32
    vmem = pl.BlockSpec(memory_space=pltpu.VMEM)
    hbm = pl.BlockSpec(memory_space=pl.ANY)
    gain_rows = 16
    dma = pltpu.SemaphoreType.DMA
    return pl.pallas_call(
        functools.partial(tail_kernel, (inner, hidden, gain_at)),
        in_specs=[vmem] * 12 + [hbm],
        out_specs=[vmem] * 4 + [hbm] * 5,
        out_shape=[
            jax.ShapeDtypeStruct(tokens.shape, low),
            jax.ShapeDtypeStruct(tokens.shape, low),
            jax.ShapeDtypeStruct(small.shape, low),
            jax.ShapeDtypeStruct((gain_rows, inner), full),
            jax.ShapeDtypeStruct((all_rows, 2 * inner), low),
            jax.ShapeDtypeStruct((2, share, inner), full),
            jax.ShapeDtypeStruct((inner, share), full),
            jax.ShapeDtypeStruct((2, share, hidden), full),
            jax.ShapeDtypeStruct((hidden, share), full),
        ],
        scratch_shapes=[
            slots_for(normed_part, tp_count),
            slots_for(ffn_part, tp_count),
            slots_for(small, plane_count),
            pltpu.VMEM((tp_count - 1, gain_rows, inner), full),
            pltpu.VMEM((gain_rows, inner), full),
            pltpu.VMEM((2, all_rows, WIDE), low),
            pltpu.VMEM((2, share, WIDE), full),
            pltpu.VMEM((2, WIDE, share), full),
            dma((2,)),
            dma((2,)),
            dma((2,)),
            dma((5, tp_count - 1)),
            dma((5, tp_count - 1)),
            dma((2, plane_count - 1)),
            dma((2, plane_count - 1)),
            gather_sems(),
            gather_sems(),
            dma(()),
        ],
        compiler_params=pltpu.CompilerParams(
            collective_id=call_id, has_side_effects=True, vmem_limit_bytes=56 * 2**20
        ),
    )(
        mix_grads,
        normed_part,
        ffn_part,
        small,
        tokens,
        middle_rows,
        middle_grad,
        gain_row,
        one_cols,
        two_cols,
        ct_cols,
        middle_cols,
        ffn_all,
    )


def after_mixer(sums, whole, own):
    (mixed,), (tokens_in,), (gain,) = sums, whole, own
    middle = tokens_in.astype(jnp.float32) + mixed
    return middle * inverse_rms(middle) * gain.astype(jnp.float32), middle


def after_ffn_back(sums, whole, own):
    (normed_grad,), (ct,), (middle, gain) = sums, whole, own
    scale = inverse_rms(middle)
    gain_grad = jnp.sum(normed_grad * middle * scale, 0, keepdims=True)
    middle_grad = ct.astype(jnp.float32) + norm_back(
        normed_grad, middle, scale, gain.astype(jnp.float32)
    )
    return middle_grad, middle_grad, gain_grad


def as_they_are(sums, whole, own):
    return sums


def per_device(
    tokens,
    mixgain,
    inproj,
    convkern,
    convbias,
    selproj,
    stepproj,
    stepbias,
    decaylog,
    skipgain,
    outproj,
    ffngain,
    gateup,
    downproj,
    cotangent,
):
    seqs, span, width = tokens.shape
    rows = seqs * span
    taps, inner = convkern.shape
    rank = stepproj.shape[0]
    n_state = decaylog.shape[1]
    tiles = inner // LANE
    gain_mix = mixgain.astype(jnp.float32)
    kernel = convkern.astype(jnp.float32)
    kernel_bias = convbias.astype(jnp.float32)
    step_bias = stepbias.astype(jnp.float32)
    skip_weight = skipgain.astype(jnp.float32)
    decay_rate = -jnp.exp(jnp.transpose(decaylog.astype(jnp.float32)))
    rate = (decay_rate * LOG2E).reshape(n_state, tiles, LANE)

    gain_mix_row, gain_ffn_row = mixgain.reshape(1, width), ffngain.reshape(1, width)
    own_rows = rows // lax.axis_size("tp")
    hidden = gateup.shape[2]
    low = jnp.bfloat16

    mix_pack = gathered_rows(
        jnp.concatenate([inproj[0], inproj[1], jnp.transpose(outproj)], 1)
    )
    ffn_pack = gathered_rows(
        jnp.concatenate([gateup[0], gateup[1], jnp.transpose(downproj)], 1)
    )

    tokens_rows = tokens.reshape(rows, width)
    hidden_in = tokens_rows.astype(jnp.float32)
    scale_one = inverse_rms(hidden_in)
    normed_one = (hidden_in * scale_one * gain_mix).astype(low)
    ct_low = cotangent.reshape(rows, width)
    normed_one_cols, ct_cols = swapped_columns(normed_one), swapped_columns(ct_low)
    normed_one, normed_one_cols, ct_cols = lax.optimization_barrier(
        (normed_one, normed_one_cols, ct_cols)
    )
    conv_in = matmul(normed_one, mix_pack[:, :inner]).astype(low)
    gate_mix = matmul(normed_one, mix_pack[:, inner : 2 * inner])
    conv_seqs = conv_in.reshape(seqs, span, inner)
    rim_rows = passed_along(conv_seqs[:, span - (taps - 1) :], "ctx", 1)
    padded_in = jnp.concatenate([rim_rows, conv_seqs], 1).astype(jnp.float32)
    conv_out = kernel_bias[None, None]
    for offset in range(taps):
        conv_out = conv_out + kernel[offset][None, None] * padded_in[:, offset : offset + span]
    conv_out = conv_out.reshape(rows, inner)
    scan_in = jax.nn.silu(conv_out).astype(low)
    scan_float = scan_in.astype(jnp.float32)
    columns = selproj.shape[1]
    select_width = -(-columns // LANE) * LANE
    select_weights = jnp.pad(selproj, ((0, 0), (0, select_width - columns)))
    (select_cols,) = exchange(
        ("tp",),
        0,
        [matmul(scan_in, select_weights)],
        [],
        [],
        as_they_are,
        [("all", (rows, select_width), jnp.float32)],
    )
    step_low = select_cols[:, :rank].astype(low)
    b_rows = select_cols[:, rank : rank + n_state].reshape(-1)
    c_rows = select_cols[:, rank + n_state : columns].reshape(-1)
    step_pre = matmul(step_low, stepproj) + step_bias[None]
    step_size = jax.nn.softplus(step_pre)
    span_decay = jnp.exp(
        decay_rate[None] * jnp.sum(step_size.reshape(seqs, span, inner), 1)[:, None]
    ).reshape(seqs, n_state, tiles, LANE)
    ends = scan_ends(step_size, scan_float, b_rows, rate, seqs, False)
    start = from_earlier(ends, span_decay, 1)
    prior, scan_out = scan_forward(start, step_size, scan_float, b_rows, c_rows, rate, seqs)
    mixer_core = scan_out + skip_weight[None] * scan_float
    gate_sig = jax.nn.silu(gate_mix)
    gated = (mixer_core * gate_sig).astype(low)
    out_weights = mix_pack[:, 2 * inner :]
    normed_two, middle = exchange(
        ("tp",),
        1,
        [matmul_nt(gated, out_weights).astype(low)],
        [tokens_rows],
        [gain_ffn_row],
        after_mixer,
        [("all", (rows, width), low), ("rows", (own_rows, width), jnp.float32)],
    )
    normed_two_cols = swapped_columns(normed_two)
    gate_up = ffn_pack[:, : 2 * hidden]
    down_weights = ffn_pack[:, 2 * hidden :]
    both_ffn = matmul(normed_two, gate_up)
    gate_ffn, up_ffn = both_ffn[:, :hidden], both_ffn[:, hidden:]
    activated = (jax.nn.silu(gate_ffn) * up_ffn).astype(low)
    act_grad = matmul(ct_low, down_weights)
    gate_grad = (act_grad * up_ffn * silu_slope(gate_ffn)).astype(low)
    up_grad = (act_grad * jax.nn.silu(gate_ffn)).astype(low)
    ffn_grads = jnp.concatenate([gate_grad, up_grad], 1)
    ffn_sent, ffn_grads = lax.optimization_barrier(
        (jnp.concatenate([activated, ffn_grads, gated], 1), ffn_grads)
    )
    ffn_all = gathered_rows(ffn_sent)
    normed_two_part = matmul_nt(ffn_grads, gate_up).astype(low)
    normed_two_part, normed_two_cols = lax.optimization_barrier((normed_two_part, normed_two_cols))
    ffn_part = matmul_nt(activated, down_weights).astype(low)
    middle_low, middle_grad, ffngain_part = exchange(
        ("tp",),
        2,
        [normed_two_part],
        [ct_low],
        [middle, gain_ffn_row],
        after_ffn_back,
        [
            ("all", (rows, width), low),
            ("rows", (own_rows, width), jnp.float32),
            ("rows", (1, width), jnp.float32),
        ],
    )
    middle_cols = swapped_columns(middle_low)
    gated_grad = matmul(middle_low, out_weights)
    core_grad = gated_grad * gate_sig
    gate_mix_grad = (gated_grad * mixer_core * silu_slope(gate_mix)).astype(low)
    grad_skipgain = jnp.sum(core_grad * scan_float, 0)
    back_ends = scan_ends(step_size, core_grad, c_rows, rate, seqs, True)
    end_grad = from_earlier(back_ends, span_decay, -1)
    end_grad, middle_cols = lax.optimization_barrier((end_grad, middle_cols))
    step_grad, input_grad, rate_grad, parts = scan_backward(
        end_grad, prior, step_size, scan_float, core_grad, b_rows, c_rows, rate, seqs
    )
    grad_decaylog = rate_grad.reshape(n_state, inner) * decay_rate
    pre_grad = step_grad * jax.nn.sigmoid(step_pre)
    grad_stepbias = jnp.sum(pre_grad, 0)
    pre_low = pre_grad.astype(low)
    grad_stepproj = matmul_tn(step_low, pre_low)
    select_part = jnp.concatenate(
        [
            matmul_nt(pre_low, stepproj),
            jnp.sum(parts, -1),
            jnp.zeros((rows, select_width - columns), jnp.float32),
        ],
        1,
    ).astype(low)
    (select_low,) = exchange(
        ("tp",),
        3,
        [select_part],
        [],
        [],
        as_they_are,
        [("all", (rows, select_width), low)],
    )
    grad_selproj = matmul_tn(select_low, scan_in)
    scan_in_grad = (
        core_grad * skip_weight[None]
        + input_grad
        + matmul_nt(select_low, select_weights)
    )
    conv_grad = scan_in_grad * silu_slope(conv_out)
    grad_convbias = jnp.sum(conv_grad, 0)
    conv_grad_seqs = conv_grad.reshape(seqs, span, inner)
    padded_grad = jnp.zeros(padded_in.shape, jnp.float32)
    kernel_rows = []
    for offset in range(taps):
        kernel_rows.append(jnp.sum(conv_grad_seqs * padded_in[:, offset : offset + span], (0, 1)))
        padded_grad = padded_grad + jnp.pad(
            kernel[offset][None, None] * conv_grad_seqs,
            ((0, 0), (offset, taps - 1 - offset), (0, 0)),
        )
    grad_convkern = jnp.stack(kernel_rows)
    returned = passed_along(padded_grad[:, : taps - 1], "ctx", -1)
    conv_in_grad = (
        (padded_grad[:, taps - 1 :] + jnp.pad(returned, ((0, 0), (span - taps + 1, 0), (0, 0))))
        .astype(low)
        .reshape(rows, inner)
    )
    mix_grads = jnp.concatenate([conv_in_grad, gate_mix_grad], 1)
    normed_one_part = matmul_nt(mix_grads, mix_pack[:, : 2 * inner])
    mixgain_part = jnp.sum(normed_one_part * hidden_in * scale_one, 0)
    normed_one_part = normed_one_part.astype(low)
    small = [
        grad_convkern,
        grad_convbias[None],
        grad_stepbias[None],
        grad_decaylog,
        grad_skipgain[None],
        grad_stepproj,
        grad_selproj[:columns],
        mixgain_part.reshape(-1, inner),
        ffngain_part.reshape(-1, inner),
    ]
    sizes = [part.shape[0] for part in small]
    gain_at = sum(sizes[:-2]) + -sum(sizes[:-2]) % 16
    small.insert(-2, jnp.zeros((gain_at - sum(sizes[:-2]), inner), jnp.float32))
    small = jnp.concatenate(small, 0).astype(low)
    share = 16 * group_size(PLANE)
    small = jnp.pad(small, ((0, -(gain_at + 16) % share + 16 - sum(sizes[-2:])), (0, 0)))
    (
        tokens_grad,
        layer_out,
        small,
        gains,
        _,
        grad_inproj,
        grad_outproj,
        grad_gateup,
        grad_downproj,
    ) = run_tail(
        4,
        gain_at,
        mix_grads,
        normed_one_part,
        ffn_part,
        small,
        tokens_rows,
        middle,
        middle_grad,
        gain_mix_row,
        normed_one_cols,
        normed_two_cols,
        ct_cols,
        middle_cols,
        ffn_all,
    )
    small = small.astype(jnp.float32)
    smalls, at = [], 0
    for size in sizes[:-2]:
        smalls.append(small[at : at + size])
        at += size
    gains = gains[: sum(sizes[-2:])].reshape(2, width)
    return (
        layer_out.reshape(tokens.shape),
        tokens_grad.reshape(tokens.shape),
        gains[0],
        grad_inproj,
        smalls[0],
        smalls[1][0],
        jnp.transpose(smalls[6]),
        smalls[5],
        smalls[2][0],
        jnp.transpose(smalls[3]),
        smalls[4][0],
        grad_outproj,
        gains[1],
        grad_gateup,
        grad_downproj,
    )


def solution(mesh):
    in_specs = (
        P("dp", "ctx", None),
        P(),
        P(None, ("dp", "ctx"), "tp"),
        P(None, "tp"),
        P("tp"),
        P("tp", None),
        P(None, "tp"),
        P("tp"),
        P("tp", None),
        P("tp"),
        P("tp", ("dp", "ctx")),
        P(),
        P(None, ("dp", "ctx"), "tp"),
        P("tp", ("dp", "ctx")),
        P("dp", "ctx", None),
    )
    out_specs = (
        P("dp", "ctx", None),
        P("dp", "ctx", None),
        P(),
        P(None, ("dp", "ctx"), "tp"),
        P(None, "tp"),
        P("tp"),
        P("tp", None),
        P(None, "tp"),
        P("tp"),
        P("tp", None),
        P("tp"),
        P("tp", ("dp", "ctx")),
        P(),
        P(None, ("dp", "ctx"), "tp"),
        P("tp", ("dp", "ctx")),
    )
    return jax.shard_map(
        per_device, mesh=mesh, in_specs=in_specs, out_specs=out_specs, check_vma=False
    )
```

```python
import functools
import math

import jax
import jax.numpy as jnp
from jax import lax
from jax.experimental import pallas as pl
from jax.experimental.pallas import tpu as pltpu
from jax.sharding import PartitionSpec as P

EPSILON = 1e-05
LOG2E = math.log2(math.e)
LN2 = math.log(2.0)
SUB = 8
LANE = 128
PLANE = ("dp", "ctx")


def passed_along(value, axis, steps):
    count = lax.axis_size(axis)
    first, last = (max(0, -steps), min(count, count - steps))
    return lax.ppermute(value, axis, [(source, source + steps) for source in range(first, last)])


def matmul(left, right):
    return jnp.dot(left, right, preferred_element_type=jnp.float32)


def matmul_nt(left, right):
    return lax.dot_general(
        left, right, (((1,), (1,)), ((), ())), preferred_element_type=jnp.float32
    )


def matmul_tn(left, right):
    return lax.dot_general(
        left, right, (((0,), (0,)), ((), ())), preferred_element_type=jnp.float32
    )


def inverse_rms(values):
    return lax.rsqrt(jnp.mean(values * values, -1, keepdims=True) + EPSILON)


def silu_slope(values):
    logistic = jax.nn.sigmoid(values)
    return logistic * (1.0 + values * (1.0 - logistic))


def norm_back(grad_norm, values, scale, gain):
    scaled_grad = grad_norm * gain
    unit_rows = values * scale
    return scale * (scaled_grad - unit_rows * jnp.mean(scaled_grad * unit_rows, -1, keepdims=True))


def stage_in(ref, group, held):
    for tile in range(held.shape[0] // SUB):
        held[pl.ds(tile * SUB, SUB), :] = ref[
            pl.ds(pl.multiple_of(group * SUB, SUB), SUB), pl.ds(tile * LANE, LANE)
        ]


def stage_out(held, ref, group):
    for tile in range(held.shape[0] // SUB):
        ref[pl.ds(pl.multiple_of(group * SUB, SUB), SUB), pl.ds(tile * LANE, LANE)] = held[
            pl.ds(tile * SUB, SUB), :
        ]


def token_row(held, at, tiles):
    return held[pl.ds(at, tiles, stride=SUB), :]


def ends_kernel(
    n_state,
    tiles,
    groups,
    reverse,
    step_ref,
    drive_ref,
    rows_ref,
    rate_ref,
    end_ref,
    step_held,
    drive_held,
):
    base = pl.program_id(0) * groups * SUB * n_state
    rates = [rate_ref[n] for n in range(n_state)]

    def one(turn, states):
        group = groups - 1 - turn if reverse else turn
        order = range(SUB - 1, -1, -1) if reverse else range(SUB)
        states = list(states)
        stage_in(step_ref, group, step_held)
        stage_in(drive_ref, group, drive_held)
        for at in order:
            step = token_row(step_held, at, tiles)
            drive = token_row(drive_held, at, tiles)
            if not reverse:
                drive = drive * step
            for n in range(n_state):
                row = rows_ref[base + (group * SUB + at) * n_state + n]
                decay = jnp.exp2(step * rates[n])
                if reverse:
                    states[n] = decay * (states[n] + drive * row)
                else:
                    states[n] = decay * states[n] + drive * row
        return tuple(states)

    zero = jnp.zeros((tiles, LANE), jnp.float32)
    states = lax.fori_loop(0, groups, one, (zero,) * n_state)
    for n in range(n_state):
        end_ref[0, n] = states[n]


def scan_ends(step, drive, rows, rate, seqs, reverse):
    n_state, tiles, _ = rate.shape
    groups = step.shape[0] // seqs // SUB
    rows_spec = pl.BlockSpec((groups * SUB, tiles * LANE), lambda s: (s, 0))
    held = pltpu.VMEM((tiles * SUB, LANE), jnp.float32)
    return pl.pallas_call(
        functools.partial(ends_kernel, n_state, tiles, groups, reverse),
        grid=(seqs,),
        in_specs=[
            rows_spec,
            rows_spec,
            pl.BlockSpec(memory_space=pltpu.SMEM),
            pl.BlockSpec((n_state, tiles, LANE), lambda s: (0, 0, 0)),
        ],
        out_specs=pl.BlockSpec((1, n_state, tiles, LANE), lambda s: (s, 0, 0, 0)),
        out_shape=jax.ShapeDtypeStruct((seqs, n_state, tiles, LANE), jnp.float32),
        scratch_shapes=[held, held],
        compiler_params=pltpu.CompilerParams(vmem_limit_bytes=32 * 2**20),
    )(step, drive, rows, rate)


def forward_kernel(
    n_state,
    tiles,
    groups,
    blocks,
    start_ref,
    step_ref,
    input_ref,
    brow_ref,
    crow_ref,
    rate_ref,
    prior_ref,
    mixed_ref,
    carried,
    step_held,
    input_held,
    mixed_held,
):
    base = (pl.program_id(0) * blocks + pl.program_id(1)) * groups * SUB * n_state

    @pl.when(pl.program_id(1) == 0)
    def _():
        carried[...] = start_ref[0]

    def one(group, states):
        states = list(states)
        stage_in(step_ref, group, step_held)
        stage_in(input_ref, group, input_held)
        for at in range(SUB):
            step = token_row(step_held, at, tiles)
            drive = step * token_row(input_held, at, tiles)
            mixed = [None] * 2
            for n in range(n_state):
                where = base + (group * SUB + at) * n_state + n
                prior_ref[group * SUB + at, n] = states[n]
                decay = jnp.exp2(step * rate_ref[n])
                states[n] = decay * states[n] + drive * brow_ref[where]
                term = states[n] * crow_ref[where]
                mixed[n % 2] = term if mixed[n % 2] is None else mixed[n % 2] + term
            mixed_held[pl.ds(at, tiles, stride=SUB), :] = mixed[0] + mixed[1]
        stage_out(mixed_held, mixed_ref, group)
        return tuple(states)

    states = lax.fori_loop(0, groups, one, tuple(carried[n] for n in range(n_state)))
    for n in range(n_state):
        carried[n] = states[n]


def scan_forward(start, step, inputs, b_rows, c_rows, rate, seqs):
    n_state, tiles, _ = rate.shape
    all_groups = step.shape[0] // SUB
    groups = math.gcd(all_groups // seqs, 4)
    blocks = all_groups // seqs // groups
    rows_spec = pl.BlockSpec((groups * SUB, tiles * LANE), lambda s, b: (s * blocks + b, 0))
    held = pltpu.VMEM((tiles * SUB, LANE), jnp.float32)
    smem = pl.BlockSpec(memory_space=pltpu.SMEM)
    tokens = all_groups * SUB
    return pl.pallas_call(
        functools.partial(forward_kernel, n_state, tiles, groups, blocks),
        grid=(seqs, blocks),
        in_specs=[
            pl.BlockSpec((1, n_state, tiles, LANE), lambda s, b: (s, 0, 0, 0)),
            rows_spec,
            rows_spec,
            smem,
            smem,
            pl.BlockSpec((n_state, tiles, LANE), lambda s, b: (0, 0, 0)),
        ],
        out_specs=[
            pl.BlockSpec(
                (groups * SUB, n_state, tiles, LANE), lambda s, b: (s * blocks + b, 0, 0, 0)
            ),
            rows_spec,
        ],
        out_shape=[
            jax.ShapeDtypeStruct((tokens, n_state, tiles, LANE), jnp.float32),
            jax.ShapeDtypeStruct(step.shape, jnp.float32),
        ],
        scratch_shapes=[pltpu.VMEM((n_state, tiles, LANE), jnp.float32)] + [held] * 3,
        compiler_params=pltpu.CompilerParams(vmem_limit_bytes=32 * 2**20),
    )(start, step, inputs, b_rows, c_rows, rate)


def backward_kernel(
    n_state,
    tiles,
    groups,
    blocks,
    end_ref,
    prior_ref,
    step_ref,
    input_ref,
    ograd_ref,
    brow_ref,
    crow_ref,
    rate_ref,
    picks_ref,
    step_grad_ref,
    input_grad_ref,
    rate_grad_ref,
    part_ref,
    carried,
    step_held,
    input_held,
    ograd_held,
    step_grad_held,
    input_grad_held,
):
    block = blocks - 1 - pl.program_id(1)
    base = (pl.program_id(0) * blocks + block) * groups * SUB * n_state

    @pl.when(pl.program_id(1) == 0)
    def _():
        carried[...] = end_ref[0]

    @pl.when((pl.program_id(0) == 0) & (pl.program_id(1) == 0))
    def _():
        rate_grad_ref[...] = jnp.zeros_like(rate_grad_ref)

    def one(turn, grads):
        group = groups - 1 - turn
        grads = list(grads)
        stage_in(step_ref, group, step_held)
        stage_in(input_ref, group, input_held)
        stage_in(ograd_ref, group, ograd_held)
        for at in range(SUB - 1, -1, -1):
            step = token_row(step_held, at, tiles)
            value = token_row(input_held, at, tiles)
            ograd = token_row(ograd_held, at, tiles)
            drive = step * value
            along_b = None
            along_rate = None
            brow_parts, crow_parts = [], []
            for n in range(n_state):
                where = base + (group * SUB + at) * n_state + n
                brow, crow = brow_ref[where], crow_ref[where]
                rate = rate_ref[n]
                decay = jnp.exp2(step * rate)
                grad = ograd * crow + grads[n]
                kept = decay * prior_ref[group * SUB + at, n]
                state = kept + drive * brow
                decay_term = grad * kept
                grads[n] = decay * grad
                rate_grad_ref[n] += decay_term * step
                by_rate, by_brow = decay_term * rate, grad * brow
                along_rate = by_rate if along_rate is None else along_rate + by_rate
                along_b = by_brow if along_b is None else along_b + by_brow
                brow_parts.append(grad * drive)
                crow_parts.append(ograd * state)
            step_grad_held[pl.ds(at, tiles, stride=SUB), :] = along_rate * LN2 + along_b * value
            input_grad_held[pl.ds(at, tiles, stride=SUB), :] = along_b * step
            parts = jnp.concatenate(brow_parts + crow_parts, 0).astype(jnp.bfloat16)
            part_ref[group * SUB + at] = jnp.dot(
                picks_ref[...], parts, preferred_element_type=jnp.float32
            )
        stage_out(step_grad_held, step_grad_ref, group)
        stage_out(input_grad_held, input_grad_ref, group)
        return tuple(grads)

    grads = lax.fori_loop(0, groups, one, tuple(carried[n] for n in range(n_state)))
    for n in range(n_state):
        carried[n] = grads[n]


def scan_backward(end_grad, prior, step, inputs, ograd, b_rows, c_rows, rate, seqs):
    n_state, tiles, _ = rate.shape
    all_groups = step.shape[0] // SUB
    groups = math.gcd(all_groups // seqs, 4)
    blocks = all_groups // seqs // groups

    def at(s, b):
        return s * blocks + blocks - 1 - b

    rows_spec = pl.BlockSpec((groups * SUB, tiles * LANE), lambda s, b: (at(s, b), 0))
    held = pltpu.VMEM((tiles * SUB, LANE), jnp.float32)
    smem = pl.BlockSpec(memory_space=pltpu.SMEM)
    tokens = all_groups * SUB
    picks = jnp.repeat(jnp.eye(2 * n_state, dtype=jnp.bfloat16), tiles, 1)
    return pl.pallas_call(
        functools.partial(backward_kernel, n_state, tiles, groups, blocks),
        grid=(seqs, blocks),
        in_specs=[
            pl.BlockSpec((1, n_state, tiles, LANE), lambda s, b: (s, 0, 0, 0)),
            pl.BlockSpec((groups * SUB, n_state, tiles, LANE), lambda s, b: (at(s, b), 0, 0, 0)),
            rows_spec,
            rows_spec,
            rows_spec,
            smem,
            smem,
            pl.BlockSpec((n_state, tiles, LANE), lambda s, b: (0, 0, 0)),
            pl.BlockSpec(picks.shape, lambda s, b: (0, 0)),
        ],
        out_specs=[
            rows_spec,
            rows_spec,
            pl.BlockSpec((n_state, tiles, LANE), lambda s, b: (0, 0, 0)),
            pl.BlockSpec((groups * SUB, 2 * n_state, LANE), lambda s, b: (at(s, b), 0, 0)),
        ],
        out_shape=[
            jax.ShapeDtypeStruct(step.shape, jnp.float32),
            jax.ShapeDtypeStruct(step.shape, jnp.float32),
            jax.ShapeDtypeStruct(rate.shape, jnp.float32),
            jax.ShapeDtypeStruct((tokens, 2 * n_state, LANE), jnp.float32),
        ],
        scratch_shapes=[pltpu.VMEM((n_state, tiles, LANE), jnp.float32)] + [held] * 5,
        compiler_params=pltpu.CompilerParams(vmem_limit_bytes=32 * 2**20),
    )(end_grad, prior, step, inputs, ograd, b_rows, c_rows, rate, picks)


def from_earlier(ends, decay, steps):
    count = lax.axis_size("ctx")
    if count == 1:
        return jnp.zeros_like(ends)
    if count == 2:
        return passed_along(ends, "ctx", steps)
    index = lax.axis_index("ctx")
    all_ends = lax.all_gather(ends, "ctx")
    all_decays = lax.all_gather(decay, "ctx")

    def one(turn, state):
        at = turn if steps > 0 else count - 1 - turn
        reached = at < index if steps > 0 else at > index
        return jnp.where(reached, all_decays[at] * state + all_ends[at], state)

    return lax.fori_loop(0, count, one, jnp.zeros_like(ends))


def gathered_rows(rows):
    return lax.all_gather(rows, PLANE, axis=0, tiled=True)


def swapped_columns(rows):
    return lax.all_to_all(rows, PLANE, split_axis=1, concat_axis=0, tiled=True)


def place_in(axes):
    index = 0
    for axis in axes:
        index = index * lax.axis_size(axis) + lax.axis_index(axis)
    return index


def device_at(axes, index):
    where = {}
    for axis in reversed(axes):
        size = lax.axis_size(axis)
        where[axis] = lax.rem(index, size)
        index = lax.div(index, size)
    return where


def greet(groups):
    barrier = pltpu.get_barrier_semaphore()
    total = 0
    for axes, others in groups:
        for other in others:
            pl.semaphore_signal(
                barrier,
                inc=1,
                device_id=device_at(axes, other),
                device_id_type=pl.DeviceIdType.MESH,
            )
            total += 1
    pl.semaphore_wait(barrier, total)


def sent(source, target, send_sem, recv_sem, where):
    copy = pltpu.make_async_remote_copy(
        src_ref=source,
        dst_ref=target,
        send_sem=send_sem,
        recv_sem=recv_sem,
        device_id=where,
        device_id_type=pl.DeviceIdType.MESH,
    )
    copy.start()
    return copy


def finish(copies):
    for copy in copies:
        copy.wait()


def rows_of(ref, index, count):
    rows = ref.shape[0] // count
    return ref.at[pl.ds(pl.multiple_of(index * rows, rows), rows), :]


class Group:
    def __init__(self, axes, send_sem, recv_sem):
        self.axes = axes
        self.count = math.prod(lax.axis_size(axis) for axis in axes)
        self.me = place_in(axes)
        self.others = [lax.rem(self.me + hop, self.count) for hop in range(1, self.count)]
        self.send_sem, self.recv_sem = send_sem, recv_sem

    def own(self, ref):
        return rows_of(ref, self.me, self.count)

    def one(self, source, target, which, hop):
        return sent(
            source,
            target,
            self.send_sem.at[which, hop],
            self.recv_sem.at[which, hop],
            device_at(self.axes, self.others[hop]),
        )

    def scatter(self, part, slot, which):
        return [
            self.one(rows_of(part, other, self.count), slot.at[hop], which, hop)
            for hop, other in enumerate(self.others)
        ]

    def total(self, part, slot):
        total = self.own(part)[...].astype(jnp.float32)
        for hop in range(self.count - 1):
            total = total + slot[hop].astype(jnp.float32)
        return total

    def spread(self, ref, which):
        return [self.one(self.own(ref), self.own(ref), which, hop) for hop in range(self.count - 1)]


def slots_for(part, count):
    return pltpu.VMEM((count - 1, part.shape[0] // count) + part.shape[1:], part.dtype)


def group_size(axes):
    return math.prod(lax.axis_size(axis) for axis in axes)


class Swap:
    def __init__(self, arrays, swapped, send_sem, recv_sem, local_sem):
        plane = Group(PLANE, send_sem, recv_sem)
        self.plane, self.arrays, self.swapped, self.local_sem = plane, arrays, swapped, local_sem

    def begin(self):
        self.copies, plane = [], self.plane
        for which, (array, swapped) in enumerate(zip(self.arrays, self.swapped)):
            share = swapped.shape[1]

            def columns(index):
                return array.at[:, pl.ds(pl.multiple_of(index * share, share), share)]

            for hop, other in enumerate(plane.others):
                self.copies.append(plane.one(columns(other), plane.own(swapped), which, hop))
            local = pltpu.make_async_copy(
                columns(plane.me), plane.own(swapped), self.local_sem.at[which]
            )
            local.start()
            self.copies.append(local)

    def end(self):
        finish(self.copies)


def swap_scratch(arrays):
    sems = pltpu.SemaphoreType.DMA((len(arrays), group_size(PLANE) - 1))
    return [sems, sems, pltpu.SemaphoreType.DMA((len(arrays),))] if arrays else []


def swap_shapes(arrays):
    count = group_size(PLANE)
    return [
        jax.ShapeDtypeStruct((array.shape[0] * count, array.shape[1] // count), array.dtype)
        for array in arrays
    ]


def swaps_in_kernels(width):
    return width // group_size(PLANE) % LANE == 0


def sum_kernel(n_swaps, part, *refs):
    arrays, refs = refs[:n_swaps], refs[n_swaps:]
    total, refs = refs[0], refs[1:]
    swapped, refs = refs[:n_swaps], refs[n_swaps:]
    slots, send_sem, recv_sem, *refs = refs
    group = Group(("tp",), send_sem, recv_sem)
    if n_swaps:
        swap = Swap(arrays, swapped, *refs)
        greet([(("tp",), group.others), (PLANE, swap.plane.others)])
    else:
        greet([(("tp",), group.others)])
    copies = group.scatter(part, slots, 0)
    if n_swaps:
        swap.begin()
    finish(copies)
    group.own(total)[...] = group.total(part, slots).astype(total.dtype)
    finish(group.spread(total, 1))
    if n_swaps:
        swap.end()


def sum_over_tp(call_id, part, arrays):
    count = group_size(("tp",))
    vmem = pl.BlockSpec(memory_space=pltpu.VMEM)
    sems = pltpu.SemaphoreType.DMA((2, count - 1))
    return pl.pallas_call(
        functools.partial(sum_kernel, len(arrays)),
        in_specs=[vmem] * (1 + len(arrays)),
        out_specs=[vmem] * (1 + len(arrays)),
        out_shape=[jax.ShapeDtypeStruct(part.shape, part.dtype)] + swap_shapes(arrays),
        scratch_shapes=[slots_for(part, count), sems, sems] + swap_scratch(arrays),
        compiler_params=pltpu.CompilerParams(
            collective_id=call_id, has_side_effects=True, vmem_limit_bytes=40 * 2**20
        ),
    )(part, *arrays)


def mixer_out_kernel(
    gated, out_all, tokens, gain, normed, middle, part, slots, send_sem, recv_sem
):
    group = Group(("tp",), send_sem, recv_sem)
    inner = gated.shape[1]
    share = out_all.shape[1]
    greet([(("tp",), group.others)])
    for at in range(out_all.shape[0] // inner):
        part[:, at * share : (at + 1) * share] = matmul(
            gated[...], out_all[at * inner : (at + 1) * inner, :]
        ).astype(part.dtype)
    finish(group.scatter(part, slots, 0))
    rows = group.own(tokens)[...].astype(jnp.float32) + group.total(part, slots)
    middle[...] = rows
    group.own(normed)[...] = (rows * inverse_rms(rows) * gain[...].astype(jnp.float32)).astype(
        normed.dtype
    )
    finish(group.spread(normed, 1))


def mixer_out(call_id, gated, out_all, tokens, gain):
    count = group_size(("tp",))
    vmem = pl.BlockSpec(memory_space=pltpu.VMEM)
    rows, width = tokens.shape
    part = jax.ShapeDtypeStruct((rows, width), jnp.bfloat16)
    sems = pltpu.SemaphoreType.DMA((2, count - 1))
    return pl.pallas_call(
        mixer_out_kernel,
        in_specs=[vmem] * 4,
        out_specs=[vmem] * 2,
        out_shape=[part, jax.ShapeDtypeStruct((rows // count, width), jnp.float32)],
        scratch_shapes=[pltpu.VMEM(part.shape, part.dtype), slots_for(part, count), sems, sems],
        compiler_params=pltpu.CompilerParams(
            collective_id=call_id, has_side_effects=True, vmem_limit_bytes=40 * 2**20
        ),
    )(gated, out_all, tokens, gain)


def ffn_back_kernel(n_swaps, part, ct, middle, gain, out_all, *refs):
    arrays, refs = refs[:n_swaps], refs[n_swaps:]
    middle_low, middle_grad, gain_grad, gated_grad, *refs = refs
    swapped, refs = refs[:n_swaps], refs[n_swaps:]
    slots, send_sem, recv_sem, *refs = refs
    group = Group(("tp",), send_sem, recv_sem)
    if n_swaps:
        swap = Swap(arrays, swapped, *refs)
        greet([(("tp",), group.others), (PLANE, swap.plane.others)])
    else:
        greet([(("tp",), group.others)])
    copies = group.scatter(part, slots, 0)
    if n_swaps:
        swap.begin()
    finish(copies)
    normed_grad = group.total(part, slots)
    rows = middle[...]
    scale = inverse_rms(rows)
    gain_grad[...] = jnp.sum(normed_grad * rows * scale, 0, keepdims=True)
    grad = group.own(ct)[...].astype(jnp.float32) + norm_back(
        normed_grad, rows, scale, gain[...].astype(jnp.float32)
    )
    middle_grad[...] = grad
    group.own(middle_low)[...] = grad.astype(middle_low.dtype)
    finish(group.spread(middle_low, 1))
    inner = gated_grad.shape[1]
    share = out_all.shape[1]
    total = None
    for at in range(out_all.shape[0] // inner):
        one = matmul_nt(
            middle_low[:, at * share : (at + 1) * share], out_all[at * inner : (at + 1) * inner, :]
        )
        total = one if total is None else total + one
    gated_grad[...] = total
    if n_swaps:
        swap.end()


def ffn_back(call_id, part, ct, middle, gain, out_all, arrays):
    count = group_size(("tp",))
    vmem = pl.BlockSpec(memory_space=pltpu.VMEM)
    rows, width = part.shape
    inner = out_all.shape[0] // group_size(PLANE)
    sems = pltpu.SemaphoreType.DMA((2, count - 1))
    return pl.pallas_call(
        functools.partial(ffn_back_kernel, len(arrays)),
        in_specs=[vmem] * (5 + len(arrays)),
        out_specs=[vmem] * (4 + len(arrays)),
        out_shape=[
            jax.ShapeDtypeStruct((rows, width), jnp.bfloat16),
            jax.ShapeDtypeStruct((rows // count, width), jnp.float32),
            jax.ShapeDtypeStruct((1, width), jnp.float32),
            jax.ShapeDtypeStruct((rows, inner), jnp.float32),
        ]
        + swap_shapes(arrays),
        scratch_shapes=[slots_for(part, count), sems, sems] + swap_scratch(arrays),
        compiler_params=pltpu.CompilerParams(
            collective_id=call_id, has_side_effects=True, vmem_limit_bytes=48 * 2**20
        ),
    )(part, ct, middle, gain, out_all, *arrays)


class PlaneGather:
    def __init__(self, own, gathered, send_sem, recv_sem):
        self.own, self.gathered = own, gathered
        self.send_sem, self.recv_sem = send_sem, recv_sem
        self.dp, self.ctx = lax.axis_index("dp"), lax.axis_index("ctx")
        self.n_dp, self.n_ctx = lax.axis_size("dp"), lax.axis_size("ctx")
        self.hands_on = relayed()
        self.count = self.n_dp * self.n_ctx
        self.me = self.dp * self.n_ctx + self.ctx
        self.others = [lax.rem(self.me + hop, self.count) for hop in range(1, self.count)]
        self.copies = {}
        if self.hands_on:
            core = lax.rem(self.dp, 2)
            over_core = self.dp + 1 - 2 * core
            over_y = lax.rem(self.dp + 2, 4)
            over_x = 1 - self.ctx
            self.core = {"dp": over_core, "ctx": self.ctx}
            self.at_x = {"dp": self.dp, "ctx": over_x}
            self.at_y = {"dp": over_y, "ctx": self.ctx}
            self.from_x = self.dp * 2 + over_x
            self.from_y = over_y * 2 + self.ctx
            self.across = over_y * 2 + over_x

    def part(self, owner, half):
        rows = self.gathered.shape[0] // self.count
        start, size = owner * rows, rows
        if half is not None:
            size = rows // 2
            start = start + half * size
        return self.gathered.at[pl.ds(pl.multiple_of(start, size), size), :]

    def send(self, which, owner, half, where):
        target = self.part(owner, half)
        source = target
        if owner is self.me:
            rows = self.own.shape[0]
            source = self.own
            if half is not None:
                source = self.own.at[pl.ds(half * (rows // 2), rows // 2), :]
        self.copies[which] = sent(
            source, target, self.send_sem.at[which], self.recv_sem.at[which], where
        )

    def arrived(self, *which):
        for one in which:
            self.copies[one].wait_recv()

    def begin(self, local_sem):
        self.local = pltpu.make_async_copy(self.own, self.part(self.me, None), local_sem)
        self.local.start()
        if not self.hands_on:
            for hop, other in enumerate(self.others):
                self.send(hop, self.me, None, device_at(PLANE, other))
            return
        self.send(0, self.me, 1, self.at_x)
        self.send(1, self.me, 0, self.at_y)
        self.send(2, self.me, None, self.core)
        self.send(3, self.me, 0, self.at_x)
        self.send(4, self.me, 1, self.at_y)

    def relay(self):
        if not self.hands_on:
            return
        self.arrived(0, 1)
        self.send(5, self.from_x, 1, self.at_y)
        self.send(6, self.from_y, 0, self.at_x)
        self.send(7, self.from_x, 1, self.core)
        self.send(8, self.from_y, 0, self.core)

    def hand_over(self):
        if not self.hands_on:
            return
        self.arrived(3, 4)
        self.send(9, self.from_x, 0, self.core)
        self.send(10, self.from_y, 1, self.core)

    def hand_over_last(self):
        if not self.hands_on:
            return
        self.arrived(5, 6)
        self.send(11, self.across, 1, self.core)
        self.send(12, self.across, 0, self.core)

    def end(self):
        if self.hands_on:
            self.arrived(2, 7, 8, 9, 10, 11, 12)
        else:
            self.arrived(*range(self.count - 1))
        for copy in self.copies.values():
            copy.wait_send()
        self.local.wait()


def relayed():
    return lax.axis_size("dp") == 4 and lax.axis_size("ctx") == 2


def gather_sems():
    count = 13 if relayed() else group_size(PLANE) - 1
    return pltpu.SemaphoreType.DMA((count,))


WIDE = 512


def products(source, first, last, dot, target, block_buf, block_sem, out_buf, out_sem):
    def fetch(j, slot):
        columns = pl.ds(pl.multiple_of(j * WIDE, WIDE), WIDE)
        return pltpu.make_async_copy(
            source.at[:, columns], block_buf.at[slot], block_sem.at[slot]
        )

    def store(j, slot):
        return pltpu.make_async_copy(out_buf.at[slot], target(j), out_sem.at[slot])

    fetch(first, first % 2).start()

    @pl.loop(first, last)
    def _(j):
        slot = lax.rem(j, 2)

        @pl.when(j + 1 < last)
        def _():
            fetch(j + 1, 1 - slot).start()

        fetch(j, slot).wait()

        @pl.when(j >= first + 2)
        def _():
            store(j - 2, slot).wait()

        out_buf[slot] = dot(block_buf[slot])
        store(j, slot).start()

    for j in range(max(first, last - 2), last):
        store(j, j % 2).wait()


def tail_kernel(
    sizes,
    mix_grads,
    normed_part,
    ffn_part,
    small,
    tokens,
    middle_rows,
    middle_grad,
    gain_row,
    one_cols,
    two_cols,
    ct_cols,
    middle_cols,
    ffn_all,
    tokens_grad,
    layer_out,
    small_sum,
    gains,
    mix_all,
    grad_inproj,
    grad_outproj,
    grad_gateup,
    grad_downproj,
    normed_slots,
    ffn_slots,
    small_slots,
    gain_slots,
    gain_own,
    block_buf,
    wide_buf,
    tall_buf,
    block_sem,
    wide_sem,
    tall_sem,
    tp_send,
    tp_recv,
    plane_send,
    plane_recv,
    gather_send,
    gather_recv,
    local_sem,
):
    inner, hidden, gain_at = sizes
    tp = Group(("tp",), tp_send, tp_recv)
    plane = Group(PLANE, plane_send, plane_recv)
    gather = PlaneGather(mix_grads, mix_all, gather_send, gather_recv)
    greet([(("tp",), tp.others), (PLANE, plane.others)])

    def flat(lhs):
        return lambda block: lax.dot_general(
            lhs[...], block, (((0,), (0,)), ((), ())), preferred_element_type=jnp.float32
        )

    def tall(rhs):
        return lambda block: lax.dot_general(
            block, rhs[...], (((0,), (0,)), ((), ())), preferred_element_type=jnp.float32
        )

    def side_by_side(ref, first):
        per = ref.shape[2] // WIDE

        def target(j):
            at = j - first
            columns = pl.ds(pl.multiple_of(lax.rem(at, per) * WIDE, WIDE), WIDE)
            return ref.at[lax.div(at, per), :, columns]

        return target

    def one_above_other(ref, first):
        return lambda j: ref.at[pl.ds(pl.multiple_of((j - first) * WIDE, WIDE), WIDE), :]

    wide = (block_buf, block_sem, wide_buf, wide_sem)
    high = (block_buf, block_sem, tall_buf, tall_sem)
    down_end = hidden // WIDE
    gu_end = 3 * hidden // WIDE
    out_end = gu_end + inner // WIDE

    normed_sent = tp.scatter(normed_part, normed_slots, 0)
    gather.begin(local_sem)
    ffn_sent = tp.scatter(ffn_part, ffn_slots, 1)
    small_sent = plane.scatter(small, small_slots, 0)
    products(
        ffn_all, down_end, gu_end, flat(two_cols), side_by_side(grad_gateup, down_end), *wide
    )
    gather.relay()
    products(ffn_all, 0, down_end, tall(ct_cols), one_above_other(grad_downproj, 0), *high)
    gather.hand_over()
    finish(normed_sent)
    hidden_in = tp.own(tokens)[...].astype(jnp.float32)
    tp.own(tokens_grad)[...] = (
        middle_grad[...]
        + norm_back(
            tp.total(normed_part, normed_slots),
            hidden_in,
            inverse_rms(hidden_in),
            gain_row[...].astype(jnp.float32),
        )
    ).astype(tokens_grad.dtype)
    tokens_sent = tp.spread(tokens_grad, 2)
    finish(small_sent)
    plane.own(small_sum)[...] = plane.total(small, small_slots).astype(small_sum.dtype)
    small_sent = plane.spread(small_sum, 1)
    products(
        ffn_all, gu_end, out_end, tall(middle_cols), one_above_other(grad_outproj, gu_end), *high
    )
    gather.hand_over_last()
    finish(ffn_sent)
    tp.own(layer_out)[...] = (middle_rows[...] + tp.total(ffn_part, ffn_slots)).astype(
        layer_out.dtype
    )
    layer_sent = tp.spread(layer_out, 3)
    finish(small_sent)
    gain_own[...] = small_sum[pl.ds(gain_at, gain_own.shape[0]), :].astype(jnp.float32)
    gain_sent = [tp.one(gain_own, gain_slots.at[hop], 4, hop) for hop in range(tp.count - 1)]
    gather.end()
    products(
        mix_all, 0, 2 * inner // WIDE, flat(one_cols), side_by_side(grad_inproj, 0), *wide
    )
    finish(gain_sent)
    total = gain_own[...]
    for hop in range(tp.count - 1):
        total = total + gain_slots[hop]
    gains[...] = total
    finish(tokens_sent)
    finish(layer_sent)


def run_tail(
    call_id,
    gain_at,
    mix_grads,
    normed_part,
    ffn_part,
    small,
    tokens,
    middle_rows,
    middle_grad,
    gain_row,
    one_cols,
    two_cols,
    ct_cols,
    middle_cols,
    ffn_all,
):
    inner = mix_grads.shape[1] // 2
    hidden = (ffn_all.shape[1] - inner) // 3
    share = one_cols.shape[1]
    all_rows = ffn_all.shape[0]
    tp_count, plane_count = group_size(("tp",)), group_size(PLANE)
    low, full = jnp.bfloat16, jnp.float32
    vmem = pl.BlockSpec(memory_space=pltpu.VMEM)
    hbm = pl.BlockSpec(memory_space=pl.ANY)
    gain_rows = 16
    dma = pltpu.SemaphoreType.DMA
    return pl.pallas_call(
        functools.partial(tail_kernel, (inner, hidden, gain_at)),
        in_specs=[vmem] * 12 + [hbm],
        out_specs=[vmem] * 4 + [hbm] * 5,
        out_shape=[
            jax.ShapeDtypeStruct(tokens.shape, low),
            jax.ShapeDtypeStruct(tokens.shape, low),
            jax.ShapeDtypeStruct(small.shape, low),
            jax.ShapeDtypeStruct((gain_rows, inner), full),
            jax.ShapeDtypeStruct((all_rows, 2 * inner), low),
            jax.ShapeDtypeStruct((2, share, inner), full),
            jax.ShapeDtypeStruct((inner, share), full),
            jax.ShapeDtypeStruct((2, share, hidden), full),
            jax.ShapeDtypeStruct((hidden, share), full),
        ],
        scratch_shapes=[
            slots_for(normed_part, tp_count),
            slots_for(ffn_part, tp_count),
            slots_for(small, plane_count),
            pltpu.VMEM((tp_count - 1, gain_rows, inner), full),
            pltpu.VMEM((gain_rows, inner), full),
            pltpu.VMEM((2, all_rows, WIDE), low),
            pltpu.VMEM((2, share, WIDE), full),
            pltpu.VMEM((2, WIDE, share), full),
            dma((2,)),
            dma((2,)),
            dma((2,)),
            dma((5, tp_count - 1)),
            dma((5, tp_count - 1)),
            dma((2, plane_count - 1)),
            dma((2, plane_count - 1)),
            gather_sems(),
            gather_sems(),
            dma(()),
        ],
        compiler_params=pltpu.CompilerParams(
            collective_id=call_id, has_side_effects=True, vmem_limit_bytes=56 * 2**20
        ),
    )(
        mix_grads,
        normed_part,
        ffn_part,
        small,
        tokens,
        middle_rows,
        middle_grad,
        gain_row,
        one_cols,
        two_cols,
        ct_cols,
        middle_cols,
        ffn_all,
    )


def head_kernel(
    tokens,
    gain,
    in_conv,
    in_gate,
    outproj,
    conv_in,
    gate_mix,
    conv_all,
    gate_all,
    out_all,
    normed,
    block_buf,
    block_sem,
    *sems,
):
    gathers = [
        PlaneGather(own, gathered, *sems[3 * at : 3 * at + 2])
        for at, (own, gathered) in enumerate(
            [(in_conv, conv_all), (in_gate, gate_all), (outproj, out_all)]
        )
    ]
    local_sems = sems[2::3]
    conv, gate, out = gathers
    greet([(PLANE, conv.others)])
    conv.begin(local_sems[0])
    gate.begin(local_sems[1])
    hidden_in = tokens[...].astype(jnp.float32)
    normed[...] = (
        hidden_in * inverse_rms(hidden_in) * gain[...].astype(jnp.float32)
    ).astype(normed.dtype)
    conv.relay()
    conv.hand_over()
    gate.relay()
    gate.hand_over()
    out.begin(local_sems[2])
    conv.hand_over_last()
    gate.hand_over_last()
    conv.end()
    gate.end()
    jobs = [
        (source, target, at)
        for source, target in ((conv_all, conv_in), (gate_all, gate_mix))
        for at in range(0, conv_in.shape[1], WIDE)
    ]

    def fetch(turn):
        source, _, at = jobs[turn]
        return pltpu.make_async_copy(
            source.at[:, at : at + WIDE], block_buf.at[turn % 2], block_sem.at[turn % 2]
        )

    fetch(0).start()
    for turn, (_, target, at) in enumerate(jobs):
        if turn + 1 < len(jobs):
            fetch(turn + 1).start()
        fetch(turn).wait()
        if turn == 1:
            out.relay()
            out.hand_over()
        target[:, at : at + WIDE] = matmul(normed[...], block_buf[turn % 2]).astype(target.dtype)
    out.hand_over_last()
    out.end()


def run_head(call_id, tokens, gain, inproj, outproj):
    rows, width = tokens.shape
    inner = inproj.shape[2]
    count = group_size(PLANE)
    low = jnp.bfloat16
    vmem = pl.BlockSpec(memory_space=pltpu.VMEM)
    hbm = pl.BlockSpec(memory_space=pl.ANY)
    return pl.pallas_call(
        head_kernel,
        in_specs=[vmem] * 2 + [hbm] * 3,
        out_specs=[vmem] * 2 + [hbm] * 3,
        out_shape=[
            jax.ShapeDtypeStruct((rows, inner), low),
            jax.ShapeDtypeStruct((rows, inner), jnp.float32),
            jax.ShapeDtypeStruct((width, inner), low),
            jax.ShapeDtypeStruct((width, inner), low),
            jax.ShapeDtypeStruct((inner * count, width // count), low),
        ],
        scratch_shapes=[
            pltpu.VMEM((rows, width), low),
            pltpu.VMEM((2, width, WIDE), low),
            pltpu.SemaphoreType.DMA((2,)),
        ]
        + [gather_sems(), gather_sems(), pltpu.SemaphoreType.DMA(())] * 3,
        compiler_params=pltpu.CompilerParams(
            collective_id=call_id, has_side_effects=True, vmem_limit_bytes=40 * 2**20
        ),
    )(tokens, gain, inproj[0], inproj[1], outproj)


def per_device(
    tokens,
    mixgain,
    inproj,
    convkern,
    convbias,
    selproj,
    stepproj,
    stepbias,
    decaylog,
    skipgain,
    outproj,
    ffngain,
    gateup,
    downproj,
    cotangent,
):
    seqs, span, width = tokens.shape
    rows = seqs * span
    taps, inner = convkern.shape
    rank = stepproj.shape[0]
    n_state = decaylog.shape[1]
    tiles = inner // LANE
    gain_mix = mixgain.astype(jnp.float32)
    kernel = convkern.astype(jnp.float32)
    kernel_bias = convbias.astype(jnp.float32)
    step_bias = stepbias.astype(jnp.float32)
    skip_weight = skipgain.astype(jnp.float32)
    decay_rate = -jnp.exp(jnp.transpose(decaylog.astype(jnp.float32)))
    rate = (decay_rate * LOG2E).reshape(n_state, tiles, LANE)

    gain_mix_row, gain_ffn_row = mixgain.reshape(1, width), ffngain.reshape(1, width)
    hidden = gateup.shape[2]
    low = jnp.bfloat16

    tokens_rows = tokens.reshape(rows, width)
    ct_low = cotangent.reshape(rows, width)
    conv_in, gate_mix, in_conv, in_gate, out_all = run_head(
        5, tokens_rows, gain_mix_row, inproj, outproj
    )
    ffn_pack, conv_in = lax.optimization_barrier(
        (jnp.concatenate([gateup[0], gateup[1], jnp.transpose(downproj)], 1), conv_in)
    )
    ffn_pack = gathered_rows(ffn_pack)
    hidden_in = tokens_rows.astype(jnp.float32)
    scale_one = inverse_rms(hidden_in)
    normed_one = (hidden_in * scale_one * gain_mix).astype(low)

    conv_seqs = conv_in.reshape(seqs, span, inner)
    rim_rows = passed_along(conv_seqs[:, span - (taps - 1) :], "ctx", 1)
    padded_in = jnp.concatenate([rim_rows, conv_seqs], 1).astype(jnp.float32)
    conv_out = kernel_bias[None, None]
    for offset in range(taps):
        conv_out = conv_out + kernel[offset][None, None] * padded_in[:, offset : offset + span]
    conv_out = conv_out.reshape(rows, inner)
    scan_in = jax.nn.silu(conv_out).astype(low)
    scan_float = scan_in.astype(jnp.float32)
    columns = selproj.shape[1]
    select_width = -(-columns // LANE) * LANE
    select_weights = jnp.pad(selproj, ((0, 0), (0, select_width - columns)))
    (select_cols,) = sum_over_tp(0, matmul(scan_in, select_weights), [])
    step_low = select_cols[:, :rank].astype(low)
    b_rows = select_cols[:, rank : rank + n_state].reshape(-1)
    c_rows = select_cols[:, rank + n_state : columns].reshape(-1)
    step_pre = matmul(step_low, stepproj) + step_bias[None]
    step_size = jax.nn.softplus(step_pre)
    span_decay = jnp.exp(
        decay_rate[None] * jnp.sum(step_size.reshape(seqs, span, inner), 1)[:, None]
    ).reshape(seqs, n_state, tiles, LANE)
    ends = scan_ends(step_size, scan_float, b_rows, rate, seqs, False)
    start = from_earlier(ends, span_decay, 1)
    prior, scan_out = scan_forward(start, step_size, scan_float, b_rows, c_rows, rate, seqs)
    mixer_core = scan_out + skip_weight[None] * scan_float
    gate_sig = jax.nn.silu(gate_mix)
    gated = (mixer_core * gate_sig).astype(low)
    normed_two, middle = mixer_out(1, gated, out_all, tokens_rows, gain_ffn_row)
    gate_up = ffn_pack[:, : 2 * hidden]
    down_weights = ffn_pack[:, 2 * hidden :]
    both_ffn = matmul(normed_two, gate_up)
    gate_ffn, up_ffn = both_ffn[:, :hidden], both_ffn[:, hidden:]
    activated = (jax.nn.silu(gate_ffn) * up_ffn).astype(low)
    act_grad = matmul(ct_low, down_weights)
    gate_grad = (act_grad * up_ffn * silu_slope(gate_ffn)).astype(low)
    up_grad = (act_grad * jax.nn.silu(gate_ffn)).astype(low)
    ffn_grads = jnp.concatenate([gate_grad, up_grad], 1)
    ffn_sent, ffn_grads = lax.optimization_barrier(
        (jnp.concatenate([activated, ffn_grads, gated], 1), ffn_grads)
    )
    ffn_all = gathered_rows(ffn_sent)
    normed_two_part = matmul_nt(ffn_grads, gate_up).astype(low)
    ffn_part = matmul_nt(activated, down_weights).astype(low)
    swap_now = swaps_in_kernels(width)
    to_swap = [normed_one, normed_two, ct_low]
    middle_low, middle_grad, ffngain_part, gated_grad, *swapped = ffn_back(
        2, normed_two_part, ct_low, middle, gain_ffn_row, out_all, to_swap if swap_now else []
    )
    if not swap_now:
        swapped = [swapped_columns(array) for array in to_swap]
    normed_one_cols, normed_two_cols, ct_cols = swapped
    core_grad = gated_grad * gate_sig
    gate_mix_grad = (gated_grad * mixer_core * silu_slope(gate_mix)).astype(low)
    grad_skipgain = jnp.sum(core_grad * scan_float, 0)
    back_ends = scan_ends(step_size, core_grad, c_rows, rate, seqs, True)
    end_grad = from_earlier(back_ends, span_decay, -1)
    step_grad, input_grad, rate_grad, parts = scan_backward(
        end_grad, prior, step_size, scan_float, core_grad, b_rows, c_rows, rate, seqs
    )
    grad_decaylog = rate_grad.reshape(n_state, inner) * decay_rate
    pre_grad = step_grad * jax.nn.sigmoid(step_pre)
    grad_stepbias = jnp.sum(pre_grad, 0)
    pre_low = pre_grad.astype(low)
    grad_stepproj = matmul_tn(step_low, pre_low)
    select_part = jnp.concatenate(
        [
            matmul_nt(pre_low, stepproj),
            jnp.sum(parts, -1),
            jnp.zeros((rows, select_width - columns), jnp.float32),
        ],
        1,
    ).astype(low)
    select_low, *swapped = sum_over_tp(3, select_part, [middle_low] if swap_now else [])
    (middle_cols,) = swapped if swap_now else [swapped_columns(middle_low)]
    grad_selproj = matmul_tn(select_low, scan_in)
    scan_in_grad = (
        core_grad * skip_weight[None]
        + input_grad
        + matmul_nt(select_low, select_weights)
    )
    conv_grad = scan_in_grad * silu_slope(conv_out)
    grad_convbias = jnp.sum(conv_grad, 0)
    conv_grad_seqs = conv_grad.reshape(seqs, span, inner)
    padded_grad = jnp.zeros(padded_in.shape, jnp.float32)
    kernel_rows = []
    for offset in range(taps):
        kernel_rows.append(jnp.sum(conv_grad_seqs * padded_in[:, offset : offset + span], (0, 1)))
        padded_grad = padded_grad + jnp.pad(
            kernel[offset][None, None] * conv_grad_seqs,
            ((0, 0), (offset, taps - 1 - offset), (0, 0)),
        )
    grad_convkern = jnp.stack(kernel_rows)
    returned = passed_along(padded_grad[:, : taps - 1], "ctx", -1)
    conv_in_grad = (
        (padded_grad[:, taps - 1 :] + jnp.pad(returned, ((0, 0), (span - taps + 1, 0), (0, 0))))
        .astype(low)
        .reshape(rows, inner)
    )
    mix_grads = jnp.concatenate([conv_in_grad, gate_mix_grad], 1)
    normed_one_part = matmul_nt(conv_in_grad, in_conv) + matmul_nt(gate_mix_grad, in_gate)
    mixgain_part = jnp.sum(normed_one_part * hidden_in * scale_one, 0)
    normed_one_part = normed_one_part.astype(low)
    small = [
        grad_convkern,
        grad_convbias[None],
        grad_stepbias[None],
        grad_decaylog,
        grad_skipgain[None],
        grad_stepproj,
        grad_selproj[:columns],
        mixgain_part.reshape(-1, inner),
        ffngain_part.reshape(-1, inner),
    ]
    sizes = [part.shape[0] for part in small]
    gain_at = sum(sizes[:-2]) + -sum(sizes[:-2]) % 16
    small.insert(-2, jnp.zeros((gain_at - sum(sizes[:-2]), inner), jnp.float32))
    small = jnp.concatenate(small, 0).astype(low)
    share = 16 * group_size(PLANE)
    small = jnp.pad(small, ((0, -(gain_at + 16) % share + 16 - sum(sizes[-2:])), (0, 0)))
    (
        tokens_grad,
        layer_out,
        small,
        gains,
        _,
        grad_inproj,
        grad_outproj,
        grad_gateup,
        grad_downproj,
    ) = run_tail(
        4,
        gain_at,
        mix_grads,
        normed_one_part,
        ffn_part,
        small,
        tokens_rows,
        middle,
        middle_grad,
        gain_mix_row,
        normed_one_cols,
        normed_two_cols,
        ct_cols,
        middle_cols,
        ffn_all,
    )
    small = small.astype(jnp.float32)
    smalls, at = [], 0
    for size in sizes[:-2]:
        smalls.append(small[at : at + size])
        at += size
    gains = gains[: sum(sizes[-2:])].reshape(2, width)
    return (
        layer_out.reshape(tokens.shape),
        tokens_grad.reshape(tokens.shape),
        gains[0],
        grad_inproj,
        smalls[0],
        smalls[1][0],
        jnp.transpose(smalls[6]),
        smalls[5],
        smalls[2][0],
        jnp.transpose(smalls[3]),
        smalls[4][0],
        grad_outproj,
        gains[1],
        grad_gateup,
        grad_downproj,
    )


def solution(mesh):
    in_specs = (
        P("dp", "ctx", None),
        P(),
        P(None, ("dp", "ctx"), "tp"),
        P(None, "tp"),
        P("tp"),
        P("tp", None),
        P(None, "tp"),
        P("tp"),
        P("tp", None),
        P("tp"),
        P("tp", ("dp", "ctx")),
        P(),
        P(None, ("dp", "ctx"), "tp"),
        P("tp", ("dp", "ctx")),
        P("dp", "ctx", None),
    )
    out_specs = (
        P("dp", "ctx", None),
        P("dp", "ctx", None),
        P(),
        P(None, ("dp", "ctx"), "tp"),
        P(None, "tp"),
        P("tp"),
        P("tp", None),
        P(None, "tp"),
        P("tp"),
        P("tp", None),
        P("tp"),
        P("tp", ("dp", "ctx")),
        P(),
        P(None, ("dp", "ctx"), "tp"),
        P("tp", ("dp", "ctx")),
    )
    return jax.shard_map(
        per_device, mesh=mesh, in_specs=in_specs, out_specs=out_specs, check_vma=False
    )
```

```python
import functools
import math

import jax
import jax.numpy as jnp
from jax import lax
from jax.experimental import pallas as pl
from jax.experimental.pallas import tpu as pltpu
from jax.sharding import PartitionSpec as P

EPSILON = 1e-05
LOG2E = math.log2(math.e)
LN2 = math.log(2.0)
SUB = 8
LANE = 128
PLANE = ("dp", "ctx")


def passed_along(value, axis, steps):
    count = lax.axis_size(axis)
    first, last = (max(0, -steps), min(count, count - steps))
    return lax.ppermute(value, axis, [(source, source + steps) for source in range(first, last)])


def matmul(left, right):
    return jnp.dot(left, right, preferred_element_type=jnp.float32)


def matmul_nt(left, right):
    return lax.dot_general(
        left, right, (((1,), (1,)), ((), ())), preferred_element_type=jnp.float32
    )


def matmul_tn(left, right):
    return lax.dot_general(
        left, right, (((0,), (0,)), ((), ())), preferred_element_type=jnp.float32
    )


def inverse_rms(values):
    return lax.rsqrt(jnp.mean(values * values, -1, keepdims=True) + EPSILON)


def silu_slope(values):
    logistic = jax.nn.sigmoid(values)
    return logistic * (1.0 + values * (1.0 - logistic))


def norm_back(grad_norm, values, scale, gain):
    scaled_grad = grad_norm * gain
    unit_rows = values * scale
    return scale * (scaled_grad - unit_rows * jnp.mean(scaled_grad * unit_rows, -1, keepdims=True))


def stage_in(ref, group, held):
    for tile in range(held.shape[0] // SUB):
        held[pl.ds(tile * SUB, SUB), :] = ref[
            pl.ds(pl.multiple_of(group * SUB, SUB), SUB), pl.ds(tile * LANE, LANE)
        ]


def stage_out(held, ref, group):
    for tile in range(held.shape[0] // SUB):
        ref[pl.ds(pl.multiple_of(group * SUB, SUB), SUB), pl.ds(tile * LANE, LANE)] = held[
            pl.ds(tile * SUB, SUB), :
        ]


def token_row(held, at, tiles):
    return held[pl.ds(at, tiles, stride=SUB), :]


def ends_kernel(
    n_state,
    tiles,
    groups,
    reverse,
    step_ref,
    drive_ref,
    rows_ref,
    rate_ref,
    end_ref,
    step_held,
    drive_held,
):
    base = pl.program_id(0) * groups * SUB * n_state
    rates = [rate_ref[n] for n in range(n_state)]

    def one(turn, states):
        group = groups - 1 - turn if reverse else turn
        order = range(SUB - 1, -1, -1) if reverse else range(SUB)
        states = list(states)
        stage_in(step_ref, group, step_held)
        stage_in(drive_ref, group, drive_held)
        for at in order:
            step = token_row(step_held, at, tiles)
            drive = token_row(drive_held, at, tiles)
            if not reverse:
                drive = drive * step
            for n in range(n_state):
                row = rows_ref[base + (group * SUB + at) * n_state + n]
                decay = jnp.exp2(step * rates[n])
                if reverse:
                    states[n] = decay * (states[n] + drive * row)
                else:
                    states[n] = decay * states[n] + drive * row
        return tuple(states)

    zero = jnp.zeros((tiles, LANE), jnp.float32)
    states = lax.fori_loop(0, groups, one, (zero,) * n_state)
    for n in range(n_state):
        end_ref[0, n] = states[n]


def scan_ends(step, drive, rows, rate, seqs, reverse):
    n_state, tiles, _ = rate.shape
    groups = step.shape[0] // seqs // SUB
    rows_spec = pl.BlockSpec((groups * SUB, tiles * LANE), lambda s: (s, 0))
    held = pltpu.VMEM((tiles * SUB, LANE), jnp.float32)
    return pl.pallas_call(
        functools.partial(ends_kernel, n_state, tiles, groups, reverse),
        grid=(seqs,),
        in_specs=[
            rows_spec,
            rows_spec,
            pl.BlockSpec(memory_space=pltpu.SMEM),
            pl.BlockSpec((n_state, tiles, LANE), lambda s: (0, 0, 0)),
        ],
        out_specs=pl.BlockSpec((1, n_state, tiles, LANE), lambda s: (s, 0, 0, 0)),
        out_shape=jax.ShapeDtypeStruct((seqs, n_state, tiles, LANE), jnp.float32),
        scratch_shapes=[held, held],
        compiler_params=pltpu.CompilerParams(vmem_limit_bytes=32 * 2**20),
    )(step, drive, rows, rate)


def forward_kernel(
    n_state,
    tiles,
    groups,
    blocks,
    start_ref,
    step_ref,
    input_ref,
    brow_ref,
    crow_ref,
    rate_ref,
    prior_ref,
    mixed_ref,
    carried,
    step_held,
    input_held,
    mixed_held,
):
    base = (pl.program_id(0) * blocks + pl.program_id(1)) * groups * SUB * n_state

    @pl.when(pl.program_id(1) == 0)
    def _():
        carried[...] = start_ref[0]

    def one(group, states):
        states = list(states)
        stage_in(step_ref, group, step_held)
        stage_in(input_ref, group, input_held)
        for at in range(SUB):
            step = token_row(step_held, at, tiles)
            drive = step * token_row(input_held, at, tiles)
            mixed = [None] * 2
            for n in range(n_state):
                where = base + (group * SUB + at) * n_state + n
                prior_ref[group * SUB + at, n] = states[n]
                decay = jnp.exp2(step * rate_ref[n])
                states[n] = decay * states[n] + drive * brow_ref[where]
                term = states[n] * crow_ref[where]
                mixed[n % 2] = term if mixed[n % 2] is None else mixed[n % 2] + term
            mixed_held[pl.ds(at, tiles, stride=SUB), :] = mixed[0] + mixed[1]
        stage_out(mixed_held, mixed_ref, group)
        return tuple(states)

    states = lax.fori_loop(0, groups, one, tuple(carried[n] for n in range(n_state)))
    for n in range(n_state):
        carried[n] = states[n]


def scan_forward(start, step, inputs, b_rows, c_rows, rate, seqs):
    n_state, tiles, _ = rate.shape
    all_groups = step.shape[0] // SUB
    groups = math.gcd(all_groups // seqs, 4)
    blocks = all_groups // seqs // groups
    rows_spec = pl.BlockSpec((groups * SUB, tiles * LANE), lambda s, b: (s * blocks + b, 0))
    held = pltpu.VMEM((tiles * SUB, LANE), jnp.float32)
    smem = pl.BlockSpec(memory_space=pltpu.SMEM)
    tokens = all_groups * SUB
    return pl.pallas_call(
        functools.partial(forward_kernel, n_state, tiles, groups, blocks),
        grid=(seqs, blocks),
        in_specs=[
            pl.BlockSpec((1, n_state, tiles, LANE), lambda s, b: (s, 0, 0, 0)),
            rows_spec,
            rows_spec,
            smem,
            smem,
            pl.BlockSpec((n_state, tiles, LANE), lambda s, b: (0, 0, 0)),
        ],
        out_specs=[
            pl.BlockSpec(
                (groups * SUB, n_state, tiles, LANE), lambda s, b: (s * blocks + b, 0, 0, 0)
            ),
            rows_spec,
        ],
        out_shape=[
            jax.ShapeDtypeStruct((tokens, n_state, tiles, LANE), jnp.float32),
            jax.ShapeDtypeStruct(step.shape, jnp.float32),
        ],
        scratch_shapes=[pltpu.VMEM((n_state, tiles, LANE), jnp.float32)] + [held] * 3,
        compiler_params=pltpu.CompilerParams(vmem_limit_bytes=32 * 2**20),
    )(start, step, inputs, b_rows, c_rows, rate)


def backward_kernel(
    n_state,
    tiles,
    groups,
    blocks,
    end_ref,
    prior_ref,
    step_ref,
    input_ref,
    ograd_ref,
    brow_ref,
    crow_ref,
    rate_ref,
    picks_ref,
    step_grad_ref,
    input_grad_ref,
    rate_grad_ref,
    part_ref,
    carried,
    step_held,
    input_held,
    ograd_held,
    step_grad_held,
    input_grad_held,
):
    block = blocks - 1 - pl.program_id(1)
    base = (pl.program_id(0) * blocks + block) * groups * SUB * n_state

    @pl.when(pl.program_id(1) == 0)
    def _():
        carried[...] = end_ref[0]

    @pl.when((pl.program_id(0) == 0) & (pl.program_id(1) == 0))
    def _():
        rate_grad_ref[...] = jnp.zeros_like(rate_grad_ref)

    def one(turn, grads):
        group = groups - 1 - turn
        grads = list(grads)
        stage_in(step_ref, group, step_held)
        stage_in(input_ref, group, input_held)
        stage_in(ograd_ref, group, ograd_held)
        for at in range(SUB - 1, -1, -1):
            step = token_row(step_held, at, tiles)
            value = token_row(input_held, at, tiles)
            ograd = token_row(ograd_held, at, tiles)
            drive = step * value
            along_b = None
            along_rate = None
            brow_parts, crow_parts = [], []
            for n in range(n_state):
                where = base + (group * SUB + at) * n_state + n
                brow, crow = brow_ref[where], crow_ref[where]
                rate = rate_ref[n]
                decay = jnp.exp2(step * rate)
                grad = ograd * crow + grads[n]
                kept = decay * prior_ref[group * SUB + at, n]
                state = kept + drive * brow
                decay_term = grad * kept
                grads[n] = decay * grad
                rate_grad_ref[n] += decay_term * step
                by_rate, by_brow = decay_term * rate, grad * brow
                along_rate = by_rate if along_rate is None else along_rate + by_rate
                along_b = by_brow if along_b is None else along_b + by_brow
                brow_parts.append(grad * drive)
                crow_parts.append(ograd * state)
            step_grad_held[pl.ds(at, tiles, stride=SUB), :] = along_rate * LN2 + along_b * value
            input_grad_held[pl.ds(at, tiles, stride=SUB), :] = along_b * step
            parts = jnp.concatenate(brow_parts + crow_parts, 0).astype(jnp.bfloat16)
            part_ref[group * SUB + at] = jnp.dot(
                picks_ref[...], parts, preferred_element_type=jnp.float32
            )
        stage_out(step_grad_held, step_grad_ref, group)
        stage_out(input_grad_held, input_grad_ref, group)
        return tuple(grads)

    grads = lax.fori_loop(0, groups, one, tuple(carried[n] for n in range(n_state)))
    for n in range(n_state):
        carried[n] = grads[n]


def scan_backward(end_grad, prior, step, inputs, ograd, b_rows, c_rows, rate, seqs):
    n_state, tiles, _ = rate.shape
    all_groups = step.shape[0] // SUB
    groups = math.gcd(all_groups // seqs, 4)
    blocks = all_groups // seqs // groups

    def at(s, b):
        return s * blocks + blocks - 1 - b

    rows_spec = pl.BlockSpec((groups * SUB, tiles * LANE), lambda s, b: (at(s, b), 0))
    held = pltpu.VMEM((tiles * SUB, LANE), jnp.float32)
    smem = pl.BlockSpec(memory_space=pltpu.SMEM)
    tokens = all_groups * SUB
    picks = jnp.repeat(jnp.eye(2 * n_state, dtype=jnp.bfloat16), tiles, 1)
    return pl.pallas_call(
        functools.partial(backward_kernel, n_state, tiles, groups, blocks),
        grid=(seqs, blocks),
        in_specs=[
            pl.BlockSpec((1, n_state, tiles, LANE), lambda s, b: (s, 0, 0, 0)),
            pl.BlockSpec((groups * SUB, n_state, tiles, LANE), lambda s, b: (at(s, b), 0, 0, 0)),
            rows_spec,
            rows_spec,
            rows_spec,
            smem,
            smem,
            pl.BlockSpec((n_state, tiles, LANE), lambda s, b: (0, 0, 0)),
            pl.BlockSpec(picks.shape, lambda s, b: (0, 0)),
        ],
        out_specs=[
            rows_spec,
            rows_spec,
            pl.BlockSpec((n_state, tiles, LANE), lambda s, b: (0, 0, 0)),
            pl.BlockSpec((groups * SUB, 2 * n_state, LANE), lambda s, b: (at(s, b), 0, 0)),
        ],
        out_shape=[
            jax.ShapeDtypeStruct(step.shape, jnp.float32),
            jax.ShapeDtypeStruct(step.shape, jnp.float32),
            jax.ShapeDtypeStruct(rate.shape, jnp.float32),
            jax.ShapeDtypeStruct((tokens, 2 * n_state, LANE), jnp.float32),
        ],
        scratch_shapes=[pltpu.VMEM((n_state, tiles, LANE), jnp.float32)] + [held] * 5,
        compiler_params=pltpu.CompilerParams(vmem_limit_bytes=32 * 2**20),
    )(end_grad, prior, step, inputs, ograd, b_rows, c_rows, rate, picks)


def from_earlier(ends, decay, steps):
    count = lax.axis_size("ctx")
    if count == 1:
        return jnp.zeros_like(ends)
    if count == 2:
        return passed_along(ends, "ctx", steps)
    index = lax.axis_index("ctx")
    all_ends = lax.all_gather(ends, "ctx")
    all_decays = lax.all_gather(decay, "ctx")

    def one(turn, state):
        at = turn if steps > 0 else count - 1 - turn
        reached = at < index if steps > 0 else at > index
        return jnp.where(reached, all_decays[at] * state + all_ends[at], state)

    return lax.fori_loop(0, count, one, jnp.zeros_like(ends))


def gathered_rows(rows):
    return lax.all_gather(rows, PLANE, axis=0, tiled=True)


def swapped_columns(rows):
    return lax.all_to_all(rows, PLANE, split_axis=1, concat_axis=0, tiled=True)


def place_in(axes):
    index = 0
    for axis in axes:
        index = index * lax.axis_size(axis) + lax.axis_index(axis)
    return index


def device_at(axes, index):
    where = {}
    for axis in reversed(axes):
        size = lax.axis_size(axis)
        where[axis] = lax.rem(index, size)
        index = lax.div(index, size)
    return where


def greet(groups):
    barrier = pltpu.get_barrier_semaphore()
    total = 0
    for axes, others in groups:
        for other in others:
            pl.semaphore_signal(
                barrier,
                inc=1,
                device_id=device_at(axes, other),
                device_id_type=pl.DeviceIdType.MESH,
            )
            total += 1
    pl.semaphore_wait(barrier, total)


def sent(source, target, send_sem, recv_sem, where):
    copy = pltpu.make_async_remote_copy(
        src_ref=source,
        dst_ref=target,
        send_sem=send_sem,
        recv_sem=recv_sem,
        device_id=where,
        device_id_type=pl.DeviceIdType.MESH,
    )
    copy.start()
    return copy


def finish(copies):
    for copy in copies:
        copy.wait()


def rows_of(ref, index, count):
    rows = ref.shape[0] // count
    return ref.at[pl.ds(pl.multiple_of(index * rows, rows), rows), :]


class Group:
    def __init__(self, axes, send_sem, recv_sem):
        self.axes = axes
        self.count = math.prod(lax.axis_size(axis) for axis in axes)
        self.me = place_in(axes)
        self.others = [lax.rem(self.me + hop, self.count) for hop in range(1, self.count)]
        self.send_sem, self.recv_sem = send_sem, recv_sem

    def own(self, ref):
        return rows_of(ref, self.me, self.count)

    def one(self, source, target, which, hop):
        return sent(
            source,
            target,
            self.send_sem.at[which, hop],
            self.recv_sem.at[which, hop],
            device_at(self.axes, self.others[hop]),
        )

    def scatter(self, part, slot, which):
        return [
            self.one(rows_of(part, other, self.count), slot.at[hop], which, hop)
            for hop, other in enumerate(self.others)
        ]

    def total(self, part, slot):
        total = self.own(part)[...].astype(jnp.float32)
        for hop in range(self.count - 1):
            total = total + slot[hop].astype(jnp.float32)
        return total

    def spread(self, ref, which):
        return [self.one(self.own(ref), self.own(ref), which, hop) for hop in range(self.count - 1)]


def slots_for(part, count):
    return pltpu.VMEM((count - 1, part.shape[0] // count) + part.shape[1:], part.dtype)


def group_size(axes):
    return math.prod(lax.axis_size(axis) for axis in axes)


class Swap:
    def __init__(self, arrays, swapped, send_sem, recv_sem, local_sem):
        plane = Group(PLANE, send_sem, recv_sem)
        self.plane, self.arrays, self.swapped, self.local_sem = plane, arrays, swapped, local_sem

    def begin(self):
        self.copies, plane = [], self.plane
        for which, (array, swapped) in enumerate(zip(self.arrays, self.swapped)):
            share = swapped.shape[1]

            def columns(index):
                return array.at[:, pl.ds(pl.multiple_of(index * share, share), share)]

            for hop, other in enumerate(plane.others):
                self.copies.append(plane.one(columns(other), plane.own(swapped), which, hop))
            local = pltpu.make_async_copy(
                columns(plane.me), plane.own(swapped), self.local_sem.at[which]
            )
            local.start()
            self.copies.append(local)

    def end(self):
        finish(self.copies)


def swap_scratch(arrays):
    sems = pltpu.SemaphoreType.DMA((len(arrays), group_size(PLANE) - 1))
    return [sems, sems, pltpu.SemaphoreType.DMA((len(arrays),))] if arrays else []


def swap_shapes(arrays):
    count = group_size(PLANE)
    return [
        jax.ShapeDtypeStruct((array.shape[0] * count, array.shape[1] // count), array.dtype)
        for array in arrays
    ]


def swaps_in_kernels(width):
    return width // group_size(PLANE) % LANE == 0


def sum_kernel(n_rows, n_swaps, part, *refs):
    own_rows, refs = refs[:n_rows], refs[n_rows:]
    arrays, refs = refs[:n_swaps], refs[n_swaps:]
    total, refs = refs[0], refs[1:]
    all_rows, refs = refs[:n_rows], refs[n_rows:]
    swapped, refs = refs[:n_swaps], refs[n_swaps:]
    slots, send_sem, recv_sem, *refs = refs
    group = Group(("tp",), send_sem, recv_sem)
    if n_swaps:
        swap = Swap(arrays, swapped, *refs)
        greet([(("tp",), group.others), (PLANE, swap.plane.others)])
    else:
        greet([(("tp",), group.others)])
    copies = group.scatter(part, slots, 0)
    if n_swaps:
        swap.begin()
    spreads = []
    for which, (own, gathered) in enumerate(zip(own_rows, all_rows)):
        group.own(gathered)[...] = own[...]
        spreads += group.spread(gathered, 2 + which)
    finish(copies)
    group.own(total)[...] = group.total(part, slots).astype(total.dtype)
    finish(group.spread(total, 1))
    finish(spreads)
    if n_swaps:
        swap.end()


def sum_over_tp(call_id, part, own_rows, arrays):
    count = group_size(("tp",))
    vmem = pl.BlockSpec(memory_space=pltpu.VMEM)
    operands = [part, *own_rows, *arrays]
    sems = pltpu.SemaphoreType.DMA((2 + len(own_rows), count - 1))
    return pl.pallas_call(
        functools.partial(sum_kernel, len(own_rows), len(arrays)),
        in_specs=[vmem] * len(operands),
        out_specs=[vmem] * len(operands),
        out_shape=[jax.ShapeDtypeStruct(part.shape, part.dtype)]
        + [
            jax.ShapeDtypeStruct((own.shape[0] * count,) + own.shape[1:], own.dtype)
            for own in own_rows
        ]
        + swap_shapes(arrays),
        scratch_shapes=[slots_for(part, count), sems, sems] + swap_scratch(arrays),
        compiler_params=pltpu.CompilerParams(
            collective_id=call_id, has_side_effects=True, vmem_limit_bytes=40 * 2**20
        ),
    )(*operands)


def mixer_out_kernel(
    gated, out_all, tokens, gain, normed, middle, part, slots, send_sem, recv_sem
):
    group = Group(("tp",), send_sem, recv_sem)
    inner = gated.shape[1]
    share = out_all.shape[1]
    greet([(("tp",), group.others)])
    for at in range(out_all.shape[0] // inner):
        part[:, at * share : (at + 1) * share] = matmul(
            gated[...], out_all[at * inner : (at + 1) * inner, :]
        ).astype(part.dtype)
    finish(group.scatter(part, slots, 0))
    rows = group.own(tokens)[...].astype(jnp.float32) + group.total(part, slots)
    middle[...] = rows
    group.own(normed)[...] = (rows * inverse_rms(rows) * gain[...].astype(jnp.float32)).astype(
        normed.dtype
    )
    finish(group.spread(normed, 1))


def mixer_out(call_id, gated, out_all, tokens, gain):
    count = group_size(("tp",))
    vmem = pl.BlockSpec(memory_space=pltpu.VMEM)
    rows, width = tokens.shape
    part = jax.ShapeDtypeStruct((rows, width), jnp.bfloat16)
    sems = pltpu.SemaphoreType.DMA((2, count - 1))
    return pl.pallas_call(
        mixer_out_kernel,
        in_specs=[vmem] * 4,
        out_specs=[vmem] * 2,
        out_shape=[part, jax.ShapeDtypeStruct((rows // count, width), jnp.float32)],
        scratch_shapes=[pltpu.VMEM(part.shape, part.dtype), slots_for(part, count), sems, sems],
        compiler_params=pltpu.CompilerParams(
            collective_id=call_id, has_side_effects=True, vmem_limit_bytes=40 * 2**20
        ),
    )(gated, out_all, tokens, gain)


def ffn_back_kernel(n_swaps, part, ct, middle, gain, out_all, *refs):
    arrays, refs = refs[:n_swaps], refs[n_swaps:]
    middle_low, middle_grad, gain_grad, gated_grad, *refs = refs
    swapped, refs = refs[:n_swaps], refs[n_swaps:]
    slots, send_sem, recv_sem, *refs = refs
    group = Group(("tp",), send_sem, recv_sem)
    if n_swaps:
        swap = Swap(arrays, swapped, *refs)
        greet([(("tp",), group.others), (PLANE, swap.plane.others)])
    else:
        greet([(("tp",), group.others)])
    copies = group.scatter(part, slots, 0)
    if n_swaps:
        swap.begin()
    finish(copies)
    normed_grad = group.total(part, slots)
    rows = middle[...]
    scale = inverse_rms(rows)
    gain_grad[...] = jnp.sum(normed_grad * rows * scale, 0, keepdims=True)
    grad = group.own(ct)[...].astype(jnp.float32) + norm_back(
        normed_grad, rows, scale, gain[...].astype(jnp.float32)
    )
    middle_grad[...] = grad
    group.own(middle_low)[...] = grad.astype(middle_low.dtype)
    finish(group.spread(middle_low, 1))
    inner = gated_grad.shape[1]
    share = out_all.shape[1]
    total = None
    for at in range(out_all.shape[0] // inner):
        one = matmul_nt(
            middle_low[:, at * share : (at + 1) * share], out_all[at * inner : (at + 1) * inner, :]
        )
        total = one if total is None else total + one
    gated_grad[...] = total
    if n_swaps:
        swap.end()


def ffn_back(call_id, part, ct, middle, gain, out_all, arrays):
    count = group_size(("tp",))
    vmem = pl.BlockSpec(memory_space=pltpu.VMEM)
    rows, width = part.shape
    inner = out_all.shape[0] // group_size(PLANE)
    sems = pltpu.SemaphoreType.DMA((2, count - 1))
    return pl.pallas_call(
        functools.partial(ffn_back_kernel, len(arrays)),
        in_specs=[vmem] * (5 + len(arrays)),
        out_specs=[vmem] * (4 + len(arrays)),
        out_shape=[
            jax.ShapeDtypeStruct((rows, width), jnp.bfloat16),
            jax.ShapeDtypeStruct((rows // count, width), jnp.float32),
            jax.ShapeDtypeStruct((1, width), jnp.float32),
            jax.ShapeDtypeStruct((rows, inner), jnp.float32),
        ]
        + swap_shapes(arrays),
        scratch_shapes=[slots_for(part, count), sems, sems] + swap_scratch(arrays),
        compiler_params=pltpu.CompilerParams(
            collective_id=call_id, has_side_effects=True, vmem_limit_bytes=48 * 2**20
        ),
    )(part, ct, middle, gain, out_all, *arrays)


def send_on(source, target, send_sem, recv_sem, ctx):
    return pltpu.make_async_remote_copy(
        src_ref=source,
        dst_ref=target,
        send_sem=send_sem,
        recv_sem=recv_sem,
        device_id={"ctx": ctx},
        device_id_type=pl.DeviceIdType.MESH,
    )


def forward_pair_kernel(
    n_state,
    tiles,
    groups,
    blocks,
    seqs,
    step_ref,
    input_ref,
    brow_ref,
    crow_ref,
    rate_ref,
    prior_ref,
    mixed_ref,
    carried,
    ends,
    starts,
    prior_buf,
    step_held,
    input_held,
    mixed_held,
    prior_sem,
    send_sem,
    recv_sem,
):
    place = lax.axis_index("ctx")
    greet([(("ctx",), [1 - place])])

    def hand_on(seq):
        return send_on(ends.at[seq], starts.at[seq], send_sem.at[seq], recv_sem.at[seq], 1)

    def store(block):
        slot = lax.rem(block, 2)
        rows = groups * SUB
        return pltpu.make_async_copy(
            prior_buf.at[slot],
            prior_ref.at[pl.ds(pl.multiple_of(block * rows, rows), rows)],
            prior_sem.at[slot],
        )

    @pl.loop(0, seqs)
    def _(seq):
        @pl.when(place == 0)
        def _():
            carried[...] = jnp.zeros_like(carried)

        @pl.when(place == 1)
        def _():
            hand_on(seq).wait_recv()
            carried[...] = starts[seq]

        @pl.loop(0, blocks)
        def _(inner_block):
            block = seq * blocks + inner_block
            slot = lax.rem(block, 2)

            @pl.when(block >= 2)
            def _():
                store(block - 2).wait()

            def one(turn, states):
                group = block * groups + turn
                states = list(states)
                stage_in(step_ref, group, step_held)
                stage_in(input_ref, group, input_held)
                for at in range(SUB):
                    step = token_row(step_held, at, tiles)
                    drive = step * token_row(input_held, at, tiles)
                    mixed = [None] * 2
                    for n in range(n_state):
                        where = (group * SUB + at) * n_state + n
                        prior_buf[slot, turn * SUB + at, n] = states[n]
                        decay = jnp.exp2(step * rate_ref[n])
                        states[n] = decay * states[n] + drive * brow_ref[where]
                        term = states[n] * crow_ref[where]
                        mixed[n % 2] = term if mixed[n % 2] is None else mixed[n % 2] + term
                    mixed_held[pl.ds(at, tiles, stride=SUB), :] = mixed[0] + mixed[1]
                stage_out(mixed_held, mixed_ref, group)
                return tuple(states)

            states = lax.fori_loop(0, groups, one, tuple(carried[n] for n in range(n_state)))
            for n in range(n_state):
                carried[n] = states[n]
            store(block).start()

        @pl.when(place == 0)
        def _():
            ends[seq] = carried[...]
            hand_on(seq).start()

    for block in range(max(0, seqs * blocks - 2), seqs * blocks):
        store(block).wait()

    @pl.when(place == 0)
    def _():
        @pl.loop(0, seqs)
        def _(seq):
            hand_on(seq).wait_send()


def scan_forward_pair(call_id, step, inputs, b_rows, c_rows, rate, seqs):
    n_state, tiles, _ = rate.shape
    tokens, inner = step.shape
    all_groups = tokens // SUB
    groups = math.gcd(all_groups // seqs, 4)
    blocks = all_groups // seqs // groups
    vmem = pl.BlockSpec(memory_space=pltpu.VMEM)
    smem = pl.BlockSpec(memory_space=pltpu.SMEM)
    full = jnp.float32
    held = pltpu.VMEM((tiles * SUB, LANE), full)
    boundary = pltpu.VMEM((seqs, n_state, tiles, LANE), full)
    dma = pltpu.SemaphoreType.DMA
    return pl.pallas_call(
        functools.partial(forward_pair_kernel, n_state, tiles, groups, blocks, seqs),
        in_specs=[vmem, vmem, smem, smem, vmem],
        out_specs=[pl.BlockSpec(memory_space=pl.ANY), vmem],
        out_shape=[
            jax.ShapeDtypeStruct((tokens, n_state, tiles, LANE), full),
            jax.ShapeDtypeStruct(step.shape, full),
        ],
        scratch_shapes=[
            pltpu.VMEM((n_state, tiles, LANE), full),
            boundary,
            boundary,
            pltpu.VMEM((2, groups * SUB, n_state, tiles, LANE), full),
            held,
            held,
            held,
            dma((2,)),
            dma((seqs,)),
            dma((seqs,)),
        ],
        compiler_params=pltpu.CompilerParams(
            collective_id=call_id, has_side_effects=True, vmem_limit_bytes=40 * 2**20
        ),
    )(step, inputs, b_rows, c_rows, rate)


def backward_pair_kernel(
    n_state,
    tiles,
    groups,
    blocks,
    seqs,
    step_ref,
    input_ref,
    ograd_ref,
    brow_ref,
    crow_ref,
    rate_ref,
    picks_ref,
    ffn_part,
    middle,
    prior_ref,
    step_grad_ref,
    input_grad_ref,
    rate_grad_ref,
    part_ref,
    layer_rows,
    carried,
    ends,
    starts,
    prior_buf,
    step_held,
    input_held,
    ograd_held,
    step_grad_held,
    input_grad_held,
    ffn_slots,
    prior_sem,
    send_sem,
    recv_sem,
    tp_send,
    tp_recv,
):
    place = lax.axis_index("ctx")
    tp = Group(("tp",), tp_send, tp_recv)
    greet([(("ctx",), [1 - place]), (("tp",), tp.others)])
    ffn_sent = tp.scatter(ffn_part, ffn_slots, 0)

    def hand_on(seq):
        return send_on(ends.at[seq], starts.at[seq], send_sem.at[seq], recv_sem.at[seq], 0)

    def fetch(turn):
        seq = lax.div(turn, blocks)
        block = seq * blocks + blocks - 1 - lax.rem(turn, blocks)
        slot = lax.rem(turn, 2)
        rows = groups * SUB
        return pltpu.make_async_copy(
            prior_ref.at[pl.ds(pl.multiple_of(block * rows, rows), rows)],
            prior_buf.at[slot],
            prior_sem.at[slot],
        )

    fetch(0).start()
    rate_grad_ref[...] = jnp.zeros_like(rate_grad_ref)

    @pl.when(place == 1)
    def _():
        @pl.loop(0, seqs)
        def _(seq):
            def one(turn, grads):
                group = (seq + 1) * blocks * groups - 1 - turn
                grads = list(grads)
                stage_in(step_ref, group, step_held)
                stage_in(ograd_ref, group, ograd_held)
                for at in range(SUB - 1, -1, -1):
                    step = token_row(step_held, at, tiles)
                    ograd = token_row(ograd_held, at, tiles)
                    for n in range(n_state):
                        row = crow_ref[(group * SUB + at) * n_state + n]
                        grads[n] = jnp.exp2(step * rate_ref[n]) * (grads[n] + ograd * row)
                return tuple(grads)

            zero = jnp.zeros((tiles, LANE), jnp.float32)
            grads = lax.fori_loop(0, blocks * groups, one, (zero,) * n_state)
            for n in range(n_state):
                ends[seq, n] = grads[n]
            hand_on(seq).start()

    @pl.loop(0, seqs)
    def _(seq):
        @pl.when(place == 1)
        def _():
            carried[...] = jnp.zeros_like(carried)

        @pl.when(place == 0)
        def _():
            hand_on(seq).wait_recv()
            carried[...] = starts[seq]

        @pl.loop(0, blocks)
        def _(inner_block):
            turn = seq * blocks + inner_block
            slot = lax.rem(turn, 2)
            first_group = (seq * blocks + blocks - 1 - inner_block) * groups

            @pl.when(turn + 1 < seqs * blocks)
            def _():
                fetch(turn + 1).start()

            fetch(turn).wait()

            def one(back, grads):
                inner_group = groups - 1 - back
                group = first_group + inner_group
                grads = list(grads)
                stage_in(step_ref, group, step_held)
                stage_in(input_ref, group, input_held)
                stage_in(ograd_ref, group, ograd_held)
                for at in range(SUB - 1, -1, -1):
                    step = token_row(step_held, at, tiles)
                    value = token_row(input_held, at, tiles)
                    ograd = token_row(ograd_held, at, tiles)
                    drive = step * value
                    along_b = None
                    along_rate = None
                    brow_parts, crow_parts = [], []
                    for n in range(n_state):
                        where = (group * SUB + at) * n_state + n
                        brow, crow = brow_ref[where], crow_ref[where]
                        rate = rate_ref[n]
                        decay = jnp.exp2(step * rate)
                        grad = ograd * crow + grads[n]
                        kept = decay * prior_buf[slot, inner_group * SUB + at, n]
                        state = kept + drive * brow
                        decay_term = grad * kept
                        grads[n] = decay * grad
                        rate_grad_ref[n] += decay_term * step
                        by_rate, by_brow = decay_term * rate, grad * brow
                        along_rate = by_rate if along_rate is None else along_rate + by_rate
                        along_b = by_brow if along_b is None else along_b + by_brow
                        brow_parts.append(grad * drive)
                        crow_parts.append(ograd * state)
                    step_grad_held[pl.ds(at, tiles, stride=SUB), :] = (
                        along_rate * LN2 + along_b * value
                    )
                    input_grad_held[pl.ds(at, tiles, stride=SUB), :] = along_b * step
                    parts = jnp.concatenate(brow_parts + crow_parts, 0).astype(jnp.bfloat16)
                    part_ref[group * SUB + at] = jnp.dot(
                        picks_ref[...], parts, preferred_element_type=jnp.float32
                    )
                stage_out(step_grad_held, step_grad_ref, group)
                stage_out(input_grad_held, input_grad_ref, group)
                return tuple(grads)

            grads = lax.fori_loop(0, groups, one, tuple(carried[n] for n in range(n_state)))
            for n in range(n_state):
                carried[n] = grads[n]

    finish(ffn_sent)
    layer_rows[...] = (middle[...] + tp.total(ffn_part, ffn_slots)).astype(layer_rows.dtype)

    @pl.when(place == 1)
    def _():
        @pl.loop(0, seqs)
        def _(seq):
            hand_on(seq).wait_send()


def scan_backward_pair(
    call_id, prior, step, inputs, ograd, b_rows, c_rows, rate, seqs, ffn_part, middle
):
    n_state, tiles, _ = rate.shape
    tokens, inner = step.shape
    all_groups = tokens // SUB
    groups = math.gcd(all_groups // seqs, 4)
    blocks = all_groups // seqs // groups
    tp_count = group_size(("tp",))
    vmem = pl.BlockSpec(memory_space=pltpu.VMEM)
    smem = pl.BlockSpec(memory_space=pltpu.SMEM)
    full = jnp.float32
    held = pltpu.VMEM((tiles * SUB, LANE), full)
    boundary = pltpu.VMEM((seqs, n_state, tiles, LANE), full)
    dma = pltpu.SemaphoreType.DMA
    picks = jnp.repeat(jnp.eye(2 * n_state, dtype=jnp.bfloat16), tiles, 1)
    return pl.pallas_call(
        functools.partial(backward_pair_kernel, n_state, tiles, groups, blocks, seqs),
        in_specs=[vmem] * 3 + [smem] * 2 + [vmem] * 4 + [pl.BlockSpec(memory_space=pl.ANY)],
        out_specs=[vmem] * 5,
        out_shape=[
            jax.ShapeDtypeStruct(step.shape, full),
            jax.ShapeDtypeStruct(step.shape, full),
            jax.ShapeDtypeStruct(rate.shape, full),
            jax.ShapeDtypeStruct((tokens, 2 * n_state, LANE), full),
            jax.ShapeDtypeStruct(middle.shape, jnp.bfloat16),
        ],
        scratch_shapes=[
            pltpu.VMEM((n_state, tiles, LANE), full),
            boundary,
            boundary,
            pltpu.VMEM((2, groups * SUB, n_state, tiles, LANE), full),
        ]
        + [held] * 5
        + [
            slots_for(ffn_part, tp_count),
            dma((2,)),
            dma((seqs,)),
            dma((seqs,)),
            dma((1, tp_count - 1)),
            dma((1, tp_count - 1)),
        ],
        compiler_params=pltpu.CompilerParams(
            collective_id=call_id, has_side_effects=True, vmem_limit_bytes=48 * 2**20
        ),
    )(step, inputs, ograd, b_rows, c_rows, rate, picks, ffn_part, middle, prior)


class PlaneGather:
    def __init__(self, own, gathered, send_sem, recv_sem):
        self.own, self.gathered = own, gathered
        self.send_sem, self.recv_sem = send_sem, recv_sem
        self.dp, self.ctx = lax.axis_index("dp"), lax.axis_index("ctx")
        self.n_dp, self.n_ctx = lax.axis_size("dp"), lax.axis_size("ctx")
        self.hands_on = relayed()
        self.count = self.n_dp * self.n_ctx
        self.me = self.dp * self.n_ctx + self.ctx
        self.others = [lax.rem(self.me + hop, self.count) for hop in range(1, self.count)]
        self.copies = {}
        if self.hands_on:
            core = lax.rem(self.dp, 2)
            over_core = self.dp + 1 - 2 * core
            over_y = lax.rem(self.dp + 2, 4)
            over_x = 1 - self.ctx
            self.core = {"dp": over_core, "ctx": self.ctx}
            self.at_x = {"dp": self.dp, "ctx": over_x}
            self.at_y = {"dp": over_y, "ctx": self.ctx}
            self.from_x = self.dp * 2 + over_x
            self.from_y = over_y * 2 + self.ctx
            self.across = over_y * 2 + over_x

    def part(self, owner, half):
        rows = self.gathered.shape[0] // self.count
        start, size = owner * rows, rows
        if half is not None:
            size = rows // 2
            start = start + half * size
        return self.gathered.at[pl.ds(pl.multiple_of(start, size), size), :]

    def send(self, which, owner, half, where):
        target = self.part(owner, half)
        source = target
        if owner is self.me:
            rows = self.own.shape[0]
            source = self.own
            if half is not None:
                source = self.own.at[pl.ds(half * (rows // 2), rows // 2), :]
        self.copies[which] = sent(
            source, target, self.send_sem.at[which], self.recv_sem.at[which], where
        )

    def arrived(self, *which):
        for one in which:
            self.copies[one].wait_recv()

    def begin(self, local_sem):
        self.local = pltpu.make_async_copy(self.own, self.part(self.me, None), local_sem)
        self.local.start()
        if not self.hands_on:
            for hop, other in enumerate(self.others):
                self.send(hop, self.me, None, device_at(PLANE, other))
            return
        self.send(0, self.me, 1, self.at_x)
        self.send(1, self.me, 0, self.at_y)
        self.send(2, self.me, None, self.core)
        self.send(3, self.me, 0, self.at_x)
        self.send(4, self.me, 1, self.at_y)

    def relay(self):
        if not self.hands_on:
            return
        self.arrived(0, 1)
        self.send(5, self.from_x, 1, self.at_y)
        self.send(6, self.from_y, 0, self.at_x)
        self.send(7, self.from_x, 1, self.core)
        self.send(8, self.from_y, 0, self.core)

    def hand_over(self):
        if not self.hands_on:
            return
        self.arrived(3, 4)
        self.send(9, self.from_x, 0, self.core)
        self.send(10, self.from_y, 1, self.core)

    def hand_over_last(self):
        if not self.hands_on:
            return
        self.arrived(5, 6)
        self.send(11, self.across, 1, self.core)
        self.send(12, self.across, 0, self.core)

    def end(self):
        if self.hands_on:
            self.arrived(2, 7, 8, 9, 10, 11, 12)
        else:
            self.arrived(*range(self.count - 1))
        for copy in self.copies.values():
            copy.wait_send()
        self.local.wait()


def relayed():
    return lax.axis_size("dp") == 4 and lax.axis_size("ctx") == 2


def gather_sems():
    count = 13 if relayed() else group_size(PLANE) - 1
    return pltpu.SemaphoreType.DMA((count,))


WIDE = 512


def products(source, first, last, dot, target, block_buf, block_sem, out_buf, out_sem):
    def fetch(j, slot):
        columns = pl.ds(pl.multiple_of(j * WIDE, WIDE), WIDE)
        return pltpu.make_async_copy(
            source.at[:, columns], block_buf.at[slot], block_sem.at[slot]
        )

    def store(j, slot):
        return pltpu.make_async_copy(out_buf.at[slot], target(j), out_sem.at[slot])

    fetch(first, first % 2).start()

    @pl.loop(first, last)
    def _(j):
        slot = lax.rem(j, 2)

        @pl.when(j + 1 < last)
        def _():
            fetch(j + 1, 1 - slot).start()

        fetch(j, slot).wait()

        @pl.when(j >= first + 2)
        def _():
            store(j - 2, slot).wait()

        out_buf[slot] = dot(block_buf[slot])
        store(j, slot).start()

    for j in range(max(first, last - 2), last):
        store(j, j % 2).wait()


def tail_kernel(
    sizes,
    mix_grads,
    normed_part,
    small,
    tokens,
    middle_grad,
    gain_row,
    one_cols,
    two_cols,
    ct_cols,
    middle_cols,
    ffn_all,
    tokens_grad,
    small_sum,
    gains,
    mix_all,
    grad_inproj,
    grad_outproj,
    grad_gateup,
    grad_downproj,
    normed_slots,
    small_slots,
    gain_slots,
    gain_own,
    block_buf,
    wide_buf,
    tall_buf,
    block_sem,
    wide_sem,
    tall_sem,
    tp_send,
    tp_recv,
    plane_send,
    plane_recv,
    gather_send,
    gather_recv,
    local_sem,
):
    inner, hidden, gain_at = sizes
    tp = Group(("tp",), tp_send, tp_recv)
    plane = Group(PLANE, plane_send, plane_recv)
    gather = PlaneGather(mix_grads, mix_all, gather_send, gather_recv)
    greet([(("tp",), tp.others), (PLANE, plane.others)])

    def flat(lhs):
        return lambda block: lax.dot_general(
            lhs[...], block, (((0,), (0,)), ((), ())), preferred_element_type=jnp.float32
        )

    def tall(rhs):
        return lambda block: lax.dot_general(
            block, rhs[...], (((0,), (0,)), ((), ())), preferred_element_type=jnp.float32
        )

    def side_by_side(ref, first):
        per = ref.shape[2] // WIDE

        def target(j):
            at = j - first
            columns = pl.ds(pl.multiple_of(lax.rem(at, per) * WIDE, WIDE), WIDE)
            return ref.at[lax.div(at, per), :, columns]

        return target

    def one_above_other(ref, first):
        return lambda j: ref.at[pl.ds(pl.multiple_of((j - first) * WIDE, WIDE), WIDE), :]

    wide = (block_buf, block_sem, wide_buf, wide_sem)
    high = (block_buf, block_sem, tall_buf, tall_sem)
    down_end = hidden // WIDE
    gu_end = 3 * hidden // WIDE
    out_end = gu_end + inner // WIDE

    normed_sent = tp.scatter(normed_part, normed_slots, 0)
    gather.begin(local_sem)
    small_sent = plane.scatter(small, small_slots, 0)
    products(
        ffn_all, down_end, gu_end, flat(two_cols), side_by_side(grad_gateup, down_end), *wide
    )
    gather.relay()
    products(ffn_all, 0, down_end, tall(ct_cols), one_above_other(grad_downproj, 0), *high)
    gather.hand_over()
    finish(normed_sent)
    hidden_in = tp.own(tokens)[...].astype(jnp.float32)
    tp.own(tokens_grad)[...] = (
        middle_grad[...]
        + norm_back(
            tp.total(normed_part, normed_slots),
            hidden_in,
            inverse_rms(hidden_in),
            gain_row[...].astype(jnp.float32),
        )
    ).astype(tokens_grad.dtype)
    tokens_sent = tp.spread(tokens_grad, 1)
    finish(small_sent)
    plane.own(small_sum)[...] = plane.total(small, small_slots).astype(small_sum.dtype)
    small_sent = plane.spread(small_sum, 1)
    products(
        ffn_all, gu_end, out_end, tall(middle_cols), one_above_other(grad_outproj, gu_end), *high
    )
    gather.hand_over_last()
    finish(small_sent)
    gain_own[...] = small_sum[pl.ds(gain_at, gain_own.shape[0]), :].astype(jnp.float32)
    gain_sent = [tp.one(gain_own, gain_slots.at[hop], 2, hop) for hop in range(tp.count - 1)]
    gather.end()
    products(
        mix_all, 0, 2 * inner // WIDE, flat(one_cols), side_by_side(grad_inproj, 0), *wide
    )
    finish(gain_sent)
    total = gain_own[...]
    for hop in range(tp.count - 1):
        total = total + gain_slots[hop]
    gains[...] = total
    finish(tokens_sent)


def run_tail(
    call_id,
    gain_at,
    mix_grads,
    normed_part,
    small,
    tokens,
    middle_grad,
    gain_row,
    one_cols,
    two_cols,
    ct_cols,
    middle_cols,
    ffn_all,
):
    inner = mix_grads.shape[1] // 2
    hidden = (ffn_all.shape[1] - inner) // 3
    share = one_cols.shape[1]
    all_rows = ffn_all.shape[0]
    tp_count, plane_count = group_size(("tp",)), group_size(PLANE)
    low, full = jnp.bfloat16, jnp.float32
    vmem = pl.BlockSpec(memory_space=pltpu.VMEM)
    hbm = pl.BlockSpec(memory_space=pl.ANY)
    gain_rows = 16
    dma = pltpu.SemaphoreType.DMA
    return pl.pallas_call(
        functools.partial(tail_kernel, (inner, hidden, gain_at)),
        in_specs=[vmem] * 10 + [hbm],
        out_specs=[vmem] * 3 + [hbm] * 5,
        out_shape=[
            jax.ShapeDtypeStruct(tokens.shape, low),
            jax.ShapeDtypeStruct(small.shape, low),
            jax.ShapeDtypeStruct((gain_rows, inner), full),
            jax.ShapeDtypeStruct((all_rows, 2 * inner), low),
            jax.ShapeDtypeStruct((2, share, inner), full),
            jax.ShapeDtypeStruct((inner, share), full),
            jax.ShapeDtypeStruct((2, share, hidden), full),
            jax.ShapeDtypeStruct((hidden, share), full),
        ],
        scratch_shapes=[
            slots_for(normed_part, tp_count),
            slots_for(small, plane_count),
            pltpu.VMEM((tp_count - 1, gain_rows, inner), full),
            pltpu.VMEM((gain_rows, inner), full),
            pltpu.VMEM((2, all_rows, WIDE), low),
            pltpu.VMEM((2, share, WIDE), full),
            pltpu.VMEM((2, WIDE, share), full),
            dma((2,)),
            dma((2,)),
            dma((2,)),
            dma((3, tp_count - 1)),
            dma((3, tp_count - 1)),
            dma((2, plane_count - 1)),
            dma((2, plane_count - 1)),
            gather_sems(),
            gather_sems(),
            dma(()),
        ],
        compiler_params=pltpu.CompilerParams(
            collective_id=call_id, has_side_effects=True, vmem_limit_bytes=56 * 2**20
        ),
    )(
        mix_grads,
        normed_part,
        small,
        tokens,
        middle_grad,
        gain_row,
        one_cols,
        two_cols,
        ct_cols,
        middle_cols,
        ffn_all,
    )


def head_kernel(
    tokens,
    gain,
    in_conv,
    in_gate,
    outproj,
    conv_in,
    gate_mix,
    conv_all,
    gate_all,
    out_all,
    normed,
    block_buf,
    block_sem,
    *sems,
):
    gathers = [
        PlaneGather(own, gathered, *sems[3 * at : 3 * at + 2])
        for at, (own, gathered) in enumerate(
            [(in_conv, conv_all), (in_gate, gate_all), (outproj, out_all)]
        )
    ]
    local_sems = sems[2::3]
    conv, gate, out = gathers
    greet([(PLANE, conv.others)])
    conv.begin(local_sems[0])
    gate.begin(local_sems[1])
    hidden_in = tokens[...].astype(jnp.float32)
    normed[...] = (
        hidden_in * inverse_rms(hidden_in) * gain[...].astype(jnp.float32)
    ).astype(normed.dtype)
    conv.relay()
    conv.hand_over()
    gate.relay()
    gate.hand_over()
    out.begin(local_sems[2])
    conv.hand_over_last()
    gate.hand_over_last()
    conv.end()
    gate.end()
    jobs = [
        (source, target, at)
        for source, target in ((conv_all, conv_in), (gate_all, gate_mix))
        for at in range(0, conv_in.shape[1], WIDE)
    ]

    def fetch(turn):
        source, _, at = jobs[turn]
        return pltpu.make_async_copy(
            source.at[:, at : at + WIDE], block_buf.at[turn % 2], block_sem.at[turn % 2]
        )

    fetch(0).start()
    for turn, (_, target, at) in enumerate(jobs):
        if turn + 1 < len(jobs):
            fetch(turn + 1).start()
        fetch(turn).wait()
        if turn == 1:
            out.relay()
            out.hand_over()
        target[:, at : at + WIDE] = matmul(normed[...], block_buf[turn % 2]).astype(target.dtype)
    out.hand_over_last()
    out.end()


def run_head(call_id, tokens, gain, inproj, outproj):
    rows, width = tokens.shape
    inner = inproj.shape[2]
    count = group_size(PLANE)
    low = jnp.bfloat16
    vmem = pl.BlockSpec(memory_space=pltpu.VMEM)
    hbm = pl.BlockSpec(memory_space=pl.ANY)
    return pl.pallas_call(
        head_kernel,
        in_specs=[vmem] * 2 + [hbm] * 3,
        out_specs=[vmem] * 2 + [hbm] * 3,
        out_shape=[
            jax.ShapeDtypeStruct((rows, inner), low),
            jax.ShapeDtypeStruct((rows, inner), jnp.float32),
            jax.ShapeDtypeStruct((width, inner), low),
            jax.ShapeDtypeStruct((width, inner), low),
            jax.ShapeDtypeStruct((inner * count, width // count), low),
        ],
        scratch_shapes=[
            pltpu.VMEM((rows, width), low),
            pltpu.VMEM((2, width, WIDE), low),
            pltpu.SemaphoreType.DMA((2,)),
        ]
        + [gather_sems(), gather_sems(), pltpu.SemaphoreType.DMA(())] * 3,
        compiler_params=pltpu.CompilerParams(
            collective_id=call_id, has_side_effects=True, vmem_limit_bytes=40 * 2**20
        ),
    )(tokens, gain, inproj[0], inproj[1], outproj)


def per_device(
    tokens,
    mixgain,
    inproj,
    convkern,
    convbias,
    selproj,
    stepproj,
    stepbias,
    decaylog,
    skipgain,
    outproj,
    ffngain,
    gateup,
    downproj,
    cotangent,
):
    seqs, span, width = tokens.shape
    rows = seqs * span
    taps, inner = convkern.shape
    rank = stepproj.shape[0]
    n_state = decaylog.shape[1]
    tiles = inner // LANE
    gain_mix = mixgain.astype(jnp.float32)
    kernel = convkern.astype(jnp.float32)
    kernel_bias = convbias.astype(jnp.float32)
    step_bias = stepbias.astype(jnp.float32)
    skip_weight = skipgain.astype(jnp.float32)
    decay_rate = -jnp.exp(jnp.transpose(decaylog.astype(jnp.float32)))
    rate = (decay_rate * LOG2E).reshape(n_state, tiles, LANE)

    gain_mix_row, gain_ffn_row = mixgain.reshape(1, width), ffngain.reshape(1, width)
    hidden = gateup.shape[2]
    low = jnp.bfloat16

    tokens_rows = tokens.reshape(rows, width)
    ct_low = cotangent.reshape(rows, width)
    conv_in, gate_mix, in_conv, in_gate, out_all = run_head(
        5, tokens_rows, gain_mix_row, inproj, outproj
    )
    ffn_pack, conv_in = lax.optimization_barrier(
        (jnp.concatenate([gateup[0], gateup[1], jnp.transpose(downproj)], 1), conv_in)
    )
    ffn_pack = gathered_rows(ffn_pack)
    hidden_in = tokens_rows.astype(jnp.float32)
    scale_one = inverse_rms(hidden_in)
    normed_one = (hidden_in * scale_one * gain_mix).astype(low)

    conv_seqs = conv_in.reshape(seqs, span, inner)
    rim_rows = passed_along(conv_seqs[:, span - (taps - 1) :], "ctx", 1)
    padded_in = jnp.concatenate([rim_rows, conv_seqs], 1).astype(jnp.float32)
    conv_out = kernel_bias[None, None]
    for offset in range(taps):
        conv_out = conv_out + kernel[offset][None, None] * padded_in[:, offset : offset + span]
    conv_out = conv_out.reshape(rows, inner)
    scan_in = jax.nn.silu(conv_out).astype(low)
    scan_float = scan_in.astype(jnp.float32)
    columns = selproj.shape[1]
    select_width = -(-columns // LANE) * LANE
    select_weights = jnp.pad(selproj, ((0, 0), (0, select_width - columns)))
    (select_cols,) = sum_over_tp(0, matmul(scan_in, select_weights), [], [])
    step_low = select_cols[:, :rank].astype(low)
    b_rows = select_cols[:, rank : rank + n_state].reshape(-1)
    c_rows = select_cols[:, rank + n_state : columns].reshape(-1)
    step_pre = matmul(step_low, stepproj) + step_bias[None]
    step_size = jax.nn.softplus(step_pre)
    in_pairs = lax.axis_size("ctx") == 2
    if in_pairs:
        prior, scan_out = scan_forward_pair(6, step_size, scan_float, b_rows, c_rows, rate, seqs)
    else:
        span_decay = jnp.exp(
            decay_rate[None] * jnp.sum(step_size.reshape(seqs, span, inner), 1)[:, None]
        ).reshape(seqs, n_state, tiles, LANE)
        ends = scan_ends(step_size, scan_float, b_rows, rate, seqs, False)
        start = from_earlier(ends, span_decay, 1)
        prior, scan_out = scan_forward(start, step_size, scan_float, b_rows, c_rows, rate, seqs)
    mixer_core = scan_out + skip_weight[None] * scan_float
    gate_sig = jax.nn.silu(gate_mix)
    gated = (mixer_core * gate_sig).astype(low)
    normed_two, middle = mixer_out(1, gated, out_all, tokens_rows, gain_ffn_row)
    gate_up = ffn_pack[:, : 2 * hidden]
    down_weights = ffn_pack[:, 2 * hidden :]
    both_ffn = matmul(normed_two, gate_up)
    gate_ffn, up_ffn = both_ffn[:, :hidden], both_ffn[:, hidden:]
    activated = (jax.nn.silu(gate_ffn) * up_ffn).astype(low)
    act_grad = matmul(ct_low, down_weights)
    gate_grad = (act_grad * up_ffn * silu_slope(gate_ffn)).astype(low)
    up_grad = (act_grad * jax.nn.silu(gate_ffn)).astype(low)
    ffn_grads = jnp.concatenate([gate_grad, up_grad], 1)
    ffn_sent, ffn_grads = lax.optimization_barrier(
        (jnp.concatenate([activated, ffn_grads, gated], 1), ffn_grads)
    )
    ffn_all = gathered_rows(ffn_sent)
    normed_two_part = matmul_nt(ffn_grads, gate_up).astype(low)
    ffn_part = matmul_nt(activated, down_weights).astype(low)
    swap_now = swaps_in_kernels(width)
    to_swap = [normed_one, normed_two, ct_low]
    middle_low, middle_grad, ffngain_part, gated_grad, *swapped = ffn_back(
        2, normed_two_part, ct_low, middle, gain_ffn_row, out_all, to_swap if swap_now else []
    )
    if not swap_now:
        swapped = [swapped_columns(array) for array in to_swap]
    normed_one_cols, normed_two_cols, ct_cols = swapped
    core_grad = gated_grad * gate_sig
    gate_mix_grad = (gated_grad * mixer_core * silu_slope(gate_mix)).astype(low)
    grad_skipgain = jnp.sum(core_grad * scan_float, 0)
    if in_pairs:
        step_grad, input_grad, rate_grad, parts, layer_rows = scan_backward_pair(
            7,
            prior,
            step_size,
            scan_float,
            core_grad,
            b_rows,
            c_rows,
            rate,
            seqs,
            ffn_part,
            middle,
        )
    else:
        back_ends = scan_ends(step_size, core_grad, c_rows, rate, seqs, True)
        end_grad = from_earlier(back_ends, span_decay, -1)
        step_grad, input_grad, rate_grad, parts = scan_backward(
            end_grad, prior, step_size, scan_float, core_grad, b_rows, c_rows, rate, seqs
        )
        ffn_sum = lax.psum_scatter(ffn_part, "tp", scatter_dimension=0, tiled=True)
        layer_rows = (middle + ffn_sum.astype(jnp.float32)).astype(low)
    grad_decaylog = rate_grad.reshape(n_state, inner) * decay_rate
    pre_grad = step_grad * jax.nn.sigmoid(step_pre)
    grad_stepbias = jnp.sum(pre_grad, 0)
    pre_low = pre_grad.astype(low)
    grad_stepproj = matmul_tn(step_low, pre_low)
    select_part = jnp.concatenate(
        [
            matmul_nt(pre_low, stepproj),
            jnp.sum(parts, -1),
            jnp.zeros((rows, select_width - columns), jnp.float32),
        ],
        1,
    ).astype(low)
    select_low, layer_out, *swapped = sum_over_tp(
        3, select_part, [layer_rows], [middle_low] if swap_now else []
    )
    (middle_cols,) = swapped if swap_now else [swapped_columns(middle_low)]
    grad_selproj = matmul_tn(select_low, scan_in)
    scan_in_grad = (
        core_grad * skip_weight[None]
        + input_grad
        + matmul_nt(select_low, select_weights)
    )
    conv_grad = scan_in_grad * silu_slope(conv_out)
    grad_convbias = jnp.sum(conv_grad, 0)
    conv_grad_seqs = conv_grad.reshape(seqs, span, inner)
    padded_grad = jnp.zeros(padded_in.shape, jnp.float32)
    kernel_rows = []
    for offset in range(taps):
        kernel_rows.append(jnp.sum(conv_grad_seqs * padded_in[:, offset : offset + span], (0, 1)))
        padded_grad = padded_grad + jnp.pad(
            kernel[offset][None, None] * conv_grad_seqs,
            ((0, 0), (offset, taps - 1 - offset), (0, 0)),
        )
    grad_convkern = jnp.stack(kernel_rows)
    returned = passed_along(padded_grad[:, : taps - 1], "ctx", -1)
    conv_in_grad = (
        (padded_grad[:, taps - 1 :] + jnp.pad(returned, ((0, 0), (span - taps + 1, 0), (0, 0))))
        .astype(low)
        .reshape(rows, inner)
    )
    mix_grads = jnp.concatenate([conv_in_grad, gate_mix_grad], 1)
    normed_one_part = matmul_nt(conv_in_grad, in_conv) + matmul_nt(gate_mix_grad, in_gate)
    mixgain_part = jnp.sum(normed_one_part * hidden_in * scale_one, 0)
    normed_one_part = normed_one_part.astype(low)
    small = [
        grad_convkern,
        grad_convbias[None],
        grad_stepbias[None],
        grad_decaylog,
        grad_skipgain[None],
        grad_stepproj,
        grad_selproj[:columns],
        mixgain_part.reshape(-1, inner),
        ffngain_part.reshape(-1, inner),
    ]
    sizes = [part.shape[0] for part in small]
    gain_at = sum(sizes[:-2]) + -sum(sizes[:-2]) % 16
    small.insert(-2, jnp.zeros((gain_at - sum(sizes[:-2]), inner), jnp.float32))
    small = jnp.concatenate(small, 0).astype(low)
    share = 16 * group_size(PLANE)
    small = jnp.pad(small, ((0, -(gain_at + 16) % share + 16 - sum(sizes[-2:])), (0, 0)))
    (
        tokens_grad,
        small,
        gains,
        _,
        grad_inproj,
        grad_outproj,
        grad_gateup,
        grad_downproj,
    ) = run_tail(
        4,
        gain_at,
        mix_grads,
        normed_one_part,
        small,
        tokens_rows,
        middle_grad,
        gain_mix_row,
        normed_one_cols,
        normed_two_cols,
        ct_cols,
        middle_cols,
        ffn_all,
    )
    small = small.astype(jnp.float32)
    smalls, at = [], 0
    for size in sizes[:-2]:
        smalls.append(small[at : at + size])
        at += size
    gains = gains[: sum(sizes[-2:])].reshape(2, width)
    return (
        layer_out.reshape(tokens.shape),
        tokens_grad.reshape(tokens.shape),
        gains[0],
        grad_inproj,
        smalls[0],
        smalls[1][0],
        jnp.transpose(smalls[6]),
        smalls[5],
        smalls[2][0],
        jnp.transpose(smalls[3]),
        smalls[4][0],
        grad_outproj,
        gains[1],
        grad_gateup,
        grad_downproj,
    )


def solution(mesh):
    in_specs = (
        P("dp", "ctx", None),
        P(),
        P(None, ("dp", "ctx"), "tp"),
        P(None, "tp"),
        P("tp"),
        P("tp", None),
        P(None, "tp"),
        P("tp"),
        P("tp", None),
        P("tp"),
        P("tp", ("dp", "ctx")),
        P(),
        P(None, ("dp", "ctx"), "tp"),
        P("tp", ("dp", "ctx")),
        P("dp", "ctx", None),
    )
    out_specs = (
        P("dp", "ctx", None),
        P("dp", "ctx", None),
        P(),
        P(None, ("dp", "ctx"), "tp"),
        P(None, "tp"),
        P("tp"),
        P("tp", None),
        P(None, "tp"),
        P("tp"),
        P("tp", None),
        P("tp"),
        P("tp", ("dp", "ctx")),
        P(),
        P(None, ("dp", "ctx"), "tp"),
        P("tp", ("dp", "ctx")),
    )
    return jax.shard_map(
        per_device, mesh=mesh, in_specs=in_specs, out_specs=out_specs, check_vma=False
    )
```

```python
import functools
import math

import jax
import jax.numpy as jnp
from jax import lax
from jax.experimental import pallas as pl
from jax.experimental.pallas import tpu as pltpu
from jax.sharding import PartitionSpec as P

EPSILON = 1e-05
LOG2E = math.log2(math.e)
LN2 = math.log(2.0)
SUB = 8
LANE = 128
PLANE = ("dp", "ctx")


def passed_along(value, axis, steps):
    count = lax.axis_size(axis)
    first, last = (max(0, -steps), min(count, count - steps))
    return lax.ppermute(value, axis, [(source, source + steps) for source in range(first, last)])


def matmul(left, right):
    return jnp.dot(left, right, preferred_element_type=jnp.float32)


def matmul_nt(left, right):
    return lax.dot_general(
        left, right, (((1,), (1,)), ((), ())), preferred_element_type=jnp.float32
    )


def matmul_tn(left, right):
    return lax.dot_general(
        left, right, (((0,), (0,)), ((), ())), preferred_element_type=jnp.float32
    )


def inverse_rms(values):
    return lax.rsqrt(jnp.mean(values * values, -1, keepdims=True) + EPSILON)


def silu_slope(values):
    logistic = jax.nn.sigmoid(values)
    return logistic * (1.0 + values * (1.0 - logistic))


def norm_back(grad_norm, values, scale, gain):
    scaled_grad = grad_norm * gain
    unit_rows = values * scale
    return scale * (scaled_grad - unit_rows * jnp.mean(scaled_grad * unit_rows, -1, keepdims=True))


def stage_in(ref, group, held):
    for tile in range(held.shape[0] // SUB):
        held[pl.ds(tile * SUB, SUB), :] = ref[
            pl.ds(pl.multiple_of(group * SUB, SUB), SUB), pl.ds(tile * LANE, LANE)
        ]


def stage_out(held, ref, group):
    for tile in range(held.shape[0] // SUB):
        ref[pl.ds(pl.multiple_of(group * SUB, SUB), SUB), pl.ds(tile * LANE, LANE)] = held[
            pl.ds(tile * SUB, SUB), :
        ]


def token_row(held, at, tiles):
    return held[pl.ds(at, tiles, stride=SUB), :]


def ends_kernel(
    n_state,
    tiles,
    groups,
    reverse,
    step_ref,
    drive_ref,
    rows_ref,
    rate_ref,
    end_ref,
    step_held,
    drive_held,
):
    base = pl.program_id(0) * groups * SUB * n_state
    rates = [rate_ref[n] for n in range(n_state)]

    def one(turn, states):
        group = groups - 1 - turn if reverse else turn
        order = range(SUB - 1, -1, -1) if reverse else range(SUB)
        states = list(states)
        stage_in(step_ref, group, step_held)
        stage_in(drive_ref, group, drive_held)
        for at in order:
            step = token_row(step_held, at, tiles)
            drive = token_row(drive_held, at, tiles)
            if not reverse:
                drive = drive * step
            for n in range(n_state):
                row = rows_ref[base + (group * SUB + at) * n_state + n]
                decay = jnp.exp2(step * rates[n])
                if reverse:
                    states[n] = decay * (states[n] + drive * row)
                else:
                    states[n] = decay * states[n] + drive * row
        return tuple(states)

    zero = jnp.zeros((tiles, LANE), jnp.float32)
    states = lax.fori_loop(0, groups, one, (zero,) * n_state)
    for n in range(n_state):
        end_ref[0, n] = states[n]


def scan_ends(step, drive, rows, rate, seqs, reverse):
    n_state, tiles, _ = rate.shape
    groups = step.shape[0] // seqs // SUB
    rows_spec = pl.BlockSpec((groups * SUB, tiles * LANE), lambda s: (s, 0))
    held = pltpu.VMEM((tiles * SUB, LANE), jnp.float32)
    return pl.pallas_call(
        functools.partial(ends_kernel, n_state, tiles, groups, reverse),
        grid=(seqs,),
        in_specs=[
            rows_spec,
            rows_spec,
            pl.BlockSpec(memory_space=pltpu.SMEM),
            pl.BlockSpec((n_state, tiles, LANE), lambda s: (0, 0, 0)),
        ],
        out_specs=pl.BlockSpec((1, n_state, tiles, LANE), lambda s: (s, 0, 0, 0)),
        out_shape=jax.ShapeDtypeStruct((seqs, n_state, tiles, LANE), jnp.float32),
        scratch_shapes=[held, held],
        compiler_params=pltpu.CompilerParams(vmem_limit_bytes=32 * 2**20),
    )(step, drive, rows, rate)


def forward_kernel(
    n_state,
    tiles,
    groups,
    blocks,
    start_ref,
    step_ref,
    input_ref,
    brow_ref,
    crow_ref,
    rate_ref,
    prior_ref,
    mixed_ref,
    carried,
    step_held,
    input_held,
    mixed_held,
):
    base = (pl.program_id(0) * blocks + pl.program_id(1)) * groups * SUB * n_state

    @pl.when(pl.program_id(1) == 0)
    def _():
        carried[...] = start_ref[0]

    def one(group, states):
        states = list(states)
        stage_in(step_ref, group, step_held)
        stage_in(input_ref, group, input_held)
        for at in range(SUB):
            step = token_row(step_held, at, tiles)
            drive = step * token_row(input_held, at, tiles)
            mixed = [None] * 2
            for n in range(n_state):
                where = base + (group * SUB + at) * n_state + n
                prior_ref[group * SUB + at, n] = states[n]
                decay = jnp.exp2(step * rate_ref[n])
                states[n] = decay * states[n] + drive * brow_ref[where]
                term = states[n] * crow_ref[where]
                mixed[n % 2] = term if mixed[n % 2] is None else mixed[n % 2] + term
            mixed_held[pl.ds(at, tiles, stride=SUB), :] = mixed[0] + mixed[1]
        stage_out(mixed_held, mixed_ref, group)
        return tuple(states)

    states = lax.fori_loop(0, groups, one, tuple(carried[n] for n in range(n_state)))
    for n in range(n_state):
        carried[n] = states[n]


def scan_forward(start, step, inputs, b_rows, c_rows, rate, seqs):
    n_state, tiles, _ = rate.shape
    all_groups = step.shape[0] // SUB
    groups = math.gcd(all_groups // seqs, 4)
    blocks = all_groups // seqs // groups
    rows_spec = pl.BlockSpec((groups * SUB, tiles * LANE), lambda s, b: (s * blocks + b, 0))
    held = pltpu.VMEM((tiles * SUB, LANE), jnp.float32)
    smem = pl.BlockSpec(memory_space=pltpu.SMEM)
    tokens = all_groups * SUB
    return pl.pallas_call(
        functools.partial(forward_kernel, n_state, tiles, groups, blocks),
        grid=(seqs, blocks),
        in_specs=[
            pl.BlockSpec((1, n_state, tiles, LANE), lambda s, b: (s, 0, 0, 0)),
            rows_spec,
            rows_spec,
            smem,
            smem,
            pl.BlockSpec((n_state, tiles, LANE), lambda s, b: (0, 0, 0)),
        ],
        out_specs=[
            pl.BlockSpec(
                (groups * SUB, n_state, tiles, LANE), lambda s, b: (s * blocks + b, 0, 0, 0)
            ),
            rows_spec,
        ],
        out_shape=[
            jax.ShapeDtypeStruct((tokens, n_state, tiles, LANE), jnp.float32),
            jax.ShapeDtypeStruct(step.shape, jnp.float32),
        ],
        scratch_shapes=[pltpu.VMEM((n_state, tiles, LANE), jnp.float32)] + [held] * 3,
        compiler_params=pltpu.CompilerParams(vmem_limit_bytes=32 * 2**20),
    )(start, step, inputs, b_rows, c_rows, rate)


def backward_kernel(
    n_state,
    tiles,
    groups,
    blocks,
    end_ref,
    prior_ref,
    step_ref,
    input_ref,
    ograd_ref,
    brow_ref,
    crow_ref,
    rate_ref,
    picks_ref,
    step_grad_ref,
    input_grad_ref,
    rate_grad_ref,
    part_ref,
    carried,
    step_held,
    input_held,
    ograd_held,
    step_grad_held,
    input_grad_held,
):
    block = blocks - 1 - pl.program_id(1)
    base = (pl.program_id(0) * blocks + block) * groups * SUB * n_state

    @pl.when(pl.program_id(1) == 0)
    def _():
        carried[...] = end_ref[0]

    @pl.when((pl.program_id(0) == 0) & (pl.program_id(1) == 0))
    def _():
        rate_grad_ref[...] = jnp.zeros_like(rate_grad_ref)

    def one(turn, grads):
        group = groups - 1 - turn
        grads = list(grads)
        stage_in(step_ref, group, step_held)
        stage_in(input_ref, group, input_held)
        stage_in(ograd_ref, group, ograd_held)
        for at in range(SUB - 1, -1, -1):
            step = token_row(step_held, at, tiles)
            value = token_row(input_held, at, tiles)
            ograd = token_row(ograd_held, at, tiles)
            drive = step * value
            along_b = None
            along_rate = None
            brow_parts, crow_parts = [], []
            for n in range(n_state):
                where = base + (group * SUB + at) * n_state + n
                brow, crow = brow_ref[where], crow_ref[where]
                rate = rate_ref[n]
                decay = jnp.exp2(step * rate)
                grad = ograd * crow + grads[n]
                kept = decay * prior_ref[group * SUB + at, n]
                state = kept + drive * brow
                decay_term = grad * kept
                grads[n] = decay * grad
                rate_grad_ref[n] += decay_term * step
                by_rate, by_brow = decay_term * rate, grad * brow
                along_rate = by_rate if along_rate is None else along_rate + by_rate
                along_b = by_brow if along_b is None else along_b + by_brow
                brow_parts.append(grad * drive)
                crow_parts.append(ograd * state)
            step_grad_held[pl.ds(at, tiles, stride=SUB), :] = along_rate * LN2 + along_b * value
            input_grad_held[pl.ds(at, tiles, stride=SUB), :] = along_b * step
            parts = jnp.concatenate(brow_parts + crow_parts, 0).astype(jnp.bfloat16)
            part_ref[group * SUB + at] = jnp.dot(
                picks_ref[...], parts, preferred_element_type=jnp.float32
            )
        stage_out(step_grad_held, step_grad_ref, group)
        stage_out(input_grad_held, input_grad_ref, group)
        return tuple(grads)

    grads = lax.fori_loop(0, groups, one, tuple(carried[n] for n in range(n_state)))
    for n in range(n_state):
        carried[n] = grads[n]


def scan_backward(end_grad, prior, step, inputs, ograd, b_rows, c_rows, rate, seqs):
    n_state, tiles, _ = rate.shape
    all_groups = step.shape[0] // SUB
    groups = math.gcd(all_groups // seqs, 4)
    blocks = all_groups // seqs // groups

    def at(s, b):
        return s * blocks + blocks - 1 - b

    rows_spec = pl.BlockSpec((groups * SUB, tiles * LANE), lambda s, b: (at(s, b), 0))
    held = pltpu.VMEM((tiles * SUB, LANE), jnp.float32)
    smem = pl.BlockSpec(memory_space=pltpu.SMEM)
    tokens = all_groups * SUB
    picks = jnp.repeat(jnp.eye(2 * n_state, dtype=jnp.bfloat16), tiles, 1)
    return pl.pallas_call(
        functools.partial(backward_kernel, n_state, tiles, groups, blocks),
        grid=(seqs, blocks),
        in_specs=[
            pl.BlockSpec((1, n_state, tiles, LANE), lambda s, b: (s, 0, 0, 0)),
            pl.BlockSpec((groups * SUB, n_state, tiles, LANE), lambda s, b: (at(s, b), 0, 0, 0)),
            rows_spec,
            rows_spec,
            rows_spec,
            smem,
            smem,
            pl.BlockSpec((n_state, tiles, LANE), lambda s, b: (0, 0, 0)),
            pl.BlockSpec(picks.shape, lambda s, b: (0, 0)),
        ],
        out_specs=[
            rows_spec,
            rows_spec,
            pl.BlockSpec((n_state, tiles, LANE), lambda s, b: (0, 0, 0)),
            pl.BlockSpec((groups * SUB, 2 * n_state, LANE), lambda s, b: (at(s, b), 0, 0)),
        ],
        out_shape=[
            jax.ShapeDtypeStruct(step.shape, jnp.float32),
            jax.ShapeDtypeStruct(step.shape, jnp.float32),
            jax.ShapeDtypeStruct(rate.shape, jnp.float32),
            jax.ShapeDtypeStruct((tokens, 2 * n_state, LANE), jnp.float32),
        ],
        scratch_shapes=[pltpu.VMEM((n_state, tiles, LANE), jnp.float32)] + [held] * 5,
        compiler_params=pltpu.CompilerParams(vmem_limit_bytes=32 * 2**20),
    )(end_grad, prior, step, inputs, ograd, b_rows, c_rows, rate, picks)


def from_earlier(ends, decay, steps):
    count = lax.axis_size("ctx")
    if count == 1:
        return jnp.zeros_like(ends)
    if count == 2:
        return passed_along(ends, "ctx", steps)
    index = lax.axis_index("ctx")
    all_ends = lax.all_gather(ends, "ctx")
    all_decays = lax.all_gather(decay, "ctx")

    def one(turn, state):
        at = turn if steps > 0 else count - 1 - turn
        reached = at < index if steps > 0 else at > index
        return jnp.where(reached, all_decays[at] * state + all_ends[at], state)

    return lax.fori_loop(0, count, one, jnp.zeros_like(ends))


def gathered_rows(rows):
    return lax.all_gather(rows, PLANE, axis=0, tiled=True)


def swapped_columns(rows):
    return lax.all_to_all(rows, PLANE, split_axis=1, concat_axis=0, tiled=True)


def place_in(axes):
    index = 0
    for axis in axes:
        index = index * lax.axis_size(axis) + lax.axis_index(axis)
    return index


def device_at(axes, index):
    where = {}
    for axis in reversed(axes):
        size = lax.axis_size(axis)
        where[axis] = lax.rem(index, size)
        index = lax.div(index, size)
    return where


def greet(groups):
    barrier = pltpu.get_barrier_semaphore()
    total = 0
    for axes, others in groups:
        for other in others:
            pl.semaphore_signal(
                barrier,
                inc=1,
                device_id=device_at(axes, other),
                device_id_type=pl.DeviceIdType.MESH,
            )
            total += 1
    pl.semaphore_wait(barrier, total)


def sent(source, target, send_sem, recv_sem, where):
    copy = pltpu.make_async_remote_copy(
        src_ref=source,
        dst_ref=target,
        send_sem=send_sem,
        recv_sem=recv_sem,
        device_id=where,
        device_id_type=pl.DeviceIdType.MESH,
    )
    copy.start()
    return copy


def finish(copies):
    for copy in copies:
        copy.wait()


def rows_of(ref, index, count):
    rows = ref.shape[0] // count
    return ref.at[pl.ds(pl.multiple_of(index * rows, rows), rows), :]


class Group:
    def __init__(self, axes, send_sem, recv_sem):
        self.axes = axes
        self.count = math.prod(lax.axis_size(axis) for axis in axes)
        self.me = place_in(axes)
        self.others = [lax.rem(self.me + hop, self.count) for hop in range(1, self.count)]
        self.send_sem, self.recv_sem = send_sem, recv_sem

    def own(self, ref):
        return rows_of(ref, self.me, self.count)

    def one(self, source, target, which, hop):
        return sent(
            source,
            target,
            self.send_sem.at[which, hop],
            self.recv_sem.at[which, hop],
            device_at(self.axes, self.others[hop]),
        )

    def scatter(self, part, slot, which):
        return [
            self.one(rows_of(part, other, self.count), slot.at[hop], which, hop)
            for hop, other in enumerate(self.others)
        ]

    def total(self, part, slot):
        total = self.own(part)[...].astype(jnp.float32)
        for hop in range(self.count - 1):
            total = total + slot[hop].astype(jnp.float32)
        return total

    def spread(self, ref, which):
        return [self.one(self.own(ref), self.own(ref), which, hop) for hop in range(self.count - 1)]


def slots_for(part, count):
    return pltpu.VMEM((count - 1, part.shape[0] // count) + part.shape[1:], part.dtype)


def group_size(axes):
    return math.prod(lax.axis_size(axis) for axis in axes)


class Swap:
    def __init__(self, arrays, swapped, send_sem, recv_sem, local_sem):
        plane = Group(PLANE, send_sem, recv_sem)
        self.plane, self.arrays, self.swapped, self.local_sem = plane, arrays, swapped, local_sem

    def begin(self):
        self.copies, plane = [], self.plane
        for which, (array, swapped) in enumerate(zip(self.arrays, self.swapped)):
            share = swapped.shape[1]

            def columns(index):
                return array.at[:, pl.ds(pl.multiple_of(index * share, share), share)]

            for hop, other in enumerate(plane.others):
                self.copies.append(plane.one(columns(other), plane.own(swapped), which, hop))
            local = pltpu.make_async_copy(
                columns(plane.me), plane.own(swapped), self.local_sem.at[which]
            )
            local.start()
            self.copies.append(local)

    def end(self):
        finish(self.copies)


def swap_scratch(arrays):
    sems = pltpu.SemaphoreType.DMA((len(arrays), group_size(PLANE) - 1))
    return [sems, sems, pltpu.SemaphoreType.DMA((len(arrays),))] if arrays else []


def swap_shapes(arrays):
    count = group_size(PLANE)
    return [
        jax.ShapeDtypeStruct((array.shape[0] * count, array.shape[1] // count), array.dtype)
        for array in arrays
    ]


def swaps_in_kernels(width):
    return width // group_size(PLANE) % LANE == 0


def sum_kernel(n_rows, n_swaps, n_gathers, part, *refs):
    own_rows, refs = refs[:n_rows], refs[n_rows:]
    arrays, refs = refs[:n_swaps], refs[n_swaps:]
    shards, refs = refs[:n_gathers], refs[n_gathers:]
    total, refs = refs[0], refs[1:]
    all_rows, refs = refs[:n_rows], refs[n_rows:]
    swapped, refs = refs[:n_swaps], refs[n_swaps:]
    gathered, refs = refs[:n_gathers], refs[n_gathers:]
    slots, send_sem, recv_sem, *refs = refs
    group = Group(("tp",), send_sem, recv_sem)
    greeted = [(("tp",), group.others)]
    if n_swaps:
        swap = Swap(arrays, swapped, *refs[:3])
        greeted.append((PLANE, swap.plane.others))
        refs = refs[3:]
    if n_gathers:
        gather = PlaneGather(shards[0], gathered[0], *refs[:2])
        if not n_swaps:
            greeted.append((PLANE, gather.others))
    greet(greeted)
    copies = group.scatter(part, slots, 0)
    if n_swaps:
        swap.begin()
    if n_gathers:
        gather.begin(refs[2])
    spreads = []
    for which, (own, everything) in enumerate(zip(own_rows, all_rows)):
        group.own(everything)[...] = own[...]
        spreads += group.spread(everything, 2 + which)
    finish(copies)
    group.own(total)[...] = group.total(part, slots).astype(total.dtype)
    copies = group.spread(total, 1)
    if n_gathers:
        gather.relay()
        gather.hand_over()
    finish(copies)
    finish(spreads)
    if n_swaps:
        swap.end()
    if n_gathers:
        gather.hand_over_last()
        gather.end()


def gathered_shape(shard):
    return jax.ShapeDtypeStruct(
        (shard.shape[0] * group_size(PLANE),) + shard.shape[1:], shard.dtype
    )


def gather_scratch():
    return [gather_sems(), gather_sems(), pltpu.SemaphoreType.DMA(())]


def sum_over_tp(call_id, part, own_rows, arrays, shards):
    count = group_size(("tp",))
    vmem = pl.BlockSpec(memory_space=pltpu.VMEM)
    hbm = pl.BlockSpec(memory_space=pl.ANY)
    operands = [part, *own_rows, *arrays]
    sems = pltpu.SemaphoreType.DMA((2 + len(own_rows), count - 1))
    return pl.pallas_call(
        functools.partial(sum_kernel, len(own_rows), len(arrays), len(shards)),
        in_specs=[vmem] * len(operands) + [hbm] * len(shards),
        out_specs=[vmem] * len(operands) + [hbm] * len(shards),
        out_shape=[jax.ShapeDtypeStruct(part.shape, part.dtype)]
        + [
            jax.ShapeDtypeStruct((own.shape[0] * count,) + own.shape[1:], own.dtype)
            for own in own_rows
        ]
        + swap_shapes(arrays)
        + [gathered_shape(shard) for shard in shards],
        scratch_shapes=[slots_for(part, count), sems, sems]
        + swap_scratch(arrays)
        + gather_scratch() * len(shards),
        compiler_params=pltpu.CompilerParams(
            collective_id=call_id, has_side_effects=True, vmem_limit_bytes=40 * 2**20
        ),
    )(*operands, *shards)


def mixer_out_kernel(
    gated, out_first, out_last, tokens, gain, normed, middle, part, slots, send_sem, recv_sem
):
    group = Group(("tp",), send_sem, recv_sem)
    half = gated.shape[1] // 2
    share = out_first.shape[1]
    greet([(("tp",), group.others)])
    for at in range(out_first.shape[0] // half):
        rows = slice(at * half, (at + 1) * half)
        part[:, at * share : (at + 1) * share] = (
            matmul(gated[:, :half], out_first[rows, :])
            + matmul(gated[:, half:], out_last[rows, :])
        ).astype(part.dtype)
    finish(group.scatter(part, slots, 0))
    rows = group.own(tokens)[...].astype(jnp.float32) + group.total(part, slots)
    middle[...] = rows
    group.own(normed)[...] = (rows * inverse_rms(rows) * gain[...].astype(jnp.float32)).astype(
        normed.dtype
    )
    finish(group.spread(normed, 1))


def mixer_out(call_id, gated, out_first, out_last, tokens, gain):
    count = group_size(("tp",))
    vmem = pl.BlockSpec(memory_space=pltpu.VMEM)
    rows, width = tokens.shape
    part = jax.ShapeDtypeStruct((rows, width), jnp.bfloat16)
    sems = pltpu.SemaphoreType.DMA((2, count - 1))
    return pl.pallas_call(
        mixer_out_kernel,
        in_specs=[vmem] * 5,
        out_specs=[vmem] * 2,
        out_shape=[part, jax.ShapeDtypeStruct((rows // count, width), jnp.float32)],
        scratch_shapes=[pltpu.VMEM(part.shape, part.dtype), slots_for(part, count), sems, sems],
        compiler_params=pltpu.CompilerParams(
            collective_id=call_id, has_side_effects=True, vmem_limit_bytes=40 * 2**20
        ),
    )(gated, out_first, out_last, tokens, gain)


def ffn_back_kernel(n_swaps, part, ct, middle, gain, out_first, out_last, *refs):
    arrays, refs = refs[:n_swaps], refs[n_swaps:]
    middle_low, middle_grad, gain_grad, gated_grad, *refs = refs
    swapped, refs = refs[:n_swaps], refs[n_swaps:]
    slots, send_sem, recv_sem, *refs = refs
    group = Group(("tp",), send_sem, recv_sem)
    if n_swaps:
        swap = Swap(arrays, swapped, *refs)
        greet([(("tp",), group.others), (PLANE, swap.plane.others)])
    else:
        greet([(("tp",), group.others)])
    copies = group.scatter(part, slots, 0)
    if n_swaps:
        swap.begin()
    finish(copies)
    normed_grad = group.total(part, slots)
    rows = middle[...]
    scale = inverse_rms(rows)
    gain_grad[...] = jnp.sum(normed_grad * rows * scale, 0, keepdims=True)
    grad = group.own(ct)[...].astype(jnp.float32) + norm_back(
        normed_grad, rows, scale, gain[...].astype(jnp.float32)
    )
    middle_grad[...] = grad
    group.own(middle_low)[...] = grad.astype(middle_low.dtype)
    finish(group.spread(middle_low, 1))
    half = gated_grad.shape[1] // 2
    share = out_first.shape[1]
    for side, weights in enumerate((out_first, out_last)):
        total = None
        for at in range(weights.shape[0] // half):
            one = matmul_nt(
                middle_low[:, at * share : (at + 1) * share],
                weights[at * half : (at + 1) * half, :],
            )
            total = one if total is None else total + one
        gated_grad[:, side * half : (side + 1) * half] = total
    if n_swaps:
        swap.end()


def ffn_back(call_id, part, ct, middle, gain, out_first, out_last, arrays):
    count = group_size(("tp",))
    vmem = pl.BlockSpec(memory_space=pltpu.VMEM)
    rows, width = part.shape
    inner = 2 * out_first.shape[0] // group_size(PLANE)
    sems = pltpu.SemaphoreType.DMA((2, count - 1))
    return pl.pallas_call(
        functools.partial(ffn_back_kernel, len(arrays)),
        in_specs=[vmem] * (6 + len(arrays)),
        out_specs=[vmem] * (4 + len(arrays)),
        out_shape=[
            jax.ShapeDtypeStruct((rows, width), jnp.bfloat16),
            jax.ShapeDtypeStruct((rows // count, width), jnp.float32),
            jax.ShapeDtypeStruct((1, width), jnp.float32),
            jax.ShapeDtypeStruct((rows, inner), jnp.float32),
        ]
        + swap_shapes(arrays),
        scratch_shapes=[slots_for(part, count), sems, sems] + swap_scratch(arrays),
        compiler_params=pltpu.CompilerParams(
            collective_id=call_id, has_side_effects=True, vmem_limit_bytes=48 * 2**20
        ),
    )(part, ct, middle, gain, out_first, out_last, *arrays)


def send_on(source, target, send_sem, recv_sem, ctx):
    return pltpu.make_async_remote_copy(
        src_ref=source,
        dst_ref=target,
        send_sem=send_sem,
        recv_sem=recv_sem,
        device_id={"ctx": ctx},
        device_id_type=pl.DeviceIdType.MESH,
    )


def forward_pair_kernel(
    n_state,
    tiles,
    groups,
    blocks,
    seqs,
    step_ref,
    input_ref,
    brow_ref,
    crow_ref,
    rate_ref,
    shard,
    prior_ref,
    mixed_ref,
    gathered,
    carried,
    ends,
    starts,
    prior_buf,
    step_held,
    input_held,
    mixed_held,
    prior_sem,
    send_sem,
    recv_sem,
    gather_send,
    gather_recv,
    local_sem,
):
    place = lax.axis_index("ctx")
    gather = PlaneGather(shard, gathered, gather_send, gather_recv)
    greet([(PLANE, gather.others)])
    gather.begin(local_sem)

    def hand_on(seq):
        return send_on(ends.at[seq], starts.at[seq], send_sem.at[seq], recv_sem.at[seq], 1)

    def store(block):
        slot = lax.rem(block, 2)
        rows = groups * SUB
        return pltpu.make_async_copy(
            prior_buf.at[slot],
            prior_ref.at[pl.ds(pl.multiple_of(block * rows, rows), rows)],
            prior_sem.at[slot],
        )

    def one_sequence(seq):
        @pl.when(place == 0)
        def _():
            carried[...] = jnp.zeros_like(carried)

        @pl.when(place == 1)
        def _():
            hand_on(seq).wait_recv()
            carried[...] = starts[seq]

        @pl.loop(0, blocks)
        def _(inner_block):
            block = seq * blocks + inner_block
            slot = lax.rem(block, 2)

            @pl.when(block >= 2)
            def _():
                store(block - 2).wait()

            def one(turn, states):
                group = block * groups + turn
                states = list(states)
                stage_in(step_ref, group, step_held)
                stage_in(input_ref, group, input_held)
                for at in range(SUB):
                    step = token_row(step_held, at, tiles)
                    drive = step * token_row(input_held, at, tiles)
                    mixed = [None] * 2
                    for n in range(n_state):
                        where = (group * SUB + at) * n_state + n
                        prior_buf[slot, turn * SUB + at, n] = states[n]
                        decay = jnp.exp2(step * rate_ref[n])
                        states[n] = decay * states[n] + drive * brow_ref[where]
                        term = states[n] * crow_ref[where]
                        mixed[n % 2] = term if mixed[n % 2] is None else mixed[n % 2] + term
                    mixed_held[pl.ds(at, tiles, stride=SUB), :] = mixed[0] + mixed[1]
                stage_out(mixed_held, mixed_ref, group)
                return tuple(states)

            states = lax.fori_loop(0, groups, one, tuple(carried[n] for n in range(n_state)))
            for n in range(n_state):
                carried[n] = states[n]
            store(block).start()

        @pl.when(place == 0)
        def _():
            ends[seq] = carried[...]
            hand_on(seq).start()

    for seq in range(seqs):
        one_sequence(seq)
        if seq == 0:
            gather.relay()
            gather.hand_over()
    gather.hand_over_last()
    for block in range(max(0, seqs * blocks - 2), seqs * blocks):
        store(block).wait()

    @pl.when(place == 0)
    def _():
        for seq in range(seqs):
            hand_on(seq).wait_send()

    gather.end()


def scan_forward_pair(call_id, step, inputs, b_rows, c_rows, rate, seqs, shard):
    n_state, tiles, _ = rate.shape
    tokens, inner = step.shape
    all_groups = tokens // SUB
    groups = math.gcd(all_groups // seqs, 4)
    blocks = all_groups // seqs // groups
    vmem = pl.BlockSpec(memory_space=pltpu.VMEM)
    smem = pl.BlockSpec(memory_space=pltpu.SMEM)
    hbm = pl.BlockSpec(memory_space=pl.ANY)
    full = jnp.float32
    held = pltpu.VMEM((tiles * SUB, LANE), full)
    boundary = pltpu.VMEM((seqs, n_state, tiles, LANE), full)
    dma = pltpu.SemaphoreType.DMA
    return pl.pallas_call(
        functools.partial(forward_pair_kernel, n_state, tiles, groups, blocks, seqs),
        in_specs=[vmem, vmem, smem, smem, vmem, hbm],
        out_specs=[hbm, vmem, hbm],
        out_shape=[
            jax.ShapeDtypeStruct((tokens, n_state, tiles, LANE), full),
            jax.ShapeDtypeStruct(step.shape, full),
            gathered_shape(shard),
        ],
        scratch_shapes=[
            pltpu.VMEM((n_state, tiles, LANE), full),
            boundary,
            boundary,
            pltpu.VMEM((2, groups * SUB, n_state, tiles, LANE), full),
            held,
            held,
            held,
            dma((2,)),
            dma((seqs,)),
            dma((seqs,)),
        ]
        + gather_scratch(),
        compiler_params=pltpu.CompilerParams(
            collective_id=call_id, has_side_effects=True, vmem_limit_bytes=40 * 2**20
        ),
    )(step, inputs, b_rows, c_rows, rate, shard)


def backward_pair_kernel(
    n_state,
    tiles,
    groups,
    blocks,
    seqs,
    step_ref,
    input_ref,
    ograd_ref,
    brow_ref,
    crow_ref,
    rate_ref,
    picks_ref,
    ffn_part,
    middle,
    prior_ref,
    step_grad_ref,
    input_grad_ref,
    rate_grad_ref,
    part_ref,
    layer_rows,
    carried,
    ends,
    starts,
    prior_buf,
    step_held,
    input_held,
    ograd_held,
    step_grad_held,
    input_grad_held,
    ffn_slots,
    prior_sem,
    send_sem,
    recv_sem,
    tp_send,
    tp_recv,
):
    place = lax.axis_index("ctx")
    tp = Group(("tp",), tp_send, tp_recv)
    greet([(("ctx",), [1 - place]), (("tp",), tp.others)])
    ffn_sent = tp.scatter(ffn_part, ffn_slots, 0)

    def hand_on(seq):
        return send_on(ends.at[seq], starts.at[seq], send_sem.at[seq], recv_sem.at[seq], 0)

    def fetch(turn):
        seq = lax.div(turn, blocks)
        block = seq * blocks + blocks - 1 - lax.rem(turn, blocks)
        slot = lax.rem(turn, 2)
        rows = groups * SUB
        return pltpu.make_async_copy(
            prior_ref.at[pl.ds(pl.multiple_of(block * rows, rows), rows)],
            prior_buf.at[slot],
            prior_sem.at[slot],
        )

    fetch(0).start()
    rate_grad_ref[...] = jnp.zeros_like(rate_grad_ref)

    @pl.when(place == 1)
    def _():
        @pl.loop(0, seqs)
        def _(seq):
            def one(turn, grads):
                group = (seq + 1) * blocks * groups - 1 - turn
                grads = list(grads)
                stage_in(step_ref, group, step_held)
                stage_in(ograd_ref, group, ograd_held)
                for at in range(SUB - 1, -1, -1):
                    step = token_row(step_held, at, tiles)
                    ograd = token_row(ograd_held, at, tiles)
                    for n in range(n_state):
                        row = crow_ref[(group * SUB + at) * n_state + n]
                        grads[n] = jnp.exp2(step * rate_ref[n]) * (grads[n] + ograd * row)
                return tuple(grads)

            zero = jnp.zeros((tiles, LANE), jnp.float32)
            grads = lax.fori_loop(0, blocks * groups, one, (zero,) * n_state)
            for n in range(n_state):
                ends[seq, n] = grads[n]
            hand_on(seq).start()

    @pl.loop(0, seqs)
    def _(seq):
        @pl.when(place == 1)
        def _():
            carried[...] = jnp.zeros_like(carried)

        @pl.when(place == 0)
        def _():
            hand_on(seq).wait_recv()
            carried[...] = starts[seq]

        @pl.loop(0, blocks)
        def _(inner_block):
            turn = seq * blocks + inner_block
            slot = lax.rem(turn, 2)
            first_group = (seq * blocks + blocks - 1 - inner_block) * groups

            @pl.when(turn + 1 < seqs * blocks)
            def _():
                fetch(turn + 1).start()

            fetch(turn).wait()

            def one(back, grads):
                inner_group = groups - 1 - back
                group = first_group + inner_group
                grads = list(grads)
                stage_in(step_ref, group, step_held)
                stage_in(input_ref, group, input_held)
                stage_in(ograd_ref, group, ograd_held)
                for at in range(SUB - 1, -1, -1):
                    step = token_row(step_held, at, tiles)
                    value = token_row(input_held, at, tiles)
                    ograd = token_row(ograd_held, at, tiles)
                    drive = step * value
                    along_b = None
                    along_rate = None
                    brow_parts, crow_parts = [], []
                    for n in range(n_state):
                        where = (group * SUB + at) * n_state + n
                        brow, crow = brow_ref[where], crow_ref[where]
                        rate = rate_ref[n]
                        decay = jnp.exp2(step * rate)
                        grad = ograd * crow + grads[n]
                        kept = decay * prior_buf[slot, inner_group * SUB + at, n]
                        state = kept + drive * brow
                        decay_term = grad * kept
                        grads[n] = decay * grad
                        rate_grad_ref[n] += decay_term * step
                        by_rate, by_brow = decay_term * rate, grad * brow
                        along_rate = by_rate if along_rate is None else along_rate + by_rate
                        along_b = by_brow if along_b is None else along_b + by_brow
                        brow_parts.append(grad * drive)
                        crow_parts.append(ograd * state)
                    step_grad_held[pl.ds(at, tiles, stride=SUB), :] = (
                        along_rate * LN2 + along_b * value
                    )
                    input_grad_held[pl.ds(at, tiles, stride=SUB), :] = along_b * step
                    parts = jnp.concatenate(brow_parts + crow_parts, 0).astype(jnp.bfloat16)
                    part_ref[group * SUB + at] = jnp.dot(
                        picks_ref[...], parts, preferred_element_type=jnp.float32
                    )
                stage_out(step_grad_held, step_grad_ref, group)
                stage_out(input_grad_held, input_grad_ref, group)
                return tuple(grads)

            grads = lax.fori_loop(0, groups, one, tuple(carried[n] for n in range(n_state)))
            for n in range(n_state):
                carried[n] = grads[n]

    finish(ffn_sent)
    layer_rows[...] = (middle[...] + tp.total(ffn_part, ffn_slots)).astype(layer_rows.dtype)

    @pl.when(place == 1)
    def _():
        @pl.loop(0, seqs)
        def _(seq):
            hand_on(seq).wait_send()


def scan_backward_pair(
    call_id, prior, step, inputs, ograd, b_rows, c_rows, rate, seqs, ffn_part, middle
):
    n_state, tiles, _ = rate.shape
    tokens, inner = step.shape
    all_groups = tokens // SUB
    groups = math.gcd(all_groups // seqs, 4)
    blocks = all_groups // seqs // groups
    tp_count = group_size(("tp",))
    vmem = pl.BlockSpec(memory_space=pltpu.VMEM)
    smem = pl.BlockSpec(memory_space=pltpu.SMEM)
    full = jnp.float32
    held = pltpu.VMEM((tiles * SUB, LANE), full)
    boundary = pltpu.VMEM((seqs, n_state, tiles, LANE), full)
    dma = pltpu.SemaphoreType.DMA
    picks = jnp.repeat(jnp.eye(2 * n_state, dtype=jnp.bfloat16), tiles, 1)
    return pl.pallas_call(
        functools.partial(backward_pair_kernel, n_state, tiles, groups, blocks, seqs),
        in_specs=[vmem] * 3 + [smem] * 2 + [vmem] * 4 + [pl.BlockSpec(memory_space=pl.ANY)],
        out_specs=[vmem] * 5,
        out_shape=[
            jax.ShapeDtypeStruct(step.shape, full),
            jax.ShapeDtypeStruct(step.shape, full),
            jax.ShapeDtypeStruct(rate.shape, full),
            jax.ShapeDtypeStruct((tokens, 2 * n_state, LANE), full),
            jax.ShapeDtypeStruct(middle.shape, jnp.bfloat16),
        ],
        scratch_shapes=[
            pltpu.VMEM((n_state, tiles, LANE), full),
            boundary,
            boundary,
            pltpu.VMEM((2, groups * SUB, n_state, tiles, LANE), full),
        ]
        + [held] * 5
        + [
            slots_for(ffn_part, tp_count),
            dma((2,)),
            dma((seqs,)),
            dma((seqs,)),
            dma((1, tp_count - 1)),
            dma((1, tp_count - 1)),
        ],
        compiler_params=pltpu.CompilerParams(
            collective_id=call_id, has_side_effects=True, vmem_limit_bytes=48 * 2**20
        ),
    )(step, inputs, ograd, b_rows, c_rows, rate, picks, ffn_part, middle, prior)


class PlaneGather:
    def __init__(self, own, gathered, send_sem, recv_sem):
        self.own, self.gathered = own, gathered
        self.send_sem, self.recv_sem = send_sem, recv_sem
        self.dp, self.ctx = lax.axis_index("dp"), lax.axis_index("ctx")
        self.n_dp, self.n_ctx = lax.axis_size("dp"), lax.axis_size("ctx")
        self.hands_on = relayed()
        self.count = self.n_dp * self.n_ctx
        self.me = self.dp * self.n_ctx + self.ctx
        self.others = [lax.rem(self.me + hop, self.count) for hop in range(1, self.count)]
        self.copies = {}
        if self.hands_on:
            core = lax.rem(self.dp, 2)
            over_core = self.dp + 1 - 2 * core
            over_y = lax.rem(self.dp + 2, 4)
            over_x = 1 - self.ctx
            self.core = {"dp": over_core, "ctx": self.ctx}
            self.at_x = {"dp": self.dp, "ctx": over_x}
            self.at_y = {"dp": over_y, "ctx": self.ctx}
            self.from_x = self.dp * 2 + over_x
            self.from_y = over_y * 2 + self.ctx
            self.across = over_y * 2 + over_x

    def part(self, owner, half):
        rows = self.gathered.shape[0] // self.count
        start, size = owner * rows, rows
        if half is not None:
            size = rows // 2
            start = start + half * size
        return self.gathered.at[pl.ds(pl.multiple_of(start, size), size), :]

    def send(self, which, owner, half, where):
        target = self.part(owner, half)
        source = target
        if owner is self.me:
            rows = self.own.shape[0]
            source = self.own
            if half is not None:
                source = self.own.at[pl.ds(half * (rows // 2), rows // 2), :]
        self.copies[which] = sent(
            source, target, self.send_sem.at[which], self.recv_sem.at[which], where
        )

    def arrived(self, *which):
        for one in which:
            self.copies[one].wait_recv()

    def begin(self, local_sem):
        self.local = pltpu.make_async_copy(self.own, self.part(self.me, None), local_sem)
        self.local.start()
        if not self.hands_on:
            for hop, other in enumerate(self.others):
                self.send(hop, self.me, None, device_at(PLANE, other))
            return
        self.send(0, self.me, 1, self.at_x)
        self.send(1, self.me, 0, self.at_y)
        self.send(2, self.me, None, self.core)
        self.send(3, self.me, 0, self.at_x)
        self.send(4, self.me, 1, self.at_y)

    def relay(self):
        if not self.hands_on:
            return
        self.arrived(0, 1)
        self.send(5, self.from_x, 1, self.at_y)
        self.send(6, self.from_y, 0, self.at_x)
        self.send(7, self.from_x, 1, self.core)
        self.send(8, self.from_y, 0, self.core)

    def hand_over(self):
        if not self.hands_on:
            return
        self.arrived(3, 4)
        self.send(9, self.from_x, 0, self.core)
        self.send(10, self.from_y, 1, self.core)

    def hand_over_last(self):
        if not self.hands_on:
            return
        self.arrived(5, 6)
        self.send(11, self.across, 1, self.core)
        self.send(12, self.across, 0, self.core)

    def end(self):
        if self.hands_on:
            self.arrived(2, 7, 8, 9, 10, 11, 12)
        else:
            self.arrived(*range(self.count - 1))
        for copy in self.copies.values():
            copy.wait_send()
        self.local.wait()


def relayed():
    return lax.axis_size("dp") == 4 and lax.axis_size("ctx") == 2


def gather_sems():
    count = 13 if relayed() else group_size(PLANE) - 1
    return pltpu.SemaphoreType.DMA((count,))


WIDE = 512


def products(source, first, last, dot, target, block_buf, block_sem, out_buf, out_sem):
    def fetch(j, slot):
        columns = pl.ds(pl.multiple_of(j * WIDE, WIDE), WIDE)
        return pltpu.make_async_copy(
            source.at[:, columns], block_buf.at[slot], block_sem.at[slot]
        )

    def store(j, slot):
        return pltpu.make_async_copy(out_buf.at[slot], target(j), out_sem.at[slot])

    fetch(first, first % 2).start()

    @pl.loop(first, last)
    def _(j):
        slot = lax.rem(j, 2)

        @pl.when(j + 1 < last)
        def _():
            fetch(j + 1, 1 - slot).start()

        fetch(j, slot).wait()

        @pl.when(j >= first + 2)
        def _():
            store(j - 2, slot).wait()

        out_buf[slot] = dot(block_buf[slot])
        store(j, slot).start()

    for j in range(max(first, last - 2), last):
        store(j, j % 2).wait()


def tail_kernel(
    sizes,
    mix_grads,
    normed_part,
    small,
    tokens,
    middle_grad,
    gain_row,
    one_cols,
    two_cols,
    ct_cols,
    middle_cols,
    ffn_all,
    tokens_grad,
    small_sum,
    gains,
    mix_all,
    grad_inproj,
    grad_outproj,
    grad_gateup,
    grad_downproj,
    normed_slots,
    small_slots,
    gain_slots,
    gain_own,
    block_buf,
    wide_buf,
    tall_buf,
    block_sem,
    wide_sem,
    tall_sem,
    tp_send,
    tp_recv,
    plane_send,
    plane_recv,
    gather_send,
    gather_recv,
    local_sem,
):
    inner, hidden, gain_at = sizes
    tp = Group(("tp",), tp_send, tp_recv)
    plane = Group(PLANE, plane_send, plane_recv)
    gather = PlaneGather(mix_grads, mix_all, gather_send, gather_recv)
    greet([(("tp",), tp.others), (PLANE, plane.others)])

    def flat(lhs):
        return lambda block: lax.dot_general(
            lhs[...], block, (((0,), (0,)), ((), ())), preferred_element_type=jnp.float32
        )

    def tall(rhs):
        return lambda block: lax.dot_general(
            block, rhs[...], (((0,), (0,)), ((), ())), preferred_element_type=jnp.float32
        )

    def side_by_side(ref, first):
        per = ref.shape[2] // WIDE

        def target(j):
            at = j - first
            columns = pl.ds(pl.multiple_of(lax.rem(at, per) * WIDE, WIDE), WIDE)
            return ref.at[lax.div(at, per), :, columns]

        return target

    def one_above_other(ref, first):
        return lambda j: ref.at[pl.ds(pl.multiple_of((j - first) * WIDE, WIDE), WIDE), :]

    wide = (block_buf, block_sem, wide_buf, wide_sem)
    high = (block_buf, block_sem, tall_buf, tall_sem)
    down_end = hidden // WIDE
    gu_end = 3 * hidden // WIDE
    out_end = gu_end + inner // WIDE

    normed_sent = tp.scatter(normed_part, normed_slots, 0)
    gather.begin(local_sem)
    small_sent = plane.scatter(small, small_slots, 0)
    products(
        ffn_all, down_end, gu_end, flat(two_cols), side_by_side(grad_gateup, down_end), *wide
    )
    gather.relay()
    products(ffn_all, 0, down_end, tall(ct_cols), one_above_other(grad_downproj, 0), *high)
    gather.hand_over()
    finish(normed_sent)
    hidden_in = tp.own(tokens)[...].astype(jnp.float32)
    tp.own(tokens_grad)[...] = (
        middle_grad[...]
        + norm_back(
            tp.total(normed_part, normed_slots),
            hidden_in,
            inverse_rms(hidden_in),
            gain_row[...].astype(jnp.float32),
        )
    ).astype(tokens_grad.dtype)
    tokens_sent = tp.spread(tokens_grad, 1)
    finish(small_sent)
    plane.own(small_sum)[...] = plane.total(small, small_slots).astype(small_sum.dtype)
    small_sent = plane.spread(small_sum, 1)
    products(
        ffn_all, gu_end, out_end, tall(middle_cols), one_above_other(grad_outproj, gu_end), *high
    )
    gather.hand_over_last()
    finish(small_sent)
    gain_own[...] = small_sum[pl.ds(gain_at, gain_own.shape[0]), :].astype(jnp.float32)
    gain_sent = [tp.one(gain_own, gain_slots.at[hop], 2, hop) for hop in range(tp.count - 1)]
    gather.end()
    products(
        mix_all, 0, 2 * inner // WIDE, flat(one_cols), side_by_side(grad_inproj, 0), *wide
    )
    finish(gain_sent)
    total = gain_own[...]
    for hop in range(tp.count - 1):
        total = total + gain_slots[hop]
    gains[...] = total
    finish(tokens_sent)


def run_tail(
    call_id,
    gain_at,
    mix_grads,
    normed_part,
    small,
    tokens,
    middle_grad,
    gain_row,
    one_cols,
    two_cols,
    ct_cols,
    middle_cols,
    ffn_all,
):
    inner = mix_grads.shape[1] // 2
    hidden = (ffn_all.shape[1] - inner) // 3
    share = one_cols.shape[1]
    all_rows = ffn_all.shape[0]
    tp_count, plane_count = group_size(("tp",)), group_size(PLANE)
    low, full = jnp.bfloat16, jnp.float32
    vmem = pl.BlockSpec(memory_space=pltpu.VMEM)
    hbm = pl.BlockSpec(memory_space=pl.ANY)
    gain_rows = 16
    dma = pltpu.SemaphoreType.DMA
    return pl.pallas_call(
        functools.partial(tail_kernel, (inner, hidden, gain_at)),
        in_specs=[vmem] * 10 + [hbm],
        out_specs=[vmem] * 3 + [hbm] * 5,
        out_shape=[
            jax.ShapeDtypeStruct(tokens.shape, low),
            jax.ShapeDtypeStruct(small.shape, low),
            jax.ShapeDtypeStruct((gain_rows, inner), full),
            jax.ShapeDtypeStruct((all_rows, 2 * inner), low),
            jax.ShapeDtypeStruct((2, share, inner), full),
            jax.ShapeDtypeStruct((inner, share), full),
            jax.ShapeDtypeStruct((2, share, hidden), full),
            jax.ShapeDtypeStruct((hidden, share), full),
        ],
        scratch_shapes=[
            slots_for(normed_part, tp_count),
            slots_for(small, plane_count),
            pltpu.VMEM((tp_count - 1, gain_rows, inner), full),
            pltpu.VMEM((gain_rows, inner), full),
            pltpu.VMEM((2, all_rows, WIDE), low),
            pltpu.VMEM((2, share, WIDE), full),
            pltpu.VMEM((2, WIDE, share), full),
            dma((2,)),
            dma((2,)),
            dma((2,)),
            dma((3, tp_count - 1)),
            dma((3, tp_count - 1)),
            dma((2, plane_count - 1)),
            dma((2, plane_count - 1)),
            gather_sems(),
            gather_sems(),
            dma(()),
        ],
        compiler_params=pltpu.CompilerParams(
            collective_id=call_id, has_side_effects=True, vmem_limit_bytes=56 * 2**20
        ),
    )(
        mix_grads,
        normed_part,
        small,
        tokens,
        middle_grad,
        gain_row,
        one_cols,
        two_cols,
        ct_cols,
        middle_cols,
        ffn_all,
    )


def head_kernel(
    tokens,
    gain,
    in_conv,
    in_gate,
    conv_in,
    gate_mix,
    conv_all,
    gate_all,
    normed,
    block_buf,
    block_sem,
    *sems,
):
    conv = PlaneGather(in_conv, conv_all, *sems[:2])
    gate = PlaneGather(in_gate, gate_all, *sems[3:5])
    greet([(PLANE, conv.others)])
    conv.begin(sems[2])
    gate.begin(sems[5])
    hidden_in = tokens[...].astype(jnp.float32)
    normed[...] = (hidden_in * inverse_rms(hidden_in) * gain[...].astype(jnp.float32)).astype(
        normed.dtype
    )

    def product(source, target):
        columns = range(0, source.shape[1], WIDE)

        def fetch(turn):
            at = columns[turn]
            return pltpu.make_async_copy(
                source.at[:, at : at + WIDE], block_buf.at[turn % 2], block_sem.at[turn % 2]
            )

        fetch(0).start()
        for turn, at in enumerate(columns):
            if turn + 1 < len(columns):
                fetch(turn + 1).start()
            fetch(turn).wait()
            target[:, at : at + WIDE] = matmul(normed[...], block_buf[turn % 2]).astype(
                target.dtype
            )

    conv.relay()
    conv.hand_over()
    gate.relay()
    conv.hand_over_last()
    gate.hand_over()
    conv.end()
    product(conv_all, conv_in)
    gate.hand_over_last()
    gate.end()
    product(gate_all, gate_mix)


def run_head(call_id, tokens, gain, inproj):
    rows, width = tokens.shape
    inner = inproj.shape[2]
    low = jnp.bfloat16
    vmem = pl.BlockSpec(memory_space=pltpu.VMEM)
    hbm = pl.BlockSpec(memory_space=pl.ANY)
    return pl.pallas_call(
        head_kernel,
        in_specs=[vmem] * 2 + [hbm] * 2,
        out_specs=[vmem] * 2 + [hbm] * 2,
        out_shape=[
            jax.ShapeDtypeStruct((rows, inner), low),
            jax.ShapeDtypeStruct((rows, inner), jnp.float32),
            jax.ShapeDtypeStruct((width, inner), low),
            jax.ShapeDtypeStruct((width, inner), low),
        ],
        scratch_shapes=[
            pltpu.VMEM((rows, width), low),
            pltpu.VMEM((2, width, WIDE), low),
            pltpu.SemaphoreType.DMA((2,)),
        ]
        + gather_scratch() * 2,
        compiler_params=pltpu.CompilerParams(
            collective_id=call_id, has_side_effects=True, vmem_limit_bytes=40 * 2**20
        ),
    )(tokens, gain, inproj[0], inproj[1])


def per_device(
    tokens,
    mixgain,
    inproj,
    convkern,
    convbias,
    selproj,
    stepproj,
    stepbias,
    decaylog,
    skipgain,
    outproj,
    ffngain,
    gateup,
    downproj,
    cotangent,
):
    seqs, span, width = tokens.shape
    rows = seqs * span
    taps, inner = convkern.shape
    rank = stepproj.shape[0]
    n_state = decaylog.shape[1]
    tiles = inner // LANE
    gain_mix = mixgain.astype(jnp.float32)
    kernel = convkern.astype(jnp.float32)
    kernel_bias = convbias.astype(jnp.float32)
    step_bias = stepbias.astype(jnp.float32)
    skip_weight = skipgain.astype(jnp.float32)
    decay_rate = -jnp.exp(jnp.transpose(decaylog.astype(jnp.float32)))
    rate = (decay_rate * LOG2E).reshape(n_state, tiles, LANE)

    gain_mix_row, gain_ffn_row = mixgain.reshape(1, width), ffngain.reshape(1, width)
    hidden = gateup.shape[2]
    low = jnp.bfloat16

    tokens_rows = tokens.reshape(rows, width)
    ct_low = cotangent.reshape(rows, width)
    ffn_pack = gathered_rows(
        jnp.concatenate([gateup[0], gateup[1], jnp.transpose(downproj)], 1)
    )
    conv_in, gate_mix, in_conv, in_gate = run_head(5, tokens_rows, gain_mix_row, inproj)
    hidden_in = tokens_rows.astype(jnp.float32)
    scale_one = inverse_rms(hidden_in)
    normed_one = (hidden_in * scale_one * gain_mix).astype(low)

    conv_seqs = conv_in.reshape(seqs, span, inner)
    rim_rows = passed_along(conv_seqs[:, span - (taps - 1) :], "ctx", 1)
    padded_in = jnp.concatenate([rim_rows, conv_seqs], 1).astype(jnp.float32)
    conv_out = kernel_bias[None, None]
    for offset in range(taps):
        conv_out = conv_out + kernel[offset][None, None] * padded_in[:, offset : offset + span]
    conv_out = conv_out.reshape(rows, inner)
    scan_in = jax.nn.silu(conv_out).astype(low)
    scan_float = scan_in.astype(jnp.float32)
    columns = selproj.shape[1]
    select_width = -(-columns // LANE) * LANE
    select_weights = jnp.pad(selproj, ((0, 0), (0, select_width - columns)))
    select_cols, out_first = sum_over_tp(
        0, matmul(scan_in, select_weights), [], [], [outproj[: inner // 2]]
    )
    step_low = select_cols[:, :rank].astype(low)
    b_rows = select_cols[:, rank : rank + n_state].reshape(-1)
    c_rows = select_cols[:, rank + n_state : columns].reshape(-1)
    step_pre = matmul(step_low, stepproj) + step_bias[None]
    step_size = jax.nn.softplus(step_pre)
    in_pairs = lax.axis_size("ctx") == 2
    if in_pairs:
        prior, scan_out, out_last = scan_forward_pair(
            6, step_size, scan_float, b_rows, c_rows, rate, seqs, outproj[inner // 2 :]
        )
    else:
        span_decay = jnp.exp(
            decay_rate[None] * jnp.sum(step_size.reshape(seqs, span, inner), 1)[:, None]
        ).reshape(seqs, n_state, tiles, LANE)
        ends = scan_ends(step_size, scan_float, b_rows, rate, seqs, False)
        start = from_earlier(ends, span_decay, 1)
        prior, scan_out = scan_forward(start, step_size, scan_float, b_rows, c_rows, rate, seqs)
        out_last = gathered_rows(outproj[inner // 2 :])
    mixer_core = scan_out + skip_weight[None] * scan_float
    gate_sig = jax.nn.silu(gate_mix)
    gated = (mixer_core * gate_sig).astype(low)
    normed_two, middle = mixer_out(1, gated, out_first, out_last, tokens_rows, gain_ffn_row)
    gate_up = ffn_pack[:, : 2 * hidden]
    down_weights = ffn_pack[:, 2 * hidden :]
    both_ffn = matmul(normed_two, gate_up)
    gate_ffn, up_ffn = both_ffn[:, :hidden], both_ffn[:, hidden:]
    activated = (jax.nn.silu(gate_ffn) * up_ffn).astype(low)
    act_grad = matmul(ct_low, down_weights)
    gate_grad = (act_grad * up_ffn * silu_slope(gate_ffn)).astype(low)
    up_grad = (act_grad * jax.nn.silu(gate_ffn)).astype(low)
    ffn_grads = jnp.concatenate([gate_grad, up_grad], 1)
    ffn_sent, ffn_grads = lax.optimization_barrier(
        (jnp.concatenate([activated, ffn_grads, gated], 1), ffn_grads)
    )
    ffn_all = gathered_rows(ffn_sent)
    normed_two_part = matmul_nt(ffn_grads, gate_up).astype(low)
    ffn_part = matmul_nt(activated, down_weights).astype(low)
    swap_now = swaps_in_kernels(width)
    to_swap = [normed_one, normed_two, ct_low]
    middle_low, middle_grad, ffngain_part, gated_grad, *swapped = ffn_back(
        2,
        normed_two_part,
        ct_low,
        middle,
        gain_ffn_row,
        out_first,
        out_last,
        to_swap if swap_now else [],
    )
    if not swap_now:
        swapped = [swapped_columns(array) for array in to_swap]
    normed_one_cols, normed_two_cols, ct_cols = swapped
    core_grad = gated_grad * gate_sig
    gate_mix_grad = (gated_grad * mixer_core * silu_slope(gate_mix)).astype(low)
    grad_skipgain = jnp.sum(core_grad * scan_float, 0)
    if in_pairs:
        step_grad, input_grad, rate_grad, parts, layer_rows = scan_backward_pair(
            7,
            prior,
            step_size,
            scan_float,
            core_grad,
            b_rows,
            c_rows,
            rate,
            seqs,
            ffn_part,
            middle,
        )
    else:
        back_ends = scan_ends(step_size, core_grad, c_rows, rate, seqs, True)
        end_grad = from_earlier(back_ends, span_decay, -1)
        step_grad, input_grad, rate_grad, parts = scan_backward(
            end_grad, prior, step_size, scan_float, core_grad, b_rows, c_rows, rate, seqs
        )
        ffn_sum = lax.psum_scatter(ffn_part, "tp", scatter_dimension=0, tiled=True)
        layer_rows = (middle + ffn_sum.astype(jnp.float32)).astype(low)
    grad_decaylog = rate_grad.reshape(n_state, inner) * decay_rate
    pre_grad = step_grad * jax.nn.sigmoid(step_pre)
    grad_stepbias = jnp.sum(pre_grad, 0)
    pre_low = pre_grad.astype(low)
    grad_stepproj = matmul_tn(step_low, pre_low)
    select_part = jnp.concatenate(
        [
            matmul_nt(pre_low, stepproj),
            jnp.sum(parts, -1),
            jnp.zeros((rows, select_width - columns), jnp.float32),
        ],
        1,
    ).astype(low)
    select_low, layer_out, *swapped = sum_over_tp(
        3, select_part, [layer_rows], [middle_low] if swap_now else [], []
    )
    (middle_cols,) = swapped if swap_now else [swapped_columns(middle_low)]
    grad_selproj = matmul_tn(select_low, scan_in)
    scan_in_grad = (
        core_grad * skip_weight[None]
        + input_grad
        + matmul_nt(select_low, select_weights)
    )
    conv_grad = scan_in_grad * silu_slope(conv_out)
    grad_convbias = jnp.sum(conv_grad, 0)
    conv_grad_seqs = conv_grad.reshape(seqs, span, inner)
    padded_grad = jnp.zeros(padded_in.shape, jnp.float32)
    kernel_rows = []
    for offset in range(taps):
        kernel_rows.append(jnp.sum(conv_grad_seqs * padded_in[:, offset : offset + span], (0, 1)))
        padded_grad = padded_grad + jnp.pad(
            kernel[offset][None, None] * conv_grad_seqs,
            ((0, 0), (offset, taps - 1 - offset), (0, 0)),
        )
    grad_convkern = jnp.stack(kernel_rows)
    returned = passed_along(padded_grad[:, : taps - 1], "ctx", -1)
    conv_in_grad = (
        (padded_grad[:, taps - 1 :] + jnp.pad(returned, ((0, 0), (span - taps + 1, 0), (0, 0))))
        .astype(low)
        .reshape(rows, inner)
    )
    mix_grads = jnp.concatenate([conv_in_grad, gate_mix_grad], 1)
    normed_one_part = matmul_nt(conv_in_grad, in_conv) + matmul_nt(gate_mix_grad, in_gate)
    mixgain_part = jnp.sum(normed_one_part * hidden_in * scale_one, 0)
    normed_one_part = normed_one_part.astype(low)
    small = [
        grad_convkern,
        grad_convbias[None],
        grad_stepbias[None],
        grad_decaylog,
        grad_skipgain[None],
        grad_stepproj,
        grad_selproj[:columns],
        mixgain_part.reshape(-1, inner),
        ffngain_part.reshape(-1, inner),
    ]
    sizes = [part.shape[0] for part in small]
    gain_at = sum(sizes[:-2]) + -sum(sizes[:-2]) % 16
    small.insert(-2, jnp.zeros((gain_at - sum(sizes[:-2]), inner), jnp.float32))
    small = jnp.concatenate(small, 0).astype(low)
    share = 16 * group_size(PLANE)
    small = jnp.pad(small, ((0, -(gain_at + 16) % share + 16 - sum(sizes[-2:])), (0, 0)))
    (
        tokens_grad,
        small,
        gains,
        _,
        grad_inproj,
        grad_outproj,
        grad_gateup,
        grad_downproj,
    ) = run_tail(
        4,
        gain_at,
        mix_grads,
        normed_one_part,
        small,
        tokens_rows,
        middle_grad,
        gain_mix_row,
        normed_one_cols,
        normed_two_cols,
        ct_cols,
        middle_cols,
        ffn_all,
    )
    small = small.astype(jnp.float32)
    smalls, at = [], 0
    for size in sizes[:-2]:
        smalls.append(small[at : at + size])
        at += size
    gains = gains[: sum(sizes[-2:])].reshape(2, width)
    return (
        layer_out.reshape(tokens.shape),
        tokens_grad.reshape(tokens.shape),
        gains[0],
        grad_inproj,
        smalls[0],
        smalls[1][0],
        jnp.transpose(smalls[6]),
        smalls[5],
        smalls[2][0],
        jnp.transpose(smalls[3]),
        smalls[4][0],
        grad_outproj,
        gains[1],
        grad_gateup,
        grad_downproj,
    )


def solution(mesh):
    in_specs = (
        P("dp", "ctx", None),
        P(),
        P(None, ("dp", "ctx"), "tp"),
        P(None, "tp"),
        P("tp"),
        P("tp", None),
        P(None, "tp"),
        P("tp"),
        P("tp", None),
        P("tp"),
        P("tp", ("dp", "ctx")),
        P(),
        P(None, ("dp", "ctx"), "tp"),
        P("tp", ("dp", "ctx")),
        P("dp", "ctx", None),
    )
    out_specs = (
        P("dp", "ctx", None),
        P("dp", "ctx", None),
        P(),
        P(None, ("dp", "ctx"), "tp"),
        P(None, "tp"),
        P("tp"),
        P("tp", None),
        P(None, "tp"),
        P("tp"),
        P("tp", None),
        P("tp"),
        P("tp", ("dp", "ctx")),
        P(),
        P(None, ("dp", "ctx"), "tp"),
        P("tp", ("dp", "ctx")),
    )
    return jax.shard_map(
        per_device, mesh=mesh, in_specs=in_specs, out_specs=out_specs, check_vma=False
    )
```

```python
import functools
import math

import jax
import jax.numpy as jnp
from jax import lax
from jax.experimental import pallas as pl
from jax.experimental.pallas import tpu as pltpu
from jax.sharding import PartitionSpec as P

EPSILON = 1e-05
LOG2E = math.log2(math.e)
LN2 = math.log(2.0)
SUB = 8
LANE = 128
PLANE = ("dp", "ctx")


def passed_along(value, axis, steps):
    count = lax.axis_size(axis)
    first, last = (max(0, -steps), min(count, count - steps))
    return lax.ppermute(value, axis, [(source, source + steps) for source in range(first, last)])


def matmul(left, right):
    return jnp.dot(left, right, preferred_element_type=jnp.float32)


def matmul_nt(left, right):
    return lax.dot_general(
        left, right, (((1,), (1,)), ((), ())), preferred_element_type=jnp.float32
    )


def matmul_tn(left, right):
    return lax.dot_general(
        left, right, (((0,), (0,)), ((), ())), preferred_element_type=jnp.float32
    )


def inverse_rms(values):
    return lax.rsqrt(jnp.mean(values * values, -1, keepdims=True) + EPSILON)


def silu_slope(values):
    logistic = jax.nn.sigmoid(values)
    return logistic * (1.0 + values * (1.0 - logistic))


def norm_back(grad_norm, values, scale, gain):
    scaled_grad = grad_norm * gain
    unit_rows = values * scale
    return scale * (scaled_grad - unit_rows * jnp.mean(scaled_grad * unit_rows, -1, keepdims=True))


def stage_in(ref, group, held):
    for tile in range(held.shape[0] // SUB):
        held[pl.ds(tile * SUB, SUB), :] = ref[
            pl.ds(pl.multiple_of(group * SUB, SUB), SUB), pl.ds(tile * LANE, LANE)
        ]


def stage_out(held, ref, group):
    for tile in range(held.shape[0] // SUB):
        ref[pl.ds(pl.multiple_of(group * SUB, SUB), SUB), pl.ds(tile * LANE, LANE)] = held[
            pl.ds(tile * SUB, SUB), :
        ]


def token_row(held, at, tiles):
    return held[pl.ds(at, tiles, stride=SUB), :]


def ends_kernel(
    n_state,
    tiles,
    groups,
    reverse,
    step_ref,
    drive_ref,
    rows_ref,
    rate_ref,
    end_ref,
    step_held,
    drive_held,
):
    base = pl.program_id(0) * groups * SUB * n_state
    rates = [rate_ref[n] for n in range(n_state)]

    def one(turn, states):
        group = groups - 1 - turn if reverse else turn
        order = range(SUB - 1, -1, -1) if reverse else range(SUB)
        states = list(states)
        stage_in(step_ref, group, step_held)
        stage_in(drive_ref, group, drive_held)
        for at in order:
            step = token_row(step_held, at, tiles)
            drive = token_row(drive_held, at, tiles)
            if not reverse:
                drive = drive * step
            for n in range(n_state):
                row = rows_ref[base + (group * SUB + at) * n_state + n]
                decay = jnp.exp2(step * rates[n])
                if reverse:
                    states[n] = decay * (states[n] + drive * row)
                else:
                    states[n] = decay * states[n] + drive * row
        return tuple(states)

    zero = jnp.zeros((tiles, LANE), jnp.float32)
    states = lax.fori_loop(0, groups, one, (zero,) * n_state)
    for n in range(n_state):
        end_ref[0, n] = states[n]


def scan_ends(step, drive, rows, rate, seqs, reverse):
    n_state, tiles, _ = rate.shape
    groups = step.shape[0] // seqs // SUB
    rows_spec = pl.BlockSpec((groups * SUB, tiles * LANE), lambda s: (s, 0))
    held = pltpu.VMEM((tiles * SUB, LANE), jnp.float32)
    return pl.pallas_call(
        functools.partial(ends_kernel, n_state, tiles, groups, reverse),
        grid=(seqs,),
        in_specs=[
            rows_spec,
            rows_spec,
            pl.BlockSpec(memory_space=pltpu.SMEM),
            pl.BlockSpec((n_state, tiles, LANE), lambda s: (0, 0, 0)),
        ],
        out_specs=pl.BlockSpec((1, n_state, tiles, LANE), lambda s: (s, 0, 0, 0)),
        out_shape=jax.ShapeDtypeStruct((seqs, n_state, tiles, LANE), jnp.float32),
        scratch_shapes=[held, held],
        compiler_params=pltpu.CompilerParams(vmem_limit_bytes=32 * 2**20),
    )(step, drive, rows, rate)


def forward_kernel(
    n_state,
    tiles,
    groups,
    blocks,
    start_ref,
    step_ref,
    input_ref,
    brow_ref,
    crow_ref,
    rate_ref,
    prior_ref,
    mixed_ref,
    carried,
    step_held,
    input_held,
    mixed_held,
):
    base = (pl.program_id(0) * blocks + pl.program_id(1)) * groups * SUB * n_state

    @pl.when(pl.program_id(1) == 0)
    def _():
        carried[...] = start_ref[0]

    def one(group, states):
        states = list(states)
        stage_in(step_ref, group, step_held)
        stage_in(input_ref, group, input_held)
        for at in range(SUB):
            step = token_row(step_held, at, tiles)
            drive = step * token_row(input_held, at, tiles)
            mixed = [None] * 2
            for n in range(n_state):
                where = base + (group * SUB + at) * n_state + n
                prior_ref[group * SUB + at, n] = states[n]
                decay = jnp.exp2(step * rate_ref[n])
                states[n] = decay * states[n] + drive * brow_ref[where]
                term = states[n] * crow_ref[where]
                mixed[n % 2] = term if mixed[n % 2] is None else mixed[n % 2] + term
            mixed_held[pl.ds(at, tiles, stride=SUB), :] = mixed[0] + mixed[1]
        stage_out(mixed_held, mixed_ref, group)
        return tuple(states)

    states = lax.fori_loop(0, groups, one, tuple(carried[n] for n in range(n_state)))
    for n in range(n_state):
        carried[n] = states[n]


def scan_forward(start, step, inputs, b_rows, c_rows, rate, seqs):
    n_state, tiles, _ = rate.shape
    all_groups = step.shape[0] // SUB
    groups = math.gcd(all_groups // seqs, 4)
    blocks = all_groups // seqs // groups
    rows_spec = pl.BlockSpec((groups * SUB, tiles * LANE), lambda s, b: (s * blocks + b, 0))
    held = pltpu.VMEM((tiles * SUB, LANE), jnp.float32)
    smem = pl.BlockSpec(memory_space=pltpu.SMEM)
    tokens = all_groups * SUB
    return pl.pallas_call(
        functools.partial(forward_kernel, n_state, tiles, groups, blocks),
        grid=(seqs, blocks),
        in_specs=[
            pl.BlockSpec((1, n_state, tiles, LANE), lambda s, b: (s, 0, 0, 0)),
            rows_spec,
            rows_spec,
            smem,
            smem,
            pl.BlockSpec((n_state, tiles, LANE), lambda s, b: (0, 0, 0)),
        ],
        out_specs=[
            pl.BlockSpec(
                (groups * SUB, n_state, tiles, LANE), lambda s, b: (s * blocks + b, 0, 0, 0)
            ),
            rows_spec,
        ],
        out_shape=[
            jax.ShapeDtypeStruct((tokens, n_state, tiles, LANE), jnp.float32),
            jax.ShapeDtypeStruct(step.shape, jnp.float32),
        ],
        scratch_shapes=[pltpu.VMEM((n_state, tiles, LANE), jnp.float32)] + [held] * 3,
        compiler_params=pltpu.CompilerParams(vmem_limit_bytes=32 * 2**20),
    )(start, step, inputs, b_rows, c_rows, rate)


def backward_kernel(
    n_state,
    tiles,
    groups,
    blocks,
    end_ref,
    prior_ref,
    step_ref,
    input_ref,
    ograd_ref,
    brow_ref,
    crow_ref,
    rate_ref,
    picks_ref,
    step_grad_ref,
    input_grad_ref,
    rate_grad_ref,
    part_ref,
    carried,
    step_held,
    input_held,
    ograd_held,
    step_grad_held,
    input_grad_held,
):
    block = blocks - 1 - pl.program_id(1)
    base = (pl.program_id(0) * blocks + block) * groups * SUB * n_state

    @pl.when(pl.program_id(1) == 0)
    def _():
        carried[...] = end_ref[0]

    @pl.when((pl.program_id(0) == 0) & (pl.program_id(1) == 0))
    def _():
        rate_grad_ref[...] = jnp.zeros_like(rate_grad_ref)

    def one(turn, grads):
        group = groups - 1 - turn
        grads = list(grads)
        stage_in(step_ref, group, step_held)
        stage_in(input_ref, group, input_held)
        stage_in(ograd_ref, group, ograd_held)
        for at in range(SUB - 1, -1, -1):
            step = token_row(step_held, at, tiles)
            value = token_row(input_held, at, tiles)
            ograd = token_row(ograd_held, at, tiles)
            drive = step * value
            along_b = None
            along_rate = None
            brow_parts, crow_parts = [], []
            for n in range(n_state):
                where = base + (group * SUB + at) * n_state + n
                brow, crow = brow_ref[where], crow_ref[where]
                rate = rate_ref[n]
                decay = jnp.exp2(step * rate)
                grad = ograd * crow + grads[n]
                kept = decay * prior_ref[group * SUB + at, n]
                state = kept + drive * brow
                decay_term = grad * kept
                grads[n] = decay * grad
                rate_grad_ref[n] += decay_term * step
                by_rate, by_brow = decay_term * rate, grad * brow
                along_rate = by_rate if along_rate is None else along_rate + by_rate
                along_b = by_brow if along_b is None else along_b + by_brow
                brow_parts.append(grad * drive)
                crow_parts.append(ograd * state)
            step_grad_held[pl.ds(at, tiles, stride=SUB), :] = along_rate * LN2 + along_b * value
            input_grad_held[pl.ds(at, tiles, stride=SUB), :] = along_b * step
            parts = jnp.concatenate(brow_parts + crow_parts, 0).astype(jnp.bfloat16)
            part_ref[group * SUB + at] = jnp.dot(
                picks_ref[...], parts, preferred_element_type=jnp.float32
            )
        stage_out(step_grad_held, step_grad_ref, group)
        stage_out(input_grad_held, input_grad_ref, group)
        return tuple(grads)

    grads = lax.fori_loop(0, groups, one, tuple(carried[n] for n in range(n_state)))
    for n in range(n_state):
        carried[n] = grads[n]


def scan_backward(end_grad, prior, step, inputs, ograd, b_rows, c_rows, rate, seqs):
    n_state, tiles, _ = rate.shape
    all_groups = step.shape[0] // SUB
    groups = math.gcd(all_groups // seqs, 4)
    blocks = all_groups // seqs // groups

    def at(s, b):
        return s * blocks + blocks - 1 - b

    rows_spec = pl.BlockSpec((groups * SUB, tiles * LANE), lambda s, b: (at(s, b), 0))
    held = pltpu.VMEM((tiles * SUB, LANE), jnp.float32)
    smem = pl.BlockSpec(memory_space=pltpu.SMEM)
    tokens = all_groups * SUB
    picks = jnp.repeat(jnp.eye(2 * n_state, dtype=jnp.bfloat16), tiles, 1)
    return pl.pallas_call(
        functools.partial(backward_kernel, n_state, tiles, groups, blocks),
        grid=(seqs, blocks),
        in_specs=[
            pl.BlockSpec((1, n_state, tiles, LANE), lambda s, b: (s, 0, 0, 0)),
            pl.BlockSpec((groups * SUB, n_state, tiles, LANE), lambda s, b: (at(s, b), 0, 0, 0)),
            rows_spec,
            rows_spec,
            rows_spec,
            smem,
            smem,
            pl.BlockSpec((n_state, tiles, LANE), lambda s, b: (0, 0, 0)),
            pl.BlockSpec(picks.shape, lambda s, b: (0, 0)),
        ],
        out_specs=[
            rows_spec,
            rows_spec,
            pl.BlockSpec((n_state, tiles, LANE), lambda s, b: (0, 0, 0)),
            pl.BlockSpec((groups * SUB, 2 * n_state, LANE), lambda s, b: (at(s, b), 0, 0)),
        ],
        out_shape=[
            jax.ShapeDtypeStruct(step.shape, jnp.float32),
            jax.ShapeDtypeStruct(step.shape, jnp.float32),
            jax.ShapeDtypeStruct(rate.shape, jnp.float32),
            jax.ShapeDtypeStruct((tokens, 2 * n_state, LANE), jnp.float32),
        ],
        scratch_shapes=[pltpu.VMEM((n_state, tiles, LANE), jnp.float32)] + [held] * 5,
        compiler_params=pltpu.CompilerParams(vmem_limit_bytes=32 * 2**20),
    )(end_grad, prior, step, inputs, ograd, b_rows, c_rows, rate, picks)


def from_earlier(ends, decay, steps):
    count = lax.axis_size("ctx")
    if count == 1:
        return jnp.zeros_like(ends)
    if count == 2:
        return passed_along(ends, "ctx", steps)
    index = lax.axis_index("ctx")
    all_ends = lax.all_gather(ends, "ctx")
    all_decays = lax.all_gather(decay, "ctx")

    def one(turn, state):
        at = turn if steps > 0 else count - 1 - turn
        reached = at < index if steps > 0 else at > index
        return jnp.where(reached, all_decays[at] * state + all_ends[at], state)

    return lax.fori_loop(0, count, one, jnp.zeros_like(ends))


def gathered_rows(rows):
    return lax.all_gather(rows, PLANE, axis=0, tiled=True)


def swapped_columns(rows):
    return lax.all_to_all(rows, PLANE, split_axis=1, concat_axis=0, tiled=True)


def place_in(axes):
    index = 0
    for axis in axes:
        index = index * lax.axis_size(axis) + lax.axis_index(axis)
    return index


def device_at(axes, index):
    where = {}
    for axis in reversed(axes):
        size = lax.axis_size(axis)
        where[axis] = lax.rem(index, size)
        index = lax.div(index, size)
    return where


def greet(groups):
    barrier = pltpu.get_barrier_semaphore()
    total = 0
    for axes, others in groups:
        for other in others:
            pl.semaphore_signal(
                barrier,
                inc=1,
                device_id=device_at(axes, other),
                device_id_type=pl.DeviceIdType.MESH,
            )
            total += 1
    pl.semaphore_wait(barrier, total)


def sent(source, target, send_sem, recv_sem, where):
    copy = pltpu.make_async_remote_copy(
        src_ref=source,
        dst_ref=target,
        send_sem=send_sem,
        recv_sem=recv_sem,
        device_id=where,
        device_id_type=pl.DeviceIdType.MESH,
    )
    copy.start()
    return copy


def finish(copies):
    for copy in copies:
        copy.wait()


def rows_of(ref, index, count):
    rows = ref.shape[0] // count
    return ref.at[pl.ds(pl.multiple_of(index * rows, rows), rows), :]


class Group:
    def __init__(self, axes, send_sem, recv_sem):
        self.axes = axes
        self.count = math.prod(lax.axis_size(axis) for axis in axes)
        self.me = place_in(axes)
        self.others = [lax.rem(self.me + hop, self.count) for hop in range(1, self.count)]
        self.send_sem, self.recv_sem = send_sem, recv_sem

    def own(self, ref):
        return rows_of(ref, self.me, self.count)

    def one(self, source, target, which, hop):
        return sent(
            source,
            target,
            self.send_sem.at[which, hop],
            self.recv_sem.at[which, hop],
            device_at(self.axes, self.others[hop]),
        )

    def scatter(self, part, slot, which):
        return [
            self.one(rows_of(part, other, self.count), slot.at[hop], which, hop)
            for hop, other in enumerate(self.others)
        ]

    def total(self, part, slot):
        total = self.own(part)[...].astype(jnp.float32)
        for hop in range(self.count - 1):
            total = total + slot[hop].astype(jnp.float32)
        return total

    def spread(self, ref, which):
        return [self.one(self.own(ref), self.own(ref), which, hop) for hop in range(self.count - 1)]


def slots_for(part, count):
    return pltpu.VMEM((count - 1, part.shape[0] // count) + part.shape[1:], part.dtype)


def group_size(axes):
    return math.prod(lax.axis_size(axis) for axis in axes)


class Swap:
    def __init__(self, arrays, swapped, send_sem, recv_sem, local_sem):
        plane = Group(PLANE, send_sem, recv_sem)
        self.plane, self.arrays, self.swapped, self.local_sem = plane, arrays, swapped, local_sem

    def begin(self):
        self.copies, plane = [], self.plane
        for which, (array, swapped) in enumerate(zip(self.arrays, self.swapped)):
            share = swapped.shape[1]

            def columns(index):
                return array.at[:, pl.ds(pl.multiple_of(index * share, share), share)]

            for hop, other in enumerate(plane.others):
                self.copies.append(plane.one(columns(other), plane.own(swapped), which, hop))
            local = pltpu.make_async_copy(
                columns(plane.me), plane.own(swapped), self.local_sem.at[which]
            )
            local.start()
            self.copies.append(local)

    def end(self):
        finish(self.copies)


def swap_scratch(arrays):
    sems = pltpu.SemaphoreType.DMA((len(arrays), group_size(PLANE) - 1))
    return [sems, sems, pltpu.SemaphoreType.DMA((len(arrays),))] if arrays else []


def swap_shapes(arrays):
    count = group_size(PLANE)
    return [
        jax.ShapeDtypeStruct((array.shape[0] * count, array.shape[1] // count), array.dtype)
        for array in arrays
    ]


def swaps_in_kernels(width):
    return width // group_size(PLANE) % LANE == 0


def sum_kernel(n_rows, n_swaps, n_gathers, part, *refs):
    own_rows, refs = refs[:n_rows], refs[n_rows:]
    arrays, refs = refs[:n_swaps], refs[n_swaps:]
    shards, refs = refs[:n_gathers], refs[n_gathers:]
    total, refs = refs[0], refs[1:]
    all_rows, refs = refs[:n_rows], refs[n_rows:]
    swapped, refs = refs[:n_swaps], refs[n_swaps:]
    gathered, refs = refs[:n_gathers], refs[n_gathers:]
    slots, send_sem, recv_sem, *refs = refs
    group = Group(("tp",), send_sem, recv_sem)
    greeted = [(("tp",), group.others)]
    if n_swaps:
        swap = Swap(arrays, swapped, *refs[:3])
        greeted.append((PLANE, swap.plane.others))
        refs = refs[3:]
    if n_gathers:
        gather = PlaneGather(shards[0], gathered[0], *refs[:2])
        if not n_swaps:
            greeted.append((PLANE, gather.others))
    greet(greeted)
    copies = group.scatter(part, slots, 0)
    if n_swaps:
        swap.begin()
    if n_gathers:
        gather.begin(refs[2])
    spreads = []
    for which, (own, everything) in enumerate(zip(own_rows, all_rows)):
        group.own(everything)[...] = own[...]
        spreads += group.spread(everything, 2 + which)
    finish(copies)
    group.own(total)[...] = group.total(part, slots).astype(total.dtype)
    copies = group.spread(total, 1)
    if n_gathers:
        gather.relay()
        gather.hand_over()
    finish(copies)
    finish(spreads)
    if n_swaps:
        swap.end()
    if n_gathers:
        gather.hand_over_last()
        gather.end()


def gathered_shape(shard):
    return jax.ShapeDtypeStruct(
        (shard.shape[0] * group_size(PLANE),) + shard.shape[1:], shard.dtype
    )


def gather_scratch():
    return [gather_sems(), gather_sems(), pltpu.SemaphoreType.DMA(())]


def sum_over_tp(call_id, part, own_rows, arrays, shards):
    count = group_size(("tp",))
    vmem = pl.BlockSpec(memory_space=pltpu.VMEM)
    hbm = pl.BlockSpec(memory_space=pl.ANY)
    operands = [part, *own_rows, *arrays]
    sems = pltpu.SemaphoreType.DMA((2 + len(own_rows), count - 1))
    return pl.pallas_call(
        functools.partial(sum_kernel, len(own_rows), len(arrays), len(shards)),
        in_specs=[vmem] * len(operands) + [hbm] * len(shards),
        out_specs=[vmem] * len(operands) + [hbm] * len(shards),
        out_shape=[jax.ShapeDtypeStruct(part.shape, part.dtype)]
        + [
            jax.ShapeDtypeStruct((own.shape[0] * count,) + own.shape[1:], own.dtype)
            for own in own_rows
        ]
        + swap_shapes(arrays)
        + [gathered_shape(shard) for shard in shards],
        scratch_shapes=[slots_for(part, count), sems, sems]
        + swap_scratch(arrays)
        + gather_scratch() * len(shards),
        compiler_params=pltpu.CompilerParams(
            collective_id=call_id, has_side_effects=True, vmem_limit_bytes=40 * 2**20
        ),
    )(*operands, *shards)


def mixer_out_kernel(n_swaps, gated, out_first, out_last, tokens, gain, *refs):
    arrays, refs = refs[:n_swaps], refs[n_swaps:]
    normed, middle, gated_all, *refs = refs
    swapped, refs = refs[:n_swaps], refs[n_swaps:]
    part, slots, send_sem, recv_sem, gather_send, gather_recv, local_sem, *refs = refs
    group = Group(("tp",), send_sem, recv_sem)
    gather = PlaneGather(gated, gated_all, gather_send, gather_recv)
    half = gated.shape[1] // 2
    share = out_first.shape[1]
    greet([(("tp",), group.others), (PLANE, gather.others)])
    gather.begin(local_sem)
    for at in range(out_first.shape[0] // half):
        rows = slice(at * half, (at + 1) * half)
        part[:, at * share : (at + 1) * share] = (
            matmul(gated[:, :half], out_first[rows, :])
            + matmul(gated[:, half:], out_last[rows, :])
        ).astype(part.dtype)
    copies = group.scatter(part, slots, 0)
    if n_swaps:
        swap = Swap(arrays, swapped, *refs)
        swap.begin()
    finish(copies)
    rows = group.own(tokens)[...].astype(jnp.float32) + group.total(part, slots)
    middle[...] = rows
    group.own(normed)[...] = (rows * inverse_rms(rows) * gain[...].astype(jnp.float32)).astype(
        normed.dtype
    )
    copies = group.spread(normed, 1)
    gather.relay()
    gather.hand_over()
    finish(copies)
    gather.hand_over_last()
    gather.end()
    if n_swaps:
        swap.end()


def mixer_out(call_id, gated, out_first, out_last, tokens, gain, arrays):
    count = group_size(("tp",))
    vmem = pl.BlockSpec(memory_space=pltpu.VMEM)
    hbm = pl.BlockSpec(memory_space=pl.ANY)
    rows, width = tokens.shape
    part = jax.ShapeDtypeStruct((rows, width), jnp.bfloat16)
    sems = pltpu.SemaphoreType.DMA((2, count - 1))
    return pl.pallas_call(
        functools.partial(mixer_out_kernel, len(arrays)),
        in_specs=[vmem] * (5 + len(arrays)),
        out_specs=[vmem] * 2 + [hbm] + [vmem] * len(arrays),
        out_shape=[
            part,
            jax.ShapeDtypeStruct((rows // count, width), jnp.float32),
            gathered_shape(gated),
        ]
        + swap_shapes(arrays),
        scratch_shapes=[pltpu.VMEM(part.shape, part.dtype), slots_for(part, count), sems, sems]
        + gather_scratch()
        + swap_scratch(arrays),
        compiler_params=pltpu.CompilerParams(
            collective_id=call_id, has_side_effects=True, vmem_limit_bytes=40 * 2**20
        ),
    )(gated, out_first, out_last, tokens, gain, *arrays)


def ffn_kernel(swaps, normed, ct, weights, made, *refs):
    hidden = weights.shape[1] // 3
    if swaps:
        *swapped, block_buf, block_sem, send_sem, recv_sem, local_sem = refs
        swap = Swap([normed, ct], swapped, send_sem, recv_sem, local_sem)
        greet([(PLANE, swap.plane.others)])
        swap.begin()
    else:
        block_buf, block_sem = refs

    def columns(j, which):
        return pl.ds(pl.multiple_of(which * hidden + j * WIDE, WIDE), WIDE)

    def fetch(j, which):
        slot = lax.rem(j, 2)
        return pltpu.make_async_copy(
            weights.at[:, columns(j, which)],
            block_buf.at[slot, which],
            block_sem.at[slot, which],
        )

    for which in range(3):
        fetch(0, which).start()

    @pl.loop(0, hidden // WIDE)
    def _(j):
        slot = lax.rem(j, 2)

        @pl.when(j + 1 < hidden // WIDE)
        def _():
            for which in range(3):
                fetch(j + 1, which).start()

        fetch(j, 0).wait()
        gate = matmul(normed[...], block_buf[slot, 0])
        fetch(j, 1).wait()
        up = matmul(normed[...], block_buf[slot, 1])
        fetch(j, 2).wait()
        act_grad = matmul(ct[...], block_buf[slot, 2])
        logistic = jax.nn.sigmoid(gate)
        silu = gate * logistic
        slope = logistic * (1.0 + gate * (1.0 - logistic))
        made[:, columns(j, 0)] = (silu * up).astype(made.dtype)
        made[:, columns(j, 1)] = (act_grad * up * slope).astype(made.dtype)
        made[:, columns(j, 2)] = (act_grad * silu).astype(made.dtype)

    if swaps:
        swap.end()


def run_ffn(call_id, normed, ct, weights, swaps):
    rows, width = normed.shape
    arrays = [normed, ct] if swaps else []
    vmem = pl.BlockSpec(memory_space=pltpu.VMEM)
    params = dict(collective_id=call_id, has_side_effects=True) if swaps else {}
    return pl.pallas_call(
        functools.partial(ffn_kernel, swaps),
        in_specs=[vmem, vmem, pl.BlockSpec(memory_space=pl.ANY)],
        out_specs=[vmem] * (1 + len(arrays)),
        out_shape=[jax.ShapeDtypeStruct((rows, weights.shape[1]), jnp.bfloat16)]
        + swap_shapes(arrays),
        scratch_shapes=[
            pltpu.VMEM((2, 3, width, WIDE), jnp.bfloat16),
            pltpu.SemaphoreType.DMA((2, 3)),
        ]
        + swap_scratch(arrays),
        compiler_params=pltpu.CompilerParams(vmem_limit_bytes=48 * 2**20, **params),
    )(normed, ct, weights)


def ffn_back_kernel(
    made,
    ct,
    middle,
    gain,
    out_first,
    out_last,
    weights,
    middle_low,
    middle_grad,
    gain_grad,
    gated_grad,
    ffn_part,
    part,
    slots,
    wide_buf,
    down_buf,
    wide_sem,
    down_sem,
    part_send,
    part_recv,
    send_sem,
    recv_sem,
):
    hidden = made.shape[1] // 3
    blocks = part.shape[1] // WIDE
    group = Group(("tp",), send_sem, recv_sem)
    greet([(("tp",), group.others)])

    def fetch(j):
        return pltpu.make_async_copy(
            weights.at[j * WIDE : (j + 1) * WIDE, : 2 * hidden],
            wide_buf.at[j % 2],
            wide_sem.at[j % 2],
        )

    def fetch_down(j):
        return pltpu.make_async_copy(
            weights.at[j * WIDE : (j + 1) * WIDE, 2 * hidden :],
            down_buf.at[j % 2],
            down_sem.at[j % 2],
        )

    fetch(0).start()
    copies = []
    for j in range(blocks):
        if j + 1 < blocks:
            fetch(j + 1).start()
        else:
            fetch_down(0).start()
        fetch(j).wait()
        columns = slice(j * WIDE, (j + 1) * WIDE)
        part[:, columns] = matmul_nt(made[:, hidden:], wide_buf[j % 2]).astype(part.dtype)
        for hop, other in enumerate(group.others):
            copies.append(
                sent(
                    rows_of(part, other, group.count).at[:, columns],
                    slots.at[hop, :, columns],
                    part_send.at[j, hop],
                    part_recv.at[j, hop],
                    device_at(("tp",), other),
                )
            )
    for j in range(blocks):
        if j + 1 < blocks:
            fetch_down(j + 1).start()
        fetch_down(j).wait()
        ffn_part[:, j * WIDE : (j + 1) * WIDE] = matmul_nt(
            made[:, :hidden], down_buf[j % 2]
        ).astype(ffn_part.dtype)
    finish(copies)
    normed_grad = group.total(part, slots)
    rows = middle[...]
    scale = inverse_rms(rows)
    gain_grad[...] = jnp.sum(normed_grad * rows * scale, 0, keepdims=True)
    grad = group.own(ct)[...].astype(jnp.float32) + norm_back(
        normed_grad, rows, scale, gain[...].astype(jnp.float32)
    )
    middle_grad[...] = grad
    group.own(middle_low)[...] = grad.astype(middle_low.dtype)
    finish(group.spread(middle_low, 0))
    half = gated_grad.shape[1] // 2
    share = out_first.shape[1]
    for side, shards in enumerate((out_first, out_last)):
        total = None
        for at in range(shards.shape[0] // half):
            one = matmul_nt(
                middle_low[:, at * share : (at + 1) * share],
                shards[at * half : (at + 1) * half, :],
            )
            total = one if total is None else total + one
        gated_grad[:, side * half : (side + 1) * half] = total


def ffn_back(call_id, made, ct, middle, gain, out_first, out_last, weights):
    count = group_size(("tp",))
    vmem = pl.BlockSpec(memory_space=pltpu.VMEM)
    rows, width = ct.shape
    hidden = made.shape[1] // 3
    inner = 2 * out_first.shape[0] // group_size(PLANE)
    low, full = jnp.bfloat16, jnp.float32
    part = jax.ShapeDtypeStruct((rows, width), low)
    dma = pltpu.SemaphoreType.DMA
    return pl.pallas_call(
        ffn_back_kernel,
        in_specs=[vmem] * 6 + [pl.BlockSpec(memory_space=pl.ANY)],
        out_specs=[vmem] * 5,
        out_shape=[
            part,
            jax.ShapeDtypeStruct((rows // count, width), full),
            jax.ShapeDtypeStruct((1, width), full),
            jax.ShapeDtypeStruct((rows, inner), full),
            part,
        ],
        scratch_shapes=[
            pltpu.VMEM(part.shape, low),
            slots_for(part, count),
            pltpu.VMEM((2, WIDE, 2 * hidden), low),
            pltpu.VMEM((2, WIDE, hidden), low),
            dma((2,)),
            dma((2,)),
            dma((width // WIDE, count - 1)),
            dma((width // WIDE, count - 1)),
            dma((1, count - 1)),
            dma((1, count - 1)),
        ],
        compiler_params=pltpu.CompilerParams(
            collective_id=call_id, has_side_effects=True, vmem_limit_bytes=52 * 2**20
        ),
    )(made, ct, middle, gain, out_first, out_last, weights)


def send_on(source, target, send_sem, recv_sem, ctx):
    return pltpu.make_async_remote_copy(
        src_ref=source,
        dst_ref=target,
        send_sem=send_sem,
        recv_sem=recv_sem,
        device_id={"ctx": ctx},
        device_id_type=pl.DeviceIdType.MESH,
    )


def forward_pair_kernel(
    n_state,
    tiles,
    groups,
    blocks,
    seqs,
    step_ref,
    input_ref,
    brow_ref,
    crow_ref,
    rate_ref,
    shard,
    prior_ref,
    mixed_ref,
    gathered,
    carried,
    ends,
    starts,
    prior_buf,
    step_held,
    input_held,
    mixed_held,
    prior_sem,
    send_sem,
    recv_sem,
    gather_send,
    gather_recv,
    local_sem,
):
    place = lax.axis_index("ctx")
    gather = PlaneGather(shard, gathered, gather_send, gather_recv)
    greet([(PLANE, gather.others)])
    gather.begin(local_sem)

    def hand_on(seq):
        return send_on(ends.at[seq], starts.at[seq], send_sem.at[seq], recv_sem.at[seq], 1)

    def store(block):
        slot = lax.rem(block, 2)
        rows = groups * SUB
        return pltpu.make_async_copy(
            prior_buf.at[slot],
            prior_ref.at[pl.ds(pl.multiple_of(block * rows, rows), rows)],
            prior_sem.at[slot],
        )

    def one_sequence(seq):
        @pl.when(place == 0)
        def _():
            carried[...] = jnp.zeros_like(carried)

        @pl.when(place == 1)
        def _():
            hand_on(seq).wait_recv()
            carried[...] = starts[seq]

        @pl.loop(0, blocks)
        def _(inner_block):
            block = seq * blocks + inner_block
            slot = lax.rem(block, 2)

            @pl.when(block >= 2)
            def _():
                store(block - 2).wait()

            def one(turn, states):
                group = block * groups + turn
                states = list(states)
                stage_in(step_ref, group, step_held)
                stage_in(input_ref, group, input_held)
                for at in range(SUB):
                    step = token_row(step_held, at, tiles)
                    drive = step * token_row(input_held, at, tiles)
                    mixed = [None] * 2
                    for n in range(n_state):
                        where = (group * SUB + at) * n_state + n
                        prior_buf[slot, turn * SUB + at, n] = states[n]
                        decay = jnp.exp2(step * rate_ref[n])
                        states[n] = decay * states[n] + drive * brow_ref[where]
                        term = states[n] * crow_ref[where]
                        mixed[n % 2] = term if mixed[n % 2] is None else mixed[n % 2] + term
                    mixed_held[pl.ds(at, tiles, stride=SUB), :] = mixed[0] + mixed[1]
                stage_out(mixed_held, mixed_ref, group)
                return tuple(states)

            states = lax.fori_loop(0, groups, one, tuple(carried[n] for n in range(n_state)))
            for n in range(n_state):
                carried[n] = states[n]
            store(block).start()

        @pl.when(place == 0)
        def _():
            ends[seq] = carried[...]
            hand_on(seq).start()

    for seq in range(seqs):
        one_sequence(seq)
        if seq == 0:
            gather.relay()
            gather.hand_over()
    gather.hand_over_last()
    for block in range(max(0, seqs * blocks - 2), seqs * blocks):
        store(block).wait()

    @pl.when(place == 0)
    def _():
        for seq in range(seqs):
            hand_on(seq).wait_send()

    gather.end()


def scan_forward_pair(call_id, step, inputs, b_rows, c_rows, rate, seqs, shard):
    n_state, tiles, _ = rate.shape
    tokens, inner = step.shape
    all_groups = tokens // SUB
    groups = math.gcd(all_groups // seqs, 4)
    blocks = all_groups // seqs // groups
    vmem = pl.BlockSpec(memory_space=pltpu.VMEM)
    smem = pl.BlockSpec(memory_space=pltpu.SMEM)
    hbm = pl.BlockSpec(memory_space=pl.ANY)
    full = jnp.float32
    held = pltpu.VMEM((tiles * SUB, LANE), full)
    boundary = pltpu.VMEM((seqs, n_state, tiles, LANE), full)
    dma = pltpu.SemaphoreType.DMA
    return pl.pallas_call(
        functools.partial(forward_pair_kernel, n_state, tiles, groups, blocks, seqs),
        in_specs=[vmem, vmem, smem, smem, vmem, hbm],
        out_specs=[hbm, vmem, hbm],
        out_shape=[
            jax.ShapeDtypeStruct((tokens, n_state, tiles, LANE), full),
            jax.ShapeDtypeStruct(step.shape, full),
            gathered_shape(shard),
        ],
        scratch_shapes=[
            pltpu.VMEM((n_state, tiles, LANE), full),
            boundary,
            boundary,
            pltpu.VMEM((2, groups * SUB, n_state, tiles, LANE), full),
            held,
            held,
            held,
            dma((2,)),
            dma((seqs,)),
            dma((seqs,)),
        ]
        + gather_scratch(),
        compiler_params=pltpu.CompilerParams(
            collective_id=call_id, has_side_effects=True, vmem_limit_bytes=40 * 2**20
        ),
    )(step, inputs, b_rows, c_rows, rate, shard)


def backward_pair_kernel(
    n_state,
    tiles,
    groups,
    blocks,
    seqs,
    step_ref,
    input_ref,
    ograd_ref,
    brow_ref,
    crow_ref,
    rate_ref,
    picks_ref,
    ffn_part,
    middle,
    prior_ref,
    step_grad_ref,
    input_grad_ref,
    rate_grad_ref,
    part_ref,
    layer_rows,
    carried,
    ends,
    starts,
    prior_buf,
    step_held,
    input_held,
    ograd_held,
    step_grad_held,
    input_grad_held,
    ffn_slots,
    prior_sem,
    send_sem,
    recv_sem,
    tp_send,
    tp_recv,
):
    place = lax.axis_index("ctx")
    tp = Group(("tp",), tp_send, tp_recv)
    greet([(("ctx",), [1 - place]), (("tp",), tp.others)])
    ffn_sent = tp.scatter(ffn_part, ffn_slots, 0)

    def hand_on(seq):
        return send_on(ends.at[seq], starts.at[seq], send_sem.at[seq], recv_sem.at[seq], 0)

    def fetch(turn):
        seq = lax.div(turn, blocks)
        block = seq * blocks + blocks - 1 - lax.rem(turn, blocks)
        slot = lax.rem(turn, 2)
        rows = groups * SUB
        return pltpu.make_async_copy(
            prior_ref.at[pl.ds(pl.multiple_of(block * rows, rows), rows)],
            prior_buf.at[slot],
            prior_sem.at[slot],
        )

    fetch(0).start()
    rate_grad_ref[...] = jnp.zeros_like(rate_grad_ref)

    @pl.when(place == 1)
    def _():
        @pl.loop(0, seqs)
        def _(seq):
            def one(turn, grads):
                group = (seq + 1) * blocks * groups - 1 - turn
                grads = list(grads)
                stage_in(step_ref, group, step_held)
                stage_in(ograd_ref, group, ograd_held)
                for at in range(SUB - 1, -1, -1):
                    step = token_row(step_held, at, tiles)
                    ograd = token_row(ograd_held, at, tiles)
                    for n in range(n_state):
                        row = crow_ref[(group * SUB + at) * n_state + n]
                        grads[n] = jnp.exp2(step * rate_ref[n]) * (grads[n] + ograd * row)
                return tuple(grads)

            zero = jnp.zeros((tiles, LANE), jnp.float32)
            grads = lax.fori_loop(0, blocks * groups, one, (zero,) * n_state)
            for n in range(n_state):
                ends[seq, n] = grads[n]
            hand_on(seq).start()

    @pl.loop(0, seqs)
    def _(seq):
        @pl.when(place == 1)
        def _():
            carried[...] = jnp.zeros_like(carried)

        @pl.when(place == 0)
        def _():
            hand_on(seq).wait_recv()
            carried[...] = starts[seq]

        @pl.loop(0, blocks)
        def _(inner_block):
            turn = seq * blocks + inner_block
            slot = lax.rem(turn, 2)
            first_group = (seq * blocks + blocks - 1 - inner_block) * groups

            @pl.when(turn + 1 < seqs * blocks)
            def _():
                fetch(turn + 1).start()

            fetch(turn).wait()

            def one(back, grads):
                inner_group = groups - 1 - back
                group = first_group + inner_group
                grads = list(grads)
                stage_in(step_ref, group, step_held)
                stage_in(input_ref, group, input_held)
                stage_in(ograd_ref, group, ograd_held)
                for at in range(SUB - 1, -1, -1):
                    step = token_row(step_held, at, tiles)
                    value = token_row(input_held, at, tiles)
                    ograd = token_row(ograd_held, at, tiles)
                    drive = step * value
                    along_b = None
                    along_rate = None
                    brow_parts, crow_parts = [], []
                    for n in range(n_state):
                        where = (group * SUB + at) * n_state + n
                        brow, crow = brow_ref[where], crow_ref[where]
                        rate = rate_ref[n]
                        decay = jnp.exp2(step * rate)
                        grad = ograd * crow + grads[n]
                        kept = decay * prior_buf[slot, inner_group * SUB + at, n]
                        state = kept + drive * brow
                        decay_term = grad * kept
                        grads[n] = decay * grad
                        rate_grad_ref[n] += decay_term * step
                        by_rate, by_brow = decay_term * rate, grad * brow
                        along_rate = by_rate if along_rate is None else along_rate + by_rate
                        along_b = by_brow if along_b is None else along_b + by_brow
                        brow_parts.append(grad * drive)
                        crow_parts.append(ograd * state)
                    step_grad_held[pl.ds(at, tiles, stride=SUB), :] = (
                        along_rate * LN2 + along_b * value
                    )
                    input_grad_held[pl.ds(at, tiles, stride=SUB), :] = along_b * step
                    parts = jnp.concatenate(brow_parts + crow_parts, 0).astype(jnp.bfloat16)
                    part_ref[group * SUB + at] = jnp.dot(
                        picks_ref[...], parts, preferred_element_type=jnp.float32
                    )
                stage_out(step_grad_held, step_grad_ref, group)
                stage_out(input_grad_held, input_grad_ref, group)
                return tuple(grads)

            grads = lax.fori_loop(0, groups, one, tuple(carried[n] for n in range(n_state)))
            for n in range(n_state):
                carried[n] = grads[n]

    finish(ffn_sent)
    layer_rows[...] = (middle[...] + tp.total(ffn_part, ffn_slots)).astype(layer_rows.dtype)

    @pl.when(place == 1)
    def _():
        @pl.loop(0, seqs)
        def _(seq):
            hand_on(seq).wait_send()


def scan_backward_pair(
    call_id, prior, step, inputs, ograd, b_rows, c_rows, rate, seqs, ffn_part, middle
):
    n_state, tiles, _ = rate.shape
    tokens, inner = step.shape
    all_groups = tokens // SUB
    groups = math.gcd(all_groups // seqs, 4)
    blocks = all_groups // seqs // groups
    tp_count = group_size(("tp",))
    vmem = pl.BlockSpec(memory_space=pltpu.VMEM)
    smem = pl.BlockSpec(memory_space=pltpu.SMEM)
    full = jnp.float32
    held = pltpu.VMEM((tiles * SUB, LANE), full)
    boundary = pltpu.VMEM((seqs, n_state, tiles, LANE), full)
    dma = pltpu.SemaphoreType.DMA
    picks = jnp.repeat(jnp.eye(2 * n_state, dtype=jnp.bfloat16), tiles, 1)
    return pl.pallas_call(
        functools.partial(backward_pair_kernel, n_state, tiles, groups, blocks, seqs),
        in_specs=[vmem] * 3 + [smem] * 2 + [vmem] * 4 + [pl.BlockSpec(memory_space=pl.ANY)],
        out_specs=[vmem] * 5,
        out_shape=[
            jax.ShapeDtypeStruct(step.shape, full),
            jax.ShapeDtypeStruct(step.shape, full),
            jax.ShapeDtypeStruct(rate.shape, full),
            jax.ShapeDtypeStruct((tokens, 2 * n_state, LANE), full),
            jax.ShapeDtypeStruct(middle.shape, jnp.bfloat16),
        ],
        scratch_shapes=[
            pltpu.VMEM((n_state, tiles, LANE), full),
            boundary,
            boundary,
            pltpu.VMEM((2, groups * SUB, n_state, tiles, LANE), full),
        ]
        + [held] * 5
        + [
            slots_for(ffn_part, tp_count),
            dma((2,)),
            dma((seqs,)),
            dma((seqs,)),
            dma((1, tp_count - 1)),
            dma((1, tp_count - 1)),
        ],
        compiler_params=pltpu.CompilerParams(
            collective_id=call_id, has_side_effects=True, vmem_limit_bytes=48 * 2**20
        ),
    )(step, inputs, ograd, b_rows, c_rows, rate, picks, ffn_part, middle, prior)


class PlaneGather:
    def __init__(self, own, gathered, send_sem, recv_sem):
        self.own, self.gathered = own, gathered
        self.send_sem, self.recv_sem = send_sem, recv_sem
        self.dp, self.ctx = lax.axis_index("dp"), lax.axis_index("ctx")
        self.n_dp, self.n_ctx = lax.axis_size("dp"), lax.axis_size("ctx")
        self.hands_on = relayed()
        self.count = self.n_dp * self.n_ctx
        self.me = self.dp * self.n_ctx + self.ctx
        self.others = [lax.rem(self.me + hop, self.count) for hop in range(1, self.count)]
        self.copies = {}
        if self.hands_on:
            core = lax.rem(self.dp, 2)
            over_core = self.dp + 1 - 2 * core
            over_y = lax.rem(self.dp + 2, 4)
            over_x = 1 - self.ctx
            self.core = {"dp": over_core, "ctx": self.ctx}
            self.at_x = {"dp": self.dp, "ctx": over_x}
            self.at_y = {"dp": over_y, "ctx": self.ctx}
            self.from_x = self.dp * 2 + over_x
            self.from_y = over_y * 2 + self.ctx
            self.across = over_y * 2 + over_x

    def part(self, owner, half):
        rows = self.gathered.shape[0] // self.count
        start, size = owner * rows, rows
        if half is not None:
            size = rows // 2
            start = start + half * size
        return self.gathered.at[pl.ds(pl.multiple_of(start, size), size), :]

    def send(self, which, owner, half, where):
        target = self.part(owner, half)
        source = target
        if owner is self.me:
            rows = self.own.shape[0]
            source = self.own
            if half is not None:
                source = self.own.at[pl.ds(half * (rows // 2), rows // 2), :]
        self.copies[which] = sent(
            source, target, self.send_sem.at[which], self.recv_sem.at[which], where
        )

    def arrived(self, *which):
        for one in which:
            self.copies[one].wait_recv()

    def begin(self, local_sem):
        self.local = pltpu.make_async_copy(self.own, self.part(self.me, None), local_sem)
        self.local.start()
        if not self.hands_on:
            for hop, other in enumerate(self.others):
                self.send(hop, self.me, None, device_at(PLANE, other))
            return
        self.send(0, self.me, 1, self.at_x)
        self.send(1, self.me, 0, self.at_y)
        self.send(2, self.me, None, self.core)
        self.send(3, self.me, 0, self.at_x)
        self.send(4, self.me, 1, self.at_y)

    def relay(self):
        if not self.hands_on:
            return
        self.arrived(0, 1)
        self.send(5, self.from_x, 1, self.at_y)
        self.send(6, self.from_y, 0, self.at_x)
        self.send(7, self.from_x, 1, self.core)
        self.send(8, self.from_y, 0, self.core)

    def hand_over(self):
        if not self.hands_on:
            return
        self.arrived(3, 4)
        self.send(9, self.from_x, 0, self.core)
        self.send(10, self.from_y, 1, self.core)

    def hand_over_last(self):
        if not self.hands_on:
            return
        self.arrived(5, 6)
        self.send(11, self.across, 1, self.core)
        self.send(12, self.across, 0, self.core)

    def end(self):
        if self.hands_on:
            self.arrived(2, 7, 8, 9, 10, 11, 12)
        else:
            self.arrived(*range(self.count - 1))
        for copy in self.copies.values():
            copy.wait_send()
        self.local.wait()


def relayed():
    return lax.axis_size("dp") == 4 and lax.axis_size("ctx") == 2


def gather_sems():
    count = 13 if relayed() else group_size(PLANE) - 1
    return pltpu.SemaphoreType.DMA((count,))


WIDE = 512


def products(source, first, last, dot, target, block_buf, block_sem, out_buf, out_sem):
    def fetch(j, slot):
        columns = pl.ds(pl.multiple_of(j * WIDE, WIDE), WIDE)
        return pltpu.make_async_copy(
            source.at[:, columns], block_buf.at[slot], block_sem.at[slot]
        )

    def store(j, slot):
        return pltpu.make_async_copy(out_buf.at[slot], target(j), out_sem.at[slot])

    fetch(first, first % 2).start()

    @pl.loop(first, last)
    def _(j):
        slot = lax.rem(j, 2)

        @pl.when(j + 1 < last)
        def _():
            fetch(j + 1, 1 - slot).start()

        fetch(j, slot).wait()

        @pl.when(j >= first + 2)
        def _():
            store(j - 2, slot).wait()

        out_buf[slot] = dot(block_buf[slot])
        store(j, slot).start()

    for j in range(max(first, last - 2), last):
        store(j, j % 2).wait()


def tail_kernel(
    sizes,
    mix_grads,
    normed_part,
    small,
    tokens,
    middle_grad,
    gain_row,
    one_cols,
    two_cols,
    ct_cols,
    middle_cols,
    ffn_all,
    gated_all,
    tokens_grad,
    small_sum,
    gains,
    mix_all,
    grad_inproj,
    grad_outproj,
    grad_gateup,
    grad_downproj,
    normed_slots,
    small_slots,
    gain_slots,
    gain_own,
    block_buf,
    wide_buf,
    tall_buf,
    block_sem,
    wide_sem,
    tall_sem,
    tp_send,
    tp_recv,
    plane_send,
    plane_recv,
    gather_send,
    gather_recv,
    local_sem,
):
    inner, hidden, gain_at = sizes
    tp = Group(("tp",), tp_send, tp_recv)
    plane = Group(PLANE, plane_send, plane_recv)
    gather = PlaneGather(mix_grads, mix_all, gather_send, gather_recv)
    greet([(("tp",), tp.others), (PLANE, plane.others)])

    def flat(lhs):
        return lambda block: lax.dot_general(
            lhs[...], block, (((0,), (0,)), ((), ())), preferred_element_type=jnp.float32
        )

    def tall(rhs):
        return lambda block: lax.dot_general(
            block, rhs[...], (((0,), (0,)), ((), ())), preferred_element_type=jnp.float32
        )

    def side_by_side(ref, first):
        per = ref.shape[2] // WIDE

        def target(j):
            at = j - first
            columns = pl.ds(pl.multiple_of(lax.rem(at, per) * WIDE, WIDE), WIDE)
            return ref.at[lax.div(at, per), :, columns]

        return target

    def one_above_other(ref, first):
        return lambda j: ref.at[pl.ds(pl.multiple_of((j - first) * WIDE, WIDE), WIDE), :]

    wide = (block_buf, block_sem, wide_buf, wide_sem)
    high = (block_buf, block_sem, tall_buf, tall_sem)
    down_end = hidden // WIDE
    gu_end = 3 * hidden // WIDE

    normed_sent = tp.scatter(normed_part, normed_slots, 0)
    gather.begin(local_sem)
    small_sent = plane.scatter(small, small_slots, 0)
    products(
        ffn_all, down_end, gu_end, flat(two_cols), side_by_side(grad_gateup, down_end), *wide
    )
    gather.relay()
    products(ffn_all, 0, down_end, tall(ct_cols), one_above_other(grad_downproj, 0), *high)
    gather.hand_over()
    finish(normed_sent)
    hidden_in = tp.own(tokens)[...].astype(jnp.float32)
    tp.own(tokens_grad)[...] = (
        middle_grad[...]
        + norm_back(
            tp.total(normed_part, normed_slots),
            hidden_in,
            inverse_rms(hidden_in),
            gain_row[...].astype(jnp.float32),
        )
    ).astype(tokens_grad.dtype)
    tokens_sent = tp.spread(tokens_grad, 1)
    finish(small_sent)
    plane.own(small_sum)[...] = plane.total(small, small_slots).astype(small_sum.dtype)
    small_sent = plane.spread(small_sum, 1)
    products(
        gated_all, 0, inner // WIDE, tall(middle_cols), one_above_other(grad_outproj, 0), *high
    )
    gather.hand_over_last()
    finish(small_sent)
    gain_own[...] = small_sum[pl.ds(gain_at, gain_own.shape[0]), :].astype(jnp.float32)
    gain_sent = [tp.one(gain_own, gain_slots.at[hop], 2, hop) for hop in range(tp.count - 1)]
    gather.end()
    products(
        mix_all, 0, 2 * inner // WIDE, flat(one_cols), side_by_side(grad_inproj, 0), *wide
    )
    finish(gain_sent)
    total = gain_own[...]
    for hop in range(tp.count - 1):
        total = total + gain_slots[hop]
    gains[...] = total
    finish(tokens_sent)


def run_tail(
    call_id,
    gain_at,
    mix_grads,
    normed_part,
    small,
    tokens,
    middle_grad,
    gain_row,
    one_cols,
    two_cols,
    ct_cols,
    middle_cols,
    ffn_all,
    gated_all,
):
    inner = mix_grads.shape[1] // 2
    hidden = ffn_all.shape[1] // 3
    share = one_cols.shape[1]
    all_rows = ffn_all.shape[0]
    tp_count, plane_count = group_size(("tp",)), group_size(PLANE)
    low, full = jnp.bfloat16, jnp.float32
    vmem = pl.BlockSpec(memory_space=pltpu.VMEM)
    hbm = pl.BlockSpec(memory_space=pl.ANY)
    gain_rows = 16
    dma = pltpu.SemaphoreType.DMA
    return pl.pallas_call(
        functools.partial(tail_kernel, (inner, hidden, gain_at)),
        in_specs=[vmem] * 10 + [hbm] * 2,
        out_specs=[vmem] * 3 + [hbm] * 5,
        out_shape=[
            jax.ShapeDtypeStruct(tokens.shape, low),
            jax.ShapeDtypeStruct(small.shape, low),
            jax.ShapeDtypeStruct((gain_rows, inner), full),
            jax.ShapeDtypeStruct((all_rows, 2 * inner), low),
            jax.ShapeDtypeStruct((2, share, inner), full),
            jax.ShapeDtypeStruct((inner, share), full),
            jax.ShapeDtypeStruct((2, share, hidden), full),
            jax.ShapeDtypeStruct((hidden, share), full),
        ],
        scratch_shapes=[
            slots_for(normed_part, tp_count),
            slots_for(small, plane_count),
            pltpu.VMEM((tp_count - 1, gain_rows, inner), full),
            pltpu.VMEM((gain_rows, inner), full),
            pltpu.VMEM((2, all_rows, WIDE), low),
            pltpu.VMEM((2, share, WIDE), full),
            pltpu.VMEM((2, WIDE, share), full),
            dma((2,)),
            dma((2,)),
            dma((2,)),
            dma((3, tp_count - 1)),
            dma((3, tp_count - 1)),
            dma((2, plane_count - 1)),
            dma((2, plane_count - 1)),
            gather_sems(),
            gather_sems(),
            dma(()),
        ],
        compiler_params=pltpu.CompilerParams(
            collective_id=call_id, has_side_effects=True, vmem_limit_bytes=56 * 2**20
        ),
    )(
        mix_grads,
        normed_part,
        small,
        tokens,
        middle_grad,
        gain_row,
        one_cols,
        two_cols,
        ct_cols,
        middle_cols,
        ffn_all,
        gated_all,
    )


def head_kernel(
    tokens,
    gain,
    in_conv,
    in_gate,
    conv_in,
    gate_mix,
    conv_all,
    gate_all,
    normed,
    block_buf,
    block_sem,
    *sems,
):
    conv = PlaneGather(in_conv, conv_all, *sems[:2])
    gate = PlaneGather(in_gate, gate_all, *sems[3:5])
    greet([(PLANE, conv.others)])
    conv.begin(sems[2])
    gate.begin(sems[5])
    hidden_in = tokens[...].astype(jnp.float32)
    normed[...] = (hidden_in * inverse_rms(hidden_in) * gain[...].astype(jnp.float32)).astype(
        normed.dtype
    )

    def product(source, target):
        columns = range(0, source.shape[1], WIDE)

        def fetch(turn):
            at = columns[turn]
            return pltpu.make_async_copy(
                source.at[:, at : at + WIDE], block_buf.at[turn % 2], block_sem.at[turn % 2]
            )

        fetch(0).start()
        for turn, at in enumerate(columns):
            if turn + 1 < len(columns):
                fetch(turn + 1).start()
            fetch(turn).wait()
            target[:, at : at + WIDE] = matmul(normed[...], block_buf[turn % 2]).astype(
                target.dtype
            )

    conv.relay()
    conv.hand_over()
    gate.relay()
    conv.hand_over_last()
    gate.hand_over()
    conv.end()
    product(conv_all, conv_in)
    gate.hand_over_last()
    gate.end()
    product(gate_all, gate_mix)


def run_head(call_id, tokens, gain, inproj):
    rows, width = tokens.shape
    inner = inproj.shape[2]
    low = jnp.bfloat16
    vmem = pl.BlockSpec(memory_space=pltpu.VMEM)
    hbm = pl.BlockSpec(memory_space=pl.ANY)
    return pl.pallas_call(
        head_kernel,
        in_specs=[vmem] * 2 + [hbm] * 2,
        out_specs=[vmem] * 2 + [hbm] * 2,
        out_shape=[
            jax.ShapeDtypeStruct((rows, inner), low),
            jax.ShapeDtypeStruct((rows, inner), jnp.float32),
            jax.ShapeDtypeStruct((width, inner), low),
            jax.ShapeDtypeStruct((width, inner), low),
        ],
        scratch_shapes=[
            pltpu.VMEM((rows, width), low),
            pltpu.VMEM((2, width, WIDE), low),
            pltpu.SemaphoreType.DMA((2,)),
        ]
        + gather_scratch() * 2,
        compiler_params=pltpu.CompilerParams(
            collective_id=call_id, has_side_effects=True, vmem_limit_bytes=40 * 2**20
        ),
    )(tokens, gain, inproj[0], inproj[1])


def per_device(
    tokens,
    mixgain,
    inproj,
    convkern,
    convbias,
    selproj,
    stepproj,
    stepbias,
    decaylog,
    skipgain,
    outproj,
    ffngain,
    gateup,
    downproj,
    cotangent,
):
    seqs, span, width = tokens.shape
    rows = seqs * span
    taps, inner = convkern.shape
    rank = stepproj.shape[0]
    n_state = decaylog.shape[1]
    tiles = inner // LANE
    gain_mix = mixgain.astype(jnp.float32)
    kernel = convkern.astype(jnp.float32)
    kernel_bias = convbias.astype(jnp.float32)
    step_bias = stepbias.astype(jnp.float32)
    skip_weight = skipgain.astype(jnp.float32)
    decay_rate = -jnp.exp(jnp.transpose(decaylog.astype(jnp.float32)))
    rate = (decay_rate * LOG2E).reshape(n_state, tiles, LANE)

    gain_mix_row, gain_ffn_row = mixgain.reshape(1, width), ffngain.reshape(1, width)
    low = jnp.bfloat16

    tokens_rows = tokens.reshape(rows, width)
    ct_low = cotangent.reshape(rows, width)
    ffn_pack = gathered_rows(
        jnp.concatenate([gateup[0], gateup[1], jnp.transpose(downproj)], 1)
    )
    conv_in, gate_mix, in_conv, in_gate = run_head(5, tokens_rows, gain_mix_row, inproj)
    hidden_in = tokens_rows.astype(jnp.float32)
    scale_one = inverse_rms(hidden_in)
    normed_one = (hidden_in * scale_one * gain_mix).astype(low)

    conv_seqs = conv_in.reshape(seqs, span, inner)
    rim_rows = passed_along(conv_seqs[:, span - (taps - 1) :], "ctx", 1)
    padded_in = jnp.concatenate([rim_rows, conv_seqs], 1).astype(jnp.float32)
    conv_out = kernel_bias[None, None]
    for offset in range(taps):
        conv_out = conv_out + kernel[offset][None, None] * padded_in[:, offset : offset + span]
    conv_out = conv_out.reshape(rows, inner)
    scan_in = jax.nn.silu(conv_out).astype(low)
    scan_float = scan_in.astype(jnp.float32)
    columns = selproj.shape[1]
    select_width = -(-columns // LANE) * LANE
    select_weights = jnp.pad(selproj, ((0, 0), (0, select_width - columns)))
    select_cols, out_first = sum_over_tp(
        0, matmul(scan_in, select_weights), [], [], [outproj[: inner // 2]]
    )
    step_low = select_cols[:, :rank].astype(low)
    b_rows = select_cols[:, rank : rank + n_state].reshape(-1)
    c_rows = select_cols[:, rank + n_state : columns].reshape(-1)
    step_pre = matmul(step_low, stepproj) + step_bias[None]
    step_size = jax.nn.softplus(step_pre)
    in_pairs = lax.axis_size("ctx") == 2
    if in_pairs:
        prior, scan_out, out_last = scan_forward_pair(
            6, step_size, scan_float, b_rows, c_rows, rate, seqs, outproj[inner // 2 :]
        )
    else:
        span_decay = jnp.exp(
            decay_rate[None] * jnp.sum(step_size.reshape(seqs, span, inner), 1)[:, None]
        ).reshape(seqs, n_state, tiles, LANE)
        ends = scan_ends(step_size, scan_float, b_rows, rate, seqs, False)
        start = from_earlier(ends, span_decay, 1)
        prior, scan_out = scan_forward(start, step_size, scan_float, b_rows, c_rows, rate, seqs)
        out_last = gathered_rows(outproj[inner // 2 :])
    mixer_core = scan_out + skip_weight[None] * scan_float
    gate_sig = jax.nn.silu(gate_mix)
    gated = (mixer_core * gate_sig).astype(low)
    swap_now = swaps_in_kernels(width)
    normed_two, middle, gated_all, *swapped = mixer_out(
        1,
        gated,
        out_first,
        out_last,
        tokens_rows,
        gain_ffn_row,
        [normed_one] if swap_now else [],
    )
    (normed_one_cols,) = swapped if swap_now else [swapped_columns(normed_one)]
    made, *swapped = run_ffn(8, normed_two, ct_low, ffn_pack, swap_now)
    if not swap_now:
        swapped = [swapped_columns(normed_two), swapped_columns(ct_low)]
    normed_two_cols, ct_cols = swapped
    ffn_all = gathered_rows(made)
    middle_low, middle_grad, ffngain_part, gated_grad, ffn_part = ffn_back(
        2, made, ct_low, middle, gain_ffn_row, out_first, out_last, ffn_pack
    )
    core_grad = gated_grad * gate_sig
    gate_mix_grad = (gated_grad * mixer_core * silu_slope(gate_mix)).astype(low)
    grad_skipgain = jnp.sum(core_grad * scan_float, 0)
    if in_pairs:
        step_grad, input_grad, rate_grad, parts, layer_rows = scan_backward_pair(
            7,
            prior,
            step_size,
            scan_float,
            core_grad,
            b_rows,
            c_rows,
            rate,
            seqs,
            ffn_part,
            middle,
        )
    else:
        back_ends = scan_ends(step_size, core_grad, c_rows, rate, seqs, True)
        end_grad = from_earlier(back_ends, span_decay, -1)
        step_grad, input_grad, rate_grad, parts = scan_backward(
            end_grad, prior, step_size, scan_float, core_grad, b_rows, c_rows, rate, seqs
        )
        ffn_sum = lax.psum_scatter(ffn_part, "tp", scatter_dimension=0, tiled=True)
        layer_rows = (middle + ffn_sum.astype(jnp.float32)).astype(low)
    grad_decaylog = rate_grad.reshape(n_state, inner) * decay_rate
    pre_grad = step_grad * jax.nn.sigmoid(step_pre)
    grad_stepbias = jnp.sum(pre_grad, 0)
    pre_low = pre_grad.astype(low)
    grad_stepproj = matmul_tn(step_low, pre_low)
    select_part = jnp.concatenate(
        [
            matmul_nt(pre_low, stepproj),
            jnp.sum(parts, -1),
            jnp.zeros((rows, select_width - columns), jnp.float32),
        ],
        1,
    ).astype(low)
    select_low, layer_out, *swapped = sum_over_tp(
        3, select_part, [layer_rows], [middle_low] if swap_now else [], []
    )
    (middle_cols,) = swapped if swap_now else [swapped_columns(middle_low)]
    grad_selproj = matmul_tn(select_low, scan_in)
    scan_in_grad = (
        core_grad * skip_weight[None]
        + input_grad
        + matmul_nt(select_low, select_weights)
    )
    conv_grad = scan_in_grad * silu_slope(conv_out)
    grad_convbias = jnp.sum(conv_grad, 0)
    conv_grad_seqs = conv_grad.reshape(seqs, span, inner)
    padded_grad = jnp.zeros(padded_in.shape, jnp.float32)
    kernel_rows = []
    for offset in range(taps):
        kernel_rows.append(jnp.sum(conv_grad_seqs * padded_in[:, offset : offset + span], (0, 1)))
        padded_grad = padded_grad + jnp.pad(
            kernel[offset][None, None] * conv_grad_seqs,
            ((0, 0), (offset, taps - 1 - offset), (0, 0)),
        )
    grad_convkern = jnp.stack(kernel_rows)
    returned = passed_along(padded_grad[:, : taps - 1], "ctx", -1)
    conv_in_grad = (
        (padded_grad[:, taps - 1 :] + jnp.pad(returned, ((0, 0), (span - taps + 1, 0), (0, 0))))
        .astype(low)
        .reshape(rows, inner)
    )
    mix_grads = jnp.concatenate([conv_in_grad, gate_mix_grad], 1)
    normed_one_part = matmul_nt(conv_in_grad, in_conv) + matmul_nt(gate_mix_grad, in_gate)
    mixgain_part = jnp.sum(normed_one_part * hidden_in * scale_one, 0)
    normed_one_part = normed_one_part.astype(low)
    small = [
        grad_convkern,
        grad_convbias[None],
        grad_stepbias[None],
        grad_decaylog,
        grad_skipgain[None],
        grad_stepproj,
        grad_selproj[:columns],
        mixgain_part.reshape(-1, inner),
        ffngain_part.reshape(-1, inner),
    ]
    sizes = [part.shape[0] for part in small]
    gain_at = sum(sizes[:-2]) + -sum(sizes[:-2]) % 16
    small.insert(-2, jnp.zeros((gain_at - sum(sizes[:-2]), inner), jnp.float32))
    small = jnp.concatenate(small, 0).astype(low)
    share = 16 * group_size(PLANE)
    small = jnp.pad(small, ((0, -(gain_at + 16) % share + 16 - sum(sizes[-2:])), (0, 0)))
    (
        tokens_grad,
        small,
        gains,
        _,
        grad_inproj,
        grad_outproj,
        grad_gateup,
        grad_downproj,
    ) = run_tail(
        4,
        gain_at,
        mix_grads,
        normed_one_part,
        small,
        tokens_rows,
        middle_grad,
        gain_mix_row,
        normed_one_cols,
        normed_two_cols,
        ct_cols,
        middle_cols,
        ffn_all,
        gated_all,
    )
    small = small.astype(jnp.float32)
    smalls, at = [], 0
    for size in sizes[:-2]:
        smalls.append(small[at : at + size])
        at += size
    gains = gains[: sum(sizes[-2:])].reshape(2, width)
    return (
        layer_out.reshape(tokens.shape),
        tokens_grad.reshape(tokens.shape),
        gains[0],
        grad_inproj,
        smalls[0],
        smalls[1][0],
        jnp.transpose(smalls[6]),
        smalls[5],
        smalls[2][0],
        jnp.transpose(smalls[3]),
        smalls[4][0],
        grad_outproj,
        gains[1],
        grad_gateup,
        grad_downproj,
    )


def solution(mesh):
    in_specs = (
        P("dp", "ctx", None),
        P(),
        P(None, ("dp", "ctx"), "tp"),
        P(None, "tp"),
        P("tp"),
        P("tp", None),
        P(None, "tp"),
        P("tp"),
        P("tp", None),
        P("tp"),
        P("tp", ("dp", "ctx")),
        P(),
        P(None, ("dp", "ctx"), "tp"),
        P("tp", ("dp", "ctx")),
        P("dp", "ctx", None),
    )
    out_specs = (
        P("dp", "ctx", None),
        P("dp", "ctx", None),
        P(),
        P(None, ("dp", "ctx"), "tp"),
        P(None, "tp"),
        P("tp"),
        P("tp", None),
        P(None, "tp"),
        P("tp"),
        P("tp", None),
        P("tp"),
        P("tp", ("dp", "ctx")),
        P(),
        P(None, ("dp", "ctx"), "tp"),
        P("tp", ("dp", "ctx")),
    )
    return jax.shard_map(
        per_device, mesh=mesh, in_specs=in_specs, out_specs=out_specs, check_vma=False
    )
```

```python
import functools
import math

import jax
import jax.numpy as jnp
from jax import lax
from jax.experimental import pallas as pl
from jax.experimental.pallas import tpu as pltpu
from jax.sharding import PartitionSpec as P

EPSILON = 1e-05
LOG2E = math.log2(math.e)
LN2 = math.log(2.0)
SUB = 8
LANE = 128
VMEM_GRANT = 60 * 2**20
PLANE = ("dp", "ctx")


def passed_along(value, axis, steps):
    count = lax.axis_size(axis)
    first, last = (max(0, -steps), min(count, count - steps))
    return lax.ppermute(value, axis, [(source, source + steps) for source in range(first, last)])


def matmul(left, right):
    return jnp.dot(left, right, preferred_element_type=jnp.float32)


def matmul_nt(left, right):
    return lax.dot_general(
        left, right, (((1,), (1,)), ((), ())), preferred_element_type=jnp.float32
    )


def matmul_tn(left, right):
    return lax.dot_general(
        left, right, (((0,), (0,)), ((), ())), preferred_element_type=jnp.float32
    )


def inverse_rms(values):
    return lax.rsqrt(jnp.mean(values * values, -1, keepdims=True) + EPSILON)


def silu_slope(values):
    logistic = jax.nn.sigmoid(values)
    return logistic * (1.0 + values * (1.0 - logistic))


def norm_back(grad_norm, values, scale, gain):
    scaled_grad = grad_norm * gain
    unit_rows = values * scale
    return scale * (scaled_grad - unit_rows * jnp.mean(scaled_grad * unit_rows, -1, keepdims=True))


def stage_in(ref, group, held):
    for tile in range(held.shape[0] // SUB):
        held[pl.ds(tile * SUB, SUB), :] = ref[
            pl.ds(pl.multiple_of(group * SUB, SUB), SUB), pl.ds(tile * LANE, LANE)
        ]


def stage_out(held, ref, group):
    for tile in range(held.shape[0] // SUB):
        ref[pl.ds(pl.multiple_of(group * SUB, SUB), SUB), pl.ds(tile * LANE, LANE)] = held[
            pl.ds(tile * SUB, SUB), :
        ]


def token_row(held, at, tiles):
    return held[pl.ds(at, tiles, stride=SUB), :]


def ends_kernel(
    n_state,
    tiles,
    groups,
    reverse,
    step_ref,
    drive_ref,
    rows_ref,
    rate_ref,
    end_ref,
    step_held,
    drive_held,
):
    base = pl.program_id(0) * groups * SUB * n_state
    rates = [rate_ref[n] for n in range(n_state)]

    def one(turn, states):
        group = groups - 1 - turn if reverse else turn
        order = range(SUB - 1, -1, -1) if reverse else range(SUB)
        states = list(states)
        stage_in(step_ref, group, step_held)
        stage_in(drive_ref, group, drive_held)
        for at in order:
            step = token_row(step_held, at, tiles)
            drive = token_row(drive_held, at, tiles)
            if not reverse:
                drive = drive * step
            for n in range(n_state):
                row = rows_ref[base + (group * SUB + at) * n_state + n]
                decay = jnp.exp2(step * rates[n])
                if reverse:
                    states[n] = decay * (states[n] + drive * row)
                else:
                    states[n] = decay * states[n] + drive * row
        return tuple(states)

    zero = jnp.zeros((tiles, LANE), jnp.float32)
    states = lax.fori_loop(0, groups, one, (zero,) * n_state)
    for n in range(n_state):
        end_ref[0, n] = states[n]


def scan_ends(step, drive, rows, rate, seqs, reverse):
    n_state, tiles, _ = rate.shape
    groups = step.shape[0] // seqs // SUB
    rows_spec = pl.BlockSpec((groups * SUB, tiles * LANE), lambda s: (s, 0))
    held = pltpu.VMEM((tiles * SUB, LANE), jnp.float32)
    return pl.pallas_call(
        functools.partial(ends_kernel, n_state, tiles, groups, reverse),
        grid=(seqs,),
        in_specs=[
            rows_spec,
            rows_spec,
            pl.BlockSpec(memory_space=pltpu.SMEM),
            pl.BlockSpec((n_state, tiles, LANE), lambda s: (0, 0, 0)),
        ],
        out_specs=pl.BlockSpec((1, n_state, tiles, LANE), lambda s: (s, 0, 0, 0)),
        out_shape=jax.ShapeDtypeStruct((seqs, n_state, tiles, LANE), jnp.float32),
        scratch_shapes=[held, held],
        compiler_params=pltpu.CompilerParams(vmem_limit_bytes=VMEM_GRANT),
    )(step, drive, rows, rate)


def forward_kernel(
    n_state,
    tiles,
    groups,
    blocks,
    start_ref,
    step_ref,
    input_ref,
    brow_ref,
    crow_ref,
    rate_ref,
    prior_ref,
    mixed_ref,
    carried,
    step_held,
    input_held,
    mixed_held,
):
    base = (pl.program_id(0) * blocks + pl.program_id(1)) * groups * SUB * n_state

    @pl.when(pl.program_id(1) == 0)
    def _():
        carried[...] = start_ref[0]

    def one(group, states):
        states = list(states)
        stage_in(step_ref, group, step_held)
        stage_in(input_ref, group, input_held)
        for at in range(SUB):
            step = token_row(step_held, at, tiles)
            drive = step * token_row(input_held, at, tiles)
            mixed = [None] * 2
            for n in range(n_state):
                where = base + (group * SUB + at) * n_state + n
                prior_ref[group * SUB + at, n] = states[n]
                decay = jnp.exp2(step * rate_ref[n])
                states[n] = decay * states[n] + drive * brow_ref[where]
                term = states[n] * crow_ref[where]
                mixed[n % 2] = term if mixed[n % 2] is None else mixed[n % 2] + term
            mixed_held[pl.ds(at, tiles, stride=SUB), :] = mixed[0] + mixed[1]
        stage_out(mixed_held, mixed_ref, group)
        return tuple(states)

    states = lax.fori_loop(0, groups, one, tuple(carried[n] for n in range(n_state)))
    for n in range(n_state):
        carried[n] = states[n]


def scan_forward(start, step, inputs, b_rows, c_rows, rate, seqs):
    n_state, tiles, _ = rate.shape
    all_groups = step.shape[0] // SUB
    groups = math.gcd(all_groups // seqs, 4)
    blocks = all_groups // seqs // groups
    rows_spec = pl.BlockSpec((groups * SUB, tiles * LANE), lambda s, b: (s * blocks + b, 0))
    held = pltpu.VMEM((tiles * SUB, LANE), jnp.float32)
    smem = pl.BlockSpec(memory_space=pltpu.SMEM)
    tokens = all_groups * SUB
    return pl.pallas_call(
        functools.partial(forward_kernel, n_state, tiles, groups, blocks),
        grid=(seqs, blocks),
        in_specs=[
            pl.BlockSpec((1, n_state, tiles, LANE), lambda s, b: (s, 0, 0, 0)),
            rows_spec,
            rows_spec,
            smem,
            smem,
            pl.BlockSpec((n_state, tiles, LANE), lambda s, b: (0, 0, 0)),
        ],
        out_specs=[
            pl.BlockSpec(
                (groups * SUB, n_state, tiles, LANE), lambda s, b: (s * blocks + b, 0, 0, 0)
            ),
            rows_spec,
        ],
        out_shape=[
            jax.ShapeDtypeStruct((tokens, n_state, tiles, LANE), jnp.float32),
            jax.ShapeDtypeStruct(step.shape, jnp.float32),
        ],
        scratch_shapes=[pltpu.VMEM((n_state, tiles, LANE), jnp.float32)] + [held] * 3,
        compiler_params=pltpu.CompilerParams(vmem_limit_bytes=VMEM_GRANT),
    )(start, step, inputs, b_rows, c_rows, rate)


def backward_kernel(
    n_state,
    tiles,
    groups,
    blocks,
    end_ref,
    prior_ref,
    step_ref,
    input_ref,
    ograd_ref,
    brow_ref,
    crow_ref,
    rate_ref,
    picks_ref,
    step_grad_ref,
    input_grad_ref,
    rate_grad_ref,
    part_ref,
    carried,
    step_held,
    input_held,
    ograd_held,
    step_grad_held,
    input_grad_held,
):
    block = blocks - 1 - pl.program_id(1)
    base = (pl.program_id(0) * blocks + block) * groups * SUB * n_state

    @pl.when(pl.program_id(1) == 0)
    def _():
        carried[...] = end_ref[0]

    @pl.when((pl.program_id(0) == 0) & (pl.program_id(1) == 0))
    def _():
        rate_grad_ref[...] = jnp.zeros_like(rate_grad_ref)

    def one(turn, grads):
        group = groups - 1 - turn
        grads = list(grads)
        stage_in(step_ref, group, step_held)
        stage_in(input_ref, group, input_held)
        stage_in(ograd_ref, group, ograd_held)
        for at in range(SUB - 1, -1, -1):
            step = token_row(step_held, at, tiles)
            value = token_row(input_held, at, tiles)
            ograd = token_row(ograd_held, at, tiles)
            drive = step * value
            along_b = None
            along_rate = None
            brow_parts, crow_parts = [], []
            for n in range(n_state):
                where = base + (group * SUB + at) * n_state + n
                brow, crow = brow_ref[where], crow_ref[where]
                rate = rate_ref[n]
                decay = jnp.exp2(step * rate)
                grad = ograd * crow + grads[n]
                kept = decay * prior_ref[group * SUB + at, n]
                state = kept + drive * brow
                decay_term = grad * kept
                grads[n] = decay * grad
                rate_grad_ref[n] += decay_term * step
                by_rate, by_brow = decay_term * rate, grad * brow
                along_rate = by_rate if along_rate is None else along_rate + by_rate
                along_b = by_brow if along_b is None else along_b + by_brow
                brow_parts.append(grad * drive)
                crow_parts.append(ograd * state)
            step_grad_held[pl.ds(at, tiles, stride=SUB), :] = along_rate * LN2 + along_b * value
            input_grad_held[pl.ds(at, tiles, stride=SUB), :] = along_b * step
            parts = jnp.concatenate(brow_parts + crow_parts, 0).astype(jnp.bfloat16)
            part_ref[group * SUB + at] = jnp.dot(
                picks_ref[...], parts, preferred_element_type=jnp.float32
            )
        stage_out(step_grad_held, step_grad_ref, group)
        stage_out(input_grad_held, input_grad_ref, group)
        return tuple(grads)

    grads = lax.fori_loop(0, groups, one, tuple(carried[n] for n in range(n_state)))
    for n in range(n_state):
        carried[n] = grads[n]


def scan_backward(end_grad, prior, step, inputs, ograd, b_rows, c_rows, rate, seqs):
    n_state, tiles, _ = rate.shape
    all_groups = step.shape[0] // SUB
    groups = math.gcd(all_groups // seqs, 4)
    blocks = all_groups // seqs // groups

    def at(s, b):
        return s * blocks + blocks - 1 - b

    rows_spec = pl.BlockSpec((groups * SUB, tiles * LANE), lambda s, b: (at(s, b), 0))
    held = pltpu.VMEM((tiles * SUB, LANE), jnp.float32)
    smem = pl.BlockSpec(memory_space=pltpu.SMEM)
    tokens = all_groups * SUB
    picks = jnp.repeat(jnp.eye(2 * n_state, dtype=jnp.bfloat16), tiles, 1)
    return pl.pallas_call(
        functools.partial(backward_kernel, n_state, tiles, groups, blocks),
        grid=(seqs, blocks),
        in_specs=[
            pl.BlockSpec((1, n_state, tiles, LANE), lambda s, b: (s, 0, 0, 0)),
            pl.BlockSpec((groups * SUB, n_state, tiles, LANE), lambda s, b: (at(s, b), 0, 0, 0)),
            rows_spec,
            rows_spec,
            rows_spec,
            smem,
            smem,
            pl.BlockSpec((n_state, tiles, LANE), lambda s, b: (0, 0, 0)),
            pl.BlockSpec(picks.shape, lambda s, b: (0, 0)),
        ],
        out_specs=[
            rows_spec,
            rows_spec,
            pl.BlockSpec((n_state, tiles, LANE), lambda s, b: (0, 0, 0)),
            pl.BlockSpec((groups * SUB, 2 * n_state, LANE), lambda s, b: (at(s, b), 0, 0)),
        ],
        out_shape=[
            jax.ShapeDtypeStruct(step.shape, jnp.float32),
            jax.ShapeDtypeStruct(step.shape, jnp.float32),
            jax.ShapeDtypeStruct(rate.shape, jnp.float32),
            jax.ShapeDtypeStruct((tokens, 2 * n_state, LANE), jnp.float32),
        ],
        scratch_shapes=[pltpu.VMEM((n_state, tiles, LANE), jnp.float32)] + [held] * 5,
        compiler_params=pltpu.CompilerParams(vmem_limit_bytes=VMEM_GRANT),
    )(end_grad, prior, step, inputs, ograd, b_rows, c_rows, rate, picks)


def from_earlier(ends, decay, steps):
    count = lax.axis_size("ctx")
    if count == 1:
        return jnp.zeros_like(ends)
    if count == 2:
        return passed_along(ends, "ctx", steps)
    index = lax.axis_index("ctx")
    all_ends = lax.all_gather(ends, "ctx")
    all_decays = lax.all_gather(decay, "ctx")

    def one(turn, state):
        at = turn if steps > 0 else count - 1 - turn
        reached = at < index if steps > 0 else at > index
        return jnp.where(reached, all_decays[at] * state + all_ends[at], state)

    return lax.fori_loop(0, count, one, jnp.zeros_like(ends))


def gathered_rows(rows):
    return lax.all_gather(rows, PLANE, axis=0, tiled=True)


def swapped_columns(rows):
    return lax.all_to_all(rows, PLANE, split_axis=1, concat_axis=0, tiled=True)


def place_in(axes):
    index = 0
    for axis in axes:
        index = index * lax.axis_size(axis) + lax.axis_index(axis)
    return index


def device_at(axes, index):
    where = {}
    for axis in reversed(axes):
        size = lax.axis_size(axis)
        where[axis] = lax.rem(index, size)
        index = lax.div(index, size)
    return where


def greet(groups):
    barrier = pltpu.get_barrier_semaphore()
    total = 0
    for axes, others in groups:
        for other in others:
            pl.semaphore_signal(
                barrier,
                inc=1,
                device_id=device_at(axes, other),
                device_id_type=pl.DeviceIdType.MESH,
            )
            total += 1
    pl.semaphore_wait(barrier, total)


def sent(source, target, send_sem, recv_sem, where):
    copy = pltpu.make_async_remote_copy(
        src_ref=source,
        dst_ref=target,
        send_sem=send_sem,
        recv_sem=recv_sem,
        device_id=where,
        device_id_type=pl.DeviceIdType.MESH,
    )
    copy.start()
    return copy


def finish(copies):
    for copy in copies:
        copy.wait()


def rows_of(ref, index, count):
    rows = ref.shape[0] // count
    return ref.at[pl.ds(pl.multiple_of(index * rows, rows), rows), :]


class Group:
    def __init__(self, axes, send_sem, recv_sem):
        self.axes = axes
        self.count = math.prod(lax.axis_size(axis) for axis in axes)
        self.me = place_in(axes)
        self.others = [lax.rem(self.me + hop, self.count) for hop in range(1, self.count)]
        self.send_sem, self.recv_sem = send_sem, recv_sem

    def own(self, ref):
        return rows_of(ref, self.me, self.count)

    def one(self, source, target, which, hop):
        return sent(
            source,
            target,
            self.send_sem.at[which, hop],
            self.recv_sem.at[which, hop],
            device_at(self.axes, self.others[hop]),
        )

    def scatter(self, part, slot, which):
        return [
            self.one(rows_of(part, other, self.count), slot.at[hop], which, hop)
            for hop, other in enumerate(self.others)
        ]

    def total(self, part, slot):
        total = self.own(part)[...].astype(jnp.float32)
        for hop in range(self.count - 1):
            total = total + slot[hop].astype(jnp.float32)
        return total

    def spread(self, ref, which):
        return [self.one(self.own(ref), self.own(ref), which, hop) for hop in range(self.count - 1)]


def slots_for(part, count):
    return pltpu.VMEM((count - 1, part.shape[0] // count) + part.shape[1:], part.dtype)


def group_size(axes):
    return math.prod(lax.axis_size(axis) for axis in axes)


class Swap:
    def __init__(self, arrays, swapped, send_sem, recv_sem, local_sem):
        plane = Group(PLANE, send_sem, recv_sem)
        self.plane, self.arrays, self.swapped, self.local_sem = plane, arrays, swapped, local_sem

    def begin(self):
        self.copies, plane = [], self.plane
        for which, (array, swapped) in enumerate(zip(self.arrays, self.swapped)):
            share = swapped.shape[1]

            def columns(index):
                return array.at[:, pl.ds(pl.multiple_of(index * share, share), share)]

            for hop, other in enumerate(plane.others):
                self.copies.append(plane.one(columns(other), plane.own(swapped), which, hop))
            local = pltpu.make_async_copy(
                columns(plane.me), plane.own(swapped), self.local_sem.at[which]
            )
            local.start()
            self.copies.append(local)

    def end(self):
        finish(self.copies)


def swap_scratch(arrays):
    sems = pltpu.SemaphoreType.DMA((len(arrays), group_size(PLANE) - 1))
    return [sems, sems, pltpu.SemaphoreType.DMA((len(arrays),))] if arrays else []


def swap_shapes(arrays):
    count = group_size(PLANE)
    return [
        jax.ShapeDtypeStruct((array.shape[0] * count, array.shape[1] // count), array.dtype)
        for array in arrays
    ]


def swaps_in_kernels(width):
    return width // group_size(PLANE) % LANE == 0


def sum_kernel(n_rows, n_swaps, n_gathers, part, *refs):
    own_rows, refs = refs[:n_rows], refs[n_rows:]
    arrays, refs = refs[:n_swaps], refs[n_swaps:]
    shards, refs = refs[:n_gathers], refs[n_gathers:]
    total, refs = refs[0], refs[1:]
    all_rows, refs = refs[:n_rows], refs[n_rows:]
    swapped, refs = refs[:n_swaps], refs[n_swaps:]
    gathered, refs = refs[:n_gathers], refs[n_gathers:]
    slots, send_sem, recv_sem, *refs = refs
    group = Group(("tp",), send_sem, recv_sem)
    greeted = [(("tp",), group.others)]
    if n_swaps:
        swap = Swap(arrays, swapped, *refs[:3])
        greeted.append((PLANE, swap.plane.others))
        refs = refs[3:]
    if n_gathers:
        gather = PlaneGather(shards[0], gathered[0], *refs[:2])
        if not n_swaps:
            greeted.append((PLANE, gather.others))
    greet(greeted)
    copies = group.scatter(part, slots, 0)
    if n_swaps:
        swap.begin()
    if n_gathers:
        gather.begin(refs[2])
    spreads = []
    for which, (own, everything) in enumerate(zip(own_rows, all_rows)):
        group.own(everything)[...] = own[...]
        spreads += group.spread(everything, 2 + which)
    finish(copies)
    group.own(total)[...] = group.total(part, slots).astype(total.dtype)
    copies = group.spread(total, 1)
    if n_gathers:
        gather.relay()
        gather.hand_over()
    finish(copies)
    finish(spreads)
    if n_swaps:
        swap.end()
    if n_gathers:
        gather.hand_over_last()
        gather.end()


def gathered_shape(shard):
    return jax.ShapeDtypeStruct(
        (shard.shape[0] * group_size(PLANE),) + shard.shape[1:], shard.dtype
    )


def gather_scratch():
    return [gather_sems(), gather_sems(), pltpu.SemaphoreType.DMA(())]


def sum_over_tp(call_id, part, own_rows, arrays, shards):
    count = group_size(("tp",))
    vmem = pl.BlockSpec(memory_space=pltpu.VMEM)
    hbm = pl.BlockSpec(memory_space=pltpu.HBM)
    operands = [part, *own_rows, *arrays]
    sems = pltpu.SemaphoreType.DMA((2 + len(own_rows), count - 1))
    return pl.pallas_call(
        functools.partial(sum_kernel, len(own_rows), len(arrays), len(shards)),
        in_specs=[vmem] * len(operands) + [hbm] * len(shards),
        out_specs=[vmem] * len(operands) + [hbm] * len(shards),
        out_shape=[jax.ShapeDtypeStruct(part.shape, part.dtype)]
        + [
            jax.ShapeDtypeStruct((own.shape[0] * count,) + own.shape[1:], own.dtype)
            for own in own_rows
        ]
        + swap_shapes(arrays)
        + [gathered_shape(shard) for shard in shards],
        scratch_shapes=[slots_for(part, count), sems, sems]
        + swap_scratch(arrays)
        + gather_scratch() * len(shards),
        compiler_params=pltpu.CompilerParams(
            collective_id=call_id, has_side_effects=True, vmem_limit_bytes=VMEM_GRANT
        ),
    )(*operands, *shards)


def mixer_out_kernel(n_swaps, gated, out_first, out_last, tokens, gain, *refs):
    arrays, refs = refs[:n_swaps], refs[n_swaps:]
    normed, middle, gated_all, *refs = refs
    swapped, refs = refs[:n_swaps], refs[n_swaps:]
    part, slots, send_sem, recv_sem, gather_send, gather_recv, local_sem, *refs = refs
    group = Group(("tp",), send_sem, recv_sem)
    gather = PlaneGather(gated, gated_all, gather_send, gather_recv)
    half = gated.shape[1] // 2
    share = out_first.shape[1]
    greet([(("tp",), group.others), (PLANE, gather.others)])
    gather.begin(local_sem)
    for at in range(out_first.shape[0] // half):
        rows = slice(at * half, (at + 1) * half)
        part[:, at * share : (at + 1) * share] = (
            matmul(gated[:, :half], out_first[rows, :])
            + matmul(gated[:, half:], out_last[rows, :])
        ).astype(part.dtype)
    copies = group.scatter(part, slots, 0)
    if n_swaps:
        swap = Swap(arrays, swapped, *refs)
        swap.begin()
    finish(copies)
    rows = group.own(tokens)[...].astype(jnp.float32) + group.total(part, slots)
    middle[...] = rows
    group.own(normed)[...] = (rows * inverse_rms(rows) * gain[...].astype(jnp.float32)).astype(
        normed.dtype
    )
    copies = group.spread(normed, 1)
    gather.relay()
    gather.hand_over()
    finish(copies)
    gather.hand_over_last()
    gather.end()
    if n_swaps:
        swap.end()


def mixer_out(call_id, gated, out_first, out_last, tokens, gain, arrays):
    count = group_size(("tp",))
    vmem = pl.BlockSpec(memory_space=pltpu.VMEM)
    hbm = pl.BlockSpec(memory_space=pltpu.HBM)
    rows, width = tokens.shape
    part = jax.ShapeDtypeStruct((rows, width), jnp.bfloat16)
    sems = pltpu.SemaphoreType.DMA((2, count - 1))
    return pl.pallas_call(
        functools.partial(mixer_out_kernel, len(arrays)),
        in_specs=[vmem] * (5 + len(arrays)),
        out_specs=[vmem] * 2 + [hbm] + [hbm] * len(arrays),
        out_shape=[
            part,
            jax.ShapeDtypeStruct((rows // count, width), jnp.float32),
            gathered_shape(gated),
        ]
        + swap_shapes(arrays),
        scratch_shapes=[pltpu.VMEM(part.shape, part.dtype), slots_for(part, count), sems, sems]
        + gather_scratch()
        + swap_scratch(arrays),
        compiler_params=pltpu.CompilerParams(
            collective_id=call_id, has_side_effects=True, vmem_limit_bytes=VMEM_GRANT
        ),
    )(gated, out_first, out_last, tokens, gain, *arrays)


def ffn_kernel(swaps, normed, ct, weights, made, *refs):
    hidden = weights.shape[1] // 3
    if swaps:
        *swapped, block_buf, block_sem, send_sem, recv_sem, local_sem = refs
        swap = Swap([normed], swapped, send_sem, recv_sem, local_sem)
        greet([(PLANE, swap.plane.others)])
        swap.begin()
    else:
        block_buf, block_sem = refs

    def columns(j, which):
        return pl.ds(pl.multiple_of(which * hidden + j * WIDE, WIDE), WIDE)

    def fetch(j, which):
        slot = lax.rem(j, 2)
        return pltpu.make_async_copy(
            weights.at[:, columns(j, which)],
            block_buf.at[slot, which],
            block_sem.at[slot, which],
        )

    for which in range(3):
        fetch(0, which).start()

    @pl.loop(0, hidden // WIDE)
    def _(j):
        slot = lax.rem(j, 2)

        @pl.when(j + 1 < hidden // WIDE)
        def _():
            for which in range(3):
                fetch(j + 1, which).start()

        fetch(j, 0).wait()
        gate = matmul(normed[...], block_buf[slot, 0])
        fetch(j, 1).wait()
        up = matmul(normed[...], block_buf[slot, 1])
        fetch(j, 2).wait()
        act_grad = matmul(ct[...], block_buf[slot, 2])
        logistic = jax.nn.sigmoid(gate)
        silu = gate * logistic
        slope = logistic * (1.0 + gate * (1.0 - logistic))
        made[:, columns(j, 0)] = (silu * up).astype(made.dtype)
        made[:, columns(j, 1)] = (act_grad * up * slope).astype(made.dtype)
        made[:, columns(j, 2)] = (act_grad * silu).astype(made.dtype)

    if swaps:
        swap.end()


def run_ffn(call_id, normed, ct, weights, swaps):
    rows, width = normed.shape
    arrays = [normed] if swaps else []
    vmem = pl.BlockSpec(memory_space=pltpu.VMEM)
    params = dict(collective_id=call_id, has_side_effects=True) if swaps else {}
    return pl.pallas_call(
        functools.partial(ffn_kernel, swaps),
        in_specs=[vmem, vmem, pl.BlockSpec(memory_space=pltpu.HBM)],
        out_specs=[vmem] + [pl.BlockSpec(memory_space=pltpu.HBM)] * len(arrays),
        out_shape=[jax.ShapeDtypeStruct((rows, weights.shape[1]), jnp.bfloat16)]
        + swap_shapes(arrays),
        scratch_shapes=[
            pltpu.VMEM((2, 3, width, WIDE), jnp.bfloat16),
            pltpu.SemaphoreType.DMA((2, 3)),
        ]
        + swap_scratch(arrays),
        compiler_params=pltpu.CompilerParams(vmem_limit_bytes=VMEM_GRANT, **params),
    )(normed, ct, weights)


def ffn_back_kernel(
    made,
    ct,
    middle,
    gain,
    out_first,
    out_last,
    weights,
    middle_low,
    middle_grad,
    gain_grad,
    gated_grad,
    ffn_part,
    part,
    slots,
    wide_buf,
    down_buf,
    wide_sem,
    down_sem,
    part_send,
    part_recv,
    send_sem,
    recv_sem,
):
    hidden = made.shape[1] // 3
    blocks = part.shape[1] // WIDE
    group = Group(("tp",), send_sem, recv_sem)
    greet([(("tp",), group.others)])

    def fetch(j):
        return pltpu.make_async_copy(
            weights.at[j * WIDE : (j + 1) * WIDE, : 2 * hidden],
            wide_buf.at[j % 2],
            wide_sem.at[j % 2],
        )

    def fetch_down(j):
        return pltpu.make_async_copy(
            weights.at[j * WIDE : (j + 1) * WIDE, 2 * hidden :],
            down_buf.at[j % 2],
            down_sem.at[j % 2],
        )

    fetch(0).start()
    copies = []
    for j in range(blocks):
        if j + 1 < blocks:
            fetch(j + 1).start()
        else:
            fetch_down(0).start()
        fetch(j).wait()
        columns = slice(j * WIDE, (j + 1) * WIDE)
        part[:, columns] = matmul_nt(made[:, hidden:], wide_buf[j % 2]).astype(part.dtype)
        for hop, other in enumerate(group.others):
            copies.append(
                sent(
                    rows_of(part, other, group.count).at[:, columns],
                    slots.at[hop, :, columns],
                    part_send.at[j, hop],
                    part_recv.at[j, hop],
                    device_at(("tp",), other),
                )
            )
    for j in range(blocks):
        if j + 1 < blocks:
            fetch_down(j + 1).start()
        fetch_down(j).wait()
        ffn_part[:, j * WIDE : (j + 1) * WIDE] = matmul_nt(
            made[:, :hidden], down_buf[j % 2]
        ).astype(ffn_part.dtype)
    finish(copies)
    normed_grad = group.total(part, slots)
    rows = middle[...]
    scale = inverse_rms(rows)
    gain_grad[...] = jnp.sum(normed_grad * rows * scale, 0, keepdims=True)
    grad = group.own(ct)[...].astype(jnp.float32) + norm_back(
        normed_grad, rows, scale, gain[...].astype(jnp.float32)
    )
    middle_grad[...] = grad
    group.own(middle_low)[...] = grad.astype(middle_low.dtype)
    finish(group.spread(middle_low, 0))
    half = gated_grad.shape[1] // 2
    share = out_first.shape[1]
    for side, shards in enumerate((out_first, out_last)):
        total = None
        for at in range(shards.shape[0] // half):
            one = matmul_nt(
                middle_low[:, at * share : (at + 1) * share],
                shards[at * half : (at + 1) * half, :],
            )
            total = one if total is None else total + one
        gated_grad[:, side * half : (side + 1) * half] = total


def ffn_back(call_id, made, ct, middle, gain, out_first, out_last, weights):
    count = group_size(("tp",))
    vmem = pl.BlockSpec(memory_space=pltpu.VMEM)
    rows, width = ct.shape
    hidden = made.shape[1] // 3
    inner = 2 * out_first.shape[0] // group_size(PLANE)
    low, full = jnp.bfloat16, jnp.float32
    part = jax.ShapeDtypeStruct((rows, width), low)
    dma = pltpu.SemaphoreType.DMA
    return pl.pallas_call(
        ffn_back_kernel,
        in_specs=[vmem] * 6 + [pl.BlockSpec(memory_space=pltpu.HBM)],
        out_specs=[vmem] * 5,
        out_shape=[
            part,
            jax.ShapeDtypeStruct((rows // count, width), full),
            jax.ShapeDtypeStruct((1, width), full),
            jax.ShapeDtypeStruct((rows, inner), full),
            part,
        ],
        scratch_shapes=[
            pltpu.VMEM(part.shape, low),
            slots_for(part, count),
            pltpu.VMEM((2, WIDE, 2 * hidden), low),
            pltpu.VMEM((2, WIDE, hidden), low),
            dma((2,)),
            dma((2,)),
            dma((width // WIDE, count - 1)),
            dma((width // WIDE, count - 1)),
            dma((1, count - 1)),
            dma((1, count - 1)),
        ],
        compiler_params=pltpu.CompilerParams(
            collective_id=call_id, has_side_effects=True, vmem_limit_bytes=VMEM_GRANT
        ),
    )(made, ct, middle, gain, out_first, out_last, weights)


def send_on(source, target, send_sem, recv_sem, ctx):
    return pltpu.make_async_remote_copy(
        src_ref=source,
        dst_ref=target,
        send_sem=send_sem,
        recv_sem=recv_sem,
        device_id={"ctx": ctx},
        device_id_type=pl.DeviceIdType.MESH,
    )


def forward_pair_kernel(
    n_state,
    tiles,
    groups,
    blocks,
    seqs,
    step_ref,
    input_ref,
    brow_ref,
    crow_ref,
    rate_ref,
    shard,
    prior_ref,
    mixed_ref,
    gathered,
    carried,
    ends,
    starts,
    prior_buf,
    step_held,
    input_held,
    mixed_held,
    prior_sem,
    send_sem,
    recv_sem,
    gather_send,
    gather_recv,
    local_sem,
):
    place = lax.axis_index("ctx")
    gather = PlaneGather(shard, gathered, gather_send, gather_recv)
    greet([(PLANE, gather.others)])
    gather.begin(local_sem)

    def hand_on(seq):
        return send_on(ends.at[seq], starts.at[seq], send_sem.at[seq], recv_sem.at[seq], 1)

    def store(block):
        slot = lax.rem(block, 2)
        rows = groups * SUB
        return pltpu.make_async_copy(
            prior_buf.at[slot],
            prior_ref.at[pl.ds(pl.multiple_of(block * rows, rows), rows)],
            prior_sem.at[slot],
        )

    def one_sequence(seq):
        @pl.when(place == 0)
        def _():
            carried[...] = jnp.zeros_like(carried)

        @pl.when(place == 1)
        def _():
            hand_on(seq).wait_recv()
            carried[...] = starts[seq]

        @pl.loop(0, blocks)
        def _(inner_block):
            block = seq * blocks + inner_block
            slot = lax.rem(block, 2)

            @pl.when(block >= 2)
            def _():
                store(block - 2).wait()

            def one(turn, states):
                group = block * groups + turn
                states = list(states)
                stage_in(step_ref, group, step_held)
                stage_in(input_ref, group, input_held)
                for at in range(SUB):
                    step = token_row(step_held, at, tiles)
                    drive = step * token_row(input_held, at, tiles)
                    mixed = [None] * 2
                    for n in range(n_state):
                        where = (group * SUB + at) * n_state + n
                        prior_buf[slot, turn * SUB + at, n] = states[n]
                        decay = jnp.exp2(step * rate_ref[n])
                        states[n] = decay * states[n] + drive * brow_ref[where]
                        term = states[n] * crow_ref[where]
                        mixed[n % 2] = term if mixed[n % 2] is None else mixed[n % 2] + term
                    mixed_held[pl.ds(at, tiles, stride=SUB), :] = mixed[0] + mixed[1]
                stage_out(mixed_held, mixed_ref, group)
                return tuple(states)

            states = lax.fori_loop(0, groups, one, tuple(carried[n] for n in range(n_state)))
            for n in range(n_state):
                carried[n] = states[n]
            store(block).start()

        @pl.when(place == 0)
        def _():
            ends[seq] = carried[...]
            hand_on(seq).start()

    for seq in range(seqs):
        one_sequence(seq)
        if seq == 0:
            gather.relay()
            gather.hand_over()
    gather.hand_over_last()
    for block in range(max(0, seqs * blocks - 2), seqs * blocks):
        store(block).wait()

    @pl.when(place == 0)
    def _():
        for seq in range(seqs):
            hand_on(seq).wait_send()

    gather.end()


def scan_forward_pair(call_id, step, inputs, b_rows, c_rows, rate, seqs, shard):
    n_state, tiles, _ = rate.shape
    tokens, inner = step.shape
    all_groups = tokens // SUB
    groups = math.gcd(all_groups // seqs, 4)
    blocks = all_groups // seqs // groups
    vmem = pl.BlockSpec(memory_space=pltpu.VMEM)
    smem = pl.BlockSpec(memory_space=pltpu.SMEM)
    hbm = pl.BlockSpec(memory_space=pltpu.HBM)
    full = jnp.float32
    held = pltpu.VMEM((tiles * SUB, LANE), full)
    boundary = pltpu.VMEM((seqs, n_state, tiles, LANE), full)
    dma = pltpu.SemaphoreType.DMA
    return pl.pallas_call(
        functools.partial(forward_pair_kernel, n_state, tiles, groups, blocks, seqs),
        in_specs=[vmem, vmem, smem, smem, vmem, hbm],
        out_specs=[hbm, vmem, hbm],
        out_shape=[
            jax.ShapeDtypeStruct((tokens, n_state, tiles, LANE), full),
            jax.ShapeDtypeStruct(step.shape, full),
            gathered_shape(shard),
        ],
        scratch_shapes=[
            pltpu.VMEM((n_state, tiles, LANE), full),
            boundary,
            boundary,
            pltpu.VMEM((2, groups * SUB, n_state, tiles, LANE), full),
            held,
            held,
            held,
            dma((2,)),
            dma((seqs,)),
            dma((seqs,)),
        ]
        + gather_scratch(),
        compiler_params=pltpu.CompilerParams(
            collective_id=call_id, has_side_effects=True, vmem_limit_bytes=VMEM_GRANT
        ),
    )(step, inputs, b_rows, c_rows, rate, shard)


def backward_pair_kernel(
    n_swaps,
    n_state,
    tiles,
    groups,
    blocks,
    seqs,
    step_ref,
    input_ref,
    ograd_ref,
    brow_ref,
    crow_ref,
    rate_ref,
    picks_ref,
    ffn_part,
    middle,
    prior_ref,
    *refs,
):
    arrays, refs = refs[:n_swaps], refs[n_swaps:]
    step_grad_ref, input_grad_ref, rate_grad_ref, part_ref, *refs = refs
    layer_first, layer_last, *refs = refs
    swapped, refs = refs[:n_swaps], refs[n_swaps:]
    carried, ends, starts, prior_buf, step_held, input_held, ograd_held, *refs = refs
    step_grad_held, input_grad_held, ffn_slots, prior_sem, send_sem, recv_sem, *refs = refs
    tp_send, tp_recv, *refs = refs
    place = lax.axis_index("ctx")
    tp = Group(("tp",), tp_send, tp_recv)
    if n_swaps:
        swap = Swap(arrays, swapped, *refs)
        greet([(PLANE, swap.plane.others), (("tp",), tp.others)])
        swap.begin()
    else:
        greet([(("ctx",), [1 - place]), (("tp",), tp.others)])
    ffn_sent = tp.scatter(ffn_part, ffn_slots, 0)

    def hand_on(seq):
        return send_on(ends.at[seq], starts.at[seq], send_sem.at[seq], recv_sem.at[seq], 0)

    def fetch(turn):
        seq = lax.div(turn, blocks)
        block = seq * blocks + blocks - 1 - lax.rem(turn, blocks)
        slot = lax.rem(turn, 2)
        rows = groups * SUB
        return pltpu.make_async_copy(
            prior_ref.at[pl.ds(pl.multiple_of(block * rows, rows), rows)],
            prior_buf.at[slot],
            prior_sem.at[slot],
        )

    fetch(0).start()
    rate_grad_ref[...] = jnp.zeros_like(rate_grad_ref)

    @pl.when(place == 1)
    def _():
        @pl.loop(0, seqs)
        def _(seq):
            def one(turn, grads):
                group = (seq + 1) * blocks * groups - 1 - turn
                grads = list(grads)
                stage_in(step_ref, group, step_held)
                stage_in(ograd_ref, group, ograd_held)
                for at in range(SUB - 1, -1, -1):
                    step = token_row(step_held, at, tiles)
                    ograd = token_row(ograd_held, at, tiles)
                    for n in range(n_state):
                        row = crow_ref[(group * SUB + at) * n_state + n]
                        grads[n] = jnp.exp2(step * rate_ref[n]) * (grads[n] + ograd * row)
                return tuple(grads)

            zero = jnp.zeros((tiles, LANE), jnp.float32)
            grads = lax.fori_loop(0, blocks * groups, one, (zero,) * n_state)
            for n in range(n_state):
                ends[seq, n] = grads[n]
            hand_on(seq).start()

    @pl.loop(0, seqs)
    def _(seq):
        @pl.when(place == 1)
        def _():
            carried[...] = jnp.zeros_like(carried)

        @pl.when(place == 0)
        def _():
            hand_on(seq).wait_recv()
            carried[...] = starts[seq]

        @pl.loop(0, blocks)
        def _(inner_block):
            turn = seq * blocks + inner_block
            slot = lax.rem(turn, 2)
            first_group = (seq * blocks + blocks - 1 - inner_block) * groups

            @pl.when(turn + 1 < seqs * blocks)
            def _():
                fetch(turn + 1).start()

            fetch(turn).wait()

            def one(back, grads):
                inner_group = groups - 1 - back
                group = first_group + inner_group
                grads = list(grads)
                stage_in(step_ref, group, step_held)
                stage_in(input_ref, group, input_held)
                stage_in(ograd_ref, group, ograd_held)
                for at in range(SUB - 1, -1, -1):
                    step = token_row(step_held, at, tiles)
                    value = token_row(input_held, at, tiles)
                    ograd = token_row(ograd_held, at, tiles)
                    drive = step * value
                    along_b = None
                    along_rate = None
                    brow_parts, crow_parts = [], []
                    for n in range(n_state):
                        where = (group * SUB + at) * n_state + n
                        brow, crow = brow_ref[where], crow_ref[where]
                        rate = rate_ref[n]
                        decay = jnp.exp2(step * rate)
                        grad = ograd * crow + grads[n]
                        kept = decay * prior_buf[slot, inner_group * SUB + at, n]
                        state = kept + drive * brow
                        decay_term = grad * kept
                        grads[n] = decay * grad
                        rate_grad_ref[n] += decay_term * step
                        by_rate, by_brow = decay_term * rate, grad * brow
                        along_rate = by_rate if along_rate is None else along_rate + by_rate
                        along_b = by_brow if along_b is None else along_b + by_brow
                        brow_parts.append(grad * drive)
                        crow_parts.append(ograd * state)
                    step_grad_held[pl.ds(at, tiles, stride=SUB), :] = (
                        along_rate * LN2 + along_b * value
                    )
                    input_grad_held[pl.ds(at, tiles, stride=SUB), :] = along_b * step
                    parts = jnp.concatenate(brow_parts + crow_parts, 0).astype(jnp.bfloat16)
                    part_ref[group * SUB + at] = jnp.dot(
                        picks_ref[...], parts, preferred_element_type=jnp.float32
                    )
                stage_out(step_grad_held, step_grad_ref, group)
                stage_out(input_grad_held, input_grad_ref, group)
                return tuple(grads)

            grads = lax.fori_loop(0, groups, one, tuple(carried[n] for n in range(n_state)))
            for n in range(n_state):
                carried[n] = grads[n]

    finish(ffn_sent)
    layer_rows = (middle[...] + tp.total(ffn_part, ffn_slots)).astype(layer_first.dtype)
    half = layer_first.shape[1]
    layer_first[...], layer_last[...] = layer_rows[:, :half], layer_rows[:, half:]

    @pl.when(place == 1)
    def _():
        @pl.loop(0, seqs)
        def _(seq):
            hand_on(seq).wait_send()

    if n_swaps:
        swap.end()


def scan_backward_pair(
    call_id, prior, step, inputs, ograd, b_rows, c_rows, rate, seqs, ffn_part, middle, arrays
):
    n_state, tiles, _ = rate.shape
    tokens, inner = step.shape
    all_groups = tokens // SUB
    groups = math.gcd(all_groups // seqs, 4)
    blocks = all_groups // seqs // groups
    tp_count = group_size(("tp",))
    vmem = pl.BlockSpec(memory_space=pltpu.VMEM)
    smem = pl.BlockSpec(memory_space=pltpu.SMEM)
    hbm = pl.BlockSpec(memory_space=pltpu.HBM)
    full = jnp.float32
    held = pltpu.VMEM((tiles * SUB, LANE), full)
    boundary = pltpu.VMEM((seqs, n_state, tiles, LANE), full)
    dma = pltpu.SemaphoreType.DMA
    layer_half = jax.ShapeDtypeStruct((middle.shape[0], middle.shape[1] // 2), jnp.bfloat16)
    picks = jnp.repeat(jnp.eye(2 * n_state, dtype=jnp.bfloat16), tiles, 1)
    return pl.pallas_call(
        functools.partial(
            backward_pair_kernel, len(arrays), n_state, tiles, groups, blocks, seqs
        ),
        in_specs=[vmem] * 3 + [smem] * 2 + [vmem] * 4 + [hbm] + [vmem] * len(arrays),
        out_specs=[vmem] * 6 + [hbm] * len(arrays),
        out_shape=[
            jax.ShapeDtypeStruct(step.shape, full),
            jax.ShapeDtypeStruct(step.shape, full),
            jax.ShapeDtypeStruct(rate.shape, full),
            jax.ShapeDtypeStruct((tokens, 2 * n_state, LANE), full),
            layer_half,
            layer_half,
        ]
        + swap_shapes(arrays),
        scratch_shapes=[
            pltpu.VMEM((n_state, tiles, LANE), full),
            boundary,
            boundary,
            pltpu.VMEM((2, groups * SUB, n_state, tiles, LANE), full),
        ]
        + [held] * 5
        + [
            slots_for(ffn_part, tp_count),
            dma((2,)),
            dma((seqs,)),
            dma((seqs,)),
            dma((1, tp_count - 1)),
            dma((1, tp_count - 1)),
        ]
        + swap_scratch(arrays),
        compiler_params=pltpu.CompilerParams(
            collective_id=call_id, has_side_effects=True, vmem_limit_bytes=VMEM_GRANT
        ),
    )(step, inputs, ograd, b_rows, c_rows, rate, picks, ffn_part, middle, prior, *arrays)


class PlaneGather:
    def __init__(self, own, gathered, send_sem, recv_sem):
        self.own, self.gathered = own, gathered
        self.send_sem, self.recv_sem = send_sem, recv_sem
        self.dp, self.ctx = lax.axis_index("dp"), lax.axis_index("ctx")
        self.n_dp, self.n_ctx = lax.axis_size("dp"), lax.axis_size("ctx")
        self.hands_on = relayed()
        self.count = self.n_dp * self.n_ctx
        self.me = self.dp * self.n_ctx + self.ctx
        self.others = [lax.rem(self.me + hop, self.count) for hop in range(1, self.count)]
        self.copies = {}
        if self.hands_on:
            core = lax.rem(self.dp, 2)
            over_core = self.dp + 1 - 2 * core
            over_y = lax.rem(self.dp + 2, 4)
            over_x = 1 - self.ctx
            self.core = {"dp": over_core, "ctx": self.ctx}
            self.at_x = {"dp": self.dp, "ctx": over_x}
            self.at_y = {"dp": over_y, "ctx": self.ctx}
            self.from_x = self.dp * 2 + over_x
            self.from_y = over_y * 2 + self.ctx
            self.across = over_y * 2 + over_x

    def part(self, owner, half):
        rows = self.gathered.shape[0] // self.count
        start, size = owner * rows, rows
        if half is not None:
            size = rows // 2
            start = start + half * size
        return self.gathered.at[pl.ds(pl.multiple_of(start, size), size), :]

    def send(self, which, owner, half, where):
        target = self.part(owner, half)
        source = target
        if owner is self.me:
            rows = self.own.shape[0]
            source = self.own
            if half is not None:
                source = self.own.at[pl.ds(half * (rows // 2), rows // 2), :]
        self.copies[which] = sent(
            source, target, self.send_sem.at[which], self.recv_sem.at[which], where
        )

    def arrived(self, *which):
        for one in which:
            self.copies[one].wait_recv()

    def begin(self, local_sem):
        self.local = pltpu.make_async_copy(self.own, self.part(self.me, None), local_sem)
        self.local.start()
        if not self.hands_on:
            for hop, other in enumerate(self.others):
                self.send(hop, self.me, None, device_at(PLANE, other))
            return
        self.send(0, self.me, 1, self.at_x)
        self.send(1, self.me, 0, self.at_y)
        self.send(2, self.me, None, self.core)
        self.send(3, self.me, 0, self.at_x)
        self.send(4, self.me, 1, self.at_y)

    def relay(self):
        if not self.hands_on:
            return
        self.arrived(0, 1)
        self.send(5, self.from_x, 1, self.at_y)
        self.send(6, self.from_y, 0, self.at_x)
        self.send(7, self.from_x, 1, self.core)
        self.send(8, self.from_y, 0, self.core)

    def hand_over(self):
        if not self.hands_on:
            return
        self.arrived(3, 4)
        self.send(9, self.from_x, 0, self.core)
        self.send(10, self.from_y, 1, self.core)

    def hand_over_last(self):
        if not self.hands_on:
            return
        self.arrived(5, 6)
        self.send(11, self.across, 1, self.core)
        self.send(12, self.across, 0, self.core)

    def end(self):
        if self.hands_on:
            self.arrived(2, 7, 8, 9, 10, 11, 12)
        else:
            self.arrived(*range(self.count - 1))
        for copy in self.copies.values():
            copy.wait_send()
        self.local.wait()


def relayed():
    return lax.axis_size("dp") == 4 and lax.axis_size("ctx") == 2


def gather_sems():
    count = 13 if relayed() else group_size(PLANE) - 1
    return pltpu.SemaphoreType.DMA((count,))


WIDE = 512


def products(source, first, last, dot, target, block_buf, block_sem, out_buf, out_sem):
    def fetch(j, slot):
        columns = pl.ds(pl.multiple_of(j * WIDE, WIDE), WIDE)
        return pltpu.make_async_copy(
            source.at[:, columns], block_buf.at[slot], block_sem.at[slot]
        )

    def store(j, slot):
        return pltpu.make_async_copy(out_buf.at[slot], target(j), out_sem.at[slot])

    fetch(first, first % 2).start()

    @pl.loop(first, last)
    def _(j):
        slot = lax.rem(j, 2)

        @pl.when(j + 1 < last)
        def _():
            fetch(j + 1, 1 - slot).start()

        fetch(j, slot).wait()

        @pl.when(j >= first + 2)
        def _():
            store(j - 2, slot).wait()

        out_buf[slot] = dot(block_buf[slot])
        store(j, slot).start()

    for j in range(max(first, last - 2), last):
        store(j, j % 2).wait()


SMALL_ROWS = 32
GAIN_ROWS = 16


def tail_kernel(
    swaps,
    conv_grad,
    gate_grad,
    convkern,
    convbias,
    stepbias,
    decaylog,
    skipgain,
    ffngain,
    layer_rows,
    middle_low,
    step_low,
    pre_low,
    select_low,
    scan_in,
    tokens,
    middle_grad,
    gain_row,
    in_conv,
    in_gate,
    one_cols,
    two_cols,
    ct_cols,
    middle_cols,
    ffn_all,
    gated_all,
    tokens_grad,
    layer_out,
    vectors_sum,
    step_sum,
    select_sum,
    gains,
    mix_all,
    grad_inproj,
    grad_outproj,
    grad_gateup,
    grad_downproj,
    mix_own,
    normed_part,
    small,
    small_sum,
    normed_slots,
    small_slots,
    gain_slots,
    gain_own,
    vectors_own,
    cols,
    in_buf,
    block_buf,
    wide_buf,
    tall_buf,
    cols_sem,
    in_sem,
    block_sem,
    wide_sem,
    tall_sem,
    part_send,
    part_recv,
    tp_send,
    tp_recv,
    plane_send,
    plane_recv,
    gather_send,
    gather_recv,
    local_sem,
    *swap_sems,
):
    inner = conv_grad.shape[1]
    hidden = ffn_all.shape[1] // 3
    width = tokens.shape[1]
    rank = step_low.shape[1]
    tp = Group(("tp",), tp_send, tp_recv)
    plane = Group(PLANE, plane_send, plane_recv)
    gather = PlaneGather(mix_own, mix_all, gather_send, gather_recv)
    sources = (one_cols, two_cols, ct_cols) if swaps else (one_cols, two_cols, ct_cols, middle_cols)
    loads = [
        pltpu.make_async_copy(source, cols.at[at], cols_sem.at[at])
        for at, source in enumerate(sources)
    ]
    if swaps:
        swap = Swap([middle_low], [cols.at[3]], *swap_sems)

    def fetch(j):
        slot = j % 2
        rows = slice(j * WIDE, (j + 1) * WIDE)
        return [
            pltpu.make_async_copy(source.at[rows, :], in_buf.at[slot, at], in_sem.at[slot, at])
            for at, source in enumerate((in_conv, in_gate))
        ]

    for copy in fetch(0) + loads:
        copy.start()
    mix_own[:, :inner] = conv_grad[...]
    mix_own[:, inner:] = gate_grad[...]
    greet([(("tp",), tp.others), (PLANE, plane.others)])
    gather.begin(local_sem)
    if swaps:
        swap.begin()

    small[...] = jnp.zeros_like(small)
    vectors_own[...] = jnp.zeros_like(vectors_own)
    at = 0
    for vector in (convkern, convbias, stepbias, decaylog, skipgain):
        vectors_own[at : at + vector.shape[0], :] = vector[...]
        at += vector.shape[0]
    at = SMALL_ROWS - GAIN_ROWS + 10
    for row in range(width // inner):
        vectors_own[at + row : at + row + 1, :] = ffngain[:, row * inner : (row + 1) * inner]
    hidden_in = tokens[...].astype(jnp.float32)
    unit_rows = hidden_in * inverse_rms(hidden_in)
    blocks = width // WIDE
    normed_sent = []
    for j in range(blocks):
        if j + 1 < blocks:
            for copy in fetch(j + 1):
                copy.start()
        finish(fetch(j))
        columns = slice(j * WIDE, (j + 1) * WIDE)
        block = matmul_nt(conv_grad[...], in_buf[j % 2, 0]) + matmul_nt(
            gate_grad[...], in_buf[j % 2, 1]
        )
        normed_part[:, columns] = block.astype(normed_part.dtype)
        for hop, other in enumerate(tp.others):
            normed_sent.append(
                sent(
                    rows_of(normed_part, other, tp.count).at[:, columns],
                    normed_slots.at[hop, :, columns],
                    part_send.at[j, hop],
                    part_recv.at[j, hop],
                    device_at(("tp",), other),
                )
            )
        gain_grad = jnp.sum(block * unit_rows[:, columns], 0, keepdims=True)
        row, at = divmod(j * WIDE, inner)
        row += SMALL_ROWS - GAIN_ROWS + 8
        vectors_own[row : row + 1, at : at + WIDE] = gain_grad
    tp.own(layer_out)[...] = layer_rows[...]
    layer_sent = tp.spread(layer_out, 2)
    small[:SMALL_ROWS, :] = vectors_own[...].astype(small.dtype)
    small[SMALL_ROWS : SMALL_ROWS + rank, :] = matmul_tn(step_low[...], pre_low[...]).astype(
        small.dtype
    )
    selected = select_sum.shape[0]
    small[SMALL_ROWS + rank : SMALL_ROWS + rank + selected, :] = matmul_tn(
        select_low[...], scan_in[...]
    )[:selected].astype(small.dtype)
    small_sent = plane.scatter(small, small_slots, 0)

    def flat(at):
        return lambda block: matmul_tn(cols[at], block)

    def tall(at):
        return lambda block: matmul_tn(block, cols[at])

    def side_by_side(ref, first):
        per = ref.shape[2] // WIDE

        def target(j):
            at = j - first
            columns = pl.ds(pl.multiple_of(lax.rem(at, per) * WIDE, WIDE), WIDE)
            return ref.at[lax.div(at, per), :, columns]

        return target

    def one_above_other(ref):
        return lambda j: ref.at[pl.ds(pl.multiple_of(j * WIDE, WIDE), WIDE), :]

    wide = (block_buf, block_sem, wide_buf, wide_sem)
    high = (block_buf, block_sem, tall_buf, tall_sem)
    down_end = hidden // WIDE
    gu_end = 3 * hidden // WIDE
    finish(loads)
    products(ffn_all, 0, down_end, tall(2), one_above_other(grad_downproj), *high)
    gather.relay()
    products(ffn_all, down_end, gu_end, flat(1), side_by_side(grad_gateup, down_end), *wide)
    gather.hand_over()
    finish(normed_sent)
    hidden_in = tp.own(tokens)[...].astype(jnp.float32)
    tp.own(tokens_grad)[...] = (
        middle_grad[...]
        + norm_back(
            tp.total(normed_part, normed_slots),
            hidden_in,
            inverse_rms(hidden_in),
            gain_row[...].astype(jnp.float32),
        )
    ).astype(tokens_grad.dtype)
    tokens_sent = tp.spread(tokens_grad, 0)
    finish(small_sent)
    plane.own(small_sum)[...] = plane.total(small, small_slots).astype(small_sum.dtype)
    small_sent = plane.spread(small_sum, 1)
    gather.hand_over_last()
    if swaps:
        swap.end()
    products(gated_all, 0, inner // WIDE, tall(3), one_above_other(grad_outproj), *high)
    finish(small_sent)
    gain_own[...] = small_sum[SMALL_ROWS - GAIN_ROWS : SMALL_ROWS, :].astype(jnp.float32)
    gain_sent = [tp.one(gain_own, gain_slots.at[hop], 1, hop) for hop in range(tp.count - 1)]
    vectors_sum[...] = small_sum[:SMALL_ROWS, :].astype(jnp.float32)
    step_sum[...] = small_sum[SMALL_ROWS : SMALL_ROWS + rank, :].astype(jnp.float32)
    select_sum[...] = small_sum[SMALL_ROWS + rank : SMALL_ROWS + rank + selected, :].astype(
        jnp.float32
    )
    gather.end()
    products(mix_all, 0, 2 * inner // WIDE, flat(0), side_by_side(grad_inproj, 0), *wide)
    finish(gain_sent)
    total = gain_own[...]
    for hop in range(tp.count - 1):
        total = total + gain_slots[hop]
    gains[...] = total
    finish(tokens_sent)
    finish(layer_sent)


def run_tail(
    call_id,
    selected,
    swaps,
    conv_grad,
    gate_grad,
    vectors,
    layer_rows,
    middle_low,
    step_low,
    pre_low,
    select_low,
    scan_in,
    tokens,
    middle_grad,
    gain_row,
    in_conv,
    in_gate,
    one_cols,
    two_cols,
    ct_cols,
    middle_cols,
    ffn_all,
    gated_all,
):
    rows, inner = conv_grad.shape
    rank = step_low.shape[1]
    hidden = ffn_all.shape[1] // 3
    width = tokens.shape[1]
    share = one_cols.shape[1]
    all_rows = ffn_all.shape[0]
    tp_count, plane_count = group_size(("tp",)), group_size(PLANE)
    low, full = jnp.bfloat16, jnp.float32
    vmem = pl.BlockSpec(memory_space=pltpu.VMEM)
    hbm = pl.BlockSpec(memory_space=pltpu.HBM)
    dma = pltpu.SemaphoreType.DMA
    small_rows = SMALL_ROWS + rank + selected
    small = jax.ShapeDtypeStruct((small_rows + -small_rows % (16 * plane_count), inner), low)
    part = jax.ShapeDtypeStruct((rows, width), low)
    return pl.pallas_call(
        functools.partial(tail_kernel, swaps),
        in_specs=[vmem] * 17 + [hbm] * 8,
        out_specs=[vmem] * 6 + [hbm] * 5,
        out_shape=[
            jax.ShapeDtypeStruct(tokens.shape, low),
            jax.ShapeDtypeStruct((rows, width // 2), low),
            jax.ShapeDtypeStruct((SMALL_ROWS, inner), full),
            jax.ShapeDtypeStruct((rank, inner), full),
            jax.ShapeDtypeStruct((selected, inner), full),
            jax.ShapeDtypeStruct((GAIN_ROWS, inner), full),
            jax.ShapeDtypeStruct((all_rows, 2 * inner), low),
            jax.ShapeDtypeStruct((2, share, inner), full),
            jax.ShapeDtypeStruct((inner, share), full),
            jax.ShapeDtypeStruct((2, share, hidden), full),
            jax.ShapeDtypeStruct((hidden, share), full),
        ],
        scratch_shapes=[
            pltpu.VMEM((rows, 2 * inner), low),
            pltpu.VMEM(part.shape, low),
            pltpu.VMEM(small.shape, low),
            pltpu.VMEM(small.shape, low),
            slots_for(part, tp_count),
            slots_for(small, plane_count),
            pltpu.VMEM((tp_count - 1, GAIN_ROWS, inner), full),
            pltpu.VMEM((GAIN_ROWS, inner), full),
            pltpu.VMEM((SMALL_ROWS, inner), full),
            pltpu.VMEM((4, all_rows, share), low),
            pltpu.VMEM((2, 2, WIDE, inner), low),
            pltpu.VMEM((2, all_rows, WIDE), low),
            pltpu.VMEM((2, share, WIDE), full),
            pltpu.VMEM((2, WIDE, share), full),
            dma((4,)),
            dma((2, 2)),
            dma((2,)),
            dma((2,)),
            dma((2,)),
            dma((width // WIDE, tp_count - 1)),
            dma((width // WIDE, tp_count - 1)),
            dma((3, tp_count - 1)),
            dma((3, tp_count - 1)),
            dma((2, plane_count - 1)),
            dma((2, plane_count - 1)),
        ]
        + gather_scratch()
        + (swap_scratch([tokens]) if swaps else []),
        compiler_params=pltpu.CompilerParams(
            collective_id=call_id, has_side_effects=True, vmem_limit_bytes=VMEM_GRANT
        ),
    )(
        conv_grad,
        gate_grad,
        *vectors,
        layer_rows,
        middle_low,
        step_low,
        pre_low,
        select_low,
        scan_in,
        tokens,
        middle_grad,
        gain_row,
        in_conv,
        in_gate,
        one_cols,
        two_cols,
        ct_cols,
        middle_cols,
        ffn_all,
        gated_all,
    )


class SplitSwap:
    def __init__(self, array, swapped, plane_send, plane_recv, tp_send, tp_recv, local_sem):
        self.plane, self.tp = Group(PLANE, plane_send, plane_recv), Group(("tp",), tp_send, tp_recv)
        self.array, self.swapped, self.local_sem = array, swapped, local_sem
        rows = array.shape[0] // self.tp.count
        self.rows = pl.ds(pl.multiple_of(self.tp.me * rows, rows), rows)

    def columns(self, index):
        share = self.swapped.shape[2]
        return self.array.at[self.rows, pl.ds(pl.multiple_of(index * share, share), share)]

    def begin(self):
        mine = self.swapped.at[self.plane.me, self.rows, :]
        self.local = pltpu.make_async_copy(
            self.columns(self.plane.me), mine, self.local_sem
        )
        self.local.start()
        self.copies = [
            self.plane.one(self.columns(other), mine, 0, hop)
            for hop, other in enumerate(self.plane.others)
        ]

    def pass_on(self):
        finish(self.copies)
        self.local.wait()
        here = self.swapped.at[:, self.rows, :]
        self.copies = [self.tp.one(here, here, 0, hop) for hop in range(self.tp.count - 1)]

    def end(self):
        finish(self.copies)


def head_kernel(
    swaps,
    tokens,
    gain,
    ct,
    in_conv,
    in_gate,
    conv_in,
    gate_mix,
    conv_all,
    gate_all,
    *refs,
):
    if swaps:
        swapped, *refs = refs
    normed, block_buf, block_sem, *sems = refs
    conv = PlaneGather(in_conv, conv_all, *sems[:2])
    gate = PlaneGather(in_gate, gate_all, *sems[3:5])
    if swaps:
        swap = SplitSwap(ct, swapped, *sems[6:])
        greet([(PLANE, conv.others), (("tp",), swap.tp.others)])
    else:
        greet([(PLANE, conv.others)])
    conv.begin(sems[2])
    if swaps:
        swap.begin()
    gate.begin(sems[5])
    hidden_in = tokens[...].astype(jnp.float32)
    normed[...] = (hidden_in * inverse_rms(hidden_in) * gain[...].astype(jnp.float32)).astype(
        normed.dtype
    )

    def product(source, target):
        columns = range(0, source.shape[1], WIDE)

        def fetch(turn):
            at = columns[turn]
            return pltpu.make_async_copy(
                source.at[:, at : at + WIDE], block_buf.at[turn % 2], block_sem.at[turn % 2]
            )

        fetch(0).start()
        for turn, at in enumerate(columns):
            if turn + 1 < len(columns):
                fetch(turn + 1).start()
            fetch(turn).wait()
            target[:, at : at + WIDE] = matmul(normed[...], block_buf[turn % 2]).astype(
                target.dtype
            )

    conv.relay()
    conv.hand_over()
    if swaps:
        swap.pass_on()
    gate.relay()
    conv.hand_over_last()
    gate.hand_over()
    conv.end()
    product(conv_all, conv_in)
    gate.hand_over_last()
    gate.end()
    product(gate_all, gate_mix)
    if swaps:
        swap.end()


def run_head(call_id, tokens, gain, ct, inproj, swaps):
    rows, width = tokens.shape
    inner = inproj.shape[2]
    low = jnp.bfloat16
    vmem = pl.BlockSpec(memory_space=pltpu.VMEM)
    hbm = pl.BlockSpec(memory_space=pltpu.HBM)
    count, tp_count = group_size(PLANE), group_size(("tp",))
    dma = pltpu.SemaphoreType.DMA
    swap_sems = [
        dma((1, count - 1)),
        dma((1, count - 1)),
        dma((1, tp_count - 1)),
        dma((1, tp_count - 1)),
        dma(()),
    ]
    swapped = [jax.ShapeDtypeStruct((count, rows, width // count), low)]
    return pl.pallas_call(
        functools.partial(head_kernel, swaps),
        in_specs=[vmem] * 3 + [hbm] * 2,
        out_specs=[vmem] * 2 + [hbm] * (3 if swaps else 2),
        out_shape=[
            jax.ShapeDtypeStruct((rows, inner), low),
            jax.ShapeDtypeStruct((rows, inner), jnp.float32),
            jax.ShapeDtypeStruct((width, inner), low),
            jax.ShapeDtypeStruct((width, inner), low),
        ]
        + (swapped if swaps else []),
        scratch_shapes=[
            pltpu.VMEM((rows, width), low),
            pltpu.VMEM((2, width, WIDE), low),
            pltpu.SemaphoreType.DMA((2,)),
        ]
        + gather_scratch() * 2
        + (swap_sems if swaps else []),
        compiler_params=pltpu.CompilerParams(
            collective_id=call_id, has_side_effects=True, vmem_limit_bytes=VMEM_GRANT
        ),
    )(tokens, gain, ct, inproj[0], inproj[1])


def per_device(
    tokens,
    mixgain,
    inproj,
    convkern,
    convbias,
    selproj,
    stepproj,
    stepbias,
    decaylog,
    skipgain,
    outproj,
    ffngain,
    gateup,
    downproj,
    cotangent,
):
    seqs, span, width = tokens.shape
    rows = seqs * span
    taps, inner = convkern.shape
    rank = stepproj.shape[0]
    n_state = decaylog.shape[1]
    tiles = inner // LANE
    gain_mix = mixgain.astype(jnp.float32)
    kernel = convkern.astype(jnp.float32)
    kernel_bias = convbias.astype(jnp.float32)
    step_bias = stepbias.astype(jnp.float32)
    skip_weight = skipgain.astype(jnp.float32)
    decay_rate = -jnp.exp(jnp.transpose(decaylog.astype(jnp.float32)))
    rate = (decay_rate * LOG2E).reshape(n_state, tiles, LANE)

    gain_mix_row, gain_ffn_row = mixgain.reshape(1, width), ffngain.reshape(1, width)
    low = jnp.bfloat16

    tokens_rows = tokens.reshape(rows, width)
    ct_low = cotangent.reshape(rows, width)
    ffn_pack = gathered_rows(
        jnp.concatenate([gateup[0], gateup[1], jnp.transpose(downproj)], 1)
    )
    swap_now = swaps_in_kernels(width)
    conv_in, gate_mix, in_conv, in_gate, *swapped = run_head(
        5, tokens_rows, gain_mix_row, ct_low, inproj, swap_now
    )
    ct_cols = swapped[0].reshape(-1, swapped[0].shape[2]) if swapped else swapped_columns(ct_low)
    hidden_in = tokens_rows.astype(jnp.float32)
    scale_one = inverse_rms(hidden_in)
    normed_one = (hidden_in * scale_one * gain_mix).astype(low)

    conv_seqs = conv_in.reshape(seqs, span, inner)
    rim_rows = passed_along(conv_seqs[:, span - (taps - 1) :], "ctx", 1)
    padded_in = jnp.concatenate([rim_rows, conv_seqs], 1).astype(jnp.float32)
    conv_out = kernel_bias[None, None]
    for offset in range(taps):
        conv_out = conv_out + kernel[offset][None, None] * padded_in[:, offset : offset + span]
    conv_out = conv_out.reshape(rows, inner)
    scan_in = jax.nn.silu(conv_out).astype(low)
    scan_float = scan_in.astype(jnp.float32)
    columns = selproj.shape[1]
    select_width = -(-columns // LANE) * LANE
    select_weights = jnp.pad(selproj, ((0, 0), (0, select_width - columns)))
    select_cols, out_first = sum_over_tp(
        0, matmul(scan_in, select_weights), [], [], [outproj[: inner // 2]]
    )
    step_low = select_cols[:, :rank].astype(low)
    b_rows = select_cols[:, rank : rank + n_state].reshape(-1)
    c_rows = select_cols[:, rank + n_state : columns].reshape(-1)
    step_pre = matmul(step_low, stepproj) + step_bias[None]
    step_size = jax.nn.softplus(step_pre)
    in_pairs = lax.axis_size("ctx") == 2
    if in_pairs:
        prior, scan_out, out_last = scan_forward_pair(
            6, step_size, scan_float, b_rows, c_rows, rate, seqs, outproj[inner // 2 :]
        )
    else:
        span_decay = jnp.exp(
            decay_rate[None] * jnp.sum(step_size.reshape(seqs, span, inner), 1)[:, None]
        ).reshape(seqs, n_state, tiles, LANE)
        ends = scan_ends(step_size, scan_float, b_rows, rate, seqs, False)
        start = from_earlier(ends, span_decay, 1)
        prior, scan_out = scan_forward(start, step_size, scan_float, b_rows, c_rows, rate, seqs)
        out_last = gathered_rows(outproj[inner // 2 :])
    mixer_core = scan_out + skip_weight[None] * scan_float
    gate_sig = jax.nn.silu(gate_mix)
    gated = (mixer_core * gate_sig).astype(low)
    normed_two, middle, gated_all, *swapped = mixer_out(
        1,
        gated,
        out_first,
        out_last,
        tokens_rows,
        gain_ffn_row,
        [normed_one] if swap_now else [],
    )
    (normed_one_cols,) = swapped if swap_now else [swapped_columns(normed_one)]
    made, *swapped = run_ffn(8, normed_two, ct_low, ffn_pack, swap_now)
    (normed_two_cols,) = swapped or [swapped_columns(normed_two)]
    ffn_all = gathered_rows(made)
    middle_low, middle_grad, ffngain_part, gated_grad, ffn_part = ffn_back(
        2, made, ct_low, middle, gain_ffn_row, out_first, out_last, ffn_pack
    )
    core_grad = gated_grad * gate_sig
    gate_mix_grad = (gated_grad * mixer_core * silu_slope(gate_mix)).astype(low)
    grad_skipgain = jnp.sum(core_grad * scan_float, 0)
    if in_pairs:
        step_grad, input_grad, rate_grad, parts, *layer_rows = scan_backward_pair(
            7,
            prior,
            step_size,
            scan_float,
            core_grad,
            b_rows,
            c_rows,
            rate,
            seqs,
            ffn_part,
            middle,
            [],
        )
    else:
        back_ends = scan_ends(step_size, core_grad, c_rows, rate, seqs, True)
        end_grad = from_earlier(back_ends, span_decay, -1)
        step_grad, input_grad, rate_grad, parts = scan_backward(
            end_grad, prior, step_size, scan_float, core_grad, b_rows, c_rows, rate, seqs
        )
        ffn_sum = lax.psum_scatter(ffn_part, "tp", scatter_dimension=0, tiled=True)
        layer_rows = jnp.split((middle + ffn_sum.astype(jnp.float32)).astype(low), 2, 1)
    grad_decaylog = rate_grad.reshape(n_state, inner) * decay_rate
    pre_grad = step_grad * jax.nn.sigmoid(step_pre)
    grad_stepbias = jnp.sum(pre_grad, 0)
    pre_low = pre_grad.astype(low)
    select_part = jnp.concatenate(
        [
            matmul_nt(pre_low, stepproj),
            jnp.sum(parts, -1),
            jnp.zeros((rows, select_width - columns), jnp.float32),
        ],
        1,
    ).astype(low)
    select_low, layer_first = sum_over_tp(3, select_part, layer_rows[:1], [], [])
    scan_in_grad = (
        core_grad * skip_weight[None]
        + input_grad
        + matmul_nt(select_low, select_weights)
    )
    conv_grad = scan_in_grad * silu_slope(conv_out)
    grad_convbias = jnp.sum(conv_grad, 0)
    conv_grad_seqs = conv_grad.reshape(seqs, span, inner)
    padded_grad = jnp.zeros(padded_in.shape, jnp.float32)
    kernel_rows = []
    for offset in range(taps):
        kernel_rows.append(jnp.sum(conv_grad_seqs * padded_in[:, offset : offset + span], (0, 1)))
        padded_grad = padded_grad + jnp.pad(
            kernel[offset][None, None] * conv_grad_seqs,
            ((0, 0), (offset, taps - 1 - offset), (0, 0)),
        )
    grad_convkern = jnp.stack(kernel_rows)
    returned = passed_along(padded_grad[:, : taps - 1], "ctx", -1)
    conv_in_grad = (
        (padded_grad[:, taps - 1 :] + jnp.pad(returned, ((0, 0), (span - taps + 1, 0), (0, 0))))
        .astype(low)
        .reshape(rows, inner)
    )
    vectors = [
        grad_convkern,
        grad_convbias[None],
        grad_stepbias[None],
        grad_decaylog,
        grad_skipgain[None],
        ffngain_part,
    ]
    (
        tokens_grad,
        layer_last,
        vectors,
        grad_stepproj,
        grad_selproj,
        gains,
        _,
        grad_inproj,
        grad_outproj,
        grad_gateup,
        grad_downproj,
    ) = run_tail(
        4,
        columns,
        swap_now,
        conv_in_grad,
        gate_mix_grad,
        vectors,
        layer_rows[1],
        middle_low,
        step_low,
        pre_low,
        select_low,
        scan_in,
        tokens_rows,
        middle_grad,
        gain_mix_row,
        in_conv,
        in_gate,
        normed_one_cols,
        normed_two_cols,
        ct_cols,
        normed_two_cols if swap_now else swapped_columns(middle_low),
        ffn_all,
        gated_all,
    )
    at = taps + 2
    return (
        jnp.concatenate([layer_first, layer_last], 1).reshape(tokens.shape),
        tokens_grad.reshape(tokens.shape),
        gains[8:10].reshape(width),
        grad_inproj,
        vectors[:taps],
        vectors[taps],
        jnp.transpose(grad_selproj),
        grad_stepproj,
        vectors[taps + 1],
        jnp.transpose(vectors[at : at + n_state]),
        vectors[at + n_state],
        grad_outproj,
        gains[10:12].reshape(width),
        grad_gateup,
        grad_downproj,
    )


def solution(mesh):
    in_specs = (
        P("dp", "ctx", None),
        P(),
        P(None, ("dp", "ctx"), "tp"),
        P(None, "tp"),
        P("tp"),
        P("tp", None),
        P(None, "tp"),
        P("tp"),
        P("tp", None),
        P("tp"),
        P("tp", ("dp", "ctx")),
        P(),
        P(None, ("dp", "ctx"), "tp"),
        P("tp", ("dp", "ctx")),
        P("dp", "ctx", None),
    )
    out_specs = (
        P("dp", "ctx", None),
        P("dp", "ctx", None),
        P(),
        P(None, ("dp", "ctx"), "tp"),
        P(None, "tp"),
        P("tp"),
        P("tp", None),
        P(None, "tp"),
        P("tp"),
        P("tp", None),
        P("tp"),
        P("tp", ("dp", "ctx")),
        P(),
        P(None, ("dp", "ctx"), "tp"),
        P("tp", ("dp", "ctx")),
    )
    return jax.shard_map(
        per_device, mesh=mesh, in_specs=in_specs, out_specs=out_specs, check_vma=False
    )
```

```python
import functools
import math

import jax
import jax.numpy as jnp
from jax import lax
from jax.experimental import pallas as pl
from jax.experimental.pallas import tpu as pltpu
from jax.sharding import PartitionSpec as P

EPSILON = 1e-05
LOG2E = math.log2(math.e)
LN2 = math.log(2.0)
SUB = 8
LANE = 128
VMEM_GRANT = 60 * 2**20
PLANE = ("dp", "ctx")


def passed_along(value, axis, steps):
    count = lax.axis_size(axis)
    first, last = (max(0, -steps), min(count, count - steps))
    return lax.ppermute(value, axis, [(source, source + steps) for source in range(first, last)])


def matmul(left, right):
    return jnp.dot(left, right, preferred_element_type=jnp.float32)


def matmul_nt(left, right):
    return lax.dot_general(
        left, right, (((1,), (1,)), ((), ())), preferred_element_type=jnp.float32
    )


def matmul_tn(left, right):
    return lax.dot_general(
        left, right, (((0,), (0,)), ((), ())), preferred_element_type=jnp.float32
    )


def inverse_rms(values):
    return lax.rsqrt(jnp.mean(values * values, -1, keepdims=True) + EPSILON)


def silu_slope(values):
    logistic = jax.nn.sigmoid(values)
    return logistic * (1.0 + values * (1.0 - logistic))


def norm_back(grad_norm, values, scale, gain):
    scaled_grad = grad_norm * gain
    unit_rows = values * scale
    return scale * (scaled_grad - unit_rows * jnp.mean(scaled_grad * unit_rows, -1, keepdims=True))


def stage_in(ref, group, held):
    for tile in range(held.shape[0] // SUB):
        held[pl.ds(tile * SUB, SUB), :] = ref[
            pl.ds(pl.multiple_of(group * SUB, SUB), SUB), pl.ds(tile * LANE, LANE)
        ]


def stage_out(held, ref, group):
    for tile in range(held.shape[0] // SUB):
        ref[pl.ds(pl.multiple_of(group * SUB, SUB), SUB), pl.ds(tile * LANE, LANE)] = held[
            pl.ds(tile * SUB, SUB), :
        ]


def token_row(held, at, tiles):
    return held[pl.ds(at, tiles, stride=SUB), :]


def ends_kernel(
    n_state,
    tiles,
    groups,
    reverse,
    step_ref,
    drive_ref,
    rows_ref,
    rate_ref,
    end_ref,
    step_held,
    drive_held,
):
    base = pl.program_id(0) * groups * SUB * n_state
    rates = [rate_ref[n] for n in range(n_state)]

    def one(turn, states):
        group = groups - 1 - turn if reverse else turn
        order = range(SUB - 1, -1, -1) if reverse else range(SUB)
        states = list(states)
        stage_in(step_ref, group, step_held)
        stage_in(drive_ref, group, drive_held)
        for at in order:
            step = token_row(step_held, at, tiles)
            drive = token_row(drive_held, at, tiles)
            if not reverse:
                drive = drive * step
            for n in range(n_state):
                row = rows_ref[base + (group * SUB + at) * n_state + n]
                decay = jnp.exp2(step * rates[n])
                if reverse:
                    states[n] = decay * (states[n] + drive * row)
                else:
                    states[n] = decay * states[n] + drive * row
        return tuple(states)

    zero = jnp.zeros((tiles, LANE), jnp.float32)
    states = lax.fori_loop(0, groups, one, (zero,) * n_state)
    for n in range(n_state):
        end_ref[0, n] = states[n]


def scan_ends(step, drive, rows, rate, seqs, reverse):
    n_state, tiles, _ = rate.shape
    groups = step.shape[0] // seqs // SUB
    rows_spec = pl.BlockSpec((groups * SUB, tiles * LANE), lambda s: (s, 0))
    held = pltpu.VMEM((tiles * SUB, LANE), jnp.float32)
    return pl.pallas_call(
        functools.partial(ends_kernel, n_state, tiles, groups, reverse),
        grid=(seqs,),
        in_specs=[
            rows_spec,
            rows_spec,
            pl.BlockSpec(memory_space=pltpu.SMEM),
            pl.BlockSpec((n_state, tiles, LANE), lambda s: (0, 0, 0)),
        ],
        out_specs=pl.BlockSpec((1, n_state, tiles, LANE), lambda s: (s, 0, 0, 0)),
        out_shape=jax.ShapeDtypeStruct((seqs, n_state, tiles, LANE), jnp.float32),
        scratch_shapes=[held, held],
        compiler_params=pltpu.CompilerParams(vmem_limit_bytes=VMEM_GRANT),
    )(step, drive, rows, rate)


def forward_kernel(
    n_state,
    tiles,
    groups,
    blocks,
    start_ref,
    step_ref,
    input_ref,
    brow_ref,
    crow_ref,
    rate_ref,
    prior_ref,
    mixed_ref,
    carried,
    step_held,
    input_held,
    mixed_held,
):
    base = (pl.program_id(0) * blocks + pl.program_id(1)) * groups * SUB * n_state

    @pl.when(pl.program_id(1) == 0)
    def _():
        carried[...] = start_ref[0]

    def one(group, states):
        states = list(states)
        stage_in(step_ref, group, step_held)
        stage_in(input_ref, group, input_held)
        for at in range(SUB):
            step = token_row(step_held, at, tiles)
            drive = step * token_row(input_held, at, tiles)
            mixed = [None] * 2
            for n in range(n_state):
                where = base + (group * SUB + at) * n_state + n
                prior_ref[group * SUB + at, n] = states[n]
                decay = jnp.exp2(step * rate_ref[n])
                states[n] = decay * states[n] + drive * brow_ref[where]
                term = states[n] * crow_ref[where]
                mixed[n % 2] = term if mixed[n % 2] is None else mixed[n % 2] + term
            mixed_held[pl.ds(at, tiles, stride=SUB), :] = mixed[0] + mixed[1]
        stage_out(mixed_held, mixed_ref, group)
        return tuple(states)

    states = lax.fori_loop(0, groups, one, tuple(carried[n] for n in range(n_state)))
    for n in range(n_state):
        carried[n] = states[n]


def scan_forward(start, step, inputs, b_rows, c_rows, rate, seqs):
    n_state, tiles, _ = rate.shape
    all_groups = step.shape[0] // SUB
    groups = math.gcd(all_groups // seqs, 4)
    blocks = all_groups // seqs // groups
    rows_spec = pl.BlockSpec((groups * SUB, tiles * LANE), lambda s, b: (s * blocks + b, 0))
    held = pltpu.VMEM((tiles * SUB, LANE), jnp.float32)
    smem = pl.BlockSpec(memory_space=pltpu.SMEM)
    tokens = all_groups * SUB
    return pl.pallas_call(
        functools.partial(forward_kernel, n_state, tiles, groups, blocks),
        grid=(seqs, blocks),
        in_specs=[
            pl.BlockSpec((1, n_state, tiles, LANE), lambda s, b: (s, 0, 0, 0)),
            rows_spec,
            rows_spec,
            smem,
            smem,
            pl.BlockSpec((n_state, tiles, LANE), lambda s, b: (0, 0, 0)),
        ],
        out_specs=[
            pl.BlockSpec(
                (groups * SUB, n_state, tiles, LANE), lambda s, b: (s * blocks + b, 0, 0, 0)
            ),
            rows_spec,
        ],
        out_shape=[
            jax.ShapeDtypeStruct((tokens, n_state, tiles, LANE), jnp.float32),
            jax.ShapeDtypeStruct(step.shape, jnp.float32),
        ],
        scratch_shapes=[pltpu.VMEM((n_state, tiles, LANE), jnp.float32)] + [held] * 3,
        compiler_params=pltpu.CompilerParams(vmem_limit_bytes=VMEM_GRANT),
    )(start, step, inputs, b_rows, c_rows, rate)


def backward_kernel(
    n_state,
    tiles,
    groups,
    blocks,
    end_ref,
    prior_ref,
    step_ref,
    input_ref,
    ograd_ref,
    brow_ref,
    crow_ref,
    rate_ref,
    picks_ref,
    step_grad_ref,
    input_grad_ref,
    rate_grad_ref,
    part_ref,
    carried,
    step_held,
    input_held,
    ograd_held,
    step_grad_held,
    input_grad_held,
):
    block = blocks - 1 - pl.program_id(1)
    base = (pl.program_id(0) * blocks + block) * groups * SUB * n_state

    @pl.when(pl.program_id(1) == 0)
    def _():
        carried[...] = end_ref[0]

    @pl.when((pl.program_id(0) == 0) & (pl.program_id(1) == 0))
    def _():
        rate_grad_ref[...] = jnp.zeros_like(rate_grad_ref)

    def one(turn, grads):
        group = groups - 1 - turn
        grads = list(grads)
        stage_in(step_ref, group, step_held)
        stage_in(input_ref, group, input_held)
        stage_in(ograd_ref, group, ograd_held)
        for at in range(SUB - 1, -1, -1):
            step = token_row(step_held, at, tiles)
            value = token_row(input_held, at, tiles)
            ograd = token_row(ograd_held, at, tiles)
            drive = step * value
            along_b = None
            along_rate = None
            brow_parts, crow_parts = [], []
            for n in range(n_state):
                where = base + (group * SUB + at) * n_state + n
                brow, crow = brow_ref[where], crow_ref[where]
                rate = rate_ref[n]
                decay = jnp.exp2(step * rate)
                grad = ograd * crow + grads[n]
                kept = decay * prior_ref[group * SUB + at, n]
                state = kept + drive * brow
                decay_term = grad * kept
                grads[n] = decay * grad
                rate_grad_ref[n] += decay_term * step
                by_rate, by_brow = decay_term * rate, grad * brow
                along_rate = by_rate if along_rate is None else along_rate + by_rate
                along_b = by_brow if along_b is None else along_b + by_brow
                brow_parts.append(grad * drive)
                crow_parts.append(ograd * state)
            step_grad_held[pl.ds(at, tiles, stride=SUB), :] = along_rate * LN2 + along_b * value
            input_grad_held[pl.ds(at, tiles, stride=SUB), :] = along_b * step
            parts = jnp.concatenate(brow_parts + crow_parts, 0).astype(jnp.bfloat16)
            part_ref[group * SUB + at] = jnp.dot(
                picks_ref[...], parts, preferred_element_type=jnp.float32
            )
        stage_out(step_grad_held, step_grad_ref, group)
        stage_out(input_grad_held, input_grad_ref, group)
        return tuple(grads)

    grads = lax.fori_loop(0, groups, one, tuple(carried[n] for n in range(n_state)))
    for n in range(n_state):
        carried[n] = grads[n]


def scan_backward(end_grad, prior, step, inputs, ograd, b_rows, c_rows, rate, seqs):
    n_state, tiles, _ = rate.shape
    all_groups = step.shape[0] // SUB
    groups = math.gcd(all_groups // seqs, 4)
    blocks = all_groups // seqs // groups

    def at(s, b):
        return s * blocks + blocks - 1 - b

    rows_spec = pl.BlockSpec((groups * SUB, tiles * LANE), lambda s, b: (at(s, b), 0))
    held = pltpu.VMEM((tiles * SUB, LANE), jnp.float32)
    smem = pl.BlockSpec(memory_space=pltpu.SMEM)
    tokens = all_groups * SUB
    picks = jnp.repeat(jnp.eye(2 * n_state, dtype=jnp.bfloat16), tiles, 1)
    return pl.pallas_call(
        functools.partial(backward_kernel, n_state, tiles, groups, blocks),
        grid=(seqs, blocks),
        in_specs=[
            pl.BlockSpec((1, n_state, tiles, LANE), lambda s, b: (s, 0, 0, 0)),
            pl.BlockSpec((groups * SUB, n_state, tiles, LANE), lambda s, b: (at(s, b), 0, 0, 0)),
            rows_spec,
            rows_spec,
            rows_spec,
            smem,
            smem,
            pl.BlockSpec((n_state, tiles, LANE), lambda s, b: (0, 0, 0)),
            pl.BlockSpec(picks.shape, lambda s, b: (0, 0)),
        ],
        out_specs=[
            rows_spec,
            rows_spec,
            pl.BlockSpec((n_state, tiles, LANE), lambda s, b: (0, 0, 0)),
            pl.BlockSpec((groups * SUB, 2 * n_state, LANE), lambda s, b: (at(s, b), 0, 0)),
        ],
        out_shape=[
            jax.ShapeDtypeStruct(step.shape, jnp.float32),
            jax.ShapeDtypeStruct(step.shape, jnp.float32),
            jax.ShapeDtypeStruct(rate.shape, jnp.float32),
            jax.ShapeDtypeStruct((tokens, 2 * n_state, LANE), jnp.float32),
        ],
        scratch_shapes=[pltpu.VMEM((n_state, tiles, LANE), jnp.float32)] + [held] * 5,
        compiler_params=pltpu.CompilerParams(vmem_limit_bytes=VMEM_GRANT),
    )(end_grad, prior, step, inputs, ograd, b_rows, c_rows, rate, picks)


def from_earlier(ends, decay, steps):
    count = lax.axis_size("ctx")
    if count == 1:
        return jnp.zeros_like(ends)
    if count == 2:
        return passed_along(ends, "ctx", steps)
    index = lax.axis_index("ctx")
    all_ends = lax.all_gather(ends, "ctx")
    all_decays = lax.all_gather(decay, "ctx")

    def one(turn, state):
        at = turn if steps > 0 else count - 1 - turn
        reached = at < index if steps > 0 else at > index
        return jnp.where(reached, all_decays[at] * state + all_ends[at], state)

    return lax.fori_loop(0, count, one, jnp.zeros_like(ends))


def gathered_rows(rows):
    return lax.all_gather(rows, PLANE, axis=0, tiled=True)


def swapped_columns(rows):
    return lax.all_to_all(rows, PLANE, split_axis=1, concat_axis=0, tiled=True)


def place_in(axes):
    index = 0
    for axis in axes:
        index = index * lax.axis_size(axis) + lax.axis_index(axis)
    return index


def device_at(axes, index):
    where = {}
    for axis in reversed(axes):
        size = lax.axis_size(axis)
        where[axis] = lax.rem(index, size)
        index = lax.div(index, size)
    return where


def greet(groups):
    barrier = pltpu.get_barrier_semaphore()
    total = 0
    for axes, others in groups:
        for other in others:
            pl.semaphore_signal(
                barrier,
                inc=1,
                device_id=device_at(axes, other),
                device_id_type=pl.DeviceIdType.MESH,
            )
            total += 1
    pl.semaphore_wait(barrier, total)


def sent(source, target, send_sem, recv_sem, where):
    copy = pltpu.make_async_remote_copy(
        src_ref=source,
        dst_ref=target,
        send_sem=send_sem,
        recv_sem=recv_sem,
        device_id=where,
        device_id_type=pl.DeviceIdType.MESH,
    )
    copy.start()
    return copy


def finish(copies):
    for copy in copies:
        copy.wait()


def rows_of(ref, index, count):
    rows = ref.shape[0] // count
    return ref.at[pl.ds(pl.multiple_of(index * rows, rows), rows), :]


class Group:
    def __init__(self, axes, send_sem, recv_sem):
        self.axes = axes
        self.count = math.prod(lax.axis_size(axis) for axis in axes)
        self.me = place_in(axes)
        self.others = [lax.rem(self.me + hop, self.count) for hop in range(1, self.count)]
        self.send_sem, self.recv_sem = send_sem, recv_sem

    def own(self, ref):
        return rows_of(ref, self.me, self.count)

    def one(self, source, target, which, hop):
        return sent(
            source,
            target,
            self.send_sem.at[which, hop],
            self.recv_sem.at[which, hop],
            device_at(self.axes, self.others[hop]),
        )

    def scatter(self, part, slot, which):
        return [
            self.one(rows_of(part, other, self.count), slot.at[hop], which, hop)
            for hop, other in enumerate(self.others)
        ]

    def total(self, part, slot):
        total = self.own(part)[...].astype(jnp.float32)
        for hop in range(self.count - 1):
            total = total + slot[hop].astype(jnp.float32)
        return total

    def spread(self, ref, which):
        return [self.one(self.own(ref), self.own(ref), which, hop) for hop in range(self.count - 1)]


def slots_for(part, count):
    return pltpu.VMEM((count - 1, part.shape[0] // count) + part.shape[1:], part.dtype)


def group_size(axes):
    return math.prod(lax.axis_size(axis) for axis in axes)


def line_of_four():
    me = lax.axis_index("tp")
    near = me + 1 - 2 * lax.rem(me, 2)
    return me, near, lax.rem(me + 2, 4), lax.rem(near + 2, 4)


class LineSum:
    def __init__(self, part, near_slots, far_slot, passed, send_sem, recv_sem):
        self.part, self.near_slots, self.far_slot = part, near_slots, far_slot
        self.passed, self.send_sem, self.recv_sem = passed, send_sem, recv_sem
        self.me, self.near, self.far, self.cross = line_of_four()
        self.blocks = send_sem.shape[1]
        self.copies = []

    def columns(self, j):
        wide = self.part.shape[1] // self.blocks
        return slice(j * wide, (j + 1) * wide)

    def rows(self, index):
        return rows_of(self.part, index, 4)

    def send(self, source, target, which, j, where):
        copy = sent(
            source.at[:, self.columns(j)],
            target.at[:, self.columns(j)],
            self.send_sem.at[which, j],
            self.recv_sem.at[which, j],
            {"tp": where},
        )
        self.copies.append((which, copy))
        return copy

    def begin(self, j):
        first = self.send(self.rows(self.cross), self.near_slots.at[0], 0, j, self.near)
        self.send(self.rows(self.near), self.near_slots.at[1], 1, j, self.near)
        return first

    def pass_on(self, j, first):
        first.wait_recv()
        columns = self.columns(j)
        self.passed[:, columns] = (
            self.rows(self.far)[:, columns].astype(jnp.float32)
            + self.near_slots[0, :, columns].astype(jnp.float32)
        ).astype(self.passed.dtype)
        self.send(self.passed, self.far_slot, 2, j, self.far)

    def total(self):
        for which, copy in self.copies:
            copy.wait_send()
            if which:
                copy.wait_recv()
        return (
            self.rows(self.me)[...].astype(jnp.float32)
            + self.near_slots[1].astype(jnp.float32)
            + self.far_slot[...].astype(jnp.float32)
        )

    def pass_all(self, firsts):
        for j, first in enumerate(firsts):
            self.pass_on(j, first)


def line_sum_scratch(part, blocks):
    share = (part.shape[0] // 4,) + part.shape[1:]
    sems = pltpu.SemaphoreType.DMA((3, blocks))
    return [
        pltpu.VMEM((2,) + share, part.dtype),
        pltpu.VMEM(share, part.dtype),
        pltpu.VMEM(share, part.dtype),
        sems,
        sems,
    ]


class LineSpread:
    def __init__(self, ref, send_sem, recv_sem):
        self.ref, self.send_sem, self.recv_sem = ref, send_sem, recv_sem
        self.me, self.near, self.far, self.cross = line_of_four()

    def send(self, owner, half, which, where):
        rows = rows_of(self.ref, owner, 4)
        if half is not None:
            wide = self.ref.shape[1] // 2
            rows = rows.at[:, half * wide : (half + 1) * wide]
        return sent(rows, rows, self.send_sem.at[which], self.recv_sem.at[which], {"tp": where})

    def begin(self):
        self.across = [self.send(self.me, half, half, self.far) for half in range(2)]
        self.within = [self.send(self.me, None, 2, self.near)]

    def pass_on(self):
        for half, copy in enumerate(self.across):
            copy.wait_recv()
            self.within.append(self.send(self.far, half, 3 + half, self.near))

    def end(self):
        for copy in self.across:
            copy.wait_send()
        finish(self.within)

    def run(self):
        self.begin()
        self.pass_on()
        self.end()


def line_spread_scratch():
    return [pltpu.SemaphoreType.DMA((5,)), pltpu.SemaphoreType.DMA((5,))]


class Swap:
    def __init__(self, arrays, swapped, send_sem, recv_sem, local_sem):
        plane = Group(PLANE, send_sem, recv_sem)
        self.plane, self.arrays, self.swapped, self.local_sem = plane, arrays, swapped, local_sem

    def begin(self):
        self.copies, plane = [], self.plane
        for which, (array, swapped) in enumerate(zip(self.arrays, self.swapped)):
            share = swapped.shape[1]

            def columns(index):
                return array.at[:, pl.ds(pl.multiple_of(index * share, share), share)]

            for hop, other in enumerate(plane.others):
                self.copies.append(plane.one(columns(other), plane.own(swapped), which, hop))
            local = pltpu.make_async_copy(
                columns(plane.me), plane.own(swapped), self.local_sem.at[which]
            )
            local.start()
            self.copies.append(local)

    def end(self):
        finish(self.copies)


def swap_scratch(arrays):
    sems = pltpu.SemaphoreType.DMA((len(arrays), group_size(PLANE) - 1))
    return [sems, sems, pltpu.SemaphoreType.DMA((len(arrays),))] if arrays else []


def swap_shapes(arrays):
    count = group_size(PLANE)
    return [
        jax.ShapeDtypeStruct((array.shape[0] * count, array.shape[1] // count), array.dtype)
        for array in arrays
    ]


def swaps_in_kernels(width):
    return width // group_size(PLANE) % LANE == 0


def gathered_shape(shard):
    return jax.ShapeDtypeStruct(
        (shard.shape[0] * group_size(PLANE),) + shard.shape[1:], shard.dtype
    )


def gather_scratch():
    return [gather_sems(), gather_sems(), pltpu.SemaphoreType.DMA(())]


def product_in_blocks(left, source, target, block_buf, block_sem):
    columns = range(0, source.shape[1], WIDE)

    def fetch(turn):
        at = columns[turn]
        return pltpu.make_async_copy(
            source.at[:, at : at + WIDE], block_buf.at[turn % 2], block_sem.at[turn % 2]
        )

    fetch(0).start()
    for turn, at in enumerate(columns):
        if turn + 1 < len(columns):
            fetch(turn + 1).start()
        fetch(turn).wait()
        target[:, at : at + WIDE] = matmul(left[...], block_buf[turn % 2]).astype(target.dtype)


def select_kernel(
    part,
    normed,
    shard,
    total,
    product,
    gathered,
    slots,
    send_sem,
    recv_sem,
    block_buf,
    block_sem,
    gather_send,
    gather_recv,
    local_sem,
):
    group = Group(("tp",), send_sem, recv_sem)
    gather = PlaneGather(shard, gathered, gather_send, gather_recv)
    greet([(("tp",), group.others), (PLANE, gather.others)])
    gather.begin(local_sem)
    finish(group.scatter(part, slots, 0))
    group.own(total)[...] = group.total(part, slots).astype(total.dtype)
    copies = group.spread(total, 1)
    gather.relay()
    gather.hand_over()
    finish(copies)
    gather.hand_over_last()
    gather.end()
    product_in_blocks(normed, gathered, product, block_buf, block_sem)


def run_select(call_id, part, normed, shard):
    count = group_size(("tp",))
    vmem = pl.BlockSpec(memory_space=pltpu.VMEM)
    hbm = pl.BlockSpec(memory_space=pltpu.HBM)
    sems = pltpu.SemaphoreType.DMA((2, count - 1))
    rows, width = normed.shape
    return pl.pallas_call(
        select_kernel,
        in_specs=[vmem, vmem, hbm],
        out_specs=[vmem, vmem, hbm],
        out_shape=[
            jax.ShapeDtypeStruct(part.shape, part.dtype),
            jax.ShapeDtypeStruct((rows, shard.shape[1]), jnp.float32),
            gathered_shape(shard),
        ],
        scratch_shapes=[
            slots_for(part, count),
            sems,
            sems,
            pltpu.VMEM((2, width, WIDE), jnp.bfloat16),
            pltpu.SemaphoreType.DMA((2,)),
        ]
        + gather_scratch(),
        compiler_params=pltpu.CompilerParams(
            collective_id=call_id, has_side_effects=True, vmem_limit_bytes=VMEM_GRANT
        ),
    )(part, normed, shard)


def sum_kernel(part, own_rows, total, all_rows, slots, send_sem, recv_sem, *line_sems):
    group = Group(("tp",), send_sem, recv_sem)
    rows = LineSpread(all_rows, *line_sems)
    greet([(("tp",), group.others)])
    copies = group.scatter(part, slots, 0)
    group.own(all_rows)[...] = own_rows[...]
    rows.begin()
    finish(copies)
    group.own(total)[...] = group.total(part, slots).astype(total.dtype)
    copies = group.spread(total, 1)
    rows.pass_on()
    finish(copies)
    rows.end()


def sum_over_tp(call_id, part, own_rows):
    count = group_size(("tp",))
    vmem = pl.BlockSpec(memory_space=pltpu.VMEM)
    sems = pltpu.SemaphoreType.DMA((2, count - 1))
    return pl.pallas_call(
        sum_kernel,
        in_specs=[vmem] * 2,
        out_specs=[vmem] * 2,
        out_shape=[
            jax.ShapeDtypeStruct(part.shape, part.dtype),
            jax.ShapeDtypeStruct((own_rows.shape[0] * count, own_rows.shape[1]), own_rows.dtype),
        ],
        scratch_shapes=[slots_for(part, count), sems, sems] + line_spread_scratch(),
        compiler_params=pltpu.CompilerParams(
            collective_id=call_id, has_side_effects=True, vmem_limit_bytes=VMEM_GRANT
        ),
    )(part, own_rows)


def mixer_out_kernel(n_swaps, gated, out_all, tokens, gain, *refs):
    arrays, refs = refs[:n_swaps], refs[n_swaps:]
    normed, middle, gated_all, *refs = refs
    swapped, refs = refs[:n_swaps], refs[n_swaps:]
    part, refs = refs[0], refs[1:]
    line = LineSum(part, *refs[:5])
    spread = LineSpread(normed, *refs[5:7])
    gather_send, gather_recv, local_sem, *refs = refs[7:]
    group = Group(("tp",), None, None)
    gather = PlaneGather(gated, gated_all, gather_send, gather_recv)
    inner = gated.shape[1]
    share = out_all.shape[1]
    greet([(("tp",), group.others), (PLANE, gather.others)])
    gather.begin(local_sem)
    for at in range(out_all.shape[0] // inner):
        part[:, at * share : (at + 1) * share] = matmul(
            gated[...], out_all[at * inner : (at + 1) * inner, :]
        ).astype(part.dtype)
    firsts = [line.begin(j) for j in range(line.blocks)]
    if n_swaps:
        swap = Swap(arrays, swapped, *refs)
        swap.begin()
    line.pass_all(firsts)
    rows = group.own(tokens)[...].astype(jnp.float32) + line.total()
    middle[...] = rows
    group.own(normed)[...] = (rows * inverse_rms(rows) * gain[...].astype(jnp.float32)).astype(
        normed.dtype
    )
    spread.begin()
    gather.relay()
    gather.hand_over()
    spread.pass_on()
    spread.end()
    gather.hand_over_last()
    gather.end()
    if n_swaps:
        swap.end()


def mixer_out(call_id, gated, out_all, tokens, gain, arrays):
    count = group_size(("tp",))
    vmem = pl.BlockSpec(memory_space=pltpu.VMEM)
    hbm = pl.BlockSpec(memory_space=pltpu.HBM)
    rows, width = tokens.shape
    part = jax.ShapeDtypeStruct((rows, width), jnp.bfloat16)
    return pl.pallas_call(
        functools.partial(mixer_out_kernel, len(arrays)),
        in_specs=[vmem] * (4 + len(arrays)),
        out_specs=[vmem] * 2 + [hbm] + [hbm] * len(arrays),
        out_shape=[
            part,
            jax.ShapeDtypeStruct((rows // count, width), jnp.float32),
            gathered_shape(gated),
        ]
        + swap_shapes(arrays),
        scratch_shapes=[pltpu.VMEM(part.shape, part.dtype)]
        + line_sum_scratch(part, 2)
        + line_spread_scratch()
        + gather_scratch()
        + swap_scratch(arrays),
        compiler_params=pltpu.CompilerParams(
            collective_id=call_id, has_side_effects=True, vmem_limit_bytes=VMEM_GRANT
        ),
    )(gated, out_all, tokens, gain, *arrays)


def ffn_kernel(swaps, normed, ct, weights, made, *refs):
    hidden = weights.shape[1] // 3
    if swaps:
        *swapped, block_buf, block_sem, send_sem, recv_sem, local_sem = refs
        swap = Swap([normed], swapped, send_sem, recv_sem, local_sem)
        greet([(PLANE, swap.plane.others)])
        swap.begin()
    else:
        block_buf, block_sem = refs

    def columns(j, which):
        return pl.ds(pl.multiple_of(which * hidden + j * WIDE, WIDE), WIDE)

    def fetch(j, which):
        slot = lax.rem(j, 2)
        return pltpu.make_async_copy(
            weights.at[:, columns(j, which)],
            block_buf.at[slot, which],
            block_sem.at[slot, which],
        )

    for which in range(3):
        fetch(0, which).start()

    @pl.loop(0, hidden // WIDE)
    def _(j):
        slot = lax.rem(j, 2)

        @pl.when(j + 1 < hidden // WIDE)
        def _():
            for which in range(3):
                fetch(j + 1, which).start()

        fetch(j, 0).wait()
        gate = matmul(normed[...], block_buf[slot, 0])
        fetch(j, 1).wait()
        up = matmul(normed[...], block_buf[slot, 1])
        fetch(j, 2).wait()
        act_grad = matmul(ct[...], block_buf[slot, 2])
        logistic = jax.nn.sigmoid(gate)
        silu = gate * logistic
        slope = logistic * (1.0 + gate * (1.0 - logistic))
        made[:, columns(j, 0)] = (silu * up).astype(made.dtype)
        made[:, columns(j, 1)] = (act_grad * up * slope).astype(made.dtype)
        made[:, columns(j, 2)] = (act_grad * silu).astype(made.dtype)

    if swaps:
        swap.end()


def run_ffn(call_id, normed, ct, weights, swaps):
    rows, width = normed.shape
    arrays = [normed] if swaps else []
    vmem = pl.BlockSpec(memory_space=pltpu.VMEM)
    params = dict(collective_id=call_id, has_side_effects=True) if swaps else {}
    return pl.pallas_call(
        functools.partial(ffn_kernel, swaps),
        in_specs=[vmem, vmem, pl.BlockSpec(memory_space=pltpu.HBM)],
        out_specs=[vmem] + [pl.BlockSpec(memory_space=pltpu.HBM)] * len(arrays),
        out_shape=[jax.ShapeDtypeStruct((rows, weights.shape[1]), jnp.bfloat16)]
        + swap_shapes(arrays),
        scratch_shapes=[
            pltpu.VMEM((2, 3, width, WIDE), jnp.bfloat16),
            pltpu.SemaphoreType.DMA((2, 3)),
        ]
        + swap_scratch(arrays),
        compiler_params=pltpu.CompilerParams(vmem_limit_bytes=VMEM_GRANT, **params),
    )(normed, ct, weights)


def ffn_back_kernel(
    made,
    ct,
    middle,
    gain,
    out_all,
    weights,
    middle_low,
    middle_grad,
    gain_grad,
    gated_grad,
    ffn_part,
    part,
    wide_buf,
    down_buf,
    wide_sem,
    down_sem,
    *sems,
):
    hidden = made.shape[1] // 3
    blocks = part.shape[1] // WIDE
    group = Group(("tp",), None, None)
    line = LineSum(part, *sems[:5])
    spread = LineSpread(middle_low, *sems[5:])
    greet([(("tp",), group.others)])

    def fetch(j):
        return pltpu.make_async_copy(
            weights.at[j * WIDE : (j + 1) * WIDE, : 2 * hidden],
            wide_buf.at[j % 2],
            wide_sem.at[j % 2],
        )

    def fetch_down(j):
        return pltpu.make_async_copy(
            weights.at[j * WIDE : (j + 1) * WIDE, 2 * hidden :],
            down_buf.at[j % 2],
            down_sem.at[j % 2],
        )

    fetch(0).start()
    firsts = []
    for j in range(blocks):
        if j + 1 < blocks:
            fetch(j + 1).start()
        else:
            fetch_down(0).start()
        fetch(j).wait()
        columns = slice(j * WIDE, (j + 1) * WIDE)
        part[:, columns] = matmul_nt(made[:, hidden:], wide_buf[j % 2]).astype(part.dtype)
        firsts.append(line.begin(j))
    for j in range(blocks):
        if j + 1 < blocks:
            fetch_down(j + 1).start()
        fetch_down(j).wait()
        ffn_part[:, j * WIDE : (j + 1) * WIDE] = matmul_nt(
            made[:, :hidden], down_buf[j % 2]
        ).astype(ffn_part.dtype)
        line.pass_on(j, firsts[j])
    normed_grad = line.total()
    rows = middle[...]
    scale = inverse_rms(rows)
    gain_grad[...] = jnp.sum(normed_grad * rows * scale, 0, keepdims=True)
    grad = group.own(ct)[...].astype(jnp.float32) + norm_back(
        normed_grad, rows, scale, gain[...].astype(jnp.float32)
    )
    middle_grad[...] = grad
    group.own(middle_low)[...] = grad.astype(middle_low.dtype)
    spread.run()
    inner = gated_grad.shape[1]
    share = out_all.shape[1]
    total = None
    for at in range(out_all.shape[0] // inner):
        one = matmul_nt(
            middle_low[:, at * share : (at + 1) * share], out_all[at * inner : (at + 1) * inner, :]
        )
        total = one if total is None else total + one
    gated_grad[...] = total


def ffn_back(call_id, made, ct, middle, gain, out_all, weights):
    count = group_size(("tp",))
    vmem = pl.BlockSpec(memory_space=pltpu.VMEM)
    rows, width = ct.shape
    hidden = made.shape[1] // 3
    inner = out_all.shape[0] // group_size(PLANE)
    low, full = jnp.bfloat16, jnp.float32
    part = jax.ShapeDtypeStruct((rows, width), low)
    dma = pltpu.SemaphoreType.DMA
    return pl.pallas_call(
        ffn_back_kernel,
        in_specs=[vmem] * 5 + [pl.BlockSpec(memory_space=pltpu.HBM)],
        out_specs=[vmem] * 5,
        out_shape=[
            part,
            jax.ShapeDtypeStruct((rows // count, width), full),
            jax.ShapeDtypeStruct((1, width), full),
            jax.ShapeDtypeStruct((rows, inner), full),
            part,
        ],
        scratch_shapes=[
            pltpu.VMEM(part.shape, low),
            pltpu.VMEM((2, WIDE, 2 * hidden), low),
            pltpu.VMEM((2, WIDE, hidden), low),
            dma((2,)),
            dma((2,)),
        ]
        + line_sum_scratch(part, width // WIDE)
        + line_spread_scratch(),
        compiler_params=pltpu.CompilerParams(
            collective_id=call_id, has_side_effects=True, vmem_limit_bytes=VMEM_GRANT
        ),
    )(made, ct, middle, gain, out_all, weights)


def send_on(source, target, send_sem, recv_sem, ctx):
    return pltpu.make_async_remote_copy(
        src_ref=source,
        dst_ref=target,
        send_sem=send_sem,
        recv_sem=recv_sem,
        device_id={"ctx": ctx},
        device_id_type=pl.DeviceIdType.MESH,
    )


def forward_pair_kernel(
    n_state,
    tiles,
    groups,
    blocks,
    seqs,
    step_ref,
    input_ref,
    brow_ref,
    crow_ref,
    rate_ref,
    shard,
    prior_ref,
    mixed_ref,
    gathered,
    carried,
    ends,
    starts,
    prior_buf,
    step_held,
    input_held,
    mixed_held,
    prior_sem,
    send_sem,
    recv_sem,
    gather_send,
    gather_recv,
    local_sem,
):
    place = lax.axis_index("ctx")
    gather = PlaneGather(shard, gathered, gather_send, gather_recv)
    greet([(PLANE, gather.others)])
    gather.begin(local_sem)

    def hand_on(seq):
        return send_on(ends.at[seq], starts.at[seq], send_sem.at[seq], recv_sem.at[seq], 1)

    def store(block):
        slot = lax.rem(block, 2)
        rows = groups * SUB
        return pltpu.make_async_copy(
            prior_buf.at[slot],
            prior_ref.at[pl.ds(pl.multiple_of(block * rows, rows), rows)],
            prior_sem.at[slot],
        )

    def one_sequence(seq):
        @pl.when(place == 0)
        def _():
            carried[...] = jnp.zeros_like(carried)

        @pl.when(place == 1)
        def _():
            hand_on(seq).wait_recv()
            carried[...] = starts[seq]

        @pl.loop(0, blocks)
        def _(inner_block):
            block = seq * blocks + inner_block
            slot = lax.rem(block, 2)

            @pl.when(block >= 2)
            def _():
                store(block - 2).wait()

            def one(turn, states):
                group = block * groups + turn
                states = list(states)
                stage_in(step_ref, group, step_held)
                stage_in(input_ref, group, input_held)
                for at in range(SUB):
                    step = token_row(step_held, at, tiles)
                    drive = step * token_row(input_held, at, tiles)
                    mixed = [None] * 2
                    for n in range(n_state):
                        where = (group * SUB + at) * n_state + n
                        prior_buf[slot, turn * SUB + at, n] = states[n]
                        decay = jnp.exp2(step * rate_ref[n])
                        states[n] = decay * states[n] + drive * brow_ref[where]
                        term = states[n] * crow_ref[where]
                        mixed[n % 2] = term if mixed[n % 2] is None else mixed[n % 2] + term
                    mixed_held[pl.ds(at, tiles, stride=SUB), :] = mixed[0] + mixed[1]
                stage_out(mixed_held, mixed_ref, group)
                return tuple(states)

            states = lax.fori_loop(0, groups, one, tuple(carried[n] for n in range(n_state)))
            for n in range(n_state):
                carried[n] = states[n]
            store(block).start()

        @pl.when(place == 0)
        def _():
            ends[seq] = carried[...]
            hand_on(seq).start()

    for seq in range(seqs):
        one_sequence(seq)
        if seq == 0:
            gather.relay()
            gather.hand_over()
    gather.hand_over_last()
    for block in range(max(0, seqs * blocks - 2), seqs * blocks):
        store(block).wait()

    @pl.when(place == 0)
    def _():
        for seq in range(seqs):
            hand_on(seq).wait_send()

    gather.end()


def scan_forward_pair(call_id, step, inputs, b_rows, c_rows, rate, seqs, shard):
    n_state, tiles, _ = rate.shape
    tokens, inner = step.shape
    all_groups = tokens // SUB
    groups = math.gcd(all_groups // seqs, 4)
    blocks = all_groups // seqs // groups
    vmem = pl.BlockSpec(memory_space=pltpu.VMEM)
    smem = pl.BlockSpec(memory_space=pltpu.SMEM)
    hbm = pl.BlockSpec(memory_space=pltpu.HBM)
    full = jnp.float32
    held = pltpu.VMEM((tiles * SUB, LANE), full)
    boundary = pltpu.VMEM((seqs, n_state, tiles, LANE), full)
    dma = pltpu.SemaphoreType.DMA
    return pl.pallas_call(
        functools.partial(forward_pair_kernel, n_state, tiles, groups, blocks, seqs),
        in_specs=[vmem, vmem, smem, smem, vmem, hbm],
        out_specs=[hbm, vmem, hbm],
        out_shape=[
            jax.ShapeDtypeStruct((tokens, n_state, tiles, LANE), full),
            jax.ShapeDtypeStruct(step.shape, full),
            gathered_shape(shard),
        ],
        scratch_shapes=[
            pltpu.VMEM((n_state, tiles, LANE), full),
            boundary,
            boundary,
            pltpu.VMEM((2, groups * SUB, n_state, tiles, LANE), full),
            held,
            held,
            held,
            dma((2,)),
            dma((seqs,)),
            dma((seqs,)),
        ]
        + gather_scratch(),
        compiler_params=pltpu.CompilerParams(
            collective_id=call_id, has_side_effects=True, vmem_limit_bytes=VMEM_GRANT
        ),
    )(step, inputs, b_rows, c_rows, rate, shard)


def backward_pair_kernel(
    n_swaps,
    n_state,
    tiles,
    groups,
    blocks,
    seqs,
    step_ref,
    input_ref,
    ograd_ref,
    brow_ref,
    crow_ref,
    rate_ref,
    picks_ref,
    ffn_part,
    middle,
    prior_ref,
    *refs,
):
    arrays, refs = refs[:n_swaps], refs[n_swaps:]
    step_grad_ref, input_grad_ref, rate_grad_ref, part_ref, *refs = refs
    layer_first, layer_last, *refs = refs
    swapped, refs = refs[:n_swaps], refs[n_swaps:]
    carried, ends, starts, prior_buf, step_held, input_held, ograd_held, *refs = refs
    step_grad_held, input_grad_held, ffn_slots, prior_sem, send_sem, recv_sem, *refs = refs
    tp_send, tp_recv, *refs = refs
    place = lax.axis_index("ctx")
    tp = Group(("tp",), tp_send, tp_recv)
    if n_swaps:
        swap = Swap(arrays, swapped, *refs)
        greet([(PLANE, swap.plane.others), (("tp",), tp.others)])
        swap.begin()
    else:
        greet([(("ctx",), [1 - place]), (("tp",), tp.others)])
    ffn_sent = tp.scatter(ffn_part, ffn_slots, 0)

    def hand_on(seq):
        return send_on(ends.at[seq], starts.at[seq], send_sem.at[seq], recv_sem.at[seq], 0)

    def fetch(turn):
        seq = lax.div(turn, blocks)
        block = seq * blocks + blocks - 1 - lax.rem(turn, blocks)
        slot = lax.rem(turn, 2)
        rows = groups * SUB
        return pltpu.make_async_copy(
            prior_ref.at[pl.ds(pl.multiple_of(block * rows, rows), rows)],
            prior_buf.at[slot],
            prior_sem.at[slot],
        )

    fetch(0).start()
    rate_grad_ref[...] = jnp.zeros_like(rate_grad_ref)

    @pl.when(place == 1)
    def _():
        @pl.loop(0, seqs)
        def _(seq):
            def one(turn, grads):
                group = (seq + 1) * blocks * groups - 1 - turn
                grads = list(grads)
                stage_in(step_ref, group, step_held)
                stage_in(ograd_ref, group, ograd_held)
                for at in range(SUB - 1, -1, -1):
                    step = token_row(step_held, at, tiles)
                    ograd = token_row(ograd_held, at, tiles)
                    for n in range(n_state):
                        row = crow_ref[(group * SUB + at) * n_state + n]
                        grads[n] = jnp.exp2(step * rate_ref[n]) * (grads[n] + ograd * row)
                return tuple(grads)

            zero = jnp.zeros((tiles, LANE), jnp.float32)
            grads = lax.fori_loop(0, blocks * groups, one, (zero,) * n_state)
            for n in range(n_state):
                ends[seq, n] = grads[n]
            hand_on(seq).start()

    @pl.loop(0, seqs)
    def _(seq):
        @pl.when(place == 1)
        def _():
            carried[...] = jnp.zeros_like(carried)

        @pl.when(place == 0)
        def _():
            hand_on(seq).wait_recv()
            carried[...] = starts[seq]

        @pl.loop(0, blocks)
        def _(inner_block):
            turn = seq * blocks + inner_block
            slot = lax.rem(turn, 2)
            first_group = (seq * blocks + blocks - 1 - inner_block) * groups

            @pl.when(turn + 1 < seqs * blocks)
            def _():
                fetch(turn + 1).start()

            fetch(turn).wait()

            def one(back, grads):
                inner_group = groups - 1 - back
                group = first_group + inner_group
                grads = list(grads)
                stage_in(step_ref, group, step_held)
                stage_in(input_ref, group, input_held)
                stage_in(ograd_ref, group, ograd_held)
                for at in range(SUB - 1, -1, -1):
                    step = token_row(step_held, at, tiles)
                    value = token_row(input_held, at, tiles)
                    ograd = token_row(ograd_held, at, tiles)
                    drive = step * value
                    along_b = None
                    along_rate = None
                    brow_parts, crow_parts = [], []
                    for n in range(n_state):
                        where = (group * SUB + at) * n_state + n
                        brow, crow = brow_ref[where], crow_ref[where]
                        rate = rate_ref[n]
                        decay = jnp.exp2(step * rate)
                        grad = ograd * crow + grads[n]
                        kept = decay * prior_buf[slot, inner_group * SUB + at, n]
                        state = kept + drive * brow
                        decay_term = grad * kept
                        grads[n] = decay * grad
                        rate_grad_ref[n] += decay_term * step
                        by_rate, by_brow = decay_term * rate, grad * brow
                        along_rate = by_rate if along_rate is None else along_rate + by_rate
                        along_b = by_brow if along_b is None else along_b + by_brow
                        brow_parts.append(grad * drive)
                        crow_parts.append(ograd * state)
                    step_grad_held[pl.ds(at, tiles, stride=SUB), :] = (
                        along_rate * LN2 + along_b * value
                    )
                    input_grad_held[pl.ds(at, tiles, stride=SUB), :] = along_b * step
                    parts = jnp.concatenate(brow_parts + crow_parts, 0).astype(jnp.bfloat16)
                    part_ref[group * SUB + at] = jnp.dot(
                        picks_ref[...], parts, preferred_element_type=jnp.float32
                    )
                stage_out(step_grad_held, step_grad_ref, group)
                stage_out(input_grad_held, input_grad_ref, group)
                return tuple(grads)

            grads = lax.fori_loop(0, groups, one, tuple(carried[n] for n in range(n_state)))
            for n in range(n_state):
                carried[n] = grads[n]

    finish(ffn_sent)
    layer_rows = (middle[...] + tp.total(ffn_part, ffn_slots)).astype(layer_first.dtype)
    half = layer_first.shape[1]
    layer_first[...], layer_last[...] = layer_rows[:, :half], layer_rows[:, half:]

    @pl.when(place == 1)
    def _():
        @pl.loop(0, seqs)
        def _(seq):
            hand_on(seq).wait_send()

    if n_swaps:
        swap.end()


def scan_backward_pair(
    call_id, prior, step, inputs, ograd, b_rows, c_rows, rate, seqs, ffn_part, middle, arrays
):
    n_state, tiles, _ = rate.shape
    tokens, inner = step.shape
    all_groups = tokens // SUB
    groups = math.gcd(all_groups // seqs, 4)
    blocks = all_groups // seqs // groups
    tp_count = group_size(("tp",))
    vmem = pl.BlockSpec(memory_space=pltpu.VMEM)
    smem = pl.BlockSpec(memory_space=pltpu.SMEM)
    hbm = pl.BlockSpec(memory_space=pltpu.HBM)
    full = jnp.float32
    held = pltpu.VMEM((tiles * SUB, LANE), full)
    boundary = pltpu.VMEM((seqs, n_state, tiles, LANE), full)
    dma = pltpu.SemaphoreType.DMA
    layer_half = jax.ShapeDtypeStruct((middle.shape[0], middle.shape[1] // 2), jnp.bfloat16)
    picks = jnp.repeat(jnp.eye(2 * n_state, dtype=jnp.bfloat16), tiles, 1)
    return pl.pallas_call(
        functools.partial(
            backward_pair_kernel, len(arrays), n_state, tiles, groups, blocks, seqs
        ),
        in_specs=[vmem] * 3 + [smem] * 2 + [vmem] * 4 + [hbm] + [vmem] * len(arrays),
        out_specs=[vmem] * 6 + [hbm] * len(arrays),
        out_shape=[
            jax.ShapeDtypeStruct(step.shape, full),
            jax.ShapeDtypeStruct(step.shape, full),
            jax.ShapeDtypeStruct(rate.shape, full),
            jax.ShapeDtypeStruct((tokens, 2 * n_state, LANE), full),
            layer_half,
            layer_half,
        ]
        + swap_shapes(arrays),
        scratch_shapes=[
            pltpu.VMEM((n_state, tiles, LANE), full),
            boundary,
            boundary,
            pltpu.VMEM((2, groups * SUB, n_state, tiles, LANE), full),
        ]
        + [held] * 5
        + [
            slots_for(ffn_part, tp_count),
            dma((2,)),
            dma((seqs,)),
            dma((seqs,)),
            dma((1, tp_count - 1)),
            dma((1, tp_count - 1)),
        ]
        + swap_scratch(arrays),
        compiler_params=pltpu.CompilerParams(
            collective_id=call_id, has_side_effects=True, vmem_limit_bytes=VMEM_GRANT
        ),
    )(step, inputs, ograd, b_rows, c_rows, rate, picks, ffn_part, middle, prior, *arrays)


class PlaneGather:
    def __init__(self, own, gathered, send_sem, recv_sem):
        self.own, self.gathered = own, gathered
        self.send_sem, self.recv_sem = send_sem, recv_sem
        self.dp, self.ctx = lax.axis_index("dp"), lax.axis_index("ctx")
        self.n_dp, self.n_ctx = lax.axis_size("dp"), lax.axis_size("ctx")
        self.hands_on = relayed()
        self.count = self.n_dp * self.n_ctx
        self.me = self.dp * self.n_ctx + self.ctx
        self.others = [lax.rem(self.me + hop, self.count) for hop in range(1, self.count)]
        self.copies = {}
        if self.hands_on:
            core = lax.rem(self.dp, 2)
            over_core = self.dp + 1 - 2 * core
            over_y = lax.rem(self.dp + 2, 4)
            over_x = 1 - self.ctx
            self.core = {"dp": over_core, "ctx": self.ctx}
            self.at_x = {"dp": self.dp, "ctx": over_x}
            self.at_y = {"dp": over_y, "ctx": self.ctx}
            self.from_x = self.dp * 2 + over_x
            self.from_y = over_y * 2 + self.ctx
            self.across = over_y * 2 + over_x

    def part(self, owner, half):
        rows = self.gathered.shape[0] // self.count
        start, size = owner * rows, rows
        if half is not None:
            size = rows // 2
            start = start + half * size
        return self.gathered.at[pl.ds(pl.multiple_of(start, size), size), :]

    def send(self, which, owner, half, where):
        target = self.part(owner, half)
        source = target
        if owner is self.me:
            rows = self.own.shape[0]
            source = self.own
            if half is not None:
                source = self.own.at[pl.ds(half * (rows // 2), rows // 2), :]
        self.copies[which] = sent(
            source, target, self.send_sem.at[which], self.recv_sem.at[which], where
        )

    def arrived(self, *which):
        for one in which:
            self.copies[one].wait_recv()

    def begin(self, local_sem):
        self.local = pltpu.make_async_copy(self.own, self.part(self.me, None), local_sem)
        self.local.start()
        if not self.hands_on:
            for hop, other in enumerate(self.others):
                self.send(hop, self.me, None, device_at(PLANE, other))
            return
        self.send(0, self.me, 1, self.at_x)
        self.send(1, self.me, 0, self.at_y)
        self.send(2, self.me, None, self.core)
        self.send(3, self.me, 0, self.at_x)
        self.send(4, self.me, 1, self.at_y)

    def relay(self):
        if not self.hands_on:
            return
        self.arrived(0, 1)
        self.send(5, self.from_x, 1, self.at_y)
        self.send(6, self.from_y, 0, self.at_x)
        self.send(7, self.from_x, 1, self.core)
        self.send(8, self.from_y, 0, self.core)

    def hand_over(self):
        if not self.hands_on:
            return
        self.arrived(3, 4)
        self.send(9, self.from_x, 0, self.core)
        self.send(10, self.from_y, 1, self.core)

    def hand_over_last(self):
        if not self.hands_on:
            return
        self.arrived(5, 6)
        self.send(11, self.across, 1, self.core)
        self.send(12, self.across, 0, self.core)

    def end(self):
        if self.hands_on:
            self.arrived(2, 7, 8, 9, 10, 11, 12)
        else:
            self.arrived(*range(self.count - 1))
        for copy in self.copies.values():
            copy.wait_send()
        self.local.wait()


def relayed():
    return lax.axis_size("dp") == 4 and lax.axis_size("ctx") == 2


def gather_sems():
    count = 13 if relayed() else group_size(PLANE) - 1
    return pltpu.SemaphoreType.DMA((count,))


WIDE = 512


def products(source, first, last, dot, target, block_buf, block_sem, out_buf, out_sem):
    def fetch(j, slot):
        columns = pl.ds(pl.multiple_of(j * WIDE, WIDE), WIDE)
        return pltpu.make_async_copy(
            source.at[:, columns], block_buf.at[slot], block_sem.at[slot]
        )

    def store(j, slot):
        return pltpu.make_async_copy(out_buf.at[slot], target(j), out_sem.at[slot])

    fetch(first, first % 2).start()

    @pl.loop(first, last)
    def _(j):
        slot = lax.rem(j, 2)

        @pl.when(j + 1 < last)
        def _():
            fetch(j + 1, 1 - slot).start()

        fetch(j, slot).wait()

        @pl.when(j >= first + 2)
        def _():
            store(j - 2, slot).wait()

        out_buf[slot] = dot(block_buf[slot])
        store(j, slot).start()

    for j in range(max(first, last - 2), last):
        store(j, j % 2).wait()


SMALL_ROWS = 32
GAIN_ROWS = 16


def tail_kernel(
    swaps,
    conv_grad,
    gate_grad,
    convkern,
    convbias,
    stepbias,
    decaylog,
    skipgain,
    ffngain,
    layer_rows,
    middle_low,
    step_low,
    pre_low,
    select_low,
    scan_in,
    tokens,
    middle_grad,
    gain_row,
    in_conv,
    in_gate,
    one_cols,
    two_cols,
    ct_cols,
    middle_cols,
    ffn_all,
    gated_all,
    tokens_grad,
    layer_out,
    vectors_sum,
    step_sum,
    select_sum,
    gains,
    mix_all,
    grad_inproj,
    grad_outproj,
    grad_gateup,
    grad_downproj,
    mix_own,
    normed_part,
    small,
    small_sum,
    small_slots,
    gain_slots,
    gain_own,
    vectors_own,
    cols,
    in_buf,
    block_buf,
    wide_buf,
    tall_buf,
    cols_sem,
    in_sem,
    block_sem,
    wide_sem,
    tall_sem,
    tp_send,
    tp_recv,
    plane_send,
    plane_recv,
    gather_send,
    gather_recv,
    local_sem,
    *sems,
):
    inner = conv_grad.shape[1]
    hidden = ffn_all.shape[1] // 3
    width = tokens.shape[1]
    rank = step_low.shape[1]
    tp = Group(("tp",), tp_send, tp_recv)
    plane = Group(PLANE, plane_send, plane_recv)
    line = LineSum(normed_part, *sems[:5])
    tokens_spread = LineSpread(tokens_grad, *sems[5:7])
    layer_spread = LineSpread(layer_out, *sems[7:9])
    swap_sems = sems[9:]
    gather = PlaneGather(mix_own, mix_all, gather_send, gather_recv)
    sources = (one_cols, two_cols, ct_cols) if swaps else (one_cols, two_cols, ct_cols, middle_cols)
    loads = [
        pltpu.make_async_copy(source, cols.at[at], cols_sem.at[at])
        for at, source in enumerate(sources)
    ]
    if swaps:
        swap = Swap([middle_low], [cols.at[3]], *swap_sems)

    def fetch(j):
        slot = j % 2
        rows = slice(j * WIDE, (j + 1) * WIDE)
        return [
            pltpu.make_async_copy(source.at[rows, :], in_buf.at[slot, at], in_sem.at[slot, at])
            for at, source in enumerate((in_conv, in_gate))
        ]

    for copy in fetch(0) + loads:
        copy.start()
    mix_own[:, :inner] = conv_grad[...]
    mix_own[:, inner:] = gate_grad[...]
    greet([(("tp",), tp.others), (PLANE, plane.others)])
    gather.begin(local_sem)
    if swaps:
        swap.begin()

    small[...] = jnp.zeros_like(small)
    vectors_own[...] = jnp.zeros_like(vectors_own)
    at = 0
    for vector in (convkern, convbias, stepbias, decaylog, skipgain):
        vectors_own[at : at + vector.shape[0], :] = vector[...]
        at += vector.shape[0]
    at = SMALL_ROWS - GAIN_ROWS + 10
    for row in range(width // inner):
        vectors_own[at + row : at + row + 1, :] = ffngain[:, row * inner : (row + 1) * inner]
    hidden_in = tokens[...].astype(jnp.float32)
    unit_rows = hidden_in * inverse_rms(hidden_in)
    blocks = width // WIDE
    firsts = []
    for j in range(blocks):
        if j + 1 < blocks:
            for copy in fetch(j + 1):
                copy.start()
        finish(fetch(j))
        columns = slice(j * WIDE, (j + 1) * WIDE)
        block = matmul_nt(conv_grad[...], in_buf[j % 2, 0]) + matmul_nt(
            gate_grad[...], in_buf[j % 2, 1]
        )
        normed_part[:, columns] = block.astype(normed_part.dtype)
        firsts.append(line.begin(j))
        gain_grad = jnp.sum(block * unit_rows[:, columns], 0, keepdims=True)
        row, at = divmod(j * WIDE, inner)
        row += SMALL_ROWS - GAIN_ROWS + 8
        vectors_own[row : row + 1, at : at + WIDE] = gain_grad
    tp.own(layer_out)[...] = layer_rows[...]
    layer_spread.begin()
    small[:SMALL_ROWS, :] = vectors_own[...].astype(small.dtype)
    small[SMALL_ROWS : SMALL_ROWS + rank, :] = matmul_tn(step_low[...], pre_low[...]).astype(
        small.dtype
    )
    selected = select_sum.shape[0]
    small[SMALL_ROWS + rank : SMALL_ROWS + rank + selected, :] = matmul_tn(
        select_low[...], scan_in[...]
    )[:selected].astype(small.dtype)
    small_sent = plane.scatter(small, small_slots, 0)
    line.pass_all(firsts)

    def flat(at):
        return lambda block: matmul_tn(cols[at], block)

    def tall(at):
        return lambda block: matmul_tn(block, cols[at])

    def side_by_side(ref, first):
        per = ref.shape[2] // WIDE

        def target(j):
            at = j - first
            columns = pl.ds(pl.multiple_of(lax.rem(at, per) * WIDE, WIDE), WIDE)
            return ref.at[lax.div(at, per), :, columns]

        return target

    def one_above_other(ref):
        return lambda j: ref.at[pl.ds(pl.multiple_of(j * WIDE, WIDE), WIDE), :]

    wide = (block_buf, block_sem, wide_buf, wide_sem)
    high = (block_buf, block_sem, tall_buf, tall_sem)
    down_end = hidden // WIDE
    gu_end = 3 * hidden // WIDE
    finish(loads)
    products(ffn_all, 0, down_end, tall(2), one_above_other(grad_downproj), *high)
    gather.relay()
    products(ffn_all, down_end, gu_end, flat(1), side_by_side(grad_gateup, down_end), *wide)
    gather.hand_over()
    layer_spread.pass_on()
    hidden_in = tp.own(tokens)[...].astype(jnp.float32)
    tp.own(tokens_grad)[...] = (
        middle_grad[...]
        + norm_back(
            line.total(),
            hidden_in,
            inverse_rms(hidden_in),
            gain_row[...].astype(jnp.float32),
        )
    ).astype(tokens_grad.dtype)
    tokens_spread.begin()
    finish(small_sent)
    plane.own(small_sum)[...] = plane.total(small, small_slots).astype(small_sum.dtype)
    small_sent = plane.spread(small_sum, 1)
    gather.hand_over_last()
    if swaps:
        swap.end()
    tokens_spread.pass_on()
    products(gated_all, 0, inner // WIDE, tall(3), one_above_other(grad_outproj), *high)
    finish(small_sent)
    gain_own[...] = small_sum[SMALL_ROWS - GAIN_ROWS : SMALL_ROWS, :].astype(jnp.float32)
    gain_sent = [tp.one(gain_own, gain_slots.at[hop], 0, hop) for hop in range(tp.count - 1)]
    vectors_sum[...] = small_sum[:SMALL_ROWS, :].astype(jnp.float32)
    step_sum[...] = small_sum[SMALL_ROWS : SMALL_ROWS + rank, :].astype(jnp.float32)
    select_sum[...] = small_sum[SMALL_ROWS + rank : SMALL_ROWS + rank + selected, :].astype(
        jnp.float32
    )
    gather.end()
    products(mix_all, 0, 2 * inner // WIDE, flat(0), side_by_side(grad_inproj, 0), *wide)
    finish(gain_sent)
    total = gain_own[...]
    for hop in range(tp.count - 1):
        total = total + gain_slots[hop]
    gains[...] = total
    tokens_spread.end()
    layer_spread.end()


def run_tail(
    call_id,
    selected,
    swaps,
    conv_grad,
    gate_grad,
    vectors,
    layer_rows,
    middle_low,
    step_low,
    pre_low,
    select_low,
    scan_in,
    tokens,
    middle_grad,
    gain_row,
    in_conv,
    in_gate,
    one_cols,
    two_cols,
    ct_cols,
    middle_cols,
    ffn_all,
    gated_all,
):
    rows, inner = conv_grad.shape
    rank = step_low.shape[1]
    hidden = ffn_all.shape[1] // 3
    width = tokens.shape[1]
    share = one_cols.shape[1]
    all_rows = ffn_all.shape[0]
    tp_count, plane_count = group_size(("tp",)), group_size(PLANE)
    low, full = jnp.bfloat16, jnp.float32
    vmem = pl.BlockSpec(memory_space=pltpu.VMEM)
    hbm = pl.BlockSpec(memory_space=pltpu.HBM)
    dma = pltpu.SemaphoreType.DMA
    small_rows = SMALL_ROWS + rank + selected
    small = jax.ShapeDtypeStruct((small_rows + -small_rows % (16 * plane_count), inner), low)
    part = jax.ShapeDtypeStruct((rows, width), low)
    return pl.pallas_call(
        functools.partial(tail_kernel, swaps),
        in_specs=[vmem] * 17 + [hbm] * 8,
        out_specs=[vmem] * 6 + [hbm] * 5,
        out_shape=[
            jax.ShapeDtypeStruct(tokens.shape, low),
            jax.ShapeDtypeStruct((rows, width // 2), low),
            jax.ShapeDtypeStruct((SMALL_ROWS, inner), full),
            jax.ShapeDtypeStruct((rank, inner), full),
            jax.ShapeDtypeStruct((selected, inner), full),
            jax.ShapeDtypeStruct((GAIN_ROWS, inner), full),
            jax.ShapeDtypeStruct((all_rows, 2 * inner), low),
            jax.ShapeDtypeStruct((2, share, inner), full),
            jax.ShapeDtypeStruct((inner, share), full),
            jax.ShapeDtypeStruct((2, share, hidden), full),
            jax.ShapeDtypeStruct((hidden, share), full),
        ],
        scratch_shapes=[
            pltpu.VMEM((rows, 2 * inner), low),
            pltpu.VMEM(part.shape, low),
            pltpu.VMEM(small.shape, low),
            pltpu.VMEM(small.shape, low),
            slots_for(small, plane_count),
            pltpu.VMEM((tp_count - 1, GAIN_ROWS, inner), full),
            pltpu.VMEM((GAIN_ROWS, inner), full),
            pltpu.VMEM((SMALL_ROWS, inner), full),
            pltpu.VMEM((4, all_rows, share), low),
            pltpu.VMEM((2, 2, WIDE, inner), low),
            pltpu.VMEM((2, all_rows, WIDE), low),
            pltpu.VMEM((2, share, WIDE), full),
            pltpu.VMEM((2, WIDE, share), full),
            dma((4,)),
            dma((2, 2)),
            dma((2,)),
            dma((2,)),
            dma((2,)),
            dma((1, tp_count - 1)),
            dma((1, tp_count - 1)),
            dma((2, plane_count - 1)),
            dma((2, plane_count - 1)),
        ]
        + gather_scratch()
        + line_sum_scratch(part, width // WIDE)
        + line_spread_scratch() * 2
        + (swap_scratch([tokens]) if swaps else []),
        compiler_params=pltpu.CompilerParams(
            collective_id=call_id, has_side_effects=True, vmem_limit_bytes=VMEM_GRANT
        ),
    )(
        conv_grad,
        gate_grad,
        *vectors,
        layer_rows,
        middle_low,
        step_low,
        pre_low,
        select_low,
        scan_in,
        tokens,
        middle_grad,
        gain_row,
        in_conv,
        in_gate,
        one_cols,
        two_cols,
        ct_cols,
        middle_cols,
        ffn_all,
        gated_all,
    )


class SplitSwap:
    def __init__(self, array, swapped, plane_send, plane_recv, tp_send, tp_recv, local_sem):
        self.plane, self.tp = Group(PLANE, plane_send, plane_recv), Group(("tp",), tp_send, tp_recv)
        self.array, self.swapped, self.local_sem = array, swapped, local_sem
        rows = array.shape[0] // self.tp.count
        self.rows = pl.ds(pl.multiple_of(self.tp.me * rows, rows), rows)

    def columns(self, index):
        share = self.swapped.shape[2]
        return self.array.at[self.rows, pl.ds(pl.multiple_of(index * share, share), share)]

    def begin(self):
        mine = self.swapped.at[self.plane.me, self.rows, :]
        self.local = pltpu.make_async_copy(
            self.columns(self.plane.me), mine, self.local_sem
        )
        self.local.start()
        self.copies = [
            self.plane.one(self.columns(other), mine, 0, hop)
            for hop, other in enumerate(self.plane.others)
        ]

    def pass_on(self):
        finish(self.copies)
        self.local.wait()
        here = self.swapped.at[:, self.rows, :]
        self.copies = [self.tp.one(here, here, 0, hop) for hop in range(self.tp.count - 1)]

    def end(self):
        finish(self.copies)


def head_kernel(
    swaps,
    tokens,
    gain,
    ct,
    in_conv,
    conv_in,
    conv_all,
    *refs,
):
    if swaps:
        swapped, *refs = refs
    normed, block_buf, block_sem, *sems = refs
    conv = PlaneGather(in_conv, conv_all, *sems[:2])
    if swaps:
        swap = SplitSwap(ct, swapped, *sems[3:])
        greet([(PLANE, conv.others), (("tp",), swap.tp.others)])
    else:
        greet([(PLANE, conv.others)])
    conv.begin(sems[2])
    if swaps:
        swap.begin()
    hidden_in = tokens[...].astype(jnp.float32)
    normed[...] = (hidden_in * inverse_rms(hidden_in) * gain[...].astype(jnp.float32)).astype(
        normed.dtype
    )

    conv.relay()
    conv.hand_over()
    conv.hand_over_last()
    if swaps:
        swap.pass_on()
    conv.end()
    product_in_blocks(normed, conv_all, conv_in, block_buf, block_sem)
    if swaps:
        swap.end()


def run_head(call_id, tokens, gain, ct, shard, swaps):
    rows, width = tokens.shape
    inner = shard.shape[1]
    low = jnp.bfloat16
    vmem = pl.BlockSpec(memory_space=pltpu.VMEM)
    hbm = pl.BlockSpec(memory_space=pltpu.HBM)
    count, tp_count = group_size(PLANE), group_size(("tp",))
    dma = pltpu.SemaphoreType.DMA
    swap_sems = [
        dma((1, count - 1)),
        dma((1, count - 1)),
        dma((1, tp_count - 1)),
        dma((1, tp_count - 1)),
        dma(()),
    ]
    swapped = [jax.ShapeDtypeStruct((count, rows, width // count), low)]
    return pl.pallas_call(
        functools.partial(head_kernel, swaps),
        in_specs=[vmem] * 3 + [hbm],
        out_specs=[vmem] + [hbm] * (2 if swaps else 1),
        out_shape=[
            jax.ShapeDtypeStruct((rows, inner), low),
            jax.ShapeDtypeStruct((width, inner), low),
        ]
        + (swapped if swaps else []),
        scratch_shapes=[
            pltpu.VMEM((rows, width), low),
            pltpu.VMEM((2, width, WIDE), low),
            pltpu.SemaphoreType.DMA((2,)),
        ]
        + gather_scratch()
        + (swap_sems if swaps else []),
        compiler_params=pltpu.CompilerParams(
            collective_id=call_id, has_side_effects=True, vmem_limit_bytes=VMEM_GRANT
        ),
    )(tokens, gain, ct, shard)


def per_device(
    tokens,
    mixgain,
    inproj,
    convkern,
    convbias,
    selproj,
    stepproj,
    stepbias,
    decaylog,
    skipgain,
    outproj,
    ffngain,
    gateup,
    downproj,
    cotangent,
):
    seqs, span, width = tokens.shape
    rows = seqs * span
    taps, inner = convkern.shape
    rank = stepproj.shape[0]
    n_state = decaylog.shape[1]
    tiles = inner // LANE
    gain_mix = mixgain.astype(jnp.float32)
    kernel = convkern.astype(jnp.float32)
    kernel_bias = convbias.astype(jnp.float32)
    step_bias = stepbias.astype(jnp.float32)
    skip_weight = skipgain.astype(jnp.float32)
    decay_rate = -jnp.exp(jnp.transpose(decaylog.astype(jnp.float32)))
    rate = (decay_rate * LOG2E).reshape(n_state, tiles, LANE)

    gain_mix_row, gain_ffn_row = mixgain.reshape(1, width), ffngain.reshape(1, width)
    low = jnp.bfloat16

    tokens_rows = tokens.reshape(rows, width)
    ct_low = cotangent.reshape(rows, width)
    ffn_pack = gathered_rows(
        jnp.concatenate([gateup[0], gateup[1], jnp.transpose(downproj)], 1)
    )
    swap_now = swaps_in_kernels(width)
    conv_in, in_conv, *swapped = run_head(
        5, tokens_rows, gain_mix_row, ct_low, inproj[0], swap_now
    )
    ct_cols = swapped[0].reshape(-1, swapped[0].shape[2]) if swapped else swapped_columns(ct_low)
    hidden_in = tokens_rows.astype(jnp.float32)
    scale_one = inverse_rms(hidden_in)
    normed_one = (hidden_in * scale_one * gain_mix).astype(low)

    conv_seqs = conv_in.reshape(seqs, span, inner)
    rim_rows = passed_along(conv_seqs[:, span - (taps - 1) :], "ctx", 1)
    padded_in = jnp.concatenate([rim_rows, conv_seqs], 1).astype(jnp.float32)
    conv_out = kernel_bias[None, None]
    for offset in range(taps):
        conv_out = conv_out + kernel[offset][None, None] * padded_in[:, offset : offset + span]
    conv_out = conv_out.reshape(rows, inner)
    scan_in = jax.nn.silu(conv_out).astype(low)
    scan_float = scan_in.astype(jnp.float32)
    columns = selproj.shape[1]
    select_width = -(-columns // LANE) * LANE
    select_weights = jnp.pad(selproj, ((0, 0), (0, select_width - columns)))
    select_cols, gate_mix, in_gate = run_select(
        0, matmul(scan_in, select_weights), normed_one, inproj[1]
    )
    step_low = select_cols[:, :rank].astype(low)
    b_rows = select_cols[:, rank : rank + n_state].reshape(-1)
    c_rows = select_cols[:, rank + n_state : columns].reshape(-1)
    step_pre = matmul(step_low, stepproj) + step_bias[None]
    step_size = jax.nn.softplus(step_pre)
    in_pairs = lax.axis_size("ctx") == 2
    if in_pairs:
        prior, scan_out, out_all = scan_forward_pair(
            6, step_size, scan_float, b_rows, c_rows, rate, seqs, outproj
        )
    else:
        span_decay = jnp.exp(
            decay_rate[None] * jnp.sum(step_size.reshape(seqs, span, inner), 1)[:, None]
        ).reshape(seqs, n_state, tiles, LANE)
        ends = scan_ends(step_size, scan_float, b_rows, rate, seqs, False)
        start = from_earlier(ends, span_decay, 1)
        prior, scan_out = scan_forward(start, step_size, scan_float, b_rows, c_rows, rate, seqs)
        out_all = gathered_rows(outproj)
    mixer_core = scan_out + skip_weight[None] * scan_float
    gate_sig = jax.nn.silu(gate_mix)
    gated = (mixer_core * gate_sig).astype(low)
    normed_two, middle, gated_all, *swapped = mixer_out(
        1,
        gated,
        out_all,
        tokens_rows,
        gain_ffn_row,
        [normed_one] if swap_now else [],
    )
    (normed_one_cols,) = swapped if swap_now else [swapped_columns(normed_one)]
    made, *swapped = run_ffn(8, normed_two, ct_low, ffn_pack, swap_now)
    (normed_two_cols,) = swapped or [swapped_columns(normed_two)]
    ffn_all = gathered_rows(made)
    middle_low, middle_grad, ffngain_part, gated_grad, ffn_part = ffn_back(
        2, made, ct_low, middle, gain_ffn_row, out_all, ffn_pack
    )
    core_grad = gated_grad * gate_sig
    gate_mix_grad = (gated_grad * mixer_core * silu_slope(gate_mix)).astype(low)
    grad_skipgain = jnp.sum(core_grad * scan_float, 0)
    if in_pairs:
        step_grad, input_grad, rate_grad, parts, *layer_rows = scan_backward_pair(
            7,
            prior,
            step_size,
            scan_float,
            core_grad,
            b_rows,
            c_rows,
            rate,
            seqs,
            ffn_part,
            middle,
            [],
        )
    else:
        back_ends = scan_ends(step_size, core_grad, c_rows, rate, seqs, True)
        end_grad = from_earlier(back_ends, span_decay, -1)
        step_grad, input_grad, rate_grad, parts = scan_backward(
            end_grad, prior, step_size, scan_float, core_grad, b_rows, c_rows, rate, seqs
        )
        ffn_sum = lax.psum_scatter(ffn_part, "tp", scatter_dimension=0, tiled=True)
        layer_rows = jnp.split((middle + ffn_sum.astype(jnp.float32)).astype(low), 2, 1)
    grad_decaylog = rate_grad.reshape(n_state, inner) * decay_rate
    pre_grad = step_grad * jax.nn.sigmoid(step_pre)
    grad_stepbias = jnp.sum(pre_grad, 0)
    pre_low = pre_grad.astype(low)
    select_part = jnp.concatenate(
        [
            matmul_nt(pre_low, stepproj),
            jnp.sum(parts, -1),
            jnp.zeros((rows, select_width - columns), jnp.float32),
        ],
        1,
    ).astype(low)
    select_low, layer_first = sum_over_tp(3, select_part, layer_rows[0])
    scan_in_grad = (
        core_grad * skip_weight[None]
        + input_grad
        + matmul_nt(select_low, select_weights)
    )
    conv_grad = scan_in_grad * silu_slope(conv_out)
    grad_convbias = jnp.sum(conv_grad, 0)
    conv_grad_seqs = conv_grad.reshape(seqs, span, inner)
    padded_grad = jnp.zeros(padded_in.shape, jnp.float32)
    kernel_rows = []
    for offset in range(taps):
        kernel_rows.append(jnp.sum(conv_grad_seqs * padded_in[:, offset : offset + span], (0, 1)))
        padded_grad = padded_grad + jnp.pad(
            kernel[offset][None, None] * conv_grad_seqs,
            ((0, 0), (offset, taps - 1 - offset), (0, 0)),
        )
    grad_convkern = jnp.stack(kernel_rows)
    returned = passed_along(padded_grad[:, : taps - 1], "ctx", -1)
    conv_in_grad = (
        (padded_grad[:, taps - 1 :] + jnp.pad(returned, ((0, 0), (span - taps + 1, 0), (0, 0))))
        .astype(low)
        .reshape(rows, inner)
    )
    vectors = [
        grad_convkern,
        grad_convbias[None],
        grad_stepbias[None],
        grad_decaylog,
        grad_skipgain[None],
        ffngain_part,
    ]
    (
        tokens_grad,
        layer_last,
        vectors,
        grad_stepproj,
        grad_selproj,
        gains,
        _,
        grad_inproj,
        grad_outproj,
        grad_gateup,
        grad_downproj,
    ) = run_tail(
        4,
        columns,
        swap_now,
        conv_in_grad,
        gate_mix_grad,
        vectors,
        layer_rows[1],
        middle_low,
        step_low,
        pre_low,
        select_low,
        scan_in,
        tokens_rows,
        middle_grad,
        gain_mix_row,
        in_conv,
        in_gate,
        normed_one_cols,
        normed_two_cols,
        ct_cols,
        normed_two_cols if swap_now else swapped_columns(middle_low),
        ffn_all,
        gated_all,
    )
    at = taps + 2
    return (
        jnp.concatenate([layer_first, layer_last], 1).reshape(tokens.shape),
        tokens_grad.reshape(tokens.shape),
        gains[8:10].reshape(width),
        grad_inproj,
        vectors[:taps],
        vectors[taps],
        jnp.transpose(grad_selproj),
        grad_stepproj,
        vectors[taps + 1],
        jnp.transpose(vectors[at : at + n_state]),
        vectors[at + n_state],
        grad_outproj,
        gains[10:12].reshape(width),
        grad_gateup,
        grad_downproj,
    )


def solution(mesh):
    in_specs = (
        P("dp", "ctx", None),
        P(),
        P(None, ("dp", "ctx"), "tp"),
        P(None, "tp"),
        P("tp"),
        P("tp", None),
        P(None, "tp"),
        P("tp"),
        P("tp", None),
        P("tp"),
        P("tp", ("dp", "ctx")),
        P(),
        P(None, ("dp", "ctx"), "tp"),
        P("tp", ("dp", "ctx")),
        P("dp", "ctx", None),
    )
    out_specs = (
        P("dp", "ctx", None),
        P("dp", "ctx", None),
        P(),
        P(None, ("dp", "ctx"), "tp"),
        P(None, "tp"),
        P("tp"),
        P("tp", None),
        P(None, "tp"),
        P("tp"),
        P("tp", None),
        P("tp"),
        P("tp", ("dp", "ctx")),
        P(),
        P(None, ("dp", "ctx"), "tp"),
        P("tp", ("dp", "ctx")),
    )
    return jax.shard_map(
        per_device, mesh=mesh, in_specs=in_specs, out_specs=out_specs, check_vma=False
    )
```

```python
import functools
import math

import jax
import jax.numpy as jnp
from jax import lax
from jax.experimental import pallas as pl
from jax.experimental.pallas import tpu as pltpu
from jax.sharding import PartitionSpec as P

EPSILON = 1e-05
LOG2E = math.log2(math.e)
LN2 = math.log(2.0)
SUB = 8
LANE = 128
VMEM_GRANT = 60 * 2**20
PLANE = ("dp", "ctx")


def passed_along(value, axis, steps):
    count = lax.axis_size(axis)
    first, last = (max(0, -steps), min(count, count - steps))
    return lax.ppermute(value, axis, [(source, source + steps) for source in range(first, last)])


def matmul(left, right):
    return jnp.dot(left, right, preferred_element_type=jnp.float32)


def matmul_nt(left, right):
    return lax.dot_general(
        left, right, (((1,), (1,)), ((), ())), preferred_element_type=jnp.float32
    )


def matmul_tn(left, right):
    return lax.dot_general(
        left, right, (((0,), (0,)), ((), ())), preferred_element_type=jnp.float32
    )


def inverse_rms(values):
    return lax.rsqrt(jnp.mean(values * values, -1, keepdims=True) + EPSILON)


def silu_slope(values):
    logistic = jax.nn.sigmoid(values)
    return logistic * (1.0 + values * (1.0 - logistic))


def norm_back(grad_norm, values, scale, gain):
    scaled_grad = grad_norm * gain
    unit_rows = values * scale
    return scale * (scaled_grad - unit_rows * jnp.mean(scaled_grad * unit_rows, -1, keepdims=True))


def stage_in(ref, group, held):
    for tile in range(held.shape[0] // SUB):
        held[pl.ds(tile * SUB, SUB), :] = ref[
            pl.ds(pl.multiple_of(group * SUB, SUB), SUB), pl.ds(tile * LANE, LANE)
        ]


def stage_out(held, ref, group):
    for tile in range(held.shape[0] // SUB):
        ref[pl.ds(pl.multiple_of(group * SUB, SUB), SUB), pl.ds(tile * LANE, LANE)] = held[
            pl.ds(tile * SUB, SUB), :
        ]


def token_row(held, at, tiles):
    return held[pl.ds(at, tiles, stride=SUB), :]


def ends_kernel(
    n_state,
    tiles,
    groups,
    reverse,
    step_ref,
    drive_ref,
    rows_ref,
    rate_ref,
    end_ref,
    step_held,
    drive_held,
):
    base = pl.program_id(0) * groups * SUB * n_state
    rates = [rate_ref[n] for n in range(n_state)]

    def one(turn, states):
        group = groups - 1 - turn if reverse else turn
        order = range(SUB - 1, -1, -1) if reverse else range(SUB)
        states = list(states)
        stage_in(step_ref, group, step_held)
        stage_in(drive_ref, group, drive_held)
        for at in order:
            step = token_row(step_held, at, tiles)
            drive = token_row(drive_held, at, tiles)
            if not reverse:
                drive = drive * step
            for n in range(n_state):
                row = rows_ref[base + (group * SUB + at) * n_state + n]
                decay = jnp.exp2(step * rates[n])
                if reverse:
                    states[n] = decay * (states[n] + drive * row)
                else:
                    states[n] = decay * states[n] + drive * row
        return tuple(states)

    zero = jnp.zeros((tiles, LANE), jnp.float32)
    states = lax.fori_loop(0, groups, one, (zero,) * n_state)
    for n in range(n_state):
        end_ref[0, n] = states[n]


def scan_ends(step, drive, rows, rate, seqs, reverse):
    n_state, tiles, _ = rate.shape
    groups = step.shape[0] // seqs // SUB
    rows_spec = pl.BlockSpec((groups * SUB, tiles * LANE), lambda s: (s, 0))
    held = pltpu.VMEM((tiles * SUB, LANE), jnp.float32)
    return pl.pallas_call(
        functools.partial(ends_kernel, n_state, tiles, groups, reverse),
        grid=(seqs,),
        in_specs=[
            rows_spec,
            rows_spec,
            pl.BlockSpec(memory_space=pltpu.SMEM),
            pl.BlockSpec((n_state, tiles, LANE), lambda s: (0, 0, 0)),
        ],
        out_specs=pl.BlockSpec((1, n_state, tiles, LANE), lambda s: (s, 0, 0, 0)),
        out_shape=jax.ShapeDtypeStruct((seqs, n_state, tiles, LANE), jnp.float32),
        scratch_shapes=[held, held],
        compiler_params=pltpu.CompilerParams(vmem_limit_bytes=VMEM_GRANT),
    )(step, drive, rows, rate)


def forward_kernel(
    n_state,
    tiles,
    groups,
    blocks,
    start_ref,
    step_ref,
    input_ref,
    brow_ref,
    crow_ref,
    rate_ref,
    prior_ref,
    mixed_ref,
    carried,
    step_held,
    input_held,
    mixed_held,
):
    base = (pl.program_id(0) * blocks + pl.program_id(1)) * groups * SUB * n_state

    @pl.when(pl.program_id(1) == 0)
    def _():
        carried[...] = start_ref[0]

    def one(group, states):
        states = list(states)
        stage_in(step_ref, group, step_held)
        stage_in(input_ref, group, input_held)
        for at in range(SUB):
            step = token_row(step_held, at, tiles)
            drive = step * token_row(input_held, at, tiles)
            mixed = [None] * 2
            for n in range(n_state):
                where = base + (group * SUB + at) * n_state + n
                prior_ref[group * SUB + at, n] = states[n]
                decay = jnp.exp2(step * rate_ref[n])
                states[n] = decay * states[n] + drive * brow_ref[where]
                term = states[n] * crow_ref[where]
                mixed[n % 2] = term if mixed[n % 2] is None else mixed[n % 2] + term
            mixed_held[pl.ds(at, tiles, stride=SUB), :] = mixed[0] + mixed[1]
        stage_out(mixed_held, mixed_ref, group)
        return tuple(states)

    states = lax.fori_loop(0, groups, one, tuple(carried[n] for n in range(n_state)))
    for n in range(n_state):
        carried[n] = states[n]


def scan_forward(start, step, inputs, b_rows, c_rows, rate, seqs):
    n_state, tiles, _ = rate.shape
    all_groups = step.shape[0] // SUB
    groups = math.gcd(all_groups // seqs, 4)
    blocks = all_groups // seqs // groups
    rows_spec = pl.BlockSpec((groups * SUB, tiles * LANE), lambda s, b: (s * blocks + b, 0))
    held = pltpu.VMEM((tiles * SUB, LANE), jnp.float32)
    smem = pl.BlockSpec(memory_space=pltpu.SMEM)
    tokens = all_groups * SUB
    return pl.pallas_call(
        functools.partial(forward_kernel, n_state, tiles, groups, blocks),
        grid=(seqs, blocks),
        in_specs=[
            pl.BlockSpec((1, n_state, tiles, LANE), lambda s, b: (s, 0, 0, 0)),
            rows_spec,
            rows_spec,
            smem,
            smem,
            pl.BlockSpec((n_state, tiles, LANE), lambda s, b: (0, 0, 0)),
        ],
        out_specs=[
            pl.BlockSpec(
                (groups * SUB, n_state, tiles, LANE), lambda s, b: (s * blocks + b, 0, 0, 0)
            ),
            rows_spec,
        ],
        out_shape=[
            jax.ShapeDtypeStruct((tokens, n_state, tiles, LANE), jnp.float32),
            jax.ShapeDtypeStruct(step.shape, jnp.float32),
        ],
        scratch_shapes=[pltpu.VMEM((n_state, tiles, LANE), jnp.float32)] + [held] * 3,
        compiler_params=pltpu.CompilerParams(vmem_limit_bytes=VMEM_GRANT),
    )(start, step, inputs, b_rows, c_rows, rate)


def backward_kernel(
    n_state,
    tiles,
    groups,
    blocks,
    end_ref,
    prior_ref,
    step_ref,
    input_ref,
    ograd_ref,
    brow_ref,
    crow_ref,
    rate_ref,
    picks_ref,
    step_grad_ref,
    input_grad_ref,
    rate_grad_ref,
    part_ref,
    carried,
    step_held,
    input_held,
    ograd_held,
    step_grad_held,
    input_grad_held,
):
    block = blocks - 1 - pl.program_id(1)
    base = (pl.program_id(0) * blocks + block) * groups * SUB * n_state

    @pl.when(pl.program_id(1) == 0)
    def _():
        carried[...] = end_ref[0]

    @pl.when((pl.program_id(0) == 0) & (pl.program_id(1) == 0))
    def _():
        rate_grad_ref[...] = jnp.zeros_like(rate_grad_ref)

    def one(turn, grads):
        group = groups - 1 - turn
        grads = list(grads)
        stage_in(step_ref, group, step_held)
        stage_in(input_ref, group, input_held)
        stage_in(ograd_ref, group, ograd_held)
        for at in range(SUB - 1, -1, -1):
            step = token_row(step_held, at, tiles)
            value = token_row(input_held, at, tiles)
            ograd = token_row(ograd_held, at, tiles)
            drive = step * value
            along_b = None
            along_rate = None
            brow_parts, crow_parts = [], []
            for n in range(n_state):
                where = base + (group * SUB + at) * n_state + n
                brow, crow = brow_ref[where], crow_ref[where]
                rate = rate_ref[n]
                decay = jnp.exp2(step * rate)
                grad = ograd * crow + grads[n]
                kept = decay * prior_ref[group * SUB + at, n]
                state = kept + drive * brow
                decay_term = grad * kept
                grads[n] = decay * grad
                rate_grad_ref[n] += decay_term * step
                by_rate, by_brow = decay_term * rate, grad * brow
                along_rate = by_rate if along_rate is None else along_rate + by_rate
                along_b = by_brow if along_b is None else along_b + by_brow
                brow_parts.append(grad * drive)
                crow_parts.append(ograd * state)
            step_grad_held[pl.ds(at, tiles, stride=SUB), :] = along_rate * LN2 + along_b * value
            input_grad_held[pl.ds(at, tiles, stride=SUB), :] = along_b * step
            parts = jnp.concatenate(brow_parts + crow_parts, 0).astype(jnp.bfloat16)
            part_ref[group * SUB + at] = jnp.dot(
                picks_ref[...], parts, preferred_element_type=jnp.float32
            )
        stage_out(step_grad_held, step_grad_ref, group)
        stage_out(input_grad_held, input_grad_ref, group)
        return tuple(grads)

    grads = lax.fori_loop(0, groups, one, tuple(carried[n] for n in range(n_state)))
    for n in range(n_state):
        carried[n] = grads[n]


def scan_backward(end_grad, prior, step, inputs, ograd, b_rows, c_rows, rate, seqs):
    n_state, tiles, _ = rate.shape
    all_groups = step.shape[0] // SUB
    groups = math.gcd(all_groups // seqs, 4)
    blocks = all_groups // seqs // groups

    def at(s, b):
        return s * blocks + blocks - 1 - b

    rows_spec = pl.BlockSpec((groups * SUB, tiles * LANE), lambda s, b: (at(s, b), 0))
    held = pltpu.VMEM((tiles * SUB, LANE), jnp.float32)
    smem = pl.BlockSpec(memory_space=pltpu.SMEM)
    tokens = all_groups * SUB
    picks = jnp.repeat(jnp.eye(2 * n_state, dtype=jnp.bfloat16), tiles, 1)
    return pl.pallas_call(
        functools.partial(backward_kernel, n_state, tiles, groups, blocks),
        grid=(seqs, blocks),
        in_specs=[
            pl.BlockSpec((1, n_state, tiles, LANE), lambda s, b: (s, 0, 0, 0)),
            pl.BlockSpec((groups * SUB, n_state, tiles, LANE), lambda s, b: (at(s, b), 0, 0, 0)),
            rows_spec,
            rows_spec,
            rows_spec,
            smem,
            smem,
            pl.BlockSpec((n_state, tiles, LANE), lambda s, b: (0, 0, 0)),
            pl.BlockSpec(picks.shape, lambda s, b: (0, 0)),
        ],
        out_specs=[
            rows_spec,
            rows_spec,
            pl.BlockSpec((n_state, tiles, LANE), lambda s, b: (0, 0, 0)),
            pl.BlockSpec((groups * SUB, 2 * n_state, LANE), lambda s, b: (at(s, b), 0, 0)),
        ],
        out_shape=[
            jax.ShapeDtypeStruct(step.shape, jnp.float32),
            jax.ShapeDtypeStruct(step.shape, jnp.float32),
            jax.ShapeDtypeStruct(rate.shape, jnp.float32),
            jax.ShapeDtypeStruct((tokens, 2 * n_state, LANE), jnp.float32),
        ],
        scratch_shapes=[pltpu.VMEM((n_state, tiles, LANE), jnp.float32)] + [held] * 5,
        compiler_params=pltpu.CompilerParams(vmem_limit_bytes=VMEM_GRANT),
    )(end_grad, prior, step, inputs, ograd, b_rows, c_rows, rate, picks)


def from_earlier(ends, decay, steps):
    count = lax.axis_size("ctx")
    if count == 1:
        return jnp.zeros_like(ends)
    if count == 2:
        return passed_along(ends, "ctx", steps)
    index = lax.axis_index("ctx")
    all_ends = lax.all_gather(ends, "ctx")
    all_decays = lax.all_gather(decay, "ctx")

    def one(turn, state):
        at = turn if steps > 0 else count - 1 - turn
        reached = at < index if steps > 0 else at > index
        return jnp.where(reached, all_decays[at] * state + all_ends[at], state)

    return lax.fori_loop(0, count, one, jnp.zeros_like(ends))


def gathered_rows(rows):
    return lax.all_gather(rows, PLANE, axis=0, tiled=True)


def swapped_columns(rows):
    return lax.all_to_all(rows, PLANE, split_axis=1, concat_axis=0, tiled=True)


def place_in(axes):
    index = 0
    for axis in axes:
        index = index * lax.axis_size(axis) + lax.axis_index(axis)
    return index


def device_at(axes, index):
    where = {}
    for axis in reversed(axes):
        size = lax.axis_size(axis)
        where[axis] = lax.rem(index, size)
        index = lax.div(index, size)
    return where


def greet(groups):
    barrier = pltpu.get_barrier_semaphore()
    total = 0
    for axes, others in groups:
        for other in others:
            pl.semaphore_signal(
                barrier,
                inc=1,
                device_id=device_at(axes, other),
                device_id_type=pl.DeviceIdType.MESH,
            )
            total += 1
    pl.semaphore_wait(barrier, total)


def sent(source, target, send_sem, recv_sem, where):
    copy = pltpu.make_async_remote_copy(
        src_ref=source,
        dst_ref=target,
        send_sem=send_sem,
        recv_sem=recv_sem,
        device_id=where,
        device_id_type=pl.DeviceIdType.MESH,
    )
    copy.start()
    return copy


def finish(copies):
    for copy in copies:
        copy.wait()


def rows_of(ref, index, count):
    rows = ref.shape[0] // count
    return ref.at[pl.ds(pl.multiple_of(index * rows, rows), rows), :]


class Group:
    def __init__(self, axes, send_sem, recv_sem):
        self.axes = axes
        self.count = math.prod(lax.axis_size(axis) for axis in axes)
        self.me = place_in(axes)
        self.others = [lax.rem(self.me + hop, self.count) for hop in range(1, self.count)]
        self.send_sem, self.recv_sem = send_sem, recv_sem

    def own(self, ref):
        return rows_of(ref, self.me, self.count)

    def one(self, source, target, which, hop):
        return sent(
            source,
            target,
            self.send_sem.at[which, hop],
            self.recv_sem.at[which, hop],
            device_at(self.axes, self.others[hop]),
        )

    def scatter(self, part, slot, which):
        return [
            self.one(rows_of(part, other, self.count), slot.at[hop], which, hop)
            for hop, other in enumerate(self.others)
        ]

    def total(self, part, slot):
        total = self.own(part)[...].astype(jnp.float32)
        for hop in range(self.count - 1):
            total = total + slot[hop].astype(jnp.float32)
        return total

    def spread(self, ref, which):
        return [self.one(self.own(ref), self.own(ref), which, hop) for hop in range(self.count - 1)]


def slots_for(part, count):
    return pltpu.VMEM((count - 1, part.shape[0] // count) + part.shape[1:], part.dtype)


def group_size(axes):
    return math.prod(lax.axis_size(axis) for axis in axes)


def line_of_four():
    me = lax.axis_index("tp")
    near = me + 1 - 2 * lax.rem(me, 2)
    return me, near, lax.rem(me + 2, 4), lax.rem(near + 2, 4)


class LineSum:
    def __init__(self, part, near_slots, far_slot, passed, send_sem, recv_sem):
        self.part, self.near_slots, self.far_slot = part, near_slots, far_slot
        self.passed, self.send_sem, self.recv_sem = passed, send_sem, recv_sem
        self.me, self.near, self.far, self.cross = line_of_four()
        self.blocks = send_sem.shape[1]
        self.copies = []

    def columns(self, j):
        wide = self.part.shape[1] // self.blocks
        return slice(j * wide, (j + 1) * wide)

    def rows(self, index):
        return rows_of(self.part, index, 4)

    def send(self, source, target, which, j, where):
        copy = sent(
            source.at[:, self.columns(j)],
            target.at[:, self.columns(j)],
            self.send_sem.at[which, j],
            self.recv_sem.at[which, j],
            {"tp": where},
        )
        self.copies.append((which, copy))
        return copy

    def begin(self, j):
        first = self.send(self.rows(self.cross), self.near_slots.at[0], 0, j, self.near)
        self.send(self.rows(self.near), self.near_slots.at[1], 1, j, self.near)
        return first

    def pass_on(self, j, first):
        first.wait_recv()
        columns = self.columns(j)
        self.passed[:, columns] = (
            self.rows(self.far)[:, columns].astype(jnp.float32)
            + self.near_slots[0, :, columns].astype(jnp.float32)
        ).astype(self.passed.dtype)
        self.send(self.passed, self.far_slot, 2, j, self.far)

    def total(self):
        for which, copy in self.copies:
            copy.wait_send()
            if which:
                copy.wait_recv()
        return (
            self.rows(self.me)[...].astype(jnp.float32)
            + self.near_slots[1].astype(jnp.float32)
            + self.far_slot[...].astype(jnp.float32)
        )

    def pass_all(self, firsts):
        for j, first in enumerate(firsts):
            self.pass_on(j, first)


def line_sum_scratch(part, blocks):
    share = (part.shape[0] // 4,) + part.shape[1:]
    sems = pltpu.SemaphoreType.DMA((3, blocks))
    return [
        pltpu.VMEM((2,) + share, part.dtype),
        pltpu.VMEM(share, part.dtype),
        pltpu.VMEM(share, part.dtype),
        sems,
        sems,
    ]


class LineSpread:
    def __init__(self, ref, send_sem, recv_sem):
        self.ref, self.send_sem, self.recv_sem = ref, send_sem, recv_sem
        self.me, self.near, self.far, self.cross = line_of_four()

    def send(self, owner, half, which, where):
        rows = rows_of(self.ref, owner, 4)
        if half is not None:
            wide = self.ref.shape[1] // 2
            rows = rows.at[:, half * wide : (half + 1) * wide]
        return sent(rows, rows, self.send_sem.at[which], self.recv_sem.at[which], {"tp": where})

    def begin(self):
        self.across = [self.send(self.me, half, half, self.far) for half in range(2)]
        self.within = [self.send(self.me, None, 2, self.near)]

    def pass_on(self):
        for half, copy in enumerate(self.across):
            copy.wait_recv()
            self.within.append(self.send(self.far, half, 3 + half, self.near))

    def end(self):
        for copy in self.across:
            copy.wait_send()
        finish(self.within)

    def run(self):
        self.begin()
        self.pass_on()
        self.end()


def line_spread_scratch():
    return [pltpu.SemaphoreType.DMA((5,)), pltpu.SemaphoreType.DMA((5,))]


class Swap:
    def __init__(self, arrays, swapped, send_sem, recv_sem, local_sem):
        plane = Group(PLANE, send_sem, recv_sem)
        self.plane, self.arrays, self.swapped, self.local_sem = plane, arrays, swapped, local_sem

    def begin(self):
        self.copies, plane = [], self.plane
        for which, (array, swapped) in enumerate(zip(self.arrays, self.swapped)):
            share = swapped.shape[1]

            def columns(index):
                return array.at[:, pl.ds(pl.multiple_of(index * share, share), share)]

            for hop, other in enumerate(plane.others):
                self.copies.append(plane.one(columns(other), plane.own(swapped), which, hop))
            local = pltpu.make_async_copy(
                columns(plane.me), plane.own(swapped), self.local_sem.at[which]
            )
            local.start()
            self.copies.append(local)

    def end(self):
        finish(self.copies)


def swap_scratch(arrays):
    sems = pltpu.SemaphoreType.DMA((len(arrays), group_size(PLANE) - 1))
    return [sems, sems, pltpu.SemaphoreType.DMA((len(arrays),))] if arrays else []


def swap_shapes(arrays):
    count = group_size(PLANE)
    return [
        jax.ShapeDtypeStruct((array.shape[0] * count, array.shape[1] // count), array.dtype)
        for array in arrays
    ]


def swaps_in_kernels(width):
    return width // group_size(PLANE) % LANE == 0


def gathered_shape(shard):
    return jax.ShapeDtypeStruct(
        (shard.shape[0] * group_size(PLANE),) + shard.shape[1:], shard.dtype
    )


def gather_scratch():
    return [gather_sems(), gather_sems(), pltpu.SemaphoreType.DMA(())]


def product_in_blocks(left, source, target, block_buf, block_sem):
    columns = range(0, source.shape[1], WIDE)

    def fetch(turn):
        at = columns[turn]
        return pltpu.make_async_copy(
            source.at[:, at : at + WIDE], block_buf.at[turn % 2], block_sem.at[turn % 2]
        )

    fetch(0).start()
    for turn, at in enumerate(columns):
        if turn + 1 < len(columns):
            fetch(turn + 1).start()
        fetch(turn).wait()
        target[:, at : at + WIDE] = matmul(left[...], block_buf[turn % 2]).astype(target.dtype)


def select_kernel(
    part,
    normed,
    shard,
    total,
    product,
    gathered,
    slots,
    send_sem,
    recv_sem,
    block_buf,
    block_sem,
    gather_send,
    gather_recv,
    local_sem,
):
    group = Group(("tp",), send_sem, recv_sem)
    gather = PlaneGather(shard, gathered, gather_send, gather_recv)
    greet([(("tp",), group.others), (PLANE, gather.others)])
    gather.begin(local_sem)
    finish(group.scatter(part, slots, 0))
    group.own(total)[...] = group.total(part, slots).astype(total.dtype)
    copies = group.spread(total, 1)
    gather.relay()
    gather.hand_over()
    finish(copies)
    gather.hand_over_last()
    gather.end()
    product_in_blocks(normed, gathered, product, block_buf, block_sem)


def run_select(call_id, part, normed, shard):
    count = group_size(("tp",))
    vmem = pl.BlockSpec(memory_space=pltpu.VMEM)
    hbm = pl.BlockSpec(memory_space=pltpu.HBM)
    sems = pltpu.SemaphoreType.DMA((2, count - 1))
    rows, width = normed.shape
    return pl.pallas_call(
        select_kernel,
        in_specs=[vmem, vmem, hbm],
        out_specs=[vmem, vmem, hbm],
        out_shape=[
            jax.ShapeDtypeStruct(part.shape, part.dtype),
            jax.ShapeDtypeStruct((rows, shard.shape[1]), jnp.float32),
            gathered_shape(shard),
        ],
        scratch_shapes=[
            slots_for(part, count),
            sems,
            sems,
            pltpu.VMEM((2, width, WIDE), jnp.bfloat16),
            pltpu.SemaphoreType.DMA((2,)),
        ]
        + gather_scratch(),
        compiler_params=pltpu.CompilerParams(
            collective_id=call_id, has_side_effects=True, vmem_limit_bytes=VMEM_GRANT
        ),
    )(part, normed, shard)


def sum_kernel(part, own_rows, total, all_rows, slots, send_sem, recv_sem, *line_sems):
    group = Group(("tp",), send_sem, recv_sem)
    rows = LineSpread(all_rows, *line_sems)
    greet([(("tp",), group.others)])
    copies = group.scatter(part, slots, 0)
    group.own(all_rows)[...] = own_rows[...]
    rows.begin()
    finish(copies)
    group.own(total)[...] = group.total(part, slots).astype(total.dtype)
    copies = group.spread(total, 1)
    rows.pass_on()
    finish(copies)
    rows.end()


def sum_over_tp(call_id, part, own_rows):
    count = group_size(("tp",))
    vmem = pl.BlockSpec(memory_space=pltpu.VMEM)
    sems = pltpu.SemaphoreType.DMA((2, count - 1))
    return pl.pallas_call(
        sum_kernel,
        in_specs=[vmem] * 2,
        out_specs=[vmem] * 2,
        out_shape=[
            jax.ShapeDtypeStruct(part.shape, part.dtype),
            jax.ShapeDtypeStruct((own_rows.shape[0] * count, own_rows.shape[1]), own_rows.dtype),
        ],
        scratch_shapes=[slots_for(part, count), sems, sems] + line_spread_scratch(),
        compiler_params=pltpu.CompilerParams(
            collective_id=call_id, has_side_effects=True, vmem_limit_bytes=VMEM_GRANT
        ),
    )(part, own_rows)


def mixer_out_kernel(n_swaps, gated, out_all, tokens, gain, *refs):
    arrays, refs = refs[:n_swaps], refs[n_swaps:]
    normed, middle, gated_all, *refs = refs
    swapped, refs = refs[:n_swaps], refs[n_swaps:]
    part, refs = refs[0], refs[1:]
    line = LineSum(part, *refs[:5])
    spread = LineSpread(normed, *refs[5:7])
    gather_send, gather_recv, local_sem, *refs = refs[7:]
    group = Group(("tp",), None, None)
    gather = PlaneGather(gated, gated_all, gather_send, gather_recv)
    inner = gated.shape[1]
    share = out_all.shape[1]
    greet([(("tp",), group.others), (PLANE, gather.others)])
    gather.begin(local_sem)
    for at in range(out_all.shape[0] // inner):
        part[:, at * share : (at + 1) * share] = matmul(
            gated[...], out_all[at * inner : (at + 1) * inner, :]
        ).astype(part.dtype)
    firsts = [line.begin(j) for j in range(line.blocks)]
    if n_swaps:
        swap = Swap(arrays, swapped, *refs)
        swap.begin()
    line.pass_all(firsts)
    rows = group.own(tokens)[...].astype(jnp.float32) + line.total()
    middle[...] = rows
    group.own(normed)[...] = (rows * inverse_rms(rows) * gain[...].astype(jnp.float32)).astype(
        normed.dtype
    )
    spread.begin()
    gather.relay()
    gather.hand_over()
    spread.pass_on()
    spread.end()
    gather.hand_over_last()
    gather.end()
    if n_swaps:
        swap.end()


def mixer_out(call_id, gated, out_all, tokens, gain, arrays):
    count = group_size(("tp",))
    vmem = pl.BlockSpec(memory_space=pltpu.VMEM)
    hbm = pl.BlockSpec(memory_space=pltpu.HBM)
    rows, width = tokens.shape
    part = jax.ShapeDtypeStruct((rows, width), jnp.bfloat16)
    return pl.pallas_call(
        functools.partial(mixer_out_kernel, len(arrays)),
        in_specs=[vmem] * (4 + len(arrays)),
        out_specs=[vmem] * 2 + [hbm] + [hbm] * len(arrays),
        out_shape=[
            part,
            jax.ShapeDtypeStruct((rows // count, width), jnp.float32),
            gathered_shape(gated),
        ]
        + swap_shapes(arrays),
        scratch_shapes=[pltpu.VMEM(part.shape, part.dtype)]
        + line_sum_scratch(part, 2)
        + line_spread_scratch()
        + gather_scratch()
        + swap_scratch(arrays),
        compiler_params=pltpu.CompilerParams(
            collective_id=call_id, has_side_effects=True, vmem_limit_bytes=VMEM_GRANT
        ),
    )(gated, out_all, tokens, gain, *arrays)


def ffn_kernel(swaps, normed, ct, weights, made, *refs):
    hidden = weights.shape[1] // 3
    if swaps:
        *swapped, block_buf, block_sem, send_sem, recv_sem, local_sem = refs
        swap = Swap([normed], swapped, send_sem, recv_sem, local_sem)
        greet([(PLANE, swap.plane.others)])
        swap.begin()
    else:
        block_buf, block_sem = refs

    def columns(j, which):
        return pl.ds(pl.multiple_of(which * hidden + j * WIDE, WIDE), WIDE)

    def fetch(j, which):
        slot = lax.rem(j, 2)
        return pltpu.make_async_copy(
            weights.at[:, columns(j, which)],
            block_buf.at[slot, which],
            block_sem.at[slot, which],
        )

    for which in range(3):
        fetch(0, which).start()

    @pl.loop(0, hidden // WIDE)
    def _(j):
        slot = lax.rem(j, 2)

        @pl.when(j + 1 < hidden // WIDE)
        def _():
            for which in range(3):
                fetch(j + 1, which).start()

        fetch(j, 0).wait()
        gate = matmul(normed[...], block_buf[slot, 0])
        fetch(j, 1).wait()
        up = matmul(normed[...], block_buf[slot, 1])
        fetch(j, 2).wait()
        act_grad = matmul(ct[...], block_buf[slot, 2])
        logistic = jax.nn.sigmoid(gate)
        silu = gate * logistic
        slope = logistic * (1.0 + gate * (1.0 - logistic))
        made[:, columns(j, 0)] = (silu * up).astype(made.dtype)
        made[:, columns(j, 1)] = (act_grad * up * slope).astype(made.dtype)
        made[:, columns(j, 2)] = (act_grad * silu).astype(made.dtype)

    if swaps:
        swap.end()


def run_ffn(call_id, normed, ct, weights, swaps):
    rows, width = normed.shape
    arrays = [normed] if swaps else []
    vmem = pl.BlockSpec(memory_space=pltpu.VMEM)
    params = dict(collective_id=call_id, has_side_effects=True) if swaps else {}
    return pl.pallas_call(
        functools.partial(ffn_kernel, swaps),
        in_specs=[vmem, vmem, pl.BlockSpec(memory_space=pltpu.HBM)],
        out_specs=[vmem] + [pl.BlockSpec(memory_space=pltpu.HBM)] * len(arrays),
        out_shape=[jax.ShapeDtypeStruct((rows, weights.shape[1]), jnp.bfloat16)]
        + swap_shapes(arrays),
        scratch_shapes=[
            pltpu.VMEM((2, 3, width, WIDE), jnp.bfloat16),
            pltpu.SemaphoreType.DMA((2, 3)),
        ]
        + swap_scratch(arrays),
        compiler_params=pltpu.CompilerParams(vmem_limit_bytes=VMEM_GRANT, **params),
    )(normed, ct, weights)


def ffn_back_kernel(
    made,
    ct,
    middle,
    gain,
    out_all,
    weights,
    middle_low,
    middle_grad,
    gain_grad,
    gated_grad,
    ffn_part,
    part,
    wide_buf,
    down_buf,
    wide_sem,
    down_sem,
    *sems,
):
    hidden = made.shape[1] // 3
    blocks = part.shape[1] // WIDE
    group = Group(("tp",), None, None)
    line = LineSum(part, *sems[:5])
    spread = LineSpread(middle_low, *sems[5:])
    greet([(("tp",), group.others)])

    def fetch(j):
        return pltpu.make_async_copy(
            weights.at[j * WIDE : (j + 1) * WIDE, : 2 * hidden],
            wide_buf.at[j % 2],
            wide_sem.at[j % 2],
        )

    def fetch_down(j):
        return pltpu.make_async_copy(
            weights.at[j * WIDE : (j + 1) * WIDE, 2 * hidden :],
            down_buf.at[j % 2],
            down_sem.at[j % 2],
        )

    fetch(0).start()
    firsts = []
    for j in range(blocks):
        if j + 1 < blocks:
            fetch(j + 1).start()
        else:
            fetch_down(0).start()
        fetch(j).wait()
        columns = slice(j * WIDE, (j + 1) * WIDE)
        part[:, columns] = matmul_nt(made[:, hidden:], wide_buf[j % 2]).astype(part.dtype)
        firsts.append(line.begin(j))
    for j in range(blocks):
        if j + 1 < blocks:
            fetch_down(j + 1).start()
        fetch_down(j).wait()
        ffn_part[:, j * WIDE : (j + 1) * WIDE] = matmul_nt(
            made[:, :hidden], down_buf[j % 2]
        ).astype(ffn_part.dtype)
        line.pass_on(j, firsts[j])
    normed_grad = line.total()
    rows = middle[...]
    scale = inverse_rms(rows)
    gain_grad[...] = jnp.sum(normed_grad * rows * scale, 0, keepdims=True)
    grad = group.own(ct)[...].astype(jnp.float32) + norm_back(
        normed_grad, rows, scale, gain[...].astype(jnp.float32)
    )
    middle_grad[...] = grad
    group.own(middle_low)[...] = grad.astype(middle_low.dtype)
    spread.run()
    inner = gated_grad.shape[1]
    share = out_all.shape[1]
    total = None
    for at in range(out_all.shape[0] // inner):
        one = matmul_nt(
            middle_low[:, at * share : (at + 1) * share], out_all[at * inner : (at + 1) * inner, :]
        )
        total = one if total is None else total + one
    gated_grad[...] = total


def ffn_back(call_id, made, ct, middle, gain, out_all, weights):
    count = group_size(("tp",))
    vmem = pl.BlockSpec(memory_space=pltpu.VMEM)
    rows, width = ct.shape
    hidden = made.shape[1] // 3
    inner = out_all.shape[0] // group_size(PLANE)
    low, full = jnp.bfloat16, jnp.float32
    part = jax.ShapeDtypeStruct((rows, width), low)
    dma = pltpu.SemaphoreType.DMA
    return pl.pallas_call(
        ffn_back_kernel,
        in_specs=[vmem] * 5 + [pl.BlockSpec(memory_space=pltpu.HBM)],
        out_specs=[vmem] * 5,
        out_shape=[
            part,
            jax.ShapeDtypeStruct((rows // count, width), full),
            jax.ShapeDtypeStruct((1, width), full),
            jax.ShapeDtypeStruct((rows, inner), full),
            part,
        ],
        scratch_shapes=[
            pltpu.VMEM(part.shape, low),
            pltpu.VMEM((2, WIDE, 2 * hidden), low),
            pltpu.VMEM((2, WIDE, hidden), low),
            dma((2,)),
            dma((2,)),
        ]
        + line_sum_scratch(part, width // WIDE)
        + line_spread_scratch(),
        compiler_params=pltpu.CompilerParams(
            collective_id=call_id, has_side_effects=True, vmem_limit_bytes=VMEM_GRANT
        ),
    )(made, ct, middle, gain, out_all, weights)


def send_on(source, target, send_sem, recv_sem, ctx):
    return pltpu.make_async_remote_copy(
        src_ref=source,
        dst_ref=target,
        send_sem=send_sem,
        recv_sem=recv_sem,
        device_id={"ctx": ctx},
        device_id_type=pl.DeviceIdType.MESH,
    )


def forward_pair_kernel(
    n_state,
    tiles,
    groups,
    blocks,
    seqs,
    step_ref,
    input_ref,
    brow_ref,
    crow_ref,
    rate_ref,
    shard,
    prior_ref,
    mixed_ref,
    gathered,
    carried,
    ends,
    starts,
    prior_buf,
    step_held,
    input_held,
    mixed_held,
    prior_sem,
    send_sem,
    recv_sem,
    gather_send,
    gather_recv,
    local_sem,
):
    place = lax.axis_index("ctx")
    gather = PlaneGather(shard, gathered, gather_send, gather_recv)
    greet([(PLANE, gather.others)])
    gather.begin(local_sem)

    def hand_on(seq):
        return send_on(ends.at[seq], starts.at[seq], send_sem.at[seq], recv_sem.at[seq], 1)

    def store(block):
        slot = lax.rem(block, 2)
        rows = groups * SUB
        return pltpu.make_async_copy(
            prior_buf.at[slot],
            prior_ref.at[pl.ds(pl.multiple_of(block * rows, rows), rows)],
            prior_sem.at[slot],
        )

    def one_sequence(seq):
        @pl.when(place == 0)
        def _():
            carried[...] = jnp.zeros_like(carried)

        @pl.when(place == 1)
        def _():
            hand_on(seq).wait_recv()
            carried[...] = starts[seq]

        @pl.loop(0, blocks)
        def _(inner_block):
            block = seq * blocks + inner_block
            slot = lax.rem(block, 2)

            @pl.when(block >= 2)
            def _():
                store(block - 2).wait()

            def one(turn, states):
                group = block * groups + turn
                states = list(states)
                stage_in(step_ref, group, step_held)
                stage_in(input_ref, group, input_held)
                for at in range(SUB):
                    step = token_row(step_held, at, tiles)
                    drive = step * token_row(input_held, at, tiles)
                    mixed = [None] * 2
                    for n in range(n_state):
                        where = (group * SUB + at) * n_state + n
                        prior_buf[slot, turn * SUB + at, n] = states[n]
                        decay = jnp.exp2(step * rate_ref[n])
                        states[n] = decay * states[n] + drive * brow_ref[where]
                        term = states[n] * crow_ref[where]
                        mixed[n % 2] = term if mixed[n % 2] is None else mixed[n % 2] + term
                    mixed_held[pl.ds(at, tiles, stride=SUB), :] = mixed[0] + mixed[1]
                stage_out(mixed_held, mixed_ref, group)
                return tuple(states)

            states = lax.fori_loop(0, groups, one, tuple(carried[n] for n in range(n_state)))
            for n in range(n_state):
                carried[n] = states[n]
            store(block).start()

        @pl.when(place == 0)
        def _():
            ends[seq] = carried[...]
            hand_on(seq).start()

    for seq in range(seqs):
        one_sequence(seq)
        if seq == 0:
            gather.relay()
            gather.hand_over()
    gather.hand_over_last()
    for block in range(max(0, seqs * blocks - 2), seqs * blocks):
        store(block).wait()

    @pl.when(place == 0)
    def _():
        for seq in range(seqs):
            hand_on(seq).wait_send()

    gather.end()


def scan_forward_pair(call_id, step, inputs, b_rows, c_rows, rate, seqs, shard):
    n_state, tiles, _ = rate.shape
    tokens, inner = step.shape
    all_groups = tokens // SUB
    groups = math.gcd(all_groups // seqs, 4)
    blocks = all_groups // seqs // groups
    vmem = pl.BlockSpec(memory_space=pltpu.VMEM)
    smem = pl.BlockSpec(memory_space=pltpu.SMEM)
    hbm = pl.BlockSpec(memory_space=pltpu.HBM)
    full = jnp.float32
    held = pltpu.VMEM((tiles * SUB, LANE), full)
    boundary = pltpu.VMEM((seqs, n_state, tiles, LANE), full)
    dma = pltpu.SemaphoreType.DMA
    return pl.pallas_call(
        functools.partial(forward_pair_kernel, n_state, tiles, groups, blocks, seqs),
        in_specs=[vmem, vmem, smem, smem, vmem, hbm],
        out_specs=[hbm, vmem, hbm],
        out_shape=[
            jax.ShapeDtypeStruct((tokens, n_state, tiles, LANE), full),
            jax.ShapeDtypeStruct(step.shape, full),
            gathered_shape(shard),
        ],
        scratch_shapes=[
            pltpu.VMEM((n_state, tiles, LANE), full),
            boundary,
            boundary,
            pltpu.VMEM((2, groups * SUB, n_state, tiles, LANE), full),
            held,
            held,
            held,
            dma((2,)),
            dma((seqs,)),
            dma((seqs,)),
        ]
        + gather_scratch(),
        compiler_params=pltpu.CompilerParams(
            collective_id=call_id, has_side_effects=True, vmem_limit_bytes=VMEM_GRANT
        ),
    )(step, inputs, b_rows, c_rows, rate, shard)


def backward_pair_kernel(
    n_swaps,
    n_state,
    tiles,
    groups,
    blocks,
    seqs,
    step_ref,
    input_ref,
    ograd_ref,
    brow_ref,
    crow_ref,
    rate_ref,
    picks_ref,
    ffn_part,
    middle,
    prior_ref,
    *refs,
):
    arrays, refs = refs[:n_swaps], refs[n_swaps:]
    step_grad_ref, input_grad_ref, rate_grad_ref, part_ref, *refs = refs
    layer_first, layer_last, *refs = refs
    swapped, refs = refs[:n_swaps], refs[n_swaps:]
    carried, ends, starts, prior_buf, step_held, input_held, ograd_held, *refs = refs
    step_grad_held, input_grad_held, ffn_slots, prior_sem, send_sem, recv_sem, *refs = refs
    tp_send, tp_recv, *refs = refs
    place = lax.axis_index("ctx")
    tp = Group(("tp",), tp_send, tp_recv)
    if n_swaps:
        swap = Swap(arrays, swapped, *refs)
        greet([(PLANE, swap.plane.others), (("tp",), tp.others)])
        swap.begin()
    else:
        greet([(("ctx",), [1 - place]), (("tp",), tp.others)])
    ffn_sent = tp.scatter(ffn_part, ffn_slots, 0)

    def hand_on(seq):
        return send_on(ends.at[seq], starts.at[seq], send_sem.at[seq], recv_sem.at[seq], 0)

    def fetch(turn):
        seq = lax.div(turn, blocks)
        block = seq * blocks + blocks - 1 - lax.rem(turn, blocks)
        slot = lax.rem(turn, 2)
        rows = groups * SUB
        return pltpu.make_async_copy(
            prior_ref.at[pl.ds(pl.multiple_of(block * rows, rows), rows)],
            prior_buf.at[slot],
            prior_sem.at[slot],
        )

    fetch(0).start()
    rate_grad_ref[...] = jnp.zeros_like(rate_grad_ref)

    @pl.when(place == 1)
    def _():
        @pl.loop(0, seqs)
        def _(seq):
            def one(turn, grads):
                group = (seq + 1) * blocks * groups - 1 - turn
                grads = list(grads)
                stage_in(step_ref, group, step_held)
                stage_in(ograd_ref, group, ograd_held)
                for at in range(SUB - 1, -1, -1):
                    step = token_row(step_held, at, tiles)
                    ograd = token_row(ograd_held, at, tiles)
                    for n in range(n_state):
                        row = crow_ref[(group * SUB + at) * n_state + n]
                        grads[n] = jnp.exp2(step * rate_ref[n]) * (grads[n] + ograd * row)
                return tuple(grads)

            zero = jnp.zeros((tiles, LANE), jnp.float32)
            grads = lax.fori_loop(0, blocks * groups, one, (zero,) * n_state)
            for n in range(n_state):
                ends[seq, n] = grads[n]
            hand_on(seq).start()

    @pl.loop(0, seqs)
    def _(seq):
        @pl.when(place == 1)
        def _():
            carried[...] = jnp.zeros_like(carried)

        @pl.when(place == 0)
        def _():
            hand_on(seq).wait_recv()
            carried[...] = starts[seq]

        @pl.loop(0, blocks)
        def _(inner_block):
            turn = seq * blocks + inner_block
            slot = lax.rem(turn, 2)
            first_group = (seq * blocks + blocks - 1 - inner_block) * groups

            @pl.when(turn + 1 < seqs * blocks)
            def _():
                fetch(turn + 1).start()

            fetch(turn).wait()

            def one(back, grads):
                inner_group = groups - 1 - back
                group = first_group + inner_group
                grads = list(grads)
                stage_in(step_ref, group, step_held)
                stage_in(input_ref, group, input_held)
                stage_in(ograd_ref, group, ograd_held)
                for at in range(SUB - 1, -1, -1):
                    step = token_row(step_held, at, tiles)
                    value = token_row(input_held, at, tiles)
                    ograd = token_row(ograd_held, at, tiles)
                    drive = step * value
                    along_b = None
                    along_rate = None
                    brow_parts, crow_parts = [], []
                    for n in range(n_state):
                        where = (group * SUB + at) * n_state + n
                        brow, crow = brow_ref[where], crow_ref[where]
                        rate = rate_ref[n]
                        decay = jnp.exp2(step * rate)
                        grad = ograd * crow + grads[n]
                        kept = decay * prior_buf[slot, inner_group * SUB + at, n]
                        state = kept + drive * brow
                        decay_term = grad * kept
                        grads[n] = decay * grad
                        rate_grad_ref[n] += decay_term * step
                        by_rate, by_brow = decay_term * rate, grad * brow
                        along_rate = by_rate if along_rate is None else along_rate + by_rate
                        along_b = by_brow if along_b is None else along_b + by_brow
                        brow_parts.append(grad * drive)
                        crow_parts.append(ograd * state)
                    step_grad_held[pl.ds(at, tiles, stride=SUB), :] = (
                        along_rate * LN2 + along_b * value
                    )
                    input_grad_held[pl.ds(at, tiles, stride=SUB), :] = along_b * step
                    parts = jnp.concatenate(brow_parts + crow_parts, 0).astype(jnp.bfloat16)
                    part_ref[group * SUB + at] = jnp.dot(
                        picks_ref[...], parts, preferred_element_type=jnp.float32
                    )
                stage_out(step_grad_held, step_grad_ref, group)
                stage_out(input_grad_held, input_grad_ref, group)
                return tuple(grads)

            grads = lax.fori_loop(0, groups, one, tuple(carried[n] for n in range(n_state)))
            for n in range(n_state):
                carried[n] = grads[n]

    finish(ffn_sent)
    layer_rows = (middle[...] + tp.total(ffn_part, ffn_slots)).astype(layer_first.dtype)
    half = layer_first.shape[1]
    layer_first[...], layer_last[...] = layer_rows[:, :half], layer_rows[:, half:]

    @pl.when(place == 1)
    def _():
        @pl.loop(0, seqs)
        def _(seq):
            hand_on(seq).wait_send()

    if n_swaps:
        swap.end()


def scan_backward_pair(
    call_id, prior, step, inputs, ograd, b_rows, c_rows, rate, seqs, ffn_part, middle, arrays
):
    n_state, tiles, _ = rate.shape
    tokens, inner = step.shape
    all_groups = tokens // SUB
    groups = math.gcd(all_groups // seqs, 4)
    blocks = all_groups // seqs // groups
    tp_count = group_size(("tp",))
    vmem = pl.BlockSpec(memory_space=pltpu.VMEM)
    smem = pl.BlockSpec(memory_space=pltpu.SMEM)
    hbm = pl.BlockSpec(memory_space=pltpu.HBM)
    full = jnp.float32
    held = pltpu.VMEM((tiles * SUB, LANE), full)
    boundary = pltpu.VMEM((seqs, n_state, tiles, LANE), full)
    dma = pltpu.SemaphoreType.DMA
    layer_half = jax.ShapeDtypeStruct((middle.shape[0], middle.shape[1] // 2), jnp.bfloat16)
    picks = jnp.repeat(jnp.eye(2 * n_state, dtype=jnp.bfloat16), tiles, 1)
    return pl.pallas_call(
        functools.partial(
            backward_pair_kernel, len(arrays), n_state, tiles, groups, blocks, seqs
        ),
        in_specs=[vmem] * 3 + [smem] * 2 + [vmem] * 4 + [hbm] + [vmem] * len(arrays),
        out_specs=[vmem] * 6 + [hbm] * len(arrays),
        out_shape=[
            jax.ShapeDtypeStruct(step.shape, full),
            jax.ShapeDtypeStruct(step.shape, full),
            jax.ShapeDtypeStruct(rate.shape, full),
            jax.ShapeDtypeStruct((tokens, 2 * n_state, LANE), full),
            layer_half,
            layer_half,
        ]
        + swap_shapes(arrays),
        scratch_shapes=[
            pltpu.VMEM((n_state, tiles, LANE), full),
            boundary,
            boundary,
            pltpu.VMEM((2, groups * SUB, n_state, tiles, LANE), full),
        ]
        + [held] * 5
        + [
            slots_for(ffn_part, tp_count),
            dma((2,)),
            dma((seqs,)),
            dma((seqs,)),
            dma((1, tp_count - 1)),
            dma((1, tp_count - 1)),
        ]
        + swap_scratch(arrays),
        compiler_params=pltpu.CompilerParams(
            collective_id=call_id, has_side_effects=True, vmem_limit_bytes=VMEM_GRANT
        ),
    )(step, inputs, ograd, b_rows, c_rows, rate, picks, ffn_part, middle, prior, *arrays)


class PlaneGather:
    def __init__(self, own, gathered, send_sem, recv_sem):
        self.own, self.gathered = own, gathered
        self.send_sem, self.recv_sem = send_sem, recv_sem
        self.dp, self.ctx = lax.axis_index("dp"), lax.axis_index("ctx")
        self.n_dp, self.n_ctx = lax.axis_size("dp"), lax.axis_size("ctx")
        self.hands_on = relayed()
        self.count = self.n_dp * self.n_ctx
        self.me = self.dp * self.n_ctx + self.ctx
        self.others = [lax.rem(self.me + hop, self.count) for hop in range(1, self.count)]
        self.copies = {}
        if self.hands_on:
            core = lax.rem(self.dp, 2)
            over_core = self.dp + 1 - 2 * core
            over_y = lax.rem(self.dp + 2, 4)
            over_x = 1 - self.ctx
            self.core = {"dp": over_core, "ctx": self.ctx}
            self.at_x = {"dp": self.dp, "ctx": over_x}
            self.at_y = {"dp": over_y, "ctx": self.ctx}
            self.from_x = self.dp * 2 + over_x
            self.from_y = over_y * 2 + self.ctx
            self.across = over_y * 2 + over_x

    def part(self, owner, half):
        rows = self.gathered.shape[0] // self.count
        start, size = owner * rows, rows
        if half is not None:
            size = rows // 2
            start = start + half * size
        return self.gathered.at[pl.ds(pl.multiple_of(start, size), size), :]

    def send(self, which, owner, half, where):
        target = self.part(owner, half)
        source = target
        if owner is self.me:
            rows = self.own.shape[0]
            source = self.own
            if half is not None:
                source = self.own.at[pl.ds(half * (rows // 2), rows // 2), :]
        self.copies[which] = sent(
            source, target, self.send_sem.at[which], self.recv_sem.at[which], where
        )

    def arrived(self, *which):
        for one in which:
            self.copies[one].wait_recv()

    def begin(self, local_sem):
        self.local = pltpu.make_async_copy(self.own, self.part(self.me, None), local_sem)
        self.local.start()
        if not self.hands_on:
            for hop, other in enumerate(self.others):
                self.send(hop, self.me, None, device_at(PLANE, other))
            return
        self.send(0, self.me, 1, self.at_x)
        self.send(1, self.me, 0, self.at_y)
        self.send(2, self.me, None, self.core)
        self.send(3, self.me, 0, self.at_x)
        self.send(4, self.me, 1, self.at_y)

    def relay(self):
        if not self.hands_on:
            return
        self.arrived(0, 1)
        self.send(5, self.from_x, 1, self.at_y)
        self.send(6, self.from_y, 0, self.at_x)
        self.send(7, self.from_x, 1, self.core)
        self.send(8, self.from_y, 0, self.core)

    def hand_over(self):
        if not self.hands_on:
            return
        self.arrived(3, 4)
        self.send(9, self.from_x, 0, self.core)
        self.send(10, self.from_y, 1, self.core)

    def hand_over_last(self):
        if not self.hands_on:
            return
        self.arrived(5, 6)
        self.send(11, self.across, 1, self.core)
        self.send(12, self.across, 0, self.core)

    def end(self):
        if self.hands_on:
            self.arrived(2, 7, 8, 9, 10, 11, 12)
        else:
            self.arrived(*range(self.count - 1))
        for copy in self.copies.values():
            copy.wait_send()
        self.local.wait()


def relayed():
    return lax.axis_size("dp") == 4 and lax.axis_size("ctx") == 2


def gather_sems():
    count = 13 if relayed() else group_size(PLANE) - 1
    return pltpu.SemaphoreType.DMA((count,))


WIDE = 512


def products(source, first, last, dot, target, block_buf, block_sem, out_buf, out_sem):
    def fetch(j, slot):
        columns = pl.ds(pl.multiple_of(j * WIDE, WIDE), WIDE)
        return pltpu.make_async_copy(
            source.at[:, columns], block_buf.at[slot], block_sem.at[slot]
        )

    def store(j, slot):
        return pltpu.make_async_copy(out_buf.at[slot], target(j), out_sem.at[slot])

    fetch(first, first % 2).start()

    @pl.loop(first, last)
    def _(j):
        slot = lax.rem(j, 2)

        @pl.when(j + 1 < last)
        def _():
            fetch(j + 1, 1 - slot).start()

        fetch(j, slot).wait()

        @pl.when(j >= first + 2)
        def _():
            store(j - 2, slot).wait()

        out_buf[slot] = dot(block_buf[slot])
        store(j, slot).start()

    for j in range(max(first, last - 2), last):
        store(j, j % 2).wait()


SMALL_ROWS = 32
GAIN_ROWS = 16


def tail_kernel(
    swaps,
    conv_grad,
    gate_grad,
    convkern,
    convbias,
    stepbias,
    decaylog,
    skipgain,
    ffngain,
    layer_first,
    layer_rows,
    middle_low,
    step_low,
    pre_low,
    select_low,
    scan_in,
    tokens,
    middle_grad,
    gain_row,
    in_conv,
    in_gate,
    one_cols,
    two_cols,
    ct_cols,
    middle_cols,
    ffn_all,
    gated_all,
    tokens_grad,
    layer_out,
    vectors_sum,
    step_sum,
    select_sum,
    gains,
    mix_all,
    grad_inproj,
    grad_outproj,
    grad_gateup,
    grad_downproj,
    mix_own,
    normed_part,
    small,
    small_sum,
    small_slots,
    gain_slots,
    gain_own,
    vectors_own,
    cols,
    in_buf,
    block_buf,
    wide_buf,
    tall_buf,
    cols_sem,
    in_sem,
    block_sem,
    wide_sem,
    tall_sem,
    tp_send,
    tp_recv,
    plane_send,
    plane_recv,
    gather_send,
    gather_recv,
    local_sem,
    *sems,
):
    inner = conv_grad.shape[1]
    hidden = ffn_all.shape[1] // 3
    width = tokens.shape[1]
    rank = step_low.shape[1]
    tp = Group(("tp",), tp_send, tp_recv)
    plane = Group(PLANE, plane_send, plane_recv)
    line = LineSum(normed_part, *sems[:5])
    tokens_spread = LineSpread(tokens_grad, *sems[5:7])
    layer_last = layer_out.at[:, width // 2 :]
    layer_spread = LineSpread(layer_last, *sems[7:9])
    swap_sems = sems[9:]
    gather = PlaneGather(mix_own, mix_all, gather_send, gather_recv)
    sources = (one_cols, two_cols, ct_cols) if swaps else (one_cols, two_cols, ct_cols, middle_cols)
    loads = [
        pltpu.make_async_copy(source, cols.at[at], cols_sem.at[at])
        for at, source in enumerate(sources)
    ]
    if swaps:
        swap = Swap([middle_low], [cols.at[3]], *swap_sems)

    def fetch(j):
        slot = j % 2
        rows = slice(j * WIDE, (j + 1) * WIDE)
        return [
            pltpu.make_async_copy(source.at[rows, :], in_buf.at[slot, at], in_sem.at[slot, at])
            for at, source in enumerate((in_conv, in_gate))
        ]

    for copy in fetch(0) + loads:
        copy.start()
    mix_own[:, :inner] = conv_grad[...]
    mix_own[:, inner:] = gate_grad[...]
    greet([(("tp",), tp.others), (PLANE, plane.others)])
    gather.begin(local_sem)

    small[...] = jnp.zeros_like(small)
    vectors_own[...] = jnp.zeros_like(vectors_own)
    at = 0
    for vector in (convkern, convbias, stepbias, decaylog, skipgain):
        vectors_own[at : at + vector.shape[0], :] = vector[...]
        at += vector.shape[0]
    at = SMALL_ROWS - GAIN_ROWS + 10
    for row in range(width // inner):
        vectors_own[at + row : at + row + 1, :] = ffngain[:, row * inner : (row + 1) * inner]
    hidden_in = tokens[...].astype(jnp.float32)
    unit_rows = hidden_in * inverse_rms(hidden_in)
    blocks = width // WIDE
    firsts = []
    for j in range(blocks):
        if j + 1 < blocks:
            for copy in fetch(j + 1):
                copy.start()
        finish(fetch(j))
        columns = slice(j * WIDE, (j + 1) * WIDE)
        block = matmul_nt(conv_grad[...], in_buf[j % 2, 0]) + matmul_nt(
            gate_grad[...], in_buf[j % 2, 1]
        )
        normed_part[:, columns] = block.astype(normed_part.dtype)
        firsts.append(line.begin(j))
        gain_grad = jnp.sum(block * unit_rows[:, columns], 0, keepdims=True)
        row, at = divmod(j * WIDE, inner)
        row += SMALL_ROWS - GAIN_ROWS + 8
        vectors_own[row : row + 1, at : at + WIDE] = gain_grad
    layer_out[:, : width // 2] = layer_first[...]
    rows_of(layer_last, tp.me, tp.count)[...] = layer_rows[...]
    layer_spread.begin()
    small[:SMALL_ROWS, :] = vectors_own[...].astype(small.dtype)
    small[SMALL_ROWS : SMALL_ROWS + rank, :] = matmul_tn(step_low[...], pre_low[...]).astype(
        small.dtype
    )
    selected = select_sum.shape[0]
    small[SMALL_ROWS + rank : SMALL_ROWS + rank + selected, :] = matmul_tn(
        select_low[...], scan_in[...]
    )[:selected].astype(small.dtype)
    small_sent = plane.scatter(small, small_slots, 0)
    line.pass_all(firsts)

    def flat(at):
        return lambda block: matmul_tn(cols[at], block)

    def tall(at):
        return lambda block: matmul_tn(block, cols[at])

    def side_by_side(ref, first):
        per = ref.shape[2] // WIDE

        def target(j):
            at = j - first
            columns = pl.ds(pl.multiple_of(lax.rem(at, per) * WIDE, WIDE), WIDE)
            return ref.at[lax.div(at, per), :, columns]

        return target

    def one_above_other(ref):
        return lambda j: ref.at[pl.ds(pl.multiple_of(j * WIDE, WIDE), WIDE), :]

    wide = (block_buf, block_sem, wide_buf, wide_sem)
    high = (block_buf, block_sem, tall_buf, tall_sem)
    down_end = hidden // WIDE
    gu_end = 3 * hidden // WIDE
    finish(loads)
    products(ffn_all, 0, down_end, tall(2), one_above_other(grad_downproj), *high)
    gather.relay()
    products(ffn_all, down_end, gu_end, flat(1), side_by_side(grad_gateup, down_end), *wide)
    gather.hand_over()
    finish(small_sent)
    plane.own(small_sum)[...] = plane.total(small, small_slots).astype(small_sum.dtype)
    small_sent = plane.spread(small_sum, 1)
    if swaps:
        swap.begin()
    layer_spread.pass_on()
    hidden_in = tp.own(tokens)[...].astype(jnp.float32)
    tp.own(tokens_grad)[...] = (
        middle_grad[...]
        + norm_back(
            line.total(),
            hidden_in,
            inverse_rms(hidden_in),
            gain_row[...].astype(jnp.float32),
        )
    ).astype(tokens_grad.dtype)
    tokens_spread.begin()
    gather.hand_over_last()
    gather.end()
    products(mix_all, 0, 2 * inner // WIDE, flat(0), side_by_side(grad_inproj, 0), *wide)
    tokens_spread.pass_on()
    finish(small_sent)
    gain_own[...] = small_sum[SMALL_ROWS - GAIN_ROWS : SMALL_ROWS, :].astype(jnp.float32)
    gain_sent = [tp.one(gain_own, gain_slots.at[hop], 0, hop) for hop in range(tp.count - 1)]
    vectors_sum[...] = small_sum[:SMALL_ROWS, :].astype(jnp.float32)
    step_sum[...] = small_sum[SMALL_ROWS : SMALL_ROWS + rank, :].astype(jnp.float32)
    select_sum[...] = small_sum[SMALL_ROWS + rank : SMALL_ROWS + rank + selected, :].astype(
        jnp.float32
    )
    if swaps:
        swap.end()
    products(gated_all, 0, inner // WIDE, tall(3), one_above_other(grad_outproj), *high)
    finish(gain_sent)
    total = gain_own[...]
    for hop in range(tp.count - 1):
        total = total + gain_slots[hop]
    gains[...] = total
    tokens_spread.end()
    layer_spread.end()


def run_tail(
    call_id,
    selected,
    swaps,
    conv_grad,
    gate_grad,
    vectors,
    layer_first,
    layer_rows,
    middle_low,
    step_low,
    pre_low,
    select_low,
    scan_in,
    tokens,
    middle_grad,
    gain_row,
    in_conv,
    in_gate,
    one_cols,
    two_cols,
    ct_cols,
    middle_cols,
    ffn_all,
    gated_all,
):
    rows, inner = conv_grad.shape
    rank = step_low.shape[1]
    hidden = ffn_all.shape[1] // 3
    width = tokens.shape[1]
    share = one_cols.shape[1]
    all_rows = ffn_all.shape[0]
    tp_count, plane_count = group_size(("tp",)), group_size(PLANE)
    low, full = jnp.bfloat16, jnp.float32
    vmem = pl.BlockSpec(memory_space=pltpu.VMEM)
    hbm = pl.BlockSpec(memory_space=pltpu.HBM)
    dma = pltpu.SemaphoreType.DMA
    small_rows = SMALL_ROWS + rank + selected
    small = jax.ShapeDtypeStruct((small_rows + -small_rows % (16 * plane_count), inner), low)
    part = jax.ShapeDtypeStruct((rows, width), low)
    return pl.pallas_call(
        functools.partial(tail_kernel, swaps),
        in_specs=[vmem] * 18 + [hbm] * 8,
        out_specs=[vmem] * 6 + [hbm] * 5,
        out_shape=[
            jax.ShapeDtypeStruct(tokens.shape, low),
            jax.ShapeDtypeStruct(tokens.shape, low),
            jax.ShapeDtypeStruct((SMALL_ROWS, inner), full),
            jax.ShapeDtypeStruct((rank, inner), full),
            jax.ShapeDtypeStruct((selected, inner), full),
            jax.ShapeDtypeStruct((GAIN_ROWS, inner), full),
            jax.ShapeDtypeStruct((all_rows, 2 * inner), low),
            jax.ShapeDtypeStruct((2, share, inner), full),
            jax.ShapeDtypeStruct((inner, share), full),
            jax.ShapeDtypeStruct((2, share, hidden), full),
            jax.ShapeDtypeStruct((hidden, share), full),
        ],
        scratch_shapes=[
            pltpu.VMEM((rows, 2 * inner), low),
            pltpu.VMEM(part.shape, low),
            pltpu.VMEM(small.shape, low),
            pltpu.VMEM(small.shape, low),
            slots_for(small, plane_count),
            pltpu.VMEM((tp_count - 1, GAIN_ROWS, inner), full),
            pltpu.VMEM((GAIN_ROWS, inner), full),
            pltpu.VMEM((SMALL_ROWS, inner), full),
            pltpu.VMEM((4, all_rows, share), low),
            pltpu.VMEM((2, 2, WIDE, inner), low),
            pltpu.VMEM((2, all_rows, WIDE), low),
            pltpu.VMEM((2, share, WIDE), full),
            pltpu.VMEM((2, WIDE, share), full),
            dma((4,)),
            dma((2, 2)),
            dma((2,)),
            dma((2,)),
            dma((2,)),
            dma((1, tp_count - 1)),
            dma((1, tp_count - 1)),
            dma((2, plane_count - 1)),
            dma((2, plane_count - 1)),
        ]
        + gather_scratch()
        + line_sum_scratch(part, width // WIDE)
        + line_spread_scratch() * 2
        + (swap_scratch([tokens]) if swaps else []),
        compiler_params=pltpu.CompilerParams(
            collective_id=call_id, has_side_effects=True, vmem_limit_bytes=VMEM_GRANT
        ),
    )(
        conv_grad,
        gate_grad,
        *vectors,
        layer_first,
        layer_rows,
        middle_low,
        step_low,
        pre_low,
        select_low,
        scan_in,
        tokens,
        middle_grad,
        gain_row,
        in_conv,
        in_gate,
        one_cols,
        two_cols,
        ct_cols,
        middle_cols,
        ffn_all,
        gated_all,
    )


class SplitSwap:
    def __init__(self, array, swapped, plane_send, plane_recv, tp_send, tp_recv, local_sem):
        self.plane, self.tp = Group(PLANE, plane_send, plane_recv), Group(("tp",), tp_send, tp_recv)
        self.array, self.swapped, self.local_sem = array, swapped, local_sem
        rows = array.shape[0] // self.tp.count
        self.rows = pl.ds(pl.multiple_of(self.tp.me * rows, rows), rows)

    def columns(self, index):
        share = self.swapped.shape[2]
        return self.array.at[self.rows, pl.ds(pl.multiple_of(index * share, share), share)]

    def begin(self):
        mine = self.swapped.at[self.plane.me, self.rows, :]
        self.local = pltpu.make_async_copy(
            self.columns(self.plane.me), mine, self.local_sem
        )
        self.local.start()
        self.copies = [
            self.plane.one(self.columns(other), mine, 0, hop)
            for hop, other in enumerate(self.plane.others)
        ]

    def pass_on(self):
        finish(self.copies)
        self.local.wait()
        here = self.swapped.at[:, self.rows, :]
        self.copies = [self.tp.one(here, here, 0, hop) for hop in range(self.tp.count - 1)]

    def end(self):
        finish(self.copies)


def head_kernel(
    swaps,
    tokens,
    gain,
    ct,
    in_conv,
    conv_in,
    conv_all,
    *refs,
):
    if swaps:
        swapped, *refs = refs
    normed, block_buf, block_sem, *sems = refs
    conv = PlaneGather(in_conv, conv_all, *sems[:2])
    if swaps:
        swap = SplitSwap(ct, swapped, *sems[3:])
        greet([(PLANE, conv.others), (("tp",), swap.tp.others)])
    else:
        greet([(PLANE, conv.others)])
    conv.begin(sems[2])
    if swaps:
        swap.begin()
    hidden_in = tokens[...].astype(jnp.float32)
    normed[...] = (hidden_in * inverse_rms(hidden_in) * gain[...].astype(jnp.float32)).astype(
        normed.dtype
    )

    conv.relay()
    conv.hand_over()
    conv.hand_over_last()
    if swaps:
        swap.pass_on()
    conv.end()
    product_in_blocks(normed, conv_all, conv_in, block_buf, block_sem)
    if swaps:
        swap.end()


def run_head(call_id, tokens, gain, ct, shard, swaps):
    rows, width = tokens.shape
    inner = shard.shape[1]
    low = jnp.bfloat16
    vmem = pl.BlockSpec(memory_space=pltpu.VMEM)
    hbm = pl.BlockSpec(memory_space=pltpu.HBM)
    count, tp_count = group_size(PLANE), group_size(("tp",))
    dma = pltpu.SemaphoreType.DMA
    swap_sems = [
        dma((1, count - 1)),
        dma((1, count - 1)),
        dma((1, tp_count - 1)),
        dma((1, tp_count - 1)),
        dma(()),
    ]
    swapped = [jax.ShapeDtypeStruct((count, rows, width // count), low)]
    return pl.pallas_call(
        functools.partial(head_kernel, swaps),
        in_specs=[vmem] * 3 + [hbm],
        out_specs=[vmem] + [hbm] * (2 if swaps else 1),
        out_shape=[
            jax.ShapeDtypeStruct((rows, inner), low),
            jax.ShapeDtypeStruct((width, inner), low),
        ]
        + (swapped if swaps else []),
        scratch_shapes=[
            pltpu.VMEM((rows, width), low),
            pltpu.VMEM((2, width, WIDE), low),
            pltpu.SemaphoreType.DMA((2,)),
        ]
        + gather_scratch()
        + (swap_sems if swaps else []),
        compiler_params=pltpu.CompilerParams(
            collective_id=call_id, has_side_effects=True, vmem_limit_bytes=VMEM_GRANT
        ),
    )(tokens, gain, ct, shard)


def per_device(
    tokens,
    mixgain,
    inproj,
    convkern,
    convbias,
    selproj,
    stepproj,
    stepbias,
    decaylog,
    skipgain,
    outproj,
    ffngain,
    gateup,
    downproj,
    cotangent,
):
    seqs, span, width = tokens.shape
    rows = seqs * span
    taps, inner = convkern.shape
    rank = stepproj.shape[0]
    n_state = decaylog.shape[1]
    tiles = inner // LANE
    gain_mix = mixgain.astype(jnp.float32)
    kernel = convkern.astype(jnp.float32)
    kernel_bias = convbias.astype(jnp.float32)
    step_bias = stepbias.astype(jnp.float32)
    skip_weight = skipgain.astype(jnp.float32)
    decay_rate = -jnp.exp(jnp.transpose(decaylog.astype(jnp.float32)))
    rate = (decay_rate * LOG2E).reshape(n_state, tiles, LANE)

    gain_mix_row, gain_ffn_row = mixgain.reshape(1, width), ffngain.reshape(1, width)
    low = jnp.bfloat16

    tokens_rows = tokens.reshape(rows, width)
    ct_low = cotangent.reshape(rows, width)
    swap_now = swaps_in_kernels(width)
    conv_in, in_conv, *swapped = run_head(
        5, tokens_rows, gain_mix_row, ct_low, inproj[0], swap_now
    )
    ffn_pack, conv_in = lax.optimization_barrier(
        (jnp.concatenate([gateup[0], gateup[1], jnp.transpose(downproj)], 1), conv_in)
    )
    ffn_pack = gathered_rows(ffn_pack)
    ct_cols = swapped[0].reshape(-1, swapped[0].shape[2]) if swapped else swapped_columns(ct_low)
    hidden_in = tokens_rows.astype(jnp.float32)
    scale_one = inverse_rms(hidden_in)
    normed_one = (hidden_in * scale_one * gain_mix).astype(low)

    conv_seqs = conv_in.reshape(seqs, span, inner)
    rim_rows = passed_along(conv_seqs[:, span - (taps - 1) :], "ctx", 1)
    padded_in = jnp.concatenate([rim_rows, conv_seqs], 1).astype(jnp.float32)
    conv_out = kernel_bias[None, None]
    for offset in range(taps):
        conv_out = conv_out + kernel[offset][None, None] * padded_in[:, offset : offset + span]
    conv_out = conv_out.reshape(rows, inner)
    scan_in = jax.nn.silu(conv_out).astype(low)
    scan_float = scan_in.astype(jnp.float32)
    columns = selproj.shape[1]
    select_width = -(-columns // LANE) * LANE
    select_weights = jnp.pad(selproj, ((0, 0), (0, select_width - columns)))
    select_cols, gate_mix, in_gate = run_select(
        0, matmul(scan_in, select_weights), normed_one, inproj[1]
    )
    step_low = select_cols[:, :rank].astype(low)
    b_rows = select_cols[:, rank : rank + n_state].reshape(-1)
    c_rows = select_cols[:, rank + n_state : columns].reshape(-1)
    step_pre = matmul(step_low, stepproj) + step_bias[None]
    step_size = jax.nn.softplus(step_pre)
    in_pairs = lax.axis_size("ctx") == 2
    if in_pairs:
        prior, scan_out, out_all = scan_forward_pair(
            6, step_size, scan_float, b_rows, c_rows, rate, seqs, outproj
        )
    else:
        span_decay = jnp.exp(
            decay_rate[None] * jnp.sum(step_size.reshape(seqs, span, inner), 1)[:, None]
        ).reshape(seqs, n_state, tiles, LANE)
        ends = scan_ends(step_size, scan_float, b_rows, rate, seqs, False)
        start = from_earlier(ends, span_decay, 1)
        prior, scan_out = scan_forward(start, step_size, scan_float, b_rows, c_rows, rate, seqs)
        out_all = gathered_rows(outproj)
    mixer_core = scan_out + skip_weight[None] * scan_float
    gate_sig = jax.nn.silu(gate_mix)
    gated = (mixer_core * gate_sig).astype(low)
    normed_two, middle, gated_all, *swapped = mixer_out(
        1,
        gated,
        out_all,
        tokens_rows,
        gain_ffn_row,
        [normed_one] if swap_now else [],
    )
    (normed_one_cols,) = swapped if swap_now else [swapped_columns(normed_one)]
    made, *swapped = run_ffn(8, normed_two, ct_low, ffn_pack, swap_now)
    (normed_two_cols,) = swapped or [swapped_columns(normed_two)]
    ffn_all = gathered_rows(made)
    middle_low, middle_grad, ffngain_part, gated_grad, ffn_part = ffn_back(
        2, made, ct_low, middle, gain_ffn_row, out_all, ffn_pack
    )
    core_grad = gated_grad * gate_sig
    gate_mix_grad = (gated_grad * mixer_core * silu_slope(gate_mix)).astype(low)
    grad_skipgain = jnp.sum(core_grad * scan_float, 0)
    if in_pairs:
        step_grad, input_grad, rate_grad, parts, *layer_rows = scan_backward_pair(
            7,
            prior,
            step_size,
            scan_float,
            core_grad,
            b_rows,
            c_rows,
            rate,
            seqs,
            ffn_part,
            middle,
            [],
        )
    else:
        back_ends = scan_ends(step_size, core_grad, c_rows, rate, seqs, True)
        end_grad = from_earlier(back_ends, span_decay, -1)
        step_grad, input_grad, rate_grad, parts = scan_backward(
            end_grad, prior, step_size, scan_float, core_grad, b_rows, c_rows, rate, seqs
        )
        ffn_sum = lax.psum_scatter(ffn_part, "tp", scatter_dimension=0, tiled=True)
        layer_rows = jnp.split((middle + ffn_sum.astype(jnp.float32)).astype(low), 2, 1)
    grad_decaylog = rate_grad.reshape(n_state, inner) * decay_rate
    pre_grad = step_grad * jax.nn.sigmoid(step_pre)
    grad_stepbias = jnp.sum(pre_grad, 0)
    pre_low = pre_grad.astype(low)
    select_part = jnp.concatenate(
        [
            matmul_nt(pre_low, stepproj),
            jnp.sum(parts, -1),
            jnp.zeros((rows, select_width - columns), jnp.float32),
        ],
        1,
    ).astype(low)
    select_low, layer_first = sum_over_tp(3, select_part, layer_rows[0])
    scan_in_grad = (
        core_grad * skip_weight[None]
        + input_grad
        + matmul_nt(select_low, select_weights)
    )
    conv_grad = scan_in_grad * silu_slope(conv_out)
    grad_convbias = jnp.sum(conv_grad, 0)
    conv_grad_seqs = conv_grad.reshape(seqs, span, inner)
    padded_grad = jnp.zeros(padded_in.shape, jnp.float32)
    kernel_rows = []
    for offset in range(taps):
        kernel_rows.append(jnp.sum(conv_grad_seqs * padded_in[:, offset : offset + span], (0, 1)))
        padded_grad = padded_grad + jnp.pad(
            kernel[offset][None, None] * conv_grad_seqs,
            ((0, 0), (offset, taps - 1 - offset), (0, 0)),
        )
    grad_convkern = jnp.stack(kernel_rows)
    returned = passed_along(padded_grad[:, : taps - 1], "ctx", -1)
    conv_in_grad = (
        (padded_grad[:, taps - 1 :] + jnp.pad(returned, ((0, 0), (span - taps + 1, 0), (0, 0))))
        .astype(low)
        .reshape(rows, inner)
    )
    vectors = [
        grad_convkern,
        grad_convbias[None],
        grad_stepbias[None],
        grad_decaylog,
        grad_skipgain[None],
        ffngain_part,
    ]
    (
        tokens_grad,
        layer_out,
        vectors,
        grad_stepproj,
        grad_selproj,
        gains,
        _,
        grad_inproj,
        grad_outproj,
        grad_gateup,
        grad_downproj,
    ) = run_tail(
        4,
        columns,
        swap_now,
        conv_in_grad,
        gate_mix_grad,
        vectors,
        layer_first,
        layer_rows[1],
        middle_low,
        step_low,
        pre_low,
        select_low,
        scan_in,
        tokens_rows,
        middle_grad,
        gain_mix_row,
        in_conv,
        in_gate,
        normed_one_cols,
        normed_two_cols,
        ct_cols,
        normed_two_cols if swap_now else swapped_columns(middle_low),
        ffn_all,
        gated_all,
    )
    at = taps + 2
    return (
        layer_out.reshape(tokens.shape),
        tokens_grad.reshape(tokens.shape),
        gains[8:10].reshape(width),
        grad_inproj,
        vectors[:taps],
        vectors[taps],
        jnp.transpose(grad_selproj),
        grad_stepproj,
        vectors[taps + 1],
        jnp.transpose(vectors[at : at + n_state]),
        vectors[at + n_state],
        grad_outproj,
        gains[10:12].reshape(width),
        grad_gateup,
        grad_downproj,
    )


def solution(mesh):
    in_specs = (
        P("dp", "ctx", None),
        P(),
        P(None, ("dp", "ctx"), "tp"),
        P(None, "tp"),
        P("tp"),
        P("tp", None),
        P(None, "tp"),
        P("tp"),
        P("tp", None),
        P("tp"),
        P("tp", ("dp", "ctx")),
        P(),
        P(None, ("dp", "ctx"), "tp"),
        P("tp", ("dp", "ctx")),
        P("dp", "ctx", None),
    )
    out_specs = (
        P("dp", "ctx", None),
        P("dp", "ctx", None),
        P(),
        P(None, ("dp", "ctx"), "tp"),
        P(None, "tp"),
        P("tp"),
        P("tp", None),
        P(None, "tp"),
        P("tp"),
        P("tp", None),
        P("tp"),
        P("tp", ("dp", "ctx")),
        P(),
        P(None, ("dp", "ctx"), "tp"),
        P("tp", ("dp", "ctx")),
    )
    return jax.shard_map(
        per_device, mesh=mesh, in_specs=in_specs, out_specs=out_specs, check_vma=False
    )
```

```python
import functools
import math

import jax
import jax.numpy as jnp
from jax import lax
from jax.experimental import pallas as pl
from jax.experimental.pallas import tpu as pltpu
from jax.sharding import PartitionSpec as P

EPSILON = 1e-05
LOG2E = math.log2(math.e)
LN2 = math.log(2.0)
SUB = 8
LANE = 128
VMEM_GRANT = 60 * 2**20
PLANE = ("dp", "ctx")


def passed_along(value, axis, steps):
    count = lax.axis_size(axis)
    first, last = (max(0, -steps), min(count, count - steps))
    return lax.ppermute(value, axis, [(source, source + steps) for source in range(first, last)])


def matmul(left, right):
    return jnp.dot(left, right, preferred_element_type=jnp.float32)


def matmul_nt(left, right):
    return lax.dot_general(
        left, right, (((1,), (1,)), ((), ())), preferred_element_type=jnp.float32
    )


def matmul_tn(left, right):
    return lax.dot_general(
        left, right, (((0,), (0,)), ((), ())), preferred_element_type=jnp.float32
    )


def inverse_rms(values):
    return lax.rsqrt(jnp.mean(values * values, -1, keepdims=True) + EPSILON)


def silu_slope(values):
    logistic = jax.nn.sigmoid(values)
    return logistic * (1.0 + values * (1.0 - logistic))


def norm_back(grad_norm, values, scale, gain):
    scaled_grad = grad_norm * gain
    unit_rows = values * scale
    return scale * (scaled_grad - unit_rows * jnp.mean(scaled_grad * unit_rows, -1, keepdims=True))


def stage_in(ref, group, held):
    for tile in range(held.shape[0] // SUB):
        held[pl.ds(tile * SUB, SUB), :] = ref[
            pl.ds(pl.multiple_of(group * SUB, SUB), SUB), pl.ds(tile * LANE, LANE)
        ]


def stage_out(held, ref, group):
    for tile in range(held.shape[0] // SUB):
        ref[pl.ds(pl.multiple_of(group * SUB, SUB), SUB), pl.ds(tile * LANE, LANE)] = held[
            pl.ds(tile * SUB, SUB), :
        ]


def token_row(held, at, tiles):
    return held[pl.ds(at, tiles, stride=SUB), :]


def ends_kernel(
    n_state,
    tiles,
    groups,
    reverse,
    step_ref,
    drive_ref,
    rows_ref,
    rate_ref,
    end_ref,
    step_held,
    drive_held,
):
    base = pl.program_id(0) * groups * SUB * n_state
    rates = [rate_ref[n] for n in range(n_state)]

    def one(turn, states):
        group = groups - 1 - turn if reverse else turn
        order = range(SUB - 1, -1, -1) if reverse else range(SUB)
        states = list(states)
        stage_in(step_ref, group, step_held)
        stage_in(drive_ref, group, drive_held)
        for at in order:
            step = token_row(step_held, at, tiles)
            drive = token_row(drive_held, at, tiles)
            if not reverse:
                drive = drive * step
            for n in range(n_state):
                row = rows_ref[base + (group * SUB + at) * n_state + n]
                decay = jnp.exp2(step * rates[n])
                if reverse:
                    states[n] = decay * (states[n] + drive * row)
                else:
                    states[n] = decay * states[n] + drive * row
        return tuple(states)

    zero = jnp.zeros((tiles, LANE), jnp.float32)
    states = lax.fori_loop(0, groups, one, (zero,) * n_state)
    for n in range(n_state):
        end_ref[0, n] = states[n]


def scan_ends(step, drive, rows, rate, seqs, reverse):
    n_state, tiles, _ = rate.shape
    groups = step.shape[0] // seqs // SUB
    rows_spec = pl.BlockSpec((groups * SUB, tiles * LANE), lambda s: (s, 0))
    held = pltpu.VMEM((tiles * SUB, LANE), jnp.float32)
    return pl.pallas_call(
        functools.partial(ends_kernel, n_state, tiles, groups, reverse),
        grid=(seqs,),
        in_specs=[
            rows_spec,
            rows_spec,
            pl.BlockSpec(memory_space=pltpu.SMEM),
            pl.BlockSpec((n_state, tiles, LANE), lambda s: (0, 0, 0)),
        ],
        out_specs=pl.BlockSpec((1, n_state, tiles, LANE), lambda s: (s, 0, 0, 0)),
        out_shape=jax.ShapeDtypeStruct((seqs, n_state, tiles, LANE), jnp.float32),
        scratch_shapes=[held, held],
        compiler_params=pltpu.CompilerParams(vmem_limit_bytes=VMEM_GRANT),
    )(step, drive, rows, rate)


def forward_kernel(
    n_state,
    tiles,
    groups,
    blocks,
    start_ref,
    step_ref,
    input_ref,
    brow_ref,
    crow_ref,
    rate_ref,
    prior_ref,
    mixed_ref,
    carried,
    step_held,
    input_held,
    mixed_held,
):
    base = (pl.program_id(0) * blocks + pl.program_id(1)) * groups * SUB * n_state

    @pl.when(pl.program_id(1) == 0)
    def _():
        carried[...] = start_ref[0]

    def one(group, states):
        states = list(states)
        stage_in(step_ref, group, step_held)
        stage_in(input_ref, group, input_held)
        for at in range(SUB):
            step = token_row(step_held, at, tiles)
            drive = step * token_row(input_held, at, tiles)
            mixed = [None] * 2
            for n in range(n_state):
                where = base + (group * SUB + at) * n_state + n
                prior_ref[group * SUB + at, n] = states[n]
                decay = jnp.exp2(step * rate_ref[n])
                states[n] = decay * states[n] + drive * brow_ref[where]
                term = states[n] * crow_ref[where]
                mixed[n % 2] = term if mixed[n % 2] is None else mixed[n % 2] + term
            mixed_held[pl.ds(at, tiles, stride=SUB), :] = mixed[0] + mixed[1]
        stage_out(mixed_held, mixed_ref, group)
        return tuple(states)

    states = lax.fori_loop(0, groups, one, tuple(carried[n] for n in range(n_state)))
    for n in range(n_state):
        carried[n] = states[n]


def scan_forward(start, step, inputs, b_rows, c_rows, rate, seqs):
    n_state, tiles, _ = rate.shape
    all_groups = step.shape[0] // SUB
    groups = math.gcd(all_groups // seqs, 4)
    blocks = all_groups // seqs // groups
    rows_spec = pl.BlockSpec((groups * SUB, tiles * LANE), lambda s, b: (s * blocks + b, 0))
    held = pltpu.VMEM((tiles * SUB, LANE), jnp.float32)
    smem = pl.BlockSpec(memory_space=pltpu.SMEM)
    tokens = all_groups * SUB
    return pl.pallas_call(
        functools.partial(forward_kernel, n_state, tiles, groups, blocks),
        grid=(seqs, blocks),
        in_specs=[
            pl.BlockSpec((1, n_state, tiles, LANE), lambda s, b: (s, 0, 0, 0)),
            rows_spec,
            rows_spec,
            smem,
            smem,
            pl.BlockSpec((n_state, tiles, LANE), lambda s, b: (0, 0, 0)),
        ],
        out_specs=[
            pl.BlockSpec(
                (groups * SUB, n_state, tiles, LANE), lambda s, b: (s * blocks + b, 0, 0, 0)
            ),
            rows_spec,
        ],
        out_shape=[
            jax.ShapeDtypeStruct((tokens, n_state, tiles, LANE), jnp.float32),
            jax.ShapeDtypeStruct(step.shape, jnp.float32),
        ],
        scratch_shapes=[pltpu.VMEM((n_state, tiles, LANE), jnp.float32)] + [held] * 3,
        compiler_params=pltpu.CompilerParams(vmem_limit_bytes=VMEM_GRANT),
    )(start, step, inputs, b_rows, c_rows, rate)


def backward_kernel(
    n_state,
    tiles,
    groups,
    blocks,
    end_ref,
    prior_ref,
    step_ref,
    input_ref,
    ograd_ref,
    brow_ref,
    crow_ref,
    rate_ref,
    picks_ref,
    step_grad_ref,
    input_grad_ref,
    rate_grad_ref,
    part_ref,
    carried,
    step_held,
    input_held,
    ograd_held,
    step_grad_held,
    input_grad_held,
):
    block = blocks - 1 - pl.program_id(1)
    base = (pl.program_id(0) * blocks + block) * groups * SUB * n_state

    @pl.when(pl.program_id(1) == 0)
    def _():
        carried[...] = end_ref[0]

    @pl.when((pl.program_id(0) == 0) & (pl.program_id(1) == 0))
    def _():
        rate_grad_ref[...] = jnp.zeros_like(rate_grad_ref)

    def one(turn, grads):
        group = groups - 1 - turn
        grads = list(grads)
        stage_in(step_ref, group, step_held)
        stage_in(input_ref, group, input_held)
        stage_in(ograd_ref, group, ograd_held)
        for at in range(SUB - 1, -1, -1):
            step = token_row(step_held, at, tiles)
            value = token_row(input_held, at, tiles)
            ograd = token_row(ograd_held, at, tiles)
            drive = step * value
            along_b = None
            along_rate = None
            brow_parts, crow_parts = [], []
            for n in range(n_state):
                where = base + (group * SUB + at) * n_state + n
                brow, crow = brow_ref[where], crow_ref[where]
                rate = rate_ref[n]
                decay = jnp.exp2(step * rate)
                grad = ograd * crow + grads[n]
                kept = decay * prior_ref[group * SUB + at, n]
                state = kept + drive * brow
                decay_term = grad * kept
                grads[n] = decay * grad
                rate_grad_ref[n] += decay_term * step
                by_rate, by_brow = decay_term * rate, grad * brow
                along_rate = by_rate if along_rate is None else along_rate + by_rate
                along_b = by_brow if along_b is None else along_b + by_brow
                brow_parts.append(grad * drive)
                crow_parts.append(ograd * state)
            step_grad_held[pl.ds(at, tiles, stride=SUB), :] = along_rate * LN2 + along_b * value
            input_grad_held[pl.ds(at, tiles, stride=SUB), :] = along_b * step
            parts = jnp.concatenate(brow_parts + crow_parts, 0).astype(jnp.bfloat16)
            part_ref[group * SUB + at] = jnp.dot(
                picks_ref[...], parts, preferred_element_type=jnp.float32
            )
        stage_out(step_grad_held, step_grad_ref, group)
        stage_out(input_grad_held, input_grad_ref, group)
        return tuple(grads)

    grads = lax.fori_loop(0, groups, one, tuple(carried[n] for n in range(n_state)))
    for n in range(n_state):
        carried[n] = grads[n]


def scan_backward(end_grad, prior, step, inputs, ograd, b_rows, c_rows, rate, seqs):
    n_state, tiles, _ = rate.shape
    all_groups = step.shape[0] // SUB
    groups = math.gcd(all_groups // seqs, 4)
    blocks = all_groups // seqs // groups

    def at(s, b):
        return s * blocks + blocks - 1 - b

    rows_spec = pl.BlockSpec((groups * SUB, tiles * LANE), lambda s, b: (at(s, b), 0))
    held = pltpu.VMEM((tiles * SUB, LANE), jnp.float32)
    smem = pl.BlockSpec(memory_space=pltpu.SMEM)
    tokens = all_groups * SUB
    picks = jnp.repeat(jnp.eye(2 * n_state, dtype=jnp.bfloat16), tiles, 1)
    return pl.pallas_call(
        functools.partial(backward_kernel, n_state, tiles, groups, blocks),
        grid=(seqs, blocks),
        in_specs=[
            pl.BlockSpec((1, n_state, tiles, LANE), lambda s, b: (s, 0, 0, 0)),
            pl.BlockSpec((groups * SUB, n_state, tiles, LANE), lambda s, b: (at(s, b), 0, 0, 0)),
            rows_spec,
            rows_spec,
            rows_spec,
            smem,
            smem,
            pl.BlockSpec((n_state, tiles, LANE), lambda s, b: (0, 0, 0)),
            pl.BlockSpec(picks.shape, lambda s, b: (0, 0)),
        ],
        out_specs=[
            rows_spec,
            rows_spec,
            pl.BlockSpec((n_state, tiles, LANE), lambda s, b: (0, 0, 0)),
            pl.BlockSpec((groups * SUB, 2 * n_state, LANE), lambda s, b: (at(s, b), 0, 0)),
        ],
        out_shape=[
            jax.ShapeDtypeStruct(step.shape, jnp.float32),
            jax.ShapeDtypeStruct(step.shape, jnp.float32),
            jax.ShapeDtypeStruct(rate.shape, jnp.float32),
            jax.ShapeDtypeStruct((tokens, 2 * n_state, LANE), jnp.float32),
        ],
        scratch_shapes=[pltpu.VMEM((n_state, tiles, LANE), jnp.float32)] + [held] * 5,
        compiler_params=pltpu.CompilerParams(vmem_limit_bytes=VMEM_GRANT),
    )(end_grad, prior, step, inputs, ograd, b_rows, c_rows, rate, picks)


def from_earlier(ends, decay, steps):
    count = lax.axis_size("ctx")
    if count == 1:
        return jnp.zeros_like(ends)
    if count == 2:
        return passed_along(ends, "ctx", steps)
    index = lax.axis_index("ctx")
    all_ends = lax.all_gather(ends, "ctx")
    all_decays = lax.all_gather(decay, "ctx")

    def one(turn, state):
        at = turn if steps > 0 else count - 1 - turn
        reached = at < index if steps > 0 else at > index
        return jnp.where(reached, all_decays[at] * state + all_ends[at], state)

    return lax.fori_loop(0, count, one, jnp.zeros_like(ends))


def gathered_rows(rows):
    return lax.all_gather(rows, PLANE, axis=0, tiled=True)


def swapped_columns(rows):
    return lax.all_to_all(rows, PLANE, split_axis=1, concat_axis=0, tiled=True)


def place_in(axes):
    index = 0
    for axis in axes:
        index = index * lax.axis_size(axis) + lax.axis_index(axis)
    return index


def device_at(axes, index):
    where = {}
    for axis in reversed(axes):
        size = lax.axis_size(axis)
        where[axis] = lax.rem(index, size)
        index = lax.div(index, size)
    return where


def greet(groups):
    barrier = pltpu.get_barrier_semaphore()
    total = 0
    for axes, others in groups:
        for other in others:
            pl.semaphore_signal(
                barrier,
                inc=1,
                device_id=device_at(axes, other),
                device_id_type=pl.DeviceIdType.MESH,
            )
            total += 1
    pl.semaphore_wait(barrier, total)


def sent(source, target, send_sem, recv_sem, where):
    copy = pltpu.make_async_remote_copy(
        src_ref=source,
        dst_ref=target,
        send_sem=send_sem,
        recv_sem=recv_sem,
        device_id=where,
        device_id_type=pl.DeviceIdType.MESH,
    )
    copy.start()
    return copy


def finish(copies):
    for copy in copies:
        copy.wait()


def rows_of(ref, index, count):
    rows = ref.shape[0] // count
    return ref.at[pl.ds(pl.multiple_of(index * rows, rows), rows), :]


class Group:
    def __init__(self, axes, send_sem, recv_sem):
        self.axes = axes
        self.count = math.prod(lax.axis_size(axis) for axis in axes)
        self.me = place_in(axes)
        self.others = [lax.rem(self.me + hop, self.count) for hop in range(1, self.count)]
        self.send_sem, self.recv_sem = send_sem, recv_sem

    def own(self, ref):
        return rows_of(ref, self.me, self.count)

    def one(self, source, target, which, hop):
        return sent(
            source,
            target,
            self.send_sem.at[which, hop],
            self.recv_sem.at[which, hop],
            device_at(self.axes, self.others[hop]),
        )

    def scatter(self, part, slot, which):
        return [
            self.one(rows_of(part, other, self.count), slot.at[hop], which, hop)
            for hop, other in enumerate(self.others)
        ]

    def total(self, part, slot):
        total = self.own(part)[...].astype(jnp.float32)
        for hop in range(self.count - 1):
            total = total + slot[hop].astype(jnp.float32)
        return total

    def spread(self, ref, which):
        return [self.one(self.own(ref), self.own(ref), which, hop) for hop in range(self.count - 1)]


def slots_for(part, count):
    return pltpu.VMEM((count - 1, part.shape[0] // count) + part.shape[1:], part.dtype)


def group_size(axes):
    return math.prod(lax.axis_size(axis) for axis in axes)


def line_of_four():
    me = lax.axis_index("tp")
    near = me + 1 - 2 * lax.rem(me, 2)
    return me, near, lax.rem(me + 2, 4), lax.rem(near + 2, 4)


class LineSum:
    def __init__(self, part, near_slots, far_slot, passed, send_sem, recv_sem):
        self.part, self.near_slots, self.far_slot = part, near_slots, far_slot
        self.passed, self.send_sem, self.recv_sem = passed, send_sem, recv_sem
        self.me, self.near, self.far, self.cross = line_of_four()
        self.blocks = send_sem.shape[1]
        self.copies = []

    def columns(self, j):
        wide = self.part.shape[1] // self.blocks
        return slice(j * wide, (j + 1) * wide)

    def rows(self, index):
        return rows_of(self.part, index, 4)

    def send(self, source, target, which, j, where):
        copy = sent(
            source.at[:, self.columns(j)],
            target.at[:, self.columns(j)],
            self.send_sem.at[which, j],
            self.recv_sem.at[which, j],
            {"tp": where},
        )
        self.copies.append((which, copy))
        return copy

    def begin(self, j):
        first = self.send(self.rows(self.cross), self.near_slots.at[0], 0, j, self.near)
        self.send(self.rows(self.near), self.near_slots.at[1], 1, j, self.near)
        return first

    def pass_on(self, j, first):
        first.wait_recv()
        columns = self.columns(j)
        self.passed[:, columns] = (
            self.rows(self.far)[:, columns].astype(jnp.float32)
            + self.near_slots[0, :, columns].astype(jnp.float32)
        ).astype(self.passed.dtype)
        self.send(self.passed, self.far_slot, 2, j, self.far)

    def total(self):
        for which, copy in self.copies:
            copy.wait_send()
            if which:
                copy.wait_recv()
        return (
            self.rows(self.me)[...].astype(jnp.float32)
            + self.near_slots[1].astype(jnp.float32)
            + self.far_slot[...].astype(jnp.float32)
        )

    def pass_all(self, firsts):
        for j, first in enumerate(firsts):
            self.pass_on(j, first)


def line_sum_scratch(part, blocks):
    share = (part.shape[0] // 4,) + part.shape[1:]
    sems = pltpu.SemaphoreType.DMA((3, blocks))
    return [
        pltpu.VMEM((2,) + share, part.dtype),
        pltpu.VMEM(share, part.dtype),
        pltpu.VMEM(share, part.dtype),
        sems,
        sems,
    ]


class LineSpread:
    def __init__(self, ref, send_sem, recv_sem):
        self.ref, self.send_sem, self.recv_sem = ref, send_sem, recv_sem
        self.me, self.near, self.far, self.cross = line_of_four()

    def send(self, owner, half, which, where):
        rows = rows_of(self.ref, owner, 4)
        if half is not None:
            wide = self.ref.shape[1] // 2
            rows = rows.at[:, half * wide : (half + 1) * wide]
        return sent(rows, rows, self.send_sem.at[which], self.recv_sem.at[which], {"tp": where})

    def begin(self):
        self.across = [self.send(self.me, half, half, self.far) for half in range(2)]
        self.within = [self.send(self.me, None, 2, self.near)]

    def pass_on(self):
        for half, copy in enumerate(self.across):
            copy.wait_recv()
            self.within.append(self.send(self.far, half, 3 + half, self.near))

    def end(self):
        for copy in self.across:
            copy.wait_send()
        finish(self.within)

    def run(self):
        self.begin()
        self.pass_on()
        self.end()


def line_spread_scratch():
    return [pltpu.SemaphoreType.DMA((5,)), pltpu.SemaphoreType.DMA((5,))]


class Swap:
    def __init__(self, arrays, swapped, send_sem, recv_sem, local_sem):
        plane = Group(PLANE, send_sem, recv_sem)
        self.plane, self.arrays, self.swapped, self.local_sem = plane, arrays, swapped, local_sem

    def begin(self):
        self.copies, plane = [], self.plane
        for which, (array, swapped) in enumerate(zip(self.arrays, self.swapped)):
            share = swapped.shape[1]

            def columns(index):
                return array.at[:, pl.ds(pl.multiple_of(index * share, share), share)]

            for hop, other in enumerate(plane.others):
                self.copies.append(plane.one(columns(other), plane.own(swapped), which, hop))
            local = pltpu.make_async_copy(
                columns(plane.me), plane.own(swapped), self.local_sem.at[which]
            )
            local.start()
            self.copies.append(local)

    def end(self):
        finish(self.copies)


class SplitSwap:
    def __init__(self, array, swapped, plane_send, plane_recv, tp_send, tp_recv, local_sem):
        self.plane, self.tp = Group(PLANE, plane_send, plane_recv), Group(("tp",), tp_send, tp_recv)
        self.array, self.swapped, self.local_sem = array, swapped, local_sem
        rows = array.shape[0] // self.tp.count
        self.rows = pl.ds(pl.multiple_of(self.tp.me * rows, rows), rows)

    def columns(self, index):
        share = self.swapped.shape[2]
        return self.array.at[self.rows, pl.ds(pl.multiple_of(index * share, share), share)]

    def begin(self):
        mine = self.swapped.at[self.plane.me, self.rows, :]
        self.local = pltpu.make_async_copy(
            self.columns(self.plane.me), mine, self.local_sem
        )
        self.local.start()
        self.copies = [
            self.plane.one(self.columns(other), mine, 0, hop)
            for hop, other in enumerate(self.plane.others)
        ]

    def pass_on(self):
        finish(self.copies)
        self.local.wait()
        here = self.swapped.at[:, self.rows, :]
        self.copies = [self.tp.one(here, here, 0, hop) for hop in range(self.tp.count - 1)]

    def end(self):
        finish(self.copies)


def split_scratch(arrays):
    dma = pltpu.SemaphoreType.DMA
    count, tp_count = group_size(PLANE), group_size(("tp",))
    sems = [dma((1, count - 1))] * 2 + [dma((1, tp_count - 1))] * 2 + [dma(())]
    return sems if arrays else []


def split_shapes(arrays):
    count = group_size(PLANE)
    return [
        jax.ShapeDtypeStruct(
            (count, array.shape[0], array.shape[1] // count), array.dtype
        )
        for array in arrays
    ]


def swap_scratch(arrays):
    sems = pltpu.SemaphoreType.DMA((len(arrays), group_size(PLANE) - 1))
    return [sems, sems, pltpu.SemaphoreType.DMA((len(arrays),))] if arrays else []


def swap_shapes(arrays):
    count = group_size(PLANE)
    return [
        jax.ShapeDtypeStruct((array.shape[0] * count, array.shape[1] // count), array.dtype)
        for array in arrays
    ]


def swaps_in_kernels(width):
    return width // group_size(PLANE) % LANE == 0


def gathered_shape(shard):
    return jax.ShapeDtypeStruct(
        (shard.shape[0] * group_size(PLANE),) + shard.shape[1:], shard.dtype
    )


def gather_scratch():
    return [gather_sems(), gather_sems(), pltpu.SemaphoreType.DMA(())]


def product_in_blocks(left, source, target, block_buf, block_sem):
    columns = range(0, source.shape[1], WIDE)

    def fetch(turn):
        at = columns[turn]
        return pltpu.make_async_copy(
            source.at[:, at : at + WIDE], block_buf.at[turn % 2], block_sem.at[turn % 2]
        )

    fetch(0).start()
    for turn, at in enumerate(columns):
        if turn + 1 < len(columns):
            fetch(turn + 1).start()
        fetch(turn).wait()
        target[:, at : at + WIDE] = matmul(left[...], block_buf[turn % 2]).astype(target.dtype)


def select_kernel(n_swaps, part, normed, shard, *refs):
    arrays, refs = refs[:n_swaps], refs[n_swaps:]
    total, product, gathered, *refs = refs
    swapped, refs = refs[:n_swaps], refs[n_swaps:]
    slots, send_sem, recv_sem, block_buf, block_sem, *refs = refs
    gather_send, gather_recv, local_sem, *swap_sems = refs
    group = Group(("tp",), send_sem, recv_sem)
    gather = PlaneGather(shard, gathered, gather_send, gather_recv)
    greet([(("tp",), group.others), (PLANE, gather.others)])
    gather.begin(local_sem)
    if n_swaps:
        swap = SplitSwap(arrays[0], swapped[0], *swap_sems)
        swap.begin()
    finish(group.scatter(part, slots, 0))
    group.own(total)[...] = group.total(part, slots).astype(total.dtype)
    copies = group.spread(total, 1)
    gather.relay()
    gather.hand_over()
    finish(copies)
    if n_swaps:
        swap.pass_on()
    gather.hand_over_last()
    gather.end()
    product_in_blocks(normed, gathered, product, block_buf, block_sem)
    if n_swaps:
        swap.end()


def run_select(call_id, part, normed, shard, arrays):
    count = group_size(("tp",))
    vmem = pl.BlockSpec(memory_space=pltpu.VMEM)
    hbm = pl.BlockSpec(memory_space=pltpu.HBM)
    sems = pltpu.SemaphoreType.DMA((2, count - 1))
    rows, width = normed.shape
    return pl.pallas_call(
        functools.partial(select_kernel, len(arrays)),
        in_specs=[vmem, vmem, hbm] + [vmem] * len(arrays),
        out_specs=[vmem, vmem, hbm] + [hbm] * len(arrays),
        out_shape=[
            jax.ShapeDtypeStruct(part.shape, part.dtype),
            jax.ShapeDtypeStruct((rows, shard.shape[1]), jnp.float32),
            gathered_shape(shard),
        ]
        + split_shapes(arrays),
        scratch_shapes=[
            slots_for(part, count),
            sems,
            sems,
            pltpu.VMEM((2, width, WIDE), jnp.bfloat16),
            pltpu.SemaphoreType.DMA((2,)),
        ]
        + gather_scratch()
        + split_scratch(arrays),
        compiler_params=pltpu.CompilerParams(
            collective_id=call_id, has_side_effects=True, vmem_limit_bytes=VMEM_GRANT
        ),
    )(part, normed, shard, *arrays)


def sum_kernel(part, own_rows, total, all_rows, slots, send_sem, recv_sem, *line_sems):
    group = Group(("tp",), send_sem, recv_sem)
    rows = LineSpread(all_rows, *line_sems)
    greet([(("tp",), group.others)])
    copies = group.scatter(part, slots, 0)
    group.own(all_rows)[...] = own_rows[...]
    rows.begin()
    finish(copies)
    group.own(total)[...] = group.total(part, slots).astype(total.dtype)
    copies = group.spread(total, 1)
    rows.pass_on()
    finish(copies)
    rows.end()


def sum_over_tp(call_id, part, own_rows):
    count = group_size(("tp",))
    vmem = pl.BlockSpec(memory_space=pltpu.VMEM)
    sems = pltpu.SemaphoreType.DMA((2, count - 1))
    return pl.pallas_call(
        sum_kernel,
        in_specs=[vmem] * 2,
        out_specs=[vmem] * 2,
        out_shape=[
            jax.ShapeDtypeStruct(part.shape, part.dtype),
            jax.ShapeDtypeStruct((own_rows.shape[0] * count, own_rows.shape[1]), own_rows.dtype),
        ],
        scratch_shapes=[slots_for(part, count), sems, sems] + line_spread_scratch(),
        compiler_params=pltpu.CompilerParams(
            collective_id=call_id, has_side_effects=True, vmem_limit_bytes=VMEM_GRANT
        ),
    )(part, own_rows)


def mixer_out_kernel(gated, out_all, tokens, gain, normed, middle, part, *sems):
    line = LineSum(part, *sems[:5])
    spread = LineSpread(normed, *sems[5:])
    group = Group(("tp",), None, None)
    inner = gated.shape[1]
    share = out_all.shape[1]
    greet([(("tp",), group.others)])
    for at in range(out_all.shape[0] // inner):
        part[:, at * share : (at + 1) * share] = matmul(
            gated[...], out_all[at * inner : (at + 1) * inner, :]
        ).astype(part.dtype)
    line.pass_all([line.begin(j) for j in range(line.blocks)])
    rows = group.own(tokens)[...].astype(jnp.float32) + line.total()
    middle[...] = rows
    group.own(normed)[...] = (rows * inverse_rms(rows) * gain[...].astype(jnp.float32)).astype(
        normed.dtype
    )
    spread.begin()
    spread.pass_on()
    spread.end()


def mixer_out(call_id, gated, out_all, tokens, gain):
    count = group_size(("tp",))
    vmem = pl.BlockSpec(memory_space=pltpu.VMEM)
    rows, width = tokens.shape
    part = jax.ShapeDtypeStruct((rows, width), jnp.bfloat16)
    return pl.pallas_call(
        mixer_out_kernel,
        in_specs=[vmem] * 4,
        out_specs=[vmem] * 2,
        out_shape=[part, jax.ShapeDtypeStruct((rows // count, width), jnp.float32)],
        scratch_shapes=[pltpu.VMEM(part.shape, part.dtype)]
        + line_sum_scratch(part, 2)
        + line_spread_scratch(),
        compiler_params=pltpu.CompilerParams(
            collective_id=call_id, has_side_effects=True, vmem_limit_bytes=VMEM_GRANT
        ),
    )(gated, out_all, tokens, gain)


def ffn_kernel(
    normed,
    ct,
    weights,
    shard,
    made,
    gathered,
    block_buf,
    block_sem,
    gather_send,
    gather_recv,
    local_sem,
):
    hidden = weights.shape[1] // 3
    blocks = hidden // WIDE
    gather = PlaneGather(shard, gathered, gather_send, gather_recv)

    def columns(j, which):
        return pl.ds(pl.multiple_of(which * hidden + j * WIDE, WIDE), WIDE)

    def fetch(j, which):
        slot = lax.rem(j, 2)
        return pltpu.make_async_copy(
            weights.at[:, columns(j, which)],
            block_buf.at[slot, which],
            block_sem.at[slot, which],
        )

    for which in range(3):
        fetch(0, which).start()
    greet([(PLANE, gather.others)])
    gather.begin(local_sem)

    def one_block(j):
        slot = lax.rem(j, 2)

        @pl.when(j + 1 < blocks)
        def _():
            for which in range(3):
                fetch(j + 1, which).start()

        fetch(j, 0).wait()
        gate = matmul(normed[...], block_buf[slot, 0])
        fetch(j, 1).wait()
        up = matmul(normed[...], block_buf[slot, 1])
        fetch(j, 2).wait()
        act_grad = matmul(ct[...], block_buf[slot, 2])
        logistic = jax.nn.sigmoid(gate)
        silu = gate * logistic
        slope = logistic * (1.0 + gate * (1.0 - logistic))
        made[:, columns(j, 0)] = (silu * up).astype(made.dtype)
        made[:, columns(j, 1)] = (act_grad * up * slope).astype(made.dtype)
        made[:, columns(j, 2)] = (act_grad * silu).astype(made.dtype)

    pl.loop(0, blocks // 2)(one_block)
    gather.relay()
    gather.hand_over()
    pl.loop(blocks // 2, blocks)(one_block)
    gather.hand_over_last()
    gather.end()


def run_ffn(call_id, normed, ct, weights, shard):
    rows, width = normed.shape
    vmem = pl.BlockSpec(memory_space=pltpu.VMEM)
    hbm = pl.BlockSpec(memory_space=pltpu.HBM)
    return pl.pallas_call(
        ffn_kernel,
        in_specs=[vmem, vmem, hbm, hbm],
        out_specs=[vmem, hbm],
        out_shape=[
            jax.ShapeDtypeStruct((rows, weights.shape[1]), jnp.bfloat16),
            gathered_shape(shard),
        ],
        scratch_shapes=[
            pltpu.VMEM((2, 3, width, WIDE), jnp.bfloat16),
            pltpu.SemaphoreType.DMA((2, 3)),
        ]
        + gather_scratch(),
        compiler_params=pltpu.CompilerParams(
            collective_id=call_id, has_side_effects=True, vmem_limit_bytes=VMEM_GRANT
        ),
    )(normed, ct, weights, shard)


def ffn_back_kernel(
    n_swaps,
    made,
    ct,
    middle,
    gain,
    out_all,
    weights,
    *refs,
):
    arrays, refs = refs[:n_swaps], refs[n_swaps:]
    middle_low, middle_grad, gain_grad, gated_grad, ffn_part, *refs = refs
    swapped, refs = refs[:n_swaps], refs[n_swaps:]
    part, wide_buf, down_buf, wide_sem, down_sem, *sems = refs
    hidden = made.shape[1] // 3
    blocks = part.shape[1] // WIDE
    group = Group(("tp",), None, None)
    line = LineSum(part, *sems[:5])
    spread = LineSpread(middle_low, *sems[5:7])
    if n_swaps:
        swap = Swap(arrays, swapped, *sems[7:])
        greet([(("tp",), group.others), (PLANE, swap.plane.others)])
        swap.begin()
    else:
        greet([(("tp",), group.others)])

    def fetch(j):
        return pltpu.make_async_copy(
            weights.at[j * WIDE : (j + 1) * WIDE, : 2 * hidden],
            wide_buf.at[j % 2],
            wide_sem.at[j % 2],
        )

    def fetch_down(j):
        return pltpu.make_async_copy(
            weights.at[j * WIDE : (j + 1) * WIDE, 2 * hidden :],
            down_buf.at[j % 2],
            down_sem.at[j % 2],
        )

    fetch(0).start()
    firsts = []
    for j in range(blocks):
        if j + 1 < blocks:
            fetch(j + 1).start()
        else:
            fetch_down(0).start()
        fetch(j).wait()
        columns = slice(j * WIDE, (j + 1) * WIDE)
        part[:, columns] = matmul_nt(made[:, hidden:], wide_buf[j % 2]).astype(part.dtype)
        firsts.append(line.begin(j))
    for j in range(blocks):
        if j + 1 < blocks:
            fetch_down(j + 1).start()
        fetch_down(j).wait()
        ffn_part[:, j * WIDE : (j + 1) * WIDE] = matmul_nt(
            made[:, :hidden], down_buf[j % 2]
        ).astype(ffn_part.dtype)
        line.pass_on(j, firsts[j])
    normed_grad = line.total()
    rows = middle[...]
    scale = inverse_rms(rows)
    gain_grad[...] = jnp.sum(normed_grad * rows * scale, 0, keepdims=True)
    grad = group.own(ct)[...].astype(jnp.float32) + norm_back(
        normed_grad, rows, scale, gain[...].astype(jnp.float32)
    )
    middle_grad[...] = grad
    group.own(middle_low)[...] = grad.astype(middle_low.dtype)
    spread.run()
    inner = gated_grad.shape[1]
    share = out_all.shape[1]
    total = None
    for at in range(out_all.shape[0] // inner):
        one = matmul_nt(
            middle_low[:, at * share : (at + 1) * share], out_all[at * inner : (at + 1) * inner, :]
        )
        total = one if total is None else total + one
    gated_grad[...] = total
    if n_swaps:
        swap.end()


def ffn_back(call_id, made, ct, middle, gain, out_all, weights, arrays):
    count = group_size(("tp",))
    vmem = pl.BlockSpec(memory_space=pltpu.VMEM)
    hbm = pl.BlockSpec(memory_space=pltpu.HBM)
    rows, width = ct.shape
    hidden = made.shape[1] // 3
    inner = out_all.shape[0] // group_size(PLANE)
    low, full = jnp.bfloat16, jnp.float32
    part = jax.ShapeDtypeStruct((rows, width), low)
    dma = pltpu.SemaphoreType.DMA
    return pl.pallas_call(
        functools.partial(ffn_back_kernel, len(arrays)),
        in_specs=[vmem] * 5 + [hbm] + [vmem] * len(arrays),
        out_specs=[vmem] * 5 + [hbm] * len(arrays),
        out_shape=[
            part,
            jax.ShapeDtypeStruct((rows // count, width), full),
            jax.ShapeDtypeStruct((1, width), full),
            jax.ShapeDtypeStruct((rows, inner), full),
            part,
        ]
        + swap_shapes(arrays),
        scratch_shapes=[
            pltpu.VMEM(part.shape, low),
            pltpu.VMEM((2, WIDE, 2 * hidden), low),
            pltpu.VMEM((2, WIDE, hidden), low),
            dma((2,)),
            dma((2,)),
        ]
        + line_sum_scratch(part, width // WIDE)
        + line_spread_scratch()
        + swap_scratch(arrays),
        compiler_params=pltpu.CompilerParams(
            collective_id=call_id, has_side_effects=True, vmem_limit_bytes=VMEM_GRANT
        ),
    )(made, ct, middle, gain, out_all, weights, *arrays)


def send_on(source, target, send_sem, recv_sem, ctx):
    return pltpu.make_async_remote_copy(
        src_ref=source,
        dst_ref=target,
        send_sem=send_sem,
        recv_sem=recv_sem,
        device_id={"ctx": ctx},
        device_id_type=pl.DeviceIdType.MESH,
    )


def forward_pair_kernel(
    n_swaps,
    n_state,
    tiles,
    groups,
    blocks,
    seqs,
    step_ref,
    input_ref,
    brow_ref,
    crow_ref,
    rate_ref,
    shard,
    *refs,
):
    arrays, refs = refs[:n_swaps], refs[n_swaps:]
    prior_ref, mixed_ref, gathered, *refs = refs
    swapped, refs = refs[:n_swaps], refs[n_swaps:]
    carried, ends, starts, prior_buf, step_held, input_held, mixed_held, *refs = refs
    prior_sem, send_sem, recv_sem, gather_send, gather_recv, local_sem, *swap_sems = refs
    place = lax.axis_index("ctx")
    gather = PlaneGather(shard, gathered, gather_send, gather_recv)
    if n_swaps:
        swap = SplitSwap(arrays[0], swapped[0], *swap_sems)
        greet([(PLANE, gather.others), (("tp",), swap.tp.others)])
        gather.begin(local_sem)
        swap.begin()
    else:
        greet([(PLANE, gather.others)])
        gather.begin(local_sem)

    def hand_on(seq):
        return send_on(ends.at[seq], starts.at[seq], send_sem.at[seq], recv_sem.at[seq], 1)

    def store(block):
        slot = lax.rem(block, 2)
        rows = groups * SUB
        return pltpu.make_async_copy(
            prior_buf.at[slot],
            prior_ref.at[pl.ds(pl.multiple_of(block * rows, rows), rows)],
            prior_sem.at[slot],
        )

    def one_sequence(seq):
        @pl.when(place == 0)
        def _():
            carried[...] = jnp.zeros_like(carried)

        @pl.when(place == 1)
        def _():
            hand_on(seq).wait_recv()
            carried[...] = starts[seq]

        @pl.loop(0, blocks)
        def _(inner_block):
            block = seq * blocks + inner_block
            slot = lax.rem(block, 2)

            @pl.when(block >= 2)
            def _():
                store(block - 2).wait()

            def one(turn, states):
                group = block * groups + turn
                states = list(states)
                stage_in(step_ref, group, step_held)
                stage_in(input_ref, group, input_held)
                for at in range(SUB):
                    step = token_row(step_held, at, tiles)
                    drive = step * token_row(input_held, at, tiles)
                    mixed = [None] * 2
                    for n in range(n_state):
                        where = (group * SUB + at) * n_state + n
                        prior_buf[slot, turn * SUB + at, n] = states[n]
                        decay = jnp.exp2(step * rate_ref[n])
                        states[n] = decay * states[n] + drive * brow_ref[where]
                        term = states[n] * crow_ref[where]
                        mixed[n % 2] = term if mixed[n % 2] is None else mixed[n % 2] + term
                    mixed_held[pl.ds(at, tiles, stride=SUB), :] = mixed[0] + mixed[1]
                stage_out(mixed_held, mixed_ref, group)
                return tuple(states)

            states = lax.fori_loop(0, groups, one, tuple(carried[n] for n in range(n_state)))
            for n in range(n_state):
                carried[n] = states[n]
            store(block).start()

        @pl.when(place == 0)
        def _():
            ends[seq] = carried[...]
            hand_on(seq).start()

    for seq in range(seqs):
        one_sequence(seq)
        if seq == 0:
            gather.relay()
            gather.hand_over()
            if n_swaps:
                swap.pass_on()
    gather.hand_over_last()
    for block in range(max(0, seqs * blocks - 2), seqs * blocks):
        store(block).wait()

    @pl.when(place == 0)
    def _():
        for seq in range(seqs):
            hand_on(seq).wait_send()

    gather.end()
    if n_swaps:
        swap.end()


def scan_forward_pair(
    call_id, step, inputs, b_rows, c_rows, rate, seqs, shard, arrays
):
    n_state, tiles, _ = rate.shape
    tokens, inner = step.shape
    all_groups = tokens // SUB
    groups = math.gcd(all_groups // seqs, 4)
    blocks = all_groups // seqs // groups
    vmem = pl.BlockSpec(memory_space=pltpu.VMEM)
    smem = pl.BlockSpec(memory_space=pltpu.SMEM)
    hbm = pl.BlockSpec(memory_space=pltpu.HBM)
    full = jnp.float32
    held = pltpu.VMEM((tiles * SUB, LANE), full)
    boundary = pltpu.VMEM((seqs, n_state, tiles, LANE), full)
    dma = pltpu.SemaphoreType.DMA
    return pl.pallas_call(
        functools.partial(
            forward_pair_kernel, len(arrays), n_state, tiles, groups, blocks, seqs
        ),
        in_specs=[vmem, vmem, smem, smem, vmem, hbm] + [vmem] * len(arrays),
        out_specs=[hbm, vmem, hbm] + [hbm] * len(arrays),
        out_shape=[
            jax.ShapeDtypeStruct((tokens, n_state, tiles, LANE), full),
            jax.ShapeDtypeStruct(step.shape, full),
            gathered_shape(shard),
        ]
        + split_shapes(arrays),
        scratch_shapes=[
            pltpu.VMEM((n_state, tiles, LANE), full),
            boundary,
            boundary,
            pltpu.VMEM((2, groups * SUB, n_state, tiles, LANE), full),
            held,
            held,
            held,
            dma((2,)),
            dma((seqs,)),
            dma((seqs,)),
        ]
        + gather_scratch()
        + split_scratch(arrays),
        compiler_params=pltpu.CompilerParams(
            collective_id=call_id, has_side_effects=True, vmem_limit_bytes=VMEM_GRANT
        ),
    )(step, inputs, b_rows, c_rows, rate, shard, *arrays)


def backward_pair_kernel(
    n_swaps,
    n_state,
    tiles,
    groups,
    blocks,
    seqs,
    step_ref,
    input_ref,
    ograd_ref,
    brow_ref,
    crow_ref,
    rate_ref,
    picks_ref,
    ffn_part,
    middle,
    prior_ref,
    *refs,
):
    arrays, refs = refs[:n_swaps], refs[n_swaps:]
    step_grad_ref, input_grad_ref, rate_grad_ref, part_ref, *refs = refs
    layer_first, layer_last, *refs = refs
    swapped, refs = refs[:n_swaps], refs[n_swaps:]
    carried, ends, starts, prior_buf, step_held, input_held, ograd_held, *refs = refs
    step_grad_held, input_grad_held, ffn_slots, prior_sem, send_sem, recv_sem, *refs = refs
    tp_send, tp_recv, *refs = refs
    place = lax.axis_index("ctx")
    tp = Group(("tp",), tp_send, tp_recv)
    if n_swaps:
        swap = Swap(arrays, swapped, *refs)
        greet([(PLANE, swap.plane.others), (("tp",), tp.others)])
        swap.begin()
    else:
        greet([(("ctx",), [1 - place]), (("tp",), tp.others)])
    ffn_sent = tp.scatter(ffn_part, ffn_slots, 0)

    def hand_on(seq):
        return send_on(ends.at[seq], starts.at[seq], send_sem.at[seq], recv_sem.at[seq], 0)

    def fetch(turn):
        seq = lax.div(turn, blocks)
        block = seq * blocks + blocks - 1 - lax.rem(turn, blocks)
        slot = lax.rem(turn, 2)
        rows = groups * SUB
        return pltpu.make_async_copy(
            prior_ref.at[pl.ds(pl.multiple_of(block * rows, rows), rows)],
            prior_buf.at[slot],
            prior_sem.at[slot],
        )

    fetch(0).start()
    rate_grad_ref[...] = jnp.zeros_like(rate_grad_ref)

    @pl.when(place == 1)
    def _():
        @pl.loop(0, seqs)
        def _(seq):
            def one(turn, grads):
                group = (seq + 1) * blocks * groups - 1 - turn
                grads = list(grads)
                stage_in(step_ref, group, step_held)
                stage_in(ograd_ref, group, ograd_held)
                for at in range(SUB - 1, -1, -1):
                    step = token_row(step_held, at, tiles)
                    ograd = token_row(ograd_held, at, tiles)
                    for n in range(n_state):
                        row = crow_ref[(group * SUB + at) * n_state + n]
                        grads[n] = jnp.exp2(step * rate_ref[n]) * (grads[n] + ograd * row)
                return tuple(grads)

            zero = jnp.zeros((tiles, LANE), jnp.float32)
            grads = lax.fori_loop(0, blocks * groups, one, (zero,) * n_state)
            for n in range(n_state):
                ends[seq, n] = grads[n]
            hand_on(seq).start()

    @pl.loop(0, seqs)
    def _(seq):
        @pl.when(place == 1)
        def _():
            carried[...] = jnp.zeros_like(carried)

        @pl.when(place == 0)
        def _():
            hand_on(seq).wait_recv()
            carried[...] = starts[seq]

        @pl.loop(0, blocks)
        def _(inner_block):
            turn = seq * blocks + inner_block
            slot = lax.rem(turn, 2)
            first_group = (seq * blocks + blocks - 1 - inner_block) * groups

            @pl.when(turn + 1 < seqs * blocks)
            def _():
                fetch(turn + 1).start()

            fetch(turn).wait()

            def one(back, grads):
                inner_group = groups - 1 - back
                group = first_group + inner_group
                grads = list(grads)
                stage_in(step_ref, group, step_held)
                stage_in(input_ref, group, input_held)
                stage_in(ograd_ref, group, ograd_held)
                for at in range(SUB - 1, -1, -1):
                    step = token_row(step_held, at, tiles)
                    value = token_row(input_held, at, tiles)
                    ograd = token_row(ograd_held, at, tiles)
                    drive = step * value
                    along_b = None
                    along_rate = None
                    brow_parts, crow_parts = [], []
                    for n in range(n_state):
                        where = (group * SUB + at) * n_state + n
                        brow, crow = brow_ref[where], crow_ref[where]
                        rate = rate_ref[n]
                        decay = jnp.exp2(step * rate)
                        grad = ograd * crow + grads[n]
                        kept = decay * prior_buf[slot, inner_group * SUB + at, n]
                        state = kept + drive * brow
                        decay_term = grad * kept
                        grads[n] = decay * grad
                        rate_grad_ref[n] += decay_term * step
                        by_rate, by_brow = decay_term * rate, grad * brow
                        along_rate = by_rate if along_rate is None else along_rate + by_rate
                        along_b = by_brow if along_b is None else along_b + by_brow
                        brow_parts.append(grad * drive)
                        crow_parts.append(ograd * state)
                    step_grad_held[pl.ds(at, tiles, stride=SUB), :] = (
                        along_rate * LN2 + along_b * value
                    )
                    input_grad_held[pl.ds(at, tiles, stride=SUB), :] = along_b * step
                    parts = jnp.concatenate(brow_parts + crow_parts, 0).astype(jnp.bfloat16)
                    part_ref[group * SUB + at] = jnp.dot(
                        picks_ref[...], parts, preferred_element_type=jnp.float32
                    )
                stage_out(step_grad_held, step_grad_ref, group)
                stage_out(input_grad_held, input_grad_ref, group)
                return tuple(grads)

            grads = lax.fori_loop(0, groups, one, tuple(carried[n] for n in range(n_state)))
            for n in range(n_state):
                carried[n] = grads[n]

    finish(ffn_sent)
    layer_rows = (middle[...] + tp.total(ffn_part, ffn_slots)).astype(layer_first.dtype)
    half = layer_first.shape[1]
    layer_first[...], layer_last[...] = layer_rows[:, :half], layer_rows[:, half:]

    @pl.when(place == 1)
    def _():
        @pl.loop(0, seqs)
        def _(seq):
            hand_on(seq).wait_send()

    if n_swaps:
        swap.end()


def scan_backward_pair(
    call_id, prior, step, inputs, ograd, b_rows, c_rows, rate, seqs, ffn_part, middle, arrays
):
    n_state, tiles, _ = rate.shape
    tokens, inner = step.shape
    all_groups = tokens // SUB
    groups = math.gcd(all_groups // seqs, 4)
    blocks = all_groups // seqs // groups
    tp_count = group_size(("tp",))
    vmem = pl.BlockSpec(memory_space=pltpu.VMEM)
    smem = pl.BlockSpec(memory_space=pltpu.SMEM)
    hbm = pl.BlockSpec(memory_space=pltpu.HBM)
    full = jnp.float32
    held = pltpu.VMEM((tiles * SUB, LANE), full)
    boundary = pltpu.VMEM((seqs, n_state, tiles, LANE), full)
    dma = pltpu.SemaphoreType.DMA
    layer_half = jax.ShapeDtypeStruct((middle.shape[0], middle.shape[1] // 2), jnp.bfloat16)
    picks = jnp.repeat(jnp.eye(2 * n_state, dtype=jnp.bfloat16), tiles, 1)
    return pl.pallas_call(
        functools.partial(
            backward_pair_kernel, len(arrays), n_state, tiles, groups, blocks, seqs
        ),
        in_specs=[vmem] * 3 + [smem] * 2 + [vmem] * 4 + [hbm] + [vmem] * len(arrays),
        out_specs=[vmem] * 6 + [hbm] * len(arrays),
        out_shape=[
            jax.ShapeDtypeStruct(step.shape, full),
            jax.ShapeDtypeStruct(step.shape, full),
            jax.ShapeDtypeStruct(rate.shape, full),
            jax.ShapeDtypeStruct((tokens, 2 * n_state, LANE), full),
            layer_half,
            layer_half,
        ]
        + swap_shapes(arrays),
        scratch_shapes=[
            pltpu.VMEM((n_state, tiles, LANE), full),
            boundary,
            boundary,
            pltpu.VMEM((2, groups * SUB, n_state, tiles, LANE), full),
        ]
        + [held] * 5
        + [
            slots_for(ffn_part, tp_count),
            dma((2,)),
            dma((seqs,)),
            dma((seqs,)),
            dma((1, tp_count - 1)),
            dma((1, tp_count - 1)),
        ]
        + swap_scratch(arrays),
        compiler_params=pltpu.CompilerParams(
            collective_id=call_id, has_side_effects=True, vmem_limit_bytes=VMEM_GRANT
        ),
    )(step, inputs, ograd, b_rows, c_rows, rate, picks, ffn_part, middle, prior, *arrays)


class PlaneGather:
    def __init__(self, own, gathered, send_sem, recv_sem):
        self.own, self.gathered = own, gathered
        self.send_sem, self.recv_sem = send_sem, recv_sem
        self.dp, self.ctx = lax.axis_index("dp"), lax.axis_index("ctx")
        self.n_dp, self.n_ctx = lax.axis_size("dp"), lax.axis_size("ctx")
        self.hands_on = relayed()
        self.count = self.n_dp * self.n_ctx
        self.me = self.dp * self.n_ctx + self.ctx
        self.others = [lax.rem(self.me + hop, self.count) for hop in range(1, self.count)]
        self.copies = {}
        if self.hands_on:
            core = lax.rem(self.dp, 2)
            over_core = self.dp + 1 - 2 * core
            over_y = lax.rem(self.dp + 2, 4)
            over_x = 1 - self.ctx
            self.core = {"dp": over_core, "ctx": self.ctx}
            self.at_x = {"dp": self.dp, "ctx": over_x}
            self.at_y = {"dp": over_y, "ctx": self.ctx}
            self.from_x = self.dp * 2 + over_x
            self.from_y = over_y * 2 + self.ctx
            self.across = over_y * 2 + over_x

    def part(self, owner, half):
        rows = self.gathered.shape[0] // self.count
        start, size = owner * rows, rows
        if half is not None:
            size = rows // 2
            start = start + half * size
        return self.gathered.at[pl.ds(pl.multiple_of(start, size), size), :]

    def send(self, which, owner, half, where):
        target = self.part(owner, half)
        source = target
        if owner is self.me:
            rows = self.own.shape[0]
            source = self.own
            if half is not None:
                source = self.own.at[pl.ds(half * (rows // 2), rows // 2), :]
        self.copies[which] = sent(
            source, target, self.send_sem.at[which], self.recv_sem.at[which], where
        )

    def arrived(self, *which):
        for one in which:
            self.copies[one].wait_recv()

    def begin(self, local_sem):
        self.local = pltpu.make_async_copy(self.own, self.part(self.me, None), local_sem)
        self.local.start()
        if not self.hands_on:
            for hop, other in enumerate(self.others):
                self.send(hop, self.me, None, device_at(PLANE, other))
            return
        self.send(0, self.me, 1, self.at_x)
        self.send(1, self.me, 0, self.at_y)
        self.send(2, self.me, None, self.core)
        self.send(3, self.me, 0, self.at_x)
        self.send(4, self.me, 1, self.at_y)

    def relay(self):
        if not self.hands_on:
            return
        self.arrived(0, 1)
        self.send(5, self.from_x, 1, self.at_y)
        self.send(6, self.from_y, 0, self.at_x)
        self.send(7, self.from_x, 1, self.core)
        self.send(8, self.from_y, 0, self.core)

    def hand_over(self):
        if not self.hands_on:
            return
        self.arrived(3, 4)
        self.send(9, self.from_x, 0, self.core)
        self.send(10, self.from_y, 1, self.core)

    def hand_over_last(self):
        if not self.hands_on:
            return
        self.arrived(5, 6)
        self.send(11, self.across, 1, self.core)
        self.send(12, self.across, 0, self.core)

    def end(self):
        if self.hands_on:
            self.arrived(2, 7, 8, 9, 10, 11, 12)
        else:
            self.arrived(*range(self.count - 1))
        for copy in self.copies.values():
            copy.wait_send()
        self.local.wait()


def relayed():
    return lax.axis_size("dp") == 4 and lax.axis_size("ctx") == 2


def gather_sems():
    count = 13 if relayed() else group_size(PLANE) - 1
    return pltpu.SemaphoreType.DMA((count,))


WIDE = 512


def products(source, first, last, dot, target, block_buf, block_sem, out_buf, out_sem):
    def fetch(j, slot):
        columns = pl.ds(pl.multiple_of(j * WIDE, WIDE), WIDE)
        return pltpu.make_async_copy(
            source.at[:, columns], block_buf.at[slot], block_sem.at[slot]
        )

    def store(j, slot):
        return pltpu.make_async_copy(out_buf.at[slot], target(j), out_sem.at[slot])

    fetch(first, first % 2).start()

    @pl.loop(first, last)
    def _(j):
        slot = lax.rem(j, 2)

        @pl.when(j + 1 < last)
        def _():
            fetch(j + 1, 1 - slot).start()

        fetch(j, slot).wait()

        @pl.when(j >= first + 2)
        def _():
            store(j - 2, slot).wait()

        out_buf[slot] = dot(block_buf[slot])
        store(j, slot).start()

    for j in range(max(first, last - 2), last):
        store(j, j % 2).wait()


SMALL_ROWS = 32
GAIN_ROWS = 16


def tail_kernel(
    swaps,
    conv_grad,
    gate_grad,
    convkern,
    convbias,
    stepbias,
    decaylog,
    skipgain,
    ffngain,
    layer_first,
    layer_rows,
    middle_low,
    step_low,
    pre_low,
    select_low,
    scan_in,
    tokens,
    middle_grad,
    gain_row,
    in_conv,
    in_gate,
    one_cols,
    two_cols,
    ct_cols,
    middle_cols,
    ffn_all,
    gated_all,
    tokens_grad,
    layer_out,
    vectors_sum,
    step_sum,
    select_sum,
    gains,
    mix_all,
    grad_inproj,
    grad_outproj,
    grad_gateup,
    grad_downproj,
    mix_own,
    normed_part,
    small,
    small_sum,
    small_slots,
    gain_slots,
    gain_own,
    vectors_own,
    cols,
    in_buf,
    block_buf,
    wide_buf,
    tall_buf,
    cols_sem,
    in_sem,
    block_sem,
    wide_sem,
    tall_sem,
    tp_send,
    tp_recv,
    plane_send,
    plane_recv,
    gather_send,
    gather_recv,
    local_sem,
    *sems,
):
    inner = conv_grad.shape[1]
    hidden = ffn_all.shape[1] // 3
    width = tokens.shape[1]
    rank = step_low.shape[1]
    tp = Group(("tp",), tp_send, tp_recv)
    plane = Group(PLANE, plane_send, plane_recv)
    line = LineSum(normed_part, *sems[:5])
    tokens_spread = LineSpread(tokens_grad, *sems[5:7])
    layer_last = layer_out.at[:, width // 2 :]
    layer_spread = LineSpread(layer_last, *sems[7:9])
    swap_sems = sems[9:]
    gather = PlaneGather(mix_own, mix_all, gather_send, gather_recv)
    sources = (one_cols, two_cols, ct_cols) if swaps else (one_cols, two_cols, ct_cols, middle_cols)
    loads = [
        pltpu.make_async_copy(source, cols.at[at], cols_sem.at[at])
        for at, source in enumerate(sources)
    ]
    if swaps:
        swap = Swap([middle_low], [cols.at[3]], *swap_sems)

    def fetch(j):
        slot = j % 2
        rows = slice(j * WIDE, (j + 1) * WIDE)
        return [
            pltpu.make_async_copy(source.at[rows, :], in_buf.at[slot, at], in_sem.at[slot, at])
            for at, source in enumerate((in_conv, in_gate))
        ]

    for copy in fetch(0) + loads:
        copy.start()
    mix_own[:, :inner] = conv_grad[...]
    mix_own[:, inner:] = gate_grad[...]
    greet([(("tp",), tp.others), (PLANE, plane.others)])
    gather.begin(local_sem)

    small[...] = jnp.zeros_like(small)
    vectors_own[...] = jnp.zeros_like(vectors_own)
    at = 0
    for vector in (convkern, convbias, stepbias, decaylog, skipgain):
        vectors_own[at : at + vector.shape[0], :] = vector[...]
        at += vector.shape[0]
    at = SMALL_ROWS - GAIN_ROWS + 10
    for row in range(width // inner):
        vectors_own[at + row : at + row + 1, :] = ffngain[:, row * inner : (row + 1) * inner]
    hidden_in = tokens[...].astype(jnp.float32)
    unit_rows = hidden_in * inverse_rms(hidden_in)
    blocks = width // WIDE
    firsts = []
    for j in range(blocks):
        if j + 1 < blocks:
            for copy in fetch(j + 1):
                copy.start()
        finish(fetch(j))
        columns = slice(j * WIDE, (j + 1) * WIDE)
        block = matmul_nt(conv_grad[...], in_buf[j % 2, 0]) + matmul_nt(
            gate_grad[...], in_buf[j % 2, 1]
        )
        normed_part[:, columns] = block.astype(normed_part.dtype)
        firsts.append(line.begin(j))
        gain_grad = jnp.sum(block * unit_rows[:, columns], 0, keepdims=True)
        row, at = divmod(j * WIDE, inner)
        row += SMALL_ROWS - GAIN_ROWS + 8
        vectors_own[row : row + 1, at : at + WIDE] = gain_grad
    layer_out[:, : width // 2] = layer_first[...]
    rows_of(layer_last, tp.me, tp.count)[...] = layer_rows[...]
    layer_spread.begin()
    small[:SMALL_ROWS, :] = vectors_own[...].astype(small.dtype)
    small[SMALL_ROWS : SMALL_ROWS + rank, :] = matmul_tn(step_low[...], pre_low[...]).astype(
        small.dtype
    )
    selected = select_sum.shape[0]
    small[SMALL_ROWS + rank : SMALL_ROWS + rank + selected, :] = matmul_tn(
        select_low[...], scan_in[...]
    )[:selected].astype(small.dtype)
    small_sent = plane.scatter(small, small_slots, 0)
    line.pass_all(firsts)

    def flat(at):
        return lambda block: matmul_tn(cols[at], block)

    def tall(at):
        return lambda block: matmul_tn(block, cols[at])

    def side_by_side(ref, first):
        per = ref.shape[2] // WIDE

        def target(j):
            at = j - first
            columns = pl.ds(pl.multiple_of(lax.rem(at, per) * WIDE, WIDE), WIDE)
            return ref.at[lax.div(at, per), :, columns]

        return target

    def one_above_other(ref):
        return lambda j: ref.at[pl.ds(pl.multiple_of(j * WIDE, WIDE), WIDE), :]

    wide = (block_buf, block_sem, wide_buf, wide_sem)
    high = (block_buf, block_sem, tall_buf, tall_sem)
    down_end = hidden // WIDE
    gu_end = 3 * hidden // WIDE
    finish(loads)
    products(ffn_all, 0, down_end, tall(2), one_above_other(grad_downproj), *high)
    gather.relay()
    products(ffn_all, down_end, gu_end, flat(1), side_by_side(grad_gateup, down_end), *wide)
    gather.hand_over()
    finish(small_sent)
    plane.own(small_sum)[...] = plane.total(small, small_slots).astype(small_sum.dtype)
    small_sent = plane.spread(small_sum, 1)
    if swaps:
        swap.begin()
    layer_spread.pass_on()
    hidden_in = tp.own(tokens)[...].astype(jnp.float32)
    tp.own(tokens_grad)[...] = (
        middle_grad[...]
        + norm_back(
            line.total(),
            hidden_in,
            inverse_rms(hidden_in),
            gain_row[...].astype(jnp.float32),
        )
    ).astype(tokens_grad.dtype)
    tokens_spread.begin()
    gather.hand_over_last()
    gather.end()
    products(mix_all, 0, 2 * inner // WIDE, flat(0), side_by_side(grad_inproj, 0), *wide)
    tokens_spread.pass_on()
    finish(small_sent)
    gain_own[...] = small_sum[SMALL_ROWS - GAIN_ROWS : SMALL_ROWS, :].astype(jnp.float32)
    gain_sent = [tp.one(gain_own, gain_slots.at[hop], 0, hop) for hop in range(tp.count - 1)]
    vectors_sum[...] = small_sum[:SMALL_ROWS, :].astype(jnp.float32)
    step_sum[...] = small_sum[SMALL_ROWS : SMALL_ROWS + rank, :].astype(jnp.float32)
    select_sum[...] = small_sum[SMALL_ROWS + rank : SMALL_ROWS + rank + selected, :].astype(
        jnp.float32
    )
    if swaps:
        swap.end()
    products(gated_all, 0, inner // WIDE, tall(3), one_above_other(grad_outproj), *high)
    finish(gain_sent)
    total = gain_own[...]
    for hop in range(tp.count - 1):
        total = total + gain_slots[hop]
    gains[...] = total
    tokens_spread.end()
    layer_spread.end()


def run_tail(
    call_id,
    selected,
    swaps,
    conv_grad,
    gate_grad,
    vectors,
    layer_first,
    layer_rows,
    middle_low,
    step_low,
    pre_low,
    select_low,
    scan_in,
    tokens,
    middle_grad,
    gain_row,
    in_conv,
    in_gate,
    one_cols,
    two_cols,
    ct_cols,
    middle_cols,
    ffn_all,
    gated_all,
):
    rows, inner = conv_grad.shape
    rank = step_low.shape[1]
    hidden = ffn_all.shape[1] // 3
    width = tokens.shape[1]
    share = one_cols.shape[1]
    all_rows = ffn_all.shape[0]
    tp_count, plane_count = group_size(("tp",)), group_size(PLANE)
    low, full = jnp.bfloat16, jnp.float32
    vmem = pl.BlockSpec(memory_space=pltpu.VMEM)
    hbm = pl.BlockSpec(memory_space=pltpu.HBM)
    dma = pltpu.SemaphoreType.DMA
    small_rows = SMALL_ROWS + rank + selected
    small = jax.ShapeDtypeStruct((small_rows + -small_rows % (16 * plane_count), inner), low)
    part = jax.ShapeDtypeStruct((rows, width), low)
    return pl.pallas_call(
        functools.partial(tail_kernel, swaps),
        in_specs=[vmem] * 18 + [hbm] * 8,
        out_specs=[vmem] * 6 + [hbm] * 5,
        out_shape=[
            jax.ShapeDtypeStruct(tokens.shape, low),
            jax.ShapeDtypeStruct(tokens.shape, low),
            jax.ShapeDtypeStruct((SMALL_ROWS, inner), full),
            jax.ShapeDtypeStruct((rank, inner), full),
            jax.ShapeDtypeStruct((selected, inner), full),
            jax.ShapeDtypeStruct((GAIN_ROWS, inner), full),
            jax.ShapeDtypeStruct((all_rows, 2 * inner), low),
            jax.ShapeDtypeStruct((2, share, inner), full),
            jax.ShapeDtypeStruct((inner, share), full),
            jax.ShapeDtypeStruct((2, share, hidden), full),
            jax.ShapeDtypeStruct((hidden, share), full),
        ],
        scratch_shapes=[
            pltpu.VMEM((rows, 2 * inner), low),
            pltpu.VMEM(part.shape, low),
            pltpu.VMEM(small.shape, low),
            pltpu.VMEM(small.shape, low),
            slots_for(small, plane_count),
            pltpu.VMEM((tp_count - 1, GAIN_ROWS, inner), full),
            pltpu.VMEM((GAIN_ROWS, inner), full),
            pltpu.VMEM((SMALL_ROWS, inner), full),
            pltpu.VMEM((4, all_rows, share), low),
            pltpu.VMEM((2, 2, WIDE, inner), low),
            pltpu.VMEM((2, all_rows, WIDE), low),
            pltpu.VMEM((2, share, WIDE), full),
            pltpu.VMEM((2, WIDE, share), full),
            dma((4,)),
            dma((2, 2)),
            dma((2,)),
            dma((2,)),
            dma((2,)),
            dma((1, tp_count - 1)),
            dma((1, tp_count - 1)),
            dma((2, plane_count - 1)),
            dma((2, plane_count - 1)),
        ]
        + gather_scratch()
        + line_sum_scratch(part, width // WIDE)
        + line_spread_scratch() * 2
        + (swap_scratch([tokens]) if swaps else []),
        compiler_params=pltpu.CompilerParams(
            collective_id=call_id, has_side_effects=True, vmem_limit_bytes=VMEM_GRANT
        ),
    )(
        conv_grad,
        gate_grad,
        *vectors,
        layer_first,
        layer_rows,
        middle_low,
        step_low,
        pre_low,
        select_low,
        scan_in,
        tokens,
        middle_grad,
        gain_row,
        in_conv,
        in_gate,
        one_cols,
        two_cols,
        ct_cols,
        middle_cols,
        ffn_all,
        gated_all,
    )


def head_kernel(
    tokens,
    gain,
    shard,
    conv_in,
    gathered,
    normed,
    block_buf,
    block_sem,
    gather_send,
    gather_recv,
    local_sem,
):
    gather = PlaneGather(shard, gathered, gather_send, gather_recv)
    greet([(PLANE, gather.others)])
    gather.begin(local_sem)
    hidden_in = tokens[...].astype(jnp.float32)
    normed[...] = (hidden_in * inverse_rms(hidden_in) * gain[...].astype(jnp.float32)).astype(
        normed.dtype
    )
    gather.relay()
    gather.hand_over()
    gather.hand_over_last()
    gather.end()
    product_in_blocks(normed, gathered, conv_in, block_buf, block_sem)


def run_head(call_id, tokens, gain, shard):
    rows, width = tokens.shape
    low = jnp.bfloat16
    vmem = pl.BlockSpec(memory_space=pltpu.VMEM)
    hbm = pl.BlockSpec(memory_space=pltpu.HBM)
    return pl.pallas_call(
        head_kernel,
        in_specs=[vmem] * 2 + [hbm],
        out_specs=[vmem, hbm],
        out_shape=[
            jax.ShapeDtypeStruct((rows, shard.shape[1]), low),
            gathered_shape(shard),
        ],
        scratch_shapes=[
            pltpu.VMEM((rows, width), low),
            pltpu.VMEM((2, width, WIDE), low),
            pltpu.SemaphoreType.DMA((2,)),
        ]
        + gather_scratch(),
        compiler_params=pltpu.CompilerParams(
            collective_id=call_id, has_side_effects=True, vmem_limit_bytes=VMEM_GRANT
        ),
    )(tokens, gain, shard)


def per_device(
    tokens,
    mixgain,
    inproj,
    convkern,
    convbias,
    selproj,
    stepproj,
    stepbias,
    decaylog,
    skipgain,
    outproj,
    ffngain,
    gateup,
    downproj,
    cotangent,
):
    seqs, span, width = tokens.shape
    rows = seqs * span
    taps, inner = convkern.shape
    rank = stepproj.shape[0]
    n_state = decaylog.shape[1]
    tiles = inner // LANE
    gain_mix = mixgain.astype(jnp.float32)
    kernel = convkern.astype(jnp.float32)
    kernel_bias = convbias.astype(jnp.float32)
    step_bias = stepbias.astype(jnp.float32)
    skip_weight = skipgain.astype(jnp.float32)
    decay_rate = -jnp.exp(jnp.transpose(decaylog.astype(jnp.float32)))
    rate = (decay_rate * LOG2E).reshape(n_state, tiles, LANE)

    gain_mix_row, gain_ffn_row = mixgain.reshape(1, width), ffngain.reshape(1, width)
    low = jnp.bfloat16

    tokens_rows = tokens.reshape(rows, width)
    ct_low = cotangent.reshape(rows, width)
    swap_now = swaps_in_kernels(width)
    conv_in, in_conv = run_head(5, tokens_rows, gain_mix_row, inproj[0])
    ffn_pack, conv_in = lax.optimization_barrier(
        (jnp.concatenate([gateup[0], gateup[1], jnp.transpose(downproj)], 1), conv_in)
    )
    ffn_pack = gathered_rows(ffn_pack)
    hidden_in = tokens_rows.astype(jnp.float32)
    scale_one = inverse_rms(hidden_in)
    normed_one = (hidden_in * scale_one * gain_mix).astype(low)

    conv_seqs = conv_in.reshape(seqs, span, inner)
    rim_rows = passed_along(conv_seqs[:, span - (taps - 1) :], "ctx", 1)
    padded_in = jnp.concatenate([rim_rows, conv_seqs], 1).astype(jnp.float32)
    conv_out = kernel_bias[None, None]
    for offset in range(taps):
        conv_out = conv_out + kernel[offset][None, None] * padded_in[:, offset : offset + span]
    conv_out = conv_out.reshape(rows, inner)
    scan_in = jax.nn.silu(conv_out).astype(low)
    scan_float = scan_in.astype(jnp.float32)
    columns = selproj.shape[1]
    select_width = -(-columns // LANE) * LANE
    select_weights = jnp.pad(selproj, ((0, 0), (0, select_width - columns)))
    select_cols, gate_mix, in_gate, *swapped = run_select(
        0,
        matmul(scan_in, select_weights),
        normed_one,
        inproj[1],
        [ct_low] if swap_now else [],
    )

    def columns_of(swapped, array):
        if not swapped:
            return swapped_columns(array)
        return swapped[0].reshape(-1, swapped[0].shape[-1])

    ct_cols = columns_of(swapped, ct_low)
    step_low = select_cols[:, :rank].astype(low)
    b_rows = select_cols[:, rank : rank + n_state].reshape(-1)
    c_rows = select_cols[:, rank + n_state : columns].reshape(-1)
    step_pre = matmul(step_low, stepproj) + step_bias[None]
    step_size = jax.nn.softplus(step_pre)
    in_pairs = lax.axis_size("ctx") == 2
    if in_pairs:
        prior, scan_out, out_all, *swapped = scan_forward_pair(
            6,
            step_size,
            scan_float,
            b_rows,
            c_rows,
            rate,
            seqs,
            outproj,
            [normed_one] if swap_now else [],
        )
    else:
        span_decay = jnp.exp(
            decay_rate[None] * jnp.sum(step_size.reshape(seqs, span, inner), 1)[:, None]
        ).reshape(seqs, n_state, tiles, LANE)
        ends = scan_ends(step_size, scan_float, b_rows, rate, seqs, False)
        start = from_earlier(ends, span_decay, 1)
        prior, scan_out = scan_forward(start, step_size, scan_float, b_rows, c_rows, rate, seqs)
        out_all, swapped = gathered_rows(outproj), []
    normed_one_cols = columns_of(swapped, normed_one)
    mixer_core = scan_out + skip_weight[None] * scan_float
    gate_sig = jax.nn.silu(gate_mix)
    gated = (mixer_core * gate_sig).astype(low)
    normed_two, middle = mixer_out(1, gated, out_all, tokens_rows, gain_ffn_row)
    made, gated_all = run_ffn(8, normed_two, ct_low, ffn_pack, gated)
    ffn_all = gathered_rows(made)
    middle_low, middle_grad, ffngain_part, gated_grad, ffn_part, *swapped = ffn_back(
        2,
        made,
        ct_low,
        middle,
        gain_ffn_row,
        out_all,
        ffn_pack,
        [normed_two] if swap_now else [],
    )
    normed_two_cols = columns_of(swapped, normed_two)
    core_grad = gated_grad * gate_sig
    gate_mix_grad = (gated_grad * mixer_core * silu_slope(gate_mix)).astype(low)
    grad_skipgain = jnp.sum(core_grad * scan_float, 0)
    if in_pairs:
        step_grad, input_grad, rate_grad, parts, *layer_rows = scan_backward_pair(
            7,
            prior,
            step_size,
            scan_float,
            core_grad,
            b_rows,
            c_rows,
            rate,
            seqs,
            ffn_part,
            middle,
            [],
        )
    else:
        back_ends = scan_ends(step_size, core_grad, c_rows, rate, seqs, True)
        end_grad = from_earlier(back_ends, span_decay, -1)
        step_grad, input_grad, rate_grad, parts = scan_backward(
            end_grad, prior, step_size, scan_float, core_grad, b_rows, c_rows, rate, seqs
        )
        ffn_sum = lax.psum_scatter(ffn_part, "tp", scatter_dimension=0, tiled=True)
        layer_rows = jnp.split((middle + ffn_sum.astype(jnp.float32)).astype(low), 2, 1)
    grad_decaylog = rate_grad.reshape(n_state, inner) * decay_rate
    pre_grad = step_grad * jax.nn.sigmoid(step_pre)
    grad_stepbias = jnp.sum(pre_grad, 0)
    pre_low = pre_grad.astype(low)
    select_part = jnp.concatenate(
        [
            matmul_nt(pre_low, stepproj),
            jnp.sum(parts, -1),
            jnp.zeros((rows, select_width - columns), jnp.float32),
        ],
        1,
    ).astype(low)
    select_low, layer_first = sum_over_tp(3, select_part, layer_rows[0])
    scan_in_grad = (
        core_grad * skip_weight[None]
        + input_grad
        + matmul_nt(select_low, select_weights)
    )
    conv_grad = scan_in_grad * silu_slope(conv_out)
    grad_convbias = jnp.sum(conv_grad, 0)
    conv_grad_seqs = conv_grad.reshape(seqs, span, inner)
    padded_grad = jnp.zeros(padded_in.shape, jnp.float32)
    kernel_rows = []
    for offset in range(taps):
        kernel_rows.append(jnp.sum(conv_grad_seqs * padded_in[:, offset : offset + span], (0, 1)))
        padded_grad = padded_grad + jnp.pad(
            kernel[offset][None, None] * conv_grad_seqs,
            ((0, 0), (offset, taps - 1 - offset), (0, 0)),
        )
    grad_convkern = jnp.stack(kernel_rows)
    returned = passed_along(padded_grad[:, : taps - 1], "ctx", -1)
    conv_in_grad = (
        (padded_grad[:, taps - 1 :] + jnp.pad(returned, ((0, 0), (span - taps + 1, 0), (0, 0))))
        .astype(low)
        .reshape(rows, inner)
    )
    vectors = [
        grad_convkern,
        grad_convbias[None],
        grad_stepbias[None],
        grad_decaylog,
        grad_skipgain[None],
        ffngain_part,
    ]
    (
        tokens_grad,
        layer_out,
        vectors,
        grad_stepproj,
        grad_selproj,
        gains,
        _,
        grad_inproj,
        grad_outproj,
        grad_gateup,
        grad_downproj,
    ) = run_tail(
        4,
        columns,
        swap_now,
        conv_in_grad,
        gate_mix_grad,
        vectors,
        layer_first,
        layer_rows[1],
        middle_low,
        step_low,
        pre_low,
        select_low,
        scan_in,
        tokens_rows,
        middle_grad,
        gain_mix_row,
        in_conv,
        in_gate,
        normed_one_cols,
        normed_two_cols,
        ct_cols,
        normed_two_cols if swap_now else swapped_columns(middle_low),
        ffn_all,
        gated_all,
    )
    at = taps + 2
    return (
        layer_out.reshape(tokens.shape),
        tokens_grad.reshape(tokens.shape),
        gains[8:10].reshape(width),
        grad_inproj,
        vectors[:taps],
        vectors[taps],
        jnp.transpose(grad_selproj),
        grad_stepproj,
        vectors[taps + 1],
        jnp.transpose(vectors[at : at + n_state]),
        vectors[at + n_state],
        grad_outproj,
        gains[10:12].reshape(width),
        grad_gateup,
        grad_downproj,
    )


def solution(mesh):
    in_specs = (
        P("dp", "ctx", None),
        P(),
        P(None, ("dp", "ctx"), "tp"),
        P(None, "tp"),
        P("tp"),
        P("tp", None),
        P(None, "tp"),
        P("tp"),
        P("tp", None),
        P("tp"),
        P("tp", ("dp", "ctx")),
        P(),
        P(None, ("dp", "ctx"), "tp"),
        P("tp", ("dp", "ctx")),
        P("dp", "ctx", None),
    )
    out_specs = (
        P("dp", "ctx", None),
        P("dp", "ctx", None),
        P(),
        P(None, ("dp", "ctx"), "tp"),
        P(None, "tp"),
        P("tp"),
        P("tp", None),
        P(None, "tp"),
        P("tp"),
        P("tp", None),
        P("tp"),
        P("tp", ("dp", "ctx")),
        P(),
        P(None, ("dp", "ctx"), "tp"),
        P("tp", ("dp", "ctx")),
    )
    return jax.shard_map(
        per_device, mesh=mesh, in_specs=in_specs, out_specs=out_specs, check_vma=False
    )
```

```python
import functools
import math

import jax
import jax.numpy as jnp
from jax import lax
from jax.experimental import pallas as pl
from jax.experimental.pallas import tpu as pltpu
from jax.sharding import PartitionSpec as P

EPSILON = 1e-05
LOG2E = math.log2(math.e)
LN2 = math.log(2.0)
SUB = 8
LANE = 128
VMEM_GRANT = 60 * 2**20
PLANE = ("dp", "ctx")


def passed_along(value, axis, steps):
    count = lax.axis_size(axis)
    first, last = (max(0, -steps), min(count, count - steps))
    return lax.ppermute(value, axis, [(source, source + steps) for source in range(first, last)])


def matmul(left, right):
    return jnp.dot(left, right, preferred_element_type=jnp.float32)


def matmul_nt(left, right):
    return lax.dot_general(
        left, right, (((1,), (1,)), ((), ())), preferred_element_type=jnp.float32
    )


def matmul_tn(left, right):
    return lax.dot_general(
        left, right, (((0,), (0,)), ((), ())), preferred_element_type=jnp.float32
    )


def inverse_rms(values):
    return lax.rsqrt(jnp.mean(values * values, -1, keepdims=True) + EPSILON)


def silu_slope(values):
    logistic = jax.nn.sigmoid(values)
    return logistic * (1.0 + values * (1.0 - logistic))


def norm_back(grad_norm, values, scale, gain):
    scaled_grad = grad_norm * gain
    unit_rows = values * scale
    return scale * (scaled_grad - unit_rows * jnp.mean(scaled_grad * unit_rows, -1, keepdims=True))


def stage_in(ref, group, held):
    for tile in range(held.shape[0] // SUB):
        held[pl.ds(tile * SUB, SUB), :] = ref[
            pl.ds(pl.multiple_of(group * SUB, SUB), SUB), pl.ds(tile * LANE, LANE)
        ]


def stage_out(held, ref, group):
    for tile in range(held.shape[0] // SUB):
        ref[pl.ds(pl.multiple_of(group * SUB, SUB), SUB), pl.ds(tile * LANE, LANE)] = held[
            pl.ds(tile * SUB, SUB), :
        ]


def token_row(held, at, tiles):
    return held[pl.ds(at, tiles, stride=SUB), :]


def ends_kernel(
    n_state,
    tiles,
    groups,
    reverse,
    step_ref,
    drive_ref,
    rows_ref,
    rate_ref,
    end_ref,
    step_held,
    drive_held,
):
    base = pl.program_id(0) * groups * SUB * n_state
    rates = [rate_ref[n] for n in range(n_state)]

    def one(turn, states):
        group = groups - 1 - turn if reverse else turn
        order = range(SUB - 1, -1, -1) if reverse else range(SUB)
        states = list(states)
        stage_in(step_ref, group, step_held)
        stage_in(drive_ref, group, drive_held)
        for at in order:
            step = token_row(step_held, at, tiles)
            drive = token_row(drive_held, at, tiles)
            if not reverse:
                drive = drive * step
            for n in range(n_state):
                row = rows_ref[base + (group * SUB + at) * n_state + n]
                decay = jnp.exp2(step * rates[n])
                if reverse:
                    states[n] = decay * (states[n] + drive * row)
                else:
                    states[n] = decay * states[n] + drive * row
        return tuple(states)

    zero = jnp.zeros((tiles, LANE), jnp.float32)
    states = lax.fori_loop(0, groups, one, (zero,) * n_state)
    for n in range(n_state):
        end_ref[0, n] = states[n]


def scan_ends(step, drive, rows, rate, seqs, reverse):
    n_state, tiles, _ = rate.shape
    groups = step.shape[0] // seqs // SUB
    rows_spec = pl.BlockSpec((groups * SUB, tiles * LANE), lambda s: (s, 0))
    held = pltpu.VMEM((tiles * SUB, LANE), jnp.float32)
    return pl.pallas_call(
        functools.partial(ends_kernel, n_state, tiles, groups, reverse),
        grid=(seqs,),
        in_specs=[
            rows_spec,
            rows_spec,
            pl.BlockSpec(memory_space=pltpu.SMEM),
            pl.BlockSpec((n_state, tiles, LANE), lambda s: (0, 0, 0)),
        ],
        out_specs=pl.BlockSpec((1, n_state, tiles, LANE), lambda s: (s, 0, 0, 0)),
        out_shape=jax.ShapeDtypeStruct((seqs, n_state, tiles, LANE), jnp.float32),
        scratch_shapes=[held, held],
        compiler_params=pltpu.CompilerParams(vmem_limit_bytes=VMEM_GRANT),
    )(step, drive, rows, rate)


def forward_kernel(
    n_state,
    tiles,
    groups,
    blocks,
    start_ref,
    step_ref,
    input_ref,
    brow_ref,
    crow_ref,
    rate_ref,
    prior_ref,
    mixed_ref,
    carried,
    step_held,
    input_held,
    mixed_held,
):
    base = (pl.program_id(0) * blocks + pl.program_id(1)) * groups * SUB * n_state

    @pl.when(pl.program_id(1) == 0)
    def _():
        carried[...] = start_ref[0]

    def one(group, states):
        states = list(states)
        stage_in(step_ref, group, step_held)
        stage_in(input_ref, group, input_held)
        for at in range(SUB):
            step = token_row(step_held, at, tiles)
            drive = step * token_row(input_held, at, tiles)
            mixed = [None] * 2
            for n in range(n_state):
                where = base + (group * SUB + at) * n_state + n
                prior_ref[group * SUB + at, n] = states[n]
                decay = jnp.exp2(step * rate_ref[n])
                states[n] = decay * states[n] + drive * brow_ref[where]
                term = states[n] * crow_ref[where]
                mixed[n % 2] = term if mixed[n % 2] is None else mixed[n % 2] + term
            mixed_held[pl.ds(at, tiles, stride=SUB), :] = mixed[0] + mixed[1]
        stage_out(mixed_held, mixed_ref, group)
        return tuple(states)

    states = lax.fori_loop(0, groups, one, tuple(carried[n] for n in range(n_state)))
    for n in range(n_state):
        carried[n] = states[n]


def scan_forward(start, step, inputs, b_rows, c_rows, rate, seqs):
    n_state, tiles, _ = rate.shape
    all_groups = step.shape[0] // SUB
    groups = math.gcd(all_groups // seqs, 4)
    blocks = all_groups // seqs // groups
    rows_spec = pl.BlockSpec((groups * SUB, tiles * LANE), lambda s, b: (s * blocks + b, 0))
    held = pltpu.VMEM((tiles * SUB, LANE), jnp.float32)
    smem = pl.BlockSpec(memory_space=pltpu.SMEM)
    tokens = all_groups * SUB
    return pl.pallas_call(
        functools.partial(forward_kernel, n_state, tiles, groups, blocks),
        grid=(seqs, blocks),
        in_specs=[
            pl.BlockSpec((1, n_state, tiles, LANE), lambda s, b: (s, 0, 0, 0)),
            rows_spec,
            rows_spec,
            smem,
            smem,
            pl.BlockSpec((n_state, tiles, LANE), lambda s, b: (0, 0, 0)),
        ],
        out_specs=[
            pl.BlockSpec(
                (groups * SUB, n_state, tiles, LANE), lambda s, b: (s * blocks + b, 0, 0, 0)
            ),
            rows_spec,
        ],
        out_shape=[
            jax.ShapeDtypeStruct((tokens, n_state, tiles, LANE), jnp.float32),
            jax.ShapeDtypeStruct(step.shape, jnp.float32),
        ],
        scratch_shapes=[pltpu.VMEM((n_state, tiles, LANE), jnp.float32)] + [held] * 3,
        compiler_params=pltpu.CompilerParams(vmem_limit_bytes=VMEM_GRANT),
    )(start, step, inputs, b_rows, c_rows, rate)


def backward_kernel(
    n_state,
    tiles,
    groups,
    blocks,
    end_ref,
    prior_ref,
    step_ref,
    input_ref,
    ograd_ref,
    brow_ref,
    crow_ref,
    rate_ref,
    picks_ref,
    step_grad_ref,
    input_grad_ref,
    rate_grad_ref,
    part_ref,
    carried,
    step_held,
    input_held,
    ograd_held,
    step_grad_held,
    input_grad_held,
):
    block = blocks - 1 - pl.program_id(1)
    base = (pl.program_id(0) * blocks + block) * groups * SUB * n_state

    @pl.when(pl.program_id(1) == 0)
    def _():
        carried[...] = end_ref[0]

    @pl.when((pl.program_id(0) == 0) & (pl.program_id(1) == 0))
    def _():
        rate_grad_ref[...] = jnp.zeros_like(rate_grad_ref)

    def one(turn, grads):
        group = groups - 1 - turn
        grads = list(grads)
        stage_in(step_ref, group, step_held)
        stage_in(input_ref, group, input_held)
        stage_in(ograd_ref, group, ograd_held)
        for at in range(SUB - 1, -1, -1):
            step = token_row(step_held, at, tiles)
            value = token_row(input_held, at, tiles)
            ograd = token_row(ograd_held, at, tiles)
            drive = step * value
            along_b = None
            along_rate = None
            brow_parts, crow_parts = [], []
            for n in range(n_state):
                where = base + (group * SUB + at) * n_state + n
                brow, crow = brow_ref[where], crow_ref[where]
                rate = rate_ref[n]
                decay = jnp.exp2(step * rate)
                grad = ograd * crow + grads[n]
                kept = decay * prior_ref[group * SUB + at, n]
                state = kept + drive * brow
                decay_term = grad * kept
                grads[n] = decay * grad
                rate_grad_ref[n] += decay_term * step
                by_rate, by_brow = decay_term * rate, grad * brow
                along_rate = by_rate if along_rate is None else along_rate + by_rate
                along_b = by_brow if along_b is None else along_b + by_brow
                brow_parts.append(grad * drive)
                crow_parts.append(ograd * state)
            step_grad_held[pl.ds(at, tiles, stride=SUB), :] = along_rate * LN2 + along_b * value
            input_grad_held[pl.ds(at, tiles, stride=SUB), :] = along_b * step
            parts = jnp.concatenate(brow_parts + crow_parts, 0).astype(jnp.bfloat16)
            part_ref[group * SUB + at] = jnp.dot(
                picks_ref[...], parts, preferred_element_type=jnp.float32
            )
        stage_out(step_grad_held, step_grad_ref, group)
        stage_out(input_grad_held, input_grad_ref, group)
        return tuple(grads)

    grads = lax.fori_loop(0, groups, one, tuple(carried[n] for n in range(n_state)))
    for n in range(n_state):
        carried[n] = grads[n]


def scan_backward(end_grad, prior, step, inputs, ograd, b_rows, c_rows, rate, seqs):
    n_state, tiles, _ = rate.shape
    all_groups = step.shape[0] // SUB
    groups = math.gcd(all_groups // seqs, 4)
    blocks = all_groups // seqs // groups

    def at(s, b):
        return s * blocks + blocks - 1 - b

    rows_spec = pl.BlockSpec((groups * SUB, tiles * LANE), lambda s, b: (at(s, b), 0))
    held = pltpu.VMEM((tiles * SUB, LANE), jnp.float32)
    smem = pl.BlockSpec(memory_space=pltpu.SMEM)
    tokens = all_groups * SUB
    picks = jnp.repeat(jnp.eye(2 * n_state, dtype=jnp.bfloat16), tiles, 1)
    return pl.pallas_call(
        functools.partial(backward_kernel, n_state, tiles, groups, blocks),
        grid=(seqs, blocks),
        in_specs=[
            pl.BlockSpec((1, n_state, tiles, LANE), lambda s, b: (s, 0, 0, 0)),
            pl.BlockSpec((groups * SUB, n_state, tiles, LANE), lambda s, b: (at(s, b), 0, 0, 0)),
            rows_spec,
            rows_spec,
            rows_spec,
            smem,
            smem,
            pl.BlockSpec((n_state, tiles, LANE), lambda s, b: (0, 0, 0)),
            pl.BlockSpec(picks.shape, lambda s, b: (0, 0)),
        ],
        out_specs=[
            rows_spec,
            rows_spec,
            pl.BlockSpec((n_state, tiles, LANE), lambda s, b: (0, 0, 0)),
            pl.BlockSpec((groups * SUB, 2 * n_state, LANE), lambda s, b: (at(s, b), 0, 0)),
        ],
        out_shape=[
            jax.ShapeDtypeStruct(step.shape, jnp.float32),
            jax.ShapeDtypeStruct(step.shape, jnp.float32),
            jax.ShapeDtypeStruct(rate.shape, jnp.float32),
            jax.ShapeDtypeStruct((tokens, 2 * n_state, LANE), jnp.float32),
        ],
        scratch_shapes=[pltpu.VMEM((n_state, tiles, LANE), jnp.float32)] + [held] * 5,
        compiler_params=pltpu.CompilerParams(vmem_limit_bytes=VMEM_GRANT),
    )(end_grad, prior, step, inputs, ograd, b_rows, c_rows, rate, picks)


def from_earlier(ends, decay, steps):
    count = lax.axis_size("ctx")
    if count == 1:
        return jnp.zeros_like(ends)
    if count == 2:
        return passed_along(ends, "ctx", steps)
    index = lax.axis_index("ctx")
    all_ends = lax.all_gather(ends, "ctx")
    all_decays = lax.all_gather(decay, "ctx")

    def one(turn, state):
        at = turn if steps > 0 else count - 1 - turn
        reached = at < index if steps > 0 else at > index
        return jnp.where(reached, all_decays[at] * state + all_ends[at], state)

    return lax.fori_loop(0, count, one, jnp.zeros_like(ends))


def gathered_rows(rows):
    return lax.all_gather(rows, PLANE, axis=0, tiled=True)


def swapped_columns(rows):
    return lax.all_to_all(rows, PLANE, split_axis=1, concat_axis=0, tiled=True)


def place_in(axes):
    index = 0
    for axis in axes:
        index = index * lax.axis_size(axis) + lax.axis_index(axis)
    return index


def device_at(axes, index):
    where = {}
    for axis in reversed(axes):
        size = lax.axis_size(axis)
        where[axis] = lax.rem(index, size)
        index = lax.div(index, size)
    return where


def greet(groups):
    barrier = pltpu.get_barrier_semaphore()
    total = 0
    for axes, others in groups:
        for other in others:
            pl.semaphore_signal(
                barrier,
                inc=1,
                device_id=device_at(axes, other),
                device_id_type=pl.DeviceIdType.MESH,
            )
            total += 1
    pl.semaphore_wait(barrier, total)


def sent(source, target, send_sem, recv_sem, where):
    copy = pltpu.make_async_remote_copy(
        src_ref=source,
        dst_ref=target,
        send_sem=send_sem,
        recv_sem=recv_sem,
        device_id=where,
        device_id_type=pl.DeviceIdType.MESH,
    )
    copy.start()
    return copy


def finish(copies):
    for copy in copies:
        copy.wait()


def rows_of(ref, index, count):
    rows = ref.shape[0] // count
    return ref.at[pl.ds(pl.multiple_of(index * rows, rows), rows), :]


class Group:
    def __init__(self, axes, send_sem, recv_sem):
        self.axes = axes
        self.count = math.prod(lax.axis_size(axis) for axis in axes)
        self.me = place_in(axes)
        self.others = [lax.rem(self.me + hop, self.count) for hop in range(1, self.count)]
        self.send_sem, self.recv_sem = send_sem, recv_sem

    def own(self, ref):
        return rows_of(ref, self.me, self.count)

    def one(self, source, target, which, hop):
        return sent(
            source,
            target,
            self.send_sem.at[which, hop],
            self.recv_sem.at[which, hop],
            device_at(self.axes, self.others[hop]),
        )

    def scatter(self, part, slot, which):
        return [
            self.one(rows_of(part, other, self.count), slot.at[hop], which, hop)
            for hop, other in enumerate(self.others)
        ]

    def total(self, part, slot):
        total = self.own(part)[...].astype(jnp.float32)
        for hop in range(self.count - 1):
            total = total + slot[hop].astype(jnp.float32)
        return total

    def spread(self, ref, which):
        return [self.one(self.own(ref), self.own(ref), which, hop) for hop in range(self.count - 1)]


def slots_for(part, count):
    return pltpu.VMEM((count - 1, part.shape[0] // count) + part.shape[1:], part.dtype)


def group_size(axes):
    return math.prod(lax.axis_size(axis) for axis in axes)


def line_of_four():
    me = lax.axis_index("tp")
    near = me + 1 - 2 * lax.rem(me, 2)
    return me, near, lax.rem(me + 2, 4), lax.rem(near + 2, 4)


class LineSum:
    def __init__(self, part, near_slots, far_slot, passed, send_sem, recv_sem):
        self.part, self.near_slots, self.far_slot = part, near_slots, far_slot
        self.passed, self.send_sem, self.recv_sem = passed, send_sem, recv_sem
        self.me, self.near, self.far, self.cross = line_of_four()
        self.blocks = send_sem.shape[1]
        self.copies = []

    def columns(self, j):
        wide = self.part.shape[1] // self.blocks
        return slice(j * wide, (j + 1) * wide)

    def rows(self, index):
        return rows_of(self.part, index, 4)

    def send(self, source, target, which, j, where):
        copy = sent(
            source.at[:, self.columns(j)],
            target.at[:, self.columns(j)],
            self.send_sem.at[which, j],
            self.recv_sem.at[which, j],
            {"tp": where},
        )
        self.copies.append((which, copy))
        return copy

    def begin(self, j):
        first = self.send(self.rows(self.cross), self.near_slots.at[0], 0, j, self.near)
        self.send(self.rows(self.near), self.near_slots.at[1], 1, j, self.near)
        return first

    def pass_on(self, j, first):
        first.wait_recv()
        columns = self.columns(j)
        self.passed[:, columns] = (
            self.rows(self.far)[:, columns].astype(jnp.float32)
            + self.near_slots[0, :, columns].astype(jnp.float32)
        ).astype(self.passed.dtype)
        self.send(self.passed, self.far_slot, 2, j, self.far)

    def total(self):
        for which, copy in self.copies:
            copy.wait_send()
            if which:
                copy.wait_recv()
        return (
            self.rows(self.me)[...].astype(jnp.float32)
            + self.near_slots[1].astype(jnp.float32)
            + self.far_slot[...].astype(jnp.float32)
        )

    def pass_all(self, firsts):
        for j, first in enumerate(firsts):
            self.pass_on(j, first)


def line_sum_scratch(part, blocks):
    share = (part.shape[0] // 4,) + part.shape[1:]
    sems = pltpu.SemaphoreType.DMA((3, blocks))
    return [
        pltpu.VMEM((2,) + share, part.dtype),
        pltpu.VMEM(share, part.dtype),
        pltpu.VMEM(share, part.dtype),
        sems,
        sems,
    ]


class LineSpread:
    def __init__(self, ref, send_sem, recv_sem):
        self.ref, self.send_sem, self.recv_sem = ref, send_sem, recv_sem
        self.me, self.near, self.far, self.cross = line_of_four()

    def send(self, owner, half, which, where):
        rows = rows_of(self.ref, owner, 4)
        if half is not None:
            wide = self.ref.shape[1] // 2
            rows = rows.at[:, half * wide : (half + 1) * wide]
        return sent(rows, rows, self.send_sem.at[which], self.recv_sem.at[which], {"tp": where})

    def begin(self):
        self.across = [self.send(self.me, half, half, self.far) for half in range(2)]
        self.within = [self.send(self.me, None, 2, self.near)]

    def pass_on(self):
        for half, copy in enumerate(self.across):
            copy.wait_recv()
            self.within.append(self.send(self.far, half, 3 + half, self.near))

    def end(self):
        for copy in self.across:
            copy.wait_send()
        finish(self.within)

    def run(self):
        self.begin()
        self.pass_on()
        self.end()


def line_spread_scratch():
    return [pltpu.SemaphoreType.DMA((5,)), pltpu.SemaphoreType.DMA((5,))]


class Swap:
    def __init__(self, arrays, swapped, send_sem, recv_sem, local_sem):
        plane = Group(PLANE, send_sem, recv_sem)
        self.plane, self.arrays, self.swapped, self.local_sem = plane, arrays, swapped, local_sem

    def begin(self):
        self.copies, plane = [], self.plane
        for which, (array, swapped) in enumerate(zip(self.arrays, self.swapped)):
            share = swapped.shape[1]

            def columns(index):
                return array.at[:, pl.ds(pl.multiple_of(index * share, share), share)]

            for hop, other in enumerate(plane.others):
                self.copies.append(plane.one(columns(other), plane.own(swapped), which, hop))
            local = pltpu.make_async_copy(
                columns(plane.me), plane.own(swapped), self.local_sem.at[which]
            )
            local.start()
            self.copies.append(local)

    def end(self):
        finish(self.copies)


def swap_scratch(arrays):
    sems = pltpu.SemaphoreType.DMA((len(arrays), group_size(PLANE) - 1))
    return [sems, sems, pltpu.SemaphoreType.DMA((len(arrays),))] if arrays else []


def swap_shapes(arrays):
    count = group_size(PLANE)
    return [
        jax.ShapeDtypeStruct((array.shape[0] * count, array.shape[1] // count), array.dtype)
        for array in arrays
    ]


def swaps_in_kernels(width):
    return width // group_size(PLANE) % LANE == 0


def gathered_shape(shard):
    return jax.ShapeDtypeStruct(
        (shard.shape[0] * group_size(PLANE),) + shard.shape[1:], shard.dtype
    )


def gather_scratch():
    return [gather_sems(), gather_sems(), pltpu.SemaphoreType.DMA(())]


def product_in_blocks(left, source, target, block_buf, block_sem):
    columns = range(0, source.shape[1], WIDE)

    def fetch(turn):
        at = columns[turn]
        return pltpu.make_async_copy(
            source.at[:, at : at + WIDE], block_buf.at[turn % 2], block_sem.at[turn % 2]
        )

    fetch(0).start()
    for turn, at in enumerate(columns):
        if turn + 1 < len(columns):
            fetch(turn + 1).start()
        fetch(turn).wait()
        target[:, at : at + WIDE] = matmul(left[...], block_buf[turn % 2]).astype(target.dtype)


def select_kernel(
    part, shard, total, gathered, slots, send_sem, recv_sem, gather_send, gather_recv, local_sem
):
    group = Group(("tp",), send_sem, recv_sem)
    gather = PlaneGather(shard, gathered, gather_send, gather_recv)
    greet([(("tp",), group.others), (PLANE, gather.others)])
    copies = group.scatter(part, slots, 0)
    gather.begin(local_sem)
    finish(copies)
    group.own(total)[...] = group.total(part, slots).astype(total.dtype)
    copies = group.spread(total, 1)
    gather.relay()
    gather.hand_over()
    finish(copies)
    gather.hand_over_last()
    gather.end()


def run_select(call_id, part, shard):
    count = group_size(("tp",))
    vmem = pl.BlockSpec(memory_space=pltpu.VMEM)
    hbm = pl.BlockSpec(memory_space=pltpu.HBM)
    sems = pltpu.SemaphoreType.DMA((2, count - 1))
    return pl.pallas_call(
        select_kernel,
        in_specs=[vmem, hbm],
        out_specs=[vmem, hbm],
        out_shape=[jax.ShapeDtypeStruct(part.shape, part.dtype), gathered_shape(shard)],
        scratch_shapes=[slots_for(part, count), sems, sems] + gather_scratch(),
        compiler_params=pltpu.CompilerParams(
            collective_id=call_id, has_side_effects=True, vmem_limit_bytes=VMEM_GRANT
        ),
    )(part, shard)


def sum_kernel(part, own_rows, total, all_rows, slots, send_sem, recv_sem, *line_sems):
    group = Group(("tp",), send_sem, recv_sem)
    rows = LineSpread(all_rows, *line_sems)
    greet([(("tp",), group.others)])
    copies = group.scatter(part, slots, 0)
    group.own(all_rows)[...] = own_rows[...]
    rows.begin()
    finish(copies)
    group.own(total)[...] = group.total(part, slots).astype(total.dtype)
    copies = group.spread(total, 1)
    rows.pass_on()
    finish(copies)
    rows.end()


def sum_over_tp(call_id, part, own_rows):
    count = group_size(("tp",))
    vmem = pl.BlockSpec(memory_space=pltpu.VMEM)
    sems = pltpu.SemaphoreType.DMA((2, count - 1))
    return pl.pallas_call(
        sum_kernel,
        in_specs=[vmem] * 2,
        out_specs=[vmem] * 2,
        out_shape=[
            jax.ShapeDtypeStruct(part.shape, part.dtype),
            jax.ShapeDtypeStruct((own_rows.shape[0] * count, own_rows.shape[1]), own_rows.dtype),
        ],
        scratch_shapes=[slots_for(part, count), sems, sems] + line_spread_scratch(),
        compiler_params=pltpu.CompilerParams(
            collective_id=call_id, has_side_effects=True, vmem_limit_bytes=VMEM_GRANT
        ),
    )(part, own_rows)


def mixer_out_kernel(n_swaps, gated, out_first, out_last, tokens, gain, *refs):
    arrays, refs = refs[:n_swaps], refs[n_swaps:]
    normed, middle, gated_all, *refs = refs
    swapped, refs = refs[:n_swaps], refs[n_swaps:]
    part, refs = refs[0], refs[1:]
    line = LineSum(part, *refs[:5])
    spread = LineSpread(normed, *refs[5:7])
    gather_send, gather_recv, local_sem, *refs = refs[7:]
    group = Group(("tp",), None, None)
    gather = PlaneGather(gated, gated_all, gather_send, gather_recv)
    half = gated.shape[1] // 2
    share = out_first.shape[1]
    greet([(("tp",), group.others), (PLANE, gather.others)])
    gather.begin(local_sem)
    for at in range(out_first.shape[0] // half):
        rows = slice(at * half, (at + 1) * half)
        part[:, at * share : (at + 1) * share] = (
            matmul(gated[:, :half], out_first[rows, :])
            + matmul(gated[:, half:], out_last[rows, :])
        ).astype(part.dtype)
    firsts = [line.begin(j) for j in range(line.blocks)]
    if n_swaps:
        swap = Swap(arrays, swapped, *refs)
        swap.begin()
    line.pass_all(firsts)
    rows = group.own(tokens)[...].astype(jnp.float32) + line.total()
    middle[...] = rows
    group.own(normed)[...] = (rows * inverse_rms(rows) * gain[...].astype(jnp.float32)).astype(
        normed.dtype
    )
    spread.begin()
    gather.relay()
    gather.hand_over()
    spread.pass_on()
    spread.end()
    gather.hand_over_last()
    gather.end()
    if n_swaps:
        swap.end()


def mixer_out(call_id, gated, out_first, out_last, tokens, gain, arrays):
    count = group_size(("tp",))
    vmem = pl.BlockSpec(memory_space=pltpu.VMEM)
    hbm = pl.BlockSpec(memory_space=pltpu.HBM)
    rows, width = tokens.shape
    part = jax.ShapeDtypeStruct((rows, width), jnp.bfloat16)
    return pl.pallas_call(
        functools.partial(mixer_out_kernel, len(arrays)),
        in_specs=[vmem] * (5 + len(arrays)),
        out_specs=[vmem] * 2 + [hbm] + [hbm] * len(arrays),
        out_shape=[
            part,
            jax.ShapeDtypeStruct((rows // count, width), jnp.float32),
            gathered_shape(gated),
        ]
        + swap_shapes(arrays),
        scratch_shapes=[pltpu.VMEM(part.shape, part.dtype)]
        + line_sum_scratch(part, 2)
        + line_spread_scratch()
        + gather_scratch()
        + swap_scratch(arrays),
        compiler_params=pltpu.CompilerParams(
            collective_id=call_id, has_side_effects=True, vmem_limit_bytes=VMEM_GRANT
        ),
    )(gated, out_first, out_last, tokens, gain, *arrays)


def ffn_kernel(swaps, normed, ct, weights, made, *refs):
    hidden = weights.shape[1] // 3
    if swaps:
        *swapped, block_buf, block_sem, send_sem, recv_sem, local_sem = refs
        swap = Swap([ct], swapped, send_sem, recv_sem, local_sem)
        greet([(PLANE, swap.plane.others)])
        swap.begin()
    else:
        block_buf, block_sem = refs

    def columns(j, which):
        return pl.ds(pl.multiple_of(which * hidden + j * WIDE, WIDE), WIDE)

    def fetch(j, which):
        slot = lax.rem(j, 2)
        return pltpu.make_async_copy(
            weights.at[:, columns(j, which)],
            block_buf.at[slot, which],
            block_sem.at[slot, which],
        )

    for which in range(3):
        fetch(0, which).start()

    @pl.loop(0, hidden // WIDE)
    def _(j):
        slot = lax.rem(j, 2)

        @pl.when(j + 1 < hidden // WIDE)
        def _():
            for which in range(3):
                fetch(j + 1, which).start()

        fetch(j, 0).wait()
        gate = matmul(normed[...], block_buf[slot, 0])
        fetch(j, 1).wait()
        up = matmul(normed[...], block_buf[slot, 1])
        fetch(j, 2).wait()
        act_grad = matmul(ct[...], block_buf[slot, 2])
        logistic = jax.nn.sigmoid(gate)
        silu = gate * logistic
        slope = logistic * (1.0 + gate * (1.0 - logistic))
        made[:, columns(j, 0)] = (silu * up).astype(made.dtype)
        made[:, columns(j, 1)] = (act_grad * up * slope).astype(made.dtype)
        made[:, columns(j, 2)] = (act_grad * silu).astype(made.dtype)

    if swaps:
        swap.end()


def run_ffn(call_id, normed, ct, weights, swaps):
    rows, width = normed.shape
    arrays = [ct] if swaps else []
    vmem = pl.BlockSpec(memory_space=pltpu.VMEM)
    params = dict(collective_id=call_id, has_side_effects=True) if swaps else {}
    return pl.pallas_call(
        functools.partial(ffn_kernel, swaps),
        in_specs=[vmem, vmem, pl.BlockSpec(memory_space=pltpu.HBM)],
        out_specs=[vmem] + [pl.BlockSpec(memory_space=pltpu.HBM)] * len(arrays),
        out_shape=[jax.ShapeDtypeStruct((rows, weights.shape[1]), jnp.bfloat16)]
        + swap_shapes(arrays),
        scratch_shapes=[
            pltpu.VMEM((2, 3, width, WIDE), jnp.bfloat16),
            pltpu.SemaphoreType.DMA((2, 3)),
        ]
        + swap_scratch(arrays),
        compiler_params=pltpu.CompilerParams(vmem_limit_bytes=VMEM_GRANT, **params),
    )(normed, ct, weights)


def ffn_back_kernel(
    n_swaps,
    made,
    ct,
    middle,
    gain,
    out_first,
    out_last,
    weights,
    *refs,
):
    arrays, refs = refs[:n_swaps], refs[n_swaps:]
    middle_low, middle_grad, gain_grad, gated_grad, ffn_part, *refs = refs
    swapped, refs = refs[:n_swaps], refs[n_swaps:]
    part, wide_buf, down_buf, wide_sem, down_sem, *sems = refs
    hidden = made.shape[1] // 3
    blocks = part.shape[1] // WIDE
    group = Group(("tp",), None, None)
    line = LineSum(part, *sems[:5])
    spread = LineSpread(middle_low, *sems[5:7])
    if n_swaps:
        swap = Swap(arrays, swapped, *sems[7:])
        greet([(("tp",), group.others), (PLANE, swap.plane.others)])
        swap.begin()
    else:
        greet([(("tp",), group.others)])

    def fetch(j):
        return pltpu.make_async_copy(
            weights.at[j * WIDE : (j + 1) * WIDE, : 2 * hidden],
            wide_buf.at[j % 2],
            wide_sem.at[j % 2],
        )

    def fetch_down(j):
        return pltpu.make_async_copy(
            weights.at[j * WIDE : (j + 1) * WIDE, 2 * hidden :],
            down_buf.at[j % 2],
            down_sem.at[j % 2],
        )

    fetch(0).start()
    firsts = []
    for j in range(blocks):
        if j + 1 < blocks:
            fetch(j + 1).start()
        else:
            fetch_down(0).start()
        fetch(j).wait()
        columns = slice(j * WIDE, (j + 1) * WIDE)
        part[:, columns] = matmul_nt(made[:, hidden:], wide_buf[j % 2]).astype(part.dtype)
        firsts.append(line.begin(j))
    for j in range(blocks):
        if j + 1 < blocks:
            fetch_down(j + 1).start()
        fetch_down(j).wait()
        ffn_part[:, j * WIDE : (j + 1) * WIDE] = matmul_nt(
            made[:, :hidden], down_buf[j % 2]
        ).astype(ffn_part.dtype)
        line.pass_on(j, firsts[j])
    normed_grad = line.total()
    rows = middle[...]
    scale = inverse_rms(rows)
    gain_grad[...] = jnp.sum(normed_grad * rows * scale, 0, keepdims=True)
    grad = group.own(ct)[...].astype(jnp.float32) + norm_back(
        normed_grad, rows, scale, gain[...].astype(jnp.float32)
    )
    middle_grad[...] = grad
    group.own(middle_low)[...] = grad.astype(middle_low.dtype)
    spread.run()
    half = gated_grad.shape[1] // 2
    share = out_first.shape[1]
    for side, shards in enumerate((out_first, out_last)):
        total = None
        for at in range(shards.shape[0] // half):
            one = matmul_nt(
                middle_low[:, at * share : (at + 1) * share],
                shards[at * half : (at + 1) * half, :],
            )
            total = one if total is None else total + one
        gated_grad[:, side * half : (side + 1) * half] = total
    if n_swaps:
        swap.end()


def ffn_back(call_id, made, ct, middle, gain, out_first, out_last, weights, arrays):
    count = group_size(("tp",))
    vmem = pl.BlockSpec(memory_space=pltpu.VMEM)
    hbm = pl.BlockSpec(memory_space=pltpu.HBM)
    rows, width = ct.shape
    hidden = made.shape[1] // 3
    inner = 2 * out_first.shape[0] // group_size(PLANE)
    low, full = jnp.bfloat16, jnp.float32
    part = jax.ShapeDtypeStruct((rows, width), low)
    dma = pltpu.SemaphoreType.DMA
    return pl.pallas_call(
        functools.partial(ffn_back_kernel, len(arrays)),
        in_specs=[vmem] * 6 + [hbm] + [vmem] * len(arrays),
        out_specs=[vmem] * 5 + [hbm] * len(arrays),
        out_shape=[
            part,
            jax.ShapeDtypeStruct((rows // count, width), full),
            jax.ShapeDtypeStruct((1, width), full),
            jax.ShapeDtypeStruct((rows, inner), full),
            part,
        ]
        + swap_shapes(arrays),
        scratch_shapes=[
            pltpu.VMEM(part.shape, low),
            pltpu.VMEM((2, WIDE, 2 * hidden), low),
            pltpu.VMEM((2, WIDE, hidden), low),
            dma((2,)),
            dma((2,)),
        ]
        + line_sum_scratch(part, width // WIDE)
        + line_spread_scratch()
        + swap_scratch(arrays),
        compiler_params=pltpu.CompilerParams(
            collective_id=call_id, has_side_effects=True, vmem_limit_bytes=VMEM_GRANT
        ),
    )(made, ct, middle, gain, out_first, out_last, weights, *arrays)


def send_on(source, target, send_sem, recv_sem, ctx):
    return pltpu.make_async_remote_copy(
        src_ref=source,
        dst_ref=target,
        send_sem=send_sem,
        recv_sem=recv_sem,
        device_id={"ctx": ctx},
        device_id_type=pl.DeviceIdType.MESH,
    )


def forward_pair_kernel(
    n_state,
    tiles,
    groups,
    blocks,
    seqs,
    step_ref,
    input_ref,
    brow_ref,
    crow_ref,
    rate_ref,
    shard,
    *refs,
):
    prior_ref, mixed_ref, gathered, *refs = refs
    carried, ends, starts, prior_buf, step_held, input_held, mixed_held, *refs = refs
    prior_sem, send_sem, recv_sem, gather_send, gather_recv, local_sem = refs
    place = lax.axis_index("ctx")
    gather = PlaneGather(shard, gathered, gather_send, gather_recv)
    greet([(PLANE, gather.others)])
    gather.begin(local_sem)

    def hand_on(seq):
        return send_on(ends.at[seq], starts.at[seq], send_sem.at[seq], recv_sem.at[seq], 1)

    def store(block):
        slot = lax.rem(block, 2)
        rows = groups * SUB
        return pltpu.make_async_copy(
            prior_buf.at[slot],
            prior_ref.at[pl.ds(pl.multiple_of(block * rows, rows), rows)],
            prior_sem.at[slot],
        )

    def one_sequence(seq):
        @pl.when(place == 0)
        def _():
            carried[...] = jnp.zeros_like(carried)

        @pl.when(place == 1)
        def _():
            hand_on(seq).wait_recv()
            carried[...] = starts[seq]

        @pl.loop(0, blocks)
        def _(inner_block):
            block = seq * blocks + inner_block
            slot = lax.rem(block, 2)

            @pl.when(block >= 2)
            def _():
                store(block - 2).wait()

            def one(turn, states):
                group = block * groups + turn
                states = list(states)
                stage_in(step_ref, group, step_held)
                stage_in(input_ref, group, input_held)
                for at in range(SUB):
                    step = token_row(step_held, at, tiles)
                    drive = step * token_row(input_held, at, tiles)
                    mixed = [None] * 2
                    for n in range(n_state):
                        where = (group * SUB + at) * n_state + n
                        prior_buf[slot, turn * SUB + at, n] = states[n]
                        decay = jnp.exp2(step * rate_ref[n])
                        states[n] = decay * states[n] + drive * brow_ref[where]
                        term = states[n] * crow_ref[where]
                        mixed[n % 2] = term if mixed[n % 2] is None else mixed[n % 2] + term
                    mixed_held[pl.ds(at, tiles, stride=SUB), :] = mixed[0] + mixed[1]
                stage_out(mixed_held, mixed_ref, group)
                return tuple(states)

            states = lax.fori_loop(0, groups, one, tuple(carried[n] for n in range(n_state)))
            for n in range(n_state):
                carried[n] = states[n]
            store(block).start()

        @pl.when(place == 0)
        def _():
            ends[seq] = carried[...]
            hand_on(seq).start()

    for seq in range(seqs):
        one_sequence(seq)
        if seq == 0:
            gather.relay()
            gather.hand_over()
    gather.hand_over_last()
    for block in range(max(0, seqs * blocks - 2), seqs * blocks):
        store(block).wait()

    @pl.when(place == 0)
    def _():
        for seq in range(seqs):
            hand_on(seq).wait_send()

    gather.end()


def scan_forward_pair(
    call_id, step, inputs, b_rows, c_rows, rate, seqs, shard
):
    n_state, tiles, _ = rate.shape
    tokens, inner = step.shape
    all_groups = tokens // SUB
    groups = math.gcd(all_groups // seqs, 4)
    blocks = all_groups // seqs // groups
    vmem = pl.BlockSpec(memory_space=pltpu.VMEM)
    smem = pl.BlockSpec(memory_space=pltpu.SMEM)
    hbm = pl.BlockSpec(memory_space=pltpu.HBM)
    full = jnp.float32
    held = pltpu.VMEM((tiles * SUB, LANE), full)
    boundary = pltpu.VMEM((seqs, n_state, tiles, LANE), full)
    dma = pltpu.SemaphoreType.DMA
    return pl.pallas_call(
        functools.partial(
            forward_pair_kernel, n_state, tiles, groups, blocks, seqs
        ),
        in_specs=[vmem, vmem, smem, smem, vmem, hbm],
        out_specs=[hbm, vmem, hbm],
        out_shape=[
            jax.ShapeDtypeStruct((tokens, n_state, tiles, LANE), full),
            jax.ShapeDtypeStruct(step.shape, full),
            gathered_shape(shard),
        ],
        scratch_shapes=[
            pltpu.VMEM((n_state, tiles, LANE), full),
            boundary,
            boundary,
            pltpu.VMEM((2, groups * SUB, n_state, tiles, LANE), full),
            held,
            held,
            held,
            dma((2,)),
            dma((seqs,)),
            dma((seqs,)),
        ]
        + gather_scratch(),
        compiler_params=pltpu.CompilerParams(
            collective_id=call_id, has_side_effects=True, vmem_limit_bytes=VMEM_GRANT
        ),
    )(step, inputs, b_rows, c_rows, rate, shard)


def backward_pair_kernel(
    n_swaps,
    n_state,
    tiles,
    groups,
    blocks,
    seqs,
    step_ref,
    input_ref,
    ograd_ref,
    brow_ref,
    crow_ref,
    rate_ref,
    picks_ref,
    ffn_part,
    middle,
    prior_ref,
    *refs,
):
    arrays, refs = refs[:n_swaps], refs[n_swaps:]
    step_grad_ref, input_grad_ref, rate_grad_ref, part_ref, *refs = refs
    layer_first, layer_last, *refs = refs
    swapped, refs = refs[:n_swaps], refs[n_swaps:]
    carried, ends, starts, prior_buf, step_held, input_held, ograd_held, *refs = refs
    step_grad_held, input_grad_held, ffn_slots, prior_sem, send_sem, recv_sem, *refs = refs
    tp_send, tp_recv, *refs = refs
    place = lax.axis_index("ctx")
    tp = Group(("tp",), tp_send, tp_recv)
    if n_swaps:
        swap = Swap(arrays, swapped, *refs)
        greet([(PLANE, swap.plane.others), (("tp",), tp.others)])
        swap.begin()
    else:
        greet([(("ctx",), [1 - place]), (("tp",), tp.others)])
    ffn_sent = tp.scatter(ffn_part, ffn_slots, 0)

    def hand_on(seq):
        return send_on(ends.at[seq], starts.at[seq], send_sem.at[seq], recv_sem.at[seq], 0)

    def fetch(turn):
        seq = lax.div(turn, blocks)
        block = seq * blocks + blocks - 1 - lax.rem(turn, blocks)
        slot = lax.rem(turn, 2)
        rows = groups * SUB
        return pltpu.make_async_copy(
            prior_ref.at[pl.ds(pl.multiple_of(block * rows, rows), rows)],
            prior_buf.at[slot],
            prior_sem.at[slot],
        )

    fetch(0).start()
    rate_grad_ref[...] = jnp.zeros_like(rate_grad_ref)

    @pl.when(place == 1)
    def _():
        @pl.loop(0, seqs)
        def _(seq):
            def one(turn, grads):
                group = (seq + 1) * blocks * groups - 1 - turn
                grads = list(grads)
                stage_in(step_ref, group, step_held)
                stage_in(ograd_ref, group, ograd_held)
                for at in range(SUB - 1, -1, -1):
                    step = token_row(step_held, at, tiles)
                    ograd = token_row(ograd_held, at, tiles)
                    for n in range(n_state):
                        row = crow_ref[(group * SUB + at) * n_state + n]
                        grads[n] = jnp.exp2(step * rate_ref[n]) * (grads[n] + ograd * row)
                return tuple(grads)

            zero = jnp.zeros((tiles, LANE), jnp.float32)
            grads = lax.fori_loop(0, blocks * groups, one, (zero,) * n_state)
            for n in range(n_state):
                ends[seq, n] = grads[n]
            hand_on(seq).start()

    @pl.loop(0, seqs)
    def _(seq):
        @pl.when(place == 1)
        def _():
            carried[...] = jnp.zeros_like(carried)

        @pl.when(place == 0)
        def _():
            hand_on(seq).wait_recv()
            carried[...] = starts[seq]

        @pl.loop(0, blocks)
        def _(inner_block):
            turn = seq * blocks + inner_block
            slot = lax.rem(turn, 2)
            first_group = (seq * blocks + blocks - 1 - inner_block) * groups

            @pl.when(turn + 1 < seqs * blocks)
            def _():
                fetch(turn + 1).start()

            fetch(turn).wait()

            def one(back, grads):
                inner_group = groups - 1 - back
                group = first_group + inner_group
                grads = list(grads)
                stage_in(step_ref, group, step_held)
                stage_in(input_ref, group, input_held)
                stage_in(ograd_ref, group, ograd_held)
                for at in range(SUB - 1, -1, -1):
                    step = token_row(step_held, at, tiles)
                    value = token_row(input_held, at, tiles)
                    ograd = token_row(ograd_held, at, tiles)
                    drive = step * value
                    along_b = None
                    along_rate = None
                    brow_parts, crow_parts = [], []
                    for n in range(n_state):
                        where = (group * SUB + at) * n_state + n
                        brow, crow = brow_ref[where], crow_ref[where]
                        rate = rate_ref[n]
                        decay = jnp.exp2(step * rate)
                        grad = ograd * crow + grads[n]
                        kept = decay * prior_buf[slot, inner_group * SUB + at, n]
                        state = kept + drive * brow
                        decay_term = grad * kept
                        grads[n] = decay * grad
                        rate_grad_ref[n] += decay_term * step
                        by_rate, by_brow = decay_term * rate, grad * brow
                        along_rate = by_rate if along_rate is None else along_rate + by_rate
                        along_b = by_brow if along_b is None else along_b + by_brow
                        brow_parts.append(grad * drive)
                        crow_parts.append(ograd * state)
                    step_grad_held[pl.ds(at, tiles, stride=SUB), :] = (
                        along_rate * LN2 + along_b * value
                    )
                    input_grad_held[pl.ds(at, tiles, stride=SUB), :] = along_b * step
                    parts = jnp.concatenate(brow_parts + crow_parts, 0).astype(jnp.bfloat16)
                    part_ref[group * SUB + at] = jnp.dot(
                        picks_ref[...], parts, preferred_element_type=jnp.float32
                    )
                stage_out(step_grad_held, step_grad_ref, group)
                stage_out(input_grad_held, input_grad_ref, group)
                return tuple(grads)

            grads = lax.fori_loop(0, groups, one, tuple(carried[n] for n in range(n_state)))
            for n in range(n_state):
                carried[n] = grads[n]

    finish(ffn_sent)
    layer_rows = (middle[...] + tp.total(ffn_part, ffn_slots)).astype(layer_first.dtype)
    half = layer_first.shape[1]
    layer_first[...], layer_last[...] = layer_rows[:, :half], layer_rows[:, half:]

    @pl.when(place == 1)
    def _():
        @pl.loop(0, seqs)
        def _(seq):
            hand_on(seq).wait_send()

    if n_swaps:
        swap.end()


def scan_backward_pair(
    call_id, prior, step, inputs, ograd, b_rows, c_rows, rate, seqs, ffn_part, middle, arrays
):
    n_state, tiles, _ = rate.shape
    tokens, inner = step.shape
    all_groups = tokens // SUB
    groups = math.gcd(all_groups // seqs, 4)
    blocks = all_groups // seqs // groups
    tp_count = group_size(("tp",))
    vmem = pl.BlockSpec(memory_space=pltpu.VMEM)
    smem = pl.BlockSpec(memory_space=pltpu.SMEM)
    hbm = pl.BlockSpec(memory_space=pltpu.HBM)
    full = jnp.float32
    held = pltpu.VMEM((tiles * SUB, LANE), full)
    boundary = pltpu.VMEM((seqs, n_state, tiles, LANE), full)
    dma = pltpu.SemaphoreType.DMA
    layer_half = jax.ShapeDtypeStruct((middle.shape[0], middle.shape[1] // 2), jnp.bfloat16)
    picks = jnp.repeat(jnp.eye(2 * n_state, dtype=jnp.bfloat16), tiles, 1)
    return pl.pallas_call(
        functools.partial(
            backward_pair_kernel, len(arrays), n_state, tiles, groups, blocks, seqs
        ),
        in_specs=[vmem] * 3 + [smem] * 2 + [vmem] * 4 + [hbm] + [vmem] * len(arrays),
        out_specs=[vmem] * 6 + [hbm] * len(arrays),
        out_shape=[
            jax.ShapeDtypeStruct(step.shape, full),
            jax.ShapeDtypeStruct(step.shape, full),
            jax.ShapeDtypeStruct(rate.shape, full),
            jax.ShapeDtypeStruct((tokens, 2 * n_state, LANE), full),
            layer_half,
            layer_half,
        ]
        + swap_shapes(arrays),
        scratch_shapes=[
            pltpu.VMEM((n_state, tiles, LANE), full),
            boundary,
            boundary,
            pltpu.VMEM((2, groups * SUB, n_state, tiles, LANE), full),
        ]
        + [held] * 5
        + [
            slots_for(ffn_part, tp_count),
            dma((2,)),
            dma((seqs,)),
            dma((seqs,)),
            dma((1, tp_count - 1)),
            dma((1, tp_count - 1)),
        ]
        + swap_scratch(arrays),
        compiler_params=pltpu.CompilerParams(
            collective_id=call_id, has_side_effects=True, vmem_limit_bytes=VMEM_GRANT
        ),
    )(step, inputs, ograd, b_rows, c_rows, rate, picks, ffn_part, middle, prior, *arrays)


class PlaneGather:
    def __init__(self, own, gathered, send_sem, recv_sem):
        self.own, self.gathered = own, gathered
        self.send_sem, self.recv_sem = send_sem, recv_sem
        self.dp, self.ctx = lax.axis_index("dp"), lax.axis_index("ctx")
        self.n_dp, self.n_ctx = lax.axis_size("dp"), lax.axis_size("ctx")
        self.hands_on = relayed()
        self.count = self.n_dp * self.n_ctx
        self.me = self.dp * self.n_ctx + self.ctx
        self.others = [lax.rem(self.me + hop, self.count) for hop in range(1, self.count)]
        self.copies = {}
        if self.hands_on:
            core = lax.rem(self.dp, 2)
            over_core = self.dp + 1 - 2 * core
            over_y = lax.rem(self.dp + 2, 4)
            over_x = 1 - self.ctx
            self.core = {"dp": over_core, "ctx": self.ctx}
            self.at_x = {"dp": self.dp, "ctx": over_x}
            self.at_y = {"dp": over_y, "ctx": self.ctx}
            self.from_x = self.dp * 2 + over_x
            self.from_y = over_y * 2 + self.ctx
            self.across = over_y * 2 + over_x

    def part(self, owner, half):
        rows = self.gathered.shape[0] // self.count
        start, size = owner * rows, rows
        if half is not None:
            size = rows // 2
            start = start + half * size
        return self.gathered.at[pl.ds(pl.multiple_of(start, size), size), :]

    def send(self, which, owner, half, where):
        target = self.part(owner, half)
        source = target
        if owner is self.me:
            rows = self.own.shape[0]
            source = self.own
            if half is not None:
                source = self.own.at[pl.ds(half * (rows // 2), rows // 2), :]
        self.copies[which] = sent(
            source, target, self.send_sem.at[which], self.recv_sem.at[which], where
        )

    def arrived(self, *which):
        for one in which:
            self.copies[one].wait_recv()

    def begin(self, local_sem):
        self.local = pltpu.make_async_copy(self.own, self.part(self.me, None), local_sem)
        self.local.start()
        if not self.hands_on:
            for hop, other in enumerate(self.others):
                self.send(hop, self.me, None, device_at(PLANE, other))
            return
        self.send(0, self.me, 1, self.at_x)
        self.send(1, self.me, 0, self.at_y)
        self.send(2, self.me, None, self.core)
        self.send(3, self.me, 0, self.at_x)
        self.send(4, self.me, 1, self.at_y)

    def relay(self):
        if not self.hands_on:
            return
        self.arrived(0, 1)
        self.send(5, self.from_x, 1, self.at_y)
        self.send(6, self.from_y, 0, self.at_x)
        self.send(7, self.from_x, 1, self.core)
        self.send(8, self.from_y, 0, self.core)

    def hand_over(self):
        if not self.hands_on:
            return
        self.arrived(3, 4)
        self.send(9, self.from_x, 0, self.core)
        self.send(10, self.from_y, 1, self.core)

    def hand_over_last(self):
        if not self.hands_on:
            return
        self.arrived(5, 6)
        self.send(11, self.across, 1, self.core)
        self.send(12, self.across, 0, self.core)

    def end(self):
        if self.hands_on:
            self.arrived(2, 7, 8, 9, 10, 11, 12)
        else:
            self.arrived(*range(self.count - 1))
        for copy in self.copies.values():
            copy.wait_send()
        self.local.wait()


def relayed():
    return lax.axis_size("dp") == 4 and lax.axis_size("ctx") == 2


def gather_sems():
    count = 13 if relayed() else group_size(PLANE) - 1
    return pltpu.SemaphoreType.DMA((count,))


WIDE = 512


def products(source, first, last, dot, target, block_buf, block_sem, out_buf, out_sem):
    def fetch(j, slot):
        columns = pl.ds(pl.multiple_of(j * WIDE, WIDE), WIDE)
        return pltpu.make_async_copy(
            source.at[:, columns], block_buf.at[slot], block_sem.at[slot]
        )

    def store(j, slot):
        return pltpu.make_async_copy(out_buf.at[slot], target(j), out_sem.at[slot])

    fetch(first, first % 2).start()

    @pl.loop(first, last)
    def _(j):
        slot = lax.rem(j, 2)

        @pl.when(j + 1 < last)
        def _():
            fetch(j + 1, 1 - slot).start()

        fetch(j, slot).wait()

        @pl.when(j >= first + 2)
        def _():
            store(j - 2, slot).wait()

        out_buf[slot] = dot(block_buf[slot])
        store(j, slot).start()

    for j in range(max(first, last - 2), last):
        store(j, j % 2).wait()


SMALL_ROWS = 32
GAIN_ROWS = 16


def tail_kernel(
    swaps,
    conv_grad,
    gate_grad,
    convkern,
    convbias,
    stepbias,
    decaylog,
    skipgain,
    ffngain,
    layer_first,
    layer_rows,
    middle_low,
    step_low,
    pre_low,
    select_low,
    scan_in,
    tokens,
    middle_grad,
    gain_row,
    in_conv,
    in_gate,
    one_cols,
    two_cols,
    ct_cols,
    middle_cols,
    ffn_all,
    gated_all,
    tokens_grad,
    layer_out,
    vectors_sum,
    step_sum,
    select_sum,
    gains,
    mix_all,
    grad_inproj,
    grad_outproj,
    grad_gateup,
    grad_downproj,
    mix_own,
    normed_part,
    small,
    small_sum,
    small_slots,
    gain_slots,
    gain_own,
    vectors_own,
    cols,
    in_buf,
    block_buf,
    wide_buf,
    tall_buf,
    cols_sem,
    in_sem,
    block_sem,
    wide_sem,
    tall_sem,
    tp_send,
    tp_recv,
    plane_send,
    plane_recv,
    gather_send,
    gather_recv,
    local_sem,
    *sems,
):
    inner = conv_grad.shape[1]
    hidden = ffn_all.shape[1] // 3
    width = tokens.shape[1]
    rank = step_low.shape[1]
    tp = Group(("tp",), tp_send, tp_recv)
    plane = Group(PLANE, plane_send, plane_recv)
    line = LineSum(normed_part, *sems[:5])
    tokens_spread = LineSpread(tokens_grad, *sems[5:7])
    layer_last = layer_out.at[:, width // 2 :]
    layer_spread = LineSpread(layer_last, *sems[7:9])
    swap_sems = sems[9:]
    gather = PlaneGather(mix_own, mix_all, gather_send, gather_recv)
    sources = (one_cols, two_cols, ct_cols) if swaps else (one_cols, two_cols, ct_cols, middle_cols)
    loads = [
        pltpu.make_async_copy(source, cols.at[at], cols_sem.at[at])
        for at, source in enumerate(sources)
    ]
    if swaps:
        swap = Swap([middle_low], [cols.at[3]], *swap_sems)

    def fetch(j):
        slot = j % 2
        rows = slice(j * WIDE, (j + 1) * WIDE)
        return [
            pltpu.make_async_copy(source.at[rows, :], in_buf.at[slot, at], in_sem.at[slot, at])
            for at, source in enumerate((in_conv, in_gate))
        ]

    for copy in fetch(0) + loads:
        copy.start()
    mix_own[:, :inner] = conv_grad[...]
    mix_own[:, inner:] = gate_grad[...]
    greet([(("tp",), tp.others), (PLANE, plane.others)])
    gather.begin(local_sem)

    small[...] = jnp.zeros_like(small)
    vectors_own[...] = jnp.zeros_like(vectors_own)
    at = 0
    for vector in (convkern, convbias, stepbias, decaylog, skipgain):
        vectors_own[at : at + vector.shape[0], :] = vector[...]
        at += vector.shape[0]
    at = SMALL_ROWS - GAIN_ROWS + 10
    for row in range(width // inner):
        vectors_own[at + row : at + row + 1, :] = ffngain[:, row * inner : (row + 1) * inner]
    hidden_in = tokens[...].astype(jnp.float32)
    unit_rows = hidden_in * inverse_rms(hidden_in)
    blocks = width // WIDE
    firsts = []
    for j in range(blocks):
        if j + 1 < blocks:
            for copy in fetch(j + 1):
                copy.start()
        finish(fetch(j))
        columns = slice(j * WIDE, (j + 1) * WIDE)
        block = matmul_nt(conv_grad[...], in_buf[j % 2, 0]) + matmul_nt(
            gate_grad[...], in_buf[j % 2, 1]
        )
        normed_part[:, columns] = block.astype(normed_part.dtype)
        firsts.append(line.begin(j))
        gain_grad = jnp.sum(block * unit_rows[:, columns], 0, keepdims=True)
        row, at = divmod(j * WIDE, inner)
        row += SMALL_ROWS - GAIN_ROWS + 8
        vectors_own[row : row + 1, at : at + WIDE] = gain_grad
    layer_out[:, : width // 2] = layer_first[...]
    rows_of(layer_last, tp.me, tp.count)[...] = layer_rows[...]
    layer_spread.begin()
    small[:SMALL_ROWS, :] = vectors_own[...].astype(small.dtype)
    small[SMALL_ROWS : SMALL_ROWS + rank, :] = matmul_tn(step_low[...], pre_low[...]).astype(
        small.dtype
    )
    selected = select_sum.shape[0]
    small[SMALL_ROWS + rank : SMALL_ROWS + rank + selected, :] = matmul_tn(
        select_low[...], scan_in[...]
    )[:selected].astype(small.dtype)
    small_sent = plane.scatter(small, small_slots, 0)
    line.pass_all(firsts)

    def flat(at):
        return lambda block: matmul_tn(cols[at], block)

    def tall(at):
        return lambda block: matmul_tn(block, cols[at])

    def side_by_side(ref, first):
        per = ref.shape[2] // WIDE

        def target(j):
            at = j - first
            columns = pl.ds(pl.multiple_of(lax.rem(at, per) * WIDE, WIDE), WIDE)
            return ref.at[lax.div(at, per), :, columns]

        return target

    def one_above_other(ref):
        return lambda j: ref.at[pl.ds(pl.multiple_of(j * WIDE, WIDE), WIDE), :]

    wide = (block_buf, block_sem, wide_buf, wide_sem)
    high = (block_buf, block_sem, tall_buf, tall_sem)
    down_end = hidden // WIDE
    gu_end = 3 * hidden // WIDE
    finish(loads)
    products(ffn_all, 0, down_end, tall(2), one_above_other(grad_downproj), *high)
    gather.relay()
    products(ffn_all, down_end, gu_end, flat(1), side_by_side(grad_gateup, down_end), *wide)
    gather.hand_over()
    finish(small_sent)
    plane.own(small_sum)[...] = plane.total(small, small_slots).astype(small_sum.dtype)
    small_sent = plane.spread(small_sum, 1)
    if swaps:
        swap.begin()
    layer_spread.pass_on()
    hidden_in = tp.own(tokens)[...].astype(jnp.float32)
    tp.own(tokens_grad)[...] = (
        middle_grad[...]
        + norm_back(
            line.total(),
            hidden_in,
            inverse_rms(hidden_in),
            gain_row[...].astype(jnp.float32),
        )
    ).astype(tokens_grad.dtype)
    tokens_spread.begin()
    gather.hand_over_last()
    gather.end()
    products(mix_all, 0, 2 * inner // WIDE, flat(0), side_by_side(grad_inproj, 0), *wide)
    tokens_spread.pass_on()
    finish(small_sent)
    gain_own[...] = small_sum[SMALL_ROWS - GAIN_ROWS : SMALL_ROWS, :].astype(jnp.float32)
    gain_sent = [tp.one(gain_own, gain_slots.at[hop], 0, hop) for hop in range(tp.count - 1)]
    vectors_sum[...] = small_sum[:SMALL_ROWS, :].astype(jnp.float32)
    step_sum[...] = small_sum[SMALL_ROWS : SMALL_ROWS + rank, :].astype(jnp.float32)
    select_sum[...] = small_sum[SMALL_ROWS + rank : SMALL_ROWS + rank + selected, :].astype(
        jnp.float32
    )
    if swaps:
        swap.end()
    products(gated_all, 0, inner // WIDE, tall(3), one_above_other(grad_outproj), *high)
    finish(gain_sent)
    total = gain_own[...]
    for hop in range(tp.count - 1):
        total = total + gain_slots[hop]
    gains[...] = total
    tokens_spread.end()
    layer_spread.end()


def run_tail(
    call_id,
    selected,
    swaps,
    conv_grad,
    gate_grad,
    vectors,
    layer_first,
    layer_rows,
    middle_low,
    step_low,
    pre_low,
    select_low,
    scan_in,
    tokens,
    middle_grad,
    gain_row,
    in_conv,
    in_gate,
    one_cols,
    two_cols,
    ct_cols,
    middle_cols,
    ffn_all,
    gated_all,
):
    rows, inner = conv_grad.shape
    rank = step_low.shape[1]
    hidden = ffn_all.shape[1] // 3
    width = tokens.shape[1]
    share = one_cols.shape[1]
    all_rows = ffn_all.shape[0]
    tp_count, plane_count = group_size(("tp",)), group_size(PLANE)
    low, full = jnp.bfloat16, jnp.float32
    vmem = pl.BlockSpec(memory_space=pltpu.VMEM)
    hbm = pl.BlockSpec(memory_space=pltpu.HBM)
    dma = pltpu.SemaphoreType.DMA
    small_rows = SMALL_ROWS + rank + selected
    small = jax.ShapeDtypeStruct((small_rows + -small_rows % (16 * plane_count), inner), low)
    part = jax.ShapeDtypeStruct((rows, width), low)
    return pl.pallas_call(
        functools.partial(tail_kernel, swaps),
        in_specs=[vmem] * 18 + [hbm] * 8,
        out_specs=[vmem] * 6 + [hbm] * 5,
        out_shape=[
            jax.ShapeDtypeStruct(tokens.shape, low),
            jax.ShapeDtypeStruct(tokens.shape, low),
            jax.ShapeDtypeStruct((SMALL_ROWS, inner), full),
            jax.ShapeDtypeStruct((rank, inner), full),
            jax.ShapeDtypeStruct((selected, inner), full),
            jax.ShapeDtypeStruct((GAIN_ROWS, inner), full),
            jax.ShapeDtypeStruct((all_rows, 2 * inner), low),
            jax.ShapeDtypeStruct((2, share, inner), full),
            jax.ShapeDtypeStruct((inner, share), full),
            jax.ShapeDtypeStruct((2, share, hidden), full),
            jax.ShapeDtypeStruct((hidden, share), full),
        ],
        scratch_shapes=[
            pltpu.VMEM((rows, 2 * inner), low),
            pltpu.VMEM(part.shape, low),
            pltpu.VMEM(small.shape, low),
            pltpu.VMEM(small.shape, low),
            slots_for(small, plane_count),
            pltpu.VMEM((tp_count - 1, GAIN_ROWS, inner), full),
            pltpu.VMEM((GAIN_ROWS, inner), full),
            pltpu.VMEM((SMALL_ROWS, inner), full),
            pltpu.VMEM((4, all_rows, share), low),
            pltpu.VMEM((2, 2, WIDE, inner), low),
            pltpu.VMEM((2, all_rows, WIDE), low),
            pltpu.VMEM((2, share, WIDE), full),
            pltpu.VMEM((2, WIDE, share), full),
            dma((4,)),
            dma((2, 2)),
            dma((2,)),
            dma((2,)),
            dma((2,)),
            dma((1, tp_count - 1)),
            dma((1, tp_count - 1)),
            dma((2, plane_count - 1)),
            dma((2, plane_count - 1)),
        ]
        + gather_scratch()
        + line_sum_scratch(part, width // WIDE)
        + line_spread_scratch() * 2
        + (swap_scratch([tokens]) if swaps else []),
        compiler_params=pltpu.CompilerParams(
            collective_id=call_id, has_side_effects=True, vmem_limit_bytes=VMEM_GRANT
        ),
    )(
        conv_grad,
        gate_grad,
        *vectors,
        layer_first,
        layer_rows,
        middle_low,
        step_low,
        pre_low,
        select_low,
        scan_in,
        tokens,
        middle_grad,
        gain_row,
        in_conv,
        in_gate,
        one_cols,
        two_cols,
        ct_cols,
        middle_cols,
        ffn_all,
        gated_all,
    )


def head_kernel(
    tokens,
    gain,
    in_conv,
    in_gate,
    conv_in,
    gate_mix,
    conv_all,
    gate_all,
    normed,
    block_buf,
    block_sem,
    *sems,
):
    conv = PlaneGather(in_conv, conv_all, *sems[:2])
    gate = PlaneGather(in_gate, gate_all, *sems[3:5])
    greet([(PLANE, conv.others)])
    conv.begin(sems[2])
    gate.begin(sems[5])
    hidden_in = tokens[...].astype(jnp.float32)
    normed[...] = (hidden_in * inverse_rms(hidden_in) * gain[...].astype(jnp.float32)).astype(
        normed.dtype
    )
    conv.relay()
    conv.hand_over()
    gate.relay()
    conv.hand_over_last()
    gate.hand_over()
    conv.end()
    product_in_blocks(normed, conv_all, conv_in, block_buf, block_sem)
    gate.hand_over_last()
    gate.end()
    product_in_blocks(normed, gate_all, gate_mix, block_buf, block_sem)


def run_head(call_id, tokens, gain, inproj):
    rows, width = tokens.shape
    inner = inproj.shape[2]
    low = jnp.bfloat16
    vmem = pl.BlockSpec(memory_space=pltpu.VMEM)
    hbm = pl.BlockSpec(memory_space=pltpu.HBM)
    return pl.pallas_call(
        head_kernel,
        in_specs=[vmem] * 2 + [hbm] * 2,
        out_specs=[vmem] * 2 + [hbm] * 2,
        out_shape=[
            jax.ShapeDtypeStruct((rows, inner), low),
            jax.ShapeDtypeStruct((rows, inner), jnp.float32),
            jax.ShapeDtypeStruct((width, inner), low),
            jax.ShapeDtypeStruct((width, inner), low),
        ],
        scratch_shapes=[
            pltpu.VMEM((rows, width), low),
            pltpu.VMEM((2, width, WIDE), low),
            pltpu.SemaphoreType.DMA((2,)),
        ]
        + gather_scratch() * 2,
        compiler_params=pltpu.CompilerParams(
            collective_id=call_id, has_side_effects=True, vmem_limit_bytes=VMEM_GRANT
        ),
    )(tokens, gain, inproj[0], inproj[1])


def per_device(
    tokens,
    mixgain,
    inproj,
    convkern,
    convbias,
    selproj,
    stepproj,
    stepbias,
    decaylog,
    skipgain,
    outproj,
    ffngain,
    gateup,
    downproj,
    cotangent,
):
    seqs, span, width = tokens.shape
    rows = seqs * span
    taps, inner = convkern.shape
    rank = stepproj.shape[0]
    n_state = decaylog.shape[1]
    tiles = inner // LANE
    gain_mix = mixgain.astype(jnp.float32)
    kernel = convkern.astype(jnp.float32)
    kernel_bias = convbias.astype(jnp.float32)
    step_bias = stepbias.astype(jnp.float32)
    skip_weight = skipgain.astype(jnp.float32)
    decay_rate = -jnp.exp(jnp.transpose(decaylog.astype(jnp.float32)))
    rate = (decay_rate * LOG2E).reshape(n_state, tiles, LANE)

    gain_mix_row, gain_ffn_row = mixgain.reshape(1, width), ffngain.reshape(1, width)
    low = jnp.bfloat16

    tokens_rows = tokens.reshape(rows, width)
    ct_low = cotangent.reshape(rows, width)
    swap_now = swaps_in_kernels(width)
    ffn_pack = gathered_rows(
        jnp.concatenate([gateup[0], gateup[1], jnp.transpose(downproj)], 1)
    )
    conv_in, gate_mix, in_conv, in_gate = run_head(5, tokens_rows, gain_mix_row, inproj)
    hidden_in = tokens_rows.astype(jnp.float32)
    scale_one = inverse_rms(hidden_in)
    normed_one = (hidden_in * scale_one * gain_mix).astype(low)

    conv_seqs = conv_in.reshape(seqs, span, inner)
    rim_rows = passed_along(conv_seqs[:, span - (taps - 1) :], "ctx", 1)
    padded_in = jnp.concatenate([rim_rows, conv_seqs], 1).astype(jnp.float32)
    conv_out = kernel_bias[None, None]
    for offset in range(taps):
        conv_out = conv_out + kernel[offset][None, None] * padded_in[:, offset : offset + span]
    conv_out = conv_out.reshape(rows, inner)
    scan_in = jax.nn.silu(conv_out).astype(low)
    scan_float = scan_in.astype(jnp.float32)
    columns = selproj.shape[1]
    select_width = -(-columns // LANE) * LANE
    select_weights = jnp.pad(selproj, ((0, 0), (0, select_width - columns)))
    select_cols, out_first = run_select(0, matmul(scan_in, select_weights), outproj[: inner // 2])

    def columns_of(swapped, array):
        if not swapped:
            return swapped_columns(array)
        return swapped[0].reshape(-1, swapped[0].shape[-1])

    step_low = select_cols[:, :rank].astype(low)
    b_rows = select_cols[:, rank : rank + n_state].reshape(-1)
    c_rows = select_cols[:, rank + n_state : columns].reshape(-1)
    step_pre = matmul(step_low, stepproj) + step_bias[None]
    step_size = jax.nn.softplus(step_pre)
    in_pairs = lax.axis_size("ctx") == 2
    if in_pairs:
        prior, scan_out, out_last = scan_forward_pair(
            6,
            step_size,
            scan_float,
            b_rows,
            c_rows,
            rate,
            seqs,
            outproj[inner // 2 :],
        )
    else:
        span_decay = jnp.exp(
            decay_rate[None] * jnp.sum(step_size.reshape(seqs, span, inner), 1)[:, None]
        ).reshape(seqs, n_state, tiles, LANE)
        ends = scan_ends(step_size, scan_float, b_rows, rate, seqs, False)
        start = from_earlier(ends, span_decay, 1)
        prior, scan_out = scan_forward(start, step_size, scan_float, b_rows, c_rows, rate, seqs)
        out_last = gathered_rows(outproj[inner // 2 :])
    mixer_core = scan_out + skip_weight[None] * scan_float
    gate_sig = jax.nn.silu(gate_mix)
    gated = (mixer_core * gate_sig).astype(low)
    normed_two, middle, gated_all, *swapped = mixer_out(
        1,
        gated,
        out_first,
        out_last,
        tokens_rows,
        gain_ffn_row,
        [normed_one] if swap_now else [],
    )
    normed_one_cols = columns_of(swapped, normed_one)
    made, *swapped = run_ffn(8, normed_two, ct_low, ffn_pack, swap_now)
    ct_cols = columns_of(swapped, ct_low)
    ffn_all = gathered_rows(made)
    middle_low, middle_grad, ffngain_part, gated_grad, ffn_part, *swapped = ffn_back(
        2,
        made,
        ct_low,
        middle,
        gain_ffn_row,
        out_first,
        out_last,
        ffn_pack,
        [normed_two] if swap_now else [],
    )
    normed_two_cols = columns_of(swapped, normed_two)
    core_grad = gated_grad * gate_sig
    gate_mix_grad = (gated_grad * mixer_core * silu_slope(gate_mix)).astype(low)
    grad_skipgain = jnp.sum(core_grad * scan_float, 0)
    if in_pairs:
        step_grad, input_grad, rate_grad, parts, *layer_rows = scan_backward_pair(
            7,
            prior,
            step_size,
            scan_float,
            core_grad,
            b_rows,
            c_rows,
            rate,
            seqs,
            ffn_part,
            middle,
            [],
        )
    else:
        back_ends = scan_ends(step_size, core_grad, c_rows, rate, seqs, True)
        end_grad = from_earlier(back_ends, span_decay, -1)
        step_grad, input_grad, rate_grad, parts = scan_backward(
            end_grad, prior, step_size, scan_float, core_grad, b_rows, c_rows, rate, seqs
        )
        ffn_sum = lax.psum_scatter(ffn_part, "tp", scatter_dimension=0, tiled=True)
        layer_rows = jnp.split((middle + ffn_sum.astype(jnp.float32)).astype(low), 2, 1)
    grad_decaylog = rate_grad.reshape(n_state, inner) * decay_rate
    pre_grad = step_grad * jax.nn.sigmoid(step_pre)
    grad_stepbias = jnp.sum(pre_grad, 0)
    pre_low = pre_grad.astype(low)
    select_part = jnp.concatenate(
        [
            matmul_nt(pre_low, stepproj),
            jnp.sum(parts, -1),
            jnp.zeros((rows, select_width - columns), jnp.float32),
        ],
        1,
    ).astype(low)
    select_low, layer_first = sum_over_tp(3, select_part, layer_rows[0])
    scan_in_grad = (
        core_grad * skip_weight[None]
        + input_grad
        + matmul_nt(select_low, select_weights)
    )
    conv_grad = scan_in_grad * silu_slope(conv_out)
    grad_convbias = jnp.sum(conv_grad, 0)
    conv_grad_seqs = conv_grad.reshape(seqs, span, inner)
    padded_grad = jnp.zeros(padded_in.shape, jnp.float32)
    kernel_rows = []
    for offset in range(taps):
        kernel_rows.append(jnp.sum(conv_grad_seqs * padded_in[:, offset : offset + span], (0, 1)))
        padded_grad = padded_grad + jnp.pad(
            kernel[offset][None, None] * conv_grad_seqs,
            ((0, 0), (offset, taps - 1 - offset), (0, 0)),
        )
    grad_convkern = jnp.stack(kernel_rows)
    returned = passed_along(padded_grad[:, : taps - 1], "ctx", -1)
    conv_in_grad = (
        (padded_grad[:, taps - 1 :] + jnp.pad(returned, ((0, 0), (span - taps + 1, 0), (0, 0))))
        .astype(low)
        .reshape(rows, inner)
    )
    vectors = [
        grad_convkern,
        grad_convbias[None],
        grad_stepbias[None],
        grad_decaylog,
        grad_skipgain[None],
        ffngain_part,
    ]
    (
        tokens_grad,
        layer_out,
        vectors,
        grad_stepproj,
        grad_selproj,
        gains,
        _,
        grad_inproj,
        grad_outproj,
        grad_gateup,
        grad_downproj,
    ) = run_tail(
        4,
        columns,
        swap_now,
        conv_in_grad,
        gate_mix_grad,
        vectors,
        layer_first,
        layer_rows[1],
        middle_low,
        step_low,
        pre_low,
        select_low,
        scan_in,
        tokens_rows,
        middle_grad,
        gain_mix_row,
        in_conv,
        in_gate,
        normed_one_cols,
        normed_two_cols,
        ct_cols,
        normed_two_cols if swap_now else swapped_columns(middle_low),
        ffn_all,
        gated_all,
    )
    at = taps + 2
    return (
        layer_out.reshape(tokens.shape),
        tokens_grad.reshape(tokens.shape),
        gains[8:10].reshape(width),
        grad_inproj,
        vectors[:taps],
        vectors[taps],
        jnp.transpose(grad_selproj),
        grad_stepproj,
        vectors[taps + 1],
        jnp.transpose(vectors[at : at + n_state]),
        vectors[at + n_state],
        grad_outproj,
        gains[10:12].reshape(width),
        grad_gateup,
        grad_downproj,
    )


def solution(mesh):
    in_specs = (
        P("dp", "ctx", None),
        P(),
        P(None, ("dp", "ctx"), "tp"),
        P(None, "tp"),
        P("tp"),
        P("tp", None),
        P(None, "tp"),
        P("tp"),
        P("tp", None),
        P("tp"),
        P("tp", ("dp", "ctx")),
        P(),
        P(None, ("dp", "ctx"), "tp"),
        P("tp", ("dp", "ctx")),
        P("dp", "ctx", None),
    )
    out_specs = (
        P("dp", "ctx", None),
        P("dp", "ctx", None),
        P(),
        P(None, ("dp", "ctx"), "tp"),
        P(None, "tp"),
        P("tp"),
        P("tp", None),
        P(None, "tp"),
        P("tp"),
        P("tp", None),
        P("tp"),
        P("tp", ("dp", "ctx")),
        P(),
        P(None, ("dp", "ctx"), "tp"),
        P("tp", ("dp", "ctx")),
    )
    return jax.shard_map(
        per_device, mesh=mesh, in_specs=in_specs, out_specs=out_specs, check_vma=False
    )
```

```python
import functools
import math

import jax
import jax.numpy as jnp
from jax import lax
from jax.experimental import pallas as pl
from jax.experimental.pallas import tpu as pltpu
from jax.sharding import PartitionSpec as P

EPSILON = 1e-05
LOG2E = math.log2(math.e)
LN2 = math.log(2.0)
SUB = 8
LANE = 128
VMEM_GRANT = 60 * 2**20
PLANE = ("dp", "ctx")


def passed_along(value, axis, steps):
    count = lax.axis_size(axis)
    first, last = (max(0, -steps), min(count, count - steps))
    return lax.ppermute(value, axis, [(source, source + steps) for source in range(first, last)])


def matmul(left, right):
    return jnp.dot(left, right, preferred_element_type=jnp.float32)


def matmul_nt(left, right):
    return lax.dot_general(
        left, right, (((1,), (1,)), ((), ())), preferred_element_type=jnp.float32
    )


def matmul_tn(left, right):
    return lax.dot_general(
        left, right, (((0,), (0,)), ((), ())), preferred_element_type=jnp.float32
    )


def inverse_rms(values):
    return lax.rsqrt(jnp.mean(values * values, -1, keepdims=True) + EPSILON)


def silu_slope(values):
    logistic = jax.nn.sigmoid(values)
    return logistic * (1.0 + values * (1.0 - logistic))


def norm_back(grad_norm, values, scale, gain):
    scaled_grad = grad_norm * gain
    unit_rows = values * scale
    return scale * (scaled_grad - unit_rows * jnp.mean(scaled_grad * unit_rows, -1, keepdims=True))


def stage_in(ref, group, held):
    for tile in range(held.shape[0] // SUB):
        held[pl.ds(tile * SUB, SUB), :] = ref[
            pl.ds(pl.multiple_of(group * SUB, SUB), SUB), pl.ds(tile * LANE, LANE)
        ]


def stage_out(held, ref, group):
    for tile in range(held.shape[0] // SUB):
        ref[pl.ds(pl.multiple_of(group * SUB, SUB), SUB), pl.ds(tile * LANE, LANE)] = held[
            pl.ds(tile * SUB, SUB), :
        ]


def token_row(held, at, tiles):
    return held[pl.ds(at, tiles, stride=SUB), :]


def ends_kernel(
    n_state,
    tiles,
    groups,
    reverse,
    step_ref,
    drive_ref,
    rows_ref,
    rate_ref,
    end_ref,
    step_held,
    drive_held,
):
    base = pl.program_id(0) * groups * SUB * n_state
    rates = [rate_ref[n] for n in range(n_state)]

    def one(turn, states):
        group = groups - 1 - turn if reverse else turn
        order = range(SUB - 1, -1, -1) if reverse else range(SUB)
        states = list(states)
        stage_in(step_ref, group, step_held)
        stage_in(drive_ref, group, drive_held)
        for at in order:
            step = token_row(step_held, at, tiles)
            drive = token_row(drive_held, at, tiles)
            if not reverse:
                drive = drive * step
            for n in range(n_state):
                row = rows_ref[base + (group * SUB + at) * n_state + n]
                decay = jnp.exp2(step * rates[n])
                if reverse:
                    states[n] = decay * (states[n] + drive * row)
                else:
                    states[n] = decay * states[n] + drive * row
        return tuple(states)

    zero = jnp.zeros((tiles, LANE), jnp.float32)
    states = lax.fori_loop(0, groups, one, (zero,) * n_state)
    for n in range(n_state):
        end_ref[0, n] = states[n]


def scan_ends(step, drive, rows, rate, seqs, reverse):
    n_state, tiles, _ = rate.shape
    groups = step.shape[0] // seqs // SUB
    rows_spec = pl.BlockSpec((groups * SUB, tiles * LANE), lambda s: (s, 0))
    held = pltpu.VMEM((tiles * SUB, LANE), jnp.float32)
    return pl.pallas_call(
        functools.partial(ends_kernel, n_state, tiles, groups, reverse),
        grid=(seqs,),
        in_specs=[
            rows_spec,
            rows_spec,
            pl.BlockSpec(memory_space=pltpu.SMEM),
            pl.BlockSpec((n_state, tiles, LANE), lambda s: (0, 0, 0)),
        ],
        out_specs=pl.BlockSpec((1, n_state, tiles, LANE), lambda s: (s, 0, 0, 0)),
        out_shape=jax.ShapeDtypeStruct((seqs, n_state, tiles, LANE), jnp.float32),
        scratch_shapes=[held, held],
        compiler_params=pltpu.CompilerParams(vmem_limit_bytes=VMEM_GRANT),
    )(step, drive, rows, rate)


def forward_kernel(
    n_state,
    tiles,
    groups,
    blocks,
    start_ref,
    step_ref,
    input_ref,
    brow_ref,
    crow_ref,
    rate_ref,
    prior_ref,
    mixed_ref,
    carried,
    step_held,
    input_held,
    mixed_held,
):
    base = (pl.program_id(0) * blocks + pl.program_id(1)) * groups * SUB * n_state

    @pl.when(pl.program_id(1) == 0)
    def _():
        carried[...] = start_ref[0]

    def one(group, states):
        states = list(states)
        stage_in(step_ref, group, step_held)
        stage_in(input_ref, group, input_held)
        for at in range(SUB):
            step = token_row(step_held, at, tiles)
            drive = step * token_row(input_held, at, tiles)
            mixed = [None] * 2
            for n in range(n_state):
                where = base + (group * SUB + at) * n_state + n
                prior_ref[group * SUB + at, n] = states[n]
                decay = jnp.exp2(step * rate_ref[n])
                states[n] = decay * states[n] + drive * brow_ref[where]
                term = states[n] * crow_ref[where]
                mixed[n % 2] = term if mixed[n % 2] is None else mixed[n % 2] + term
            mixed_held[pl.ds(at, tiles, stride=SUB), :] = mixed[0] + mixed[1]
        stage_out(mixed_held, mixed_ref, group)
        return tuple(states)

    states = lax.fori_loop(0, groups, one, tuple(carried[n] for n in range(n_state)))
    for n in range(n_state):
        carried[n] = states[n]


def scan_forward(start, step, inputs, b_rows, c_rows, rate, seqs):
    n_state, tiles, _ = rate.shape
    all_groups = step.shape[0] // SUB
    groups = math.gcd(all_groups // seqs, 4)
    blocks = all_groups // seqs // groups
    rows_spec = pl.BlockSpec((groups * SUB, tiles * LANE), lambda s, b: (s * blocks + b, 0))
    held = pltpu.VMEM((tiles * SUB, LANE), jnp.float32)
    smem = pl.BlockSpec(memory_space=pltpu.SMEM)
    tokens = all_groups * SUB
    return pl.pallas_call(
        functools.partial(forward_kernel, n_state, tiles, groups, blocks),
        grid=(seqs, blocks),
        in_specs=[
            pl.BlockSpec((1, n_state, tiles, LANE), lambda s, b: (s, 0, 0, 0)),
            rows_spec,
            rows_spec,
            smem,
            smem,
            pl.BlockSpec((n_state, tiles, LANE), lambda s, b: (0, 0, 0)),
        ],
        out_specs=[
            pl.BlockSpec(
                (groups * SUB, n_state, tiles, LANE), lambda s, b: (s * blocks + b, 0, 0, 0)
            ),
            rows_spec,
        ],
        out_shape=[
            jax.ShapeDtypeStruct((tokens, n_state, tiles, LANE), jnp.float32),
            jax.ShapeDtypeStruct(step.shape, jnp.float32),
        ],
        scratch_shapes=[pltpu.VMEM((n_state, tiles, LANE), jnp.float32)] + [held] * 3,
        compiler_params=pltpu.CompilerParams(vmem_limit_bytes=VMEM_GRANT),
    )(start, step, inputs, b_rows, c_rows, rate)


def backward_kernel(
    n_state,
    tiles,
    groups,
    blocks,
    end_ref,
    prior_ref,
    step_ref,
    input_ref,
    ograd_ref,
    brow_ref,
    crow_ref,
    rate_ref,
    picks_ref,
    step_grad_ref,
    input_grad_ref,
    rate_grad_ref,
    part_ref,
    carried,
    step_held,
    input_held,
    ograd_held,
    step_grad_held,
    input_grad_held,
):
    block = blocks - 1 - pl.program_id(1)
    base = (pl.program_id(0) * blocks + block) * groups * SUB * n_state

    @pl.when(pl.program_id(1) == 0)
    def _():
        carried[...] = end_ref[0]

    @pl.when((pl.program_id(0) == 0) & (pl.program_id(1) == 0))
    def _():
        rate_grad_ref[...] = jnp.zeros_like(rate_grad_ref)

    def one(turn, grads):
        group = groups - 1 - turn
        grads = list(grads)
        stage_in(step_ref, group, step_held)
        stage_in(input_ref, group, input_held)
        stage_in(ograd_ref, group, ograd_held)
        for at in range(SUB - 1, -1, -1):
            step = token_row(step_held, at, tiles)
            value = token_row(input_held, at, tiles)
            ograd = token_row(ograd_held, at, tiles)
            drive = step * value
            along_b = None
            along_rate = None
            brow_parts, crow_parts = [], []
            for n in range(n_state):
                where = base + (group * SUB + at) * n_state + n
                brow, crow = brow_ref[where], crow_ref[where]
                rate = rate_ref[n]
                decay = jnp.exp2(step * rate)
                grad = ograd * crow + grads[n]
                kept = decay * prior_ref[group * SUB + at, n]
                state = kept + drive * brow
                decay_term = grad * kept
                grads[n] = decay * grad
                rate_grad_ref[n] += decay_term * step
                by_rate, by_brow = decay_term * rate, grad * brow
                along_rate = by_rate if along_rate is None else along_rate + by_rate
                along_b = by_brow if along_b is None else along_b + by_brow
                brow_parts.append(grad * drive)
                crow_parts.append(ograd * state)
            step_grad_held[pl.ds(at, tiles, stride=SUB), :] = along_rate * LN2 + along_b * value
            input_grad_held[pl.ds(at, tiles, stride=SUB), :] = along_b * step
            parts = jnp.concatenate(brow_parts + crow_parts, 0).astype(jnp.bfloat16)
            part_ref[group * SUB + at] = jnp.dot(
                picks_ref[...], parts, preferred_element_type=jnp.float32
            )
        stage_out(step_grad_held, step_grad_ref, group)
        stage_out(input_grad_held, input_grad_ref, group)
        return tuple(grads)

    grads = lax.fori_loop(0, groups, one, tuple(carried[n] for n in range(n_state)))
    for n in range(n_state):
        carried[n] = grads[n]


def scan_backward(end_grad, prior, step, inputs, ograd, b_rows, c_rows, rate, seqs):
    n_state, tiles, _ = rate.shape
    all_groups = step.shape[0] // SUB
    groups = math.gcd(all_groups // seqs, 4)
    blocks = all_groups // seqs // groups

    def at(s, b):
        return s * blocks + blocks - 1 - b

    rows_spec = pl.BlockSpec((groups * SUB, tiles * LANE), lambda s, b: (at(s, b), 0))
    held = pltpu.VMEM((tiles * SUB, LANE), jnp.float32)
    smem = pl.BlockSpec(memory_space=pltpu.SMEM)
    tokens = all_groups * SUB
    picks = jnp.repeat(jnp.eye(2 * n_state, dtype=jnp.bfloat16), tiles, 1)
    return pl.pallas_call(
        functools.partial(backward_kernel, n_state, tiles, groups, blocks),
        grid=(seqs, blocks),
        in_specs=[
            pl.BlockSpec((1, n_state, tiles, LANE), lambda s, b: (s, 0, 0, 0)),
            pl.BlockSpec((groups * SUB, n_state, tiles, LANE), lambda s, b: (at(s, b), 0, 0, 0)),
            rows_spec,
            rows_spec,
            rows_spec,
            smem,
            smem,
            pl.BlockSpec((n_state, tiles, LANE), lambda s, b: (0, 0, 0)),
            pl.BlockSpec(picks.shape, lambda s, b: (0, 0)),
        ],
        out_specs=[
            rows_spec,
            rows_spec,
            pl.BlockSpec((n_state, tiles, LANE), lambda s, b: (0, 0, 0)),
            pl.BlockSpec((groups * SUB, 2 * n_state, LANE), lambda s, b: (at(s, b), 0, 0)),
        ],
        out_shape=[
            jax.ShapeDtypeStruct(step.shape, jnp.float32),
            jax.ShapeDtypeStruct(step.shape, jnp.float32),
            jax.ShapeDtypeStruct(rate.shape, jnp.float32),
            jax.ShapeDtypeStruct((tokens, 2 * n_state, LANE), jnp.float32),
        ],
        scratch_shapes=[pltpu.VMEM((n_state, tiles, LANE), jnp.float32)] + [held] * 5,
        compiler_params=pltpu.CompilerParams(vmem_limit_bytes=VMEM_GRANT),
    )(end_grad, prior, step, inputs, ograd, b_rows, c_rows, rate, picks)


def from_earlier(ends, decay, steps):
    count = lax.axis_size("ctx")
    if count == 1:
        return jnp.zeros_like(ends)
    if count == 2:
        return passed_along(ends, "ctx", steps)
    index = lax.axis_index("ctx")
    all_ends = lax.all_gather(ends, "ctx")
    all_decays = lax.all_gather(decay, "ctx")

    def one(turn, state):
        at = turn if steps > 0 else count - 1 - turn
        reached = at < index if steps > 0 else at > index
        return jnp.where(reached, all_decays[at] * state + all_ends[at], state)

    return lax.fori_loop(0, count, one, jnp.zeros_like(ends))


def gathered_rows(rows):
    return lax.all_gather(rows, PLANE, axis=0, tiled=True)


def swapped_columns(rows):
    return lax.all_to_all(rows, PLANE, split_axis=1, concat_axis=0, tiled=True)


def place_in(axes):
    index = 0
    for axis in axes:
        index = index * lax.axis_size(axis) + lax.axis_index(axis)
    return index


def device_at(axes, index):
    where = {}
    for axis in reversed(axes):
        size = lax.axis_size(axis)
        where[axis] = lax.rem(index, size)
        index = lax.div(index, size)
    return where


def greet(groups):
    barrier = pltpu.get_barrier_semaphore()
    total = 0
    for axes, others in groups:
        for other in others:
            pl.semaphore_signal(
                barrier,
                inc=1,
                device_id=device_at(axes, other),
                device_id_type=pl.DeviceIdType.MESH,
            )
            total += 1
    pl.semaphore_wait(barrier, total)


def sent(source, target, send_sem, recv_sem, where):
    copy = pltpu.make_async_remote_copy(
        src_ref=source,
        dst_ref=target,
        send_sem=send_sem,
        recv_sem=recv_sem,
        device_id=where,
        device_id_type=pl.DeviceIdType.MESH,
    )
    copy.start()
    return copy


def finish(copies):
    for copy in copies:
        copy.wait()


def rows_of(ref, index, count):
    rows = ref.shape[0] // count
    return ref.at[pl.ds(pl.multiple_of(index * rows, rows), rows), :]


class Group:
    def __init__(self, axes, send_sem, recv_sem):
        self.axes = axes
        self.count = math.prod(lax.axis_size(axis) for axis in axes)
        self.me = place_in(axes)
        self.others = [lax.rem(self.me + hop, self.count) for hop in range(1, self.count)]
        self.send_sem, self.recv_sem = send_sem, recv_sem

    def own(self, ref):
        return rows_of(ref, self.me, self.count)

    def one(self, source, target, which, hop):
        return sent(
            source,
            target,
            self.send_sem.at[which, hop],
            self.recv_sem.at[which, hop],
            device_at(self.axes, self.others[hop]),
        )

    def scatter(self, part, slot, which):
        return [
            self.one(rows_of(part, other, self.count), slot.at[hop], which, hop)
            for hop, other in enumerate(self.others)
        ]

    def total(self, part, slot):
        total = self.own(part)[...].astype(jnp.float32)
        for hop in range(self.count - 1):
            total = total + slot[hop].astype(jnp.float32)
        return total

    def spread(self, ref, which):
        return [self.one(self.own(ref), self.own(ref), which, hop) for hop in range(self.count - 1)]


def slots_for(part, count):
    return pltpu.VMEM((count - 1, part.shape[0] // count) + part.shape[1:], part.dtype)


def group_size(axes):
    return math.prod(lax.axis_size(axis) for axis in axes)


def line_of_four():
    me = lax.axis_index("tp")
    near = me + 1 - 2 * lax.rem(me, 2)
    return me, near, lax.rem(me + 2, 4), lax.rem(near + 2, 4)


class LineSum:
    def __init__(self, part, near_slots, far_slot, passed, send_sem, recv_sem):
        self.part, self.near_slots, self.far_slot = part, near_slots, far_slot
        self.passed, self.send_sem, self.recv_sem = passed, send_sem, recv_sem
        self.me, self.near, self.far, self.cross = line_of_four()
        self.blocks = send_sem.shape[1]
        self.copies = []

    def columns(self, j):
        wide = self.part.shape[1] // self.blocks
        return slice(j * wide, (j + 1) * wide)

    def rows(self, index):
        return rows_of(self.part, index, 4)

    def send(self, source, target, which, j, where):
        copy = sent(
            source.at[:, self.columns(j)],
            target.at[:, self.columns(j)],
            self.send_sem.at[which, j],
            self.recv_sem.at[which, j],
            {"tp": where},
        )
        self.copies.append((which, copy))
        return copy

    def begin(self, j):
        first = self.send(self.rows(self.cross), self.near_slots.at[0], 0, j, self.near)
        self.send(self.rows(self.near), self.near_slots.at[1], 1, j, self.near)
        return first

    def pass_on(self, j, first):
        first.wait_recv()
        columns = self.columns(j)
        self.passed[:, columns] = (
            self.rows(self.far)[:, columns].astype(jnp.float32)
            + self.near_slots[0, :, columns].astype(jnp.float32)
        ).astype(self.passed.dtype)
        self.send(self.passed, self.far_slot, 2, j, self.far)

    def total(self):
        for which, copy in self.copies:
            copy.wait_send()
            if which:
                copy.wait_recv()
        return (
            self.rows(self.me)[...].astype(jnp.float32)
            + self.near_slots[1].astype(jnp.float32)
            + self.far_slot[...].astype(jnp.float32)
        )

    def pass_all(self, firsts):
        for j, first in enumerate(firsts):
            self.pass_on(j, first)


def line_sum_scratch(part, blocks):
    share = (part.shape[0] // 4,) + part.shape[1:]
    sems = pltpu.SemaphoreType.DMA((3, blocks))
    return [
        pltpu.VMEM((2,) + share, part.dtype),
        pltpu.VMEM(share, part.dtype),
        pltpu.VMEM(share, part.dtype),
        sems,
        sems,
    ]


class LineSpread:
    def __init__(self, ref, send_sem, recv_sem):
        self.ref, self.send_sem, self.recv_sem = ref, send_sem, recv_sem
        self.me, self.near, self.far, self.cross = line_of_four()

    def send(self, owner, half, which, where):
        rows = rows_of(self.ref, owner, 4)
        if half is not None:
            wide = self.ref.shape[1] // 2
            rows = rows.at[:, half * wide : (half + 1) * wide]
        return sent(rows, rows, self.send_sem.at[which], self.recv_sem.at[which], {"tp": where})

    def begin(self):
        self.across = [self.send(self.me, half, half, self.far) for half in range(2)]
        self.within = [self.send(self.me, None, 2, self.near)]

    def pass_on(self):
        for half, copy in enumerate(self.across):
            copy.wait_recv()
            self.within.append(self.send(self.far, half, 3 + half, self.near))

    def end(self):
        for copy in self.across:
            copy.wait_send()
        finish(self.within)

    def run(self):
        self.begin()
        self.pass_on()
        self.end()


def line_spread_scratch():
    return [pltpu.SemaphoreType.DMA((5,)), pltpu.SemaphoreType.DMA((5,))]


class Swap:
    def __init__(self, arrays, swapped, send_sem, recv_sem, local_sem):
        plane = Group(PLANE, send_sem, recv_sem)
        self.plane, self.arrays, self.swapped, self.local_sem = plane, arrays, swapped, local_sem

    def begin(self):
        self.copies, plane = [], self.plane
        for which, (array, swapped) in enumerate(zip(self.arrays, self.swapped)):
            share = swapped.shape[1]

            def columns(index):
                return array.at[:, pl.ds(pl.multiple_of(index * share, share), share)]

            for hop, other in enumerate(plane.others):
                self.copies.append(plane.one(columns(other), plane.own(swapped), which, hop))
            local = pltpu.make_async_copy(
                columns(plane.me), plane.own(swapped), self.local_sem.at[which]
            )
            local.start()
            self.copies.append(local)

    def end(self):
        finish(self.copies)


def swap_scratch(arrays):
    sems = pltpu.SemaphoreType.DMA((len(arrays), group_size(PLANE) - 1))
    return [sems, sems, pltpu.SemaphoreType.DMA((len(arrays),))] if arrays else []


def swap_shapes(arrays):
    count = group_size(PLANE)
    return [
        jax.ShapeDtypeStruct((array.shape[0] * count, array.shape[1] // count), array.dtype)
        for array in arrays
    ]


def swaps_in_kernels(width):
    return width // group_size(PLANE) % LANE == 0


def gathered_shape(shard):
    return jax.ShapeDtypeStruct(
        (shard.shape[0] * group_size(PLANE),) + shard.shape[1:], shard.dtype
    )


def gather_scratch():
    return [gather_sems(), gather_sems(), pltpu.SemaphoreType.DMA(())]


def product_in_blocks(left, source, target, block_buf, block_sem):
    columns = range(0, source.shape[1], WIDE)

    def fetch(turn):
        at = columns[turn]
        return pltpu.make_async_copy(
            source.at[:, at : at + WIDE], block_buf.at[turn % 2], block_sem.at[turn % 2]
        )

    fetch(0).start()
    for turn, at in enumerate(columns):
        if turn + 1 < len(columns):
            fetch(turn + 1).start()
        fetch(turn).wait()
        target[:, at : at + WIDE] = matmul(left[...], block_buf[turn % 2]).astype(target.dtype)


def select_kernel(
    part, shard, total, gathered, slots, send_sem, recv_sem, gather_send, gather_recv, local_sem
):
    group = Group(("tp",), send_sem, recv_sem)
    gather = PlaneGather(shard, gathered, gather_send, gather_recv)
    greet([(("tp",), group.others), (PLANE, gather.others)])
    copies = group.scatter(part, slots, 0)
    gather.begin(local_sem)
    finish(copies)
    group.own(total)[...] = group.total(part, slots).astype(total.dtype)
    copies = group.spread(total, 1)
    gather.relay()
    gather.hand_over()
    finish(copies)
    gather.hand_over_last()
    gather.end()


def run_select(call_id, part, shard):
    count = group_size(("tp",))
    vmem = pl.BlockSpec(memory_space=pltpu.VMEM)
    hbm = pl.BlockSpec(memory_space=pltpu.HBM)
    sems = pltpu.SemaphoreType.DMA((2, count - 1))
    return pl.pallas_call(
        select_kernel,
        in_specs=[vmem, hbm],
        out_specs=[vmem, hbm],
        out_shape=[jax.ShapeDtypeStruct(part.shape, part.dtype), gathered_shape(shard)],
        scratch_shapes=[slots_for(part, count), sems, sems] + gather_scratch(),
        compiler_params=pltpu.CompilerParams(
            collective_id=call_id, has_side_effects=True, vmem_limit_bytes=VMEM_GRANT
        ),
    )(part, shard)


def sum_kernel(part, own_rows, total, all_rows, slots, send_sem, recv_sem, *line_sems):
    group = Group(("tp",), send_sem, recv_sem)
    rows = LineSpread(all_rows, *line_sems)
    greet([(("tp",), group.others)])
    copies = group.scatter(part, slots, 0)
    group.own(all_rows)[...] = own_rows[...]
    rows.begin()
    finish(copies)
    group.own(total)[...] = group.total(part, slots).astype(total.dtype)
    copies = group.spread(total, 1)
    rows.pass_on()
    finish(copies)
    rows.end()


def sum_over_tp(call_id, part, own_rows):
    count = group_size(("tp",))
    vmem = pl.BlockSpec(memory_space=pltpu.VMEM)
    sems = pltpu.SemaphoreType.DMA((2, count - 1))
    return pl.pallas_call(
        sum_kernel,
        in_specs=[vmem] * 2,
        out_specs=[vmem] * 2,
        out_shape=[
            jax.ShapeDtypeStruct(part.shape, part.dtype),
            jax.ShapeDtypeStruct((own_rows.shape[0] * count, own_rows.shape[1]), own_rows.dtype),
        ],
        scratch_shapes=[slots_for(part, count), sems, sems] + line_spread_scratch(),
        compiler_params=pltpu.CompilerParams(
            collective_id=call_id, has_side_effects=True, vmem_limit_bytes=VMEM_GRANT
        ),
    )(part, own_rows)


def mixer_out_kernel(n_swaps, gated, out_first, out_last, tokens, gain, *refs):
    arrays, refs = refs[:n_swaps], refs[n_swaps:]
    normed, middle, gated_all, *refs = refs
    swapped, refs = refs[:n_swaps], refs[n_swaps:]
    part, refs = refs[0], refs[1:]
    line = LineSum(part, *refs[:5])
    spread = LineSpread(normed, *refs[5:7])
    gather_send, gather_recv, local_sem, *refs = refs[7:]
    group = Group(("tp",), None, None)
    gather = PlaneGather(gated, gated_all, gather_send, gather_recv)
    half = gated.shape[1] // 2
    share = out_first.shape[1]
    greet([(("tp",), group.others), (PLANE, gather.others)])
    gather.begin(local_sem)
    for at in range(out_first.shape[0] // half):
        rows = slice(at * half, (at + 1) * half)
        part[:, at * share : (at + 1) * share] = (
            matmul(gated[:, :half], out_first[rows, :])
            + matmul(gated[:, half:], out_last[rows, :])
        ).astype(part.dtype)
    firsts = [line.begin(j) for j in range(line.blocks)]
    if n_swaps:
        swap = Swap(arrays, swapped, *refs)
        swap.begin()
    line.pass_all(firsts)
    rows = group.own(tokens)[...].astype(jnp.float32) + line.total()
    middle[...] = rows
    group.own(normed)[...] = (rows * inverse_rms(rows) * gain[...].astype(jnp.float32)).astype(
        normed.dtype
    )
    spread.begin()
    gather.relay()
    gather.hand_over()
    spread.pass_on()
    spread.end()
    gather.hand_over_last()
    gather.end()
    if n_swaps:
        swap.end()


def mixer_out(call_id, gated, out_first, out_last, tokens, gain, arrays):
    count = group_size(("tp",))
    vmem = pl.BlockSpec(memory_space=pltpu.VMEM)
    hbm = pl.BlockSpec(memory_space=pltpu.HBM)
    rows, width = tokens.shape
    part = jax.ShapeDtypeStruct((rows, width), jnp.bfloat16)
    return pl.pallas_call(
        functools.partial(mixer_out_kernel, len(arrays)),
        in_specs=[vmem] * (5 + len(arrays)),
        out_specs=[vmem] * 2 + [hbm] + [hbm] * len(arrays),
        out_shape=[
            part,
            jax.ShapeDtypeStruct((rows // count, width), jnp.float32),
            gathered_shape(gated),
        ]
        + swap_shapes(arrays),
        scratch_shapes=[pltpu.VMEM(part.shape, part.dtype)]
        + line_sum_scratch(part, 2)
        + line_spread_scratch()
        + gather_scratch()
        + swap_scratch(arrays),
        compiler_params=pltpu.CompilerParams(
            collective_id=call_id, has_side_effects=True, vmem_limit_bytes=VMEM_GRANT
        ),
    )(gated, out_first, out_last, tokens, gain, *arrays)


def ffn_kernel(swaps, normed, ct, weights, made, *refs):
    hidden = weights.shape[1] // 3
    if swaps:
        *swapped, block_buf, block_sem, send_sem, recv_sem, local_sem = refs
        swap = Swap([ct], swapped, send_sem, recv_sem, local_sem)
        greet([(PLANE, swap.plane.others)])
        swap.begin()
    else:
        block_buf, block_sem = refs

    def columns(j, which):
        return pl.ds(pl.multiple_of(which * hidden + j * WIDE, WIDE), WIDE)

    def fetch(j, which):
        slot = lax.rem(j, 2)
        return pltpu.make_async_copy(
            weights.at[:, columns(j, which)],
            block_buf.at[slot, which],
            block_sem.at[slot, which],
        )

    for which in range(3):
        fetch(0, which).start()

    @pl.loop(0, hidden // WIDE)
    def _(j):
        slot = lax.rem(j, 2)

        @pl.when(j + 1 < hidden // WIDE)
        def _():
            for which in range(3):
                fetch(j + 1, which).start()

        fetch(j, 0).wait()
        gate = matmul(normed[...], block_buf[slot, 0])
        fetch(j, 1).wait()
        up = matmul(normed[...], block_buf[slot, 1])
        fetch(j, 2).wait()
        act_grad = matmul(ct[...], block_buf[slot, 2])
        logistic = jax.nn.sigmoid(gate)
        silu = gate * logistic
        slope = logistic * (1.0 + gate * (1.0 - logistic))
        made[:, columns(j, 0)] = (silu * up).astype(made.dtype)
        made[:, columns(j, 1)] = (act_grad * up * slope).astype(made.dtype)
        made[:, columns(j, 2)] = (act_grad * silu).astype(made.dtype)

    if swaps:
        swap.end()


def run_ffn(call_id, normed, ct, weights, swaps):
    rows, width = normed.shape
    arrays = [ct] if swaps else []
    vmem = pl.BlockSpec(memory_space=pltpu.VMEM)
    params = dict(collective_id=call_id, has_side_effects=True) if swaps else {}
    return pl.pallas_call(
        functools.partial(ffn_kernel, swaps),
        in_specs=[vmem, vmem, pl.BlockSpec(memory_space=pltpu.HBM)],
        out_specs=[vmem] + [pl.BlockSpec(memory_space=pltpu.HBM)] * len(arrays),
        out_shape=[jax.ShapeDtypeStruct((rows, weights.shape[1]), jnp.bfloat16)]
        + swap_shapes(arrays),
        scratch_shapes=[
            pltpu.VMEM((2, 3, width, WIDE), jnp.bfloat16),
            pltpu.SemaphoreType.DMA((2, 3)),
        ]
        + swap_scratch(arrays),
        compiler_params=pltpu.CompilerParams(vmem_limit_bytes=VMEM_GRANT, **params),
    )(normed, ct, weights)


def ffn_back_kernel(
    n_swaps,
    made,
    ct,
    middle,
    gain,
    out_first,
    out_last,
    weights,
    *refs,
):
    arrays, refs = refs[:n_swaps], refs[n_swaps:]
    middle_low, middle_grad, gain_grad, gated_grad, ffn_part, *refs = refs
    swapped, refs = refs[:n_swaps], refs[n_swaps:]
    part, wide_buf, down_buf, wide_sem, down_sem, *sems = refs
    hidden = made.shape[1] // 3
    blocks = part.shape[1] // WIDE
    group = Group(("tp",), None, None)
    line = LineSum(part, *sems[:5])
    spread = LineSpread(middle_low, *sems[5:7])
    if n_swaps:
        swap = Swap(arrays, swapped, *sems[7:])
        greet([(("tp",), group.others), (PLANE, swap.plane.others)])
        swap.begin()
    else:
        greet([(("tp",), group.others)])

    def fetch(j):
        return pltpu.make_async_copy(
            weights.at[j * WIDE : (j + 1) * WIDE, : 2 * hidden],
            wide_buf.at[j % 2],
            wide_sem.at[j % 2],
        )

    def fetch_down(j):
        return pltpu.make_async_copy(
            weights.at[j * WIDE : (j + 1) * WIDE, 2 * hidden :],
            down_buf.at[j % 2],
            down_sem.at[j % 2],
        )

    fetch(0).start()
    firsts = []
    for j in range(blocks):
        if j + 1 < blocks:
            fetch(j + 1).start()
        else:
            fetch_down(0).start()
        fetch(j).wait()
        columns = slice(j * WIDE, (j + 1) * WIDE)
        part[:, columns] = matmul_nt(made[:, hidden:], wide_buf[j % 2]).astype(part.dtype)
        firsts.append(line.begin(j))
    for j in range(blocks):
        if j + 1 < blocks:
            fetch_down(j + 1).start()
        fetch_down(j).wait()
        ffn_part[:, j * WIDE : (j + 1) * WIDE] = matmul_nt(
            made[:, :hidden], down_buf[j % 2]
        ).astype(ffn_part.dtype)
        line.pass_on(j, firsts[j])
    normed_grad = line.total()
    rows = middle[...]
    scale = inverse_rms(rows)
    gain_grad[...] = jnp.sum(normed_grad * rows * scale, 0, keepdims=True)
    grad = group.own(ct)[...].astype(jnp.float32) + norm_back(
        normed_grad, rows, scale, gain[...].astype(jnp.float32)
    )
    middle_grad[...] = grad
    group.own(middle_low)[...] = grad.astype(middle_low.dtype)
    spread.run()
    half = gated_grad.shape[1] // 2
    share = out_first.shape[1]
    for side, shards in enumerate((out_first, out_last)):
        total = None
        for at in range(shards.shape[0] // half):
            one = matmul_nt(
                middle_low[:, at * share : (at + 1) * share],
                shards[at * half : (at + 1) * half, :],
            )
            total = one if total is None else total + one
        gated_grad[:, side * half : (side + 1) * half] = total
    if n_swaps:
        swap.end()


def ffn_back(call_id, made, ct, middle, gain, out_first, out_last, weights, arrays):
    count = group_size(("tp",))
    vmem = pl.BlockSpec(memory_space=pltpu.VMEM)
    hbm = pl.BlockSpec(memory_space=pltpu.HBM)
    rows, width = ct.shape
    hidden = made.shape[1] // 3
    inner = 2 * out_first.shape[0] // group_size(PLANE)
    low, full = jnp.bfloat16, jnp.float32
    part = jax.ShapeDtypeStruct((rows, width), low)
    dma = pltpu.SemaphoreType.DMA
    return pl.pallas_call(
        functools.partial(ffn_back_kernel, len(arrays)),
        in_specs=[vmem] * 6 + [hbm] + [vmem] * len(arrays),
        out_specs=[vmem] * 5 + [hbm] * len(arrays),
        out_shape=[
            part,
            jax.ShapeDtypeStruct((rows // count, width), full),
            jax.ShapeDtypeStruct((1, width), full),
            jax.ShapeDtypeStruct((rows, inner), full),
            part,
        ]
        + swap_shapes(arrays),
        scratch_shapes=[
            pltpu.VMEM(part.shape, low),
            pltpu.VMEM((2, WIDE, 2 * hidden), low),
            pltpu.VMEM((2, WIDE, hidden), low),
            dma((2,)),
            dma((2,)),
        ]
        + line_sum_scratch(part, width // WIDE)
        + line_spread_scratch()
        + swap_scratch(arrays),
        compiler_params=pltpu.CompilerParams(
            collective_id=call_id, has_side_effects=True, vmem_limit_bytes=VMEM_GRANT
        ),
    )(made, ct, middle, gain, out_first, out_last, weights, *arrays)


def send_on(source, target, send_sem, recv_sem, ctx):
    return pltpu.make_async_remote_copy(
        src_ref=source,
        dst_ref=target,
        send_sem=send_sem,
        recv_sem=recv_sem,
        device_id={"ctx": ctx},
        device_id_type=pl.DeviceIdType.MESH,
    )


def forward_pair_kernel(
    n_state,
    tiles,
    groups,
    blocks,
    seqs,
    step_ref,
    input_ref,
    brow_ref,
    crow_ref,
    rate_ref,
    shard,
    *refs,
):
    prior_ref, mixed_ref, gathered, *refs = refs
    carried, ends, starts, prior_buf, step_held, input_held, mixed_held, *refs = refs
    prior_sem, send_sem, recv_sem, gather_send, gather_recv, local_sem = refs
    place = lax.axis_index("ctx")
    gather = PlaneGather(shard, gathered, gather_send, gather_recv)
    greet([(PLANE, gather.others)])
    gather.begin(local_sem)

    def hand_on(seq):
        return send_on(ends.at[seq], starts.at[seq], send_sem.at[seq], recv_sem.at[seq], 1)

    def store(block):
        slot = lax.rem(block, 2)
        rows = groups * SUB
        return pltpu.make_async_copy(
            prior_buf.at[slot],
            prior_ref.at[pl.ds(pl.multiple_of(block * rows, rows), rows)],
            prior_sem.at[slot],
        )

    def one_sequence(seq):
        @pl.when(place == 0)
        def _():
            carried[...] = jnp.zeros_like(carried)

        @pl.when(place == 1)
        def _():
            hand_on(seq).wait_recv()
            carried[...] = starts[seq]

        @pl.loop(0, blocks)
        def _(inner_block):
            block = seq * blocks + inner_block
            slot = lax.rem(block, 2)

            @pl.when(block >= 2)
            def _():
                store(block - 2).wait()

            def one(turn, states):
                group = block * groups + turn
                states = list(states)
                stage_in(step_ref, group, step_held)
                stage_in(input_ref, group, input_held)
                for at in range(SUB):
                    step = token_row(step_held, at, tiles)
                    drive = step * token_row(input_held, at, tiles)
                    mixed = [None] * 2
                    for n in range(n_state):
                        where = (group * SUB + at) * n_state + n
                        prior_buf[slot, turn * SUB + at, n] = states[n]
                        decay = jnp.exp2(step * rate_ref[n])
                        states[n] = decay * states[n] + drive * brow_ref[where]
                        term = states[n] * crow_ref[where]
                        mixed[n % 2] = term if mixed[n % 2] is None else mixed[n % 2] + term
                    mixed_held[pl.ds(at, tiles, stride=SUB), :] = mixed[0] + mixed[1]
                stage_out(mixed_held, mixed_ref, group)
                return tuple(states)

            states = lax.fori_loop(0, groups, one, tuple(carried[n] for n in range(n_state)))
            for n in range(n_state):
                carried[n] = states[n]
            store(block).start()

        @pl.when(place == 0)
        def _():
            ends[seq] = carried[...]
            hand_on(seq).start()

    for seq in range(seqs):
        one_sequence(seq)
        if seq == 0:
            gather.relay()
            gather.hand_over()
    gather.hand_over_last()
    for block in range(max(0, seqs * blocks - 2), seqs * blocks):
        store(block).wait()

    @pl.when(place == 0)
    def _():
        for seq in range(seqs):
            hand_on(seq).wait_send()

    gather.end()


def scan_forward_pair(
    call_id, step, inputs, b_rows, c_rows, rate, seqs, shard
):
    n_state, tiles, _ = rate.shape
    tokens, inner = step.shape
    all_groups = tokens // SUB
    groups = math.gcd(all_groups // seqs, 4)
    blocks = all_groups // seqs // groups
    vmem = pl.BlockSpec(memory_space=pltpu.VMEM)
    smem = pl.BlockSpec(memory_space=pltpu.SMEM)
    hbm = pl.BlockSpec(memory_space=pltpu.HBM)
    full = jnp.float32
    held = pltpu.VMEM((tiles * SUB, LANE), full)
    boundary = pltpu.VMEM((seqs, n_state, tiles, LANE), full)
    dma = pltpu.SemaphoreType.DMA
    return pl.pallas_call(
        functools.partial(
            forward_pair_kernel, n_state, tiles, groups, blocks, seqs
        ),
        in_specs=[vmem, vmem, smem, smem, vmem, hbm],
        out_specs=[hbm, vmem, hbm],
        out_shape=[
            jax.ShapeDtypeStruct((tokens, n_state, tiles, LANE), full),
            jax.ShapeDtypeStruct(step.shape, full),
            gathered_shape(shard),
        ],
        scratch_shapes=[
            pltpu.VMEM((n_state, tiles, LANE), full),
            boundary,
            boundary,
            pltpu.VMEM((2, groups * SUB, n_state, tiles, LANE), full),
            held,
            held,
            held,
            dma((2,)),
            dma((seqs,)),
            dma((seqs,)),
        ]
        + gather_scratch(),
        compiler_params=pltpu.CompilerParams(
            collective_id=call_id, has_side_effects=True, vmem_limit_bytes=VMEM_GRANT
        ),
    )(step, inputs, b_rows, c_rows, rate, shard)


def backward_pair_kernel(
    n_swaps,
    n_state,
    tiles,
    groups,
    blocks,
    seqs,
    step_ref,
    input_ref,
    ograd_ref,
    brow_ref,
    crow_ref,
    rate_ref,
    picks_ref,
    ffn_part,
    middle,
    prior_ref,
    *refs,
):
    arrays, refs = refs[:n_swaps], refs[n_swaps:]
    step_grad_ref, input_grad_ref, rate_grad_ref, part_ref, *refs = refs
    layer_first, layer_last, *refs = refs
    swapped, refs = refs[:n_swaps], refs[n_swaps:]
    carried, ends, starts, prior_buf, step_held, input_held, ograd_held, *refs = refs
    step_grad_held, input_grad_held, ffn_slots, prior_sem, send_sem, recv_sem, *refs = refs
    tp_send, tp_recv, *refs = refs
    place = lax.axis_index("ctx")
    tp = Group(("tp",), tp_send, tp_recv)
    if n_swaps:
        swap = Swap(arrays, swapped, *refs)
        greet([(PLANE, swap.plane.others), (("tp",), tp.others)])
        swap.begin()
    else:
        greet([(("ctx",), [1 - place]), (("tp",), tp.others)])
    ffn_sent = tp.scatter(ffn_part, ffn_slots, 0)

    def hand_on(seq):
        return send_on(ends.at[seq], starts.at[seq], send_sem.at[seq], recv_sem.at[seq], 0)

    def fetch(turn):
        seq = lax.div(turn, blocks)
        block = seq * blocks + blocks - 1 - lax.rem(turn, blocks)
        slot = lax.rem(turn, 2)
        rows = groups * SUB
        return pltpu.make_async_copy(
            prior_ref.at[pl.ds(pl.multiple_of(block * rows, rows), rows)],
            prior_buf.at[slot],
            prior_sem.at[slot],
        )

    fetch(0).start()
    rate_grad_ref[...] = jnp.zeros_like(rate_grad_ref)

    @pl.when(place == 1)
    def _():
        @pl.loop(0, seqs)
        def _(seq):
            def one(turn, grads):
                group = (seq + 1) * blocks * groups - 1 - turn
                grads = list(grads)
                stage_in(step_ref, group, step_held)
                stage_in(ograd_ref, group, ograd_held)
                for at in range(SUB - 1, -1, -1):
                    step = token_row(step_held, at, tiles)
                    ograd = token_row(ograd_held, at, tiles)
                    for n in range(n_state):
                        row = crow_ref[(group * SUB + at) * n_state + n]
                        grads[n] = jnp.exp2(step * rate_ref[n]) * (grads[n] + ograd * row)
                return tuple(grads)

            zero = jnp.zeros((tiles, LANE), jnp.float32)
            grads = lax.fori_loop(0, blocks * groups, one, (zero,) * n_state)
            for n in range(n_state):
                ends[seq, n] = grads[n]
            hand_on(seq).start()

    @pl.loop(0, seqs)
    def _(seq):
        @pl.when(place == 1)
        def _():
            carried[...] = jnp.zeros_like(carried)

        @pl.when(place == 0)
        def _():
            hand_on(seq).wait_recv()
            carried[...] = starts[seq]

        @pl.loop(0, blocks)
        def _(inner_block):
            turn = seq * blocks + inner_block
            slot = lax.rem(turn, 2)
            first_group = (seq * blocks + blocks - 1 - inner_block) * groups

            @pl.when(turn + 1 < seqs * blocks)
            def _():
                fetch(turn + 1).start()

            fetch(turn).wait()

            def one(back, grads):
                inner_group = groups - 1 - back
                group = first_group + inner_group
                grads = list(grads)
                stage_in(step_ref, group, step_held)
                stage_in(input_ref, group, input_held)
                stage_in(ograd_ref, group, ograd_held)
                for at in range(SUB - 1, -1, -1):
                    step = token_row(step_held, at, tiles)
                    value = token_row(input_held, at, tiles)
                    ograd = token_row(ograd_held, at, tiles)
                    drive = step * value
                    along_b = None
                    along_rate = None
                    brow_parts, crow_parts = [], []
                    for n in range(n_state):
                        where = (group * SUB + at) * n_state + n
                        brow, crow = brow_ref[where], crow_ref[where]
                        rate = rate_ref[n]
                        decay = jnp.exp2(step * rate)
                        grad = ograd * crow + grads[n]
                        kept = decay * prior_buf[slot, inner_group * SUB + at, n]
                        state = kept + drive * brow
                        decay_term = grad * kept
                        grads[n] = decay * grad
                        rate_grad_ref[n] += decay_term * step
                        by_rate, by_brow = decay_term * rate, grad * brow
                        along_rate = by_rate if along_rate is None else along_rate + by_rate
                        along_b = by_brow if along_b is None else along_b + by_brow
                        brow_parts.append(grad * drive)
                        crow_parts.append(ograd * state)
                    step_grad_held[pl.ds(at, tiles, stride=SUB), :] = (
                        along_rate * LN2 + along_b * value
                    )
                    input_grad_held[pl.ds(at, tiles, stride=SUB), :] = along_b * step
                    parts = jnp.concatenate(brow_parts + crow_parts, 0).astype(jnp.bfloat16)
                    part_ref[group * SUB + at] = jnp.dot(
                        picks_ref[...], parts, preferred_element_type=jnp.float32
                    )
                stage_out(step_grad_held, step_grad_ref, group)
                stage_out(input_grad_held, input_grad_ref, group)
                return tuple(grads)

            grads = lax.fori_loop(0, groups, one, tuple(carried[n] for n in range(n_state)))
            for n in range(n_state):
                carried[n] = grads[n]

    finish(ffn_sent)
    layer_rows = (middle[...] + tp.total(ffn_part, ffn_slots)).astype(layer_first.dtype)
    half = layer_first.shape[1]
    layer_first[...], layer_last[...] = layer_rows[:, :half], layer_rows[:, half:]

    @pl.when(place == 1)
    def _():
        @pl.loop(0, seqs)
        def _(seq):
            hand_on(seq).wait_send()

    if n_swaps:
        swap.end()


def scan_backward_pair(
    call_id, prior, step, inputs, ograd, b_rows, c_rows, rate, seqs, ffn_part, middle, arrays
):
    n_state, tiles, _ = rate.shape
    tokens, inner = step.shape
    all_groups = tokens // SUB
    groups = math.gcd(all_groups // seqs, 4)
    blocks = all_groups // seqs // groups
    tp_count = group_size(("tp",))
    vmem = pl.BlockSpec(memory_space=pltpu.VMEM)
    smem = pl.BlockSpec(memory_space=pltpu.SMEM)
    hbm = pl.BlockSpec(memory_space=pltpu.HBM)
    full = jnp.float32
    held = pltpu.VMEM((tiles * SUB, LANE), full)
    boundary = pltpu.VMEM((seqs, n_state, tiles, LANE), full)
    dma = pltpu.SemaphoreType.DMA
    layer_half = jax.ShapeDtypeStruct((middle.shape[0], middle.shape[1] // 2), jnp.bfloat16)
    picks = jnp.repeat(jnp.eye(2 * n_state, dtype=jnp.bfloat16), tiles, 1)
    return pl.pallas_call(
        functools.partial(
            backward_pair_kernel, len(arrays), n_state, tiles, groups, blocks, seqs
        ),
        in_specs=[vmem] * 3 + [smem] * 2 + [vmem] * 4 + [hbm] + [vmem] * len(arrays),
        out_specs=[vmem] * 6 + [hbm] * len(arrays),
        out_shape=[
            jax.ShapeDtypeStruct(step.shape, full),
            jax.ShapeDtypeStruct(step.shape, full),
            jax.ShapeDtypeStruct(rate.shape, full),
            jax.ShapeDtypeStruct((tokens, 2 * n_state, LANE), full),
            layer_half,
            layer_half,
        ]
        + swap_shapes(arrays),
        scratch_shapes=[
            pltpu.VMEM((n_state, tiles, LANE), full),
            boundary,
            boundary,
            pltpu.VMEM((2, groups * SUB, n_state, tiles, LANE), full),
        ]
        + [held] * 5
        + [
            slots_for(ffn_part, tp_count),
            dma((2,)),
            dma((seqs,)),
            dma((seqs,)),
            dma((1, tp_count - 1)),
            dma((1, tp_count - 1)),
        ]
        + swap_scratch(arrays),
        compiler_params=pltpu.CompilerParams(
            collective_id=call_id, has_side_effects=True, vmem_limit_bytes=VMEM_GRANT
        ),
    )(step, inputs, ograd, b_rows, c_rows, rate, picks, ffn_part, middle, prior, *arrays)


class PlaneGather:
    def __init__(self, own, gathered, send_sem, recv_sem):
        self.own, self.gathered = own, gathered
        self.send_sem, self.recv_sem = send_sem, recv_sem
        self.dp, self.ctx = lax.axis_index("dp"), lax.axis_index("ctx")
        self.n_dp, self.n_ctx = lax.axis_size("dp"), lax.axis_size("ctx")
        self.hands_on = relayed()
        self.count = self.n_dp * self.n_ctx
        self.me = self.dp * self.n_ctx + self.ctx
        self.others = [lax.rem(self.me + hop, self.count) for hop in range(1, self.count)]
        self.copies = {}
        if self.hands_on:
            core = lax.rem(self.dp, 2)
            over_core = self.dp + 1 - 2 * core
            over_y = lax.rem(self.dp + 2, 4)
            over_x = 1 - self.ctx
            self.core = {"dp": over_core, "ctx": self.ctx}
            self.at_x = {"dp": self.dp, "ctx": over_x}
            self.at_y = {"dp": over_y, "ctx": self.ctx}
            self.from_x = self.dp * 2 + over_x
            self.from_y = over_y * 2 + self.ctx
            self.across = over_y * 2 + over_x

    def part(self, owner, half):
        rows = self.gathered.shape[0] // self.count
        start, size = owner * rows, rows
        if half is not None:
            size = rows // 2
            start = start + half * size
        return self.gathered.at[pl.ds(pl.multiple_of(start, size), size), :]

    def send(self, which, owner, half, where):
        target = self.part(owner, half)
        source = target
        if owner is self.me:
            rows = self.own.shape[0]
            source = self.own
            if half is not None:
                source = self.own.at[pl.ds(half * (rows // 2), rows // 2), :]
        self.copies[which] = sent(
            source, target, self.send_sem.at[which], self.recv_sem.at[which], where
        )

    def arrived(self, *which):
        for one in which:
            self.copies[one].wait_recv()

    def begin(self, local_sem):
        self.local = pltpu.make_async_copy(self.own, self.part(self.me, None), local_sem)
        self.local.start()
        if not self.hands_on:
            for hop, other in enumerate(self.others):
                self.send(hop, self.me, None, device_at(PLANE, other))
            return
        self.send(0, self.me, 1, self.at_x)
        self.send(1, self.me, 0, self.at_y)
        self.send(2, self.me, None, self.core)
        self.send(3, self.me, 0, self.at_x)
        self.send(4, self.me, 1, self.at_y)

    def relay(self):
        if not self.hands_on:
            return
        self.arrived(0, 1)
        self.send(5, self.from_x, 1, self.at_y)
        self.send(6, self.from_y, 0, self.at_x)
        self.send(7, self.from_x, 1, self.core)
        self.send(8, self.from_y, 0, self.core)

    def hand_over(self):
        if not self.hands_on:
            return
        self.arrived(3, 4)
        self.send(9, self.from_x, 0, self.core)
        self.send(10, self.from_y, 1, self.core)

    def hand_over_last(self):
        if not self.hands_on:
            return
        self.arrived(5, 6)
        self.send(11, self.across, 1, self.core)
        self.send(12, self.across, 0, self.core)

    def end(self):
        if self.hands_on:
            self.arrived(2, 7, 8, 9, 10, 11, 12)
        else:
            self.arrived(*range(self.count - 1))
        for copy in self.copies.values():
            copy.wait_send()
        self.local.wait()


def relayed():
    return lax.axis_size("dp") == 4 and lax.axis_size("ctx") == 2


def gather_sems():
    count = 13 if relayed() else group_size(PLANE) - 1
    return pltpu.SemaphoreType.DMA((count,))


WIDE = 512


def products(source, first, last, dot, target, block_buf, block_sem, out_buf, out_sem):
    def fetch(j, slot):
        columns = pl.ds(pl.multiple_of(j * WIDE, WIDE), WIDE)
        return pltpu.make_async_copy(
            source.at[:, columns], block_buf.at[slot], block_sem.at[slot]
        )

    def store(j, slot):
        return pltpu.make_async_copy(out_buf.at[slot], target(j), out_sem.at[slot])

    fetch(first, first % 2).start()

    @pl.loop(first, last)
    def _(j):
        slot = lax.rem(j, 2)

        @pl.when(j + 1 < last)
        def _():
            fetch(j + 1, 1 - slot).start()

        fetch(j, slot).wait()

        @pl.when(j >= first + 2)
        def _():
            store(j - 2, slot).wait()

        out_buf[slot] = dot(block_buf[slot])
        store(j, slot).start()

    for j in range(max(first, last - 2), last):
        store(j, j % 2).wait()


SMALL_ROWS = 32
GAIN_ROWS = 16


def tail_kernel(
    swaps,
    conv_grad,
    gate_grad,
    convkern,
    convbias,
    stepbias,
    decaylog,
    skipgain,
    ffngain,
    layer_first,
    layer_rows,
    middle_low,
    step_low,
    pre_low,
    select_low,
    scan_in,
    tokens,
    middle_grad,
    gain_row,
    in_conv,
    in_gate,
    one_cols,
    two_cols,
    ct_cols,
    middle_cols,
    ffn_all,
    gated_all,
    tokens_grad,
    layer_out,
    vectors_sum,
    step_sum,
    select_sum,
    gains,
    mix_all,
    grad_inproj,
    grad_outproj,
    grad_gateup,
    grad_downproj,
    mix_own,
    normed_part,
    small,
    small_sum,
    small_slots,
    gain_slots,
    gain_own,
    vectors_own,
    cols,
    in_buf,
    block_buf,
    wide_buf,
    tall_buf,
    cols_sem,
    in_sem,
    block_sem,
    wide_sem,
    tall_sem,
    tp_send,
    tp_recv,
    plane_send,
    plane_recv,
    gather_send,
    gather_recv,
    local_sem,
    *sems,
):
    inner = conv_grad.shape[1]
    hidden = ffn_all.shape[1] // 3
    width = tokens.shape[1]
    rank = step_low.shape[1]
    tp = Group(("tp",), tp_send, tp_recv)
    plane = Group(PLANE, plane_send, plane_recv)
    line = LineSum(normed_part, *sems[:5])
    tokens_spread = LineSpread(tokens_grad, *sems[5:7])
    layer_last = layer_out.at[:, width // 2 :]
    layer_spread = LineSpread(layer_last, *sems[7:9])
    swap_sems = sems[9:]
    gather = PlaneGather(mix_own, mix_all, gather_send, gather_recv)
    sources = (one_cols, two_cols, ct_cols) if swaps else (one_cols, two_cols, ct_cols, middle_cols)
    loads = [
        pltpu.make_async_copy(source, cols.at[at], cols_sem.at[at])
        for at, source in enumerate(sources)
    ]
    if swaps:
        swap = Swap([middle_low], [cols.at[3]], *swap_sems)

    def fetch(j):
        slot = j % 2
        rows = slice(j * WIDE, (j + 1) * WIDE)
        return [
            pltpu.make_async_copy(source.at[rows, :], in_buf.at[slot, at], in_sem.at[slot, at])
            for at, source in enumerate((in_conv, in_gate))
        ]

    for copy in fetch(0) + loads:
        copy.start()
    mix_own[:, :inner] = conv_grad[...]
    mix_own[:, inner:] = gate_grad[...]
    greet([(("tp",), tp.others), (PLANE, plane.others)])
    gather.begin(local_sem)

    small[...] = jnp.zeros_like(small)
    vectors_own[...] = jnp.zeros_like(vectors_own)
    at = 0
    for vector in (convkern, convbias, stepbias, decaylog, skipgain):
        vectors_own[at : at + vector.shape[0], :] = vector[...]
        at += vector.shape[0]
    at = SMALL_ROWS - GAIN_ROWS + 10
    for row in range(width // inner):
        vectors_own[at + row : at + row + 1, :] = ffngain[:, row * inner : (row + 1) * inner]
    hidden_in = tokens[...].astype(jnp.float32)
    unit_rows = hidden_in * inverse_rms(hidden_in)
    blocks = width // WIDE
    firsts = []
    for j in range(blocks):
        if j + 1 < blocks:
            for copy in fetch(j + 1):
                copy.start()
        finish(fetch(j))
        columns = slice(j * WIDE, (j + 1) * WIDE)
        block = matmul_nt(conv_grad[...], in_buf[j % 2, 0]) + matmul_nt(
            gate_grad[...], in_buf[j % 2, 1]
        )
        normed_part[:, columns] = block.astype(normed_part.dtype)
        firsts.append(line.begin(j))
        gain_grad = jnp.sum(block * unit_rows[:, columns], 0, keepdims=True)
        if j:
            line.pass_on(j - 1, firsts[j - 1])
        row, at = divmod(j * WIDE, inner)
        row += SMALL_ROWS - GAIN_ROWS + 8
        vectors_own[row : row + 1, at : at + WIDE] = gain_grad
    layer_out[:, : width // 2] = layer_first[...]
    rows_of(layer_last, tp.me, tp.count)[...] = layer_rows[...]
    layer_spread.begin()
    small[:SMALL_ROWS, :] = vectors_own[...].astype(small.dtype)
    small[SMALL_ROWS : SMALL_ROWS + rank, :] = matmul_tn(step_low[...], pre_low[...]).astype(
        small.dtype
    )
    selected = select_sum.shape[0]
    small[SMALL_ROWS + rank : SMALL_ROWS + rank + selected, :] = matmul_tn(
        select_low[...], scan_in[...]
    )[:selected].astype(small.dtype)
    small_sent = plane.scatter(small, small_slots, 0)
    line.pass_on(blocks - 1, firsts[-1])

    def flat(at):
        return lambda block: matmul_tn(cols[at], block)

    def tall(at):
        return lambda block: matmul_tn(block, cols[at])

    def side_by_side(ref, first):
        per = ref.shape[2] // WIDE

        def target(j):
            at = j - first
            columns = pl.ds(pl.multiple_of(lax.rem(at, per) * WIDE, WIDE), WIDE)
            return ref.at[lax.div(at, per), :, columns]

        return target

    def one_above_other(ref):
        return lambda j: ref.at[pl.ds(pl.multiple_of(j * WIDE, WIDE), WIDE), :]

    wide = (block_buf, block_sem, wide_buf, wide_sem)
    high = (block_buf, block_sem, tall_buf, tall_sem)
    down_end = hidden // WIDE
    gu_end = 3 * hidden // WIDE
    finish(loads)
    gu_middle = (down_end + gu_end) // 2
    to_gateup = side_by_side(grad_gateup, down_end)
    products(ffn_all, 0, down_end, tall(2), one_above_other(grad_downproj), *high)
    gather.relay()
    products(ffn_all, down_end, gu_middle, flat(1), to_gateup, *wide)
    hidden_in = tp.own(tokens)[...].astype(jnp.float32)
    tp.own(tokens_grad)[...] = (
        middle_grad[...]
        + norm_back(
            line.total(),
            hidden_in,
            inverse_rms(hidden_in),
            gain_row[...].astype(jnp.float32),
        )
    ).astype(tokens_grad.dtype)
    tokens_spread.begin()
    layer_spread.pass_on()
    gather.hand_over()
    finish(small_sent)
    plane.own(small_sum)[...] = plane.total(small, small_slots).astype(small_sum.dtype)
    small_sent = plane.spread(small_sum, 1)
    if swaps:
        swap.begin()
    products(ffn_all, gu_middle, gu_end, flat(1), to_gateup, *wide)
    tokens_spread.pass_on()
    gather.hand_over_last()
    gather.end()
    products(mix_all, 0, 2 * inner // WIDE, flat(0), side_by_side(grad_inproj, 0), *wide)
    finish(small_sent)
    gain_own[...] = small_sum[SMALL_ROWS - GAIN_ROWS : SMALL_ROWS, :].astype(jnp.float32)
    gain_sent = [tp.one(gain_own, gain_slots.at[hop], 0, hop) for hop in range(tp.count - 1)]
    vectors_sum[...] = small_sum[:SMALL_ROWS, :].astype(jnp.float32)
    step_sum[...] = small_sum[SMALL_ROWS : SMALL_ROWS + rank, :].astype(jnp.float32)
    select_sum[...] = small_sum[SMALL_ROWS + rank : SMALL_ROWS + rank + selected, :].astype(
        jnp.float32
    )
    if swaps:
        swap.end()
    products(gated_all, 0, inner // WIDE, tall(3), one_above_other(grad_outproj), *high)
    finish(gain_sent)
    total = gain_own[...]
    for hop in range(tp.count - 1):
        total = total + gain_slots[hop]
    gains[...] = total
    tokens_spread.end()
    layer_spread.end()


def run_tail(
    call_id,
    selected,
    swaps,
    conv_grad,
    gate_grad,
    vectors,
    layer_first,
    layer_rows,
    middle_low,
    step_low,
    pre_low,
    select_low,
    scan_in,
    tokens,
    middle_grad,
    gain_row,
    in_conv,
    in_gate,
    one_cols,
    two_cols,
    ct_cols,
    middle_cols,
    ffn_all,
    gated_all,
):
    rows, inner = conv_grad.shape
    rank = step_low.shape[1]
    hidden = ffn_all.shape[1] // 3
    width = tokens.shape[1]
    share = one_cols.shape[1]
    all_rows = ffn_all.shape[0]
    tp_count, plane_count = group_size(("tp",)), group_size(PLANE)
    low, full = jnp.bfloat16, jnp.float32
    vmem = pl.BlockSpec(memory_space=pltpu.VMEM)
    hbm = pl.BlockSpec(memory_space=pltpu.HBM)
    dma = pltpu.SemaphoreType.DMA
    small_rows = SMALL_ROWS + rank + selected
    small = jax.ShapeDtypeStruct((small_rows + -small_rows % (16 * plane_count), inner), low)
    part = jax.ShapeDtypeStruct((rows, width), low)
    return pl.pallas_call(
        functools.partial(tail_kernel, swaps),
        in_specs=[vmem] * 18 + [hbm] * 8,
        out_specs=[vmem] * 6 + [hbm] * 5,
        out_shape=[
            jax.ShapeDtypeStruct(tokens.shape, low),
            jax.ShapeDtypeStruct(tokens.shape, low),
            jax.ShapeDtypeStruct((SMALL_ROWS, inner), full),
            jax.ShapeDtypeStruct((rank, inner), full),
            jax.ShapeDtypeStruct((selected, inner), full),
            jax.ShapeDtypeStruct((GAIN_ROWS, inner), full),
            jax.ShapeDtypeStruct((all_rows, 2 * inner), low),
            jax.ShapeDtypeStruct((2, share, inner), full),
            jax.ShapeDtypeStruct((inner, share), full),
            jax.ShapeDtypeStruct((2, share, hidden), full),
            jax.ShapeDtypeStruct((hidden, share), full),
        ],
        scratch_shapes=[
            pltpu.VMEM((rows, 2 * inner), low),
            pltpu.VMEM(part.shape, low),
            pltpu.VMEM(small.shape, low),
            pltpu.VMEM(small.shape, low),
            slots_for(small, plane_count),
            pltpu.VMEM((tp_count - 1, GAIN_ROWS, inner), full),
            pltpu.VMEM((GAIN_ROWS, inner), full),
            pltpu.VMEM((SMALL_ROWS, inner), full),
            pltpu.VMEM((4, all_rows, share), low),
            pltpu.VMEM((2, 2, WIDE, inner), low),
            pltpu.VMEM((2, all_rows, WIDE), low),
            pltpu.VMEM((2, share, WIDE), full),
            pltpu.VMEM((2, WIDE, share), full),
            dma((4,)),
            dma((2, 2)),
            dma((2,)),
            dma((2,)),
            dma((2,)),
            dma((1, tp_count - 1)),
            dma((1, tp_count - 1)),
            dma((2, plane_count - 1)),
            dma((2, plane_count - 1)),
        ]
        + gather_scratch()
        + line_sum_scratch(part, width // WIDE)
        + line_spread_scratch() * 2
        + (swap_scratch([tokens]) if swaps else []),
        compiler_params=pltpu.CompilerParams(
            collective_id=call_id, has_side_effects=True, vmem_limit_bytes=VMEM_GRANT
        ),
    )(
        conv_grad,
        gate_grad,
        *vectors,
        layer_first,
        layer_rows,
        middle_low,
        step_low,
        pre_low,
        select_low,
        scan_in,
        tokens,
        middle_grad,
        gain_row,
        in_conv,
        in_gate,
        one_cols,
        two_cols,
        ct_cols,
        middle_cols,
        ffn_all,
        gated_all,
    )


BORDER = 16


def head_kernel(
    tokens,
    gain,
    in_conv,
    in_gate,
    conv_in,
    gate_mix,
    border,
    conv_all,
    gate_all,
    normed,
    block_buf,
    block_sem,
    border_send,
    border_recv,
    *sems,
):
    place, places = lax.axis_index("ctx"), lax.axis_size("ctx")
    seqs = border.shape[0] // BORDER
    span = conv_in.shape[0] // seqs

    def to_next(seq):
        return send_on(
            conv_in.at[pl.ds((seq + 1) * span - BORDER, BORDER), :],
            border.at[pl.ds(seq * BORDER, BORDER), :],
            border_send.at[seq],
            border_recv.at[seq],
            place + 1,
        )

    conv = PlaneGather(in_conv, conv_all, *sems[:2])
    gate = PlaneGather(in_gate, gate_all, *sems[3:5])
    greet([(PLANE, conv.others)])
    conv.begin(sems[2])
    gate.begin(sems[5])
    hidden_in = tokens[...].astype(jnp.float32)
    normed[...] = (hidden_in * inverse_rms(hidden_in) * gain[...].astype(jnp.float32)).astype(
        normed.dtype
    )
    conv.relay()
    conv.hand_over()
    gate.relay()
    conv.hand_over_last()
    gate.hand_over()
    conv.end()
    product_in_blocks(normed, conv_all, conv_in, block_buf, block_sem)

    @pl.when(place == 0)
    def _():
        border[...] = jnp.zeros_like(border)

    @pl.when(place < places - 1)
    def _():
        for seq in range(seqs):
            to_next(seq).start()

    gate.hand_over_last()
    gate.end()
    product_in_blocks(normed, gate_all, gate_mix, block_buf, block_sem)

    @pl.when(place < places - 1)
    def _():
        for seq in range(seqs):
            to_next(seq).wait_send()

    @pl.when(place > 0)
    def _():
        for seq in range(seqs):
            to_next(seq).wait_recv()


def run_head(call_id, tokens, gain, inproj, seqs):
    rows, width = tokens.shape
    inner = inproj.shape[2]
    low = jnp.bfloat16
    vmem = pl.BlockSpec(memory_space=pltpu.VMEM)
    hbm = pl.BlockSpec(memory_space=pltpu.HBM)
    return pl.pallas_call(
        head_kernel,
        in_specs=[vmem] * 2 + [hbm] * 2,
        out_specs=[vmem] * 3 + [hbm] * 2,
        out_shape=[
            jax.ShapeDtypeStruct((rows, inner), low),
            jax.ShapeDtypeStruct((rows, inner), jnp.float32),
            jax.ShapeDtypeStruct((seqs * BORDER, inner), low),
            jax.ShapeDtypeStruct((width, inner), low),
            jax.ShapeDtypeStruct((width, inner), low),
        ],
        scratch_shapes=[
            pltpu.VMEM((rows, width), low),
            pltpu.VMEM((2, width, WIDE), low),
            pltpu.SemaphoreType.DMA((2,)),
            pltpu.SemaphoreType.DMA((seqs,)),
            pltpu.SemaphoreType.DMA((seqs,)),
        ]
        + gather_scratch() * 2,
        compiler_params=pltpu.CompilerParams(
            collective_id=call_id, has_side_effects=True, vmem_limit_bytes=VMEM_GRANT
        ),
    )(tokens, gain, inproj[0], inproj[1])


def per_device(
    tokens,
    mixgain,
    inproj,
    convkern,
    convbias,
    selproj,
    stepproj,
    stepbias,
    decaylog,
    skipgain,
    outproj,
    ffngain,
    gateup,
    downproj,
    cotangent,
):
    seqs, span, width = tokens.shape
    rows = seqs * span
    taps, inner = convkern.shape
    rank = stepproj.shape[0]
    n_state = decaylog.shape[1]
    tiles = inner // LANE
    gain_mix = mixgain.astype(jnp.float32)
    kernel = convkern.astype(jnp.float32)
    kernel_bias = convbias.astype(jnp.float32)
    step_bias = stepbias.astype(jnp.float32)
    skip_weight = skipgain.astype(jnp.float32)
    decay_rate = -jnp.exp(jnp.transpose(decaylog.astype(jnp.float32)))
    rate = (decay_rate * LOG2E).reshape(n_state, tiles, LANE)

    gain_mix_row, gain_ffn_row = mixgain.reshape(1, width), ffngain.reshape(1, width)
    low = jnp.bfloat16

    tokens_rows = tokens.reshape(rows, width)
    ct_low = cotangent.reshape(rows, width)
    swap_now = swaps_in_kernels(width)
    ffn_pack = gathered_rows(
        jnp.concatenate([gateup[0], gateup[1], jnp.transpose(downproj)], 1)
    )
    conv_in, gate_mix, border, in_conv, in_gate = run_head(
        5, tokens_rows, gain_mix_row, inproj, seqs
    )
    hidden_in = tokens_rows.astype(jnp.float32)
    scale_one = inverse_rms(hidden_in)
    normed_one = (hidden_in * scale_one * gain_mix).astype(low)

    conv_seqs = conv_in.reshape(seqs, span, inner)
    rim_rows = border.reshape(seqs, BORDER, inner)[:, BORDER - (taps - 1) :]
    padded_in = jnp.concatenate([rim_rows, conv_seqs], 1).astype(jnp.float32)
    conv_out = kernel_bias[None, None]
    for offset in range(taps):
        conv_out = conv_out + kernel[offset][None, None] * padded_in[:, offset : offset + span]
    conv_out = conv_out.reshape(rows, inner)
    scan_in = jax.nn.silu(conv_out).astype(low)
    scan_float = scan_in.astype(jnp.float32)
    columns = selproj.shape[1]
    select_width = -(-columns // LANE) * LANE
    select_weights = jnp.pad(selproj, ((0, 0), (0, select_width - columns)))
    select_cols, out_first = run_select(0, matmul(scan_in, select_weights), outproj[: inner // 2])

    def columns_of(swapped, array):
        if not swapped:
            return swapped_columns(array)
        return swapped[0].reshape(-1, swapped[0].shape[-1])

    step_low = select_cols[:, :rank].astype(low)
    b_rows = select_cols[:, rank : rank + n_state].reshape(-1)
    c_rows = select_cols[:, rank + n_state : columns].reshape(-1)
    step_pre = matmul(step_low, stepproj) + step_bias[None]
    step_size = jax.nn.softplus(step_pre)
    in_pairs = lax.axis_size("ctx") == 2
    if in_pairs:
        prior, scan_out, out_last = scan_forward_pair(
            6,
            step_size,
            scan_float,
            b_rows,
            c_rows,
            rate,
            seqs,
            outproj[inner // 2 :],
        )
    else:
        span_decay = jnp.exp(
            decay_rate[None] * jnp.sum(step_size.reshape(seqs, span, inner), 1)[:, None]
        ).reshape(seqs, n_state, tiles, LANE)
        ends = scan_ends(step_size, scan_float, b_rows, rate, seqs, False)
        start = from_earlier(ends, span_decay, 1)
        prior, scan_out = scan_forward(start, step_size, scan_float, b_rows, c_rows, rate, seqs)
        out_last = gathered_rows(outproj[inner // 2 :])
    mixer_core = scan_out + skip_weight[None] * scan_float
    gate_sig = jax.nn.silu(gate_mix)
    gated = (mixer_core * gate_sig).astype(low)
    normed_two, middle, gated_all, *swapped = mixer_out(
        1,
        gated,
        out_first,
        out_last,
        tokens_rows,
        gain_ffn_row,
        [normed_one] if swap_now else [],
    )
    normed_one_cols = columns_of(swapped, normed_one)
    made, *swapped = run_ffn(8, normed_two, ct_low, ffn_pack, swap_now)
    ct_cols = columns_of(swapped, ct_low)
    ffn_all = gathered_rows(made)
    middle_low, middle_grad, ffngain_part, gated_grad, ffn_part, *swapped = ffn_back(
        2,
        made,
        ct_low,
        middle,
        gain_ffn_row,
        out_first,
        out_last,
        ffn_pack,
        [normed_two] if swap_now else [],
    )
    normed_two_cols = columns_of(swapped, normed_two)
    core_grad = gated_grad * gate_sig
    gate_mix_grad = (gated_grad * mixer_core * silu_slope(gate_mix)).astype(low)
    grad_skipgain = jnp.sum(core_grad * scan_float, 0)
    if in_pairs:
        step_grad, input_grad, rate_grad, parts, *layer_rows = scan_backward_pair(
            7,
            prior,
            step_size,
            scan_float,
            core_grad,
            b_rows,
            c_rows,
            rate,
            seqs,
            ffn_part,
            middle,
            [],
        )
    else:
        back_ends = scan_ends(step_size, core_grad, c_rows, rate, seqs, True)
        end_grad = from_earlier(back_ends, span_decay, -1)
        step_grad, input_grad, rate_grad, parts = scan_backward(
            end_grad, prior, step_size, scan_float, core_grad, b_rows, c_rows, rate, seqs
        )
        ffn_sum = lax.psum_scatter(ffn_part, "tp", scatter_dimension=0, tiled=True)
        layer_rows = jnp.split((middle + ffn_sum.astype(jnp.float32)).astype(low), 2, 1)
    grad_decaylog = rate_grad.reshape(n_state, inner) * decay_rate
    pre_grad = step_grad * jax.nn.sigmoid(step_pre)
    grad_stepbias = jnp.sum(pre_grad, 0)
    pre_low = pre_grad.astype(low)
    select_part = jnp.concatenate(
        [
            matmul_nt(pre_low, stepproj),
            jnp.sum(parts, -1),
            jnp.zeros((rows, select_width - columns), jnp.float32),
        ],
        1,
    ).astype(low)
    select_low, layer_first = sum_over_tp(3, select_part, layer_rows[0])
    scan_in_grad = (
        core_grad * skip_weight[None]
        + input_grad
        + matmul_nt(select_low, select_weights)
    )
    conv_grad = scan_in_grad * silu_slope(conv_out)
    grad_convbias = jnp.sum(conv_grad, 0)
    conv_grad_seqs = conv_grad.reshape(seqs, span, inner)
    padded_grad = jnp.zeros(padded_in.shape, jnp.float32)
    kernel_rows = []
    for offset in range(taps):
        kernel_rows.append(jnp.sum(conv_grad_seqs * padded_in[:, offset : offset + span], (0, 1)))
        padded_grad = padded_grad + jnp.pad(
            kernel[offset][None, None] * conv_grad_seqs,
            ((0, 0), (offset, taps - 1 - offset), (0, 0)),
        )
    grad_convkern = jnp.stack(kernel_rows)
    returned = passed_along(padded_grad[:, : taps - 1], "ctx", -1)
    conv_in_grad = (
        (padded_grad[:, taps - 1 :] + jnp.pad(returned, ((0, 0), (span - taps + 1, 0), (0, 0))))
        .astype(low)
        .reshape(rows, inner)
    )
    vectors = [
        grad_convkern,
        grad_convbias[None],
        grad_stepbias[None],
        grad_decaylog,
        grad_skipgain[None],
        ffngain_part,
    ]
    (
        tokens_grad,
        layer_out,
        vectors,
        grad_stepproj,
        grad_selproj,
        gains,
        _,
        grad_inproj,
        grad_outproj,
        grad_gateup,
        grad_downproj,
    ) = run_tail(
        4,
        columns,
        swap_now,
        conv_in_grad,
        gate_mix_grad,
        vectors,
        layer_first,
        layer_rows[1],
        middle_low,
        step_low,
        pre_low,
        select_low,
        scan_in,
        tokens_rows,
        middle_grad,
        gain_mix_row,
        in_conv,
        in_gate,
        normed_one_cols,
        normed_two_cols,
        ct_cols,
        normed_two_cols if swap_now else swapped_columns(middle_low),
        ffn_all,
        gated_all,
    )
    at = taps + 2
    return (
        layer_out.reshape(tokens.shape),
        tokens_grad.reshape(tokens.shape),
        gains[8:10].reshape(width),
        grad_inproj,
        vectors[:taps],
        vectors[taps],
        jnp.transpose(grad_selproj),
        grad_stepproj,
        vectors[taps + 1],
        jnp.transpose(vectors[at : at + n_state]),
        vectors[at + n_state],
        grad_outproj,
        gains[10:12].reshape(width),
        grad_gateup,
        grad_downproj,
    )


def solution(mesh):
    in_specs = (
        P("dp", "ctx", None),
        P(),
        P(None, ("dp", "ctx"), "tp"),
        P(None, "tp"),
        P("tp"),
        P("tp", None),
        P(None, "tp"),
        P("tp"),
        P("tp", None),
        P("tp"),
        P("tp", ("dp", "ctx")),
        P(),
        P(None, ("dp", "ctx"), "tp"),
        P("tp", ("dp", "ctx")),
        P("dp", "ctx", None),
    )
    out_specs = (
        P("dp", "ctx", None),
        P("dp", "ctx", None),
        P(),
        P(None, ("dp", "ctx"), "tp"),
        P(None, "tp"),
        P("tp"),
        P("tp", None),
        P(None, "tp"),
        P("tp"),
        P("tp", None),
        P("tp"),
        P("tp", ("dp", "ctx")),
        P(),
        P(None, ("dp", "ctx"), "tp"),
        P("tp", ("dp", "ctx")),
    )
    return jax.shard_map(
        per_device, mesh=mesh, in_specs=in_specs, out_specs=out_specs, check_vma=False
    )
```

```python
import functools
import math

import jax
import jax.numpy as jnp
from jax import lax
from jax.experimental import pallas as pl
from jax.experimental.pallas import tpu as pltpu
from jax.sharding import PartitionSpec as P

EPSILON = 1e-05
LOG2E = math.log2(math.e)
LN2 = math.log(2.0)
SUB = 8
LANE = 128
VMEM_GRANT = 60 * 2**20
PLANE = ("dp", "ctx")


def passed_along(value, axis, steps):
    count = lax.axis_size(axis)
    first, last = (max(0, -steps), min(count, count - steps))
    return lax.ppermute(value, axis, [(source, source + steps) for source in range(first, last)])


def matmul(left, right):
    return jnp.dot(left, right, preferred_element_type=jnp.float32)


def matmul_nt(left, right):
    return lax.dot_general(
        left, right, (((1,), (1,)), ((), ())), preferred_element_type=jnp.float32
    )


def matmul_tn(left, right):
    return lax.dot_general(
        left, right, (((0,), (0,)), ((), ())), preferred_element_type=jnp.float32
    )


def inverse_rms(values):
    return lax.rsqrt(jnp.mean(values * values, -1, keepdims=True) + EPSILON)


def silu_slope(values):
    logistic = jax.nn.sigmoid(values)
    return logistic * (1.0 + values * (1.0 - logistic))


def norm_back(grad_norm, values, scale, gain):
    scaled_grad = grad_norm * gain
    unit_rows = values * scale
    return scale * (scaled_grad - unit_rows * jnp.mean(scaled_grad * unit_rows, -1, keepdims=True))


def stage_in(ref, group, held):
    for tile in range(held.shape[0] // SUB):
        held[pl.ds(tile * SUB, SUB), :] = ref[
            pl.ds(pl.multiple_of(group * SUB, SUB), SUB), pl.ds(tile * LANE, LANE)
        ]


def stage_out(held, ref, group):
    for tile in range(held.shape[0] // SUB):
        ref[pl.ds(pl.multiple_of(group * SUB, SUB), SUB), pl.ds(tile * LANE, LANE)] = held[
            pl.ds(tile * SUB, SUB), :
        ]


def token_row(held, at, tiles):
    return held[pl.ds(at, tiles, stride=SUB), :]


def ends_kernel(
    n_state,
    tiles,
    groups,
    reverse,
    step_ref,
    drive_ref,
    rows_ref,
    rate_ref,
    end_ref,
    step_held,
    drive_held,
):
    base = pl.program_id(0) * groups * SUB * n_state
    rates = [rate_ref[n] for n in range(n_state)]

    def one(turn, states):
        group = groups - 1 - turn if reverse else turn
        order = range(SUB - 1, -1, -1) if reverse else range(SUB)
        states = list(states)
        stage_in(step_ref, group, step_held)
        stage_in(drive_ref, group, drive_held)
        for at in order:
            step = token_row(step_held, at, tiles)
            drive = token_row(drive_held, at, tiles)
            if not reverse:
                drive = drive * step
            for n in range(n_state):
                row = rows_ref[base + (group * SUB + at) * n_state + n]
                decay = jnp.exp2(step * rates[n])
                if reverse:
                    states[n] = decay * (states[n] + drive * row)
                else:
                    states[n] = decay * states[n] + drive * row
        return tuple(states)

    zero = jnp.zeros((tiles, LANE), jnp.float32)
    states = lax.fori_loop(0, groups, one, (zero,) * n_state)
    for n in range(n_state):
        end_ref[0, n] = states[n]


def scan_ends(step, drive, rows, rate, seqs, reverse):
    n_state, tiles, _ = rate.shape
    groups = step.shape[0] // seqs // SUB
    rows_spec = pl.BlockSpec((groups * SUB, tiles * LANE), lambda s: (s, 0))
    held = pltpu.VMEM((tiles * SUB, LANE), jnp.float32)
    return pl.pallas_call(
        functools.partial(ends_kernel, n_state, tiles, groups, reverse),
        grid=(seqs,),
        in_specs=[
            rows_spec,
            rows_spec,
            pl.BlockSpec(memory_space=pltpu.SMEM),
            pl.BlockSpec((n_state, tiles, LANE), lambda s: (0, 0, 0)),
        ],
        out_specs=pl.BlockSpec((1, n_state, tiles, LANE), lambda s: (s, 0, 0, 0)),
        out_shape=jax.ShapeDtypeStruct((seqs, n_state, tiles, LANE), jnp.float32),
        scratch_shapes=[held, held],
        compiler_params=pltpu.CompilerParams(vmem_limit_bytes=VMEM_GRANT),
    )(step, drive, rows, rate)


def forward_kernel(
    n_state,
    tiles,
    groups,
    blocks,
    start_ref,
    step_ref,
    input_ref,
    brow_ref,
    crow_ref,
    rate_ref,
    prior_ref,
    mixed_ref,
    carried,
    step_held,
    input_held,
    mixed_held,
):
    base = (pl.program_id(0) * blocks + pl.program_id(1)) * groups * SUB * n_state

    @pl.when(pl.program_id(1) == 0)
    def _():
        carried[...] = start_ref[0]

    def one(group, states):
        states = list(states)
        stage_in(step_ref, group, step_held)
        stage_in(input_ref, group, input_held)
        for at in range(SUB):
            step = token_row(step_held, at, tiles)
            drive = step * token_row(input_held, at, tiles)
            mixed = [None] * 2
            for n in range(n_state):
                where = base + (group * SUB + at) * n_state + n
                prior_ref[group * SUB + at, n] = states[n]
                decay = jnp.exp2(step * rate_ref[n])
                states[n] = decay * states[n] + drive * brow_ref[where]
                term = states[n] * crow_ref[where]
                mixed[n % 2] = term if mixed[n % 2] is None else mixed[n % 2] + term
            mixed_held[pl.ds(at, tiles, stride=SUB), :] = mixed[0] + mixed[1]
        stage_out(mixed_held, mixed_ref, group)
        return tuple(states)

    states = lax.fori_loop(0, groups, one, tuple(carried[n] for n in range(n_state)))
    for n in range(n_state):
        carried[n] = states[n]


def scan_forward(start, step, inputs, b_rows, c_rows, rate, seqs):
    n_state, tiles, _ = rate.shape
    all_groups = step.shape[0] // SUB
    groups = math.gcd(all_groups // seqs, 4)
    blocks = all_groups // seqs // groups
    rows_spec = pl.BlockSpec((groups * SUB, tiles * LANE), lambda s, b: (s * blocks + b, 0))
    held = pltpu.VMEM((tiles * SUB, LANE), jnp.float32)
    smem = pl.BlockSpec(memory_space=pltpu.SMEM)
    tokens = all_groups * SUB
    return pl.pallas_call(
        functools.partial(forward_kernel, n_state, tiles, groups, blocks),
        grid=(seqs, blocks),
        in_specs=[
            pl.BlockSpec((1, n_state, tiles, LANE), lambda s, b: (s, 0, 0, 0)),
            rows_spec,
            rows_spec,
            smem,
            smem,
            pl.BlockSpec((n_state, tiles, LANE), lambda s, b: (0, 0, 0)),
        ],
        out_specs=[
            pl.BlockSpec(
                (groups * SUB, n_state, tiles, LANE), lambda s, b: (s * blocks + b, 0, 0, 0)
            ),
            rows_spec,
        ],
        out_shape=[
            jax.ShapeDtypeStruct((tokens, n_state, tiles, LANE), jnp.float32),
            jax.ShapeDtypeStruct(step.shape, jnp.float32),
        ],
        scratch_shapes=[pltpu.VMEM((n_state, tiles, LANE), jnp.float32)] + [held] * 3,
        compiler_params=pltpu.CompilerParams(vmem_limit_bytes=VMEM_GRANT),
    )(start, step, inputs, b_rows, c_rows, rate)


def backward_kernel(
    n_state,
    tiles,
    groups,
    blocks,
    end_ref,
    prior_ref,
    step_ref,
    input_ref,
    ograd_ref,
    brow_ref,
    crow_ref,
    rate_ref,
    picks_ref,
    step_grad_ref,
    input_grad_ref,
    rate_grad_ref,
    part_ref,
    carried,
    step_held,
    input_held,
    ograd_held,
    step_grad_held,
    input_grad_held,
):
    block = blocks - 1 - pl.program_id(1)
    base = (pl.program_id(0) * blocks + block) * groups * SUB * n_state

    @pl.when(pl.program_id(1) == 0)
    def _():
        carried[...] = end_ref[0]

    @pl.when((pl.program_id(0) == 0) & (pl.program_id(1) == 0))
    def _():
        rate_grad_ref[...] = jnp.zeros_like(rate_grad_ref)

    def one(turn, grads):
        group = groups - 1 - turn
        grads = list(grads)
        stage_in(step_ref, group, step_held)
        stage_in(input_ref, group, input_held)
        stage_in(ograd_ref, group, ograd_held)
        for at in range(SUB - 1, -1, -1):
            step = token_row(step_held, at, tiles)
            value = token_row(input_held, at, tiles)
            ograd = token_row(ograd_held, at, tiles)
            drive = step * value
            along_b = None
            along_rate = None
            brow_parts, crow_parts = [], []
            for n in range(n_state):
                where = base + (group * SUB + at) * n_state + n
                brow, crow = brow_ref[where], crow_ref[where]
                rate = rate_ref[n]
                decay = jnp.exp2(step * rate)
                grad = ograd * crow + grads[n]
                kept = decay * prior_ref[group * SUB + at, n]
                state = kept + drive * brow
                decay_term = grad * kept
                grads[n] = decay * grad
                rate_grad_ref[n] += decay_term * step
                by_rate, by_brow = decay_term * rate, grad * brow
                along_rate = by_rate if along_rate is None else along_rate + by_rate
                along_b = by_brow if along_b is None else along_b + by_brow
                brow_parts.append(grad * drive)
                crow_parts.append(ograd * state)
            step_grad_held[pl.ds(at, tiles, stride=SUB), :] = along_rate * LN2 + along_b * value
            input_grad_held[pl.ds(at, tiles, stride=SUB), :] = along_b * step
            parts = jnp.concatenate(brow_parts + crow_parts, 0).astype(jnp.bfloat16)
            part_ref[group * SUB + at] = jnp.dot(
                picks_ref[...], parts, preferred_element_type=jnp.float32
            )
        stage_out(step_grad_held, step_grad_ref, group)
        stage_out(input_grad_held, input_grad_ref, group)
        return tuple(grads)

    grads = lax.fori_loop(0, groups, one, tuple(carried[n] for n in range(n_state)))
    for n in range(n_state):
        carried[n] = grads[n]


def scan_backward(end_grad, prior, step, inputs, ograd, b_rows, c_rows, rate, seqs):
    n_state, tiles, _ = rate.shape
    all_groups = step.shape[0] // SUB
    groups = math.gcd(all_groups // seqs, 4)
    blocks = all_groups // seqs // groups

    def at(s, b):
        return s * blocks + blocks - 1 - b

    rows_spec = pl.BlockSpec((groups * SUB, tiles * LANE), lambda s, b: (at(s, b), 0))
    held = pltpu.VMEM((tiles * SUB, LANE), jnp.float32)
    smem = pl.BlockSpec(memory_space=pltpu.SMEM)
    tokens = all_groups * SUB
    picks = jnp.repeat(jnp.eye(2 * n_state, dtype=jnp.bfloat16), tiles, 1)
    return pl.pallas_call(
        functools.partial(backward_kernel, n_state, tiles, groups, blocks),
        grid=(seqs, blocks),
        in_specs=[
            pl.BlockSpec((1, n_state, tiles, LANE), lambda s, b: (s, 0, 0, 0)),
            pl.BlockSpec((groups * SUB, n_state, tiles, LANE), lambda s, b: (at(s, b), 0, 0, 0)),
            rows_spec,
            rows_spec,
            rows_spec,
            smem,
            smem,
            pl.BlockSpec((n_state, tiles, LANE), lambda s, b: (0, 0, 0)),
            pl.BlockSpec(picks.shape, lambda s, b: (0, 0)),
        ],
        out_specs=[
            rows_spec,
            rows_spec,
            pl.BlockSpec((n_state, tiles, LANE), lambda s, b: (0, 0, 0)),
            pl.BlockSpec((groups * SUB, 2 * n_state, LANE), lambda s, b: (at(s, b), 0, 0)),
        ],
        out_shape=[
            jax.ShapeDtypeStruct(step.shape, jnp.float32),
            jax.ShapeDtypeStruct(step.shape, jnp.float32),
            jax.ShapeDtypeStruct(rate.shape, jnp.float32),
            jax.ShapeDtypeStruct((tokens, 2 * n_state, LANE), jnp.float32),
        ],
        scratch_shapes=[pltpu.VMEM((n_state, tiles, LANE), jnp.float32)] + [held] * 5,
        compiler_params=pltpu.CompilerParams(vmem_limit_bytes=VMEM_GRANT),
    )(end_grad, prior, step, inputs, ograd, b_rows, c_rows, rate, picks)


def from_earlier(ends, decay, steps):
    count = lax.axis_size("ctx")
    if count == 1:
        return jnp.zeros_like(ends)
    if count == 2:
        return passed_along(ends, "ctx", steps)
    index = lax.axis_index("ctx")
    all_ends = lax.all_gather(ends, "ctx")
    all_decays = lax.all_gather(decay, "ctx")

    def one(turn, state):
        at = turn if steps > 0 else count - 1 - turn
        reached = at < index if steps > 0 else at > index
        return jnp.where(reached, all_decays[at] * state + all_ends[at], state)

    return lax.fori_loop(0, count, one, jnp.zeros_like(ends))


def gathered_rows(rows):
    return lax.all_gather(rows, PLANE, axis=0, tiled=True)


def swapped_columns(rows):
    return lax.all_to_all(rows, PLANE, split_axis=1, concat_axis=0, tiled=True)


def place_in(axes):
    index = 0
    for axis in axes:
        index = index * lax.axis_size(axis) + lax.axis_index(axis)
    return index


def device_at(axes, index):
    where = {}
    for axis in reversed(axes):
        size = lax.axis_size(axis)
        where[axis] = lax.rem(index, size)
        index = lax.div(index, size)
    return where


def greet(groups):
    barrier = pltpu.get_barrier_semaphore()
    total = 0
    for axes, others in groups:
        for other in others:
            pl.semaphore_signal(
                barrier,
                inc=1,
                device_id=device_at(axes, other),
                device_id_type=pl.DeviceIdType.MESH,
            )
            total += 1
    pl.semaphore_wait(barrier, total)


def sent(source, target, send_sem, recv_sem, where):
    copy = pltpu.make_async_remote_copy(
        src_ref=source,
        dst_ref=target,
        send_sem=send_sem,
        recv_sem=recv_sem,
        device_id=where,
        device_id_type=pl.DeviceIdType.MESH,
    )
    copy.start()
    return copy


def finish(copies):
    for copy in copies:
        copy.wait()


def rows_of(ref, index, count):
    rows = ref.shape[0] // count
    return ref.at[pl.ds(pl.multiple_of(index * rows, rows), rows), :]


class Group:
    def __init__(self, axes, send_sem, recv_sem):
        self.axes = axes
        self.count = math.prod(lax.axis_size(axis) for axis in axes)
        self.me = place_in(axes)
        self.others = [lax.rem(self.me + hop, self.count) for hop in range(1, self.count)]
        self.send_sem, self.recv_sem = send_sem, recv_sem

    def own(self, ref):
        return rows_of(ref, self.me, self.count)

    def one(self, source, target, which, hop):
        return sent(
            source,
            target,
            self.send_sem.at[which, hop],
            self.recv_sem.at[which, hop],
            device_at(self.axes, self.others[hop]),
        )

    def scatter(self, part, slot, which):
        return [
            self.one(rows_of(part, other, self.count), slot.at[hop], which, hop)
            for hop, other in enumerate(self.others)
        ]

    def total(self, part, slot):
        total = self.own(part)[...].astype(jnp.float32)
        for hop in range(self.count - 1):
            total = total + slot[hop].astype(jnp.float32)
        return total

    def spread(self, ref, which):
        return [self.one(self.own(ref), self.own(ref), which, hop) for hop in range(self.count - 1)]


def slots_for(part, count):
    return pltpu.VMEM((count - 1, part.shape[0] // count) + part.shape[1:], part.dtype)


def group_size(axes):
    return math.prod(lax.axis_size(axis) for axis in axes)


def line_of_four():
    me = lax.axis_index("tp")
    near = me + 1 - 2 * lax.rem(me, 2)
    return me, near, lax.rem(me + 2, 4), lax.rem(near + 2, 4)


class LineSum:
    def __init__(self, part, near_slots, far_slot, passed, send_sem, recv_sem):
        self.part, self.near_slots, self.far_slot = part, near_slots, far_slot
        self.passed, self.send_sem, self.recv_sem = passed, send_sem, recv_sem
        self.me, self.near, self.far, self.cross = line_of_four()
        self.blocks = send_sem.shape[1]
        self.copies = []

    def columns(self, j):
        wide = self.part.shape[1] // self.blocks
        return slice(j * wide, (j + 1) * wide)

    def rows(self, index):
        return rows_of(self.part, index, 4)

    def send(self, source, target, which, j, where):
        copy = sent(
            source.at[:, self.columns(j)],
            target.at[:, self.columns(j)],
            self.send_sem.at[which, j],
            self.recv_sem.at[which, j],
            {"tp": where},
        )
        self.copies.append((which, copy))
        return copy

    def begin(self, j):
        first = self.send(self.rows(self.cross), self.near_slots.at[0], 0, j, self.near)
        self.send(self.rows(self.near), self.near_slots.at[1], 1, j, self.near)
        return first

    def pass_on(self, j, first):
        first.wait_recv()
        columns = self.columns(j)
        self.passed[:, columns] = (
            self.rows(self.far)[:, columns].astype(jnp.float32)
            + self.near_slots[0, :, columns].astype(jnp.float32)
        ).astype(self.passed.dtype)
        self.send(self.passed, self.far_slot, 2, j, self.far)

    def total(self):
        for which, copy in self.copies:
            copy.wait_send()
            if which:
                copy.wait_recv()
        return (
            self.rows(self.me)[...].astype(jnp.float32)
            + self.near_slots[1].astype(jnp.float32)
            + self.far_slot[...].astype(jnp.float32)
        )

    def pass_all(self, firsts):
        for j, first in enumerate(firsts):
            self.pass_on(j, first)


def line_sum_scratch(part, blocks):
    share = (part.shape[0] // 4,) + part.shape[1:]
    sems = pltpu.SemaphoreType.DMA((3, blocks))
    return [
        pltpu.VMEM((2,) + share, part.dtype),
        pltpu.VMEM(share, part.dtype),
        pltpu.VMEM(share, part.dtype),
        sems,
        sems,
    ]


class LineSpread:
    def __init__(self, ref, send_sem, recv_sem):
        self.ref, self.send_sem, self.recv_sem = ref, send_sem, recv_sem
        self.me, self.near, self.far, self.cross = line_of_four()

    def send(self, owner, half, which, where):
        rows = rows_of(self.ref, owner, 4)
        if half is not None:
            wide = self.ref.shape[1] // 2
            rows = rows.at[:, half * wide : (half + 1) * wide]
        return sent(rows, rows, self.send_sem.at[which], self.recv_sem.at[which], {"tp": where})

    def begin(self):
        self.across = [self.send(self.me, half, half, self.far) for half in range(2)]
        self.within = [self.send(self.me, None, 2, self.near)]

    def pass_on(self):
        for half, copy in enumerate(self.across):
            copy.wait_recv()
            self.within.append(self.send(self.far, half, 3 + half, self.near))

    def end(self):
        for copy in self.across:
            copy.wait_send()
        finish(self.within)

    def run(self):
        self.begin()
        self.pass_on()
        self.end()


def line_spread_scratch():
    return [pltpu.SemaphoreType.DMA((5,)), pltpu.SemaphoreType.DMA((5,))]


class Swap:
    def __init__(self, arrays, swapped, send_sem, recv_sem, local_sem):
        plane = Group(PLANE, send_sem, recv_sem)
        self.plane, self.arrays, self.swapped, self.local_sem = plane, arrays, swapped, local_sem

    def begin(self):
        self.copies, plane = [], self.plane
        for which, (array, swapped) in enumerate(zip(self.arrays, self.swapped)):
            share = swapped.shape[1]

            def columns(index):
                return array.at[:, pl.ds(pl.multiple_of(index * share, share), share)]

            for hop, other in enumerate(plane.others):
                self.copies.append(plane.one(columns(other), plane.own(swapped), which, hop))
            local = pltpu.make_async_copy(
                columns(plane.me), plane.own(swapped), self.local_sem.at[which]
            )
            local.start()
            self.copies.append(local)

    def end(self):
        finish(self.copies)


def swap_scratch(arrays):
    sems = pltpu.SemaphoreType.DMA((len(arrays), group_size(PLANE) - 1))
    return [sems, sems, pltpu.SemaphoreType.DMA((len(arrays),))] if arrays else []


def swap_shapes(arrays):
    count = group_size(PLANE)
    return [
        jax.ShapeDtypeStruct((array.shape[0] * count, array.shape[1] // count), array.dtype)
        for array in arrays
    ]


def swaps_in_kernels(width):
    return width // group_size(PLANE) % LANE == 0


def gathered_shape(shard):
    return jax.ShapeDtypeStruct(
        (shard.shape[0] * group_size(PLANE),) + shard.shape[1:], shard.dtype
    )


def gather_scratch():
    return [gather_sems(), gather_sems(), pltpu.SemaphoreType.DMA(())]


def product_in_blocks(left, source, target, block_buf, block_sem):
    columns = range(0, source.shape[1], WIDE)

    def fetch(turn):
        at = columns[turn]
        return pltpu.make_async_copy(
            source.at[:, at : at + WIDE], block_buf.at[turn % 2], block_sem.at[turn % 2]
        )

    fetch(0).start()
    for turn, at in enumerate(columns):
        if turn + 1 < len(columns):
            fetch(turn + 1).start()
        fetch(turn).wait()
        target[:, at : at + WIDE] = matmul(left[...], block_buf[turn % 2]).astype(target.dtype)


def select_kernel(
    part, shard, total, gathered, slots, send_sem, recv_sem, gather_send, gather_recv, local_sem
):
    group = Group(("tp",), send_sem, recv_sem)
    gather = PlaneGather(shard, gathered, gather_send, gather_recv)
    greet([(("tp",), group.others), (PLANE, gather.others)])
    copies = group.scatter(part, slots, 0)
    gather.begin(local_sem)
    finish(copies)
    group.own(total)[...] = group.total(part, slots).astype(total.dtype)
    copies = group.spread(total, 1)
    gather.relay()
    gather.hand_over()
    finish(copies)
    gather.hand_over_last()
    gather.end()


def run_select(call_id, part, shard):
    count = group_size(("tp",))
    vmem = pl.BlockSpec(memory_space=pltpu.VMEM)
    hbm = pl.BlockSpec(memory_space=pltpu.HBM)
    sems = pltpu.SemaphoreType.DMA((2, count - 1))
    return pl.pallas_call(
        select_kernel,
        in_specs=[vmem, hbm],
        out_specs=[vmem, hbm],
        out_shape=[jax.ShapeDtypeStruct(part.shape, part.dtype), gathered_shape(shard)],
        scratch_shapes=[slots_for(part, count), sems, sems] + gather_scratch(),
        compiler_params=pltpu.CompilerParams(
            collective_id=call_id, has_side_effects=True, vmem_limit_bytes=VMEM_GRANT
        ),
    )(part, shard)


def sum_kernel(part, own_rows, total, all_rows, slots, send_sem, recv_sem, *line_sems):
    group = Group(("tp",), send_sem, recv_sem)
    rows = LineSpread(all_rows, *line_sems)
    greet([(("tp",), group.others)])
    copies = group.scatter(part, slots, 0)
    group.own(all_rows)[...] = own_rows[...]
    rows.begin()
    finish(copies)
    group.own(total)[...] = group.total(part, slots).astype(total.dtype)
    copies = group.spread(total, 1)
    rows.pass_on()
    finish(copies)
    rows.end()


def sum_over_tp(call_id, part, own_rows):
    count = group_size(("tp",))
    vmem = pl.BlockSpec(memory_space=pltpu.VMEM)
    sems = pltpu.SemaphoreType.DMA((2, count - 1))
    return pl.pallas_call(
        sum_kernel,
        in_specs=[vmem] * 2,
        out_specs=[vmem] * 2,
        out_shape=[
            jax.ShapeDtypeStruct(part.shape, part.dtype),
            jax.ShapeDtypeStruct((own_rows.shape[0] * count, own_rows.shape[1]), own_rows.dtype),
        ],
        scratch_shapes=[slots_for(part, count), sems, sems] + line_spread_scratch(),
        compiler_params=pltpu.CompilerParams(
            collective_id=call_id, has_side_effects=True, vmem_limit_bytes=VMEM_GRANT
        ),
    )(part, own_rows)


def mixer_out_kernel(n_swaps, gated, out_first, out_last, tokens, gain, *refs):
    arrays, refs = refs[:n_swaps], refs[n_swaps:]
    normed, middle, gated_all, *refs = refs
    swapped, refs = refs[:n_swaps], refs[n_swaps:]
    part, refs = refs[0], refs[1:]
    line = LineSum(part, *refs[:5])
    spread = LineSpread(normed, *refs[5:7])
    gather_send, gather_recv, local_sem, *refs = refs[7:]
    group = Group(("tp",), None, None)
    gather = PlaneGather(gated, gated_all, gather_send, gather_recv)
    half = gated.shape[1] // 2
    share = out_first.shape[1]
    greet([(("tp",), group.others), (PLANE, gather.others)])
    gather.begin(local_sem)
    for at in range(out_first.shape[0] // half):
        rows = slice(at * half, (at + 1) * half)
        part[:, at * share : (at + 1) * share] = (
            matmul(gated[:, :half], out_first[rows, :])
            + matmul(gated[:, half:], out_last[rows, :])
        ).astype(part.dtype)
    firsts = [line.begin(j) for j in range(line.blocks)]
    if n_swaps:
        swap = Swap(arrays, swapped, *refs)
        swap.begin()
    line.pass_all(firsts)
    rows = group.own(tokens)[...].astype(jnp.float32) + line.total()
    middle[...] = rows
    group.own(normed)[...] = (rows * inverse_rms(rows) * gain[...].astype(jnp.float32)).astype(
        normed.dtype
    )
    spread.begin()
    gather.relay()
    gather.hand_over()
    spread.pass_on()
    spread.end()
    gather.hand_over_last()
    gather.end()
    if n_swaps:
        swap.end()


def mixer_out(call_id, gated, out_first, out_last, tokens, gain, arrays):
    count = group_size(("tp",))
    vmem = pl.BlockSpec(memory_space=pltpu.VMEM)
    hbm = pl.BlockSpec(memory_space=pltpu.HBM)
    rows, width = tokens.shape
    part = jax.ShapeDtypeStruct((rows, width), jnp.bfloat16)
    return pl.pallas_call(
        functools.partial(mixer_out_kernel, len(arrays)),
        in_specs=[vmem] * (5 + len(arrays)),
        out_specs=[vmem] * 2 + [hbm] + [hbm] * len(arrays),
        out_shape=[
            part,
            jax.ShapeDtypeStruct((rows // count, width), jnp.float32),
            gathered_shape(gated),
        ]
        + swap_shapes(arrays),
        scratch_shapes=[pltpu.VMEM(part.shape, part.dtype)]
        + line_sum_scratch(part, 2)
        + line_spread_scratch()
        + gather_scratch()
        + swap_scratch(arrays),
        compiler_params=pltpu.CompilerParams(
            collective_id=call_id, has_side_effects=True, vmem_limit_bytes=VMEM_GRANT
        ),
    )(gated, out_first, out_last, tokens, gain, *arrays)


def ffn_kernel(swaps, normed, ct, weights, made, *refs):
    hidden = weights.shape[1] // 3
    if swaps:
        *swapped, block_buf, block_sem, send_sem, recv_sem, local_sem = refs
        swap = Swap([ct], swapped, send_sem, recv_sem, local_sem)
        greet([(PLANE, swap.plane.others)])
        swap.begin()
    else:
        block_buf, block_sem = refs

    def columns(j, which):
        return pl.ds(pl.multiple_of(which * hidden + j * WIDE, WIDE), WIDE)

    def fetch(j, which):
        slot = lax.rem(j, 2)
        return pltpu.make_async_copy(
            weights.at[:, columns(j, which)],
            block_buf.at[slot, which],
            block_sem.at[slot, which],
        )

    for which in range(3):
        fetch(0, which).start()

    @pl.loop(0, hidden // WIDE)
    def _(j):
        slot = lax.rem(j, 2)

        @pl.when(j + 1 < hidden // WIDE)
        def _():
            for which in range(3):
                fetch(j + 1, which).start()

        fetch(j, 0).wait()
        gate = matmul(normed[...], block_buf[slot, 0])
        fetch(j, 1).wait()
        up = matmul(normed[...], block_buf[slot, 1])
        fetch(j, 2).wait()
        act_grad = matmul(ct[...], block_buf[slot, 2])
        logistic = jax.nn.sigmoid(gate)
        silu = gate * logistic
        slope = logistic * (1.0 + gate * (1.0 - logistic))
        made[:, columns(j, 0)] = (silu * up).astype(made.dtype)
        made[:, columns(j, 1)] = (act_grad * up * slope).astype(made.dtype)
        made[:, columns(j, 2)] = (act_grad * silu).astype(made.dtype)

    if swaps:
        swap.end()


def run_ffn(call_id, normed, ct, weights, swaps):
    rows, width = normed.shape
    arrays = [ct] if swaps else []
    vmem = pl.BlockSpec(memory_space=pltpu.VMEM)
    params = dict(collective_id=call_id, has_side_effects=True) if swaps else {}
    return pl.pallas_call(
        functools.partial(ffn_kernel, swaps),
        in_specs=[vmem, vmem, pl.BlockSpec(memory_space=pltpu.HBM)],
        out_specs=[vmem] + [pl.BlockSpec(memory_space=pltpu.HBM)] * len(arrays),
        out_shape=[jax.ShapeDtypeStruct((rows, weights.shape[1]), jnp.bfloat16)]
        + swap_shapes(arrays),
        scratch_shapes=[
            pltpu.VMEM((2, 3, width, WIDE), jnp.bfloat16),
            pltpu.SemaphoreType.DMA((2, 3)),
        ]
        + swap_scratch(arrays),
        compiler_params=pltpu.CompilerParams(vmem_limit_bytes=VMEM_GRANT, **params),
    )(normed, ct, weights)


def ffn_back_kernel(
    n_swaps,
    made,
    ct,
    middle,
    gain,
    out_first,
    out_last,
    weights,
    *refs,
):
    arrays, refs = refs[:n_swaps], refs[n_swaps:]
    middle_low, middle_grad, gain_grad, gated_grad, ffn_part, *refs = refs
    swapped, refs = refs[:n_swaps], refs[n_swaps:]
    part, wide_buf, down_buf, wide_sem, down_sem, *sems = refs
    hidden = made.shape[1] // 3
    blocks = part.shape[1] // WIDE
    group = Group(("tp",), None, None)
    line = LineSum(part, *sems[:5])
    spread = LineSpread(middle_low, *sems[5:7])
    if n_swaps:
        swap = Swap(arrays, swapped, *sems[7:])
        greet([(("tp",), group.others), (PLANE, swap.plane.others)])
        swap.begin()
    else:
        greet([(("tp",), group.others)])

    def fetch(j):
        return pltpu.make_async_copy(
            weights.at[j * WIDE : (j + 1) * WIDE, : 2 * hidden],
            wide_buf.at[j % 2],
            wide_sem.at[j % 2],
        )

    def fetch_down(j):
        return pltpu.make_async_copy(
            weights.at[j * WIDE : (j + 1) * WIDE, 2 * hidden :],
            down_buf.at[j % 2],
            down_sem.at[j % 2],
        )

    fetch(0).start()
    firsts = []
    for j in range(blocks):
        if j + 1 < blocks:
            fetch(j + 1).start()
        else:
            fetch_down(0).start()
        fetch(j).wait()
        columns = slice(j * WIDE, (j + 1) * WIDE)
        part[:, columns] = matmul_nt(made[:, hidden:], wide_buf[j % 2]).astype(part.dtype)
        firsts.append(line.begin(j))
    for j in range(blocks):
        if j + 1 < blocks:
            fetch_down(j + 1).start()
        fetch_down(j).wait()
        ffn_part[:, j * WIDE : (j + 1) * WIDE] = matmul_nt(
            made[:, :hidden], down_buf[j % 2]
        ).astype(ffn_part.dtype)
        line.pass_on(j, firsts[j])
    normed_grad = line.total()
    rows = middle[...]
    scale = inverse_rms(rows)
    gain_grad[...] = jnp.sum(normed_grad * rows * scale, 0, keepdims=True)
    grad = group.own(ct)[...].astype(jnp.float32) + norm_back(
        normed_grad, rows, scale, gain[...].astype(jnp.float32)
    )
    middle_grad[...] = grad
    group.own(middle_low)[...] = grad.astype(middle_low.dtype)
    spread.run()
    half = gated_grad.shape[1] // 2
    share = out_first.shape[1]
    for side, shards in enumerate((out_first, out_last)):
        total = None
        for at in range(shards.shape[0] // half):
            one = matmul_nt(
                middle_low[:, at * share : (at + 1) * share],
                shards[at * half : (at + 1) * half, :],
            )
            total = one if total is None else total + one
        gated_grad[:, side * half : (side + 1) * half] = total
    if n_swaps:
        swap.end()


def ffn_back(call_id, made, ct, middle, gain, out_first, out_last, weights, arrays):
    count = group_size(("tp",))
    vmem = pl.BlockSpec(memory_space=pltpu.VMEM)
    hbm = pl.BlockSpec(memory_space=pltpu.HBM)
    rows, width = ct.shape
    hidden = made.shape[1] // 3
    inner = 2 * out_first.shape[0] // group_size(PLANE)
    low, full = jnp.bfloat16, jnp.float32
    part = jax.ShapeDtypeStruct((rows, width), low)
    dma = pltpu.SemaphoreType.DMA
    return pl.pallas_call(
        functools.partial(ffn_back_kernel, len(arrays)),
        in_specs=[vmem] * 6 + [hbm] + [vmem] * len(arrays),
        out_specs=[vmem] * 5 + [hbm] * len(arrays),
        out_shape=[
            part,
            jax.ShapeDtypeStruct((rows // count, width), full),
            jax.ShapeDtypeStruct((1, width), full),
            jax.ShapeDtypeStruct((rows, inner), full),
            part,
        ]
        + swap_shapes(arrays),
        scratch_shapes=[
            pltpu.VMEM(part.shape, low),
            pltpu.VMEM((2, WIDE, 2 * hidden), low),
            pltpu.VMEM((2, WIDE, hidden), low),
            dma((2,)),
            dma((2,)),
        ]
        + line_sum_scratch(part, width // WIDE)
        + line_spread_scratch()
        + swap_scratch(arrays),
        compiler_params=pltpu.CompilerParams(
            collective_id=call_id, has_side_effects=True, vmem_limit_bytes=VMEM_GRANT
        ),
    )(made, ct, middle, gain, out_first, out_last, weights, *arrays)


def send_on(source, target, send_sem, recv_sem, ctx):
    return pltpu.make_async_remote_copy(
        src_ref=source,
        dst_ref=target,
        send_sem=send_sem,
        recv_sem=recv_sem,
        device_id={"ctx": ctx},
        device_id_type=pl.DeviceIdType.MESH,
    )


def forward_pair_kernel(
    n_state,
    tiles,
    groups,
    blocks,
    seqs,
    step_ref,
    input_ref,
    brow_ref,
    crow_ref,
    rate_ref,
    shard,
    *refs,
):
    prior_ref, mixed_ref, gathered, *refs = refs
    carried, ends, starts, prior_buf, step_held, input_held, mixed_held, *refs = refs
    prior_sem, send_sem, recv_sem, gather_send, gather_recv, local_sem = refs
    place = lax.axis_index("ctx")
    gather = PlaneGather(shard, gathered, gather_send, gather_recv)
    greet([(PLANE, gather.others)])
    gather.begin(local_sem)

    def hand_on(seq):
        return send_on(ends.at[seq], starts.at[seq], send_sem.at[seq], recv_sem.at[seq], 1)

    def store(block):
        slot = lax.rem(block, 2)
        rows = groups * SUB
        return pltpu.make_async_copy(
            prior_buf.at[slot],
            prior_ref.at[pl.ds(pl.multiple_of(block * rows, rows), rows)],
            prior_sem.at[slot],
        )

    def one_sequence(seq):
        @pl.when(place == 0)
        def _():
            carried[...] = jnp.zeros_like(carried)

        @pl.when(place == 1)
        def _():
            hand_on(seq).wait_recv()
            carried[...] = starts[seq]

        @pl.loop(0, blocks)
        def _(inner_block):
            block = seq * blocks + inner_block
            slot = lax.rem(block, 2)

            @pl.when(block >= 2)
            def _():
                store(block - 2).wait()

            def one(turn, states):
                group = block * groups + turn
                states = list(states)
                stage_in(step_ref, group, step_held)
                stage_in(input_ref, group, input_held)
                for at in range(SUB):
                    step = token_row(step_held, at, tiles)
                    drive = step * token_row(input_held, at, tiles)
                    mixed = [None] * 2
                    for n in range(n_state):
                        where = (group * SUB + at) * n_state + n
                        prior_buf[slot, turn * SUB + at, n] = states[n]
                        decay = jnp.exp2(step * rate_ref[n])
                        states[n] = decay * states[n] + drive * brow_ref[where]
                        term = states[n] * crow_ref[where]
                        mixed[n % 2] = term if mixed[n % 2] is None else mixed[n % 2] + term
                    mixed_held[pl.ds(at, tiles, stride=SUB), :] = mixed[0] + mixed[1]
                stage_out(mixed_held, mixed_ref, group)
                return tuple(states)

            states = lax.fori_loop(0, groups, one, tuple(carried[n] for n in range(n_state)))
            for n in range(n_state):
                carried[n] = states[n]
            store(block).start()

        @pl.when(place == 0)
        def _():
            ends[seq] = carried[...]
            hand_on(seq).start()

    for seq in range(seqs):
        one_sequence(seq)
        if seq == 0:
            gather.relay()
            gather.hand_over()
    gather.hand_over_last()
    for block in range(max(0, seqs * blocks - 2), seqs * blocks):
        store(block).wait()

    @pl.when(place == 0)
    def _():
        for seq in range(seqs):
            hand_on(seq).wait_send()

    gather.end()


def scan_forward_pair(
    call_id, step, inputs, b_rows, c_rows, rate, seqs, shard
):
    n_state, tiles, _ = rate.shape
    tokens, inner = step.shape
    all_groups = tokens // SUB
    groups = math.gcd(all_groups // seqs, 4)
    blocks = all_groups // seqs // groups
    vmem = pl.BlockSpec(memory_space=pltpu.VMEM)
    smem = pl.BlockSpec(memory_space=pltpu.SMEM)
    hbm = pl.BlockSpec(memory_space=pltpu.HBM)
    full = jnp.float32
    held = pltpu.VMEM((tiles * SUB, LANE), full)
    boundary = pltpu.VMEM((seqs, n_state, tiles, LANE), full)
    dma = pltpu.SemaphoreType.DMA
    return pl.pallas_call(
        functools.partial(
            forward_pair_kernel, n_state, tiles, groups, blocks, seqs
        ),
        in_specs=[vmem, vmem, smem, smem, vmem, hbm],
        out_specs=[hbm, vmem, hbm],
        out_shape=[
            jax.ShapeDtypeStruct((tokens, n_state, tiles, LANE), full),
            jax.ShapeDtypeStruct(step.shape, full),
            gathered_shape(shard),
        ],
        scratch_shapes=[
            pltpu.VMEM((n_state, tiles, LANE), full),
            boundary,
            boundary,
            pltpu.VMEM((2, groups * SUB, n_state, tiles, LANE), full),
            held,
            held,
            held,
            dma((2,)),
            dma((seqs,)),
            dma((seqs,)),
        ]
        + gather_scratch(),
        compiler_params=pltpu.CompilerParams(
            collective_id=call_id, has_side_effects=True, vmem_limit_bytes=VMEM_GRANT
        ),
    )(step, inputs, b_rows, c_rows, rate, shard)


def backward_pair_kernel(
    n_swaps,
    n_state,
    tiles,
    groups,
    blocks,
    seqs,
    step_ref,
    input_ref,
    ograd_ref,
    brow_ref,
    crow_ref,
    rate_ref,
    picks_ref,
    ffn_part,
    middle,
    prior_ref,
    *refs,
):
    arrays, refs = refs[:n_swaps], refs[n_swaps:]
    step_grad_ref, input_grad_ref, rate_grad_ref, part_ref, *refs = refs
    layer_first, layer_last, *refs = refs
    swapped, refs = refs[:n_swaps], refs[n_swaps:]
    carried, ends, starts, prior_buf, step_held, input_held, ograd_held, *refs = refs
    step_grad_held, input_grad_held, ffn_slots, prior_sem, send_sem, recv_sem, *refs = refs
    tp_send, tp_recv, *refs = refs
    place = lax.axis_index("ctx")
    tp = Group(("tp",), tp_send, tp_recv)
    if n_swaps:
        swap = Swap(arrays, swapped, *refs)
        greet([(PLANE, swap.plane.others), (("tp",), tp.others)])
        swap.begin()
    else:
        greet([(("ctx",), [1 - place]), (("tp",), tp.others)])
    ffn_sent = tp.scatter(ffn_part, ffn_slots, 0)

    def hand_on(seq):
        return send_on(ends.at[seq], starts.at[seq], send_sem.at[seq], recv_sem.at[seq], 0)

    def fetch(turn):
        seq = lax.div(turn, blocks)
        block = seq * blocks + blocks - 1 - lax.rem(turn, blocks)
        slot = lax.rem(turn, 2)
        rows = groups * SUB
        return pltpu.make_async_copy(
            prior_ref.at[pl.ds(pl.multiple_of(block * rows, rows), rows)],
            prior_buf.at[slot],
            prior_sem.at[slot],
        )

    fetch(0).start()
    rate_grad_ref[...] = jnp.zeros_like(rate_grad_ref)

    @pl.when(place == 1)
    def _():
        @pl.loop(0, seqs)
        def _(seq):
            def one(turn, grads):
                group = (seq + 1) * blocks * groups - 1 - turn
                grads = list(grads)
                stage_in(step_ref, group, step_held)
                stage_in(ograd_ref, group, ograd_held)
                for at in range(SUB - 1, -1, -1):
                    step = token_row(step_held, at, tiles)
                    ograd = token_row(ograd_held, at, tiles)
                    for n in range(n_state):
                        row = crow_ref[(group * SUB + at) * n_state + n]
                        grads[n] = jnp.exp2(step * rate_ref[n]) * (grads[n] + ograd * row)
                return tuple(grads)

            zero = jnp.zeros((tiles, LANE), jnp.float32)
            grads = lax.fori_loop(0, blocks * groups, one, (zero,) * n_state)
            for n in range(n_state):
                ends[seq, n] = grads[n]
            hand_on(seq).start()

    @pl.loop(0, seqs)
    def _(seq):
        @pl.when(place == 1)
        def _():
            carried[...] = jnp.zeros_like(carried)

        @pl.when(place == 0)
        def _():
            hand_on(seq).wait_recv()
            carried[...] = starts[seq]

        @pl.loop(0, blocks)
        def _(inner_block):
            turn = seq * blocks + inner_block
            slot = lax.rem(turn, 2)
            first_group = (seq * blocks + blocks - 1 - inner_block) * groups

            @pl.when(turn + 1 < seqs * blocks)
            def _():
                fetch(turn + 1).start()

            fetch(turn).wait()

            def one(back, grads):
                inner_group = groups - 1 - back
                group = first_group + inner_group
                grads = list(grads)
                stage_in(step_ref, group, step_held)
                stage_in(input_ref, group, input_held)
                stage_in(ograd_ref, group, ograd_held)
                for at in range(SUB - 1, -1, -1):
                    step = token_row(step_held, at, tiles)
                    value = token_row(input_held, at, tiles)
                    ograd = token_row(ograd_held, at, tiles)
                    drive = step * value
                    along_b = None
                    along_rate = None
                    brow_parts, crow_parts = [], []
                    for n in range(n_state):
                        where = (group * SUB + at) * n_state + n
                        brow, crow = brow_ref[where], crow_ref[where]
                        rate = rate_ref[n]
                        decay = jnp.exp2(step * rate)
                        grad = ograd * crow + grads[n]
                        kept = decay * prior_buf[slot, inner_group * SUB + at, n]
                        state = kept + drive * brow
                        decay_term = grad * kept
                        grads[n] = decay * grad
                        rate_grad_ref[n] += decay_term * step
                        by_rate, by_brow = decay_term * rate, grad * brow
                        along_rate = by_rate if along_rate is None else along_rate + by_rate
                        along_b = by_brow if along_b is None else along_b + by_brow
                        brow_parts.append(grad * drive)
                        crow_parts.append(ograd * state)
                    step_grad_held[pl.ds(at, tiles, stride=SUB), :] = (
                        along_rate * LN2 + along_b * value
                    )
                    input_grad_held[pl.ds(at, tiles, stride=SUB), :] = along_b * step
                    parts = jnp.concatenate(brow_parts + crow_parts, 0).astype(jnp.bfloat16)
                    part_ref[group * SUB + at] = jnp.dot(
                        picks_ref[...], parts, preferred_element_type=jnp.float32
                    )
                stage_out(step_grad_held, step_grad_ref, group)
                stage_out(input_grad_held, input_grad_ref, group)
                return tuple(grads)

            grads = lax.fori_loop(0, groups, one, tuple(carried[n] for n in range(n_state)))
            for n in range(n_state):
                carried[n] = grads[n]

    finish(ffn_sent)
    layer_rows = (middle[...] + tp.total(ffn_part, ffn_slots)).astype(layer_first.dtype)
    half = layer_first.shape[1]
    layer_first[...], layer_last[...] = layer_rows[:, :half], layer_rows[:, half:]

    @pl.when(place == 1)
    def _():
        @pl.loop(0, seqs)
        def _(seq):
            hand_on(seq).wait_send()

    if n_swaps:
        swap.end()


def scan_backward_pair(
    call_id, prior, step, inputs, ograd, b_rows, c_rows, rate, seqs, ffn_part, middle, arrays
):
    n_state, tiles, _ = rate.shape
    tokens, inner = step.shape
    all_groups = tokens // SUB
    groups = math.gcd(all_groups // seqs, 4)
    blocks = all_groups // seqs // groups
    tp_count = group_size(("tp",))
    vmem = pl.BlockSpec(memory_space=pltpu.VMEM)
    smem = pl.BlockSpec(memory_space=pltpu.SMEM)
    hbm = pl.BlockSpec(memory_space=pltpu.HBM)
    full = jnp.float32
    held = pltpu.VMEM((tiles * SUB, LANE), full)
    boundary = pltpu.VMEM((seqs, n_state, tiles, LANE), full)
    dma = pltpu.SemaphoreType.DMA
    layer_half = jax.ShapeDtypeStruct((middle.shape[0], middle.shape[1] // 2), jnp.bfloat16)
    picks = jnp.repeat(jnp.eye(2 * n_state, dtype=jnp.bfloat16), tiles, 1)
    return pl.pallas_call(
        functools.partial(
            backward_pair_kernel, len(arrays), n_state, tiles, groups, blocks, seqs
        ),
        in_specs=[vmem] * 3 + [smem] * 2 + [vmem] * 4 + [hbm] + [vmem] * len(arrays),
        out_specs=[vmem] * 6 + [hbm] * len(arrays),
        out_shape=[
            jax.ShapeDtypeStruct(step.shape, full),
            jax.ShapeDtypeStruct(step.shape, full),
            jax.ShapeDtypeStruct(rate.shape, full),
            jax.ShapeDtypeStruct((tokens, 2 * n_state, LANE), full),
            layer_half,
            layer_half,
        ]
        + swap_shapes(arrays),
        scratch_shapes=[
            pltpu.VMEM((n_state, tiles, LANE), full),
            boundary,
            boundary,
            pltpu.VMEM((2, groups * SUB, n_state, tiles, LANE), full),
        ]
        + [held] * 5
        + [
            slots_for(ffn_part, tp_count),
            dma((2,)),
            dma((seqs,)),
            dma((seqs,)),
            dma((1, tp_count - 1)),
            dma((1, tp_count - 1)),
        ]
        + swap_scratch(arrays),
        compiler_params=pltpu.CompilerParams(
            collective_id=call_id, has_side_effects=True, vmem_limit_bytes=VMEM_GRANT
        ),
    )(step, inputs, ograd, b_rows, c_rows, rate, picks, ffn_part, middle, prior, *arrays)


class PlaneGather:
    def __init__(self, own, gathered, send_sem, recv_sem):
        self.own, self.gathered = own, gathered
        self.send_sem, self.recv_sem = send_sem, recv_sem
        self.dp, self.ctx = lax.axis_index("dp"), lax.axis_index("ctx")
        self.n_dp, self.n_ctx = lax.axis_size("dp"), lax.axis_size("ctx")
        self.hands_on = relayed()
        self.count = self.n_dp * self.n_ctx
        self.me = self.dp * self.n_ctx + self.ctx
        self.others = [lax.rem(self.me + hop, self.count) for hop in range(1, self.count)]
        self.copies = {}
        if self.hands_on:
            core = lax.rem(self.dp, 2)
            over_core = self.dp + 1 - 2 * core
            over_y = lax.rem(self.dp + 2, 4)
            over_x = 1 - self.ctx
            self.core = {"dp": over_core, "ctx": self.ctx}
            self.at_x = {"dp": self.dp, "ctx": over_x}
            self.at_y = {"dp": over_y, "ctx": self.ctx}
            self.from_x = self.dp * 2 + over_x
            self.from_y = over_y * 2 + self.ctx
            self.across = over_y * 2 + over_x

    def part(self, owner, half):
        rows = self.gathered.shape[0] // self.count
        start, size = owner * rows, rows
        if half is not None:
            size = rows // 2
            start = start + half * size
        return self.gathered.at[pl.ds(pl.multiple_of(start, size), size), :]

    def send(self, which, owner, half, where):
        target = self.part(owner, half)
        source = target
        if owner is self.me:
            rows = self.own.shape[0]
            source = self.own
            if half is not None:
                source = self.own.at[pl.ds(half * (rows // 2), rows // 2), :]
        self.copies[which] = sent(
            source, target, self.send_sem.at[which], self.recv_sem.at[which], where
        )

    def arrived(self, *which):
        for one in which:
            self.copies[one].wait_recv()

    def begin(self, local_sem):
        self.local = pltpu.make_async_copy(self.own, self.part(self.me, None), local_sem)
        self.local.start()
        if not self.hands_on:
            for hop, other in enumerate(self.others):
                self.send(hop, self.me, None, device_at(PLANE, other))
            return
        self.send(0, self.me, 1, self.at_x)
        self.send(1, self.me, 0, self.at_y)
        self.send(2, self.me, None, self.core)
        self.send(3, self.me, 0, self.at_x)
        self.send(4, self.me, 1, self.at_y)

    def relay(self):
        if not self.hands_on:
            return
        self.arrived(0, 1)
        self.send(5, self.from_x, 1, self.at_y)
        self.send(6, self.from_y, 0, self.at_x)
        self.send(7, self.from_x, 1, self.core)
        self.send(8, self.from_y, 0, self.core)

    def hand_over(self):
        if not self.hands_on:
            return
        self.arrived(3, 4)
        self.send(9, self.from_x, 0, self.core)
        self.send(10, self.from_y, 1, self.core)

    def hand_over_last(self):
        if not self.hands_on:
            return
        self.arrived(5, 6)
        self.send(11, self.across, 1, self.core)
        self.send(12, self.across, 0, self.core)

    def end(self):
        if self.hands_on:
            self.arrived(2, 7, 8, 9, 10, 11, 12)
        else:
            self.arrived(*range(self.count - 1))
        for copy in self.copies.values():
            copy.wait_send()
        self.local.wait()


def relayed():
    return lax.axis_size("dp") == 4 and lax.axis_size("ctx") == 2


def gather_sems():
    count = 13 if relayed() else group_size(PLANE) - 1
    return pltpu.SemaphoreType.DMA((count,))


WIDE = 512


def products(source, first, last, dot, target, block_buf, block_sem, out_buf, out_sem):
    def fetch(j, slot):
        columns = pl.ds(pl.multiple_of(j * WIDE, WIDE), WIDE)
        return pltpu.make_async_copy(
            source.at[:, columns], block_buf.at[slot], block_sem.at[slot]
        )

    def store(j, slot):
        return pltpu.make_async_copy(out_buf.at[slot], target(j), out_sem.at[slot])

    fetch(first, first % 2).start()

    @pl.loop(first, last)
    def _(j):
        slot = lax.rem(j, 2)

        @pl.when(j + 1 < last)
        def _():
            fetch(j + 1, 1 - slot).start()

        fetch(j, slot).wait()

        @pl.when(j >= first + 2)
        def _():
            store(j - 2, slot).wait()

        out_buf[slot] = dot(block_buf[slot])
        store(j, slot).start()

    for j in range(max(first, last - 2), last):
        store(j, j % 2).wait()


class PlaneSum:
    def __init__(self, array, total, *refs):
        self.array, self.result = array, total
        self.hands_on = relayed()
        if not self.hands_on:
            self.slots, send_sem, recv_sem = refs
            self.group = Group(PLANE, send_sem, recv_sem)
            return
        self.core_slot, self.pair, self.chip_slots, *self.sems = refs
        dp, ctx = lax.axis_index("dp"), lax.axis_index("ctx")
        self.half = lax.rem(dp, 2)
        self.other_core = {"dp": dp + 1 - 2 * self.half, "ctx": ctx}
        over_y, over_x = lax.rem(dp + 2, 4), 1 - ctx
        self.quarter = lax.div(dp, 2) * 2 + ctx
        self.chips = [
            ({"dp": a, "ctx": b}, lax.div(a, 2) * 2 + b)
            for a, b in ((dp, over_x), (over_y, ctx), (over_y, over_x))
        ]

    def to_core(self, source, target, which):
        core_send, core_recv = self.sems[:2]
        return sent(
            source, target, core_send.at[which], core_recv.at[which], self.other_core
        )

    def to_chip(self, source, target, which, at):
        chip_send, chip_recv = self.sems[2:]
        return sent(
            source,
            target,
            chip_send.at[which, at],
            chip_recv.at[which, at],
            self.chips[at][0],
        )

    def begin(self):
        if not self.hands_on:
            self.copies = self.group.scatter(self.array, self.slots, 0)
            return
        self.copies = [self.to_core(rows_of(self.array, 1 - self.half, 2), self.core_slot, 0)]

    def add_pair(self):
        if not self.hands_on:
            return
        finish(self.copies)
        self.pair[...] = (
            rows_of(self.array, self.half, 2)[...].astype(jnp.float32)
            + self.core_slot[...].astype(jnp.float32)
        ).astype(self.pair.dtype)
        self.copies = [
            self.to_chip(rows_of(self.pair, index, 4), self.chip_slots.at[at], 0, at)
            for at, (_, index) in enumerate(self.chips)
        ]

    def add_all(self):
        finish(self.copies)
        if not self.hands_on:
            self.group.own(self.result)[...] = self.group.total(self.array, self.slots).astype(
                self.result.dtype
            )
            self.copies = self.group.spread(self.result, 1)
            return
        total = rows_of(self.pair, self.quarter, 4)[...].astype(jnp.float32)
        for at in range(3):
            total = total + self.chip_slots[at].astype(jnp.float32)
        mine = rows_of(self.result, self.half * 4 + self.quarter, 8)
        mine[...] = total.astype(self.result.dtype)
        self.copies = [self.to_chip(mine, mine, 1, at) for at in range(3)]

    def hand_over(self):
        if not self.hands_on:
            return
        finish(self.copies)
        half = rows_of(self.result, self.half, 2)
        self.copies = [self.to_core(half, half, 1)]

    def end(self):
        finish(self.copies)


def plane_sum_scratch(array):
    dma = pltpu.SemaphoreType.DMA
    count = group_size(PLANE)
    if not relayed():
        return [slots_for(array, count), dma((2, count - 1)), dma((2, count - 1))]
    rows, width = array.shape
    return [
        pltpu.VMEM((rows // 2, width), array.dtype),
        pltpu.VMEM((rows // 2, width), array.dtype),
        pltpu.VMEM((3, rows // 8, width), array.dtype),
        dma((2,)),
        dma((2,)),
        dma((2, 3)),
        dma((2, 3)),
    ]


SMALL_ROWS = 32
GAIN_ROWS = 16


def tail_kernel(
    swaps,
    conv_grad,
    gate_grad,
    convkern,
    convbias,
    stepbias,
    decaylog,
    skipgain,
    ffngain,
    layer_first,
    layer_rows,
    middle_low,
    step_low,
    pre_low,
    select_low,
    scan_in,
    tokens,
    middle_grad,
    gain_row,
    in_conv,
    in_gate,
    one_cols,
    two_cols,
    ct_cols,
    middle_cols,
    ffn_all,
    gated_all,
    tokens_grad,
    layer_out,
    vectors_sum,
    step_sum,
    select_sum,
    gains,
    mix_all,
    grad_inproj,
    grad_outproj,
    grad_gateup,
    grad_downproj,
    mix_own,
    normed_part,
    small,
    small_sum,
    gain_slots,
    gain_own,
    vectors_own,
    cols,
    in_buf,
    block_buf,
    wide_buf,
    tall_buf,
    cols_sem,
    in_sem,
    block_sem,
    wide_sem,
    tall_sem,
    tp_send,
    tp_recv,
    gather_send,
    gather_recv,
    local_sem,
    *sems,
):
    inner = conv_grad.shape[1]
    hidden = ffn_all.shape[1] // 3
    width = tokens.shape[1]
    rank = step_low.shape[1]
    tp = Group(("tp",), tp_send, tp_recv)
    line = LineSum(normed_part, *sems[:5])
    tokens_spread = LineSpread(tokens_grad, *sems[5:7])
    layer_last = layer_out.at[:, width // 2 :]
    layer_spread = LineSpread(layer_last, *sems[7:9])
    count = 7 if relayed() else 3
    small_total = PlaneSum(small, small_sum, *sems[9 : 9 + count])
    swap_sems = sems[9 + count :]
    gather = PlaneGather(mix_own, mix_all, gather_send, gather_recv)
    sources = (one_cols, two_cols, ct_cols) if swaps else (one_cols, two_cols, ct_cols, middle_cols)
    loads = [
        pltpu.make_async_copy(source, cols.at[at], cols_sem.at[at])
        for at, source in enumerate(sources)
    ]
    if swaps:
        swap = Swap([middle_low], [cols.at[3]], *swap_sems)

    def fetch(j):
        slot = j % 2
        rows = slice(j * WIDE, (j + 1) * WIDE)
        return [
            pltpu.make_async_copy(source.at[rows, :], in_buf.at[slot, at], in_sem.at[slot, at])
            for at, source in enumerate((in_conv, in_gate))
        ]

    for copy in fetch(0) + loads:
        copy.start()
    mix_own[:, :inner] = conv_grad[...]
    mix_own[:, inner:] = gate_grad[...]
    greet([(("tp",), tp.others), (PLANE, gather.others)])
    gather.begin(local_sem)

    small[...] = jnp.zeros_like(small)
    vectors_own[...] = jnp.zeros_like(vectors_own)
    at = 0
    for vector in (convkern, convbias, stepbias, decaylog, skipgain):
        vectors_own[at : at + vector.shape[0], :] = vector[...]
        at += vector.shape[0]
    at = SMALL_ROWS - GAIN_ROWS + 10
    for row in range(width // inner):
        vectors_own[at + row : at + row + 1, :] = ffngain[:, row * inner : (row + 1) * inner]
    hidden_in = tokens[...].astype(jnp.float32)
    unit_rows = hidden_in * inverse_rms(hidden_in)
    blocks = width // WIDE
    firsts = []
    for j in range(blocks):
        if j + 1 < blocks:
            for copy in fetch(j + 1):
                copy.start()
        finish(fetch(j))
        columns = slice(j * WIDE, (j + 1) * WIDE)
        block = matmul_nt(conv_grad[...], in_buf[j % 2, 0]) + matmul_nt(
            gate_grad[...], in_buf[j % 2, 1]
        )
        normed_part[:, columns] = block.astype(normed_part.dtype)
        firsts.append(line.begin(j))
        gain_grad = jnp.sum(block * unit_rows[:, columns], 0, keepdims=True)
        if j:
            line.pass_on(j - 1, firsts[j - 1])
        row, at = divmod(j * WIDE, inner)
        row += SMALL_ROWS - GAIN_ROWS + 8
        vectors_own[row : row + 1, at : at + WIDE] = gain_grad
    layer_out[:, : width // 2] = layer_first[...]
    rows_of(layer_last, tp.me, tp.count)[...] = layer_rows[...]
    layer_spread.begin()
    small[:SMALL_ROWS, :] = vectors_own[...].astype(small.dtype)
    small[SMALL_ROWS : SMALL_ROWS + rank, :] = matmul_tn(step_low[...], pre_low[...]).astype(
        small.dtype
    )
    selected = select_sum.shape[0]
    small[SMALL_ROWS + rank : SMALL_ROWS + rank + selected, :] = matmul_tn(
        select_low[...], scan_in[...]
    )[:selected].astype(small.dtype)
    small_total.begin()
    line.pass_on(blocks - 1, firsts[-1])

    def flat(at):
        return lambda block: matmul_tn(cols[at], block)

    def tall(at):
        return lambda block: matmul_tn(block, cols[at])

    def side_by_side(ref, first):
        per = ref.shape[2] // WIDE

        def target(j):
            at = j - first
            columns = pl.ds(pl.multiple_of(lax.rem(at, per) * WIDE, WIDE), WIDE)
            return ref.at[lax.div(at, per), :, columns]

        return target

    def one_above_other(ref):
        return lambda j: ref.at[pl.ds(pl.multiple_of(j * WIDE, WIDE), WIDE), :]

    wide = (block_buf, block_sem, wide_buf, wide_sem)
    high = (block_buf, block_sem, tall_buf, tall_sem)
    down_end = hidden // WIDE
    gu_end = 3 * hidden // WIDE
    finish(loads)
    gu_middle = (down_end + gu_end) // 2
    to_gateup = side_by_side(grad_gateup, down_end)
    products(ffn_all, 0, down_end, tall(2), one_above_other(grad_downproj), *high)
    gather.relay()
    small_total.add_pair()
    products(ffn_all, down_end, gu_middle, flat(1), to_gateup, *wide)
    hidden_in = tp.own(tokens)[...].astype(jnp.float32)
    tp.own(tokens_grad)[...] = (
        middle_grad[...]
        + norm_back(
            line.total(),
            hidden_in,
            inverse_rms(hidden_in),
            gain_row[...].astype(jnp.float32),
        )
    ).astype(tokens_grad.dtype)
    tokens_spread.begin()
    layer_spread.pass_on()
    gather.hand_over()
    small_total.add_all()
    if swaps:
        swap.begin()
    products(ffn_all, gu_middle, gu_end, flat(1), to_gateup, *wide)
    tokens_spread.pass_on()
    gather.hand_over_last()
    small_total.hand_over()
    gather.end()
    products(mix_all, 0, 2 * inner // WIDE, flat(0), side_by_side(grad_inproj, 0), *wide)
    small_total.end()
    gain_own[...] = small_sum[SMALL_ROWS - GAIN_ROWS : SMALL_ROWS, :].astype(jnp.float32)
    gain_sent = [tp.one(gain_own, gain_slots.at[hop], 0, hop) for hop in range(tp.count - 1)]
    vectors_sum[...] = small_sum[:SMALL_ROWS, :].astype(jnp.float32)
    step_sum[...] = small_sum[SMALL_ROWS : SMALL_ROWS + rank, :].astype(jnp.float32)
    select_sum[...] = small_sum[SMALL_ROWS + rank : SMALL_ROWS + rank + selected, :].astype(
        jnp.float32
    )
    if swaps:
        swap.end()
    products(gated_all, 0, inner // WIDE, tall(3), one_above_other(grad_outproj), *high)
    finish(gain_sent)
    total = gain_own[...]
    for hop in range(tp.count - 1):
        total = total + gain_slots[hop]
    gains[...] = total
    tokens_spread.end()
    layer_spread.end()


def run_tail(
    call_id,
    selected,
    swaps,
    conv_grad,
    gate_grad,
    vectors,
    layer_first,
    layer_rows,
    middle_low,
    step_low,
    pre_low,
    select_low,
    scan_in,
    tokens,
    middle_grad,
    gain_row,
    in_conv,
    in_gate,
    one_cols,
    two_cols,
    ct_cols,
    middle_cols,
    ffn_all,
    gated_all,
):
    rows, inner = conv_grad.shape
    rank = step_low.shape[1]
    hidden = ffn_all.shape[1] // 3
    width = tokens.shape[1]
    share = one_cols.shape[1]
    all_rows = ffn_all.shape[0]
    tp_count, plane_count = group_size(("tp",)), group_size(PLANE)
    low, full = jnp.bfloat16, jnp.float32
    vmem = pl.BlockSpec(memory_space=pltpu.VMEM)
    hbm = pl.BlockSpec(memory_space=pltpu.HBM)
    dma = pltpu.SemaphoreType.DMA
    small_rows = SMALL_ROWS + rank + selected
    small = jax.ShapeDtypeStruct((small_rows + -small_rows % (16 * plane_count), inner), low)
    part = jax.ShapeDtypeStruct((rows, width), low)
    return pl.pallas_call(
        functools.partial(tail_kernel, swaps),
        in_specs=[vmem] * 18 + [hbm] * 8,
        out_specs=[vmem] * 6 + [hbm] * 5,
        out_shape=[
            jax.ShapeDtypeStruct(tokens.shape, low),
            jax.ShapeDtypeStruct(tokens.shape, low),
            jax.ShapeDtypeStruct((SMALL_ROWS, inner), full),
            jax.ShapeDtypeStruct((rank, inner), full),
            jax.ShapeDtypeStruct((selected, inner), full),
            jax.ShapeDtypeStruct((GAIN_ROWS, inner), full),
            jax.ShapeDtypeStruct((all_rows, 2 * inner), low),
            jax.ShapeDtypeStruct((2, share, inner), full),
            jax.ShapeDtypeStruct((inner, share), full),
            jax.ShapeDtypeStruct((2, share, hidden), full),
            jax.ShapeDtypeStruct((hidden, share), full),
        ],
        scratch_shapes=[
            pltpu.VMEM((rows, 2 * inner), low),
            pltpu.VMEM(part.shape, low),
            pltpu.VMEM(small.shape, low),
            pltpu.VMEM(small.shape, low),
            pltpu.VMEM((tp_count - 1, GAIN_ROWS, inner), full),
            pltpu.VMEM((GAIN_ROWS, inner), full),
            pltpu.VMEM((SMALL_ROWS, inner), full),
            pltpu.VMEM((4, all_rows, share), low),
            pltpu.VMEM((2, 2, WIDE, inner), low),
            pltpu.VMEM((2, all_rows, WIDE), low),
            pltpu.VMEM((2, share, WIDE), full),
            pltpu.VMEM((2, WIDE, share), full),
            dma((4,)),
            dma((2, 2)),
            dma((2,)),
            dma((2,)),
            dma((2,)),
            dma((1, tp_count - 1)),
            dma((1, tp_count - 1)),
        ]
        + gather_scratch()
        + line_sum_scratch(part, width // WIDE)
        + line_spread_scratch() * 2
        + plane_sum_scratch(small)
        + (swap_scratch([tokens]) if swaps else []),
        compiler_params=pltpu.CompilerParams(
            collective_id=call_id, has_side_effects=True, vmem_limit_bytes=VMEM_GRANT
        ),
    )(
        conv_grad,
        gate_grad,
        *vectors,
        layer_first,
        layer_rows,
        middle_low,
        step_low,
        pre_low,
        select_low,
        scan_in,
        tokens,
        middle_grad,
        gain_row,
        in_conv,
        in_gate,
        one_cols,
        two_cols,
        ct_cols,
        middle_cols,
        ffn_all,
        gated_all,
    )


BORDER = 16


def head_kernel(
    tokens,
    gain,
    in_conv,
    in_gate,
    conv_in,
    gate_mix,
    border,
    conv_all,
    gate_all,
    normed,
    block_buf,
    block_sem,
    border_send,
    border_recv,
    *sems,
):
    place, places = lax.axis_index("ctx"), lax.axis_size("ctx")
    seqs = border.shape[0] // BORDER
    span = conv_in.shape[0] // seqs

    def to_next(seq):
        return send_on(
            conv_in.at[pl.ds((seq + 1) * span - BORDER, BORDER), :],
            border.at[pl.ds(seq * BORDER, BORDER), :],
            border_send.at[seq],
            border_recv.at[seq],
            place + 1,
        )

    conv = PlaneGather(in_conv, conv_all, *sems[:2])
    gate = PlaneGather(in_gate, gate_all, *sems[3:5])
    greet([(PLANE, conv.others)])
    conv.begin(sems[2])
    gate.begin(sems[5])
    hidden_in = tokens[...].astype(jnp.float32)
    normed[...] = (hidden_in * inverse_rms(hidden_in) * gain[...].astype(jnp.float32)).astype(
        normed.dtype
    )
    conv.relay()
    conv.hand_over()
    gate.relay()
    conv.hand_over_last()
    gate.hand_over()
    conv.end()
    product_in_blocks(normed, conv_all, conv_in, block_buf, block_sem)

    @pl.when(place == 0)
    def _():
        border[...] = jnp.zeros_like(border)

    @pl.when(place < places - 1)
    def _():
        for seq in range(seqs):
            to_next(seq).start()

    gate.hand_over_last()
    gate.end()
    product_in_blocks(normed, gate_all, gate_mix, block_buf, block_sem)

    @pl.when(place < places - 1)
    def _():
        for seq in range(seqs):
            to_next(seq).wait_send()

    @pl.when(place > 0)
    def _():
        for seq in range(seqs):
            to_next(seq).wait_recv()


def run_head(call_id, tokens, gain, inproj, seqs):
    rows, width = tokens.shape
    inner = inproj.shape[2]
    low = jnp.bfloat16
    vmem = pl.BlockSpec(memory_space=pltpu.VMEM)
    hbm = pl.BlockSpec(memory_space=pltpu.HBM)
    return pl.pallas_call(
        head_kernel,
        in_specs=[vmem] * 2 + [hbm] * 2,
        out_specs=[vmem] * 3 + [hbm] * 2,
        out_shape=[
            jax.ShapeDtypeStruct((rows, inner), low),
            jax.ShapeDtypeStruct((rows, inner), jnp.float32),
            jax.ShapeDtypeStruct((seqs * BORDER, inner), low),
            jax.ShapeDtypeStruct((width, inner), low),
            jax.ShapeDtypeStruct((width, inner), low),
        ],
        scratch_shapes=[
            pltpu.VMEM((rows, width), low),
            pltpu.VMEM((2, width, WIDE), low),
            pltpu.SemaphoreType.DMA((2,)),
            pltpu.SemaphoreType.DMA((seqs,)),
            pltpu.SemaphoreType.DMA((seqs,)),
        ]
        + gather_scratch() * 2,
        compiler_params=pltpu.CompilerParams(
            collective_id=call_id, has_side_effects=True, vmem_limit_bytes=VMEM_GRANT
        ),
    )(tokens, gain, inproj[0], inproj[1])


def per_device(
    tokens,
    mixgain,
    inproj,
    convkern,
    convbias,
    selproj,
    stepproj,
    stepbias,
    decaylog,
    skipgain,
    outproj,
    ffngain,
    gateup,
    downproj,
    cotangent,
):
    seqs, span, width = tokens.shape
    rows = seqs * span
    taps, inner = convkern.shape
    rank = stepproj.shape[0]
    n_state = decaylog.shape[1]
    tiles = inner // LANE
    gain_mix = mixgain.astype(jnp.float32)
    kernel = convkern.astype(jnp.float32)
    kernel_bias = convbias.astype(jnp.float32)
    step_bias = stepbias.astype(jnp.float32)
    skip_weight = skipgain.astype(jnp.float32)
    decay_rate = -jnp.exp(jnp.transpose(decaylog.astype(jnp.float32)))
    rate = (decay_rate * LOG2E).reshape(n_state, tiles, LANE)

    gain_mix_row, gain_ffn_row = mixgain.reshape(1, width), ffngain.reshape(1, width)
    low = jnp.bfloat16

    tokens_rows = tokens.reshape(rows, width)
    ct_low = cotangent.reshape(rows, width)
    swap_now = swaps_in_kernels(width)
    ffn_pack = gathered_rows(
        jnp.concatenate([gateup[0], gateup[1], jnp.transpose(downproj)], 1)
    )
    conv_in, gate_mix, border, in_conv, in_gate = run_head(
        5, tokens_rows, gain_mix_row, inproj, seqs
    )
    hidden_in = tokens_rows.astype(jnp.float32)
    scale_one = inverse_rms(hidden_in)
    normed_one = (hidden_in * scale_one * gain_mix).astype(low)

    conv_seqs = conv_in.reshape(seqs, span, inner)
    rim_rows = border.reshape(seqs, BORDER, inner)[:, BORDER - (taps - 1) :]
    padded_in = jnp.concatenate([rim_rows, conv_seqs], 1).astype(jnp.float32)
    conv_out = kernel_bias[None, None]
    for offset in range(taps):
        conv_out = conv_out + kernel[offset][None, None] * padded_in[:, offset : offset + span]
    conv_out = conv_out.reshape(rows, inner)
    scan_in = jax.nn.silu(conv_out).astype(low)
    scan_float = scan_in.astype(jnp.float32)
    columns = selproj.shape[1]
    select_width = -(-columns // LANE) * LANE
    select_weights = jnp.pad(selproj, ((0, 0), (0, select_width - columns)))
    select_cols, out_first = run_select(0, matmul(scan_in, select_weights), outproj[: inner // 2])

    def columns_of(swapped, array):
        if not swapped:
            return swapped_columns(array)
        return swapped[0].reshape(-1, swapped[0].shape[-1])

    step_low = select_cols[:, :rank].astype(low)
    b_rows = select_cols[:, rank : rank + n_state].reshape(-1)
    c_rows = select_cols[:, rank + n_state : columns].reshape(-1)
    step_pre = matmul(step_low, stepproj) + step_bias[None]
    step_size = jax.nn.softplus(step_pre)
    in_pairs = lax.axis_size("ctx") == 2
    if in_pairs:
        prior, scan_out, out_last = scan_forward_pair(
            6,
            step_size,
            scan_float,
            b_rows,
            c_rows,
            rate,
            seqs,
            outproj[inner // 2 :],
        )
    else:
        span_decay = jnp.exp(
            decay_rate[None] * jnp.sum(step_size.reshape(seqs, span, inner), 1)[:, None]
        ).reshape(seqs, n_state, tiles, LANE)
        ends = scan_ends(step_size, scan_float, b_rows, rate, seqs, False)
        start = from_earlier(ends, span_decay, 1)
        prior, scan_out = scan_forward(start, step_size, scan_float, b_rows, c_rows, rate, seqs)
        out_last = gathered_rows(outproj[inner // 2 :])
    mixer_core = scan_out + skip_weight[None] * scan_float
    gate_sig = jax.nn.silu(gate_mix)
    gated = (mixer_core * gate_sig).astype(low)
    normed_two, middle, gated_all, *swapped = mixer_out(
        1,
        gated,
        out_first,
        out_last,
        tokens_rows,
        gain_ffn_row,
        [normed_one] if swap_now else [],
    )
    normed_one_cols = columns_of(swapped, normed_one)
    made, *swapped = run_ffn(8, normed_two, ct_low, ffn_pack, swap_now)
    ct_cols = columns_of(swapped, ct_low)
    ffn_all = gathered_rows(made)
    middle_low, middle_grad, ffngain_part, gated_grad, ffn_part, *swapped = ffn_back(
        2,
        made,
        ct_low,
        middle,
        gain_ffn_row,
        out_first,
        out_last,
        ffn_pack,
        [normed_two] if swap_now else [],
    )
    normed_two_cols = columns_of(swapped, normed_two)
    core_grad = gated_grad * gate_sig
    gate_mix_grad = (gated_grad * mixer_core * silu_slope(gate_mix)).astype(low)
    grad_skipgain = jnp.sum(core_grad * scan_float, 0)
    if in_pairs:
        step_grad, input_grad, rate_grad, parts, *layer_rows = scan_backward_pair(
            7,
            prior,
            step_size,
            scan_float,
            core_grad,
            b_rows,
            c_rows,
            rate,
            seqs,
            ffn_part,
            middle,
            [],
        )
    else:
        back_ends = scan_ends(step_size, core_grad, c_rows, rate, seqs, True)
        end_grad = from_earlier(back_ends, span_decay, -1)
        step_grad, input_grad, rate_grad, parts = scan_backward(
            end_grad, prior, step_size, scan_float, core_grad, b_rows, c_rows, rate, seqs
        )
        ffn_sum = lax.psum_scatter(ffn_part, "tp", scatter_dimension=0, tiled=True)
        layer_rows = jnp.split((middle + ffn_sum.astype(jnp.float32)).astype(low), 2, 1)
    grad_decaylog = rate_grad.reshape(n_state, inner) * decay_rate
    pre_grad = step_grad * jax.nn.sigmoid(step_pre)
    grad_stepbias = jnp.sum(pre_grad, 0)
    pre_low = pre_grad.astype(low)
    select_part = jnp.concatenate(
        [
            matmul_nt(pre_low, stepproj),
            jnp.sum(parts, -1),
            jnp.zeros((rows, select_width - columns), jnp.float32),
        ],
        1,
    ).astype(low)
    select_low, layer_first = sum_over_tp(3, select_part, layer_rows[0])
    scan_in_grad = (
        core_grad * skip_weight[None]
        + input_grad
        + matmul_nt(select_low, select_weights)
    )
    conv_grad = scan_in_grad * silu_slope(conv_out)
    grad_convbias = jnp.sum(conv_grad, 0)
    conv_grad_seqs = conv_grad.reshape(seqs, span, inner)
    padded_grad = jnp.zeros(padded_in.shape, jnp.float32)
    kernel_rows = []
    for offset in range(taps):
        kernel_rows.append(jnp.sum(conv_grad_seqs * padded_in[:, offset : offset + span], (0, 1)))
        padded_grad = padded_grad + jnp.pad(
            kernel[offset][None, None] * conv_grad_seqs,
            ((0, 0), (offset, taps - 1 - offset), (0, 0)),
        )
    grad_convkern = jnp.stack(kernel_rows)
    returned = passed_along(padded_grad[:, : taps - 1], "ctx", -1)
    conv_in_grad = (
        (padded_grad[:, taps - 1 :] + jnp.pad(returned, ((0, 0), (span - taps + 1, 0), (0, 0))))
        .astype(low)
        .reshape(rows, inner)
    )
    vectors = [
        grad_convkern,
        grad_convbias[None],
        grad_stepbias[None],
        grad_decaylog,
        grad_skipgain[None],
        ffngain_part,
    ]
    (
        tokens_grad,
        layer_out,
        vectors,
        grad_stepproj,
        grad_selproj,
        gains,
        _,
        grad_inproj,
        grad_outproj,
        grad_gateup,
        grad_downproj,
    ) = run_tail(
        4,
        columns,
        swap_now,
        conv_in_grad,
        gate_mix_grad,
        vectors,
        layer_first,
        layer_rows[1],
        middle_low,
        step_low,
        pre_low,
        select_low,
        scan_in,
        tokens_rows,
        middle_grad,
        gain_mix_row,
        in_conv,
        in_gate,
        normed_one_cols,
        normed_two_cols,
        ct_cols,
        normed_two_cols if swap_now else swapped_columns(middle_low),
        ffn_all,
        gated_all,
    )
    at = taps + 2
    return (
        layer_out.reshape(tokens.shape),
        tokens_grad.reshape(tokens.shape),
        gains[8:10].reshape(width),
        grad_inproj,
        vectors[:taps],
        vectors[taps],
        jnp.transpose(grad_selproj),
        grad_stepproj,
        vectors[taps + 1],
        jnp.transpose(vectors[at : at + n_state]),
        vectors[at + n_state],
        grad_outproj,
        gains[10:12].reshape(width),
        grad_gateup,
        grad_downproj,
    )


def solution(mesh):
    in_specs = (
        P("dp", "ctx", None),
        P(),
        P(None, ("dp", "ctx"), "tp"),
        P(None, "tp"),
        P("tp"),
        P("tp", None),
        P(None, "tp"),
        P("tp"),
        P("tp", None),
        P("tp"),
        P("tp", ("dp", "ctx")),
        P(),
        P(None, ("dp", "ctx"), "tp"),
        P("tp", ("dp", "ctx")),
        P("dp", "ctx", None),
    )
    out_specs = (
        P("dp", "ctx", None),
        P("dp", "ctx", None),
        P(),
        P(None, ("dp", "ctx"), "tp"),
        P(None, "tp"),
        P("tp"),
        P("tp", None),
        P(None, "tp"),
        P("tp"),
        P("tp", None),
        P("tp"),
        P("tp", ("dp", "ctx")),
        P(),
        P(None, ("dp", "ctx"), "tp"),
        P("tp", ("dp", "ctx")),
    )
    return jax.shard_map(
        per_device, mesh=mesh, in_specs=in_specs, out_specs=out_specs, check_vma=False
    )
```

```python
import functools
import math

import jax
import jax.numpy as jnp
from jax import lax
from jax.experimental import pallas as pl
from jax.experimental.pallas import tpu as pltpu
from jax.sharding import PartitionSpec as P

EPSILON = 1e-05
LOG2E = math.log2(math.e)
LN2 = math.log(2.0)
SUB = 8
LANE = 128
VMEM_GRANT = 60 * 2**20
PLANE = ("dp", "ctx")


def passed_along(value, axis, steps):
    count = lax.axis_size(axis)
    first, last = (max(0, -steps), min(count, count - steps))
    return lax.ppermute(value, axis, [(source, source + steps) for source in range(first, last)])


def matmul(left, right):
    return jnp.dot(left, right, preferred_element_type=jnp.float32)


def matmul_nt(left, right):
    return lax.dot_general(
        left, right, (((1,), (1,)), ((), ())), preferred_element_type=jnp.float32
    )


def matmul_tn(left, right):
    return lax.dot_general(
        left, right, (((0,), (0,)), ((), ())), preferred_element_type=jnp.float32
    )


def inverse_rms(values):
    return lax.rsqrt(jnp.mean(values * values, -1, keepdims=True) + EPSILON)


def silu_slope(values):
    logistic = jax.nn.sigmoid(values)
    return logistic * (1.0 + values * (1.0 - logistic))


def norm_back(grad_norm, values, scale, gain):
    scaled_grad = grad_norm * gain
    unit_rows = values * scale
    return scale * (scaled_grad - unit_rows * jnp.mean(scaled_grad * unit_rows, -1, keepdims=True))


def stage_in(ref, group, held):
    for tile in range(held.shape[0] // SUB):
        held[pl.ds(tile * SUB, SUB), :] = ref[
            pl.ds(pl.multiple_of(group * SUB, SUB), SUB), pl.ds(tile * LANE, LANE)
        ]


def stage_out(held, ref, group):
    for tile in range(held.shape[0] // SUB):
        ref[pl.ds(pl.multiple_of(group * SUB, SUB), SUB), pl.ds(tile * LANE, LANE)] = held[
            pl.ds(tile * SUB, SUB), :
        ]


def token_row(held, at, tiles):
    return held[pl.ds(at, tiles, stride=SUB), :]


def ends_kernel(
    n_state,
    tiles,
    groups,
    reverse,
    step_ref,
    drive_ref,
    rows_ref,
    rate_ref,
    end_ref,
    step_held,
    drive_held,
):
    base = pl.program_id(0) * groups * SUB * n_state
    rates = [rate_ref[n] for n in range(n_state)]

    def one(turn, states):
        group = groups - 1 - turn if reverse else turn
        order = range(SUB - 1, -1, -1) if reverse else range(SUB)
        states = list(states)
        stage_in(step_ref, group, step_held)
        stage_in(drive_ref, group, drive_held)
        for at in order:
            step = token_row(step_held, at, tiles)
            drive = token_row(drive_held, at, tiles)
            if not reverse:
                drive = drive * step
            for n in range(n_state):
                row = rows_ref[base + (group * SUB + at) * n_state + n]
                decay = jnp.exp2(step * rates[n])
                if reverse:
                    states[n] = decay * (states[n] + drive * row)
                else:
                    states[n] = decay * states[n] + drive * row
        return tuple(states)

    zero = jnp.zeros((tiles, LANE), jnp.float32)
    states = lax.fori_loop(0, groups, one, (zero,) * n_state)
    for n in range(n_state):
        end_ref[0, n] = states[n]


def scan_ends(step, drive, rows, rate, seqs, reverse):
    n_state, tiles, _ = rate.shape
    groups = step.shape[0] // seqs // SUB
    rows_spec = pl.BlockSpec((groups * SUB, tiles * LANE), lambda s: (s, 0))
    held = pltpu.VMEM((tiles * SUB, LANE), jnp.float32)
    return pl.pallas_call(
        functools.partial(ends_kernel, n_state, tiles, groups, reverse),
        grid=(seqs,),
        in_specs=[
            rows_spec,
            rows_spec,
            pl.BlockSpec(memory_space=pltpu.SMEM),
            pl.BlockSpec((n_state, tiles, LANE), lambda s: (0, 0, 0)),
        ],
        out_specs=pl.BlockSpec((1, n_state, tiles, LANE), lambda s: (s, 0, 0, 0)),
        out_shape=jax.ShapeDtypeStruct((seqs, n_state, tiles, LANE), jnp.float32),
        scratch_shapes=[held, held],
        compiler_params=pltpu.CompilerParams(vmem_limit_bytes=VMEM_GRANT),
    )(step, drive, rows, rate)


def forward_kernel(
    n_state,
    tiles,
    groups,
    blocks,
    start_ref,
    step_ref,
    input_ref,
    brow_ref,
    crow_ref,
    rate_ref,
    prior_ref,
    mixed_ref,
    carried,
    step_held,
    input_held,
    mixed_held,
):
    base = (pl.program_id(0) * blocks + pl.program_id(1)) * groups * SUB * n_state

    @pl.when(pl.program_id(1) == 0)
    def _():
        carried[...] = start_ref[0]

    def one(group, states):
        states = list(states)
        stage_in(step_ref, group, step_held)
        stage_in(input_ref, group, input_held)
        for at in range(SUB):
            step = token_row(step_held, at, tiles)
            drive = step * token_row(input_held, at, tiles)
            mixed = [None] * 2
            for n in range(n_state):
                where = base + (group * SUB + at) * n_state + n
                prior_ref[group * SUB + at, n] = states[n]
                decay = jnp.exp2(step * rate_ref[n])
                states[n] = decay * states[n] + drive * brow_ref[where]
                term = states[n] * crow_ref[where]
                mixed[n % 2] = term if mixed[n % 2] is None else mixed[n % 2] + term
            mixed_held[pl.ds(at, tiles, stride=SUB), :] = mixed[0] + mixed[1]
        stage_out(mixed_held, mixed_ref, group)
        return tuple(states)

    states = lax.fori_loop(0, groups, one, tuple(carried[n] for n in range(n_state)))
    for n in range(n_state):
        carried[n] = states[n]


def scan_forward(start, step, inputs, b_rows, c_rows, rate, seqs):
    n_state, tiles, _ = rate.shape
    all_groups = step.shape[0] // SUB
    groups = math.gcd(all_groups // seqs, 4)
    blocks = all_groups // seqs // groups
    rows_spec = pl.BlockSpec((groups * SUB, tiles * LANE), lambda s, b: (s * blocks + b, 0))
    held = pltpu.VMEM((tiles * SUB, LANE), jnp.float32)
    smem = pl.BlockSpec(memory_space=pltpu.SMEM)
    tokens = all_groups * SUB
    return pl.pallas_call(
        functools.partial(forward_kernel, n_state, tiles, groups, blocks),
        grid=(seqs, blocks),
        in_specs=[
            pl.BlockSpec((1, n_state, tiles, LANE), lambda s, b: (s, 0, 0, 0)),
            rows_spec,
            rows_spec,
            smem,
            smem,
            pl.BlockSpec((n_state, tiles, LANE), lambda s, b: (0, 0, 0)),
        ],
        out_specs=[
            pl.BlockSpec(
                (groups * SUB, n_state, tiles, LANE), lambda s, b: (s * blocks + b, 0, 0, 0)
            ),
            rows_spec,
        ],
        out_shape=[
            jax.ShapeDtypeStruct((tokens, n_state, tiles, LANE), jnp.float32),
            jax.ShapeDtypeStruct(step.shape, jnp.float32),
        ],
        scratch_shapes=[pltpu.VMEM((n_state, tiles, LANE), jnp.float32)] + [held] * 3,
        compiler_params=pltpu.CompilerParams(vmem_limit_bytes=VMEM_GRANT),
    )(start, step, inputs, b_rows, c_rows, rate)


def backward_kernel(
    n_state,
    tiles,
    groups,
    blocks,
    end_ref,
    prior_ref,
    step_ref,
    input_ref,
    ograd_ref,
    brow_ref,
    crow_ref,
    rate_ref,
    picks_ref,
    step_grad_ref,
    input_grad_ref,
    rate_grad_ref,
    part_ref,
    carried,
    step_held,
    input_held,
    ograd_held,
    step_grad_held,
    input_grad_held,
):
    block = blocks - 1 - pl.program_id(1)
    base = (pl.program_id(0) * blocks + block) * groups * SUB * n_state

    @pl.when(pl.program_id(1) == 0)
    def _():
        carried[...] = end_ref[0]

    @pl.when((pl.program_id(0) == 0) & (pl.program_id(1) == 0))
    def _():
        rate_grad_ref[...] = jnp.zeros_like(rate_grad_ref)

    def one(turn, grads):
        group = groups - 1 - turn
        grads = list(grads)
        stage_in(step_ref, group, step_held)
        stage_in(input_ref, group, input_held)
        stage_in(ograd_ref, group, ograd_held)
        for at in range(SUB - 1, -1, -1):
            step = token_row(step_held, at, tiles)
            value = token_row(input_held, at, tiles)
            ograd = token_row(ograd_held, at, tiles)
            drive = step * value
            along_b = None
            along_rate = None
            brow_parts, crow_parts = [], []
            for n in range(n_state):
                where = base + (group * SUB + at) * n_state + n
                brow, crow = brow_ref[where], crow_ref[where]
                rate = rate_ref[n]
                decay = jnp.exp2(step * rate)
                grad = ograd * crow + grads[n]
                kept = decay * prior_ref[group * SUB + at, n]
                state = kept + drive * brow
                decay_term = grad * kept
                grads[n] = decay * grad
                rate_grad_ref[n] += decay_term * step
                by_rate, by_brow = decay_term * rate, grad * brow
                along_rate = by_rate if along_rate is None else along_rate + by_rate
                along_b = by_brow if along_b is None else along_b + by_brow
                brow_parts.append(grad * drive)
                crow_parts.append(ograd * state)
            step_grad_held[pl.ds(at, tiles, stride=SUB), :] = along_rate * LN2 + along_b * value
            input_grad_held[pl.ds(at, tiles, stride=SUB), :] = along_b * step
            parts = jnp.concatenate(brow_parts + crow_parts, 0).astype(jnp.bfloat16)
            part_ref[group * SUB + at] = jnp.dot(
                picks_ref[...], parts, preferred_element_type=jnp.float32
            )
        stage_out(step_grad_held, step_grad_ref, group)
        stage_out(input_grad_held, input_grad_ref, group)
        return tuple(grads)

    grads = lax.fori_loop(0, groups, one, tuple(carried[n] for n in range(n_state)))
    for n in range(n_state):
        carried[n] = grads[n]


def scan_backward(end_grad, prior, step, inputs, ograd, b_rows, c_rows, rate, seqs):
    n_state, tiles, _ = rate.shape
    all_groups = step.shape[0] // SUB
    groups = math.gcd(all_groups // seqs, 4)
    blocks = all_groups // seqs // groups

    def at(s, b):
        return s * blocks + blocks - 1 - b

    rows_spec = pl.BlockSpec((groups * SUB, tiles * LANE), lambda s, b: (at(s, b), 0))
    held = pltpu.VMEM((tiles * SUB, LANE), jnp.float32)
    smem = pl.BlockSpec(memory_space=pltpu.SMEM)
    tokens = all_groups * SUB
    picks = jnp.repeat(jnp.eye(2 * n_state, dtype=jnp.bfloat16), tiles, 1)
    return pl.pallas_call(
        functools.partial(backward_kernel, n_state, tiles, groups, blocks),
        grid=(seqs, blocks),
        in_specs=[
            pl.BlockSpec((1, n_state, tiles, LANE), lambda s, b: (s, 0, 0, 0)),
            pl.BlockSpec((groups * SUB, n_state, tiles, LANE), lambda s, b: (at(s, b), 0, 0, 0)),
            rows_spec,
            rows_spec,
            rows_spec,
            smem,
            smem,
            pl.BlockSpec((n_state, tiles, LANE), lambda s, b: (0, 0, 0)),
            pl.BlockSpec(picks.shape, lambda s, b: (0, 0)),
        ],
        out_specs=[
            rows_spec,
            rows_spec,
            pl.BlockSpec((n_state, tiles, LANE), lambda s, b: (0, 0, 0)),
            pl.BlockSpec((groups * SUB, 2 * n_state, LANE), lambda s, b: (at(s, b), 0, 0)),
        ],
        out_shape=[
            jax.ShapeDtypeStruct(step.shape, jnp.float32),
            jax.ShapeDtypeStruct(step.shape, jnp.float32),
            jax.ShapeDtypeStruct(rate.shape, jnp.float32),
            jax.ShapeDtypeStruct((tokens, 2 * n_state, LANE), jnp.float32),
        ],
        scratch_shapes=[pltpu.VMEM((n_state, tiles, LANE), jnp.float32)] + [held] * 5,
        compiler_params=pltpu.CompilerParams(vmem_limit_bytes=VMEM_GRANT),
    )(end_grad, prior, step, inputs, ograd, b_rows, c_rows, rate, picks)


def from_earlier(ends, decay, steps):
    count = lax.axis_size("ctx")
    if count == 1:
        return jnp.zeros_like(ends)
    if count == 2:
        return passed_along(ends, "ctx", steps)
    index = lax.axis_index("ctx")
    all_ends = lax.all_gather(ends, "ctx")
    all_decays = lax.all_gather(decay, "ctx")

    def one(turn, state):
        at = turn if steps > 0 else count - 1 - turn
        reached = at < index if steps > 0 else at > index
        return jnp.where(reached, all_decays[at] * state + all_ends[at], state)

    return lax.fori_loop(0, count, one, jnp.zeros_like(ends))


def gathered_rows(rows):
    return lax.all_gather(rows, PLANE, axis=0, tiled=True)


def swapped_columns(rows):
    return lax.all_to_all(rows, PLANE, split_axis=1, concat_axis=0, tiled=True)


def place_in(axes):
    index = 0
    for axis in axes:
        index = index * lax.axis_size(axis) + lax.axis_index(axis)
    return index


def device_at(axes, index):
    where = {}
    for axis in reversed(axes):
        size = lax.axis_size(axis)
        where[axis] = lax.rem(index, size)
        index = lax.div(index, size)
    return where


def greet(groups):
    barrier = pltpu.get_barrier_semaphore()
    total = 0
    for axes, others in groups:
        for other in others:
            pl.semaphore_signal(
                barrier,
                inc=1,
                device_id=device_at(axes, other),
                device_id_type=pl.DeviceIdType.MESH,
            )
            total += 1
    pl.semaphore_wait(barrier, total)


def sent(source, target, send_sem, recv_sem, where):
    copy = pltpu.make_async_remote_copy(
        src_ref=source,
        dst_ref=target,
        send_sem=send_sem,
        recv_sem=recv_sem,
        device_id=where,
        device_id_type=pl.DeviceIdType.MESH,
    )
    copy.start()
    return copy


def finish(copies):
    for copy in copies:
        copy.wait()


def rows_of(ref, index, count):
    rows = ref.shape[0] // count
    return ref.at[pl.ds(pl.multiple_of(index * rows, rows), rows), :]


class Group:
    def __init__(self, axes, send_sem, recv_sem):
        self.axes = axes
        self.count = math.prod(lax.axis_size(axis) for axis in axes)
        self.me = place_in(axes)
        self.others = [lax.rem(self.me + hop, self.count) for hop in range(1, self.count)]
        self.send_sem, self.recv_sem = send_sem, recv_sem

    def own(self, ref):
        return rows_of(ref, self.me, self.count)

    def one(self, source, target, which, hop):
        return sent(
            source,
            target,
            self.send_sem.at[which, hop],
            self.recv_sem.at[which, hop],
            device_at(self.axes, self.others[hop]),
        )

    def scatter(self, part, slot, which):
        return [
            self.one(rows_of(part, other, self.count), slot.at[hop], which, hop)
            for hop, other in enumerate(self.others)
        ]

    def total(self, part, slot):
        total = self.own(part)[...].astype(jnp.float32)
        for hop in range(self.count - 1):
            total = total + slot[hop].astype(jnp.float32)
        return total

    def spread(self, ref, which):
        return [self.one(self.own(ref), self.own(ref), which, hop) for hop in range(self.count - 1)]


def slots_for(part, count):
    return pltpu.VMEM((count - 1, part.shape[0] // count) + part.shape[1:], part.dtype)


def group_size(axes):
    return math.prod(lax.axis_size(axis) for axis in axes)


def line_of_four():
    me = lax.axis_index("tp")
    near = me + 1 - 2 * lax.rem(me, 2)
    return me, near, lax.rem(me + 2, 4), lax.rem(near + 2, 4)


class LineSum:
    def __init__(self, part, near_slots, far_slot, passed, send_sem, recv_sem):
        self.part, self.near_slots, self.far_slot = part, near_slots, far_slot
        self.passed, self.send_sem, self.recv_sem = passed, send_sem, recv_sem
        self.me, self.near, self.far, self.cross = line_of_four()
        self.blocks = send_sem.shape[1]
        self.copies = []

    def columns(self, j):
        wide = self.part.shape[1] // self.blocks
        return slice(j * wide, (j + 1) * wide)

    def rows(self, index):
        return rows_of(self.part, index, 4)

    def send(self, source, target, which, j, where):
        copy = sent(
            source.at[:, self.columns(j)],
            target.at[:, self.columns(j)],
            self.send_sem.at[which, j],
            self.recv_sem.at[which, j],
            {"tp": where},
        )
        self.copies.append((which, copy))
        return copy

    def begin(self, j):
        first = self.send(self.rows(self.cross), self.near_slots.at[0], 0, j, self.near)
        self.send(self.rows(self.near), self.near_slots.at[1], 1, j, self.near)
        return first

    def pass_on(self, j, first):
        first.wait_recv()
        columns = self.columns(j)
        self.passed[:, columns] = (
            self.rows(self.far)[:, columns].astype(jnp.float32)
            + self.near_slots[0, :, columns].astype(jnp.float32)
        ).astype(self.passed.dtype)
        self.send(self.passed, self.far_slot, 2, j, self.far)

    def total(self):
        for which, copy in self.copies:
            copy.wait_send()
            if which:
                copy.wait_recv()
        return (
            self.rows(self.me)[...].astype(jnp.float32)
            + self.near_slots[1].astype(jnp.float32)
            + self.far_slot[...].astype(jnp.float32)
        )

    def pass_all(self, firsts):
        for j, first in enumerate(firsts):
            self.pass_on(j, first)


def line_sum_scratch(part, blocks):
    share = (part.shape[0] // 4,) + part.shape[1:]
    sems = pltpu.SemaphoreType.DMA((3, blocks))
    return [
        pltpu.VMEM((2,) + share, part.dtype),
        pltpu.VMEM(share, part.dtype),
        pltpu.VMEM(share, part.dtype),
        sems,
        sems,
    ]


class LineSpread:
    def __init__(self, ref, send_sem, recv_sem):
        self.ref, self.send_sem, self.recv_sem = ref, send_sem, recv_sem
        self.me, self.near, self.far, self.cross = line_of_four()

    def send(self, owner, half, which, where):
        rows = rows_of(self.ref, owner, 4)
        if half is not None:
            wide = self.ref.shape[1] // 2
            rows = rows.at[:, half * wide : (half + 1) * wide]
        return sent(rows, rows, self.send_sem.at[which], self.recv_sem.at[which], {"tp": where})

    def begin(self):
        self.across = [self.send(self.me, half, half, self.far) for half in range(2)]
        self.within = [self.send(self.me, None, 2, self.near)]

    def pass_on(self):
        for half, copy in enumerate(self.across):
            copy.wait_recv()
            self.within.append(self.send(self.far, half, 3 + half, self.near))

    def end(self):
        for copy in self.across:
            copy.wait_send()
        finish(self.within)

    def run(self):
        self.begin()
        self.pass_on()
        self.end()


def line_spread_scratch():
    return [pltpu.SemaphoreType.DMA((5,)), pltpu.SemaphoreType.DMA((5,))]


class Swap:
    def __init__(self, arrays, swapped, send_sem, recv_sem, local_sem):
        plane = Group(PLANE, send_sem, recv_sem)
        self.plane, self.arrays, self.swapped, self.local_sem = plane, arrays, swapped, local_sem

    def begin(self):
        self.copies, plane = [], self.plane
        for which, (array, swapped) in enumerate(zip(self.arrays, self.swapped)):
            share = swapped.shape[1]

            def columns(index):
                return array.at[:, pl.ds(pl.multiple_of(index * share, share), share)]

            for hop, other in enumerate(plane.others):
                self.copies.append(plane.one(columns(other), plane.own(swapped), which, hop))
            local = pltpu.make_async_copy(
                columns(plane.me), plane.own(swapped), self.local_sem.at[which]
            )
            local.start()
            self.copies.append(local)

    def end(self):
        finish(self.copies)


def swap_scratch(arrays):
    sems = pltpu.SemaphoreType.DMA((len(arrays), group_size(PLANE) - 1))
    return [sems, sems, pltpu.SemaphoreType.DMA((len(arrays),))] if arrays else []


def swap_shapes(arrays):
    count = group_size(PLANE)
    return [
        jax.ShapeDtypeStruct((array.shape[0] * count, array.shape[1] // count), array.dtype)
        for array in arrays
    ]


def swaps_in_kernels(width):
    return width // group_size(PLANE) % LANE == 0


def gathered_shape(shard):
    return jax.ShapeDtypeStruct(
        (shard.shape[0] * group_size(PLANE),) + shard.shape[1:], shard.dtype
    )


def gather_scratch():
    return [gather_sems(), gather_sems(), pltpu.SemaphoreType.DMA(())]


def product_in_blocks(left, source, target, block_buf, block_sem):
    columns = range(0, source.shape[1], WIDE)

    def fetch(turn):
        at = columns[turn]
        return pltpu.make_async_copy(
            source.at[:, at : at + WIDE], block_buf.at[turn % 2], block_sem.at[turn % 2]
        )

    fetch(0).start()
    for turn, at in enumerate(columns):
        if turn + 1 < len(columns):
            fetch(turn + 1).start()
        fetch(turn).wait()
        target[:, at : at + WIDE] = matmul(left[...], block_buf[turn % 2]).astype(target.dtype)


def select_kernel(part, total, slots, send_sem, recv_sem):
    group = Group(("tp",), send_sem, recv_sem)
    greet([(("tp",), group.others)])
    finish(group.scatter(part, slots, 0))
    group.own(total)[...] = group.total(part, slots).astype(total.dtype)
    finish(group.spread(total, 1))


def run_select(call_id, part):
    count = group_size(("tp",))
    vmem = pl.BlockSpec(memory_space=pltpu.VMEM)
    sems = pltpu.SemaphoreType.DMA((2, count - 1))
    return pl.pallas_call(
        select_kernel,
        in_specs=[vmem],
        out_specs=vmem,
        out_shape=jax.ShapeDtypeStruct(part.shape, part.dtype),
        scratch_shapes=[slots_for(part, count), sems, sems],
        compiler_params=pltpu.CompilerParams(
            collective_id=call_id, has_side_effects=True, vmem_limit_bytes=VMEM_GRANT
        ),
    )(part)


def sum_kernel(part, own_rows, total, all_rows, slots, send_sem, recv_sem, *line_sems):
    group = Group(("tp",), send_sem, recv_sem)
    rows = LineSpread(all_rows, *line_sems)
    greet([(("tp",), group.others)])
    copies = group.scatter(part, slots, 0)
    group.own(all_rows)[...] = own_rows[...]
    rows.begin()
    finish(copies)
    group.own(total)[...] = group.total(part, slots).astype(total.dtype)
    copies = group.spread(total, 1)
    rows.pass_on()
    finish(copies)
    rows.end()


def sum_over_tp(call_id, part, own_rows):
    count = group_size(("tp",))
    vmem = pl.BlockSpec(memory_space=pltpu.VMEM)
    sems = pltpu.SemaphoreType.DMA((2, count - 1))
    return pl.pallas_call(
        sum_kernel,
        in_specs=[vmem] * 2,
        out_specs=[vmem] * 2,
        out_shape=[
            jax.ShapeDtypeStruct(part.shape, part.dtype),
            jax.ShapeDtypeStruct((own_rows.shape[0] * count, own_rows.shape[1]), own_rows.dtype),
        ],
        scratch_shapes=[slots_for(part, count), sems, sems] + line_spread_scratch(),
        compiler_params=pltpu.CompilerParams(
            collective_id=call_id, has_side_effects=True, vmem_limit_bytes=VMEM_GRANT
        ),
    )(part, own_rows)


def mixer_out_kernel(n_swaps, gated, out_first, out_last, tokens, gain, *refs):
    arrays, refs = refs[:n_swaps], refs[n_swaps:]
    normed, middle, gated_all, *refs = refs
    swapped, refs = refs[:n_swaps], refs[n_swaps:]
    part, refs = refs[0], refs[1:]
    line = LineSum(part, *refs[:5])
    spread = LineSpread(normed, *refs[5:7])
    gather_send, gather_recv, local_sem, *refs = refs[7:]
    group = Group(("tp",), None, None)
    gather = PlaneGather(gated, gated_all, gather_send, gather_recv)
    half = gated.shape[1] // 2
    share = out_first.shape[1]
    greet([(("tp",), group.others), (PLANE, gather.others)])
    gather.begin(local_sem)
    for at in range(out_first.shape[0] // half):
        rows = slice(at * half, (at + 1) * half)
        part[:, at * share : (at + 1) * share] = (
            matmul(gated[:, :half], out_first[rows, :])
            + matmul(gated[:, half:], out_last[rows, :])
        ).astype(part.dtype)
    firsts = [line.begin(j) for j in range(line.blocks)]
    if n_swaps:
        swap = Swap(arrays, swapped, *refs)
        swap.begin()
    line.pass_all(firsts)
    rows = group.own(tokens)[...].astype(jnp.float32) + line.total()
    middle[...] = rows
    group.own(normed)[...] = (rows * inverse_rms(rows) * gain[...].astype(jnp.float32)).astype(
        normed.dtype
    )
    spread.begin()
    gather.relay()
    gather.hand_over()
    spread.pass_on()
    spread.end()
    gather.hand_over_last()
    gather.end()
    if n_swaps:
        swap.end()


def mixer_out(call_id, gated, out_first, out_last, tokens, gain, arrays):
    count = group_size(("tp",))
    vmem = pl.BlockSpec(memory_space=pltpu.VMEM)
    hbm = pl.BlockSpec(memory_space=pltpu.HBM)
    rows, width = tokens.shape
    part = jax.ShapeDtypeStruct((rows, width), jnp.bfloat16)
    return pl.pallas_call(
        functools.partial(mixer_out_kernel, len(arrays)),
        in_specs=[vmem] * (5 + len(arrays)),
        out_specs=[vmem] * 2 + [hbm] + [hbm] * len(arrays),
        out_shape=[
            part,
            jax.ShapeDtypeStruct((rows // count, width), jnp.float32),
            gathered_shape(gated),
        ]
        + swap_shapes(arrays),
        scratch_shapes=[pltpu.VMEM(part.shape, part.dtype)]
        + line_sum_scratch(part, 2)
        + line_spread_scratch()
        + gather_scratch()
        + swap_scratch(arrays),
        compiler_params=pltpu.CompilerParams(
            collective_id=call_id, has_side_effects=True, vmem_limit_bytes=VMEM_GRANT
        ),
    )(gated, out_first, out_last, tokens, gain, *arrays)


def ffn_kernel(swaps, normed, ct, weights, made, *refs):
    hidden = weights.shape[1] // 3
    if swaps:
        *swapped, block_buf, block_sem, send_sem, recv_sem, local_sem = refs
        swap = Swap([ct], swapped, send_sem, recv_sem, local_sem)
        greet([(PLANE, swap.plane.others)])
        swap.begin()
    else:
        block_buf, block_sem = refs

    def columns(j, which):
        return pl.ds(pl.multiple_of(which * hidden + j * WIDE, WIDE), WIDE)

    def fetch(j, which):
        slot = lax.rem(j, 2)
        return pltpu.make_async_copy(
            weights.at[:, columns(j, which)],
            block_buf.at[slot, which],
            block_sem.at[slot, which],
        )

    for which in range(3):
        fetch(0, which).start()

    @pl.loop(0, hidden // WIDE)
    def _(j):
        slot = lax.rem(j, 2)

        @pl.when(j + 1 < hidden // WIDE)
        def _():
            for which in range(3):
                fetch(j + 1, which).start()

        fetch(j, 0).wait()
        gate = matmul(normed[...], block_buf[slot, 0])
        fetch(j, 1).wait()
        up = matmul(normed[...], block_buf[slot, 1])
        fetch(j, 2).wait()
        act_grad = matmul(ct[...], block_buf[slot, 2])
        logistic = jax.nn.sigmoid(gate)
        silu = gate * logistic
        slope = logistic * (1.0 + gate * (1.0 - logistic))
        made[:, columns(j, 0)] = (silu * up).astype(made.dtype)
        made[:, columns(j, 1)] = (act_grad * up * slope).astype(made.dtype)
        made[:, columns(j, 2)] = (act_grad * silu).astype(made.dtype)

    if swaps:
        swap.end()


def run_ffn(call_id, normed, ct, weights, swaps):
    rows, width = normed.shape
    arrays = [ct] if swaps else []
    vmem = pl.BlockSpec(memory_space=pltpu.VMEM)
    params = dict(collective_id=call_id, has_side_effects=True) if swaps else {}
    return pl.pallas_call(
        functools.partial(ffn_kernel, swaps),
        in_specs=[vmem, vmem, pl.BlockSpec(memory_space=pltpu.HBM)],
        out_specs=[vmem] + [pl.BlockSpec(memory_space=pltpu.HBM)] * len(arrays),
        out_shape=[jax.ShapeDtypeStruct((rows, weights.shape[1]), jnp.bfloat16)]
        + swap_shapes(arrays),
        scratch_shapes=[
            pltpu.VMEM((2, 3, width, WIDE), jnp.bfloat16),
            pltpu.SemaphoreType.DMA((2, 3)),
        ]
        + swap_scratch(arrays),
        compiler_params=pltpu.CompilerParams(vmem_limit_bytes=VMEM_GRANT, **params),
    )(normed, ct, weights)


def ffn_back_kernel(
    n_swaps,
    made,
    ct,
    middle,
    gain,
    out_first,
    out_last,
    weights,
    *refs,
):
    arrays, refs = refs[:n_swaps], refs[n_swaps:]
    middle_low, middle_grad, gain_grad, gated_grad, ffn_part, *refs = refs
    swapped, refs = refs[:n_swaps], refs[n_swaps:]
    part, wide_buf, down_buf, wide_sem, down_sem, *sems = refs
    hidden = made.shape[1] // 3
    blocks = part.shape[1] // WIDE
    group = Group(("tp",), None, None)
    line = LineSum(part, *sems[:5])
    spread = LineSpread(middle_low, *sems[5:7])
    if n_swaps:
        swap = Swap(arrays, swapped, *sems[7:])
        greet([(("tp",), group.others), (PLANE, swap.plane.others)])
        swap.begin()
    else:
        greet([(("tp",), group.others)])

    def fetch(j):
        return pltpu.make_async_copy(
            weights.at[j * WIDE : (j + 1) * WIDE, : 2 * hidden],
            wide_buf.at[j % 2],
            wide_sem.at[j % 2],
        )

    def fetch_down(j):
        return pltpu.make_async_copy(
            weights.at[j * WIDE : (j + 1) * WIDE, 2 * hidden :],
            down_buf.at[j % 2],
            down_sem.at[j % 2],
        )

    fetch(0).start()
    firsts = []
    for j in range(blocks):
        if j + 1 < blocks:
            fetch(j + 1).start()
        else:
            fetch_down(0).start()
        fetch(j).wait()
        columns = slice(j * WIDE, (j + 1) * WIDE)
        part[:, columns] = matmul_nt(made[:, hidden:], wide_buf[j % 2]).astype(part.dtype)
        firsts.append(line.begin(j))
    for j in range(blocks):
        if j + 1 < blocks:
            fetch_down(j + 1).start()
        fetch_down(j).wait()
        ffn_part[:, j * WIDE : (j + 1) * WIDE] = matmul_nt(
            made[:, :hidden], down_buf[j % 2]
        ).astype(ffn_part.dtype)
        line.pass_on(j, firsts[j])
    normed_grad = line.total()
    rows = middle[...]
    scale = inverse_rms(rows)
    gain_grad[...] = jnp.sum(normed_grad * rows * scale, 0, keepdims=True)
    grad = group.own(ct)[...].astype(jnp.float32) + norm_back(
        normed_grad, rows, scale, gain[...].astype(jnp.float32)
    )
    middle_grad[...] = grad
    group.own(middle_low)[...] = grad.astype(middle_low.dtype)
    spread.run()
    half = gated_grad.shape[1] // 2
    share = out_first.shape[1]
    for side, shards in enumerate((out_first, out_last)):
        total = None
        for at in range(shards.shape[0] // half):
            one = matmul_nt(
                middle_low[:, at * share : (at + 1) * share],
                shards[at * half : (at + 1) * half, :],
            )
            total = one if total is None else total + one
        gated_grad[:, side * half : (side + 1) * half] = total
    if n_swaps:
        swap.end()


def ffn_back(call_id, made, ct, middle, gain, out_first, out_last, weights, arrays):
    count = group_size(("tp",))
    vmem = pl.BlockSpec(memory_space=pltpu.VMEM)
    hbm = pl.BlockSpec(memory_space=pltpu.HBM)
    rows, width = ct.shape
    hidden = made.shape[1] // 3
    inner = 2 * out_first.shape[0] // group_size(PLANE)
    low, full = jnp.bfloat16, jnp.float32
    part = jax.ShapeDtypeStruct((rows, width), low)
    dma = pltpu.SemaphoreType.DMA
    return pl.pallas_call(
        functools.partial(ffn_back_kernel, len(arrays)),
        in_specs=[vmem] * 6 + [hbm] + [vmem] * len(arrays),
        out_specs=[vmem] * 5 + [hbm] * len(arrays),
        out_shape=[
            part,
            jax.ShapeDtypeStruct((rows // count, width), full),
            jax.ShapeDtypeStruct((1, width), full),
            jax.ShapeDtypeStruct((rows, inner), full),
            part,
        ]
        + swap_shapes(arrays),
        scratch_shapes=[
            pltpu.VMEM(part.shape, low),
            pltpu.VMEM((2, WIDE, 2 * hidden), low),
            pltpu.VMEM((2, WIDE, hidden), low),
            dma((2,)),
            dma((2,)),
        ]
        + line_sum_scratch(part, width // WIDE)
        + line_spread_scratch()
        + swap_scratch(arrays),
        compiler_params=pltpu.CompilerParams(
            collective_id=call_id, has_side_effects=True, vmem_limit_bytes=VMEM_GRANT
        ),
    )(made, ct, middle, gain, out_first, out_last, weights, *arrays)


def send_on(source, target, send_sem, recv_sem, ctx):
    return pltpu.make_async_remote_copy(
        src_ref=source,
        dst_ref=target,
        send_sem=send_sem,
        recv_sem=recv_sem,
        device_id={"ctx": ctx},
        device_id_type=pl.DeviceIdType.MESH,
    )


def forward_pair_kernel(
    n_state,
    tiles,
    groups,
    blocks,
    seqs,
    step_ref,
    input_ref,
    brow_ref,
    crow_ref,
    rate_ref,
    shard,
    *refs,
):
    prior_ref, mixed_ref, gathered, *refs = refs
    carried, ends, starts, prior_buf, step_held, input_held, mixed_held, *refs = refs
    prior_sem, send_sem, recv_sem, gather_send, gather_recv, local_sem = refs
    place = lax.axis_index("ctx")
    gather = PlaneGather(shard, gathered, gather_send, gather_recv)
    greet([(PLANE, gather.others)])
    gather.begin(local_sem)

    def hand_on(seq):
        return send_on(ends.at[seq], starts.at[seq], send_sem.at[seq], recv_sem.at[seq], 1)

    def store(block):
        slot = lax.rem(block, 2)
        rows = groups * SUB
        return pltpu.make_async_copy(
            prior_buf.at[slot],
            prior_ref.at[pl.ds(pl.multiple_of(block * rows, rows), rows)],
            prior_sem.at[slot],
        )

    def one_sequence(seq):
        @pl.when(place == 0)
        def _():
            carried[...] = jnp.zeros_like(carried)

        @pl.when(place == 1)
        def _():
            hand_on(seq).wait_recv()
            carried[...] = starts[seq]

        @pl.loop(0, blocks)
        def _(inner_block):
            block = seq * blocks + inner_block
            slot = lax.rem(block, 2)

            @pl.when(block >= 2)
            def _():
                store(block - 2).wait()

            def one(turn, states):
                group = block * groups + turn
                states = list(states)
                stage_in(step_ref, group, step_held)
                stage_in(input_ref, group, input_held)
                for at in range(SUB):
                    step = token_row(step_held, at, tiles)
                    drive = step * token_row(input_held, at, tiles)
                    mixed = [None] * 2
                    for n in range(n_state):
                        where = (group * SUB + at) * n_state + n
                        prior_buf[slot, turn * SUB + at, n] = states[n]
                        decay = jnp.exp2(step * rate_ref[n])
                        states[n] = decay * states[n] + drive * brow_ref[where]
                        term = states[n] * crow_ref[where]
                        mixed[n % 2] = term if mixed[n % 2] is None else mixed[n % 2] + term
                    mixed_held[pl.ds(at, tiles, stride=SUB), :] = mixed[0] + mixed[1]
                stage_out(mixed_held, mixed_ref, group)
                return tuple(states)

            states = lax.fori_loop(0, groups, one, tuple(carried[n] for n in range(n_state)))
            for n in range(n_state):
                carried[n] = states[n]
            store(block).start()

        @pl.when(place == 0)
        def _():
            ends[seq] = carried[...]
            hand_on(seq).start()

    for seq in range(seqs):
        one_sequence(seq)
        if seq == 0:
            gather.relay()
            gather.hand_over()
    gather.hand_over_last()
    for block in range(max(0, seqs * blocks - 2), seqs * blocks):
        store(block).wait()

    @pl.when(place == 0)
    def _():
        for seq in range(seqs):
            hand_on(seq).wait_send()

    gather.end()


def scan_forward_pair(
    call_id, step, inputs, b_rows, c_rows, rate, seqs, shard
):
    n_state, tiles, _ = rate.shape
    tokens, inner = step.shape
    all_groups = tokens // SUB
    groups = math.gcd(all_groups // seqs, 4)
    blocks = all_groups // seqs // groups
    vmem = pl.BlockSpec(memory_space=pltpu.VMEM)
    smem = pl.BlockSpec(memory_space=pltpu.SMEM)
    hbm = pl.BlockSpec(memory_space=pltpu.HBM)
    full = jnp.float32
    held = pltpu.VMEM((tiles * SUB, LANE), full)
    boundary = pltpu.VMEM((seqs, n_state, tiles, LANE), full)
    dma = pltpu.SemaphoreType.DMA
    return pl.pallas_call(
        functools.partial(
            forward_pair_kernel, n_state, tiles, groups, blocks, seqs
        ),
        in_specs=[vmem, vmem, smem, smem, vmem, hbm],
        out_specs=[hbm, vmem, hbm],
        out_shape=[
            jax.ShapeDtypeStruct((tokens, n_state, tiles, LANE), full),
            jax.ShapeDtypeStruct(step.shape, full),
            gathered_shape(shard),
        ],
        scratch_shapes=[
            pltpu.VMEM((n_state, tiles, LANE), full),
            boundary,
            boundary,
            pltpu.VMEM((2, groups * SUB, n_state, tiles, LANE), full),
            held,
            held,
            held,
            dma((2,)),
            dma((seqs,)),
            dma((seqs,)),
        ]
        + gather_scratch(),
        compiler_params=pltpu.CompilerParams(
            collective_id=call_id, has_side_effects=True, vmem_limit_bytes=VMEM_GRANT
        ),
    )(step, inputs, b_rows, c_rows, rate, shard)


def backward_pair_kernel(
    n_swaps,
    n_state,
    tiles,
    groups,
    blocks,
    seqs,
    step_ref,
    input_ref,
    ograd_ref,
    brow_ref,
    crow_ref,
    rate_ref,
    picks_ref,
    ffn_part,
    middle,
    prior_ref,
    *refs,
):
    arrays, refs = refs[:n_swaps], refs[n_swaps:]
    step_grad_ref, input_grad_ref, rate_grad_ref, part_ref, *refs = refs
    layer_first, layer_last, *refs = refs
    swapped, refs = refs[:n_swaps], refs[n_swaps:]
    carried, ends, starts, prior_buf, step_held, input_held, ograd_held, *refs = refs
    step_grad_held, input_grad_held, ffn_slots, prior_sem, send_sem, recv_sem, *refs = refs
    tp_send, tp_recv, *refs = refs
    place = lax.axis_index("ctx")
    tp = Group(("tp",), tp_send, tp_recv)
    if n_swaps:
        swap = Swap(arrays, swapped, *refs)
        greet([(PLANE, swap.plane.others), (("tp",), tp.others)])
        swap.begin()
    else:
        greet([(("ctx",), [1 - place]), (("tp",), tp.others)])
    ffn_sent = tp.scatter(ffn_part, ffn_slots, 0)

    def hand_on(seq):
        return send_on(ends.at[seq], starts.at[seq], send_sem.at[seq], recv_sem.at[seq], 0)

    def fetch(turn):
        seq = lax.div(turn, blocks)
        block = seq * blocks + blocks - 1 - lax.rem(turn, blocks)
        slot = lax.rem(turn, 2)
        rows = groups * SUB
        return pltpu.make_async_copy(
            prior_ref.at[pl.ds(pl.multiple_of(block * rows, rows), rows)],
            prior_buf.at[slot],
            prior_sem.at[slot],
        )

    fetch(0).start()
    rate_grad_ref[...] = jnp.zeros_like(rate_grad_ref)

    @pl.when(place == 1)
    def _():
        @pl.loop(0, seqs)
        def _(seq):
            def one(turn, grads):
                group = (seq + 1) * blocks * groups - 1 - turn
                grads = list(grads)
                stage_in(step_ref, group, step_held)
                stage_in(ograd_ref, group, ograd_held)
                for at in range(SUB - 1, -1, -1):
                    step = token_row(step_held, at, tiles)
                    ograd = token_row(ograd_held, at, tiles)
                    for n in range(n_state):
                        row = crow_ref[(group * SUB + at) * n_state + n]
                        grads[n] = jnp.exp2(step * rate_ref[n]) * (grads[n] + ograd * row)
                return tuple(grads)

            zero = jnp.zeros((tiles, LANE), jnp.float32)
            grads = lax.fori_loop(0, blocks * groups, one, (zero,) * n_state)
            for n in range(n_state):
                ends[seq, n] = grads[n]
            hand_on(seq).start()

    @pl.loop(0, seqs)
    def _(seq):
        @pl.when(place == 1)
        def _():
            carried[...] = jnp.zeros_like(carried)

        @pl.when(place == 0)
        def _():
            hand_on(seq).wait_recv()
            carried[...] = starts[seq]

        @pl.loop(0, blocks)
        def _(inner_block):
            turn = seq * blocks + inner_block
            slot = lax.rem(turn, 2)
            first_group = (seq * blocks + blocks - 1 - inner_block) * groups

            @pl.when(turn + 1 < seqs * blocks)
            def _():
                fetch(turn + 1).start()

            fetch(turn).wait()

            def one(back, grads):
                inner_group = groups - 1 - back
                group = first_group + inner_group
                grads = list(grads)
                stage_in(step_ref, group, step_held)
                stage_in(input_ref, group, input_held)
                stage_in(ograd_ref, group, ograd_held)
                for at in range(SUB - 1, -1, -1):
                    step = token_row(step_held, at, tiles)
                    value = token_row(input_held, at, tiles)
                    ograd = token_row(ograd_held, at, tiles)
                    drive = step * value
                    along_b = None
                    along_rate = None
                    brow_parts, crow_parts = [], []
                    for n in range(n_state):
                        where = (group * SUB + at) * n_state + n
                        brow, crow = brow_ref[where], crow_ref[where]
                        rate = rate_ref[n]
                        decay = jnp.exp2(step * rate)
                        grad = ograd * crow + grads[n]
                        kept = decay * prior_buf[slot, inner_group * SUB + at, n]
                        state = kept + drive * brow
                        decay_term = grad * kept
                        grads[n] = decay * grad
                        rate_grad_ref[n] += decay_term * step
                        by_rate, by_brow = decay_term * rate, grad * brow
                        along_rate = by_rate if along_rate is None else along_rate + by_rate
                        along_b = by_brow if along_b is None else along_b + by_brow
                        brow_parts.append(grad * drive)
                        crow_parts.append(ograd * state)
                    step_grad_held[pl.ds(at, tiles, stride=SUB), :] = (
                        along_rate * LN2 + along_b * value
                    )
                    input_grad_held[pl.ds(at, tiles, stride=SUB), :] = along_b * step
                    parts = jnp.concatenate(brow_parts + crow_parts, 0).astype(jnp.bfloat16)
                    part_ref[group * SUB + at] = jnp.dot(
                        picks_ref[...], parts, preferred_element_type=jnp.float32
                    )
                stage_out(step_grad_held, step_grad_ref, group)
                stage_out(input_grad_held, input_grad_ref, group)
                return tuple(grads)

            grads = lax.fori_loop(0, groups, one, tuple(carried[n] for n in range(n_state)))
            for n in range(n_state):
                carried[n] = grads[n]

    finish(ffn_sent)
    layer_rows = (middle[...] + tp.total(ffn_part, ffn_slots)).astype(layer_first.dtype)
    half = layer_first.shape[1]
    layer_first[...], layer_last[...] = layer_rows[:, :half], layer_rows[:, half:]

    @pl.when(place == 1)
    def _():
        @pl.loop(0, seqs)
        def _(seq):
            hand_on(seq).wait_send()

    if n_swaps:
        swap.end()


def scan_backward_pair(
    call_id, prior, step, inputs, ograd, b_rows, c_rows, rate, seqs, ffn_part, middle, arrays
):
    n_state, tiles, _ = rate.shape
    tokens, inner = step.shape
    all_groups = tokens // SUB
    groups = math.gcd(all_groups // seqs, 4)
    blocks = all_groups // seqs // groups
    tp_count = group_size(("tp",))
    vmem = pl.BlockSpec(memory_space=pltpu.VMEM)
    smem = pl.BlockSpec(memory_space=pltpu.SMEM)
    hbm = pl.BlockSpec(memory_space=pltpu.HBM)
    full = jnp.float32
    held = pltpu.VMEM((tiles * SUB, LANE), full)
    boundary = pltpu.VMEM((seqs, n_state, tiles, LANE), full)
    dma = pltpu.SemaphoreType.DMA
    layer_half = jax.ShapeDtypeStruct((middle.shape[0], middle.shape[1] // 2), jnp.bfloat16)
    picks = jnp.repeat(jnp.eye(2 * n_state, dtype=jnp.bfloat16), tiles, 1)
    return pl.pallas_call(
        functools.partial(
            backward_pair_kernel, len(arrays), n_state, tiles, groups, blocks, seqs
        ),
        in_specs=[vmem] * 3 + [smem] * 2 + [vmem] * 4 + [hbm] + [vmem] * len(arrays),
        out_specs=[vmem] * 6 + [hbm] * len(arrays),
        out_shape=[
            jax.ShapeDtypeStruct(step.shape, full),
            jax.ShapeDtypeStruct(step.shape, full),
            jax.ShapeDtypeStruct(rate.shape, full),
            jax.ShapeDtypeStruct((tokens, 2 * n_state, LANE), full),
            layer_half,
            layer_half,
        ]
        + swap_shapes(arrays),
        scratch_shapes=[
            pltpu.VMEM((n_state, tiles, LANE), full),
            boundary,
            boundary,
            pltpu.VMEM((2, groups * SUB, n_state, tiles, LANE), full),
        ]
        + [held] * 5
        + [
            slots_for(ffn_part, tp_count),
            dma((2,)),
            dma((seqs,)),
            dma((seqs,)),
            dma((1, tp_count - 1)),
            dma((1, tp_count - 1)),
        ]
        + swap_scratch(arrays),
        compiler_params=pltpu.CompilerParams(
            collective_id=call_id, has_side_effects=True, vmem_limit_bytes=VMEM_GRANT
        ),
    )(step, inputs, ograd, b_rows, c_rows, rate, picks, ffn_part, middle, prior, *arrays)


class PlaneGather:
    def __init__(self, own, gathered, send_sem, recv_sem):
        self.own, self.gathered = own, gathered
        self.send_sem, self.recv_sem = send_sem, recv_sem
        self.dp, self.ctx = lax.axis_index("dp"), lax.axis_index("ctx")
        self.n_dp, self.n_ctx = lax.axis_size("dp"), lax.axis_size("ctx")
        self.hands_on = relayed()
        self.count = self.n_dp * self.n_ctx
        self.me = self.dp * self.n_ctx + self.ctx
        self.others = [lax.rem(self.me + hop, self.count) for hop in range(1, self.count)]
        self.copies = {}
        if self.hands_on:
            core = lax.rem(self.dp, 2)
            over_core = self.dp + 1 - 2 * core
            over_y = lax.rem(self.dp + 2, 4)
            over_x = 1 - self.ctx
            self.core = {"dp": over_core, "ctx": self.ctx}
            self.at_x = {"dp": self.dp, "ctx": over_x}
            self.at_y = {"dp": over_y, "ctx": self.ctx}
            self.from_x = self.dp * 2 + over_x
            self.from_y = over_y * 2 + self.ctx
            self.across = over_y * 2 + over_x

    def part(self, owner, half):
        rows = self.gathered.shape[0] // self.count
        start, size = owner * rows, rows
        if half is not None:
            size = rows // 2
            start = start + half * size
        return self.gathered.at[pl.ds(pl.multiple_of(start, size), size), :]

    def send(self, which, owner, half, where):
        target = self.part(owner, half)
        source = target
        if owner is self.me:
            rows = self.own.shape[0]
            source = self.own
            if half is not None:
                source = self.own.at[pl.ds(half * (rows // 2), rows // 2), :]
        self.copies[which] = sent(
            source, target, self.send_sem.at[which], self.recv_sem.at[which], where
        )

    def arrived(self, *which):
        for one in which:
            self.copies[one].wait_recv()

    def begin(self, local_sem):
        self.local = pltpu.make_async_copy(self.own, self.part(self.me, None), local_sem)
        self.local.start()
        if not self.hands_on:
            for hop, other in enumerate(self.others):
                self.send(hop, self.me, None, device_at(PLANE, other))
            return
        self.send(0, self.me, 1, self.at_x)
        self.send(1, self.me, 0, self.at_y)
        self.send(2, self.me, None, self.core)
        self.send(3, self.me, 0, self.at_x)
        self.send(4, self.me, 1, self.at_y)

    def relay(self):
        if not self.hands_on:
            return
        self.arrived(0, 1)
        self.send(5, self.from_x, 1, self.at_y)
        self.send(6, self.from_y, 0, self.at_x)
        self.send(7, self.from_x, 1, self.core)
        self.send(8, self.from_y, 0, self.core)

    def hand_over(self):
        if not self.hands_on:
            return
        self.arrived(3, 4)
        self.send(9, self.from_x, 0, self.core)
        self.send(10, self.from_y, 1, self.core)

    def hand_over_last(self):
        if not self.hands_on:
            return
        self.arrived(5, 6)
        self.send(11, self.across, 1, self.core)
        self.send(12, self.across, 0, self.core)

    def end(self):
        if self.hands_on:
            self.arrived(2, 7, 8, 9, 10, 11, 12)
        else:
            self.arrived(*range(self.count - 1))
        for copy in self.copies.values():
            copy.wait_send()
        self.local.wait()


def relayed():
    return lax.axis_size("dp") == 4 and lax.axis_size("ctx") == 2


def gather_sems():
    count = 13 if relayed() else group_size(PLANE) - 1
    return pltpu.SemaphoreType.DMA((count,))


WIDE = 512


def products(source, first, last, dot, target, block_buf, block_sem, out_buf, out_sem):
    def fetch(j, slot):
        columns = pl.ds(pl.multiple_of(j * WIDE, WIDE), WIDE)
        return pltpu.make_async_copy(
            source.at[:, columns], block_buf.at[slot], block_sem.at[slot]
        )

    def store(j, slot):
        return pltpu.make_async_copy(out_buf.at[slot], target(j), out_sem.at[slot])

    fetch(first, first % 2).start()

    @pl.loop(first, last)
    def _(j):
        slot = lax.rem(j, 2)

        @pl.when(j + 1 < last)
        def _():
            fetch(j + 1, 1 - slot).start()

        fetch(j, slot).wait()

        @pl.when(j >= first + 2)
        def _():
            store(j - 2, slot).wait()

        out_buf[slot] = dot(block_buf[slot])
        store(j, slot).start()

    for j in range(max(first, last - 2), last):
        store(j, j % 2).wait()


class PlaneSum:
    def __init__(self, array, total, *refs):
        self.array, self.result = array, total
        self.hands_on = relayed()
        if not self.hands_on:
            self.slots, send_sem, recv_sem = refs
            self.group = Group(PLANE, send_sem, recv_sem)
            return
        self.core_slot, self.pair, self.chip_slots, *self.sems = refs
        dp, ctx = lax.axis_index("dp"), lax.axis_index("ctx")
        self.half = lax.rem(dp, 2)
        self.other_core = {"dp": dp + 1 - 2 * self.half, "ctx": ctx}
        over_y, over_x = lax.rem(dp + 2, 4), 1 - ctx
        self.quarter = lax.div(dp, 2) * 2 + ctx
        self.chips = [
            ({"dp": a, "ctx": b}, lax.div(a, 2) * 2 + b)
            for a, b in ((dp, over_x), (over_y, ctx), (over_y, over_x))
        ]

    def to_core(self, source, target, which):
        core_send, core_recv = self.sems[:2]
        return sent(
            source, target, core_send.at[which], core_recv.at[which], self.other_core
        )

    def to_chip(self, source, target, which, at):
        chip_send, chip_recv = self.sems[2:]
        return sent(
            source,
            target,
            chip_send.at[which, at],
            chip_recv.at[which, at],
            self.chips[at][0],
        )

    def begin(self):
        if not self.hands_on:
            self.copies = self.group.scatter(self.array, self.slots, 0)
            return
        self.copies = [self.to_core(rows_of(self.array, 1 - self.half, 2), self.core_slot, 0)]

    def add_pair(self):
        if not self.hands_on:
            return
        finish(self.copies)
        self.pair[...] = (
            rows_of(self.array, self.half, 2)[...].astype(jnp.float32)
            + self.core_slot[...].astype(jnp.float32)
        ).astype(self.pair.dtype)
        self.copies = [
            self.to_chip(rows_of(self.pair, index, 4), self.chip_slots.at[at], 0, at)
            for at, (_, index) in enumerate(self.chips)
        ]

    def add_all(self):
        finish(self.copies)
        if not self.hands_on:
            self.group.own(self.result)[...] = self.group.total(self.array, self.slots).astype(
                self.result.dtype
            )
            self.copies = self.group.spread(self.result, 1)
            return
        total = rows_of(self.pair, self.quarter, 4)[...].astype(jnp.float32)
        for at in range(3):
            total = total + self.chip_slots[at].astype(jnp.float32)
        mine = rows_of(self.result, self.half * 4 + self.quarter, 8)
        mine[...] = total.astype(self.result.dtype)
        self.copies = [self.to_chip(mine, mine, 1, at) for at in range(3)]

    def hand_over(self):
        if not self.hands_on:
            return
        finish(self.copies)
        half = rows_of(self.result, self.half, 2)
        self.copies = [self.to_core(half, half, 1)]

    def end(self):
        finish(self.copies)


def plane_sum_scratch(array):
    dma = pltpu.SemaphoreType.DMA
    count = group_size(PLANE)
    if not relayed():
        return [slots_for(array, count), dma((2, count - 1)), dma((2, count - 1))]
    rows, width = array.shape
    return [
        pltpu.VMEM((rows // 2, width), array.dtype),
        pltpu.VMEM((rows // 2, width), array.dtype),
        pltpu.VMEM((3, rows // 8, width), array.dtype),
        dma((2,)),
        dma((2,)),
        dma((2, 3)),
        dma((2, 3)),
    ]


SMALL_ROWS = 32
GAIN_ROWS = 16


def tail_kernel(
    swaps,
    conv_grad,
    gate_grad,
    convkern,
    convbias,
    stepbias,
    decaylog,
    skipgain,
    ffngain,
    layer_first,
    layer_rows,
    middle_low,
    step_low,
    pre_low,
    select_low,
    scan_in,
    tokens,
    middle_grad,
    gain_row,
    in_conv,
    in_gate,
    one_cols,
    two_cols,
    ct_cols,
    middle_cols,
    ffn_all,
    gated_all,
    tokens_grad,
    layer_out,
    vectors_sum,
    step_sum,
    select_sum,
    gains,
    mix_all,
    grad_inproj,
    grad_outproj,
    grad_gateup,
    grad_downproj,
    mix_own,
    normed_part,
    small,
    small_sum,
    gain_slots,
    gain_own,
    vectors_own,
    cols,
    in_buf,
    block_buf,
    wide_buf,
    tall_buf,
    cols_sem,
    in_sem,
    block_sem,
    wide_sem,
    tall_sem,
    tp_send,
    tp_recv,
    gather_send,
    gather_recv,
    local_sem,
    *sems,
):
    inner = conv_grad.shape[1]
    hidden = ffn_all.shape[1] // 3
    width = tokens.shape[1]
    rank = step_low.shape[1]
    tp = Group(("tp",), tp_send, tp_recv)
    line = LineSum(normed_part, *sems[:5])
    tokens_spread = LineSpread(tokens_grad, *sems[5:7])
    layer_last = layer_out.at[:, width // 2 :]
    layer_spread = LineSpread(layer_last, *sems[7:9])
    count = 7 if relayed() else 3
    small_total = PlaneSum(small, small_sum, *sems[9 : 9 + count])
    swap_sems = sems[9 + count :]
    gather = PlaneGather(mix_own, mix_all, gather_send, gather_recv)
    sources = (one_cols, two_cols, ct_cols) if swaps else (one_cols, two_cols, ct_cols, middle_cols)
    loads = [
        pltpu.make_async_copy(source, cols.at[at], cols_sem.at[at])
        for at, source in enumerate(sources)
    ]
    if swaps:
        swap = Swap([middle_low], [cols.at[3]], *swap_sems)

    def fetch(j):
        slot = j % 2
        rows = slice(j * WIDE, (j + 1) * WIDE)
        return [
            pltpu.make_async_copy(source.at[rows, :], in_buf.at[slot, at], in_sem.at[slot, at])
            for at, source in enumerate((in_conv, in_gate))
        ]

    for copy in fetch(0) + loads:
        copy.start()
    mix_own[:, :inner] = conv_grad[...]
    mix_own[:, inner:] = gate_grad[...]
    greet([(("tp",), tp.others), (PLANE, gather.others)])
    gather.begin(local_sem)

    small[...] = jnp.zeros_like(small)
    vectors_own[...] = jnp.zeros_like(vectors_own)
    at = 0
    for vector in (convkern, convbias, stepbias, decaylog, skipgain):
        vectors_own[at : at + vector.shape[0], :] = vector[...]
        at += vector.shape[0]
    at = SMALL_ROWS - GAIN_ROWS + 10
    for row in range(width // inner):
        vectors_own[at + row : at + row + 1, :] = ffngain[:, row * inner : (row + 1) * inner]
    hidden_in = tokens[...].astype(jnp.float32)
    unit_rows = hidden_in * inverse_rms(hidden_in)
    blocks = width // WIDE
    firsts = []
    for j in range(blocks):
        if j + 1 < blocks:
            for copy in fetch(j + 1):
                copy.start()
        finish(fetch(j))
        columns = slice(j * WIDE, (j + 1) * WIDE)
        block = matmul_nt(conv_grad[...], in_buf[j % 2, 0]) + matmul_nt(
            gate_grad[...], in_buf[j % 2, 1]
        )
        normed_part[:, columns] = block.astype(normed_part.dtype)
        firsts.append(line.begin(j))
        gain_grad = jnp.sum(block * unit_rows[:, columns], 0, keepdims=True)
        if j:
            line.pass_on(j - 1, firsts[j - 1])
        row, at = divmod(j * WIDE, inner)
        row += SMALL_ROWS - GAIN_ROWS + 8
        vectors_own[row : row + 1, at : at + WIDE] = gain_grad
    layer_out[:, : width // 2] = layer_first[...]
    rows_of(layer_last, tp.me, tp.count)[...] = layer_rows[...]
    layer_spread.begin()
    small[:SMALL_ROWS, :] = vectors_own[...].astype(small.dtype)
    small[SMALL_ROWS : SMALL_ROWS + rank, :] = matmul_tn(step_low[...], pre_low[...]).astype(
        small.dtype
    )
    selected = select_sum.shape[0]
    small[SMALL_ROWS + rank : SMALL_ROWS + rank + selected, :] = matmul_tn(
        select_low[...], scan_in[...]
    )[:selected].astype(small.dtype)
    small_total.begin()
    line.pass_on(blocks - 1, firsts[-1])

    def flat(at):
        return lambda block: matmul_tn(cols[at], block)

    def tall(at):
        return lambda block: matmul_tn(block, cols[at])

    def side_by_side(ref, first):
        per = ref.shape[2] // WIDE

        def target(j):
            at = j - first
            columns = pl.ds(pl.multiple_of(lax.rem(at, per) * WIDE, WIDE), WIDE)
            return ref.at[lax.div(at, per), :, columns]

        return target

    def one_above_other(ref):
        return lambda j: ref.at[pl.ds(pl.multiple_of(j * WIDE, WIDE), WIDE), :]

    wide = (block_buf, block_sem, wide_buf, wide_sem)
    high = (block_buf, block_sem, tall_buf, tall_sem)
    down_end = hidden // WIDE
    gu_end = 3 * hidden // WIDE
    finish(loads)
    gu_middle = (down_end + gu_end) // 2
    to_gateup = side_by_side(grad_gateup, down_end)
    products(ffn_all, 0, down_end, tall(2), one_above_other(grad_downproj), *high)
    gather.relay()
    small_total.add_pair()
    products(ffn_all, down_end, gu_middle, flat(1), to_gateup, *wide)
    hidden_in = tp.own(tokens)[...].astype(jnp.float32)
    tp.own(tokens_grad)[...] = (
        middle_grad[...]
        + norm_back(
            line.total(),
            hidden_in,
            inverse_rms(hidden_in),
            gain_row[...].astype(jnp.float32),
        )
    ).astype(tokens_grad.dtype)
    tokens_spread.begin()
    layer_spread.pass_on()
    gather.hand_over()
    small_total.add_all()
    if swaps:
        swap.begin()
    products(ffn_all, gu_middle, gu_end, flat(1), to_gateup, *wide)
    tokens_spread.pass_on()
    gather.hand_over_last()
    small_total.hand_over()
    gather.end()
    products(mix_all, 0, 2 * inner // WIDE, flat(0), side_by_side(grad_inproj, 0), *wide)
    small_total.end()
    gain_own[...] = small_sum[SMALL_ROWS - GAIN_ROWS : SMALL_ROWS, :].astype(jnp.float32)
    gain_sent = [tp.one(gain_own, gain_slots.at[hop], 0, hop) for hop in range(tp.count - 1)]
    vectors_sum[...] = small_sum[:SMALL_ROWS, :].astype(jnp.float32)
    step_sum[...] = small_sum[SMALL_ROWS : SMALL_ROWS + rank, :].astype(jnp.float32)
    select_sum[...] = small_sum[SMALL_ROWS + rank : SMALL_ROWS + rank + selected, :].astype(
        jnp.float32
    )
    if swaps:
        swap.end()
    products(gated_all, 0, inner // WIDE, tall(3), one_above_other(grad_outproj), *high)
    finish(gain_sent)
    total = gain_own[...]
    for hop in range(tp.count - 1):
        total = total + gain_slots[hop]
    gains[...] = total
    tokens_spread.end()
    layer_spread.end()


def run_tail(
    call_id,
    selected,
    swaps,
    conv_grad,
    gate_grad,
    vectors,
    layer_first,
    layer_rows,
    middle_low,
    step_low,
    pre_low,
    select_low,
    scan_in,
    tokens,
    middle_grad,
    gain_row,
    in_conv,
    in_gate,
    one_cols,
    two_cols,
    ct_cols,
    middle_cols,
    ffn_all,
    gated_all,
):
    rows, inner = conv_grad.shape
    rank = step_low.shape[1]
    hidden = ffn_all.shape[1] // 3
    width = tokens.shape[1]
    share = one_cols.shape[1]
    all_rows = ffn_all.shape[0]
    tp_count, plane_count = group_size(("tp",)), group_size(PLANE)
    low, full = jnp.bfloat16, jnp.float32
    vmem = pl.BlockSpec(memory_space=pltpu.VMEM)
    hbm = pl.BlockSpec(memory_space=pltpu.HBM)
    dma = pltpu.SemaphoreType.DMA
    small_rows = SMALL_ROWS + rank + selected
    small = jax.ShapeDtypeStruct((small_rows + -small_rows % (16 * plane_count), inner), low)
    part = jax.ShapeDtypeStruct((rows, width), low)
    return pl.pallas_call(
        functools.partial(tail_kernel, swaps),
        in_specs=[vmem] * 18 + [hbm] * 8,
        out_specs=[vmem] * 6 + [hbm] * 5,
        out_shape=[
            jax.ShapeDtypeStruct(tokens.shape, low),
            jax.ShapeDtypeStruct(tokens.shape, low),
            jax.ShapeDtypeStruct((SMALL_ROWS, inner), full),
            jax.ShapeDtypeStruct((rank, inner), full),
            jax.ShapeDtypeStruct((selected, inner), full),
            jax.ShapeDtypeStruct((GAIN_ROWS, inner), full),
            jax.ShapeDtypeStruct((all_rows, 2 * inner), low),
            jax.ShapeDtypeStruct((2, share, inner), full),
            jax.ShapeDtypeStruct((inner, share), full),
            jax.ShapeDtypeStruct((2, share, hidden), full),
            jax.ShapeDtypeStruct((hidden, share), full),
        ],
        scratch_shapes=[
            pltpu.VMEM((rows, 2 * inner), low),
            pltpu.VMEM(part.shape, low),
            pltpu.VMEM(small.shape, low),
            pltpu.VMEM(small.shape, low),
            pltpu.VMEM((tp_count - 1, GAIN_ROWS, inner), full),
            pltpu.VMEM((GAIN_ROWS, inner), full),
            pltpu.VMEM((SMALL_ROWS, inner), full),
            pltpu.VMEM((4, all_rows, share), low),
            pltpu.VMEM((2, 2, WIDE, inner), low),
            pltpu.VMEM((2, all_rows, WIDE), low),
            pltpu.VMEM((2, share, WIDE), full),
            pltpu.VMEM((2, WIDE, share), full),
            dma((4,)),
            dma((2, 2)),
            dma((2,)),
            dma((2,)),
            dma((2,)),
            dma((1, tp_count - 1)),
            dma((1, tp_count - 1)),
        ]
        + gather_scratch()
        + line_sum_scratch(part, width // WIDE)
        + line_spread_scratch() * 2
        + plane_sum_scratch(small)
        + (swap_scratch([tokens]) if swaps else []),
        compiler_params=pltpu.CompilerParams(
            collective_id=call_id, has_side_effects=True, vmem_limit_bytes=VMEM_GRANT
        ),
    )(
        conv_grad,
        gate_grad,
        *vectors,
        layer_first,
        layer_rows,
        middle_low,
        step_low,
        pre_low,
        select_low,
        scan_in,
        tokens,
        middle_grad,
        gain_row,
        in_conv,
        in_gate,
        one_cols,
        two_cols,
        ct_cols,
        middle_cols,
        ffn_all,
        gated_all,
    )


BORDER = 16


def head_kernel(
    tokens,
    gain,
    in_conv,
    in_gate,
    conv_in,
    gate_mix,
    border,
    conv_all,
    gate_all,
    normed,
    block_buf,
    block_sem,
    border_send,
    border_recv,
    *sems,
):
    place, places = lax.axis_index("ctx"), lax.axis_size("ctx")
    seqs = border.shape[0] // BORDER
    span = conv_in.shape[0] // seqs

    def to_next(seq):
        return send_on(
            conv_in.at[pl.ds((seq + 1) * span - BORDER, BORDER), :],
            border.at[pl.ds(seq * BORDER, BORDER), :],
            border_send.at[seq],
            border_recv.at[seq],
            place + 1,
        )

    conv = PlaneGather(in_conv, conv_all, *sems[:2])
    gate = PlaneGather(in_gate, gate_all, *sems[3:5])
    greet([(PLANE, conv.others)])
    conv.begin(sems[2])
    gate.begin(sems[5])
    hidden_in = tokens[...].astype(jnp.float32)
    normed[...] = (hidden_in * inverse_rms(hidden_in) * gain[...].astype(jnp.float32)).astype(
        normed.dtype
    )
    conv.relay()
    conv.hand_over()
    gate.relay()
    conv.hand_over_last()
    gate.hand_over()
    conv.end()
    product_in_blocks(normed, conv_all, conv_in, block_buf, block_sem)

    @pl.when(place == 0)
    def _():
        border[...] = jnp.zeros_like(border)

    @pl.when(place < places - 1)
    def _():
        for seq in range(seqs):
            to_next(seq).start()

    gate.hand_over_last()
    gate.end()
    product_in_blocks(normed, gate_all, gate_mix, block_buf, block_sem)

    @pl.when(place < places - 1)
    def _():
        for seq in range(seqs):
            to_next(seq).wait_send()

    @pl.when(place > 0)
    def _():
        for seq in range(seqs):
            to_next(seq).wait_recv()


def run_head(call_id, tokens, gain, inproj, seqs):
    rows, width = tokens.shape
    inner = inproj.shape[2]
    low = jnp.bfloat16
    vmem = pl.BlockSpec(memory_space=pltpu.VMEM)
    hbm = pl.BlockSpec(memory_space=pltpu.HBM)
    return pl.pallas_call(
        head_kernel,
        in_specs=[vmem] * 2 + [hbm] * 2,
        out_specs=[vmem] * 3 + [hbm] * 2,
        out_shape=[
            jax.ShapeDtypeStruct((rows, inner), low),
            jax.ShapeDtypeStruct((rows, inner), jnp.float32),
            jax.ShapeDtypeStruct((seqs * BORDER, inner), low),
            jax.ShapeDtypeStruct((width, inner), low),
            jax.ShapeDtypeStruct((width, inner), low),
        ],
        scratch_shapes=[
            pltpu.VMEM((rows, width), low),
            pltpu.VMEM((2, width, WIDE), low),
            pltpu.SemaphoreType.DMA((2,)),
            pltpu.SemaphoreType.DMA((seqs,)),
            pltpu.SemaphoreType.DMA((seqs,)),
        ]
        + gather_scratch() * 2,
        compiler_params=pltpu.CompilerParams(
            collective_id=call_id, has_side_effects=True, vmem_limit_bytes=VMEM_GRANT
        ),
    )(tokens, gain, inproj[0], inproj[1])


def per_device(
    tokens,
    mixgain,
    inproj,
    convkern,
    convbias,
    selproj,
    stepproj,
    stepbias,
    decaylog,
    skipgain,
    outproj,
    ffngain,
    gateup,
    downproj,
    cotangent,
):
    seqs, span, width = tokens.shape
    rows = seqs * span
    taps, inner = convkern.shape
    rank = stepproj.shape[0]
    n_state = decaylog.shape[1]
    tiles = inner // LANE
    gain_mix = mixgain.astype(jnp.float32)
    kernel = convkern.astype(jnp.float32)
    kernel_bias = convbias.astype(jnp.float32)
    step_bias = stepbias.astype(jnp.float32)
    skip_weight = skipgain.astype(jnp.float32)
    decay_rate = -jnp.exp(jnp.transpose(decaylog.astype(jnp.float32)))
    rate = (decay_rate * LOG2E).reshape(n_state, tiles, LANE)

    gain_mix_row, gain_ffn_row = mixgain.reshape(1, width), ffngain.reshape(1, width)
    low = jnp.bfloat16

    tokens_rows = tokens.reshape(rows, width)
    ct_low = cotangent.reshape(rows, width)
    swap_now = swaps_in_kernels(width)
    out_first = gathered_rows(outproj[: inner // 2])
    ffn_pack = gathered_rows(
        jnp.concatenate([gateup[0], gateup[1], jnp.transpose(downproj)], 1)
    )
    conv_in, gate_mix, border, in_conv, in_gate = run_head(
        5, tokens_rows, gain_mix_row, inproj, seqs
    )
    hidden_in = tokens_rows.astype(jnp.float32)
    scale_one = inverse_rms(hidden_in)
    normed_one = (hidden_in * scale_one * gain_mix).astype(low)

    conv_seqs = conv_in.reshape(seqs, span, inner)
    rim_rows = border.reshape(seqs, BORDER, inner)[:, BORDER - (taps - 1) :]
    padded_in = jnp.concatenate([rim_rows, conv_seqs], 1).astype(jnp.float32)
    conv_out = kernel_bias[None, None]
    for offset in range(taps):
        conv_out = conv_out + kernel[offset][None, None] * padded_in[:, offset : offset + span]
    conv_out = conv_out.reshape(rows, inner)
    scan_in = jax.nn.silu(conv_out).astype(low)
    scan_float = scan_in.astype(jnp.float32)
    columns = selproj.shape[1]
    select_width = -(-columns // LANE) * LANE
    select_weights = jnp.pad(selproj, ((0, 0), (0, select_width - columns)))
    select_cols = run_select(0, matmul(scan_in, select_weights))

    def columns_of(swapped, array):
        if not swapped:
            return swapped_columns(array)
        return swapped[0].reshape(-1, swapped[0].shape[-1])

    step_low = select_cols[:, :rank].astype(low)
    b_rows = select_cols[:, rank : rank + n_state].reshape(-1)
    c_rows = select_cols[:, rank + n_state : columns].reshape(-1)
    step_pre = matmul(step_low, stepproj) + step_bias[None]
    step_size = jax.nn.softplus(step_pre)
    in_pairs = lax.axis_size("ctx") == 2
    if in_pairs:
        prior, scan_out, out_last = scan_forward_pair(
            6,
            step_size,
            scan_float,
            b_rows,
            c_rows,
            rate,
            seqs,
            outproj[inner // 2 :],
        )
    else:
        span_decay = jnp.exp(
            decay_rate[None] * jnp.sum(step_size.reshape(seqs, span, inner), 1)[:, None]
        ).reshape(seqs, n_state, tiles, LANE)
        ends = scan_ends(step_size, scan_float, b_rows, rate, seqs, False)
        start = from_earlier(ends, span_decay, 1)
        prior, scan_out = scan_forward(start, step_size, scan_float, b_rows, c_rows, rate, seqs)
        out_last = gathered_rows(outproj[inner // 2 :])
    mixer_core = scan_out + skip_weight[None] * scan_float
    gate_sig = jax.nn.silu(gate_mix)
    gated = (mixer_core * gate_sig).astype(low)
    normed_two, middle, gated_all, *swapped = mixer_out(
        1,
        gated,
        out_first,
        out_last,
        tokens_rows,
        gain_ffn_row,
        [normed_one] if swap_now else [],
    )
    normed_one_cols = columns_of(swapped, normed_one)
    made, *swapped = run_ffn(8, normed_two, ct_low, ffn_pack, swap_now)
    ct_cols = columns_of(swapped, ct_low)
    ffn_all = gathered_rows(made)
    middle_low, middle_grad, ffngain_part, gated_grad, ffn_part, *swapped = ffn_back(
        2,
        made,
        ct_low,
        middle,
        gain_ffn_row,
        out_first,
        out_last,
        ffn_pack,
        [normed_two] if swap_now else [],
    )
    normed_two_cols = columns_of(swapped, normed_two)
    core_grad = gated_grad * gate_sig
    gate_mix_grad = (gated_grad * mixer_core * silu_slope(gate_mix)).astype(low)
    grad_skipgain = jnp.sum(core_grad * scan_float, 0)
    if in_pairs:
        step_grad, input_grad, rate_grad, parts, *layer_rows = scan_backward_pair(
            7,
            prior,
            step_size,
            scan_float,
            core_grad,
            b_rows,
            c_rows,
            rate,
            seqs,
            ffn_part,
            middle,
            [],
        )
    else:
        back_ends = scan_ends(step_size, core_grad, c_rows, rate, seqs, True)
        end_grad = from_earlier(back_ends, span_decay, -1)
        step_grad, input_grad, rate_grad, parts = scan_backward(
            end_grad, prior, step_size, scan_float, core_grad, b_rows, c_rows, rate, seqs
        )
        ffn_sum = lax.psum_scatter(ffn_part, "tp", scatter_dimension=0, tiled=True)
        layer_rows = jnp.split((middle + ffn_sum.astype(jnp.float32)).astype(low), 2, 1)
    grad_decaylog = rate_grad.reshape(n_state, inner) * decay_rate
    pre_grad = step_grad * jax.nn.sigmoid(step_pre)
    grad_stepbias = jnp.sum(pre_grad, 0)
    pre_low = pre_grad.astype(low)
    select_part = jnp.concatenate(
        [
            matmul_nt(pre_low, stepproj),
            jnp.sum(parts, -1),
            jnp.zeros((rows, select_width - columns), jnp.float32),
        ],
        1,
    ).astype(low)
    select_low, layer_first = sum_over_tp(3, select_part, layer_rows[0])
    scan_in_grad = (
        core_grad * skip_weight[None]
        + input_grad
        + matmul_nt(select_low, select_weights)
    )
    conv_grad = scan_in_grad * silu_slope(conv_out)
    grad_convbias = jnp.sum(conv_grad, 0)
    conv_grad_seqs = conv_grad.reshape(seqs, span, inner)
    padded_grad = jnp.zeros(padded_in.shape, jnp.float32)
    kernel_rows = []
    for offset in range(taps):
        kernel_rows.append(jnp.sum(conv_grad_seqs * padded_in[:, offset : offset + span], (0, 1)))
        padded_grad = padded_grad + jnp.pad(
            kernel[offset][None, None] * conv_grad_seqs,
            ((0, 0), (offset, taps - 1 - offset), (0, 0)),
        )
    grad_convkern = jnp.stack(kernel_rows)
    returned = passed_along(padded_grad[:, : taps - 1], "ctx", -1)
    conv_in_grad = (
        (padded_grad[:, taps - 1 :] + jnp.pad(returned, ((0, 0), (span - taps + 1, 0), (0, 0))))
        .astype(low)
        .reshape(rows, inner)
    )
    vectors = [
        grad_convkern,
        grad_convbias[None],
        grad_stepbias[None],
        grad_decaylog,
        grad_skipgain[None],
        ffngain_part,
    ]
    (
        tokens_grad,
        layer_out,
        vectors,
        grad_stepproj,
        grad_selproj,
        gains,
        _,
        grad_inproj,
        grad_outproj,
        grad_gateup,
        grad_downproj,
    ) = run_tail(
        4,
        columns,
        swap_now,
        conv_in_grad,
        gate_mix_grad,
        vectors,
        layer_first,
        layer_rows[1],
        middle_low,
        step_low,
        pre_low,
        select_low,
        scan_in,
        tokens_rows,
        middle_grad,
        gain_mix_row,
        in_conv,
        in_gate,
        normed_one_cols,
        normed_two_cols,
        ct_cols,
        normed_two_cols if swap_now else swapped_columns(middle_low),
        ffn_all,
        gated_all,
    )
    at = taps + 2
    return (
        layer_out.reshape(tokens.shape),
        tokens_grad.reshape(tokens.shape),
        gains[8:10].reshape(width),
        grad_inproj,
        vectors[:taps],
        vectors[taps],
        jnp.transpose(grad_selproj),
        grad_stepproj,
        vectors[taps + 1],
        jnp.transpose(vectors[at : at + n_state]),
        vectors[at + n_state],
        grad_outproj,
        gains[10:12].reshape(width),
        grad_gateup,
        grad_downproj,
    )


def solution(mesh):
    in_specs = (
        P("dp", "ctx", None),
        P(),
        P(None, ("dp", "ctx"), "tp"),
        P(None, "tp"),
        P("tp"),
        P("tp", None),
        P(None, "tp"),
        P("tp"),
        P("tp", None),
        P("tp"),
        P("tp", ("dp", "ctx")),
        P(),
        P(None, ("dp", "ctx"), "tp"),
        P("tp", ("dp", "ctx")),
        P("dp", "ctx", None),
    )
    out_specs = (
        P("dp", "ctx", None),
        P("dp", "ctx", None),
        P(),
        P(None, ("dp", "ctx"), "tp"),
        P(None, "tp"),
        P("tp"),
        P("tp", None),
        P(None, "tp"),
        P("tp"),
        P("tp", None),
        P("tp"),
        P("tp", ("dp", "ctx")),
        P(),
        P(None, ("dp", "ctx"), "tp"),
        P("tp", ("dp", "ctx")),
    )
    return jax.shard_map(
        per_device, mesh=mesh, in_specs=in_specs, out_specs=out_specs, check_vma=False
    )
```

```python
import functools
import math

import jax
import jax.numpy as jnp
from jax import lax
from jax.experimental import pallas as pl
from jax.experimental.pallas import tpu as pltpu
from jax.sharding import PartitionSpec as P

EPSILON = 1e-05
LOG2E = math.log2(math.e)
LN2 = math.log(2.0)
SUB = 8
LANE = 128
VMEM_GRANT = 60 * 2**20
PLANE = ("dp", "ctx")


def passed_along(value, axis, steps):
    count = lax.axis_size(axis)
    first, last = (max(0, -steps), min(count, count - steps))
    return lax.ppermute(value, axis, [(source, source + steps) for source in range(first, last)])


def matmul(left, right):
    return jnp.dot(left, right, preferred_element_type=jnp.float32)


def matmul_nt(left, right):
    return lax.dot_general(
        left, right, (((1,), (1,)), ((), ())), preferred_element_type=jnp.float32
    )


def matmul_tn(left, right):
    return lax.dot_general(
        left, right, (((0,), (0,)), ((), ())), preferred_element_type=jnp.float32
    )


def inverse_rms(values):
    return lax.rsqrt(jnp.mean(values * values, -1, keepdims=True) + EPSILON)


def silu_slope(values):
    logistic = jax.nn.sigmoid(values)
    return logistic * (1.0 + values * (1.0 - logistic))


def norm_back(grad_norm, values, scale, gain):
    scaled_grad = grad_norm * gain
    unit_rows = values * scale
    return scale * (scaled_grad - unit_rows * jnp.mean(scaled_grad * unit_rows, -1, keepdims=True))


def stage_in(ref, group, held):
    for tile in range(held.shape[0] // SUB):
        held[pl.ds(tile * SUB, SUB), :] = ref[
            pl.ds(pl.multiple_of(group * SUB, SUB), SUB), pl.ds(tile * LANE, LANE)
        ]


def stage_out(held, ref, group):
    for tile in range(held.shape[0] // SUB):
        ref[pl.ds(pl.multiple_of(group * SUB, SUB), SUB), pl.ds(tile * LANE, LANE)] = held[
            pl.ds(tile * SUB, SUB), :
        ]


def token_row(held, at, tiles):
    return held[pl.ds(at, tiles, stride=SUB), :]


def ends_kernel(
    n_state,
    tiles,
    groups,
    reverse,
    step_ref,
    drive_ref,
    rows_ref,
    rate_ref,
    end_ref,
    step_held,
    drive_held,
):
    base = pl.program_id(0) * groups * SUB * n_state
    rates = [rate_ref[n] for n in range(n_state)]

    def one(turn, states):
        group = groups - 1 - turn if reverse else turn
        order = range(SUB - 1, -1, -1) if reverse else range(SUB)
        states = list(states)
        stage_in(step_ref, group, step_held)
        stage_in(drive_ref, group, drive_held)
        for at in order:
            step = token_row(step_held, at, tiles)
            drive = token_row(drive_held, at, tiles)
            if not reverse:
                drive = drive * step
            for n in range(n_state):
                row = rows_ref[base + (group * SUB + at) * n_state + n]
                decay = jnp.exp2(step * rates[n])
                if reverse:
                    states[n] = decay * (states[n] + drive * row)
                else:
                    states[n] = decay * states[n] + drive * row
        return tuple(states)

    zero = jnp.zeros((tiles, LANE), jnp.float32)
    states = lax.fori_loop(0, groups, one, (zero,) * n_state)
    for n in range(n_state):
        end_ref[0, n] = states[n]


def scan_ends(step, drive, rows, rate, seqs, reverse):
    n_state, tiles, _ = rate.shape
    groups = step.shape[0] // seqs // SUB
    rows_spec = pl.BlockSpec((groups * SUB, tiles * LANE), lambda s: (s, 0))
    held = pltpu.VMEM((tiles * SUB, LANE), jnp.float32)
    return pl.pallas_call(
        functools.partial(ends_kernel, n_state, tiles, groups, reverse),
        grid=(seqs,),
        in_specs=[
            rows_spec,
            rows_spec,
            pl.BlockSpec(memory_space=pltpu.SMEM),
            pl.BlockSpec((n_state, tiles, LANE), lambda s: (0, 0, 0)),
        ],
        out_specs=pl.BlockSpec((1, n_state, tiles, LANE), lambda s: (s, 0, 0, 0)),
        out_shape=jax.ShapeDtypeStruct((seqs, n_state, tiles, LANE), jnp.float32),
        scratch_shapes=[held, held],
        compiler_params=pltpu.CompilerParams(vmem_limit_bytes=VMEM_GRANT),
    )(step, drive, rows, rate)


def forward_kernel(
    n_state,
    tiles,
    groups,
    blocks,
    start_ref,
    step_ref,
    input_ref,
    brow_ref,
    crow_ref,
    rate_ref,
    prior_ref,
    mixed_ref,
    carried,
    step_held,
    input_held,
    mixed_held,
):
    base = (pl.program_id(0) * blocks + pl.program_id(1)) * groups * SUB * n_state

    @pl.when(pl.program_id(1) == 0)
    def _():
        carried[...] = start_ref[0]

    def one(group, states):
        states = list(states)
        stage_in(step_ref, group, step_held)
        stage_in(input_ref, group, input_held)
        for at in range(SUB):
            step = token_row(step_held, at, tiles)
            drive = step * token_row(input_held, at, tiles)
            mixed = [None] * 2
            for n in range(n_state):
                where = base + (group * SUB + at) * n_state + n
                prior_ref[group * SUB + at, n] = states[n]
                decay = jnp.exp2(step * rate_ref[n])
                states[n] = decay * states[n] + drive * brow_ref[where]
                term = states[n] * crow_ref[where]
                mixed[n % 2] = term if mixed[n % 2] is None else mixed[n % 2] + term
            mixed_held[pl.ds(at, tiles, stride=SUB), :] = mixed[0] + mixed[1]
        stage_out(mixed_held, mixed_ref, group)
        return tuple(states)

    states = lax.fori_loop(0, groups, one, tuple(carried[n] for n in range(n_state)))
    for n in range(n_state):
        carried[n] = states[n]


def scan_forward(start, step, inputs, b_rows, c_rows, rate, seqs):
    n_state, tiles, _ = rate.shape
    all_groups = step.shape[0] // SUB
    groups = math.gcd(all_groups // seqs, 4)
    blocks = all_groups // seqs // groups
    rows_spec = pl.BlockSpec((groups * SUB, tiles * LANE), lambda s, b: (s * blocks + b, 0))
    held = pltpu.VMEM((tiles * SUB, LANE), jnp.float32)
    smem = pl.BlockSpec(memory_space=pltpu.SMEM)
    tokens = all_groups * SUB
    return pl.pallas_call(
        functools.partial(forward_kernel, n_state, tiles, groups, blocks),
        grid=(seqs, blocks),
        in_specs=[
            pl.BlockSpec((1, n_state, tiles, LANE), lambda s, b: (s, 0, 0, 0)),
            rows_spec,
            rows_spec,
            smem,
            smem,
            pl.BlockSpec((n_state, tiles, LANE), lambda s, b: (0, 0, 0)),
        ],
        out_specs=[
            pl.BlockSpec(
                (groups * SUB, n_state, tiles, LANE), lambda s, b: (s * blocks + b, 0, 0, 0)
            ),
            rows_spec,
        ],
        out_shape=[
            jax.ShapeDtypeStruct((tokens, n_state, tiles, LANE), jnp.float32),
            jax.ShapeDtypeStruct(step.shape, jnp.float32),
        ],
        scratch_shapes=[pltpu.VMEM((n_state, tiles, LANE), jnp.float32)] + [held] * 3,
        compiler_params=pltpu.CompilerParams(vmem_limit_bytes=VMEM_GRANT),
    )(start, step, inputs, b_rows, c_rows, rate)


def backward_kernel(
    n_state,
    tiles,
    groups,
    blocks,
    end_ref,
    prior_ref,
    step_ref,
    input_ref,
    ograd_ref,
    brow_ref,
    crow_ref,
    rate_ref,
    picks_ref,
    step_grad_ref,
    input_grad_ref,
    rate_grad_ref,
    part_ref,
    carried,
    step_held,
    input_held,
    ograd_held,
    step_grad_held,
    input_grad_held,
):
    block = blocks - 1 - pl.program_id(1)
    base = (pl.program_id(0) * blocks + block) * groups * SUB * n_state

    @pl.when(pl.program_id(1) == 0)
    def _():
        carried[...] = end_ref[0]

    @pl.when((pl.program_id(0) == 0) & (pl.program_id(1) == 0))
    def _():
        rate_grad_ref[...] = jnp.zeros_like(rate_grad_ref)

    def one(turn, grads):
        group = groups - 1 - turn
        grads = list(grads)
        stage_in(step_ref, group, step_held)
        stage_in(input_ref, group, input_held)
        stage_in(ograd_ref, group, ograd_held)
        for at in range(SUB - 1, -1, -1):
            step = token_row(step_held, at, tiles)
            value = token_row(input_held, at, tiles)
            ograd = token_row(ograd_held, at, tiles)
            drive = step * value
            along_b = None
            along_rate = None
            brow_parts, crow_parts = [], []
            for n in range(n_state):
                where = base + (group * SUB + at) * n_state + n
                brow, crow = brow_ref[where], crow_ref[where]
                rate = rate_ref[n]
                decay = jnp.exp2(step * rate)
                grad = ograd * crow + grads[n]
                kept = decay * prior_ref[group * SUB + at, n]
                state = kept + drive * brow
                decay_term = grad * kept
                grads[n] = decay * grad
                rate_grad_ref[n] += decay_term * step
                by_rate, by_brow = decay_term * rate, grad * brow
                along_rate = by_rate if along_rate is None else along_rate + by_rate
                along_b = by_brow if along_b is None else along_b + by_brow
                brow_parts.append(grad * drive)
                crow_parts.append(ograd * state)
            step_grad_held[pl.ds(at, tiles, stride=SUB), :] = along_rate * LN2 + along_b * value
            input_grad_held[pl.ds(at, tiles, stride=SUB), :] = along_b * step
            parts = jnp.concatenate(brow_parts + crow_parts, 0).astype(jnp.bfloat16)
            part_ref[group * SUB + at] = jnp.dot(
                picks_ref[...], parts, preferred_element_type=jnp.float32
            )
        stage_out(step_grad_held, step_grad_ref, group)
        stage_out(input_grad_held, input_grad_ref, group)
        return tuple(grads)

    grads = lax.fori_loop(0, groups, one, tuple(carried[n] for n in range(n_state)))
    for n in range(n_state):
        carried[n] = grads[n]


def scan_backward(end_grad, prior, step, inputs, ograd, b_rows, c_rows, rate, seqs):
    n_state, tiles, _ = rate.shape
    all_groups = step.shape[0] // SUB
    groups = math.gcd(all_groups // seqs, 4)
    blocks = all_groups // seqs // groups

    def at(s, b):
        return s * blocks + blocks - 1 - b

    rows_spec = pl.BlockSpec((groups * SUB, tiles * LANE), lambda s, b: (at(s, b), 0))
    held = pltpu.VMEM((tiles * SUB, LANE), jnp.float32)
    smem = pl.BlockSpec(memory_space=pltpu.SMEM)
    tokens = all_groups * SUB
    picks = jnp.repeat(jnp.eye(2 * n_state, dtype=jnp.bfloat16), tiles, 1)
    return pl.pallas_call(
        functools.partial(backward_kernel, n_state, tiles, groups, blocks),
        grid=(seqs, blocks),
        in_specs=[
            pl.BlockSpec((1, n_state, tiles, LANE), lambda s, b: (s, 0, 0, 0)),
            pl.BlockSpec((groups * SUB, n_state, tiles, LANE), lambda s, b: (at(s, b), 0, 0, 0)),
            rows_spec,
            rows_spec,
            rows_spec,
            smem,
            smem,
            pl.BlockSpec((n_state, tiles, LANE), lambda s, b: (0, 0, 0)),
            pl.BlockSpec(picks.shape, lambda s, b: (0, 0)),
        ],
        out_specs=[
            rows_spec,
            rows_spec,
            pl.BlockSpec((n_state, tiles, LANE), lambda s, b: (0, 0, 0)),
            pl.BlockSpec((groups * SUB, 2 * n_state, LANE), lambda s, b: (at(s, b), 0, 0)),
        ],
        out_shape=[
            jax.ShapeDtypeStruct(step.shape, jnp.float32),
            jax.ShapeDtypeStruct(step.shape, jnp.float32),
            jax.ShapeDtypeStruct(rate.shape, jnp.float32),
            jax.ShapeDtypeStruct((tokens, 2 * n_state, LANE), jnp.float32),
        ],
        scratch_shapes=[pltpu.VMEM((n_state, tiles, LANE), jnp.float32)] + [held] * 5,
        compiler_params=pltpu.CompilerParams(vmem_limit_bytes=VMEM_GRANT),
    )(end_grad, prior, step, inputs, ograd, b_rows, c_rows, rate, picks)


def from_earlier(ends, decay, steps):
    count = lax.axis_size("ctx")
    if count == 1:
        return jnp.zeros_like(ends)
    if count == 2:
        return passed_along(ends, "ctx", steps)
    index = lax.axis_index("ctx")
    all_ends = lax.all_gather(ends, "ctx")
    all_decays = lax.all_gather(decay, "ctx")

    def one(turn, state):
        at = turn if steps > 0 else count - 1 - turn
        reached = at < index if steps > 0 else at > index
        return jnp.where(reached, all_decays[at] * state + all_ends[at], state)

    return lax.fori_loop(0, count, one, jnp.zeros_like(ends))


def gathered_rows(rows):
    return lax.all_gather(rows, PLANE, axis=0, tiled=True)


def swapped_columns(rows):
    return lax.all_to_all(rows, PLANE, split_axis=1, concat_axis=0, tiled=True)


def place_in(axes):
    index = 0
    for axis in axes:
        index = index * lax.axis_size(axis) + lax.axis_index(axis)
    return index


def device_at(axes, index):
    where = {}
    for axis in reversed(axes):
        size = lax.axis_size(axis)
        where[axis] = lax.rem(index, size)
        index = lax.div(index, size)
    return where


def greet(groups):
    barrier = pltpu.get_barrier_semaphore()
    total = 0
    for axes, others in groups:
        for other in others:
            pl.semaphore_signal(
                barrier,
                inc=1,
                device_id=device_at(axes, other),
                device_id_type=pl.DeviceIdType.MESH,
            )
            total += 1
    pl.semaphore_wait(barrier, total)


def sent(source, target, send_sem, recv_sem, where):
    copy = pltpu.make_async_remote_copy(
        src_ref=source,
        dst_ref=target,
        send_sem=send_sem,
        recv_sem=recv_sem,
        device_id=where,
        device_id_type=pl.DeviceIdType.MESH,
    )
    copy.start()
    return copy


def finish(copies):
    for copy in copies:
        copy.wait()


def rows_of(ref, index, count):
    rows = ref.shape[0] // count
    return ref.at[pl.ds(pl.multiple_of(index * rows, rows), rows), :]


class Group:
    def __init__(self, axes, send_sem, recv_sem):
        self.axes = axes
        self.count = math.prod(lax.axis_size(axis) for axis in axes)
        self.me = place_in(axes)
        self.others = [lax.rem(self.me + hop, self.count) for hop in range(1, self.count)]
        self.send_sem, self.recv_sem = send_sem, recv_sem

    def own(self, ref):
        return rows_of(ref, self.me, self.count)

    def one(self, source, target, which, hop):
        return sent(
            source,
            target,
            self.send_sem.at[which, hop],
            self.recv_sem.at[which, hop],
            device_at(self.axes, self.others[hop]),
        )

    def scatter(self, part, slot, which):
        return [
            self.one(rows_of(part, other, self.count), slot.at[hop], which, hop)
            for hop, other in enumerate(self.others)
        ]

    def total(self, part, slot):
        total = self.own(part)[...].astype(jnp.float32)
        for hop in range(self.count - 1):
            total = total + slot[hop].astype(jnp.float32)
        return total

    def spread(self, ref, which):
        return [self.one(self.own(ref), self.own(ref), which, hop) for hop in range(self.count - 1)]


def slots_for(part, count):
    return pltpu.VMEM((count - 1, part.shape[0] // count) + part.shape[1:], part.dtype)


def group_size(axes):
    return math.prod(lax.axis_size(axis) for axis in axes)


def line_of_four():
    me = lax.axis_index("tp")
    near = me + 1 - 2 * lax.rem(me, 2)
    return me, near, lax.rem(me + 2, 4), lax.rem(near + 2, 4)


class LineSum:
    def __init__(self, part, near_slots, far_slot, passed, send_sem, recv_sem):
        self.part, self.near_slots, self.far_slot = part, near_slots, far_slot
        self.passed, self.send_sem, self.recv_sem = passed, send_sem, recv_sem
        self.me, self.near, self.far, self.cross = line_of_four()
        self.blocks = send_sem.shape[1]
        self.copies = []

    def columns(self, j):
        wide = self.part.shape[1] // self.blocks
        return slice(j * wide, (j + 1) * wide)

    def rows(self, index):
        return rows_of(self.part, index, 4)

    def send(self, source, target, which, j, where):
        copy = sent(
            source.at[:, self.columns(j)],
            target.at[:, self.columns(j)],
            self.send_sem.at[which, j],
            self.recv_sem.at[which, j],
            {"tp": where},
        )
        self.copies.append((which, copy))
        return copy

    def begin(self, j):
        first = self.send(self.rows(self.cross), self.near_slots.at[0], 0, j, self.near)
        self.send(self.rows(self.near), self.near_slots.at[1], 1, j, self.near)
        return first

    def pass_on(self, j, first):
        first.wait_recv()
        columns = self.columns(j)
        self.passed[:, columns] = (
            self.rows(self.far)[:, columns].astype(jnp.float32)
            + self.near_slots[0, :, columns].astype(jnp.float32)
        ).astype(self.passed.dtype)
        self.send(self.passed, self.far_slot, 2, j, self.far)

    def total(self):
        for which, copy in self.copies:
            copy.wait_send()
            if which:
                copy.wait_recv()
        return (
            self.rows(self.me)[...].astype(jnp.float32)
            + self.near_slots[1].astype(jnp.float32)
            + self.far_slot[...].astype(jnp.float32)
        )

    def pass_all(self, firsts):
        for j, first in enumerate(firsts):
            self.pass_on(j, first)


def line_sum_scratch(part, blocks):
    share = (part.shape[0] // 4,) + part.shape[1:]
    sems = pltpu.SemaphoreType.DMA((3, blocks))
    return [
        pltpu.VMEM((2,) + share, part.dtype),
        pltpu.VMEM(share, part.dtype),
        pltpu.VMEM(share, part.dtype),
        sems,
        sems,
    ]


class LineSpread:
    def __init__(self, ref, send_sem, recv_sem):
        self.ref, self.send_sem, self.recv_sem = ref, send_sem, recv_sem
        self.me, self.near, self.far, self.cross = line_of_four()

    def send(self, owner, half, which, where):
        rows = rows_of(self.ref, owner, 4)
        if half is not None:
            wide = self.ref.shape[1] // 2
            rows = rows.at[:, half * wide : (half + 1) * wide]
        return sent(rows, rows, self.send_sem.at[which], self.recv_sem.at[which], {"tp": where})

    def begin(self):
        self.across = [self.send(self.me, half, half, self.far) for half in range(2)]
        self.within = [self.send(self.me, None, 2, self.near)]

    def pass_on(self):
        for half, copy in enumerate(self.across):
            copy.wait_recv()
            self.within.append(self.send(self.far, half, 3 + half, self.near))

    def end(self):
        for copy in self.across:
            copy.wait_send()
        finish(self.within)

    def run(self):
        self.begin()
        self.pass_on()
        self.end()


def line_spread_scratch():
    return [pltpu.SemaphoreType.DMA((5,)), pltpu.SemaphoreType.DMA((5,))]


class Swap:
    def __init__(self, arrays, swapped, send_sem, recv_sem, local_sem):
        plane = Group(PLANE, send_sem, recv_sem)
        self.plane, self.arrays, self.swapped, self.local_sem = plane, arrays, swapped, local_sem

    def begin(self):
        self.copies, plane = [], self.plane
        for which, (array, swapped) in enumerate(zip(self.arrays, self.swapped)):
            share = swapped.shape[1]

            def columns(index):
                return array.at[:, pl.ds(pl.multiple_of(index * share, share), share)]

            for hop, other in enumerate(plane.others):
                self.copies.append(plane.one(columns(other), plane.own(swapped), which, hop))
            local = pltpu.make_async_copy(
                columns(plane.me), plane.own(swapped), self.local_sem.at[which]
            )
            local.start()
            self.copies.append(local)

    def end(self):
        finish(self.copies)


def swap_scratch(arrays):
    sems = pltpu.SemaphoreType.DMA((len(arrays), group_size(PLANE) - 1))
    return [sems, sems, pltpu.SemaphoreType.DMA((len(arrays),))] if arrays else []


def swap_shapes(arrays):
    count = group_size(PLANE)
    return [
        jax.ShapeDtypeStruct((array.shape[0] * count, array.shape[1] // count), array.dtype)
        for array in arrays
    ]


def swaps_in_kernels(width):
    return width // group_size(PLANE) % LANE == 0


def gathered_shape(shard):
    return jax.ShapeDtypeStruct(
        (shard.shape[0] * group_size(PLANE),) + shard.shape[1:], shard.dtype
    )


def gather_scratch():
    return [gather_sems(), gather_sems(), pltpu.SemaphoreType.DMA(())]


def product_in_blocks(left, source, target, block_buf, block_sem):
    columns = range(0, source.shape[1], WIDE)

    def fetch(turn):
        at = columns[turn]
        return pltpu.make_async_copy(
            source.at[:, at : at + WIDE], block_buf.at[turn % 2], block_sem.at[turn % 2]
        )

    fetch(0).start()
    for turn, at in enumerate(columns):
        if turn + 1 < len(columns):
            fetch(turn + 1).start()
        fetch(turn).wait()
        target[:, at : at + WIDE] = matmul(left[...], block_buf[turn % 2]).astype(target.dtype)


def select_kernel(part, total, slots, send_sem, recv_sem):
    group = Group(("tp",), send_sem, recv_sem)
    greet([(("tp",), group.others)])
    finish(group.scatter(part, slots, 0))
    group.own(total)[...] = group.total(part, slots).astype(total.dtype)
    finish(group.spread(total, 1))


def run_select(call_id, part):
    count = group_size(("tp",))
    vmem = pl.BlockSpec(memory_space=pltpu.VMEM)
    sems = pltpu.SemaphoreType.DMA((2, count - 1))
    return pl.pallas_call(
        select_kernel,
        in_specs=[vmem],
        out_specs=vmem,
        out_shape=jax.ShapeDtypeStruct(part.shape, part.dtype),
        scratch_shapes=[slots_for(part, count), sems, sems],
        compiler_params=pltpu.CompilerParams(
            collective_id=call_id, has_side_effects=True, vmem_limit_bytes=VMEM_GRANT
        ),
    )(part)


def sum_kernel(part, own_rows, total, all_rows, slots, send_sem, recv_sem, *line_sems):
    group = Group(("tp",), send_sem, recv_sem)
    rows = LineSpread(all_rows, *line_sems)
    greet([(("tp",), group.others)])
    copies = group.scatter(part, slots, 0)
    group.own(all_rows)[...] = own_rows[...]
    rows.begin()
    finish(copies)
    group.own(total)[...] = group.total(part, slots).astype(total.dtype)
    copies = group.spread(total, 1)
    rows.pass_on()
    finish(copies)
    rows.end()


def sum_over_tp(call_id, part, own_rows):
    count = group_size(("tp",))
    vmem = pl.BlockSpec(memory_space=pltpu.VMEM)
    sems = pltpu.SemaphoreType.DMA((2, count - 1))
    return pl.pallas_call(
        sum_kernel,
        in_specs=[vmem] * 2,
        out_specs=[vmem] * 2,
        out_shape=[
            jax.ShapeDtypeStruct(part.shape, part.dtype),
            jax.ShapeDtypeStruct((own_rows.shape[0] * count, own_rows.shape[1]), own_rows.dtype),
        ],
        scratch_shapes=[slots_for(part, count), sems, sems] + line_spread_scratch(),
        compiler_params=pltpu.CompilerParams(
            collective_id=call_id, has_side_effects=True, vmem_limit_bytes=VMEM_GRANT
        ),
    )(part, own_rows)


def mixer_out_kernel(n_swaps, gated, out_first, out_last, tokens, gain, *refs):
    arrays, refs = refs[:n_swaps], refs[n_swaps:]
    normed, middle, gated_all, *refs = refs
    swapped, refs = refs[:n_swaps], refs[n_swaps:]
    part, refs = refs[0], refs[1:]
    line = LineSum(part, *refs[:5])
    spread = LineSpread(normed, *refs[5:7])
    gather_send, gather_recv, local_sem, *refs = refs[7:]
    group = Group(("tp",), None, None)
    gather = PlaneGather(gated, gated_all, gather_send, gather_recv)
    inner, share = gated.shape[1], out_first.shape[1]
    first = out_first.shape[0] * share // part.shape[1]
    last = inner - first
    greet([(("tp",), group.others), (PLANE, gather.others)])
    gather.begin(local_sem)
    for at in range(out_first.shape[0] // first):
        part[:, at * share : (at + 1) * share] = (
            matmul(gated[:, :first], out_first[at * first : (at + 1) * first, :])
            + matmul(gated[:, first:], out_last[at * last : (at + 1) * last, :])
        ).astype(part.dtype)
    firsts = [line.begin(j) for j in range(line.blocks)]
    if n_swaps:
        swap = Swap(arrays, swapped, *refs)
        swap.begin()
    line.pass_all(firsts)
    rows = group.own(tokens)[...].astype(jnp.float32) + line.total()
    middle[...] = rows
    group.own(normed)[...] = (rows * inverse_rms(rows) * gain[...].astype(jnp.float32)).astype(
        normed.dtype
    )
    spread.begin()
    gather.relay()
    gather.hand_over()
    spread.pass_on()
    spread.end()
    gather.hand_over_last()
    gather.end()
    if n_swaps:
        swap.end()


def mixer_out(call_id, gated, out_first, out_last, tokens, gain, arrays):
    count = group_size(("tp",))
    vmem = pl.BlockSpec(memory_space=pltpu.VMEM)
    hbm = pl.BlockSpec(memory_space=pltpu.HBM)
    rows, width = tokens.shape
    part = jax.ShapeDtypeStruct((rows, width), jnp.bfloat16)
    return pl.pallas_call(
        functools.partial(mixer_out_kernel, len(arrays)),
        in_specs=[vmem] * (5 + len(arrays)),
        out_specs=[vmem] * 2 + [hbm] + [hbm] * len(arrays),
        out_shape=[
            part,
            jax.ShapeDtypeStruct((rows // count, width), jnp.float32),
            gathered_shape(gated),
        ]
        + swap_shapes(arrays),
        scratch_shapes=[pltpu.VMEM(part.shape, part.dtype)]
        + line_sum_scratch(part, 2)
        + line_spread_scratch()
        + gather_scratch()
        + swap_scratch(arrays),
        compiler_params=pltpu.CompilerParams(
            collective_id=call_id, has_side_effects=True, vmem_limit_bytes=VMEM_GRANT
        ),
    )(gated, out_first, out_last, tokens, gain, *arrays)


def ffn_kernel(swaps, normed, ct, weights, made, *refs):
    hidden = weights.shape[1] // 3
    if swaps:
        *swapped, block_buf, block_sem, send_sem, recv_sem, local_sem = refs
        swap = Swap([ct], swapped, send_sem, recv_sem, local_sem)
        greet([(PLANE, swap.plane.others)])
        swap.begin()
    else:
        block_buf, block_sem = refs

    def columns(j, which):
        return pl.ds(pl.multiple_of(which * hidden + j * WIDE, WIDE), WIDE)

    def fetch(j, which):
        slot = lax.rem(j, 2)
        return pltpu.make_async_copy(
            weights.at[:, columns(j, which)],
            block_buf.at[slot, which],
            block_sem.at[slot, which],
        )

    for which in range(3):
        fetch(0, which).start()

    @pl.loop(0, hidden // WIDE)
    def _(j):
        slot = lax.rem(j, 2)

        @pl.when(j + 1 < hidden // WIDE)
        def _():
            for which in range(3):
                fetch(j + 1, which).start()

        fetch(j, 0).wait()
        gate = matmul(normed[...], block_buf[slot, 0])
        fetch(j, 1).wait()
        up = matmul(normed[...], block_buf[slot, 1])
        fetch(j, 2).wait()
        act_grad = matmul(ct[...], block_buf[slot, 2])
        logistic = jax.nn.sigmoid(gate)
        silu = gate * logistic
        slope = logistic * (1.0 + gate * (1.0 - logistic))
        made[:, columns(j, 0)] = (silu * up).astype(made.dtype)
        made[:, columns(j, 1)] = (act_grad * up * slope).astype(made.dtype)
        made[:, columns(j, 2)] = (act_grad * silu).astype(made.dtype)

    if swaps:
        swap.end()


def run_ffn(call_id, normed, ct, weights, swaps):
    rows, width = normed.shape
    arrays = [ct] if swaps else []
    vmem = pl.BlockSpec(memory_space=pltpu.VMEM)
    params = dict(collective_id=call_id, has_side_effects=True) if swaps else {}
    return pl.pallas_call(
        functools.partial(ffn_kernel, swaps),
        in_specs=[vmem, vmem, pl.BlockSpec(memory_space=pltpu.HBM)],
        out_specs=[vmem] + [pl.BlockSpec(memory_space=pltpu.HBM)] * len(arrays),
        out_shape=[jax.ShapeDtypeStruct((rows, weights.shape[1]), jnp.bfloat16)]
        + swap_shapes(arrays),
        scratch_shapes=[
            pltpu.VMEM((2, 3, width, WIDE), jnp.bfloat16),
            pltpu.SemaphoreType.DMA((2, 3)),
        ]
        + swap_scratch(arrays),
        compiler_params=pltpu.CompilerParams(vmem_limit_bytes=VMEM_GRANT, **params),
    )(normed, ct, weights)


def ffn_back_kernel(
    n_swaps,
    made,
    ct,
    middle,
    gain,
    out_first,
    out_last,
    weights,
    *refs,
):
    arrays, refs = refs[:n_swaps], refs[n_swaps:]
    middle_low, middle_grad, gain_grad, gated_grad, ffn_part, *refs = refs
    swapped, refs = refs[:n_swaps], refs[n_swaps:]
    part, wide_buf, down_buf, wide_sem, down_sem, *sems = refs
    hidden = made.shape[1] // 3
    blocks = part.shape[1] // WIDE
    group = Group(("tp",), None, None)
    line = LineSum(part, *sems[:5])
    spread = LineSpread(middle_low, *sems[5:7])
    if n_swaps:
        swap = Swap(arrays, swapped, *sems[7:])
        greet([(("tp",), group.others), (PLANE, swap.plane.others)])
        swap.begin()
    else:
        greet([(("tp",), group.others)])

    def fetch(j):
        return pltpu.make_async_copy(
            weights.at[j * WIDE : (j + 1) * WIDE, : 2 * hidden],
            wide_buf.at[j % 2],
            wide_sem.at[j % 2],
        )

    def fetch_down(j):
        return pltpu.make_async_copy(
            weights.at[j * WIDE : (j + 1) * WIDE, 2 * hidden :],
            down_buf.at[j % 2],
            down_sem.at[j % 2],
        )

    fetch(0).start()
    firsts = []
    for j in range(blocks):
        if j + 1 < blocks:
            fetch(j + 1).start()
        else:
            fetch_down(0).start()
        fetch(j).wait()
        columns = slice(j * WIDE, (j + 1) * WIDE)
        part[:, columns] = matmul_nt(made[:, hidden:], wide_buf[j % 2]).astype(part.dtype)
        firsts.append(line.begin(j))
    for j in range(blocks):
        if j + 1 < blocks:
            fetch_down(j + 1).start()
        fetch_down(j).wait()
        ffn_part[:, j * WIDE : (j + 1) * WIDE] = matmul_nt(
            made[:, :hidden], down_buf[j % 2]
        ).astype(ffn_part.dtype)
        line.pass_on(j, firsts[j])
    normed_grad = line.total()
    rows = middle[...]
    scale = inverse_rms(rows)
    gain_grad[...] = jnp.sum(normed_grad * rows * scale, 0, keepdims=True)
    grad = group.own(ct)[...].astype(jnp.float32) + norm_back(
        normed_grad, rows, scale, gain[...].astype(jnp.float32)
    )
    middle_grad[...] = grad
    group.own(middle_low)[...] = grad.astype(middle_low.dtype)
    spread.run()
    share, at_column = out_first.shape[1], 0
    for shards in (out_first, out_last):
        depth = shards.shape[0] * share // middle_low.shape[1]
        total = None
        for at in range(shards.shape[0] // depth):
            one = matmul_nt(
                middle_low[:, at * share : (at + 1) * share],
                shards[at * depth : (at + 1) * depth, :],
            )
            total = one if total is None else total + one
        gated_grad[:, at_column : at_column + depth] = total
        at_column += depth
    if n_swaps:
        swap.end()


def ffn_back(call_id, made, ct, middle, gain, out_first, out_last, weights, arrays):
    count = group_size(("tp",))
    vmem = pl.BlockSpec(memory_space=pltpu.VMEM)
    hbm = pl.BlockSpec(memory_space=pltpu.HBM)
    rows, width = ct.shape
    hidden = made.shape[1] // 3
    inner = (out_first.shape[0] + out_last.shape[0]) // group_size(PLANE)
    low, full = jnp.bfloat16, jnp.float32
    part = jax.ShapeDtypeStruct((rows, width), low)
    dma = pltpu.SemaphoreType.DMA
    return pl.pallas_call(
        functools.partial(ffn_back_kernel, len(arrays)),
        in_specs=[vmem] * 6 + [hbm] + [vmem] * len(arrays),
        out_specs=[vmem] * 5 + [hbm] * len(arrays),
        out_shape=[
            part,
            jax.ShapeDtypeStruct((rows // count, width), full),
            jax.ShapeDtypeStruct((1, width), full),
            jax.ShapeDtypeStruct((rows, inner), full),
            part,
        ]
        + swap_shapes(arrays),
        scratch_shapes=[
            pltpu.VMEM(part.shape, low),
            pltpu.VMEM((2, WIDE, 2 * hidden), low),
            pltpu.VMEM((2, WIDE, hidden), low),
            dma((2,)),
            dma((2,)),
        ]
        + line_sum_scratch(part, width // WIDE)
        + line_spread_scratch()
        + swap_scratch(arrays),
        compiler_params=pltpu.CompilerParams(
            collective_id=call_id, has_side_effects=True, vmem_limit_bytes=VMEM_GRANT
        ),
    )(made, ct, middle, gain, out_first, out_last, weights, *arrays)


def send_on(source, target, send_sem, recv_sem, ctx):
    return pltpu.make_async_remote_copy(
        src_ref=source,
        dst_ref=target,
        send_sem=send_sem,
        recv_sem=recv_sem,
        device_id={"ctx": ctx},
        device_id_type=pl.DeviceIdType.MESH,
    )


def forward_pair_kernel(
    n_state,
    tiles,
    groups,
    blocks,
    seqs,
    step_ref,
    input_ref,
    brow_ref,
    crow_ref,
    rate_ref,
    shard,
    *refs,
):
    prior_ref, mixed_ref, gathered, *refs = refs
    carried, ends, starts, prior_buf, step_held, input_held, mixed_held, *refs = refs
    prior_sem, send_sem, recv_sem, gather_send, gather_recv, local_sem = refs
    place = lax.axis_index("ctx")
    gather = PlaneGather(shard, gathered, gather_send, gather_recv)
    greet([(PLANE, gather.others)])
    gather.begin(local_sem)

    def hand_on(seq):
        return send_on(ends.at[seq], starts.at[seq], send_sem.at[seq], recv_sem.at[seq], 1)

    def store(block):
        slot = lax.rem(block, 2)
        rows = groups * SUB
        return pltpu.make_async_copy(
            prior_buf.at[slot],
            prior_ref.at[pl.ds(pl.multiple_of(block * rows, rows), rows)],
            prior_sem.at[slot],
        )

    def one_sequence(seq):
        @pl.when(place == 0)
        def _():
            carried[...] = jnp.zeros_like(carried)

        @pl.when(place == 1)
        def _():
            hand_on(seq).wait_recv()
            carried[...] = starts[seq]

        @pl.loop(0, blocks)
        def _(inner_block):
            block = seq * blocks + inner_block
            slot = lax.rem(block, 2)

            @pl.when(block >= 2)
            def _():
                store(block - 2).wait()

            def one(turn, states):
                group = block * groups + turn
                states = list(states)
                stage_in(step_ref, group, step_held)
                stage_in(input_ref, group, input_held)
                for at in range(SUB):
                    step = token_row(step_held, at, tiles)
                    drive = step * token_row(input_held, at, tiles)
                    mixed = [None] * 2
                    for n in range(n_state):
                        where = (group * SUB + at) * n_state + n
                        prior_buf[slot, turn * SUB + at, n] = states[n]
                        decay = jnp.exp2(step * rate_ref[n])
                        states[n] = decay * states[n] + drive * brow_ref[where]
                        term = states[n] * crow_ref[where]
                        mixed[n % 2] = term if mixed[n % 2] is None else mixed[n % 2] + term
                    mixed_held[pl.ds(at, tiles, stride=SUB), :] = mixed[0] + mixed[1]
                stage_out(mixed_held, mixed_ref, group)
                return tuple(states)

            states = lax.fori_loop(0, groups, one, tuple(carried[n] for n in range(n_state)))
            for n in range(n_state):
                carried[n] = states[n]
            store(block).start()

        @pl.when(place == 0)
        def _():
            ends[seq] = carried[...]
            hand_on(seq).start()

    for seq in range(seqs):
        one_sequence(seq)
        if seq == 0:
            gather.relay()
            gather.hand_over()
    gather.hand_over_last()
    for block in range(max(0, seqs * blocks - 2), seqs * blocks):
        store(block).wait()

    @pl.when(place == 0)
    def _():
        for seq in range(seqs):
            hand_on(seq).wait_send()

    gather.end()


def scan_forward_pair(
    call_id, step, inputs, b_rows, c_rows, rate, seqs, shard
):
    n_state, tiles, _ = rate.shape
    tokens, inner = step.shape
    all_groups = tokens // SUB
    groups = math.gcd(all_groups // seqs, 4)
    blocks = all_groups // seqs // groups
    vmem = pl.BlockSpec(memory_space=pltpu.VMEM)
    smem = pl.BlockSpec(memory_space=pltpu.SMEM)
    hbm = pl.BlockSpec(memory_space=pltpu.HBM)
    full = jnp.float32
    held = pltpu.VMEM((tiles * SUB, LANE), full)
    boundary = pltpu.VMEM((seqs, n_state, tiles, LANE), full)
    dma = pltpu.SemaphoreType.DMA
    return pl.pallas_call(
        functools.partial(
            forward_pair_kernel, n_state, tiles, groups, blocks, seqs
        ),
        in_specs=[vmem, vmem, smem, smem, vmem, hbm],
        out_specs=[hbm, vmem, hbm],
        out_shape=[
            jax.ShapeDtypeStruct((tokens, n_state, tiles, LANE), full),
            jax.ShapeDtypeStruct(step.shape, full),
            gathered_shape(shard),
        ],
        scratch_shapes=[
            pltpu.VMEM((n_state, tiles, LANE), full),
            boundary,
            boundary,
            pltpu.VMEM((2, groups * SUB, n_state, tiles, LANE), full),
            held,
            held,
            held,
            dma((2,)),
            dma((seqs,)),
            dma((seqs,)),
        ]
        + gather_scratch(),
        compiler_params=pltpu.CompilerParams(
            collective_id=call_id, has_side_effects=True, vmem_limit_bytes=VMEM_GRANT
        ),
    )(step, inputs, b_rows, c_rows, rate, shard)


def backward_pair_kernel(
    n_swaps,
    n_state,
    tiles,
    groups,
    blocks,
    seqs,
    step_ref,
    input_ref,
    ograd_ref,
    brow_ref,
    crow_ref,
    rate_ref,
    picks_ref,
    ffn_part,
    middle,
    prior_ref,
    *refs,
):
    arrays, refs = refs[:n_swaps], refs[n_swaps:]
    step_grad_ref, input_grad_ref, rate_grad_ref, part_ref, *refs = refs
    layer_first, layer_last, *refs = refs
    swapped, refs = refs[:n_swaps], refs[n_swaps:]
    carried, ends, starts, prior_buf, step_held, input_held, ograd_held, *refs = refs
    step_grad_held, input_grad_held, ffn_slots, prior_sem, send_sem, recv_sem, *refs = refs
    tp_send, tp_recv, *refs = refs
    place = lax.axis_index("ctx")
    tp = Group(("tp",), tp_send, tp_recv)
    if n_swaps:
        swap = Swap(arrays, swapped, *refs)
        greet([(PLANE, swap.plane.others), (("tp",), tp.others)])
        swap.begin()
    else:
        greet([(("ctx",), [1 - place]), (("tp",), tp.others)])
    ffn_sent = tp.scatter(ffn_part, ffn_slots, 0)

    def hand_on(seq):
        return send_on(ends.at[seq], starts.at[seq], send_sem.at[seq], recv_sem.at[seq], 0)

    def fetch(turn):
        seq = lax.div(turn, blocks)
        block = seq * blocks + blocks - 1 - lax.rem(turn, blocks)
        slot = lax.rem(turn, 2)
        rows = groups * SUB
        return pltpu.make_async_copy(
            prior_ref.at[pl.ds(pl.multiple_of(block * rows, rows), rows)],
            prior_buf.at[slot],
            prior_sem.at[slot],
        )

    fetch(0).start()
    rate_grad_ref[...] = jnp.zeros_like(rate_grad_ref)

    @pl.when(place == 1)
    def _():
        @pl.loop(0, seqs)
        def _(seq):
            def one(turn, grads):
                group = (seq + 1) * blocks * groups - 1 - turn
                grads = list(grads)
                stage_in(step_ref, group, step_held)
                stage_in(ograd_ref, group, ograd_held)
                for at in range(SUB - 1, -1, -1):
                    step = token_row(step_held, at, tiles)
                    ograd = token_row(ograd_held, at, tiles)
                    for n in range(n_state):
                        row = crow_ref[(group * SUB + at) * n_state + n]
                        grads[n] = jnp.exp2(step * rate_ref[n]) * (grads[n] + ograd * row)
                return tuple(grads)

            zero = jnp.zeros((tiles, LANE), jnp.float32)
            grads = lax.fori_loop(0, blocks * groups, one, (zero,) * n_state)
            for n in range(n_state):
                ends[seq, n] = grads[n]
            hand_on(seq).start()

    @pl.loop(0, seqs)
    def _(seq):
        @pl.when(place == 1)
        def _():
            carried[...] = jnp.zeros_like(carried)

        @pl.when(place == 0)
        def _():
            hand_on(seq).wait_recv()
            carried[...] = starts[seq]

        @pl.loop(0, blocks)
        def _(inner_block):
            turn = seq * blocks + inner_block
            slot = lax.rem(turn, 2)
            first_group = (seq * blocks + blocks - 1 - inner_block) * groups

            @pl.when(turn + 1 < seqs * blocks)
            def _():
                fetch(turn + 1).start()

            fetch(turn).wait()

            def one(back, grads):
                inner_group = groups - 1 - back
                group = first_group + inner_group
                grads = list(grads)
                stage_in(step_ref, group, step_held)
                stage_in(input_ref, group, input_held)
                stage_in(ograd_ref, group, ograd_held)
                for at in range(SUB - 1, -1, -1):
                    step = token_row(step_held, at, tiles)
                    value = token_row(input_held, at, tiles)
                    ograd = token_row(ograd_held, at, tiles)
                    drive = step * value
                    along_b = None
                    along_rate = None
                    brow_parts, crow_parts = [], []
                    for n in range(n_state):
                        where = (group * SUB + at) * n_state + n
                        brow, crow = brow_ref[where], crow_ref[where]
                        rate = rate_ref[n]
                        decay = jnp.exp2(step * rate)
                        grad = ograd * crow + grads[n]
                        kept = decay * prior_buf[slot, inner_group * SUB + at, n]
                        state = kept + drive * brow
                        decay_term = grad * kept
                        grads[n] = decay * grad
                        rate_grad_ref[n] += decay_term * step
                        by_rate, by_brow = decay_term * rate, grad * brow
                        along_rate = by_rate if along_rate is None else along_rate + by_rate
                        along_b = by_brow if along_b is None else along_b + by_brow
                        brow_parts.append(grad * drive)
                        crow_parts.append(ograd * state)
                    step_grad_held[pl.ds(at, tiles, stride=SUB), :] = (
                        along_rate * LN2 + along_b * value
                    )
                    input_grad_held[pl.ds(at, tiles, stride=SUB), :] = along_b * step
                    parts = jnp.concatenate(brow_parts + crow_parts, 0).astype(jnp.bfloat16)
                    part_ref[group * SUB + at] = jnp.dot(
                        picks_ref[...], parts, preferred_element_type=jnp.float32
                    )
                stage_out(step_grad_held, step_grad_ref, group)
                stage_out(input_grad_held, input_grad_ref, group)
                return tuple(grads)

            grads = lax.fori_loop(0, groups, one, tuple(carried[n] for n in range(n_state)))
            for n in range(n_state):
                carried[n] = grads[n]

    finish(ffn_sent)
    layer_rows = (middle[...] + tp.total(ffn_part, ffn_slots)).astype(layer_first.dtype)
    half = layer_first.shape[1]
    layer_first[...], layer_last[...] = layer_rows[:, :half], layer_rows[:, half:]

    @pl.when(place == 1)
    def _():
        @pl.loop(0, seqs)
        def _(seq):
            hand_on(seq).wait_send()

    if n_swaps:
        swap.end()


def scan_backward_pair(
    call_id, prior, step, inputs, ograd, b_rows, c_rows, rate, seqs, ffn_part, middle, arrays
):
    n_state, tiles, _ = rate.shape
    tokens, inner = step.shape
    all_groups = tokens // SUB
    groups = math.gcd(all_groups // seqs, 4)
    blocks = all_groups // seqs // groups
    tp_count = group_size(("tp",))
    vmem = pl.BlockSpec(memory_space=pltpu.VMEM)
    smem = pl.BlockSpec(memory_space=pltpu.SMEM)
    hbm = pl.BlockSpec(memory_space=pltpu.HBM)
    full = jnp.float32
    held = pltpu.VMEM((tiles * SUB, LANE), full)
    boundary = pltpu.VMEM((seqs, n_state, tiles, LANE), full)
    dma = pltpu.SemaphoreType.DMA
    layer_half = jax.ShapeDtypeStruct((middle.shape[0], middle.shape[1] // 2), jnp.bfloat16)
    picks = jnp.repeat(jnp.eye(2 * n_state, dtype=jnp.bfloat16), tiles, 1)
    return pl.pallas_call(
        functools.partial(
            backward_pair_kernel, len(arrays), n_state, tiles, groups, blocks, seqs
        ),
        in_specs=[vmem] * 3 + [smem] * 2 + [vmem] * 4 + [hbm] + [vmem] * len(arrays),
        out_specs=[vmem] * 6 + [hbm] * len(arrays),
        out_shape=[
            jax.ShapeDtypeStruct(step.shape, full),
            jax.ShapeDtypeStruct(step.shape, full),
            jax.ShapeDtypeStruct(rate.shape, full),
            jax.ShapeDtypeStruct((tokens, 2 * n_state, LANE), full),
            layer_half,
            layer_half,
        ]
        + swap_shapes(arrays),
        scratch_shapes=[
            pltpu.VMEM((n_state, tiles, LANE), full),
            boundary,
            boundary,
            pltpu.VMEM((2, groups * SUB, n_state, tiles, LANE), full),
        ]
        + [held] * 5
        + [
            slots_for(ffn_part, tp_count),
            dma((2,)),
            dma((seqs,)),
            dma((seqs,)),
            dma((1, tp_count - 1)),
            dma((1, tp_count - 1)),
        ]
        + swap_scratch(arrays),
        compiler_params=pltpu.CompilerParams(
            collective_id=call_id, has_side_effects=True, vmem_limit_bytes=VMEM_GRANT
        ),
    )(step, inputs, ograd, b_rows, c_rows, rate, picks, ffn_part, middle, prior, *arrays)


class PlaneGather:
    def __init__(self, own, gathered, send_sem, recv_sem):
        self.own, self.gathered = own, gathered
        self.send_sem, self.recv_sem = send_sem, recv_sem
        self.dp, self.ctx = lax.axis_index("dp"), lax.axis_index("ctx")
        self.n_dp, self.n_ctx = lax.axis_size("dp"), lax.axis_size("ctx")
        self.hands_on = relayed()
        self.count = self.n_dp * self.n_ctx
        self.me = self.dp * self.n_ctx + self.ctx
        self.others = [lax.rem(self.me + hop, self.count) for hop in range(1, self.count)]
        self.copies = {}
        if self.hands_on:
            core = lax.rem(self.dp, 2)
            over_core = self.dp + 1 - 2 * core
            over_y = lax.rem(self.dp + 2, 4)
            over_x = 1 - self.ctx
            self.core = {"dp": over_core, "ctx": self.ctx}
            self.at_x = {"dp": self.dp, "ctx": over_x}
            self.at_y = {"dp": over_y, "ctx": self.ctx}
            self.from_x = self.dp * 2 + over_x
            self.from_y = over_y * 2 + self.ctx
            self.across = over_y * 2 + over_x

    def part(self, owner, half):
        rows = self.gathered.shape[0] // self.count
        start, size = owner * rows, rows
        if half is not None:
            size = rows // 2
            start = start + half * size
        return self.gathered.at[pl.ds(pl.multiple_of(start, size), size), :]

    def send(self, which, owner, half, where):
        target = self.part(owner, half)
        source = target
        if owner is self.me:
            rows = self.own.shape[0]
            source = self.own
            if half is not None:
                source = self.own.at[pl.ds(half * (rows // 2), rows // 2), :]
        self.copies[which] = sent(
            source, target, self.send_sem.at[which], self.recv_sem.at[which], where
        )

    def arrived(self, *which):
        for one in which:
            self.copies[one].wait_recv()

    def begin(self, local_sem):
        self.local = pltpu.make_async_copy(self.own, self.part(self.me, None), local_sem)
        self.local.start()
        if not self.hands_on:
            for hop, other in enumerate(self.others):
                self.send(hop, self.me, None, device_at(PLANE, other))
            return
        self.send(0, self.me, 1, self.at_x)
        self.send(1, self.me, 0, self.at_y)
        self.send(2, self.me, None, self.core)
        self.send(3, self.me, 0, self.at_x)
        self.send(4, self.me, 1, self.at_y)

    def relay(self):
        if not self.hands_on:
            return
        self.arrived(0, 1)
        self.send(5, self.from_x, 1, self.at_y)
        self.send(6, self.from_y, 0, self.at_x)
        self.send(7, self.from_x, 1, self.core)
        self.send(8, self.from_y, 0, self.core)

    def hand_over(self):
        if not self.hands_on:
            return
        self.arrived(3, 4)
        self.send(9, self.from_x, 0, self.core)
        self.send(10, self.from_y, 1, self.core)

    def hand_over_last(self):
        if not self.hands_on:
            return
        self.arrived(5, 6)
        self.send(11, self.across, 1, self.core)
        self.send(12, self.across, 0, self.core)

    def end(self):
        if self.hands_on:
            self.arrived(2, 7, 8, 9, 10, 11, 12)
        else:
            self.arrived(*range(self.count - 1))
        for copy in self.copies.values():
            copy.wait_send()
        self.local.wait()


def relayed():
    return lax.axis_size("dp") == 4 and lax.axis_size("ctx") == 2


def gather_sems():
    count = 13 if relayed() else group_size(PLANE) - 1
    return pltpu.SemaphoreType.DMA((count,))


WIDE = 512


def products(source, first, last, dot, target, block_buf, block_sem, out_buf, out_sem):
    def fetch(j, slot):
        columns = pl.ds(pl.multiple_of(j * WIDE, WIDE), WIDE)
        return pltpu.make_async_copy(
            source.at[:, columns], block_buf.at[slot], block_sem.at[slot]
        )

    def store(j, slot):
        return pltpu.make_async_copy(out_buf.at[slot], target(j), out_sem.at[slot])

    fetch(first, first % 2).start()

    @pl.loop(first, last)
    def _(j):
        slot = lax.rem(j, 2)

        @pl.when(j + 1 < last)
        def _():
            fetch(j + 1, 1 - slot).start()

        fetch(j, slot).wait()

        @pl.when(j >= first + 2)
        def _():
            store(j - 2, slot).wait()

        out_buf[slot] = dot(block_buf[slot])
        store(j, slot).start()

    for j in range(max(first, last - 2), last):
        store(j, j % 2).wait()


class PlaneSum:
    def __init__(self, array, total, *refs):
        self.array, self.result = array, total
        self.hands_on = relayed()
        if not self.hands_on:
            self.slots, send_sem, recv_sem = refs
            self.group = Group(PLANE, send_sem, recv_sem)
            return
        self.core_slot, self.pair, self.chip_slots, *self.sems = refs
        dp, ctx = lax.axis_index("dp"), lax.axis_index("ctx")
        self.half = lax.rem(dp, 2)
        self.other_core = {"dp": dp + 1 - 2 * self.half, "ctx": ctx}
        over_y, over_x = lax.rem(dp + 2, 4), 1 - ctx
        self.quarter = lax.div(dp, 2) * 2 + ctx
        self.chips = [
            ({"dp": a, "ctx": b}, lax.div(a, 2) * 2 + b)
            for a, b in ((dp, over_x), (over_y, ctx), (over_y, over_x))
        ]

    def to_core(self, source, target, which):
        core_send, core_recv = self.sems[:2]
        return sent(
            source, target, core_send.at[which], core_recv.at[which], self.other_core
        )

    def to_chip(self, source, target, which, at):
        chip_send, chip_recv = self.sems[2:]
        return sent(
            source,
            target,
            chip_send.at[which, at],
            chip_recv.at[which, at],
            self.chips[at][0],
        )

    def begin(self):
        if not self.hands_on:
            self.copies = self.group.scatter(self.array, self.slots, 0)
            return
        self.copies = [self.to_core(rows_of(self.array, 1 - self.half, 2), self.core_slot, 0)]

    def add_pair(self):
        if not self.hands_on:
            return
        finish(self.copies)
        self.pair[...] = (
            rows_of(self.array, self.half, 2)[...].astype(jnp.float32)
            + self.core_slot[...].astype(jnp.float32)
        ).astype(self.pair.dtype)
        self.copies = [
            self.to_chip(rows_of(self.pair, index, 4), self.chip_slots.at[at], 0, at)
            for at, (_, index) in enumerate(self.chips)
        ]

    def add_all(self):
        finish(self.copies)
        if not self.hands_on:
            self.group.own(self.result)[...] = self.group.total(self.array, self.slots).astype(
                self.result.dtype
            )
            self.copies = self.group.spread(self.result, 1)
            return
        total = rows_of(self.pair, self.quarter, 4)[...].astype(jnp.float32)
        for at in range(3):
            total = total + self.chip_slots[at].astype(jnp.float32)
        mine = rows_of(self.result, self.half * 4 + self.quarter, 8)
        mine[...] = total.astype(self.result.dtype)
        self.copies = [self.to_chip(mine, mine, 1, at) for at in range(3)]

    def hand_over(self):
        if not self.hands_on:
            return
        finish(self.copies)
        half = rows_of(self.result, self.half, 2)
        self.copies = [self.to_core(half, half, 1)]

    def end(self):
        finish(self.copies)


def plane_sum_scratch(array):
    dma = pltpu.SemaphoreType.DMA
    count = group_size(PLANE)
    if not relayed():
        return [slots_for(array, count), dma((2, count - 1)), dma((2, count - 1))]
    rows, width = array.shape
    return [
        pltpu.VMEM((rows // 2, width), array.dtype),
        pltpu.VMEM((rows // 2, width), array.dtype),
        pltpu.VMEM((3, rows // 8, width), array.dtype),
        dma((2,)),
        dma((2,)),
        dma((2, 3)),
        dma((2, 3)),
    ]


SMALL_ROWS = 32
GAIN_ROWS = 16


def tail_kernel(
    swaps,
    conv_grad,
    gate_grad,
    convkern,
    convbias,
    stepbias,
    decaylog,
    skipgain,
    ffngain,
    layer_first,
    layer_rows,
    middle_low,
    step_low,
    pre_low,
    select_low,
    scan_in,
    tokens,
    middle_grad,
    gain_row,
    in_conv,
    in_gate,
    one_cols,
    two_cols,
    ct_cols,
    middle_cols,
    ffn_all,
    gated_all,
    tokens_grad,
    layer_out,
    vectors_sum,
    step_sum,
    select_sum,
    gains,
    mix_all,
    grad_inproj,
    grad_outproj,
    grad_gateup,
    grad_downproj,
    mix_own,
    normed_part,
    small,
    small_sum,
    gain_slots,
    gain_own,
    vectors_own,
    cols,
    in_buf,
    block_buf,
    wide_buf,
    tall_buf,
    cols_sem,
    in_sem,
    block_sem,
    wide_sem,
    tall_sem,
    tp_send,
    tp_recv,
    gather_send,
    gather_recv,
    local_sem,
    *sems,
):
    inner = conv_grad.shape[1]
    hidden = ffn_all.shape[1] // 3
    width = tokens.shape[1]
    rank = step_low.shape[1]
    tp = Group(("tp",), tp_send, tp_recv)
    line = LineSum(normed_part, *sems[:5])
    tokens_spread = LineSpread(tokens_grad, *sems[5:7])
    layer_last = layer_out.at[:, width // 2 :]
    layer_spread = LineSpread(layer_last, *sems[7:9])
    count = 7 if relayed() else 3
    small_total = PlaneSum(small, small_sum, *sems[9 : 9 + count])
    swap_sems = sems[9 + count :]
    gather = PlaneGather(mix_own, mix_all, gather_send, gather_recv)
    sources = (one_cols, two_cols, ct_cols) if swaps else (one_cols, two_cols, ct_cols, middle_cols)
    loads = [
        pltpu.make_async_copy(source, cols.at[at], cols_sem.at[at])
        for at, source in enumerate(sources)
    ]
    if swaps:
        swap = Swap([middle_low], [cols.at[3]], *swap_sems)

    def fetch(j):
        slot = j % 2
        rows = slice(j * WIDE, (j + 1) * WIDE)
        return [
            pltpu.make_async_copy(source.at[rows, :], in_buf.at[slot, at], in_sem.at[slot, at])
            for at, source in enumerate((in_conv, in_gate))
        ]

    for copy in fetch(0) + loads:
        copy.start()
    mix_own[:, :inner] = conv_grad[...]
    mix_own[:, inner:] = gate_grad[...]
    greet([(("tp",), tp.others), (PLANE, gather.others)])
    gather.begin(local_sem)

    small[...] = jnp.zeros_like(small)
    vectors_own[...] = jnp.zeros_like(vectors_own)
    at = 0
    for vector in (convkern, convbias, stepbias, decaylog, skipgain):
        vectors_own[at : at + vector.shape[0], :] = vector[...]
        at += vector.shape[0]
    at = SMALL_ROWS - GAIN_ROWS + 10
    for row in range(width // inner):
        vectors_own[at + row : at + row + 1, :] = ffngain[:, row * inner : (row + 1) * inner]
    hidden_in = tokens[...].astype(jnp.float32)
    unit_rows = hidden_in * inverse_rms(hidden_in)
    blocks = width // WIDE
    firsts = []
    for j in range(blocks):
        if j + 1 < blocks:
            for copy in fetch(j + 1):
                copy.start()
        finish(fetch(j))
        columns = slice(j * WIDE, (j + 1) * WIDE)
        block = matmul_nt(conv_grad[...], in_buf[j % 2, 0]) + matmul_nt(
            gate_grad[...], in_buf[j % 2, 1]
        )
        normed_part[:, columns] = block.astype(normed_part.dtype)
        firsts.append(line.begin(j))
        gain_grad = jnp.sum(block * unit_rows[:, columns], 0, keepdims=True)
        if j:
            line.pass_on(j - 1, firsts[j - 1])
        row, at = divmod(j * WIDE, inner)
        row += SMALL_ROWS - GAIN_ROWS + 8
        vectors_own[row : row + 1, at : at + WIDE] = gain_grad
    layer_out[:, : width // 2] = layer_first[...]
    rows_of(layer_last, tp.me, tp.count)[...] = layer_rows[...]
    layer_spread.begin()
    small[:SMALL_ROWS, :] = vectors_own[...].astype(small.dtype)
    small[SMALL_ROWS : SMALL_ROWS + rank, :] = matmul_tn(step_low[...], pre_low[...]).astype(
        small.dtype
    )
    selected = select_sum.shape[0]
    small[SMALL_ROWS + rank : SMALL_ROWS + rank + selected, :] = matmul_tn(
        select_low[...], scan_in[...]
    )[:selected].astype(small.dtype)
    small_total.begin()
    line.pass_on(blocks - 1, firsts[-1])

    def flat(at):
        return lambda block: matmul_tn(cols[at], block)

    def tall(at):
        return lambda block: matmul_tn(block, cols[at])

    def side_by_side(ref, first):
        per = ref.shape[2] // WIDE

        def target(j):
            at = j - first
            columns = pl.ds(pl.multiple_of(lax.rem(at, per) * WIDE, WIDE), WIDE)
            return ref.at[lax.div(at, per), :, columns]

        return target

    def one_above_other(ref):
        return lambda j: ref.at[pl.ds(pl.multiple_of(j * WIDE, WIDE), WIDE), :]

    wide = (block_buf, block_sem, wide_buf, wide_sem)
    high = (block_buf, block_sem, tall_buf, tall_sem)
    down_end = hidden // WIDE
    gu_end = 3 * hidden // WIDE
    finish(loads)
    gu_middle = (down_end + gu_end) // 2
    to_gateup = side_by_side(grad_gateup, down_end)
    products(ffn_all, 0, down_end, tall(2), one_above_other(grad_downproj), *high)
    gather.relay()
    small_total.add_pair()
    products(ffn_all, down_end, gu_middle, flat(1), to_gateup, *wide)
    hidden_in = tp.own(tokens)[...].astype(jnp.float32)
    tp.own(tokens_grad)[...] = (
        middle_grad[...]
        + norm_back(
            line.total(),
            hidden_in,
            inverse_rms(hidden_in),
            gain_row[...].astype(jnp.float32),
        )
    ).astype(tokens_grad.dtype)
    tokens_spread.begin()
    layer_spread.pass_on()
    gather.hand_over()
    small_total.add_all()
    if swaps:
        swap.begin()
    products(ffn_all, gu_middle, gu_end, flat(1), to_gateup, *wide)
    tokens_spread.pass_on()
    gather.hand_over_last()
    small_total.hand_over()
    gather.end()
    products(mix_all, 0, 2 * inner // WIDE, flat(0), side_by_side(grad_inproj, 0), *wide)
    small_total.end()
    gain_own[...] = small_sum[SMALL_ROWS - GAIN_ROWS : SMALL_ROWS, :].astype(jnp.float32)
    gain_sent = [tp.one(gain_own, gain_slots.at[hop], 0, hop) for hop in range(tp.count - 1)]
    vectors_sum[...] = small_sum[:SMALL_ROWS, :].astype(jnp.float32)
    step_sum[...] = small_sum[SMALL_ROWS : SMALL_ROWS + rank, :].astype(jnp.float32)
    select_sum[...] = small_sum[SMALL_ROWS + rank : SMALL_ROWS + rank + selected, :].astype(
        jnp.float32
    )
    if swaps:
        swap.end()
    products(gated_all, 0, inner // WIDE, tall(3), one_above_other(grad_outproj), *high)
    finish(gain_sent)
    total = gain_own[...]
    for hop in range(tp.count - 1):
        total = total + gain_slots[hop]
    gains[...] = total
    tokens_spread.end()
    layer_spread.end()


def run_tail(
    call_id,
    selected,
    swaps,
    conv_grad,
    gate_grad,
    vectors,
    layer_first,
    layer_rows,
    middle_low,
    step_low,
    pre_low,
    select_low,
    scan_in,
    tokens,
    middle_grad,
    gain_row,
    in_conv,
    in_gate,
    one_cols,
    two_cols,
    ct_cols,
    middle_cols,
    ffn_all,
    gated_all,
):
    rows, inner = conv_grad.shape
    rank = step_low.shape[1]
    hidden = ffn_all.shape[1] // 3
    width = tokens.shape[1]
    share = one_cols.shape[1]
    all_rows = ffn_all.shape[0]
    tp_count, plane_count = group_size(("tp",)), group_size(PLANE)
    low, full = jnp.bfloat16, jnp.float32
    vmem = pl.BlockSpec(memory_space=pltpu.VMEM)
    hbm = pl.BlockSpec(memory_space=pltpu.HBM)
    dma = pltpu.SemaphoreType.DMA
    small_rows = SMALL_ROWS + rank + selected
    small = jax.ShapeDtypeStruct((small_rows + -small_rows % (16 * plane_count), inner), low)
    part = jax.ShapeDtypeStruct((rows, width), low)
    return pl.pallas_call(
        functools.partial(tail_kernel, swaps),
        in_specs=[vmem] * 18 + [hbm] * 8,
        out_specs=[vmem] * 6 + [hbm] * 5,
        out_shape=[
            jax.ShapeDtypeStruct(tokens.shape, low),
            jax.ShapeDtypeStruct(tokens.shape, low),
            jax.ShapeDtypeStruct((SMALL_ROWS, inner), full),
            jax.ShapeDtypeStruct((rank, inner), full),
            jax.ShapeDtypeStruct((selected, inner), full),
            jax.ShapeDtypeStruct((GAIN_ROWS, inner), full),
            jax.ShapeDtypeStruct((all_rows, 2 * inner), low),
            jax.ShapeDtypeStruct((2, share, inner), full),
            jax.ShapeDtypeStruct((inner, share), full),
            jax.ShapeDtypeStruct((2, share, hidden), full),
            jax.ShapeDtypeStruct((hidden, share), full),
        ],
        scratch_shapes=[
            pltpu.VMEM((rows, 2 * inner), low),
            pltpu.VMEM(part.shape, low),
            pltpu.VMEM(small.shape, low),
            pltpu.VMEM(small.shape, low),
            pltpu.VMEM((tp_count - 1, GAIN_ROWS, inner), full),
            pltpu.VMEM((GAIN_ROWS, inner), full),
            pltpu.VMEM((SMALL_ROWS, inner), full),
            pltpu.VMEM((4, all_rows, share), low),
            pltpu.VMEM((2, 2, WIDE, inner), low),
            pltpu.VMEM((2, all_rows, WIDE), low),
            pltpu.VMEM((2, share, WIDE), full),
            pltpu.VMEM((2, WIDE, share), full),
            dma((4,)),
            dma((2, 2)),
            dma((2,)),
            dma((2,)),
            dma((2,)),
            dma((1, tp_count - 1)),
            dma((1, tp_count - 1)),
        ]
        + gather_scratch()
        + line_sum_scratch(part, width // WIDE)
        + line_spread_scratch() * 2
        + plane_sum_scratch(small)
        + (swap_scratch([tokens]) if swaps else []),
        compiler_params=pltpu.CompilerParams(
            collective_id=call_id, has_side_effects=True, vmem_limit_bytes=VMEM_GRANT
        ),
    )(
        conv_grad,
        gate_grad,
        *vectors,
        layer_first,
        layer_rows,
        middle_low,
        step_low,
        pre_low,
        select_low,
        scan_in,
        tokens,
        middle_grad,
        gain_row,
        in_conv,
        in_gate,
        one_cols,
        two_cols,
        ct_cols,
        middle_cols,
        ffn_all,
        gated_all,
    )


BORDER = 16


def head_kernel(
    tokens,
    gain,
    in_conv,
    in_gate,
    conv_in,
    gate_mix,
    border,
    conv_all,
    gate_all,
    normed,
    block_buf,
    block_sem,
    border_send,
    border_recv,
    *sems,
):
    place, places = lax.axis_index("ctx"), lax.axis_size("ctx")
    seqs = border.shape[0] // BORDER
    span = conv_in.shape[0] // seqs

    def to_next(seq):
        return send_on(
            conv_in.at[pl.ds((seq + 1) * span - BORDER, BORDER), :],
            border.at[pl.ds(seq * BORDER, BORDER), :],
            border_send.at[seq],
            border_recv.at[seq],
            place + 1,
        )

    conv = PlaneGather(in_conv, conv_all, *sems[:2])
    gate = PlaneGather(in_gate, gate_all, *sems[3:5])
    greet([(PLANE, conv.others)])
    conv.begin(sems[2])
    gate.begin(sems[5])
    hidden_in = tokens[...].astype(jnp.float32)
    normed[...] = (hidden_in * inverse_rms(hidden_in) * gain[...].astype(jnp.float32)).astype(
        normed.dtype
    )
    conv.relay()
    conv.hand_over()
    gate.relay()
    conv.hand_over_last()
    gate.hand_over()
    conv.end()
    product_in_blocks(normed, conv_all, conv_in, block_buf, block_sem)

    @pl.when(place == 0)
    def _():
        border[...] = jnp.zeros_like(border)

    @pl.when(place < places - 1)
    def _():
        for seq in range(seqs):
            to_next(seq).start()

    gate.hand_over_last()
    gate.end()
    product_in_blocks(normed, gate_all, gate_mix, block_buf, block_sem)

    @pl.when(place < places - 1)
    def _():
        for seq in range(seqs):
            to_next(seq).wait_send()

    @pl.when(place > 0)
    def _():
        for seq in range(seqs):
            to_next(seq).wait_recv()


def run_head(call_id, tokens, gain, inproj, seqs):
    rows, width = tokens.shape
    inner = inproj.shape[2]
    low = jnp.bfloat16
    vmem = pl.BlockSpec(memory_space=pltpu.VMEM)
    hbm = pl.BlockSpec(memory_space=pltpu.HBM)
    return pl.pallas_call(
        head_kernel,
        in_specs=[vmem] * 2 + [hbm] * 2,
        out_specs=[vmem] * 3 + [hbm] * 2,
        out_shape=[
            jax.ShapeDtypeStruct((rows, inner), low),
            jax.ShapeDtypeStruct((rows, inner), jnp.float32),
            jax.ShapeDtypeStruct((seqs * BORDER, inner), low),
            jax.ShapeDtypeStruct((width, inner), low),
            jax.ShapeDtypeStruct((width, inner), low),
        ],
        scratch_shapes=[
            pltpu.VMEM((rows, width), low),
            pltpu.VMEM((2, width, WIDE), low),
            pltpu.SemaphoreType.DMA((2,)),
            pltpu.SemaphoreType.DMA((seqs,)),
            pltpu.SemaphoreType.DMA((seqs,)),
        ]
        + gather_scratch() * 2,
        compiler_params=pltpu.CompilerParams(
            collective_id=call_id, has_side_effects=True, vmem_limit_bytes=VMEM_GRANT
        ),
    )(tokens, gain, inproj[0], inproj[1])


def per_device(
    tokens,
    mixgain,
    inproj,
    convkern,
    convbias,
    selproj,
    stepproj,
    stepbias,
    decaylog,
    skipgain,
    outproj,
    ffngain,
    gateup,
    downproj,
    cotangent,
):
    seqs, span, width = tokens.shape
    rows = seqs * span
    taps, inner = convkern.shape
    rank = stepproj.shape[0]
    n_state = decaylog.shape[1]
    tiles = inner // LANE
    gain_mix = mixgain.astype(jnp.float32)
    kernel = convkern.astype(jnp.float32)
    kernel_bias = convbias.astype(jnp.float32)
    step_bias = stepbias.astype(jnp.float32)
    skip_weight = skipgain.astype(jnp.float32)
    decay_rate = -jnp.exp(jnp.transpose(decaylog.astype(jnp.float32)))
    rate = (decay_rate * LOG2E).reshape(n_state, tiles, LANE)

    gain_mix_row, gain_ffn_row = mixgain.reshape(1, width), ffngain.reshape(1, width)
    low = jnp.bfloat16

    tokens_rows = tokens.reshape(rows, width)
    ct_low = cotangent.reshape(rows, width)
    swap_now = swaps_in_kernels(width)
    out_first = gathered_rows(outproj[: inner // 4])
    ffn_pack = gathered_rows(
        jnp.concatenate([gateup[0], gateup[1], jnp.transpose(downproj)], 1)
    )
    conv_in, gate_mix, border, in_conv, in_gate = run_head(
        5, tokens_rows, gain_mix_row, inproj, seqs
    )
    hidden_in = tokens_rows.astype(jnp.float32)
    scale_one = inverse_rms(hidden_in)
    normed_one = (hidden_in * scale_one * gain_mix).astype(low)

    conv_seqs = conv_in.reshape(seqs, span, inner)
    rim_rows = border.reshape(seqs, BORDER, inner)[:, BORDER - (taps - 1) :]
    padded_in = jnp.concatenate([rim_rows, conv_seqs], 1).astype(jnp.float32)
    conv_out = kernel_bias[None, None]
    for offset in range(taps):
        conv_out = conv_out + kernel[offset][None, None] * padded_in[:, offset : offset + span]
    conv_out = conv_out.reshape(rows, inner)
    scan_in = jax.nn.silu(conv_out).astype(low)
    scan_float = scan_in.astype(jnp.float32)
    columns = selproj.shape[1]
    select_width = -(-columns // LANE) * LANE
    select_weights = jnp.pad(selproj, ((0, 0), (0, select_width - columns)))
    select_cols = run_select(0, matmul(scan_in, select_weights))

    def columns_of(swapped, array):
        if not swapped:
            return swapped_columns(array)
        return swapped[0].reshape(-1, swapped[0].shape[-1])

    step_low = select_cols[:, :rank].astype(low)
    b_rows = select_cols[:, rank : rank + n_state].reshape(-1)
    c_rows = select_cols[:, rank + n_state : columns].reshape(-1)
    step_pre = matmul(step_low, stepproj) + step_bias[None]
    step_size = jax.nn.softplus(step_pre)
    in_pairs = lax.axis_size("ctx") == 2
    if in_pairs:
        prior, scan_out, out_last = scan_forward_pair(
            6,
            step_size,
            scan_float,
            b_rows,
            c_rows,
            rate,
            seqs,
            outproj[inner // 4 :],
        )
    else:
        span_decay = jnp.exp(
            decay_rate[None] * jnp.sum(step_size.reshape(seqs, span, inner), 1)[:, None]
        ).reshape(seqs, n_state, tiles, LANE)
        ends = scan_ends(step_size, scan_float, b_rows, rate, seqs, False)
        start = from_earlier(ends, span_decay, 1)
        prior, scan_out = scan_forward(start, step_size, scan_float, b_rows, c_rows, rate, seqs)
        out_last = gathered_rows(outproj[inner // 4 :])
    mixer_core = scan_out + skip_weight[None] * scan_float
    gate_sig = jax.nn.silu(gate_mix)
    gated = (mixer_core * gate_sig).astype(low)
    normed_two, middle, gated_all, *swapped = mixer_out(
        1,
        gated,
        out_first,
        out_last,
        tokens_rows,
        gain_ffn_row,
        [normed_one] if swap_now else [],
    )
    normed_one_cols = columns_of(swapped, normed_one)
    made, *swapped = run_ffn(8, normed_two, ct_low, ffn_pack, swap_now)
    ct_cols = columns_of(swapped, ct_low)
    ffn_all = gathered_rows(made)
    middle_low, middle_grad, ffngain_part, gated_grad, ffn_part, *swapped = ffn_back(
        2,
        made,
        ct_low,
        middle,
        gain_ffn_row,
        out_first,
        out_last,
        ffn_pack,
        [normed_two] if swap_now else [],
    )
    normed_two_cols = columns_of(swapped, normed_two)
    core_grad = gated_grad * gate_sig
    gate_mix_grad = (gated_grad * mixer_core * silu_slope(gate_mix)).astype(low)
    grad_skipgain = jnp.sum(core_grad * scan_float, 0)
    if in_pairs:
        step_grad, input_grad, rate_grad, parts, *layer_rows = scan_backward_pair(
            7,
            prior,
            step_size,
            scan_float,
            core_grad,
            b_rows,
            c_rows,
            rate,
            seqs,
            ffn_part,
            middle,
            [],
        )
    else:
        back_ends = scan_ends(step_size, core_grad, c_rows, rate, seqs, True)
        end_grad = from_earlier(back_ends, span_decay, -1)
        step_grad, input_grad, rate_grad, parts = scan_backward(
            end_grad, prior, step_size, scan_float, core_grad, b_rows, c_rows, rate, seqs
        )
        ffn_sum = lax.psum_scatter(ffn_part, "tp", scatter_dimension=0, tiled=True)
        layer_rows = jnp.split((middle + ffn_sum.astype(jnp.float32)).astype(low), 2, 1)
    grad_decaylog = rate_grad.reshape(n_state, inner) * decay_rate
    pre_grad = step_grad * jax.nn.sigmoid(step_pre)
    grad_stepbias = jnp.sum(pre_grad, 0)
    pre_low = pre_grad.astype(low)
    select_part = jnp.concatenate(
        [
            matmul_nt(pre_low, stepproj),
            jnp.sum(parts, -1),
            jnp.zeros((rows, select_width - columns), jnp.float32),
        ],
        1,
    ).astype(low)
    select_low, layer_first = sum_over_tp(3, select_part, layer_rows[0])
    scan_in_grad = (
        core_grad * skip_weight[None]
        + input_grad
        + matmul_nt(select_low, select_weights)
    )
    conv_grad = scan_in_grad * silu_slope(conv_out)
    grad_convbias = jnp.sum(conv_grad, 0)
    conv_grad_seqs = conv_grad.reshape(seqs, span, inner)
    padded_grad = jnp.zeros(padded_in.shape, jnp.float32)
    kernel_rows = []
    for offset in range(taps):
        kernel_rows.append(jnp.sum(conv_grad_seqs * padded_in[:, offset : offset + span], (0, 1)))
        padded_grad = padded_grad + jnp.pad(
            kernel[offset][None, None] * conv_grad_seqs,
            ((0, 0), (offset, taps - 1 - offset), (0, 0)),
        )
    grad_convkern = jnp.stack(kernel_rows)
    returned = passed_along(padded_grad[:, : taps - 1], "ctx", -1)
    conv_in_grad = (
        (padded_grad[:, taps - 1 :] + jnp.pad(returned, ((0, 0), (span - taps + 1, 0), (0, 0))))
        .astype(low)
        .reshape(rows, inner)
    )
    vectors = [
        grad_convkern,
        grad_convbias[None],
        grad_stepbias[None],
        grad_decaylog,
        grad_skipgain[None],
        ffngain_part,
    ]
    (
        tokens_grad,
        layer_out,
        vectors,
        grad_stepproj,
        grad_selproj,
        gains,
        _,
        grad_inproj,
        grad_outproj,
        grad_gateup,
        grad_downproj,
    ) = run_tail(
        4,
        columns,
        swap_now,
        conv_in_grad,
        gate_mix_grad,
        vectors,
        layer_first,
        layer_rows[1],
        middle_low,
        step_low,
        pre_low,
        select_low,
        scan_in,
        tokens_rows,
        middle_grad,
        gain_mix_row,
        in_conv,
        in_gate,
        normed_one_cols,
        normed_two_cols,
        ct_cols,
        normed_two_cols if swap_now else swapped_columns(middle_low),
        ffn_all,
        gated_all,
    )
    at = taps + 2
    return (
        layer_out.reshape(tokens.shape),
        tokens_grad.reshape(tokens.shape),
        gains[8:10].reshape(width),
        grad_inproj,
        vectors[:taps],
        vectors[taps],
        jnp.transpose(grad_selproj),
        grad_stepproj,
        vectors[taps + 1],
        jnp.transpose(vectors[at : at + n_state]),
        vectors[at + n_state],
        grad_outproj,
        gains[10:12].reshape(width),
        grad_gateup,
        grad_downproj,
    )


def solution(mesh):
    in_specs = (
        P("dp", "ctx", None),
        P(),
        P(None, ("dp", "ctx"), "tp"),
        P(None, "tp"),
        P("tp"),
        P("tp", None),
        P(None, "tp"),
        P("tp"),
        P("tp", None),
        P("tp"),
        P("tp", ("dp", "ctx")),
        P(),
        P(None, ("dp", "ctx"), "tp"),
        P("tp", ("dp", "ctx")),
        P("dp", "ctx", None),
    )
    out_specs = (
        P("dp", "ctx", None),
        P("dp", "ctx", None),
        P(),
        P(None, ("dp", "ctx"), "tp"),
        P(None, "tp"),
        P("tp"),
        P("tp", None),
        P(None, "tp"),
        P("tp"),
        P("tp", None),
        P("tp"),
        P("tp", ("dp", "ctx")),
        P(),
        P(None, ("dp", "ctx"), "tp"),
        P("tp", ("dp", "ctx")),
    )
    return jax.shard_map(
        per_device, mesh=mesh, in_specs=in_specs, out_specs=out_specs, check_vma=False
    )
```

```python
import functools
import math

import jax
import jax.numpy as jnp
from jax import lax
from jax.experimental import pallas as pl
from jax.experimental.pallas import tpu as pltpu
from jax.sharding import PartitionSpec as P

EPSILON = 1e-05
LOG2E = math.log2(math.e)
LN2 = math.log(2.0)
SUB = 8
LANE = 128
VMEM_GRANT = 60 * 2**20
PLANE = ("dp", "ctx")


def passed_along(value, axis, steps):
    count = lax.axis_size(axis)
    first, last = (max(0, -steps), min(count, count - steps))
    return lax.ppermute(value, axis, [(source, source + steps) for source in range(first, last)])


def matmul(left, right):
    return jnp.dot(left, right, preferred_element_type=jnp.float32)


def matmul_nt(left, right):
    return lax.dot_general(
        left, right, (((1,), (1,)), ((), ())), preferred_element_type=jnp.float32
    )


def matmul_tn(left, right):
    return lax.dot_general(
        left, right, (((0,), (0,)), ((), ())), preferred_element_type=jnp.float32
    )


def inverse_rms(values):
    return lax.rsqrt(jnp.mean(values * values, -1, keepdims=True) + EPSILON)


def silu_slope(values):
    logistic = jax.nn.sigmoid(values)
    return logistic * (1.0 + values * (1.0 - logistic))


def norm_back(grad_norm, values, scale, gain):
    scaled_grad = grad_norm * gain
    unit_rows = values * scale
    return scale * (scaled_grad - unit_rows * jnp.mean(scaled_grad * unit_rows, -1, keepdims=True))


def stage_in(ref, group, held):
    for tile in range(held.shape[0] // SUB):
        held[pl.ds(tile * SUB, SUB), :] = ref[
            pl.ds(pl.multiple_of(group * SUB, SUB), SUB), pl.ds(tile * LANE, LANE)
        ]


def stage_out(held, ref, group):
    for tile in range(held.shape[0] // SUB):
        ref[pl.ds(pl.multiple_of(group * SUB, SUB), SUB), pl.ds(tile * LANE, LANE)] = held[
            pl.ds(tile * SUB, SUB), :
        ]


def token_row(held, at, tiles):
    return held[pl.ds(at, tiles, stride=SUB), :]


def ends_kernel(
    n_state,
    tiles,
    groups,
    reverse,
    step_ref,
    drive_ref,
    rows_ref,
    rate_ref,
    end_ref,
    step_held,
    drive_held,
):
    base = pl.program_id(0) * groups * SUB * n_state
    rates = [rate_ref[n] for n in range(n_state)]

    def one(turn, states):
        group = groups - 1 - turn if reverse else turn
        order = range(SUB - 1, -1, -1) if reverse else range(SUB)
        states = list(states)
        stage_in(step_ref, group, step_held)
        stage_in(drive_ref, group, drive_held)
        for at in order:
            step = token_row(step_held, at, tiles)
            drive = token_row(drive_held, at, tiles)
            if not reverse:
                drive = drive * step
            for n in range(n_state):
                row = rows_ref[base + (group * SUB + at) * n_state + n]
                decay = jnp.exp2(step * rates[n])
                if reverse:
                    states[n] = decay * (states[n] + drive * row)
                else:
                    states[n] = decay * states[n] + drive * row
        return tuple(states)

    zero = jnp.zeros((tiles, LANE), jnp.float32)
    states = lax.fori_loop(0, groups, one, (zero,) * n_state)
    for n in range(n_state):
        end_ref[0, n] = states[n]


def scan_ends(step, drive, rows, rate, seqs, reverse):
    n_state, tiles, _ = rate.shape
    groups = step.shape[0] // seqs // SUB
    rows_spec = pl.BlockSpec((groups * SUB, tiles * LANE), lambda s: (s, 0))
    held = pltpu.VMEM((tiles * SUB, LANE), jnp.float32)
    return pl.pallas_call(
        functools.partial(ends_kernel, n_state, tiles, groups, reverse),
        grid=(seqs,),
        in_specs=[
            rows_spec,
            rows_spec,
            pl.BlockSpec(memory_space=pltpu.SMEM),
            pl.BlockSpec((n_state, tiles, LANE), lambda s: (0, 0, 0)),
        ],
        out_specs=pl.BlockSpec((1, n_state, tiles, LANE), lambda s: (s, 0, 0, 0)),
        out_shape=jax.ShapeDtypeStruct((seqs, n_state, tiles, LANE), jnp.float32),
        scratch_shapes=[held, held],
        compiler_params=pltpu.CompilerParams(vmem_limit_bytes=VMEM_GRANT),
    )(step, drive, rows, rate)


def forward_kernel(
    n_state,
    tiles,
    groups,
    blocks,
    start_ref,
    step_ref,
    input_ref,
    brow_ref,
    crow_ref,
    rate_ref,
    prior_ref,
    mixed_ref,
    carried,
    step_held,
    input_held,
    mixed_held,
):
    base = (pl.program_id(0) * blocks + pl.program_id(1)) * groups * SUB * n_state

    @pl.when(pl.program_id(1) == 0)
    def _():
        carried[...] = start_ref[0]

    def one(group, states):
        states = list(states)
        stage_in(step_ref, group, step_held)
        stage_in(input_ref, group, input_held)
        for at in range(SUB):
            step = token_row(step_held, at, tiles)
            drive = step * token_row(input_held, at, tiles)
            mixed = [None] * 2
            for n in range(n_state):
                where = base + (group * SUB + at) * n_state + n
                prior_ref[group * SUB + at, n] = states[n]
                decay = jnp.exp2(step * rate_ref[n])
                states[n] = decay * states[n] + drive * brow_ref[where]
                term = states[n] * crow_ref[where]
                mixed[n % 2] = term if mixed[n % 2] is None else mixed[n % 2] + term
            mixed_held[pl.ds(at, tiles, stride=SUB), :] = mixed[0] + mixed[1]
        stage_out(mixed_held, mixed_ref, group)
        return tuple(states)

    states = lax.fori_loop(0, groups, one, tuple(carried[n] for n in range(n_state)))
    for n in range(n_state):
        carried[n] = states[n]


def scan_forward(start, step, inputs, b_rows, c_rows, rate, seqs):
    n_state, tiles, _ = rate.shape
    all_groups = step.shape[0] // SUB
    groups = math.gcd(all_groups // seqs, 4)
    blocks = all_groups // seqs // groups
    rows_spec = pl.BlockSpec((groups * SUB, tiles * LANE), lambda s, b: (s * blocks + b, 0))
    held = pltpu.VMEM((tiles * SUB, LANE), jnp.float32)
    smem = pl.BlockSpec(memory_space=pltpu.SMEM)
    tokens = all_groups * SUB
    return pl.pallas_call(
        functools.partial(forward_kernel, n_state, tiles, groups, blocks),
        grid=(seqs, blocks),
        in_specs=[
            pl.BlockSpec((1, n_state, tiles, LANE), lambda s, b: (s, 0, 0, 0)),
            rows_spec,
            rows_spec,
            smem,
            smem,
            pl.BlockSpec((n_state, tiles, LANE), lambda s, b: (0, 0, 0)),
        ],
        out_specs=[
            pl.BlockSpec(
                (groups * SUB, n_state, tiles, LANE), lambda s, b: (s * blocks + b, 0, 0, 0)
            ),
            rows_spec,
        ],
        out_shape=[
            jax.ShapeDtypeStruct((tokens, n_state, tiles, LANE), jnp.float32),
            jax.ShapeDtypeStruct(step.shape, jnp.float32),
        ],
        scratch_shapes=[pltpu.VMEM((n_state, tiles, LANE), jnp.float32)] + [held] * 3,
        compiler_params=pltpu.CompilerParams(vmem_limit_bytes=VMEM_GRANT),
    )(start, step, inputs, b_rows, c_rows, rate)


def backward_kernel(
    n_state,
    tiles,
    groups,
    blocks,
    end_ref,
    prior_ref,
    step_ref,
    input_ref,
    ograd_ref,
    brow_ref,
    crow_ref,
    rate_ref,
    picks_ref,
    step_grad_ref,
    input_grad_ref,
    rate_grad_ref,
    part_ref,
    carried,
    step_held,
    input_held,
    ograd_held,
    step_grad_held,
    input_grad_held,
):
    block = blocks - 1 - pl.program_id(1)
    base = (pl.program_id(0) * blocks + block) * groups * SUB * n_state

    @pl.when(pl.program_id(1) == 0)
    def _():
        carried[...] = end_ref[0]

    @pl.when((pl.program_id(0) == 0) & (pl.program_id(1) == 0))
    def _():
        rate_grad_ref[...] = jnp.zeros_like(rate_grad_ref)

    def one(turn, grads):
        group = groups - 1 - turn
        grads = list(grads)
        stage_in(step_ref, group, step_held)
        stage_in(input_ref, group, input_held)
        stage_in(ograd_ref, group, ograd_held)
        for at in range(SUB - 1, -1, -1):
            step = token_row(step_held, at, tiles)
            value = token_row(input_held, at, tiles)
            ograd = token_row(ograd_held, at, tiles)
            drive = step * value
            along_b = None
            along_rate = None
            brow_parts, crow_parts = [], []
            for n in range(n_state):
                where = base + (group * SUB + at) * n_state + n
                brow, crow = brow_ref[where], crow_ref[where]
                rate = rate_ref[n]
                decay = jnp.exp2(step * rate)
                grad = ograd * crow + grads[n]
                kept = decay * prior_ref[group * SUB + at, n]
                state = kept + drive * brow
                decay_term = grad * kept
                grads[n] = decay * grad
                rate_grad_ref[n] += decay_term * step
                by_rate, by_brow = decay_term * rate, grad * brow
                along_rate = by_rate if along_rate is None else along_rate + by_rate
                along_b = by_brow if along_b is None else along_b + by_brow
                brow_parts.append(grad * drive)
                crow_parts.append(ograd * state)
            step_grad_held[pl.ds(at, tiles, stride=SUB), :] = along_rate * LN2 + along_b * value
            input_grad_held[pl.ds(at, tiles, stride=SUB), :] = along_b * step
            parts = jnp.concatenate(brow_parts + crow_parts, 0).astype(jnp.bfloat16)
            part_ref[group * SUB + at] = jnp.dot(
                picks_ref[...], parts, preferred_element_type=jnp.float32
            )
        stage_out(step_grad_held, step_grad_ref, group)
        stage_out(input_grad_held, input_grad_ref, group)
        return tuple(grads)

    grads = lax.fori_loop(0, groups, one, tuple(carried[n] for n in range(n_state)))
    for n in range(n_state):
        carried[n] = grads[n]


def scan_backward(end_grad, prior, step, inputs, ograd, b_rows, c_rows, rate, seqs):
    n_state, tiles, _ = rate.shape
    all_groups = step.shape[0] // SUB
    groups = math.gcd(all_groups // seqs, 4)
    blocks = all_groups // seqs // groups

    def at(s, b):
        return s * blocks + blocks - 1 - b

    rows_spec = pl.BlockSpec((groups * SUB, tiles * LANE), lambda s, b: (at(s, b), 0))
    held = pltpu.VMEM((tiles * SUB, LANE), jnp.float32)
    smem = pl.BlockSpec(memory_space=pltpu.SMEM)
    tokens = all_groups * SUB
    picks = jnp.repeat(jnp.eye(2 * n_state, dtype=jnp.bfloat16), tiles, 1)
    return pl.pallas_call(
        functools.partial(backward_kernel, n_state, tiles, groups, blocks),
        grid=(seqs, blocks),
        in_specs=[
            pl.BlockSpec((1, n_state, tiles, LANE), lambda s, b: (s, 0, 0, 0)),
            pl.BlockSpec((groups * SUB, n_state, tiles, LANE), lambda s, b: (at(s, b), 0, 0, 0)),
            rows_spec,
            rows_spec,
            rows_spec,
            smem,
            smem,
            pl.BlockSpec((n_state, tiles, LANE), lambda s, b: (0, 0, 0)),
            pl.BlockSpec(picks.shape, lambda s, b: (0, 0)),
        ],
        out_specs=[
            rows_spec,
            rows_spec,
            pl.BlockSpec((n_state, tiles, LANE), lambda s, b: (0, 0, 0)),
            pl.BlockSpec((groups * SUB, 2 * n_state, LANE), lambda s, b: (at(s, b), 0, 0)),
        ],
        out_shape=[
            jax.ShapeDtypeStruct(step.shape, jnp.float32),
            jax.ShapeDtypeStruct(step.shape, jnp.float32),
            jax.ShapeDtypeStruct(rate.shape, jnp.float32),
            jax.ShapeDtypeStruct((tokens, 2 * n_state, LANE), jnp.float32),
        ],
        scratch_shapes=[pltpu.VMEM((n_state, tiles, LANE), jnp.float32)] + [held] * 5,
        compiler_params=pltpu.CompilerParams(vmem_limit_bytes=VMEM_GRANT),
    )(end_grad, prior, step, inputs, ograd, b_rows, c_rows, rate, picks)


def from_earlier(ends, decay, steps):
    count = lax.axis_size("ctx")
    if count == 1:
        return jnp.zeros_like(ends)
    if count == 2:
        return passed_along(ends, "ctx", steps)
    index = lax.axis_index("ctx")
    all_ends = lax.all_gather(ends, "ctx")
    all_decays = lax.all_gather(decay, "ctx")

    def one(turn, state):
        at = turn if steps > 0 else count - 1 - turn
        reached = at < index if steps > 0 else at > index
        return jnp.where(reached, all_decays[at] * state + all_ends[at], state)

    return lax.fori_loop(0, count, one, jnp.zeros_like(ends))


def gathered_rows(rows):
    return lax.all_gather(rows, PLANE, axis=0, tiled=True)


def swapped_columns(rows):
    return lax.all_to_all(rows, PLANE, split_axis=1, concat_axis=0, tiled=True)


def place_in(axes):
    index = 0
    for axis in axes:
        index = index * lax.axis_size(axis) + lax.axis_index(axis)
    return index


def device_at(axes, index):
    where = {}
    for axis in reversed(axes):
        size = lax.axis_size(axis)
        where[axis] = lax.rem(index, size)
        index = lax.div(index, size)
    return where


def greet(groups):
    barrier = pltpu.get_barrier_semaphore()
    total = 0
    for axes, others in groups:
        for other in others:
            pl.semaphore_signal(
                barrier,
                inc=1,
                device_id=device_at(axes, other),
                device_id_type=pl.DeviceIdType.MESH,
            )
            total += 1
    pl.semaphore_wait(barrier, total)


def sent(source, target, send_sem, recv_sem, where):
    copy = pltpu.make_async_remote_copy(
        src_ref=source,
        dst_ref=target,
        send_sem=send_sem,
        recv_sem=recv_sem,
        device_id=where,
        device_id_type=pl.DeviceIdType.MESH,
    )
    copy.start()
    return copy


def finish(copies):
    for copy in copies:
        copy.wait()


def rows_of(ref, index, count):
    rows = ref.shape[0] // count
    return ref.at[pl.ds(pl.multiple_of(index * rows, rows), rows), :]


class Group:
    def __init__(self, axes, send_sem, recv_sem):
        self.axes = axes
        self.count = math.prod(lax.axis_size(axis) for axis in axes)
        self.me = place_in(axes)
        self.others = [lax.rem(self.me + hop, self.count) for hop in range(1, self.count)]
        self.send_sem, self.recv_sem = send_sem, recv_sem

    def own(self, ref):
        return rows_of(ref, self.me, self.count)

    def one(self, source, target, which, hop):
        return sent(
            source,
            target,
            self.send_sem.at[which, hop],
            self.recv_sem.at[which, hop],
            device_at(self.axes, self.others[hop]),
        )

    def scatter(self, part, slot, which):
        return [
            self.one(rows_of(part, other, self.count), slot.at[hop], which, hop)
            for hop, other in enumerate(self.others)
        ]

    def total(self, part, slot):
        total = self.own(part)[...].astype(jnp.float32)
        for hop in range(self.count - 1):
            total = total + slot[hop].astype(jnp.float32)
        return total

    def spread(self, ref, which):
        return [self.one(self.own(ref), self.own(ref), which, hop) for hop in range(self.count - 1)]


def slots_for(part, count):
    return pltpu.VMEM((count - 1, part.shape[0] // count) + part.shape[1:], part.dtype)


def group_size(axes):
    return math.prod(lax.axis_size(axis) for axis in axes)


def line_of_four():
    me = lax.axis_index("tp")
    near = me + 1 - 2 * lax.rem(me, 2)
    return me, near, lax.rem(me + 2, 4), lax.rem(near + 2, 4)


class LineSum:
    def __init__(self, part, near_slots, far_slot, passed, send_sem, recv_sem):
        self.part, self.near_slots, self.far_slot = part, near_slots, far_slot
        self.passed, self.send_sem, self.recv_sem = passed, send_sem, recv_sem
        self.me, self.near, self.far, self.cross = line_of_four()
        self.blocks = send_sem.shape[1]
        self.copies = []

    def columns(self, j):
        wide = self.part.shape[1] // self.blocks
        return slice(j * wide, (j + 1) * wide)

    def rows(self, index):
        return rows_of(self.part, index, 4)

    def send(self, source, target, which, j, where):
        copy = sent(
            source.at[:, self.columns(j)],
            target.at[:, self.columns(j)],
            self.send_sem.at[which, j],
            self.recv_sem.at[which, j],
            {"tp": where},
        )
        self.copies.append((which, copy))
        return copy

    def begin(self, j):
        first = self.send(self.rows(self.cross), self.near_slots.at[0], 0, j, self.near)
        self.send(self.rows(self.near), self.near_slots.at[1], 1, j, self.near)
        return first

    def pass_on(self, j, first):
        first.wait_recv()
        columns = self.columns(j)
        self.passed[:, columns] = (
            self.rows(self.far)[:, columns].astype(jnp.float32)
            + self.near_slots[0, :, columns].astype(jnp.float32)
        ).astype(self.passed.dtype)
        self.send(self.passed, self.far_slot, 2, j, self.far)

    def total(self):
        for which, copy in self.copies:
            copy.wait_send()
            if which:
                copy.wait_recv()
        return (
            self.rows(self.me)[...].astype(jnp.float32)
            + self.near_slots[1].astype(jnp.float32)
            + self.far_slot[...].astype(jnp.float32)
        )

    def pass_all(self, firsts):
        for j, first in enumerate(firsts):
            self.pass_on(j, first)


def line_sum_scratch(part, blocks):
    share = (part.shape[0] // 4,) + part.shape[1:]
    sems = pltpu.SemaphoreType.DMA((3, blocks))
    return [
        pltpu.VMEM((2,) + share, part.dtype),
        pltpu.VMEM(share, part.dtype),
        pltpu.VMEM(share, part.dtype),
        sems,
        sems,
    ]


class LineSpread:
    def __init__(self, ref, send_sem, recv_sem):
        self.ref, self.send_sem, self.recv_sem = ref, send_sem, recv_sem
        self.me, self.near, self.far, self.cross = line_of_four()

    def send(self, owner, half, which, where):
        rows = rows_of(self.ref, owner, 4)
        if half is not None:
            wide = self.ref.shape[1] // 2
            rows = rows.at[:, half * wide : (half + 1) * wide]
        return sent(rows, rows, self.send_sem.at[which], self.recv_sem.at[which], {"tp": where})

    def begin(self):
        self.across = [self.send(self.me, half, half, self.far) for half in range(2)]
        self.within = [self.send(self.me, None, 2, self.near)]

    def pass_on(self):
        for half, copy in enumerate(self.across):
            copy.wait_recv()
            self.within.append(self.send(self.far, half, 3 + half, self.near))

    def end(self):
        for copy in self.across:
            copy.wait_send()
        finish(self.within)

    def run(self):
        self.begin()
        self.pass_on()
        self.end()


def line_spread_scratch():
    return [pltpu.SemaphoreType.DMA((5,)), pltpu.SemaphoreType.DMA((5,))]


class Swap:
    def __init__(self, arrays, swapped, send_sem, recv_sem, local_sem):
        plane = Group(PLANE, send_sem, recv_sem)
        self.plane, self.arrays, self.swapped, self.local_sem = plane, arrays, swapped, local_sem

    def begin(self):
        self.copies, plane = [], self.plane
        for which, (array, swapped) in enumerate(zip(self.arrays, self.swapped)):
            share = swapped.shape[1]

            def columns(index):
                return array.at[:, pl.ds(pl.multiple_of(index * share, share), share)]

            for hop, other in enumerate(plane.others):
                self.copies.append(plane.one(columns(other), plane.own(swapped), which, hop))
            local = pltpu.make_async_copy(
                columns(plane.me), plane.own(swapped), self.local_sem.at[which]
            )
            local.start()
            self.copies.append(local)

    def end(self):
        finish(self.copies)


def swap_scratch(arrays):
    sems = pltpu.SemaphoreType.DMA((len(arrays), group_size(PLANE) - 1))
    return [sems, sems, pltpu.SemaphoreType.DMA((len(arrays),))] if arrays else []


def swap_shapes(arrays):
    count = group_size(PLANE)
    return [
        jax.ShapeDtypeStruct((array.shape[0] * count, array.shape[1] // count), array.dtype)
        for array in arrays
    ]


def swaps_in_kernels(width):
    return width // group_size(PLANE) % LANE == 0


def gathered_shape(shard):
    return jax.ShapeDtypeStruct(
        (shard.shape[0] * group_size(PLANE),) + shard.shape[1:], shard.dtype
    )


def gather_scratch():
    return [gather_sems(), gather_sems(), pltpu.SemaphoreType.DMA(())]


def product_in_blocks(left, source, target, block_buf, block_sem):
    columns = range(0, source.shape[1], WIDE)

    def fetch(turn):
        at = columns[turn]
        return pltpu.make_async_copy(
            source.at[:, at : at + WIDE], block_buf.at[turn % 2], block_sem.at[turn % 2]
        )

    fetch(0).start()
    for turn, at in enumerate(columns):
        if turn + 1 < len(columns):
            fetch(turn + 1).start()
        fetch(turn).wait()
        target[:, at : at + WIDE] = matmul(left[...], block_buf[turn % 2]).astype(target.dtype)


def select_kernel(part, total, slots, send_sem, recv_sem):
    group = Group(("tp",), send_sem, recv_sem)
    greet([(("tp",), group.others)])
    finish(group.scatter(part, slots, 0))
    group.own(total)[...] = group.total(part, slots).astype(total.dtype)
    finish(group.spread(total, 1))


def run_select(call_id, part):
    count = group_size(("tp",))
    vmem = pl.BlockSpec(memory_space=pltpu.VMEM)
    sems = pltpu.SemaphoreType.DMA((2, count - 1))
    return pl.pallas_call(
        select_kernel,
        in_specs=[vmem],
        out_specs=vmem,
        out_shape=jax.ShapeDtypeStruct(part.shape, part.dtype),
        scratch_shapes=[slots_for(part, count), sems, sems],
        compiler_params=pltpu.CompilerParams(
            collective_id=call_id, has_side_effects=True, vmem_limit_bytes=VMEM_GRANT
        ),
    )(part)


def sum_kernel(part, own_rows, total, all_rows, slots, send_sem, recv_sem, *line_sems):
    group = Group(("tp",), send_sem, recv_sem)
    rows = LineSpread(all_rows, *line_sems)
    greet([(("tp",), group.others)])
    copies = group.scatter(part, slots, 0)
    group.own(all_rows)[...] = own_rows[...]
    rows.begin()
    finish(copies)
    group.own(total)[...] = group.total(part, slots).astype(total.dtype)
    copies = group.spread(total, 1)
    rows.pass_on()
    finish(copies)
    rows.end()


def sum_over_tp(call_id, part, own_rows):
    count = group_size(("tp",))
    vmem = pl.BlockSpec(memory_space=pltpu.VMEM)
    sems = pltpu.SemaphoreType.DMA((2, count - 1))
    return pl.pallas_call(
        sum_kernel,
        in_specs=[vmem] * 2,
        out_specs=[vmem] * 2,
        out_shape=[
            jax.ShapeDtypeStruct(part.shape, part.dtype),
            jax.ShapeDtypeStruct((own_rows.shape[0] * count, own_rows.shape[1]), own_rows.dtype),
        ],
        scratch_shapes=[slots_for(part, count), sems, sems] + line_spread_scratch(),
        compiler_params=pltpu.CompilerParams(
            collective_id=call_id, has_side_effects=True, vmem_limit_bytes=VMEM_GRANT
        ),
    )(part, own_rows)


def mixer_out_kernel(n_swaps, gated, out_first, out_last, tokens, gain, *refs):
    arrays, refs = refs[:n_swaps], refs[n_swaps:]
    normed, middle, gated_all, *refs = refs
    swapped, refs = refs[:n_swaps], refs[n_swaps:]
    part, refs = refs[0], refs[1:]
    line = LineSum(part, *refs[:5])
    spread = LineSpread(normed, *refs[5:7])
    gather_send, gather_recv, local_sem, *refs = refs[7:]
    group = Group(("tp",), None, None)
    gather = PlaneGather(gated, gated_all, gather_send, gather_recv)
    half = gated.shape[1] // 2
    share = out_first.shape[1]
    greet([(("tp",), group.others), (PLANE, gather.others)])
    gather.begin(local_sem)
    for at in range(out_first.shape[0] // half):
        rows = slice(at * half, (at + 1) * half)
        part[:, at * share : (at + 1) * share] = (
            matmul(gated[:, :half], out_first[rows, :])
            + matmul(gated[:, half:], out_last[rows, :])
        ).astype(part.dtype)
    firsts = [line.begin(j) for j in range(line.blocks)]
    if n_swaps:
        swap = Swap(arrays, swapped, *refs)
        swap.begin()
    line.pass_all(firsts)
    rows = group.own(tokens)[...].astype(jnp.float32) + line.total()
    middle[...] = rows
    group.own(normed)[...] = (rows * inverse_rms(rows) * gain[...].astype(jnp.float32)).astype(
        normed.dtype
    )
    spread.begin()
    gather.relay()
    gather.hand_over()
    spread.pass_on()
    spread.end()
    gather.hand_over_last()
    gather.end()
    if n_swaps:
        swap.end()


def mixer_out(call_id, gated, out_first, out_last, tokens, gain, arrays):
    count = group_size(("tp",))
    vmem = pl.BlockSpec(memory_space=pltpu.VMEM)
    hbm = pl.BlockSpec(memory_space=pltpu.HBM)
    rows, width = tokens.shape
    part = jax.ShapeDtypeStruct((rows, width), jnp.bfloat16)
    return pl.pallas_call(
        functools.partial(mixer_out_kernel, len(arrays)),
        in_specs=[vmem] * (5 + len(arrays)),
        out_specs=[vmem] * 2 + [hbm] + [hbm] * len(arrays),
        out_shape=[
            part,
            jax.ShapeDtypeStruct((rows // count, width), jnp.float32),
            gathered_shape(gated),
        ]
        + swap_shapes(arrays),
        scratch_shapes=[pltpu.VMEM(part.shape, part.dtype)]
        + line_sum_scratch(part, 2)
        + line_spread_scratch()
        + gather_scratch()
        + swap_scratch(arrays),
        compiler_params=pltpu.CompilerParams(
            collective_id=call_id, has_side_effects=True, vmem_limit_bytes=VMEM_GRANT
        ),
    )(gated, out_first, out_last, tokens, gain, *arrays)


def ffn_kernel(n_swaps, normed, ct, weights, *refs):
    hidden = weights.shape[1] // 3
    arrays, refs = refs[:n_swaps], refs[n_swaps:]
    made, *refs = refs
    swapped, refs = refs[:n_swaps], refs[n_swaps:]
    block_buf, block_sem, *swap_sems = refs
    if n_swaps:
        swap = Swap(arrays, swapped, *swap_sems)
        greet([(PLANE, swap.plane.others)])
        swap.begin()

    def columns(j, which):
        return pl.ds(pl.multiple_of(which * hidden + j * WIDE, WIDE), WIDE)

    def fetch(j, which):
        slot = lax.rem(j, 2)
        return pltpu.make_async_copy(
            weights.at[:, columns(j, which)],
            block_buf.at[slot, which],
            block_sem.at[slot, which],
        )

    for which in range(3):
        fetch(0, which).start()

    @pl.loop(0, hidden // WIDE)
    def _(j):
        slot = lax.rem(j, 2)

        @pl.when(j + 1 < hidden // WIDE)
        def _():
            for which in range(3):
                fetch(j + 1, which).start()

        fetch(j, 0).wait()
        gate = matmul(normed[...], block_buf[slot, 0])
        fetch(j, 1).wait()
        up = matmul(normed[...], block_buf[slot, 1])
        fetch(j, 2).wait()
        act_grad = matmul(ct[...], block_buf[slot, 2])
        logistic = jax.nn.sigmoid(gate)
        silu = gate * logistic
        slope = logistic * (1.0 + gate * (1.0 - logistic))
        made[:, columns(j, 0)] = (silu * up).astype(made.dtype)
        made[:, columns(j, 1)] = (act_grad * up * slope).astype(made.dtype)
        made[:, columns(j, 2)] = (act_grad * silu).astype(made.dtype)

    if n_swaps:
        swap.end()


def run_ffn(call_id, normed, ct, weights, arrays):
    rows, width = normed.shape
    vmem = pl.BlockSpec(memory_space=pltpu.VMEM)
    params = dict(collective_id=call_id, has_side_effects=True) if arrays else {}
    return pl.pallas_call(
        functools.partial(ffn_kernel, len(arrays)),
        in_specs=[vmem, vmem, pl.BlockSpec(memory_space=pltpu.HBM)] + [vmem] * len(arrays),
        out_specs=[vmem] + [pl.BlockSpec(memory_space=pltpu.HBM)] * len(arrays),
        out_shape=[jax.ShapeDtypeStruct((rows, weights.shape[1]), jnp.bfloat16)]
        + swap_shapes(arrays),
        scratch_shapes=[
            pltpu.VMEM((2, 3, width, WIDE), jnp.bfloat16),
            pltpu.SemaphoreType.DMA((2, 3)),
        ]
        + swap_scratch(arrays),
        compiler_params=pltpu.CompilerParams(vmem_limit_bytes=VMEM_GRANT, **params),
    )(normed, ct, weights, *arrays)


def ffn_back_kernel(
    n_swaps,
    made,
    ct,
    middle,
    gain,
    out_first,
    out_last,
    weights,
    *refs,
):
    arrays, refs = refs[:n_swaps], refs[n_swaps:]
    middle_low, middle_grad, gain_grad, gated_grad, ffn_part, *refs = refs
    swapped, refs = refs[:n_swaps], refs[n_swaps:]
    part, wide_buf, down_buf, wide_sem, down_sem, *sems = refs
    hidden = made.shape[1] // 3
    blocks = part.shape[1] // WIDE
    group = Group(("tp",), None, None)
    line = LineSum(part, *sems[:5])
    spread = LineSpread(middle_low, *sems[5:7])
    if n_swaps:
        swap = Swap(arrays, swapped, *sems[7:])
        greet([(("tp",), group.others), (PLANE, swap.plane.others)])
        swap.begin()
    else:
        greet([(("tp",), group.others)])

    def fetch(j):
        return pltpu.make_async_copy(
            weights.at[j * WIDE : (j + 1) * WIDE, : 2 * hidden],
            wide_buf.at[j % 2],
            wide_sem.at[j % 2],
        )

    def fetch_down(j):
        return pltpu.make_async_copy(
            weights.at[j * WIDE : (j + 1) * WIDE, 2 * hidden :],
            down_buf.at[j % 2],
            down_sem.at[j % 2],
        )

    fetch(0).start()
    firsts = []
    for j in range(blocks):
        if j + 1 < blocks:
            fetch(j + 1).start()
        else:
            fetch_down(0).start()
        fetch(j).wait()
        columns = slice(j * WIDE, (j + 1) * WIDE)
        part[:, columns] = matmul_nt(made[:, hidden:], wide_buf[j % 2]).astype(part.dtype)
        firsts.append(line.begin(j))
    for j in range(blocks):
        if j + 1 < blocks:
            fetch_down(j + 1).start()
        fetch_down(j).wait()
        ffn_part[:, j * WIDE : (j + 1) * WIDE] = matmul_nt(
            made[:, :hidden], down_buf[j % 2]
        ).astype(ffn_part.dtype)
        line.pass_on(j, firsts[j])
    normed_grad = line.total()
    rows = middle[...]
    scale = inverse_rms(rows)
    gain_grad[...] = jnp.sum(normed_grad * rows * scale, 0, keepdims=True)
    grad = group.own(ct)[...].astype(jnp.float32) + norm_back(
        normed_grad, rows, scale, gain[...].astype(jnp.float32)
    )
    middle_grad[...] = grad
    group.own(middle_low)[...] = grad.astype(middle_low.dtype)
    spread.run()
    half = gated_grad.shape[1] // 2
    share = out_first.shape[1]
    for side, shards in enumerate((out_first, out_last)):
        total = None
        for at in range(shards.shape[0] // half):
            one = matmul_nt(
                middle_low[:, at * share : (at + 1) * share],
                shards[at * half : (at + 1) * half, :],
            )
            total = one if total is None else total + one
        gated_grad[:, side * half : (side + 1) * half] = total
    if n_swaps:
        swap.end()


def ffn_back(call_id, made, ct, middle, gain, out_first, out_last, weights, arrays):
    count = group_size(("tp",))
    vmem = pl.BlockSpec(memory_space=pltpu.VMEM)
    hbm = pl.BlockSpec(memory_space=pltpu.HBM)
    rows, width = ct.shape
    hidden = made.shape[1] // 3
    inner = 2 * out_first.shape[0] // group_size(PLANE)
    low, full = jnp.bfloat16, jnp.float32
    part = jax.ShapeDtypeStruct((rows, width), low)
    dma = pltpu.SemaphoreType.DMA
    return pl.pallas_call(
        functools.partial(ffn_back_kernel, len(arrays)),
        in_specs=[vmem] * 6 + [hbm] + [vmem] * len(arrays),
        out_specs=[vmem] * 5 + [hbm] * len(arrays),
        out_shape=[
            part,
            jax.ShapeDtypeStruct((rows // count, width), full),
            jax.ShapeDtypeStruct((1, width), full),
            jax.ShapeDtypeStruct((rows, inner), full),
            part,
        ]
        + swap_shapes(arrays),
        scratch_shapes=[
            pltpu.VMEM(part.shape, low),
            pltpu.VMEM((2, WIDE, 2 * hidden), low),
            pltpu.VMEM((2, WIDE, hidden), low),
            dma((2,)),
            dma((2,)),
        ]
        + line_sum_scratch(part, width // WIDE)
        + line_spread_scratch()
        + swap_scratch(arrays),
        compiler_params=pltpu.CompilerParams(
            collective_id=call_id, has_side_effects=True, vmem_limit_bytes=VMEM_GRANT
        ),
    )(made, ct, middle, gain, out_first, out_last, weights, *arrays)


def send_on(source, target, send_sem, recv_sem, ctx):
    return pltpu.make_async_remote_copy(
        src_ref=source,
        dst_ref=target,
        send_sem=send_sem,
        recv_sem=recv_sem,
        device_id={"ctx": ctx},
        device_id_type=pl.DeviceIdType.MESH,
    )


def forward_pair_kernel(
    n_state,
    tiles,
    groups,
    blocks,
    seqs,
    step_ref,
    input_ref,
    brow_ref,
    crow_ref,
    rate_ref,
    shard,
    *refs,
):
    prior_ref, mixed_ref, gathered, *refs = refs
    carried, ends, starts, prior_buf, step_held, input_held, mixed_held, *refs = refs
    prior_sem, send_sem, recv_sem, gather_send, gather_recv, local_sem = refs
    place = lax.axis_index("ctx")
    gather = PlaneGather(shard, gathered, gather_send, gather_recv)
    greet([(PLANE, gather.others)])
    gather.begin(local_sem)

    def hand_on(seq):
        return send_on(ends.at[seq], starts.at[seq], send_sem.at[seq], recv_sem.at[seq], 1)

    def store(block):
        slot = lax.rem(block, 2)
        rows = groups * SUB
        return pltpu.make_async_copy(
            prior_buf.at[slot],
            prior_ref.at[pl.ds(pl.multiple_of(block * rows, rows), rows)],
            prior_sem.at[slot],
        )

    def one_sequence(seq):
        @pl.when(place == 0)
        def _():
            carried[...] = jnp.zeros_like(carried)

        @pl.when(place == 1)
        def _():
            hand_on(seq).wait_recv()
            carried[...] = starts[seq]

        @pl.loop(0, blocks)
        def _(inner_block):
            block = seq * blocks + inner_block
            slot = lax.rem(block, 2)

            @pl.when(block >= 2)
            def _():
                store(block - 2).wait()

            def one(turn, states):
                group = block * groups + turn
                states = list(states)
                stage_in(step_ref, group, step_held)
                stage_in(input_ref, group, input_held)
                for at in range(SUB):
                    step = token_row(step_held, at, tiles)
                    drive = step * token_row(input_held, at, tiles)
                    mixed = [None] * 2
                    for n in range(n_state):
                        where = (group * SUB + at) * n_state + n
                        prior_buf[slot, turn * SUB + at, n] = states[n]
                        decay = jnp.exp2(step * rate_ref[n])
                        states[n] = decay * states[n] + drive * brow_ref[where]
                        term = states[n] * crow_ref[where]
                        mixed[n % 2] = term if mixed[n % 2] is None else mixed[n % 2] + term
                    mixed_held[pl.ds(at, tiles, stride=SUB), :] = mixed[0] + mixed[1]
                stage_out(mixed_held, mixed_ref, group)
                return tuple(states)

            states = lax.fori_loop(0, groups, one, tuple(carried[n] for n in range(n_state)))
            for n in range(n_state):
                carried[n] = states[n]
            store(block).start()

        @pl.when(place == 0)
        def _():
            ends[seq] = carried[...]
            hand_on(seq).start()

    for seq in range(seqs):
        one_sequence(seq)
        if seq == 0:
            gather.relay()
            gather.hand_over()
    gather.hand_over_last()
    for block in range(max(0, seqs * blocks - 2), seqs * blocks):
        store(block).wait()

    @pl.when(place == 0)
    def _():
        for seq in range(seqs):
            hand_on(seq).wait_send()

    gather.end()


def scan_forward_pair(
    call_id, step, inputs, b_rows, c_rows, rate, seqs, shard
):
    n_state, tiles, _ = rate.shape
    tokens, inner = step.shape
    all_groups = tokens // SUB
    groups = math.gcd(all_groups // seqs, 4)
    blocks = all_groups // seqs // groups
    vmem = pl.BlockSpec(memory_space=pltpu.VMEM)
    smem = pl.BlockSpec(memory_space=pltpu.SMEM)
    hbm = pl.BlockSpec(memory_space=pltpu.HBM)
    full = jnp.float32
    held = pltpu.VMEM((tiles * SUB, LANE), full)
    boundary = pltpu.VMEM((seqs, n_state, tiles, LANE), full)
    dma = pltpu.SemaphoreType.DMA
    return pl.pallas_call(
        functools.partial(
            forward_pair_kernel, n_state, tiles, groups, blocks, seqs
        ),
        in_specs=[vmem, vmem, smem, smem, vmem, hbm],
        out_specs=[hbm, vmem, hbm],
        out_shape=[
            jax.ShapeDtypeStruct((tokens, n_state, tiles, LANE), full),
            jax.ShapeDtypeStruct(step.shape, full),
            gathered_shape(shard),
        ],
        scratch_shapes=[
            pltpu.VMEM((n_state, tiles, LANE), full),
            boundary,
            boundary,
            pltpu.VMEM((2, groups * SUB, n_state, tiles, LANE), full),
            held,
            held,
            held,
            dma((2,)),
            dma((seqs,)),
            dma((seqs,)),
        ]
        + gather_scratch(),
        compiler_params=pltpu.CompilerParams(
            collective_id=call_id, has_side_effects=True, vmem_limit_bytes=VMEM_GRANT
        ),
    )(step, inputs, b_rows, c_rows, rate, shard)


def backward_pair_kernel(
    n_swaps,
    n_state,
    tiles,
    groups,
    blocks,
    seqs,
    step_ref,
    input_ref,
    ograd_ref,
    brow_ref,
    crow_ref,
    rate_ref,
    picks_ref,
    ffn_part,
    middle,
    prior_ref,
    *refs,
):
    arrays, refs = refs[:n_swaps], refs[n_swaps:]
    step_grad_ref, input_grad_ref, rate_grad_ref, part_ref, *refs = refs
    layer_first, layer_last, *refs = refs
    swapped, refs = refs[:n_swaps], refs[n_swaps:]
    carried, ends, starts, prior_buf, step_held, input_held, ograd_held, *refs = refs
    step_grad_held, input_grad_held, ffn_slots, prior_sem, send_sem, recv_sem, *refs = refs
    tp_send, tp_recv, *refs = refs
    place = lax.axis_index("ctx")
    tp = Group(("tp",), tp_send, tp_recv)
    if n_swaps:
        swap = Swap(arrays, swapped, *refs)
        greet([(PLANE, swap.plane.others), (("tp",), tp.others)])
        swap.begin()
    else:
        greet([(("ctx",), [1 - place]), (("tp",), tp.others)])
    ffn_sent = tp.scatter(ffn_part, ffn_slots, 0)

    def hand_on(seq):
        return send_on(ends.at[seq], starts.at[seq], send_sem.at[seq], recv_sem.at[seq], 0)

    def fetch(turn):
        seq = lax.div(turn, blocks)
        block = seq * blocks + blocks - 1 - lax.rem(turn, blocks)
        slot = lax.rem(turn, 2)
        rows = groups * SUB
        return pltpu.make_async_copy(
            prior_ref.at[pl.ds(pl.multiple_of(block * rows, rows), rows)],
            prior_buf.at[slot],
            prior_sem.at[slot],
        )

    fetch(0).start()
    rate_grad_ref[...] = jnp.zeros_like(rate_grad_ref)

    @pl.when(place == 1)
    def _():
        @pl.loop(0, seqs)
        def _(seq):
            def one(turn, grads):
                group = (seq + 1) * blocks * groups - 1 - turn
                grads = list(grads)
                stage_in(step_ref, group, step_held)
                stage_in(ograd_ref, group, ograd_held)
                for at in range(SUB - 1, -1, -1):
                    step = token_row(step_held, at, tiles)
                    ograd = token_row(ograd_held, at, tiles)
                    for n in range(n_state):
                        row = crow_ref[(group * SUB + at) * n_state + n]
                        grads[n] = jnp.exp2(step * rate_ref[n]) * (grads[n] + ograd * row)
                return tuple(grads)

            zero = jnp.zeros((tiles, LANE), jnp.float32)
            grads = lax.fori_loop(0, blocks * groups, one, (zero,) * n_state)
            for n in range(n_state):
                ends[seq, n] = grads[n]
            hand_on(seq).start()

    @pl.loop(0, seqs)
    def _(seq):
        @pl.when(place == 1)
        def _():
            carried[...] = jnp.zeros_like(carried)

        @pl.when(place == 0)
        def _():
            hand_on(seq).wait_recv()
            carried[...] = starts[seq]

        @pl.loop(0, blocks)
        def _(inner_block):
            turn = seq * blocks + inner_block
            slot = lax.rem(turn, 2)
            first_group = (seq * blocks + blocks - 1 - inner_block) * groups

            @pl.when(turn + 1 < seqs * blocks)
            def _():
                fetch(turn + 1).start()

            fetch(turn).wait()

            def one(back, grads):
                inner_group = groups - 1 - back
                group = first_group + inner_group
                grads = list(grads)
                stage_in(step_ref, group, step_held)
                stage_in(input_ref, group, input_held)
                stage_in(ograd_ref, group, ograd_held)
                for at in range(SUB - 1, -1, -1):
                    step = token_row(step_held, at, tiles)
                    value = token_row(input_held, at, tiles)
                    ograd = token_row(ograd_held, at, tiles)
                    drive = step * value
                    along_b = None
                    along_rate = None
                    brow_parts, crow_parts = [], []
                    for n in range(n_state):
                        where = (group * SUB + at) * n_state + n
                        brow, crow = brow_ref[where], crow_ref[where]
                        rate = rate_ref[n]
                        decay = jnp.exp2(step * rate)
                        grad = ograd * crow + grads[n]
                        kept = decay * prior_buf[slot, inner_group * SUB + at, n]
                        state = kept + drive * brow
                        decay_term = grad * kept
                        grads[n] = decay * grad
                        rate_grad_ref[n] += decay_term * step
                        by_rate, by_brow = decay_term * rate, grad * brow
                        along_rate = by_rate if along_rate is None else along_rate + by_rate
                        along_b = by_brow if along_b is None else along_b + by_brow
                        brow_parts.append(grad * drive)
                        crow_parts.append(ograd * state)
                    step_grad_held[pl.ds(at, tiles, stride=SUB), :] = (
                        along_rate * LN2 + along_b * value
                    )
                    input_grad_held[pl.ds(at, tiles, stride=SUB), :] = along_b * step
                    parts = jnp.concatenate(brow_parts + crow_parts, 0).astype(jnp.bfloat16)
                    part_ref[group * SUB + at] = jnp.dot(
                        picks_ref[...], parts, preferred_element_type=jnp.float32
                    )
                stage_out(step_grad_held, step_grad_ref, group)
                stage_out(input_grad_held, input_grad_ref, group)
                return tuple(grads)

            grads = lax.fori_loop(0, groups, one, tuple(carried[n] for n in range(n_state)))
            for n in range(n_state):
                carried[n] = grads[n]

    finish(ffn_sent)
    layer_rows = (middle[...] + tp.total(ffn_part, ffn_slots)).astype(layer_first.dtype)
    half = layer_first.shape[1]
    layer_first[...], layer_last[...] = layer_rows[:, :half], layer_rows[:, half:]

    @pl.when(place == 1)
    def _():
        @pl.loop(0, seqs)
        def _(seq):
            hand_on(seq).wait_send()

    if n_swaps:
        swap.end()


def scan_backward_pair(
    call_id, prior, step, inputs, ograd, b_rows, c_rows, rate, seqs, ffn_part, middle, arrays
):
    n_state, tiles, _ = rate.shape
    tokens, inner = step.shape
    all_groups = tokens // SUB
    groups = math.gcd(all_groups // seqs, 4)
    blocks = all_groups // seqs // groups
    tp_count = group_size(("tp",))
    vmem = pl.BlockSpec(memory_space=pltpu.VMEM)
    smem = pl.BlockSpec(memory_space=pltpu.SMEM)
    hbm = pl.BlockSpec(memory_space=pltpu.HBM)
    full = jnp.float32
    held = pltpu.VMEM((tiles * SUB, LANE), full)
    boundary = pltpu.VMEM((seqs, n_state, tiles, LANE), full)
    dma = pltpu.SemaphoreType.DMA
    layer_half = jax.ShapeDtypeStruct((middle.shape[0], middle.shape[1] // 2), jnp.bfloat16)
    picks = jnp.repeat(jnp.eye(2 * n_state, dtype=jnp.bfloat16), tiles, 1)
    return pl.pallas_call(
        functools.partial(
            backward_pair_kernel, len(arrays), n_state, tiles, groups, blocks, seqs
        ),
        in_specs=[vmem] * 3 + [smem] * 2 + [vmem] * 4 + [hbm] + [vmem] * len(arrays),
        out_specs=[vmem] * 6 + [hbm] * len(arrays),
        out_shape=[
            jax.ShapeDtypeStruct(step.shape, full),
            jax.ShapeDtypeStruct(step.shape, full),
            jax.ShapeDtypeStruct(rate.shape, full),
            jax.ShapeDtypeStruct((tokens, 2 * n_state, LANE), full),
            layer_half,
            layer_half,
        ]
        + swap_shapes(arrays),
        scratch_shapes=[
            pltpu.VMEM((n_state, tiles, LANE), full),
            boundary,
            boundary,
            pltpu.VMEM((2, groups * SUB, n_state, tiles, LANE), full),
        ]
        + [held] * 5
        + [
            slots_for(ffn_part, tp_count),
            dma((2,)),
            dma((seqs,)),
            dma((seqs,)),
            dma((1, tp_count - 1)),
            dma((1, tp_count - 1)),
        ]
        + swap_scratch(arrays),
        compiler_params=pltpu.CompilerParams(
            collective_id=call_id, has_side_effects=True, vmem_limit_bytes=VMEM_GRANT
        ),
    )(step, inputs, ograd, b_rows, c_rows, rate, picks, ffn_part, middle, prior, *arrays)


class PlaneGather:
    def __init__(self, own, gathered, send_sem, recv_sem):
        self.own, self.gathered = own, gathered
        self.send_sem, self.recv_sem = send_sem, recv_sem
        self.dp, self.ctx = lax.axis_index("dp"), lax.axis_index("ctx")
        self.n_dp, self.n_ctx = lax.axis_size("dp"), lax.axis_size("ctx")
        self.hands_on = relayed()
        self.count = self.n_dp * self.n_ctx
        self.me = self.dp * self.n_ctx + self.ctx
        self.others = [lax.rem(self.me + hop, self.count) for hop in range(1, self.count)]
        self.copies = {}
        if self.hands_on:
            core = lax.rem(self.dp, 2)
            over_core = self.dp + 1 - 2 * core
            over_y = lax.rem(self.dp + 2, 4)
            over_x = 1 - self.ctx
            self.core = {"dp": over_core, "ctx": self.ctx}
            self.at_x = {"dp": self.dp, "ctx": over_x}
            self.at_y = {"dp": over_y, "ctx": self.ctx}
            self.from_x = self.dp * 2 + over_x
            self.from_y = over_y * 2 + self.ctx
            self.across = over_y * 2 + over_x

    def part(self, owner, half):
        rows = self.gathered.shape[0] // self.count
        start, size = owner * rows, rows
        if half is not None:
            size = rows // 2
            start = start + half * size
        return self.gathered.at[pl.ds(pl.multiple_of(start, size), size), :]

    def send(self, which, owner, half, where):
        target = self.part(owner, half)
        source = target
        if owner is self.me:
            rows = self.own.shape[0]
            source = self.own
            if half is not None:
                source = self.own.at[pl.ds(half * (rows // 2), rows // 2), :]
        self.copies[which] = sent(
            source, target, self.send_sem.at[which], self.recv_sem.at[which], where
        )

    def arrived(self, *which):
        for one in which:
            self.copies[one].wait_recv()

    def begin(self, local_sem):
        self.local = pltpu.make_async_copy(self.own, self.part(self.me, None), local_sem)
        self.local.start()
        if not self.hands_on:
            for hop, other in enumerate(self.others):
                self.send(hop, self.me, None, device_at(PLANE, other))
            return
        self.send(0, self.me, 1, self.at_x)
        self.send(1, self.me, 0, self.at_y)
        self.send(2, self.me, None, self.core)
        self.send(3, self.me, 0, self.at_x)
        self.send(4, self.me, 1, self.at_y)

    def relay(self):
        if not self.hands_on:
            return
        self.arrived(0, 1)
        self.send(5, self.from_x, 1, self.at_y)
        self.send(6, self.from_y, 0, self.at_x)
        self.send(7, self.from_x, 1, self.core)
        self.send(8, self.from_y, 0, self.core)

    def hand_over(self):
        if not self.hands_on:
            return
        self.arrived(3, 4)
        self.send(9, self.from_x, 0, self.core)
        self.send(10, self.from_y, 1, self.core)

    def hand_over_last(self):
        if not self.hands_on:
            return
        self.arrived(5, 6)
        self.send(11, self.across, 1, self.core)
        self.send(12, self.across, 0, self.core)

    def end(self):
        if self.hands_on:
            self.arrived(2, 7, 8, 9, 10, 11, 12)
        else:
            self.arrived(*range(self.count - 1))
        for copy in self.copies.values():
            copy.wait_send()
        self.local.wait()


def relayed():
    return lax.axis_size("dp") == 4 and lax.axis_size("ctx") == 2


def gather_sems():
    count = 13 if relayed() else group_size(PLANE) - 1
    return pltpu.SemaphoreType.DMA((count,))


WIDE = 512


def products(source, first, last, dot, target, block_buf, block_sem, out_buf, out_sem):
    def fetch(j, slot):
        columns = pl.ds(pl.multiple_of(j * WIDE, WIDE), WIDE)
        return pltpu.make_async_copy(
            source.at[:, columns], block_buf.at[slot], block_sem.at[slot]
        )

    def store(j, slot):
        return pltpu.make_async_copy(out_buf.at[slot], target(j), out_sem.at[slot])

    fetch(first, first % 2).start()

    @pl.loop(first, last)
    def _(j):
        slot = lax.rem(j, 2)

        @pl.when(j + 1 < last)
        def _():
            fetch(j + 1, 1 - slot).start()

        fetch(j, slot).wait()

        @pl.when(j >= first + 2)
        def _():
            store(j - 2, slot).wait()

        out_buf[slot] = dot(block_buf[slot])
        store(j, slot).start()

    for j in range(max(first, last - 2), last):
        store(j, j % 2).wait()


class PlaneSum:
    def __init__(self, array, total, *refs):
        self.array, self.result = array, total
        self.hands_on = relayed()
        if not self.hands_on:
            self.slots, send_sem, recv_sem = refs
            self.group = Group(PLANE, send_sem, recv_sem)
            return
        self.core_slot, self.pair, self.chip_slots, *self.sems = refs
        dp, ctx = lax.axis_index("dp"), lax.axis_index("ctx")
        self.half = lax.rem(dp, 2)
        self.other_core = {"dp": dp + 1 - 2 * self.half, "ctx": ctx}
        over_y, over_x = lax.rem(dp + 2, 4), 1 - ctx
        self.quarter = lax.div(dp, 2) * 2 + ctx
        self.chips = [
            ({"dp": a, "ctx": b}, lax.div(a, 2) * 2 + b)
            for a, b in ((dp, over_x), (over_y, ctx), (over_y, over_x))
        ]

    def to_core(self, source, target, which):
        core_send, core_recv = self.sems[:2]
        return sent(
            source, target, core_send.at[which], core_recv.at[which], self.other_core
        )

    def to_chip(self, source, target, which, at):
        chip_send, chip_recv = self.sems[2:]
        return sent(
            source,
            target,
            chip_send.at[which, at],
            chip_recv.at[which, at],
            self.chips[at][0],
        )

    def begin(self):
        if not self.hands_on:
            self.copies = self.group.scatter(self.array, self.slots, 0)
            return
        self.copies = [self.to_core(rows_of(self.array, 1 - self.half, 2), self.core_slot, 0)]

    def add_pair(self):
        if not self.hands_on:
            return
        finish(self.copies)
        self.pair[...] = (
            rows_of(self.array, self.half, 2)[...].astype(jnp.float32)
            + self.core_slot[...].astype(jnp.float32)
        ).astype(self.pair.dtype)
        self.copies = [
            self.to_chip(rows_of(self.pair, index, 4), self.chip_slots.at[at], 0, at)
            for at, (_, index) in enumerate(self.chips)
        ]

    def add_all(self):
        finish(self.copies)
        if not self.hands_on:
            self.group.own(self.result)[...] = self.group.total(self.array, self.slots).astype(
                self.result.dtype
            )
            self.copies = self.group.spread(self.result, 1)
            return
        total = rows_of(self.pair, self.quarter, 4)[...].astype(jnp.float32)
        for at in range(3):
            total = total + self.chip_slots[at].astype(jnp.float32)
        mine = rows_of(self.result, self.half * 4 + self.quarter, 8)
        mine[...] = total.astype(self.result.dtype)
        self.copies = [self.to_chip(mine, mine, 1, at) for at in range(3)]

    def hand_over(self):
        if not self.hands_on:
            return
        finish(self.copies)
        half = rows_of(self.result, self.half, 2)
        self.copies = [self.to_core(half, half, 1)]

    def end(self):
        finish(self.copies)


def plane_sum_scratch(array):
    dma = pltpu.SemaphoreType.DMA
    count = group_size(PLANE)
    if not relayed():
        return [slots_for(array, count), dma((2, count - 1)), dma((2, count - 1))]
    rows, width = array.shape
    return [
        pltpu.VMEM((rows // 2, width), array.dtype),
        pltpu.VMEM((rows // 2, width), array.dtype),
        pltpu.VMEM((3, rows // 8, width), array.dtype),
        dma((2,)),
        dma((2,)),
        dma((2, 3)),
        dma((2, 3)),
    ]


SMALL_ROWS = 32
GAIN_ROWS = 16


def tail_kernel(
    swaps,
    conv_grad,
    gate_grad,
    convkern,
    convbias,
    stepbias,
    decaylog,
    skipgain,
    ffngain,
    layer_first,
    layer_rows,
    middle_low,
    step_low,
    pre_low,
    select_low,
    scan_in,
    tokens,
    middle_grad,
    gain_row,
    in_conv,
    in_gate,
    one_cols,
    two_cols,
    ct_cols,
    middle_cols,
    ffn_all,
    gated_all,
    tokens_grad,
    layer_out,
    vectors_sum,
    step_sum,
    select_sum,
    gains,
    mix_all,
    grad_inproj,
    grad_outproj,
    grad_gateup,
    grad_downproj,
    mix_own,
    normed_part,
    small,
    small_sum,
    gain_slots,
    gain_own,
    vectors_own,
    cols,
    in_buf,
    block_buf,
    wide_buf,
    tall_buf,
    cols_sem,
    in_sem,
    block_sem,
    wide_sem,
    tall_sem,
    tp_send,
    tp_recv,
    gather_send,
    gather_recv,
    local_sem,
    *sems,
):
    inner = conv_grad.shape[1]
    hidden = ffn_all.shape[1] // 3
    width = tokens.shape[1]
    rank = step_low.shape[1]
    tp = Group(("tp",), tp_send, tp_recv)
    line = LineSum(normed_part, *sems[:5])
    tokens_spread = LineSpread(tokens_grad, *sems[5:7])
    layer_last = layer_out.at[:, width // 2 :]
    layer_spread = LineSpread(layer_last, *sems[7:9])
    count = 7 if relayed() else 3
    small_total = PlaneSum(small, small_sum, *sems[9 : 9 + count])
    swap_sems = sems[9 + count :]
    gather = PlaneGather(mix_own, mix_all, gather_send, gather_recv)
    sources = (one_cols, two_cols, ct_cols) if swaps else (one_cols, two_cols, ct_cols, middle_cols)
    loads = [
        pltpu.make_async_copy(source, cols.at[at], cols_sem.at[at])
        for at, source in enumerate(sources)
    ]
    if swaps:
        swap = Swap([middle_low], [cols.at[3]], *swap_sems)

    def fetch(j):
        slot = j % 2
        rows = slice(j * WIDE, (j + 1) * WIDE)
        return [
            pltpu.make_async_copy(source.at[rows, :], in_buf.at[slot, at], in_sem.at[slot, at])
            for at, source in enumerate((in_conv, in_gate))
        ]

    for copy in fetch(0) + loads:
        copy.start()
    mix_own[:, :inner] = conv_grad[...]
    mix_own[:, inner:] = gate_grad[...]
    greet([(("tp",), tp.others), (PLANE, gather.others)])
    gather.begin(local_sem)

    small[...] = jnp.zeros_like(small)
    vectors_own[...] = jnp.zeros_like(vectors_own)
    at = 0
    for vector in (convkern, convbias, stepbias, decaylog, skipgain):
        vectors_own[at : at + vector.shape[0], :] = vector[...]
        at += vector.shape[0]
    at = SMALL_ROWS - GAIN_ROWS + 10
    for row in range(width // inner):
        vectors_own[at + row : at + row + 1, :] = ffngain[:, row * inner : (row + 1) * inner]
    hidden_in = tokens[...].astype(jnp.float32)
    unit_rows = hidden_in * inverse_rms(hidden_in)
    blocks = width // WIDE
    firsts = []
    for j in range(blocks):
        if j + 1 < blocks:
            for copy in fetch(j + 1):
                copy.start()
        finish(fetch(j))
        columns = slice(j * WIDE, (j + 1) * WIDE)
        block = matmul_nt(conv_grad[...], in_buf[j % 2, 0]) + matmul_nt(
            gate_grad[...], in_buf[j % 2, 1]
        )
        normed_part[:, columns] = block.astype(normed_part.dtype)
        firsts.append(line.begin(j))
        gain_grad = jnp.sum(block * unit_rows[:, columns], 0, keepdims=True)
        if j:
            line.pass_on(j - 1, firsts[j - 1])
        row, at = divmod(j * WIDE, inner)
        row += SMALL_ROWS - GAIN_ROWS + 8
        vectors_own[row : row + 1, at : at + WIDE] = gain_grad
    layer_out[:, : width // 2] = layer_first[...]
    rows_of(layer_last, tp.me, tp.count)[...] = layer_rows[...]
    layer_spread.begin()
    small[:SMALL_ROWS, :] = vectors_own[...].astype(small.dtype)
    small[SMALL_ROWS : SMALL_ROWS + rank, :] = matmul_tn(step_low[...], pre_low[...]).astype(
        small.dtype
    )
    selected = select_sum.shape[0]
    small[SMALL_ROWS + rank : SMALL_ROWS + rank + selected, :] = matmul_tn(
        select_low[...], scan_in[...]
    )[:selected].astype(small.dtype)
    small_total.begin()
    line.pass_on(blocks - 1, firsts[-1])

    def flat(at):
        return lambda block: matmul_tn(cols[at], block)

    def tall(at):
        return lambda block: matmul_tn(block, cols[at])

    def side_by_side(ref, first):
        per = ref.shape[2] // WIDE

        def target(j):
            at = j - first
            columns = pl.ds(pl.multiple_of(lax.rem(at, per) * WIDE, WIDE), WIDE)
            return ref.at[lax.div(at, per), :, columns]

        return target

    def one_above_other(ref):
        return lambda j: ref.at[pl.ds(pl.multiple_of(j * WIDE, WIDE), WIDE), :]

    wide = (block_buf, block_sem, wide_buf, wide_sem)
    high = (block_buf, block_sem, tall_buf, tall_sem)
    down_end = hidden // WIDE
    gu_end = 3 * hidden // WIDE
    finish(loads)
    gu_middle = (down_end + gu_end) // 2
    to_gateup = side_by_side(grad_gateup, down_end)
    products(ffn_all, 0, down_end, tall(2), one_above_other(grad_downproj), *high)
    gather.relay()
    small_total.add_pair()
    products(ffn_all, down_end, gu_middle, flat(1), to_gateup, *wide)
    hidden_in = tp.own(tokens)[...].astype(jnp.float32)
    tp.own(tokens_grad)[...] = (
        middle_grad[...]
        + norm_back(
            line.total(),
            hidden_in,
            inverse_rms(hidden_in),
            gain_row[...].astype(jnp.float32),
        )
    ).astype(tokens_grad.dtype)
    tokens_spread.begin()
    layer_spread.pass_on()
    gather.hand_over()
    small_total.add_all()
    if swaps:
        swap.begin()
    products(ffn_all, gu_middle, gu_end, flat(1), to_gateup, *wide)
    gather.hand_over_last()
    small_total.hand_over()
    tokens_spread.pass_on()
    gather.end()
    products(mix_all, 0, 2 * inner // WIDE, flat(0), side_by_side(grad_inproj, 0), *wide)
    small_total.end()
    gain_own[...] = small_sum[SMALL_ROWS - GAIN_ROWS : SMALL_ROWS, :].astype(jnp.float32)
    gain_sent = [tp.one(gain_own, gain_slots.at[hop], 0, hop) for hop in range(tp.count - 1)]
    vectors_sum[...] = small_sum[:SMALL_ROWS, :].astype(jnp.float32)
    step_sum[...] = small_sum[SMALL_ROWS : SMALL_ROWS + rank, :].astype(jnp.float32)
    select_sum[...] = small_sum[SMALL_ROWS + rank : SMALL_ROWS + rank + selected, :].astype(
        jnp.float32
    )
    if swaps:
        swap.end()
    products(gated_all, 0, inner // WIDE, tall(3), one_above_other(grad_outproj), *high)
    finish(gain_sent)
    total = gain_own[...]
    for hop in range(tp.count - 1):
        total = total + gain_slots[hop]
    gains[...] = total
    tokens_spread.end()
    layer_spread.end()


def run_tail(
    call_id,
    selected,
    swaps,
    conv_grad,
    gate_grad,
    vectors,
    layer_first,
    layer_rows,
    middle_low,
    step_low,
    pre_low,
    select_low,
    scan_in,
    tokens,
    middle_grad,
    gain_row,
    in_conv,
    in_gate,
    one_cols,
    two_cols,
    ct_cols,
    middle_cols,
    ffn_all,
    gated_all,
):
    rows, inner = conv_grad.shape
    rank = step_low.shape[1]
    hidden = ffn_all.shape[1] // 3
    width = tokens.shape[1]
    share = one_cols.shape[1]
    all_rows = ffn_all.shape[0]
    tp_count, plane_count = group_size(("tp",)), group_size(PLANE)
    low, full = jnp.bfloat16, jnp.float32
    vmem = pl.BlockSpec(memory_space=pltpu.VMEM)
    hbm = pl.BlockSpec(memory_space=pltpu.HBM)
    dma = pltpu.SemaphoreType.DMA
    small_rows = SMALL_ROWS + rank + selected
    small = jax.ShapeDtypeStruct((small_rows + -small_rows % (16 * plane_count), inner), low)
    part = jax.ShapeDtypeStruct((rows, width), low)
    return pl.pallas_call(
        functools.partial(tail_kernel, swaps),
        in_specs=[vmem] * 18 + [hbm] * 8,
        out_specs=[vmem] * 6 + [hbm] * 5,
        out_shape=[
            jax.ShapeDtypeStruct(tokens.shape, low),
            jax.ShapeDtypeStruct(tokens.shape, low),
            jax.ShapeDtypeStruct((SMALL_ROWS, inner), full),
            jax.ShapeDtypeStruct((rank, inner), full),
            jax.ShapeDtypeStruct((selected, inner), full),
            jax.ShapeDtypeStruct((GAIN_ROWS, inner), full),
            jax.ShapeDtypeStruct((all_rows, 2 * inner), low),
            jax.ShapeDtypeStruct((2, share, inner), full),
            jax.ShapeDtypeStruct((inner, share), full),
            jax.ShapeDtypeStruct((2, share, hidden), full),
            jax.ShapeDtypeStruct((hidden, share), full),
        ],
        scratch_shapes=[
            pltpu.VMEM((rows, 2 * inner), low),
            pltpu.VMEM(part.shape, low),
            pltpu.VMEM(small.shape, low),
            pltpu.VMEM(small.shape, low),
            pltpu.VMEM((tp_count - 1, GAIN_ROWS, inner), full),
            pltpu.VMEM((GAIN_ROWS, inner), full),
            pltpu.VMEM((SMALL_ROWS, inner), full),
            pltpu.VMEM((4, all_rows, share), low),
            pltpu.VMEM((2, 2, WIDE, inner), low),
            pltpu.VMEM((2, all_rows, WIDE), low),
            pltpu.VMEM((2, share, WIDE), full),
            pltpu.VMEM((2, WIDE, share), full),
            dma((4,)),
            dma((2, 2)),
            dma((2,)),
            dma((2,)),
            dma((2,)),
            dma((1, tp_count - 1)),
            dma((1, tp_count - 1)),
        ]
        + gather_scratch()
        + line_sum_scratch(part, width // WIDE)
        + line_spread_scratch() * 2
        + plane_sum_scratch(small)
        + (swap_scratch([tokens]) if swaps else []),
        compiler_params=pltpu.CompilerParams(
            collective_id=call_id, has_side_effects=True, vmem_limit_bytes=VMEM_GRANT
        ),
    )(
        conv_grad,
        gate_grad,
        *vectors,
        layer_first,
        layer_rows,
        middle_low,
        step_low,
        pre_low,
        select_low,
        scan_in,
        tokens,
        middle_grad,
        gain_row,
        in_conv,
        in_gate,
        one_cols,
        two_cols,
        ct_cols,
        middle_cols,
        ffn_all,
        gated_all,
    )


BORDER = 16


def head_kernel(
    tokens,
    gain,
    in_conv,
    in_gate,
    conv_in,
    gate_mix,
    border,
    conv_all,
    gate_all,
    normed,
    block_buf,
    block_sem,
    border_send,
    border_recv,
    *sems,
):
    place, places = lax.axis_index("ctx"), lax.axis_size("ctx")
    seqs = border.shape[0] // BORDER
    span = conv_in.shape[0] // seqs

    def to_next(seq):
        return send_on(
            conv_in.at[pl.ds((seq + 1) * span - BORDER, BORDER), :],
            border.at[pl.ds(seq * BORDER, BORDER), :],
            border_send.at[seq],
            border_recv.at[seq],
            place + 1,
        )

    conv = PlaneGather(in_conv, conv_all, *sems[:2])
    gate = PlaneGather(in_gate, gate_all, *sems[3:5])
    greet([(PLANE, conv.others)])
    conv.begin(sems[2])
    gate.begin(sems[5])
    hidden_in = tokens[...].astype(jnp.float32)
    normed[...] = (hidden_in * inverse_rms(hidden_in) * gain[...].astype(jnp.float32)).astype(
        normed.dtype
    )
    conv.relay()
    conv.hand_over()
    gate.relay()
    conv.hand_over_last()
    gate.hand_over()
    conv.end()
    product_in_blocks(normed, conv_all, conv_in, block_buf, block_sem)

    @pl.when(place == 0)
    def _():
        border[...] = jnp.zeros_like(border)

    @pl.when(place < places - 1)
    def _():
        for seq in range(seqs):
            to_next(seq).start()

    gate.hand_over_last()
    gate.end()
    product_in_blocks(normed, gate_all, gate_mix, block_buf, block_sem)

    @pl.when(place < places - 1)
    def _():
        for seq in range(seqs):
            to_next(seq).wait_send()

    @pl.when(place > 0)
    def _():
        for seq in range(seqs):
            to_next(seq).wait_recv()


def run_head(call_id, tokens, gain, inproj, seqs):
    rows, width = tokens.shape
    inner = inproj.shape[2]
    low = jnp.bfloat16
    vmem = pl.BlockSpec(memory_space=pltpu.VMEM)
    hbm = pl.BlockSpec(memory_space=pltpu.HBM)
    return pl.pallas_call(
        head_kernel,
        in_specs=[vmem] * 2 + [hbm] * 2,
        out_specs=[vmem] * 3 + [hbm] * 2,
        out_shape=[
            jax.ShapeDtypeStruct((rows, inner), low),
            jax.ShapeDtypeStruct((rows, inner), jnp.float32),
            jax.ShapeDtypeStruct((seqs * BORDER, inner), low),
            jax.ShapeDtypeStruct((width, inner), low),
            jax.ShapeDtypeStruct((width, inner), low),
        ],
        scratch_shapes=[
            pltpu.VMEM((rows, width), low),
            pltpu.VMEM((2, width, WIDE), low),
            pltpu.SemaphoreType.DMA((2,)),
            pltpu.SemaphoreType.DMA((seqs,)),
            pltpu.SemaphoreType.DMA((seqs,)),
        ]
        + gather_scratch() * 2,
        compiler_params=pltpu.CompilerParams(
            collective_id=call_id, has_side_effects=True, vmem_limit_bytes=VMEM_GRANT
        ),
    )(tokens, gain, inproj[0], inproj[1])


def per_device(
    tokens,
    mixgain,
    inproj,
    convkern,
    convbias,
    selproj,
    stepproj,
    stepbias,
    decaylog,
    skipgain,
    outproj,
    ffngain,
    gateup,
    downproj,
    cotangent,
):
    seqs, span, width = tokens.shape
    rows = seqs * span
    taps, inner = convkern.shape
    rank = stepproj.shape[0]
    n_state = decaylog.shape[1]
    tiles = inner // LANE
    gain_mix = mixgain.astype(jnp.float32)
    kernel = convkern.astype(jnp.float32)
    kernel_bias = convbias.astype(jnp.float32)
    step_bias = stepbias.astype(jnp.float32)
    skip_weight = skipgain.astype(jnp.float32)
    decay_rate = -jnp.exp(jnp.transpose(decaylog.astype(jnp.float32)))
    rate = (decay_rate * LOG2E).reshape(n_state, tiles, LANE)

    gain_mix_row, gain_ffn_row = mixgain.reshape(1, width), ffngain.reshape(1, width)
    low = jnp.bfloat16

    tokens_rows = tokens.reshape(rows, width)
    ct_low = cotangent.reshape(rows, width)
    swap_now = swaps_in_kernels(width)
    out_first = gathered_rows(outproj[: inner // 2])
    ffn_pack = gathered_rows(
        jnp.concatenate([gateup[0], gateup[1], jnp.transpose(downproj)], 1)
    )
    conv_in, gate_mix, border, in_conv, in_gate = run_head(
        5, tokens_rows, gain_mix_row, inproj, seqs
    )
    hidden_in = tokens_rows.astype(jnp.float32)
    scale_one = inverse_rms(hidden_in)
    normed_one = (hidden_in * scale_one * gain_mix).astype(low)

    conv_seqs = conv_in.reshape(seqs, span, inner)
    rim_rows = border.reshape(seqs, BORDER, inner)[:, BORDER - (taps - 1) :]
    padded_in = jnp.concatenate([rim_rows, conv_seqs], 1).astype(jnp.float32)
    conv_out = kernel_bias[None, None]
    for offset in range(taps):
        conv_out = conv_out + kernel[offset][None, None] * padded_in[:, offset : offset + span]
    conv_out = conv_out.reshape(rows, inner)
    scan_in = jax.nn.silu(conv_out).astype(low)
    scan_float = scan_in.astype(jnp.float32)
    columns = selproj.shape[1]
    select_width = -(-columns // LANE) * LANE
    select_weights = jnp.pad(selproj, ((0, 0), (0, select_width - columns)))
    select_cols = run_select(0, matmul(scan_in, select_weights))

    def columns_of(swapped, array):
        if not swapped:
            return swapped_columns(array)
        return swapped[0].reshape(-1, swapped[0].shape[-1])

    step_low = select_cols[:, :rank].astype(low)
    b_rows = select_cols[:, rank : rank + n_state].reshape(-1)
    c_rows = select_cols[:, rank + n_state : columns].reshape(-1)
    step_pre = matmul(step_low, stepproj) + step_bias[None]
    step_size = jax.nn.softplus(step_pre)
    in_pairs = lax.axis_size("ctx") == 2
    if in_pairs:
        prior, scan_out, out_last = scan_forward_pair(
            6,
            step_size,
            scan_float,
            b_rows,
            c_rows,
            rate,
            seqs,
            outproj[inner // 2 :],
        )
    else:
        span_decay = jnp.exp(
            decay_rate[None] * jnp.sum(step_size.reshape(seqs, span, inner), 1)[:, None]
        ).reshape(seqs, n_state, tiles, LANE)
        ends = scan_ends(step_size, scan_float, b_rows, rate, seqs, False)
        start = from_earlier(ends, span_decay, 1)
        prior, scan_out = scan_forward(start, step_size, scan_float, b_rows, c_rows, rate, seqs)
        out_last = gathered_rows(outproj[inner // 2 :])
    mixer_core = scan_out + skip_weight[None] * scan_float
    gate_sig = jax.nn.silu(gate_mix)
    gated = (mixer_core * gate_sig).astype(low)
    normed_two, middle, gated_all = mixer_out(
        1,
        gated,
        out_first,
        out_last,
        tokens_rows,
        gain_ffn_row,
        [],
    )
    to_swap = [ct_low, normed_one] if swap_now else []
    made, *swapped = run_ffn(8, normed_two, ct_low, ffn_pack, to_swap)
    ct_cols = columns_of(swapped[:1], ct_low)
    normed_one_cols = columns_of(swapped[1:], normed_one)
    ffn_all = gathered_rows(made)
    middle_low, middle_grad, ffngain_part, gated_grad, ffn_part, *swapped = ffn_back(
        2,
        made,
        ct_low,
        middle,
        gain_ffn_row,
        out_first,
        out_last,
        ffn_pack,
        [normed_two] if swap_now else [],
    )
    normed_two_cols = columns_of(swapped, normed_two)
    core_grad = gated_grad * gate_sig
    gate_mix_grad = (gated_grad * mixer_core * silu_slope(gate_mix)).astype(low)
    grad_skipgain = jnp.sum(core_grad * scan_float, 0)
    if in_pairs:
        step_grad, input_grad, rate_grad, parts, *layer_rows = scan_backward_pair(
            7,
            prior,
            step_size,
            scan_float,
            core_grad,
            b_rows,
            c_rows,
            rate,
            seqs,
            ffn_part,
            middle,
            [],
        )
    else:
        back_ends = scan_ends(step_size, core_grad, c_rows, rate, seqs, True)
        end_grad = from_earlier(back_ends, span_decay, -1)
        step_grad, input_grad, rate_grad, parts = scan_backward(
            end_grad, prior, step_size, scan_float, core_grad, b_rows, c_rows, rate, seqs
        )
        ffn_sum = lax.psum_scatter(ffn_part, "tp", scatter_dimension=0, tiled=True)
        layer_rows = jnp.split((middle + ffn_sum.astype(jnp.float32)).astype(low), 2, 1)
    grad_decaylog = rate_grad.reshape(n_state, inner) * decay_rate
    pre_grad = step_grad * jax.nn.sigmoid(step_pre)
    grad_stepbias = jnp.sum(pre_grad, 0)
    pre_low = pre_grad.astype(low)
    select_part = jnp.concatenate(
        [
            matmul_nt(pre_low, stepproj),
            jnp.sum(parts, -1),
            jnp.zeros((rows, select_width - columns), jnp.float32),
        ],
        1,
    ).astype(low)
    select_low, layer_first = sum_over_tp(3, select_part, layer_rows[0])
    scan_in_grad = (
        core_grad * skip_weight[None]
        + input_grad
        + matmul_nt(select_low, select_weights)
    )
    conv_grad = scan_in_grad * silu_slope(conv_out)
    grad_convbias = jnp.sum(conv_grad, 0)
    conv_grad_seqs = conv_grad.reshape(seqs, span, inner)
    padded_grad = jnp.zeros(padded_in.shape, jnp.float32)
    kernel_rows = []
    for offset in range(taps):
        kernel_rows.append(jnp.sum(conv_grad_seqs * padded_in[:, offset : offset + span], (0, 1)))
        padded_grad = padded_grad + jnp.pad(
            kernel[offset][None, None] * conv_grad_seqs,
            ((0, 0), (offset, taps - 1 - offset), (0, 0)),
        )
    grad_convkern = jnp.stack(kernel_rows)
    returned = passed_along(padded_grad[:, : taps - 1], "ctx", -1)
    conv_in_grad = (
        (padded_grad[:, taps - 1 :] + jnp.pad(returned, ((0, 0), (span - taps + 1, 0), (0, 0))))
        .astype(low)
        .reshape(rows, inner)
    )
    vectors = [
        grad_convkern,
        grad_convbias[None],
        grad_stepbias[None],
        grad_decaylog,
        grad_skipgain[None],
        ffngain_part,
    ]
    (
        tokens_grad,
        layer_out,
        vectors,
        grad_stepproj,
        grad_selproj,
        gains,
        _,
        grad_inproj,
        grad_outproj,
        grad_gateup,
        grad_downproj,
    ) = run_tail(
        4,
        columns,
        swap_now,
        conv_in_grad,
        gate_mix_grad,
        vectors,
        layer_first,
        layer_rows[1],
        middle_low,
        step_low,
        pre_low,
        select_low,
        scan_in,
        tokens_rows,
        middle_grad,
        gain_mix_row,
        in_conv,
        in_gate,
        normed_one_cols,
        normed_two_cols,
        ct_cols,
        normed_two_cols if swap_now else swapped_columns(middle_low),
        ffn_all,
        gated_all,
    )
    at = taps + 2
    return (
        layer_out.reshape(tokens.shape),
        tokens_grad.reshape(tokens.shape),
        gains[8:10].reshape(width),
        grad_inproj,
        vectors[:taps],
        vectors[taps],
        jnp.transpose(grad_selproj),
        grad_stepproj,
        vectors[taps + 1],
        jnp.transpose(vectors[at : at + n_state]),
        vectors[at + n_state],
        grad_outproj,
        gains[10:12].reshape(width),
        grad_gateup,
        grad_downproj,
    )


def solution(mesh):
    in_specs = (
        P("dp", "ctx", None),
        P(),
        P(None, ("dp", "ctx"), "tp"),
        P(None, "tp"),
        P("tp"),
        P("tp", None),
        P(None, "tp"),
        P("tp"),
        P("tp", None),
        P("tp"),
        P("tp", ("dp", "ctx")),
        P(),
        P(None, ("dp", "ctx"), "tp"),
        P("tp", ("dp", "ctx")),
        P("dp", "ctx", None),
    )
    out_specs = (
        P("dp", "ctx", None),
        P("dp", "ctx", None),
        P(),
        P(None, ("dp", "ctx"), "tp"),
        P(None, "tp"),
        P("tp"),
        P("tp", None),
        P(None, "tp"),
        P("tp"),
        P("tp", None),
        P("tp"),
        P("tp", ("dp", "ctx")),
        P(),
        P(None, ("dp", "ctx"), "tp"),
        P("tp", ("dp", "ctx")),
    )
    return jax.shard_map(
        per_device, mesh=mesh, in_specs=in_specs, out_specs=out_specs, check_vma=False
    )
```

```python
import functools
import math

import jax
import jax.numpy as jnp
from jax import lax
from jax.experimental import pallas as pl
from jax.experimental.pallas import tpu as pltpu
from jax.sharding import PartitionSpec as P

EPSILON = 1e-05
LOG2E = math.log2(math.e)
LN2 = math.log(2.0)
SUB = 8
LANE = 128
VMEM_GRANT = 60 * 2**20
PLANE = ("dp", "ctx")


def passed_along(value, axis, steps):
    count = lax.axis_size(axis)
    first, last = (max(0, -steps), min(count, count - steps))
    return lax.ppermute(value, axis, [(source, source + steps) for source in range(first, last)])


def matmul(left, right):
    return jnp.dot(left, right, preferred_element_type=jnp.float32)


def matmul_nt(left, right):
    return lax.dot_general(
        left, right, (((1,), (1,)), ((), ())), preferred_element_type=jnp.float32
    )


def matmul_tn(left, right):
    return lax.dot_general(
        left, right, (((0,), (0,)), ((), ())), preferred_element_type=jnp.float32
    )


def inverse_rms(values):
    return lax.rsqrt(jnp.mean(values * values, -1, keepdims=True) + EPSILON)


def silu_slope(values):
    logistic = jax.nn.sigmoid(values)
    return logistic * (1.0 + values * (1.0 - logistic))


def norm_back(grad_norm, values, scale, gain):
    scaled_grad = grad_norm * gain
    unit_rows = values * scale
    return scale * (scaled_grad - unit_rows * jnp.mean(scaled_grad * unit_rows, -1, keepdims=True))


def stage_in(ref, group, held):
    for tile in range(held.shape[0] // SUB):
        held[pl.ds(tile * SUB, SUB), :] = ref[
            pl.ds(pl.multiple_of(group * SUB, SUB), SUB), pl.ds(tile * LANE, LANE)
        ]


def stage_out(held, ref, group):
    for tile in range(held.shape[0] // SUB):
        ref[pl.ds(pl.multiple_of(group * SUB, SUB), SUB), pl.ds(tile * LANE, LANE)] = held[
            pl.ds(tile * SUB, SUB), :
        ]


def token_row(held, at, tiles):
    return held[pl.ds(at, tiles, stride=SUB), :]


def ends_kernel(
    n_state,
    tiles,
    groups,
    reverse,
    step_ref,
    drive_ref,
    rows_ref,
    rate_ref,
    end_ref,
    step_held,
    drive_held,
):
    base = pl.program_id(0) * groups * SUB * n_state
    rates = [rate_ref[n] for n in range(n_state)]

    def one(turn, states):
        group = groups - 1 - turn if reverse else turn
        order = range(SUB - 1, -1, -1) if reverse else range(SUB)
        states = list(states)
        stage_in(step_ref, group, step_held)
        stage_in(drive_ref, group, drive_held)
        for at in order:
            step = token_row(step_held, at, tiles)
            drive = token_row(drive_held, at, tiles)
            if not reverse:
                drive = drive * step
            for n in range(n_state):
                row = rows_ref[base + (group * SUB + at) * n_state + n]
                decay = jnp.exp2(step * rates[n])
                if reverse:
                    states[n] = decay * (states[n] + drive * row)
                else:
                    states[n] = decay * states[n] + drive * row
        return tuple(states)

    zero = jnp.zeros((tiles, LANE), jnp.float32)
    states = lax.fori_loop(0, groups, one, (zero,) * n_state)
    for n in range(n_state):
        end_ref[0, n] = states[n]


def scan_ends(step, drive, rows, rate, seqs, reverse):
    n_state, tiles, _ = rate.shape
    groups = step.shape[0] // seqs // SUB
    rows_spec = pl.BlockSpec((groups * SUB, tiles * LANE), lambda s: (s, 0))
    held = pltpu.VMEM((tiles * SUB, LANE), jnp.float32)
    return pl.pallas_call(
        functools.partial(ends_kernel, n_state, tiles, groups, reverse),
        grid=(seqs,),
        in_specs=[
            rows_spec,
            rows_spec,
            pl.BlockSpec(memory_space=pltpu.SMEM),
            pl.BlockSpec((n_state, tiles, LANE), lambda s: (0, 0, 0)),
        ],
        out_specs=pl.BlockSpec((1, n_state, tiles, LANE), lambda s: (s, 0, 0, 0)),
        out_shape=jax.ShapeDtypeStruct((seqs, n_state, tiles, LANE), jnp.float32),
        scratch_shapes=[held, held],
        compiler_params=pltpu.CompilerParams(vmem_limit_bytes=VMEM_GRANT),
    )(step, drive, rows, rate)


def forward_kernel(
    n_state,
    tiles,
    groups,
    blocks,
    start_ref,
    step_ref,
    input_ref,
    brow_ref,
    crow_ref,
    rate_ref,
    prior_ref,
    mixed_ref,
    carried,
    step_held,
    input_held,
    mixed_held,
):
    base = (pl.program_id(0) * blocks + pl.program_id(1)) * groups * SUB * n_state

    @pl.when(pl.program_id(1) == 0)
    def _():
        carried[...] = start_ref[0]

    def one(group, states):
        states = list(states)
        stage_in(step_ref, group, step_held)
        stage_in(input_ref, group, input_held)
        for at in range(SUB):
            step = token_row(step_held, at, tiles)
            drive = step * token_row(input_held, at, tiles)
            mixed = [None] * 2
            for n in range(n_state):
                where = base + (group * SUB + at) * n_state + n
                prior_ref[group * SUB + at, n] = states[n]
                decay = jnp.exp2(step * rate_ref[n])
                states[n] = decay * states[n] + drive * brow_ref[where]
                term = states[n] * crow_ref[where]
                mixed[n % 2] = term if mixed[n % 2] is None else mixed[n % 2] + term
            mixed_held[pl.ds(at, tiles, stride=SUB), :] = mixed[0] + mixed[1]
        stage_out(mixed_held, mixed_ref, group)
        return tuple(states)

    states = lax.fori_loop(0, groups, one, tuple(carried[n] for n in range(n_state)))
    for n in range(n_state):
        carried[n] = states[n]


def scan_forward(start, step, inputs, b_rows, c_rows, rate, seqs):
    n_state, tiles, _ = rate.shape
    all_groups = step.shape[0] // SUB
    groups = math.gcd(all_groups // seqs, 4)
    blocks = all_groups // seqs // groups
    rows_spec = pl.BlockSpec((groups * SUB, tiles * LANE), lambda s, b: (s * blocks + b, 0))
    held = pltpu.VMEM((tiles * SUB, LANE), jnp.float32)
    smem = pl.BlockSpec(memory_space=pltpu.SMEM)
    tokens = all_groups * SUB
    return pl.pallas_call(
        functools.partial(forward_kernel, n_state, tiles, groups, blocks),
        grid=(seqs, blocks),
        in_specs=[
            pl.BlockSpec((1, n_state, tiles, LANE), lambda s, b: (s, 0, 0, 0)),
            rows_spec,
            rows_spec,
            smem,
            smem,
            pl.BlockSpec((n_state, tiles, LANE), lambda s, b: (0, 0, 0)),
        ],
        out_specs=[
            pl.BlockSpec(
                (groups * SUB, n_state, tiles, LANE), lambda s, b: (s * blocks + b, 0, 0, 0)
            ),
            rows_spec,
        ],
        out_shape=[
            jax.ShapeDtypeStruct((tokens, n_state, tiles, LANE), jnp.float32),
            jax.ShapeDtypeStruct(step.shape, jnp.float32),
        ],
        scratch_shapes=[pltpu.VMEM((n_state, tiles, LANE), jnp.float32)] + [held] * 3,
        compiler_params=pltpu.CompilerParams(vmem_limit_bytes=VMEM_GRANT),
    )(start, step, inputs, b_rows, c_rows, rate)


def backward_kernel(
    n_state,
    tiles,
    groups,
    blocks,
    end_ref,
    prior_ref,
    step_ref,
    input_ref,
    ograd_ref,
    brow_ref,
    crow_ref,
    rate_ref,
    picks_ref,
    step_grad_ref,
    input_grad_ref,
    rate_grad_ref,
    part_ref,
    carried,
    step_held,
    input_held,
    ograd_held,
    step_grad_held,
    input_grad_held,
):
    block = blocks - 1 - pl.program_id(1)
    base = (pl.program_id(0) * blocks + block) * groups * SUB * n_state

    @pl.when(pl.program_id(1) == 0)
    def _():
        carried[...] = end_ref[0]

    @pl.when((pl.program_id(0) == 0) & (pl.program_id(1) == 0))
    def _():
        rate_grad_ref[...] = jnp.zeros_like(rate_grad_ref)

    def one(turn, grads):
        group = groups - 1 - turn
        grads = list(grads)
        stage_in(step_ref, group, step_held)
        stage_in(input_ref, group, input_held)
        stage_in(ograd_ref, group, ograd_held)
        for at in range(SUB - 1, -1, -1):
            step = token_row(step_held, at, tiles)
            value = token_row(input_held, at, tiles)
            ograd = token_row(ograd_held, at, tiles)
            drive = step * value
            along_b = None
            along_rate = None
            brow_parts, crow_parts = [], []
            for n in range(n_state):
                where = base + (group * SUB + at) * n_state + n
                brow, crow = brow_ref[where], crow_ref[where]
                rate = rate_ref[n]
                decay = jnp.exp2(step * rate)
                grad = ograd * crow + grads[n]
                kept = decay * prior_ref[group * SUB + at, n]
                state = kept + drive * brow
                decay_term = grad * kept
                grads[n] = decay * grad
                rate_grad_ref[n] += decay_term * step
                by_rate, by_brow = decay_term * rate, grad * brow
                along_rate = by_rate if along_rate is None else along_rate + by_rate
                along_b = by_brow if along_b is None else along_b + by_brow
                brow_parts.append(grad * drive)
                crow_parts.append(ograd * state)
            step_grad_held[pl.ds(at, tiles, stride=SUB), :] = along_rate * LN2 + along_b * value
            input_grad_held[pl.ds(at, tiles, stride=SUB), :] = along_b * step
            parts = jnp.concatenate(brow_parts + crow_parts, 0).astype(jnp.bfloat16)
            part_ref[group * SUB + at] = jnp.dot(
                picks_ref[...], parts, preferred_element_type=jnp.float32
            )
        stage_out(step_grad_held, step_grad_ref, group)
        stage_out(input_grad_held, input_grad_ref, group)
        return tuple(grads)

    grads = lax.fori_loop(0, groups, one, tuple(carried[n] for n in range(n_state)))
    for n in range(n_state):
        carried[n] = grads[n]


def scan_backward(end_grad, prior, step, inputs, ograd, b_rows, c_rows, rate, seqs):
    n_state, tiles, _ = rate.shape
    all_groups = step.shape[0] // SUB
    groups = math.gcd(all_groups // seqs, 4)
    blocks = all_groups // seqs // groups

    def at(s, b):
        return s * blocks + blocks - 1 - b

    rows_spec = pl.BlockSpec((groups * SUB, tiles * LANE), lambda s, b: (at(s, b), 0))
    held = pltpu.VMEM((tiles * SUB, LANE), jnp.float32)
    smem = pl.BlockSpec(memory_space=pltpu.SMEM)
    tokens = all_groups * SUB
    picks = jnp.repeat(jnp.eye(2 * n_state, dtype=jnp.bfloat16), tiles, 1)
    return pl.pallas_call(
        functools.partial(backward_kernel, n_state, tiles, groups, blocks),
        grid=(seqs, blocks),
        in_specs=[
            pl.BlockSpec((1, n_state, tiles, LANE), lambda s, b: (s, 0, 0, 0)),
            pl.BlockSpec((groups * SUB, n_state, tiles, LANE), lambda s, b: (at(s, b), 0, 0, 0)),
            rows_spec,
            rows_spec,
            rows_spec,
            smem,
            smem,
            pl.BlockSpec((n_state, tiles, LANE), lambda s, b: (0, 0, 0)),
            pl.BlockSpec(picks.shape, lambda s, b: (0, 0)),
        ],
        out_specs=[
            rows_spec,
            rows_spec,
            pl.BlockSpec((n_state, tiles, LANE), lambda s, b: (0, 0, 0)),
            pl.BlockSpec((groups * SUB, 2 * n_state, LANE), lambda s, b: (at(s, b), 0, 0)),
        ],
        out_shape=[
            jax.ShapeDtypeStruct(step.shape, jnp.float32),
            jax.ShapeDtypeStruct(step.shape, jnp.float32),
            jax.ShapeDtypeStruct(rate.shape, jnp.float32),
            jax.ShapeDtypeStruct((tokens, 2 * n_state, LANE), jnp.float32),
        ],
        scratch_shapes=[pltpu.VMEM((n_state, tiles, LANE), jnp.float32)] + [held] * 5,
        compiler_params=pltpu.CompilerParams(vmem_limit_bytes=VMEM_GRANT),
    )(end_grad, prior, step, inputs, ograd, b_rows, c_rows, rate, picks)


def from_earlier(ends, decay, steps):
    count = lax.axis_size("ctx")
    if count == 1:
        return jnp.zeros_like(ends)
    if count == 2:
        return passed_along(ends, "ctx", steps)
    index = lax.axis_index("ctx")
    all_ends = lax.all_gather(ends, "ctx")
    all_decays = lax.all_gather(decay, "ctx")

    def one(turn, state):
        at = turn if steps > 0 else count - 1 - turn
        reached = at < index if steps > 0 else at > index
        return jnp.where(reached, all_decays[at] * state + all_ends[at], state)

    return lax.fori_loop(0, count, one, jnp.zeros_like(ends))


def gathered_rows(rows):
    return lax.all_gather(rows, PLANE, axis=0, tiled=True)


def swapped_columns(rows):
    return lax.all_to_all(rows, PLANE, split_axis=1, concat_axis=0, tiled=True)


def place_in(axes):
    index = 0
    for axis in axes:
        index = index * lax.axis_size(axis) + lax.axis_index(axis)
    return index


def device_at(axes, index):
    where = {}
    for axis in reversed(axes):
        size = lax.axis_size(axis)
        where[axis] = lax.rem(index, size)
        index = lax.div(index, size)
    return where


def greet(groups):
    barrier = pltpu.get_barrier_semaphore()
    total = 0
    for axes, others in groups:
        for other in others:
            pl.semaphore_signal(
                barrier,
                inc=1,
                device_id=device_at(axes, other),
                device_id_type=pl.DeviceIdType.MESH,
            )
            total += 1
    pl.semaphore_wait(barrier, total)


def sent(source, target, send_sem, recv_sem, where):
    copy = pltpu.make_async_remote_copy(
        src_ref=source,
        dst_ref=target,
        send_sem=send_sem,
        recv_sem=recv_sem,
        device_id=where,
        device_id_type=pl.DeviceIdType.MESH,
    )
    copy.start()
    return copy


def finish(copies):
    for copy in copies:
        copy.wait()


def rows_of(ref, index, count):
    rows = ref.shape[0] // count
    return ref.at[pl.ds(pl.multiple_of(index * rows, rows), rows), :]


class Group:
    def __init__(self, axes, send_sem, recv_sem):
        self.axes = axes
        self.count = math.prod(lax.axis_size(axis) for axis in axes)
        self.me = place_in(axes)
        self.others = [lax.rem(self.me + hop, self.count) for hop in range(1, self.count)]
        self.send_sem, self.recv_sem = send_sem, recv_sem

    def own(self, ref):
        return rows_of(ref, self.me, self.count)

    def one(self, source, target, which, hop):
        return sent(
            source,
            target,
            self.send_sem.at[which, hop],
            self.recv_sem.at[which, hop],
            device_at(self.axes, self.others[hop]),
        )

    def scatter(self, part, slot, which):
        return [
            self.one(rows_of(part, other, self.count), slot.at[hop], which, hop)
            for hop, other in enumerate(self.others)
        ]

    def total(self, part, slot):
        total = self.own(part)[...].astype(jnp.float32)
        for hop in range(self.count - 1):
            total = total + slot[hop].astype(jnp.float32)
        return total

    def spread(self, ref, which):
        return [self.one(self.own(ref), self.own(ref), which, hop) for hop in range(self.count - 1)]


def slots_for(part, count):
    return pltpu.VMEM((count - 1, part.shape[0] // count) + part.shape[1:], part.dtype)


def group_size(axes):
    return math.prod(lax.axis_size(axis) for axis in axes)


def line_of_four():
    me = lax.axis_index("tp")
    near = me + 1 - 2 * lax.rem(me, 2)
    return me, near, lax.rem(me + 2, 4), lax.rem(near + 2, 4)


class LineSum:
    def __init__(self, part, near_slots, far_slot, passed, send_sem, recv_sem):
        self.part, self.near_slots, self.far_slot = part, near_slots, far_slot
        self.passed, self.send_sem, self.recv_sem = passed, send_sem, recv_sem
        self.me, self.near, self.far, self.cross = line_of_four()
        self.blocks = send_sem.shape[1]
        self.copies = []

    def columns(self, j):
        wide = self.part.shape[1] // self.blocks
        return slice(j * wide, (j + 1) * wide)

    def rows(self, index):
        return rows_of(self.part, index, 4)

    def send(self, source, target, which, j, where):
        copy = sent(
            source.at[:, self.columns(j)],
            target.at[:, self.columns(j)],
            self.send_sem.at[which, j],
            self.recv_sem.at[which, j],
            {"tp": where},
        )
        self.copies.append((which, copy))
        return copy

    def begin(self, j):
        first = self.send(self.rows(self.cross), self.near_slots.at[0], 0, j, self.near)
        self.send(self.rows(self.near), self.near_slots.at[1], 1, j, self.near)
        return first

    def pass_on(self, j, first):
        first.wait_recv()
        columns = self.columns(j)
        self.passed[:, columns] = (
            self.rows(self.far)[:, columns].astype(jnp.float32)
            + self.near_slots[0, :, columns].astype(jnp.float32)
        ).astype(self.passed.dtype)
        self.send(self.passed, self.far_slot, 2, j, self.far)

    def total(self):
        for which, copy in self.copies:
            copy.wait_send()
            if which:
                copy.wait_recv()
        return (
            self.rows(self.me)[...].astype(jnp.float32)
            + self.near_slots[1].astype(jnp.float32)
            + self.far_slot[...].astype(jnp.float32)
        )

    def pass_all(self, firsts):
        for j, first in enumerate(firsts):
            self.pass_on(j, first)


def line_sum_scratch(part, blocks):
    share = (part.shape[0] // 4,) + part.shape[1:]
    sems = pltpu.SemaphoreType.DMA((3, blocks))
    return [
        pltpu.VMEM((2,) + share, part.dtype),
        pltpu.VMEM(share, part.dtype),
        pltpu.VMEM(share, part.dtype),
        sems,
        sems,
    ]


class LineSpread:
    def __init__(self, ref, send_sem, recv_sem):
        self.ref, self.send_sem, self.recv_sem = ref, send_sem, recv_sem
        self.me, self.near, self.far, self.cross = line_of_four()

    def send(self, owner, half, which, where):
        rows = rows_of(self.ref, owner, 4)
        if half is not None:
            wide = self.ref.shape[1] // 2
            rows = rows.at[:, half * wide : (half + 1) * wide]
        return sent(rows, rows, self.send_sem.at[which], self.recv_sem.at[which], {"tp": where})

    def begin(self):
        self.across = [self.send(self.me, half, half, self.far) for half in range(2)]
        self.within = [self.send(self.me, None, 2, self.near)]

    def pass_on(self):
        for half, copy in enumerate(self.across):
            copy.wait_recv()
            self.within.append(self.send(self.far, half, 3 + half, self.near))

    def end(self):
        for copy in self.across:
            copy.wait_send()
        finish(self.within)

    def run(self):
        self.begin()
        self.pass_on()
        self.end()


def line_spread_scratch():
    return [pltpu.SemaphoreType.DMA((5,)), pltpu.SemaphoreType.DMA((5,))]


class Swap:
    def __init__(self, arrays, swapped, send_sem, recv_sem, local_sem):
        plane = Group(PLANE, send_sem, recv_sem)
        self.plane, self.arrays, self.swapped, self.local_sem = plane, arrays, swapped, local_sem

    def begin(self):
        self.copies, plane = [], self.plane
        for which, (array, swapped) in enumerate(zip(self.arrays, self.swapped)):
            share = swapped.shape[1]

            def columns(index):
                return array.at[:, pl.ds(pl.multiple_of(index * share, share), share)]

            for hop, other in enumerate(plane.others):
                self.copies.append(plane.one(columns(other), plane.own(swapped), which, hop))
            local = pltpu.make_async_copy(
                columns(plane.me), plane.own(swapped), self.local_sem.at[which]
            )
            local.start()
            self.copies.append(local)

    def end(self):
        finish(self.copies)


def swap_scratch(arrays):
    sems = pltpu.SemaphoreType.DMA((len(arrays), group_size(PLANE) - 1))
    return [sems, sems, pltpu.SemaphoreType.DMA((len(arrays),))] if arrays else []


def swap_shapes(arrays):
    count = group_size(PLANE)
    return [
        jax.ShapeDtypeStruct((array.shape[0] * count, array.shape[1] // count), array.dtype)
        for array in arrays
    ]


def swaps_in_kernels(width):
    return width // group_size(PLANE) % LANE == 0


def gathered_shape(shard):
    return jax.ShapeDtypeStruct(
        (shard.shape[0] * group_size(PLANE),) + shard.shape[1:], shard.dtype
    )


def gather_scratch():
    return [gather_sems(), gather_sems(), pltpu.SemaphoreType.DMA(())]


def product_in_blocks(left, source, target, block_buf, block_sem):
    columns = range(0, source.shape[1], WIDE)

    def fetch(turn):
        at = columns[turn]
        return pltpu.make_async_copy(
            source.at[:, at : at + WIDE], block_buf.at[turn % 2], block_sem.at[turn % 2]
        )

    fetch(0).start()
    for turn, at in enumerate(columns):
        if turn + 1 < len(columns):
            fetch(turn + 1).start()
        fetch(turn).wait()
        target[:, at : at + WIDE] = matmul(left[...], block_buf[turn % 2]).astype(target.dtype)


def select_kernel(part, total, slots, send_sem, recv_sem):
    group = Group(("tp",), send_sem, recv_sem)
    greet([(("tp",), group.others)])
    finish(group.scatter(part, slots, 0))
    group.own(total)[...] = group.total(part, slots).astype(total.dtype)
    finish(group.spread(total, 1))


def run_select(call_id, part):
    count = group_size(("tp",))
    vmem = pl.BlockSpec(memory_space=pltpu.VMEM)
    sems = pltpu.SemaphoreType.DMA((2, count - 1))
    return pl.pallas_call(
        select_kernel,
        in_specs=[vmem],
        out_specs=vmem,
        out_shape=jax.ShapeDtypeStruct(part.shape, part.dtype),
        scratch_shapes=[slots_for(part, count), sems, sems],
        compiler_params=pltpu.CompilerParams(
            collective_id=call_id, has_side_effects=True, vmem_limit_bytes=VMEM_GRANT
        ),
    )(part)


def sum_kernel(part, own_rows, total, all_rows, slots, send_sem, recv_sem, *line_sems):
    group = Group(("tp",), send_sem, recv_sem)
    rows = LineSpread(all_rows, *line_sems)
    greet([(("tp",), group.others)])
    copies = group.scatter(part, slots, 0)
    group.own(all_rows)[...] = own_rows[...]
    rows.begin()
    finish(copies)
    group.own(total)[...] = group.total(part, slots).astype(total.dtype)
    copies = group.spread(total, 1)
    rows.pass_on()
    finish(copies)
    rows.end()


def sum_over_tp(call_id, part, own_rows):
    count = group_size(("tp",))
    vmem = pl.BlockSpec(memory_space=pltpu.VMEM)
    sems = pltpu.SemaphoreType.DMA((2, count - 1))
    return pl.pallas_call(
        sum_kernel,
        in_specs=[vmem] * 2,
        out_specs=[vmem] * 2,
        out_shape=[
            jax.ShapeDtypeStruct(part.shape, part.dtype),
            jax.ShapeDtypeStruct((own_rows.shape[0] * count, own_rows.shape[1]), own_rows.dtype),
        ],
        scratch_shapes=[slots_for(part, count), sems, sems] + line_spread_scratch(),
        compiler_params=pltpu.CompilerParams(
            collective_id=call_id, has_side_effects=True, vmem_limit_bytes=VMEM_GRANT
        ),
    )(part, own_rows)


def mixer_out_kernel(n_swaps, gated, out_first, out_last, tokens, gain, *refs):
    arrays, refs = refs[:n_swaps], refs[n_swaps:]
    normed, middle, gated_all, *refs = refs
    swapped, refs = refs[:n_swaps], refs[n_swaps:]
    part, refs = refs[0], refs[1:]
    line = LineSum(part, *refs[:5])
    spread = LineSpread(normed, *refs[5:7])
    gather_send, gather_recv, local_sem, *refs = refs[7:]
    group = Group(("tp",), None, None)
    gather = PlaneGather(gated, gated_all, gather_send, gather_recv)
    half = gated.shape[1] // 2
    share = out_first.shape[1]
    greet([(("tp",), group.others), (PLANE, gather.others)])
    gather.begin(local_sem)
    for at in range(out_first.shape[0] // half):
        rows = slice(at * half, (at + 1) * half)
        part[:, at * share : (at + 1) * share] = (
            matmul(gated[:, :half], out_first[rows, :])
            + matmul(gated[:, half:], out_last[rows, :])
        ).astype(part.dtype)
    firsts = [line.begin(j) for j in range(line.blocks)]
    if n_swaps:
        swap = Swap(arrays, swapped, *refs)
        swap.begin()
    line.pass_all(firsts)
    rows = group.own(tokens)[...].astype(jnp.float32) + line.total()
    middle[...] = rows
    group.own(normed)[...] = (rows * inverse_rms(rows) * gain[...].astype(jnp.float32)).astype(
        normed.dtype
    )
    spread.begin()
    gather.relay()
    gather.hand_over()
    spread.pass_on()
    spread.end()
    gather.hand_over_last()
    gather.end()
    if n_swaps:
        swap.end()


def mixer_out(call_id, gated, out_first, out_last, tokens, gain, arrays):
    count = group_size(("tp",))
    vmem = pl.BlockSpec(memory_space=pltpu.VMEM)
    hbm = pl.BlockSpec(memory_space=pltpu.HBM)
    rows, width = tokens.shape
    part = jax.ShapeDtypeStruct((rows, width), jnp.bfloat16)
    return pl.pallas_call(
        functools.partial(mixer_out_kernel, len(arrays)),
        in_specs=[vmem] * (5 + len(arrays)),
        out_specs=[vmem] * 2 + [hbm] + [hbm] * len(arrays),
        out_shape=[
            part,
            jax.ShapeDtypeStruct((rows // count, width), jnp.float32),
            gathered_shape(gated),
        ]
        + swap_shapes(arrays),
        scratch_shapes=[pltpu.VMEM(part.shape, part.dtype)]
        + line_sum_scratch(part, 2)
        + line_spread_scratch()
        + gather_scratch()
        + swap_scratch(arrays),
        compiler_params=pltpu.CompilerParams(
            collective_id=call_id, has_side_effects=True, vmem_limit_bytes=VMEM_GRANT
        ),
    )(gated, out_first, out_last, tokens, gain, *arrays)


def ffn_kernel(swaps, normed, ct, weights, made, *refs):
    hidden = weights.shape[1] // 3
    if swaps:
        *swapped, block_buf, block_sem, send_sem, recv_sem, local_sem = refs
        swap = Swap([ct], swapped, send_sem, recv_sem, local_sem)
        greet([(PLANE, swap.plane.others)])
        swap.begin()
    else:
        block_buf, block_sem = refs

    def columns(j, which):
        return pl.ds(pl.multiple_of(which * hidden + j * WIDE, WIDE), WIDE)

    def fetch(j, which):
        slot = lax.rem(j, 2)
        return pltpu.make_async_copy(
            weights.at[:, columns(j, which)],
            block_buf.at[slot, which],
            block_sem.at[slot, which],
        )

    for which in range(3):
        fetch(0, which).start()

    @pl.loop(0, hidden // WIDE)
    def _(j):
        slot = lax.rem(j, 2)

        @pl.when(j + 1 < hidden // WIDE)
        def _():
            for which in range(3):
                fetch(j + 1, which).start()

        fetch(j, 0).wait()
        gate = matmul(normed[...], block_buf[slot, 0])
        fetch(j, 1).wait()
        up = matmul(normed[...], block_buf[slot, 1])
        fetch(j, 2).wait()
        act_grad = matmul(ct[...], block_buf[slot, 2])
        logistic = jax.nn.sigmoid(gate)
        silu = gate * logistic
        slope = logistic * (1.0 + gate * (1.0 - logistic))
        made[:, columns(j, 0)] = (silu * up).astype(made.dtype)
        made[:, columns(j, 1)] = (act_grad * up * slope).astype(made.dtype)
        made[:, columns(j, 2)] = (act_grad * silu).astype(made.dtype)

    if swaps:
        swap.end()


def run_ffn(call_id, normed, ct, weights, swaps):
    rows, width = normed.shape
    arrays = [ct] if swaps else []
    vmem = pl.BlockSpec(memory_space=pltpu.VMEM)
    params = dict(collective_id=call_id, has_side_effects=True) if swaps else {}
    return pl.pallas_call(
        functools.partial(ffn_kernel, swaps),
        in_specs=[vmem, vmem, pl.BlockSpec(memory_space=pltpu.HBM)],
        out_specs=[vmem] + [pl.BlockSpec(memory_space=pltpu.HBM)] * len(arrays),
        out_shape=[jax.ShapeDtypeStruct((rows, weights.shape[1]), jnp.bfloat16)]
        + swap_shapes(arrays),
        scratch_shapes=[
            pltpu.VMEM((2, 3, width, WIDE), jnp.bfloat16),
            pltpu.SemaphoreType.DMA((2, 3)),
        ]
        + swap_scratch(arrays),
        compiler_params=pltpu.CompilerParams(vmem_limit_bytes=VMEM_GRANT, **params),
    )(normed, ct, weights)


def ffn_back_kernel(
    n_swaps,
    made,
    ct,
    middle,
    gain,
    out_first,
    out_last,
    weights,
    *refs,
):
    arrays, refs = refs[:n_swaps], refs[n_swaps:]
    middle_low, middle_grad, gain_grad, gated_grad, ffn_part, *refs = refs
    swapped, refs = refs[:n_swaps], refs[n_swaps:]
    part, wide_buf, down_buf, wide_sem, down_sem, *sems = refs
    hidden = made.shape[1] // 3
    blocks = part.shape[1] // WIDE
    group = Group(("tp",), None, None)
    line = LineSum(part, *sems[:5])
    spread = LineSpread(middle_low, *sems[5:7])
    if n_swaps:
        swap = Swap(arrays, swapped, *sems[7:])
        greet([(("tp",), group.others), (PLANE, swap.plane.others)])
        swap.begin()
    else:
        greet([(("tp",), group.others)])

    def fetch(j):
        return pltpu.make_async_copy(
            weights.at[j * WIDE : (j + 1) * WIDE, : 2 * hidden],
            wide_buf.at[j % 2],
            wide_sem.at[j % 2],
        )

    def fetch_down(j):
        return pltpu.make_async_copy(
            weights.at[j * WIDE : (j + 1) * WIDE, 2 * hidden :],
            down_buf.at[j % 2],
            down_sem.at[j % 2],
        )

    fetch(0).start()
    firsts = []
    for j in range(blocks):
        if j + 1 < blocks:
            fetch(j + 1).start()
        else:
            fetch_down(0).start()
        fetch(j).wait()
        columns = slice(j * WIDE, (j + 1) * WIDE)
        part[:, columns] = matmul_nt(made[:, hidden:], wide_buf[j % 2]).astype(part.dtype)
        firsts.append(line.begin(j))
    for j in range(blocks):
        if j + 1 < blocks:
            fetch_down(j + 1).start()
        fetch_down(j).wait()
        ffn_part[:, j * WIDE : (j + 1) * WIDE] = matmul_nt(
            made[:, :hidden], down_buf[j % 2]
        ).astype(ffn_part.dtype)
        line.pass_on(j, firsts[j])
    normed_grad = line.total()
    rows = middle[...]
    scale = inverse_rms(rows)
    gain_grad[...] = jnp.sum(normed_grad * rows * scale, 0, keepdims=True)
    grad = group.own(ct)[...].astype(jnp.float32) + norm_back(
        normed_grad, rows, scale, gain[...].astype(jnp.float32)
    )
    middle_grad[...] = grad
    group.own(middle_low)[...] = grad.astype(middle_low.dtype)
    spread.run()
    half = gated_grad.shape[1] // 2
    share = out_first.shape[1]
    for side, shards in enumerate((out_first, out_last)):
        total = None
        for at in range(shards.shape[0] // half):
            one = matmul_nt(
                middle_low[:, at * share : (at + 1) * share],
                shards[at * half : (at + 1) * half, :],
            )
            total = one if total is None else total + one
        gated_grad[:, side * half : (side + 1) * half] = total
    if n_swaps:
        swap.end()


def ffn_back(call_id, made, ct, middle, gain, out_first, out_last, weights, arrays):
    count = group_size(("tp",))
    vmem = pl.BlockSpec(memory_space=pltpu.VMEM)
    hbm = pl.BlockSpec(memory_space=pltpu.HBM)
    rows, width = ct.shape
    hidden = made.shape[1] // 3
    inner = 2 * out_first.shape[0] // group_size(PLANE)
    low, full = jnp.bfloat16, jnp.float32
    part = jax.ShapeDtypeStruct((rows, width), low)
    dma = pltpu.SemaphoreType.DMA
    return pl.pallas_call(
        functools.partial(ffn_back_kernel, len(arrays)),
        in_specs=[vmem] * 6 + [hbm] + [vmem] * len(arrays),
        out_specs=[vmem] * 5 + [hbm] * len(arrays),
        out_shape=[
            part,
            jax.ShapeDtypeStruct((rows // count, width), full),
            jax.ShapeDtypeStruct((1, width), full),
            jax.ShapeDtypeStruct((rows, inner), full),
            part,
        ]
        + swap_shapes(arrays),
        scratch_shapes=[
            pltpu.VMEM(part.shape, low),
            pltpu.VMEM((2, WIDE, 2 * hidden), low),
            pltpu.VMEM((2, WIDE, hidden), low),
            dma((2,)),
            dma((2,)),
        ]
        + line_sum_scratch(part, width // WIDE)
        + line_spread_scratch()
        + swap_scratch(arrays),
        compiler_params=pltpu.CompilerParams(
            collective_id=call_id, has_side_effects=True, vmem_limit_bytes=VMEM_GRANT
        ),
    )(made, ct, middle, gain, out_first, out_last, weights, *arrays)


def send_on(source, target, send_sem, recv_sem, ctx):
    return pltpu.make_async_remote_copy(
        src_ref=source,
        dst_ref=target,
        send_sem=send_sem,
        recv_sem=recv_sem,
        device_id={"ctx": ctx},
        device_id_type=pl.DeviceIdType.MESH,
    )


def forward_pair_kernel(
    n_state,
    tiles,
    groups,
    blocks,
    seqs,
    step_ref,
    input_ref,
    brow_ref,
    crow_ref,
    rate_ref,
    shard,
    *refs,
):
    prior_ref, mixed_ref, gathered, *refs = refs
    carried, ends, starts, prior_buf, step_held, input_held, mixed_held, *refs = refs
    prior_sem, send_sem, recv_sem, gather_send, gather_recv, local_sem = refs
    place = lax.axis_index("ctx")
    gather = PlaneGather(shard, gathered, gather_send, gather_recv)
    greet([(PLANE, gather.others)])
    gather.begin(local_sem)

    def hand_on(seq):
        return send_on(ends.at[seq], starts.at[seq], send_sem.at[seq], recv_sem.at[seq], 1)

    def store(block):
        slot = lax.rem(block, 2)
        rows = groups * SUB
        return pltpu.make_async_copy(
            prior_buf.at[slot],
            prior_ref.at[pl.ds(pl.multiple_of(block * rows, rows), rows)],
            prior_sem.at[slot],
        )

    def one_sequence(seq):
        @pl.when(place == 0)
        def _():
            carried[...] = jnp.zeros_like(carried)

        @pl.when(place == 1)
        def _():
            hand_on(seq).wait_recv()
            carried[...] = starts[seq]

        @pl.loop(0, blocks)
        def _(inner_block):
            block = seq * blocks + inner_block
            slot = lax.rem(block, 2)

            @pl.when(block >= 2)
            def _():
                store(block - 2).wait()

            def one(turn, states):
                group = block * groups + turn
                states = list(states)
                stage_in(step_ref, group, step_held)
                stage_in(input_ref, group, input_held)
                for at in range(SUB):
                    step = token_row(step_held, at, tiles)
                    drive = step * token_row(input_held, at, tiles)
                    mixed = [None] * 2
                    for n in range(n_state):
                        where = (group * SUB + at) * n_state + n
                        prior_buf[slot, turn * SUB + at, n] = states[n]
                        decay = jnp.exp2(step * rate_ref[n])
                        states[n] = decay * states[n] + drive * brow_ref[where]
                        term = states[n] * crow_ref[where]
                        mixed[n % 2] = term if mixed[n % 2] is None else mixed[n % 2] + term
                    mixed_held[pl.ds(at, tiles, stride=SUB), :] = mixed[0] + mixed[1]
                stage_out(mixed_held, mixed_ref, group)
                return tuple(states)

            states = lax.fori_loop(0, groups, one, tuple(carried[n] for n in range(n_state)))
            for n in range(n_state):
                carried[n] = states[n]
            store(block).start()

        @pl.when(place == 0)
        def _():
            ends[seq] = carried[...]
            hand_on(seq).start()

    for seq in range(seqs):
        one_sequence(seq)
        if seq == 0:
            gather.relay()
            gather.hand_over()
    gather.hand_over_last()
    for block in range(max(0, seqs * blocks - 2), seqs * blocks):
        store(block).wait()

    @pl.when(place == 0)
    def _():
        for seq in range(seqs):
            hand_on(seq).wait_send()

    gather.end()


def scan_forward_pair(
    call_id, step, inputs, b_rows, c_rows, rate, seqs, shard
):
    n_state, tiles, _ = rate.shape
    tokens, inner = step.shape
    all_groups = tokens // SUB
    groups = math.gcd(all_groups // seqs, 4)
    blocks = all_groups // seqs // groups
    vmem = pl.BlockSpec(memory_space=pltpu.VMEM)
    smem = pl.BlockSpec(memory_space=pltpu.SMEM)
    hbm = pl.BlockSpec(memory_space=pltpu.HBM)
    full = jnp.float32
    held = pltpu.VMEM((tiles * SUB, LANE), full)
    boundary = pltpu.VMEM((seqs, n_state, tiles, LANE), full)
    dma = pltpu.SemaphoreType.DMA
    return pl.pallas_call(
        functools.partial(
            forward_pair_kernel, n_state, tiles, groups, blocks, seqs
        ),
        in_specs=[vmem, vmem, smem, smem, vmem, hbm],
        out_specs=[hbm, vmem, hbm],
        out_shape=[
            jax.ShapeDtypeStruct((tokens, n_state, tiles, LANE), full),
            jax.ShapeDtypeStruct(step.shape, full),
            gathered_shape(shard),
        ],
        scratch_shapes=[
            pltpu.VMEM((n_state, tiles, LANE), full),
            boundary,
            boundary,
            pltpu.VMEM((2, groups * SUB, n_state, tiles, LANE), full),
            held,
            held,
            held,
            dma((2,)),
            dma((seqs,)),
            dma((seqs,)),
        ]
        + gather_scratch(),
        compiler_params=pltpu.CompilerParams(
            collective_id=call_id, has_side_effects=True, vmem_limit_bytes=VMEM_GRANT
        ),
    )(step, inputs, b_rows, c_rows, rate, shard)


def backward_pair_kernel(
    n_swaps,
    n_state,
    tiles,
    groups,
    blocks,
    seqs,
    step_ref,
    input_ref,
    ograd_ref,
    brow_ref,
    crow_ref,
    rate_ref,
    picks_ref,
    ffn_part,
    middle,
    prior_ref,
    *refs,
):
    arrays, refs = refs[:n_swaps], refs[n_swaps:]
    step_grad_ref, input_grad_ref, rate_grad_ref, part_ref, *refs = refs
    layer_first, layer_last, *refs = refs
    swapped, refs = refs[:n_swaps], refs[n_swaps:]
    carried, ends, starts, prior_buf, step_held, input_held, ograd_held, *refs = refs
    step_grad_held, input_grad_held, ffn_slots, prior_sem, send_sem, recv_sem, *refs = refs
    tp_send, tp_recv, *refs = refs
    place = lax.axis_index("ctx")
    tp = Group(("tp",), tp_send, tp_recv)
    if n_swaps:
        swap = Swap(arrays, swapped, *refs)
        greet([(PLANE, swap.plane.others), (("tp",), tp.others)])
        swap.begin()
    else:
        greet([(("ctx",), [1 - place]), (("tp",), tp.others)])
    ffn_sent = tp.scatter(ffn_part, ffn_slots, 0)

    def hand_on(seq):
        return send_on(ends.at[seq], starts.at[seq], send_sem.at[seq], recv_sem.at[seq], 0)

    def fetch(turn):
        seq = lax.div(turn, blocks)
        block = seq * blocks + blocks - 1 - lax.rem(turn, blocks)
        slot = lax.rem(turn, 2)
        rows = groups * SUB
        return pltpu.make_async_copy(
            prior_ref.at[pl.ds(pl.multiple_of(block * rows, rows), rows)],
            prior_buf.at[slot],
            prior_sem.at[slot],
        )

    fetch(0).start()
    rate_grad_ref[...] = jnp.zeros_like(rate_grad_ref)

    @pl.when(place == 1)
    def _():
        @pl.loop(0, seqs)
        def _(seq):
            def one(turn, grads):
                group = (seq + 1) * blocks * groups - 1 - turn
                grads = list(grads)
                stage_in(step_ref, group, step_held)
                stage_in(ograd_ref, group, ograd_held)
                for at in range(SUB - 1, -1, -1):
                    step = token_row(step_held, at, tiles)
                    ograd = token_row(ograd_held, at, tiles)
                    for n in range(n_state):
                        row = crow_ref[(group * SUB + at) * n_state + n]
                        grads[n] = jnp.exp2(step * rate_ref[n]) * (grads[n] + ograd * row)
                return tuple(grads)

            zero = jnp.zeros((tiles, LANE), jnp.float32)
            grads = lax.fori_loop(0, blocks * groups, one, (zero,) * n_state)
            for n in range(n_state):
                ends[seq, n] = grads[n]
            hand_on(seq).start()

    @pl.loop(0, seqs)
    def _(seq):
        @pl.when(place == 1)
        def _():
            carried[...] = jnp.zeros_like(carried)

        @pl.when(place == 0)
        def _():
            hand_on(seq).wait_recv()
            carried[...] = starts[seq]

        @pl.loop(0, blocks)
        def _(inner_block):
            turn = seq * blocks + inner_block
            slot = lax.rem(turn, 2)
            first_group = (seq * blocks + blocks - 1 - inner_block) * groups

            @pl.when(turn + 1 < seqs * blocks)
            def _():
                fetch(turn + 1).start()

            fetch(turn).wait()

            def one(back, grads):
                inner_group = groups - 1 - back
                group = first_group + inner_group
                grads = list(grads)
                stage_in(step_ref, group, step_held)
                stage_in(input_ref, group, input_held)
                stage_in(ograd_ref, group, ograd_held)
                for at in range(SUB - 1, -1, -1):
                    step = token_row(step_held, at, tiles)
                    value = token_row(input_held, at, tiles)
                    ograd = token_row(ograd_held, at, tiles)
                    drive = step * value
                    along_b = None
                    along_rate = None
                    brow_parts, crow_parts = [], []
                    for n in range(n_state):
                        where = (group * SUB + at) * n_state + n
                        brow, crow = brow_ref[where], crow_ref[where]
                        rate = rate_ref[n]
                        decay = jnp.exp2(step * rate)
                        grad = ograd * crow + grads[n]
                        kept = decay * prior_buf[slot, inner_group * SUB + at, n]
                        state = kept + drive * brow
                        decay_term = grad * kept
                        grads[n] = decay * grad
                        rate_grad_ref[n] += decay_term * step
                        by_rate, by_brow = decay_term * rate, grad * brow
                        along_rate = by_rate if along_rate is None else along_rate + by_rate
                        along_b = by_brow if along_b is None else along_b + by_brow
                        brow_parts.append(grad * drive)
                        crow_parts.append(ograd * state)
                    step_grad_held[pl.ds(at, tiles, stride=SUB), :] = (
                        along_rate * LN2 + along_b * value
                    )
                    input_grad_held[pl.ds(at, tiles, stride=SUB), :] = along_b * step
                    parts = jnp.concatenate(brow_parts + crow_parts, 0).astype(jnp.bfloat16)
                    part_ref[group * SUB + at] = jnp.dot(
                        picks_ref[...], parts, preferred_element_type=jnp.float32
                    )
                stage_out(step_grad_held, step_grad_ref, group)
                stage_out(input_grad_held, input_grad_ref, group)
                return tuple(grads)

            grads = lax.fori_loop(0, groups, one, tuple(carried[n] for n in range(n_state)))
            for n in range(n_state):
                carried[n] = grads[n]

    finish(ffn_sent)
    layer_rows = (middle[...] + tp.total(ffn_part, ffn_slots)).astype(layer_first.dtype)
    half = layer_first.shape[1]
    layer_first[...], layer_last[...] = layer_rows[:, :half], layer_rows[:, half:]

    @pl.when(place == 1)
    def _():
        @pl.loop(0, seqs)
        def _(seq):
            hand_on(seq).wait_send()

    if n_swaps:
        swap.end()


def scan_backward_pair(
    call_id, prior, step, inputs, ograd, b_rows, c_rows, rate, seqs, ffn_part, middle, arrays
):
    n_state, tiles, _ = rate.shape
    tokens, inner = step.shape
    all_groups = tokens // SUB
    groups = math.gcd(all_groups // seqs, 4)
    blocks = all_groups // seqs // groups
    tp_count = group_size(("tp",))
    vmem = pl.BlockSpec(memory_space=pltpu.VMEM)
    smem = pl.BlockSpec(memory_space=pltpu.SMEM)
    hbm = pl.BlockSpec(memory_space=pltpu.HBM)
    full = jnp.float32
    held = pltpu.VMEM((tiles * SUB, LANE), full)
    boundary = pltpu.VMEM((seqs, n_state, tiles, LANE), full)
    dma = pltpu.SemaphoreType.DMA
    layer_half = jax.ShapeDtypeStruct((middle.shape[0], middle.shape[1] // 2), jnp.bfloat16)
    picks = jnp.repeat(jnp.eye(2 * n_state, dtype=jnp.bfloat16), tiles, 1)
    return pl.pallas_call(
        functools.partial(
            backward_pair_kernel, len(arrays), n_state, tiles, groups, blocks, seqs
        ),
        in_specs=[vmem] * 3 + [smem] * 2 + [vmem] * 4 + [hbm] + [vmem] * len(arrays),
        out_specs=[vmem] * 6 + [hbm] * len(arrays),
        out_shape=[
            jax.ShapeDtypeStruct(step.shape, full),
            jax.ShapeDtypeStruct(step.shape, full),
            jax.ShapeDtypeStruct(rate.shape, full),
            jax.ShapeDtypeStruct((tokens, 2 * n_state, LANE), full),
            layer_half,
            layer_half,
        ]
        + swap_shapes(arrays),
        scratch_shapes=[
            pltpu.VMEM((n_state, tiles, LANE), full),
            boundary,
            boundary,
            pltpu.VMEM((2, groups * SUB, n_state, tiles, LANE), full),
        ]
        + [held] * 5
        + [
            slots_for(ffn_part, tp_count),
            dma((2,)),
            dma((seqs,)),
            dma((seqs,)),
            dma((1, tp_count - 1)),
            dma((1, tp_count - 1)),
        ]
        + swap_scratch(arrays),
        compiler_params=pltpu.CompilerParams(
            collective_id=call_id, has_side_effects=True, vmem_limit_bytes=VMEM_GRANT
        ),
    )(step, inputs, ograd, b_rows, c_rows, rate, picks, ffn_part, middle, prior, *arrays)


class PlaneGather:
    def __init__(self, own, gathered, send_sem, recv_sem):
        self.own, self.gathered = own, gathered
        self.send_sem, self.recv_sem = send_sem, recv_sem
        self.dp, self.ctx = lax.axis_index("dp"), lax.axis_index("ctx")
        self.n_dp, self.n_ctx = lax.axis_size("dp"), lax.axis_size("ctx")
        self.hands_on = relayed()
        self.count = self.n_dp * self.n_ctx
        self.me = self.dp * self.n_ctx + self.ctx
        self.others = [lax.rem(self.me + hop, self.count) for hop in range(1, self.count)]
        self.copies = {}
        if self.hands_on:
            core = lax.rem(self.dp, 2)
            over_core = self.dp + 1 - 2 * core
            over_y = lax.rem(self.dp + 2, 4)
            over_x = 1 - self.ctx
            self.core = {"dp": over_core, "ctx": self.ctx}
            self.at_x = {"dp": self.dp, "ctx": over_x}
            self.at_y = {"dp": over_y, "ctx": self.ctx}
            self.from_x = self.dp * 2 + over_x
            self.from_y = over_y * 2 + self.ctx
            self.across = over_y * 2 + over_x

    def part(self, owner, half):
        rows = self.gathered.shape[0] // self.count
        start, size = owner * rows, rows
        if half is not None:
            size = rows // 2
            start = start + half * size
        return self.gathered.at[pl.ds(pl.multiple_of(start, size), size), :]

    def send(self, which, owner, half, where):
        target = self.part(owner, half)
        source = target
        if owner is self.me:
            rows = self.own.shape[0]
            source = self.own
            if half is not None:
                source = self.own.at[pl.ds(half * (rows // 2), rows // 2), :]
        self.copies[which] = sent(
            source, target, self.send_sem.at[which], self.recv_sem.at[which], where
        )

    def arrived(self, *which):
        for one in which:
            self.copies[one].wait_recv()

    def begin(self, local_sem):
        self.local = pltpu.make_async_copy(self.own, self.part(self.me, None), local_sem)
        self.local.start()
        if not self.hands_on:
            for hop, other in enumerate(self.others):
                self.send(hop, self.me, None, device_at(PLANE, other))
            return
        self.send(0, self.me, 1, self.at_x)
        self.send(1, self.me, 0, self.at_y)
        self.send(2, self.me, None, self.core)
        self.send(3, self.me, 0, self.at_x)
        self.send(4, self.me, 1, self.at_y)

    def relay(self):
        if not self.hands_on:
            return
        self.arrived(0, 1)
        self.send(5, self.from_x, 1, self.at_y)
        self.send(6, self.from_y, 0, self.at_x)
        self.send(7, self.from_x, 1, self.core)
        self.send(8, self.from_y, 0, self.core)

    def hand_over(self):
        if not self.hands_on:
            return
        self.arrived(3, 4)
        self.send(9, self.from_x, 0, self.core)
        self.send(10, self.from_y, 1, self.core)

    def hand_over_last(self):
        if not self.hands_on:
            return
        self.arrived(5, 6)
        self.send(11, self.across, 1, self.core)
        self.send(12, self.across, 0, self.core)

    def end(self):
        if self.hands_on:
            self.arrived(2, 7, 8, 9, 10, 11, 12)
        else:
            self.arrived(*range(self.count - 1))
        for copy in self.copies.values():
            copy.wait_send()
        self.local.wait()


def relayed():
    return lax.axis_size("dp") == 4 and lax.axis_size("ctx") == 2


def gather_sems():
    count = 13 if relayed() else group_size(PLANE) - 1
    return pltpu.SemaphoreType.DMA((count,))


WIDE = 512


def products(source, first, last, dot, target, block_buf, block_sem, out_buf, out_sem):
    def fetch(j, slot):
        columns = pl.ds(pl.multiple_of(j * WIDE, WIDE), WIDE)
        return pltpu.make_async_copy(
            source.at[:, columns], block_buf.at[slot], block_sem.at[slot]
        )

    def store(j, slot):
        return pltpu.make_async_copy(out_buf.at[slot], target(j), out_sem.at[slot])

    fetch(first, first % 2).start()

    @pl.loop(first, last)
    def _(j):
        slot = lax.rem(j, 2)

        @pl.when(j + 1 < last)
        def _():
            fetch(j + 1, 1 - slot).start()

        fetch(j, slot).wait()

        @pl.when(j >= first + 2)
        def _():
            store(j - 2, slot).wait()

        out_buf[slot] = dot(block_buf[slot])
        store(j, slot).start()

    for j in range(max(first, last - 2), last):
        store(j, j % 2).wait()


class PlaneSum:
    def __init__(self, array, total, *refs):
        self.array, self.result = array, total
        self.hands_on = relayed()
        if not self.hands_on:
            self.slots, send_sem, recv_sem = refs
            self.group = Group(PLANE, send_sem, recv_sem)
            return
        self.core_slot, self.pair, self.chip_slots, *self.sems = refs
        dp, ctx = lax.axis_index("dp"), lax.axis_index("ctx")
        self.half = lax.rem(dp, 2)
        self.other_core = {"dp": dp + 1 - 2 * self.half, "ctx": ctx}
        over_y, over_x = lax.rem(dp + 2, 4), 1 - ctx
        self.quarter = lax.div(dp, 2) * 2 + ctx
        self.chips = [
            ({"dp": a, "ctx": b}, lax.div(a, 2) * 2 + b)
            for a, b in ((dp, over_x), (over_y, ctx), (over_y, over_x))
        ]

    def to_core(self, source, target, which):
        core_send, core_recv = self.sems[:2]
        return sent(
            source, target, core_send.at[which], core_recv.at[which], self.other_core
        )

    def to_chip(self, source, target, which, at):
        chip_send, chip_recv = self.sems[2:]
        return sent(
            source,
            target,
            chip_send.at[which, at],
            chip_recv.at[which, at],
            self.chips[at][0],
        )

    def begin(self):
        if not self.hands_on:
            self.copies = self.group.scatter(self.array, self.slots, 0)
            return
        self.copies = [self.to_core(rows_of(self.array, 1 - self.half, 2), self.core_slot, 0)]

    def add_pair(self):
        if not self.hands_on:
            return
        finish(self.copies)
        self.pair[...] = (
            rows_of(self.array, self.half, 2)[...].astype(jnp.float32)
            + self.core_slot[...].astype(jnp.float32)
        ).astype(self.pair.dtype)
        self.copies = [
            self.to_chip(rows_of(self.pair, index, 4), self.chip_slots.at[at], 0, at)
            for at, (_, index) in enumerate(self.chips)
        ]

    def add_all(self):
        finish(self.copies)
        if not self.hands_on:
            self.group.own(self.result)[...] = self.group.total(self.array, self.slots).astype(
                self.result.dtype
            )
            self.copies = self.group.spread(self.result, 1)
            return
        total = rows_of(self.pair, self.quarter, 4)[...].astype(jnp.float32)
        for at in range(3):
            total = total + self.chip_slots[at].astype(jnp.float32)
        mine = rows_of(self.result, self.half * 4 + self.quarter, 8)
        mine[...] = total.astype(self.result.dtype)
        self.copies = [self.to_chip(mine, mine, 1, at) for at in range(3)]

    def hand_over(self):
        if not self.hands_on:
            return
        finish(self.copies)
        half = rows_of(self.result, self.half, 2)
        self.copies = [self.to_core(half, half, 1)]

    def end(self):
        finish(self.copies)


def plane_sum_scratch(array):
    dma = pltpu.SemaphoreType.DMA
    count = group_size(PLANE)
    if not relayed():
        return [slots_for(array, count), dma((2, count - 1)), dma((2, count - 1))]
    rows, width = array.shape
    return [
        pltpu.VMEM((rows // 2, width), array.dtype),
        pltpu.VMEM((rows // 2, width), array.dtype),
        pltpu.VMEM((3, rows // 8, width), array.dtype),
        dma((2,)),
        dma((2,)),
        dma((2, 3)),
        dma((2, 3)),
    ]


SMALL_ROWS = 32
GAIN_ROWS = 16


def tail_kernel(
    swaps,
    conv_grad,
    gate_grad,
    convkern,
    convbias,
    stepbias,
    decaylog,
    skipgain,
    ffngain,
    layer_first,
    layer_rows,
    middle_low,
    step_low,
    pre_low,
    select_low,
    scan_in,
    tokens,
    middle_grad,
    gain_row,
    in_conv,
    in_gate,
    one_cols,
    two_cols,
    ct_cols,
    middle_cols,
    ffn_all,
    gated_all,
    tokens_grad,
    layer_out,
    vectors_sum,
    step_sum,
    select_sum,
    gains,
    mix_all,
    grad_inproj,
    grad_outproj,
    grad_gateup,
    grad_downproj,
    mix_own,
    normed_part,
    small,
    small_sum,
    gain_slots,
    gain_own,
    vectors_own,
    cols,
    in_buf,
    block_buf,
    wide_buf,
    tall_buf,
    cols_sem,
    in_sem,
    block_sem,
    wide_sem,
    tall_sem,
    tp_send,
    tp_recv,
    gather_send,
    gather_recv,
    local_sem,
    *sems,
):
    inner = conv_grad.shape[1]
    hidden = ffn_all.shape[1] // 3
    width = tokens.shape[1]
    rank = step_low.shape[1]
    tp = Group(("tp",), tp_send, tp_recv)
    line = LineSum(normed_part, *sems[:5])
    tokens_spread = LineSpread(tokens_grad, *sems[5:7])
    layer_last = layer_out.at[:, width // 2 :]
    layer_spread = LineSpread(layer_last, *sems[7:9])
    count = 7 if relayed() else 3
    small_total = PlaneSum(small, small_sum, *sems[9 : 9 + count])
    swap_sems = sems[9 + count :]
    gather = PlaneGather(mix_own, mix_all, gather_send, gather_recv)
    sources = (one_cols, two_cols, ct_cols) if swaps else (one_cols, two_cols, ct_cols, middle_cols)
    loads = [
        pltpu.make_async_copy(source, cols.at[at], cols_sem.at[at])
        for at, source in enumerate(sources)
    ]
    if swaps:
        swap = Swap([middle_low], [cols.at[3]], *swap_sems)

    def fetch(j):
        slot = j % 2
        rows = slice(j * WIDE, (j + 1) * WIDE)
        return [
            pltpu.make_async_copy(source.at[rows, :], in_buf.at[slot, at], in_sem.at[slot, at])
            for at, source in enumerate((in_conv, in_gate))
        ]

    for copy in fetch(0) + loads:
        copy.start()
    mix_own[:, :inner] = conv_grad[...]
    mix_own[:, inner:] = gate_grad[...]
    greet([(("tp",), tp.others), (PLANE, gather.others)])
    gather.begin(local_sem)

    small[...] = jnp.zeros_like(small)
    vectors_own[...] = jnp.zeros_like(vectors_own)
    at = 0
    for vector in (convkern, convbias, stepbias, decaylog, skipgain):
        vectors_own[at : at + vector.shape[0], :] = vector[...]
        at += vector.shape[0]
    at = SMALL_ROWS - GAIN_ROWS + 10
    for row in range(width // inner):
        vectors_own[at + row : at + row + 1, :] = ffngain[:, row * inner : (row + 1) * inner]
    hidden_in = tokens[...].astype(jnp.float32)
    unit_rows = hidden_in * inverse_rms(hidden_in)
    blocks = width // WIDE
    firsts = []
    for j in range(blocks):
        if j + 1 < blocks:
            for copy in fetch(j + 1):
                copy.start()
        finish(fetch(j))
        columns = slice(j * WIDE, (j + 1) * WIDE)
        block = matmul_nt(conv_grad[...], in_buf[j % 2, 0]) + matmul_nt(
            gate_grad[...], in_buf[j % 2, 1]
        )
        normed_part[:, columns] = block.astype(normed_part.dtype)
        firsts.append(line.begin(j))
        gain_grad = jnp.sum(block * unit_rows[:, columns], 0, keepdims=True)
        if j:
            line.pass_on(j - 1, firsts[j - 1])
        row, at = divmod(j * WIDE, inner)
        row += SMALL_ROWS - GAIN_ROWS + 8
        vectors_own[row : row + 1, at : at + WIDE] = gain_grad
    layer_out[:, : width // 2] = layer_first[...]
    rows_of(layer_last, tp.me, tp.count)[...] = layer_rows[...]
    layer_spread.begin()
    small[:SMALL_ROWS, :] = vectors_own[...].astype(small.dtype)
    small[SMALL_ROWS : SMALL_ROWS + rank, :] = matmul_tn(step_low[...], pre_low[...]).astype(
        small.dtype
    )
    selected = select_sum.shape[0]
    small[SMALL_ROWS + rank : SMALL_ROWS + rank + selected, :] = matmul_tn(
        select_low[...], scan_in[...]
    )[:selected].astype(small.dtype)
    small_total.begin()
    line.pass_on(blocks - 1, firsts[-1])

    def flat(at):
        return lambda block: matmul_tn(cols[at], block)

    def tall(at):
        return lambda block: matmul_tn(block, cols[at])

    def side_by_side(ref, first):
        per = ref.shape[2] // WIDE

        def target(j):
            at = j - first
            columns = pl.ds(pl.multiple_of(lax.rem(at, per) * WIDE, WIDE), WIDE)
            return ref.at[lax.div(at, per), :, columns]

        return target

    def one_above_other(ref):
        return lambda j: ref.at[pl.ds(pl.multiple_of(j * WIDE, WIDE), WIDE), :]

    wide = (block_buf, block_sem, wide_buf, wide_sem)
    high = (block_buf, block_sem, tall_buf, tall_sem)
    down_end = hidden // WIDE
    gu_end = 3 * hidden // WIDE
    finish(loads)
    gu_middle = (down_end + gu_end) // 2
    to_gateup = side_by_side(grad_gateup, down_end)
    products(ffn_all, 0, down_end, tall(2), one_above_other(grad_downproj), *high)
    gather.relay()
    small_total.add_pair()
    products(ffn_all, down_end, gu_middle, flat(1), to_gateup, *wide)
    hidden_in = tp.own(tokens)[...].astype(jnp.float32)
    tp.own(tokens_grad)[...] = (
        middle_grad[...]
        + norm_back(
            line.total(),
            hidden_in,
            inverse_rms(hidden_in),
            gain_row[...].astype(jnp.float32),
        )
    ).astype(tokens_grad.dtype)
    tokens_spread.begin()
    layer_spread.pass_on()
    gather.hand_over()
    small_total.add_all()
    if swaps:
        swap.begin()
    products(ffn_all, gu_middle, gu_end, flat(1), to_gateup, *wide)
    gather.hand_over_last()
    small_total.hand_over()
    tokens_spread.pass_on()
    gather.end()
    products(mix_all, 0, 2 * inner // WIDE, flat(0), side_by_side(grad_inproj, 0), *wide)
    small_total.end()
    gain_own[...] = small_sum[SMALL_ROWS - GAIN_ROWS : SMALL_ROWS, :].astype(jnp.float32)
    gain_sent = [tp.one(gain_own, gain_slots.at[hop], 0, hop) for hop in range(tp.count - 1)]
    vectors_sum[...] = small_sum[:SMALL_ROWS, :].astype(jnp.float32)
    step_sum[...] = small_sum[SMALL_ROWS : SMALL_ROWS + rank, :].astype(jnp.float32)
    select_sum[...] = small_sum[SMALL_ROWS + rank : SMALL_ROWS + rank + selected, :].astype(
        jnp.float32
    )
    if swaps:
        swap.end()
    products(gated_all, 0, inner // WIDE, tall(3), one_above_other(grad_outproj), *high)
    finish(gain_sent)
    total = gain_own[...]
    for hop in range(tp.count - 1):
        total = total + gain_slots[hop]
    gains[...] = total
    tokens_spread.end()
    layer_spread.end()


def run_tail(
    call_id,
    selected,
    swaps,
    conv_grad,
    gate_grad,
    vectors,
    layer_first,
    layer_rows,
    middle_low,
    step_low,
    pre_low,
    select_low,
    scan_in,
    tokens,
    middle_grad,
    gain_row,
    in_conv,
    in_gate,
    one_cols,
    two_cols,
    ct_cols,
    middle_cols,
    ffn_all,
    gated_all,
):
    rows, inner = conv_grad.shape
    rank = step_low.shape[1]
    hidden = ffn_all.shape[1] // 3
    width = tokens.shape[1]
    share = one_cols.shape[1]
    all_rows = ffn_all.shape[0]
    tp_count, plane_count = group_size(("tp",)), group_size(PLANE)
    low, full = jnp.bfloat16, jnp.float32
    vmem = pl.BlockSpec(memory_space=pltpu.VMEM)
    hbm = pl.BlockSpec(memory_space=pltpu.HBM)
    dma = pltpu.SemaphoreType.DMA
    small_rows = SMALL_ROWS + rank + selected
    small = jax.ShapeDtypeStruct((small_rows + -small_rows % (16 * plane_count), inner), low)
    part = jax.ShapeDtypeStruct((rows, width), low)
    return pl.pallas_call(
        functools.partial(tail_kernel, swaps),
        in_specs=[vmem] * 18 + [hbm] * 8,
        out_specs=[vmem] * 6 + [hbm] * 5,
        out_shape=[
            jax.ShapeDtypeStruct(tokens.shape, low),
            jax.ShapeDtypeStruct(tokens.shape, low),
            jax.ShapeDtypeStruct((SMALL_ROWS, inner), full),
            jax.ShapeDtypeStruct((rank, inner), full),
            jax.ShapeDtypeStruct((selected, inner), full),
            jax.ShapeDtypeStruct((GAIN_ROWS, inner), full),
            jax.ShapeDtypeStruct((all_rows, 2 * inner), low),
            jax.ShapeDtypeStruct((2, share, inner), full),
            jax.ShapeDtypeStruct((inner, share), full),
            jax.ShapeDtypeStruct((2, share, hidden), full),
            jax.ShapeDtypeStruct((hidden, share), full),
        ],
        scratch_shapes=[
            pltpu.VMEM((rows, 2 * inner), low),
            pltpu.VMEM(part.shape, low),
            pltpu.VMEM(small.shape, low),
            pltpu.VMEM(small.shape, low),
            pltpu.VMEM((tp_count - 1, GAIN_ROWS, inner), full),
            pltpu.VMEM((GAIN_ROWS, inner), full),
            pltpu.VMEM((SMALL_ROWS, inner), full),
            pltpu.VMEM((4, all_rows, share), low),
            pltpu.VMEM((2, 2, WIDE, inner), low),
            pltpu.VMEM((2, all_rows, WIDE), low),
            pltpu.VMEM((2, share, WIDE), full),
            pltpu.VMEM((2, WIDE, share), full),
            dma((4,)),
            dma((2, 2)),
            dma((2,)),
            dma((2,)),
            dma((2,)),
            dma((1, tp_count - 1)),
            dma((1, tp_count - 1)),
        ]
        + gather_scratch()
        + line_sum_scratch(part, width // WIDE)
        + line_spread_scratch() * 2
        + plane_sum_scratch(small)
        + (swap_scratch([tokens]) if swaps else []),
        compiler_params=pltpu.CompilerParams(
            collective_id=call_id, has_side_effects=True, vmem_limit_bytes=VMEM_GRANT
        ),
    )(
        conv_grad,
        gate_grad,
        *vectors,
        layer_first,
        layer_rows,
        middle_low,
        step_low,
        pre_low,
        select_low,
        scan_in,
        tokens,
        middle_grad,
        gain_row,
        in_conv,
        in_gate,
        one_cols,
        two_cols,
        ct_cols,
        middle_cols,
        ffn_all,
        gated_all,
    )


BORDER = 16


def head_kernel(
    tokens,
    gain,
    in_conv,
    in_gate,
    conv_in,
    gate_mix,
    border,
    conv_all,
    gate_all,
    normed,
    block_buf,
    block_sem,
    border_send,
    border_recv,
    *sems,
):
    place, places = lax.axis_index("ctx"), lax.axis_size("ctx")
    seqs = border.shape[0] // BORDER
    span = conv_in.shape[0] // seqs

    def to_next(seq):
        return send_on(
            conv_in.at[pl.ds((seq + 1) * span - BORDER, BORDER), :],
            border.at[pl.ds(seq * BORDER, BORDER), :],
            border_send.at[seq],
            border_recv.at[seq],
            place + 1,
        )

    conv = PlaneGather(in_conv, conv_all, *sems[:2])
    gate = PlaneGather(in_gate, gate_all, *sems[3:5])
    greet([(PLANE, conv.others)])
    conv.begin(sems[2])
    gate.begin(sems[5])
    hidden_in = tokens[...].astype(jnp.float32)
    normed[...] = (hidden_in * inverse_rms(hidden_in) * gain[...].astype(jnp.float32)).astype(
        normed.dtype
    )
    conv.relay()
    conv.hand_over()
    gate.relay()
    conv.hand_over_last()
    gate.hand_over()
    conv.end()
    product_in_blocks(normed, conv_all, conv_in, block_buf, block_sem)

    @pl.when(place == 0)
    def _():
        border[...] = jnp.zeros_like(border)

    @pl.when(place < places - 1)
    def _():
        for seq in range(seqs):
            to_next(seq).start()

    gate.hand_over_last()
    gate.end()
    product_in_blocks(normed, gate_all, gate_mix, block_buf, block_sem)

    @pl.when(place < places - 1)
    def _():
        for seq in range(seqs):
            to_next(seq).wait_send()

    @pl.when(place > 0)
    def _():
        for seq in range(seqs):
            to_next(seq).wait_recv()


def run_head(call_id, tokens, gain, inproj, seqs):
    rows, width = tokens.shape
    inner = inproj.shape[2]
    low = jnp.bfloat16
    vmem = pl.BlockSpec(memory_space=pltpu.VMEM)
    hbm = pl.BlockSpec(memory_space=pltpu.HBM)
    return pl.pallas_call(
        head_kernel,
        in_specs=[vmem] * 2 + [hbm] * 2,
        out_specs=[vmem] * 3 + [hbm] * 2,
        out_shape=[
            jax.ShapeDtypeStruct((rows, inner), low),
            jax.ShapeDtypeStruct((rows, inner), jnp.float32),
            jax.ShapeDtypeStruct((seqs * BORDER, inner), low),
            jax.ShapeDtypeStruct((width, inner), low),
            jax.ShapeDtypeStruct((width, inner), low),
        ],
        scratch_shapes=[
            pltpu.VMEM((rows, width), low),
            pltpu.VMEM((2, width, WIDE), low),
            pltpu.SemaphoreType.DMA((2,)),
            pltpu.SemaphoreType.DMA((seqs,)),
            pltpu.SemaphoreType.DMA((seqs,)),
        ]
        + gather_scratch() * 2,
        compiler_params=pltpu.CompilerParams(
            collective_id=call_id, has_side_effects=True, vmem_limit_bytes=VMEM_GRANT
        ),
    )(tokens, gain, inproj[0], inproj[1])


def per_device(
    tokens,
    mixgain,
    inproj,
    convkern,
    convbias,
    selproj,
    stepproj,
    stepbias,
    decaylog,
    skipgain,
    outproj,
    ffngain,
    gateup,
    downproj,
    cotangent,
):
    seqs, span, width = tokens.shape
    rows = seqs * span
    taps, inner = convkern.shape
    rank = stepproj.shape[0]
    n_state = decaylog.shape[1]
    tiles = inner // LANE
    gain_mix = mixgain.astype(jnp.float32)
    kernel = convkern.astype(jnp.float32)
    kernel_bias = convbias.astype(jnp.float32)
    step_bias = stepbias.astype(jnp.float32)
    skip_weight = skipgain.astype(jnp.float32)
    decay_rate = -jnp.exp(jnp.transpose(decaylog.astype(jnp.float32)))
    rate = (decay_rate * LOG2E).reshape(n_state, tiles, LANE)

    gain_mix_row, gain_ffn_row = mixgain.reshape(1, width), ffngain.reshape(1, width)
    low = jnp.bfloat16

    tokens_rows = tokens.reshape(rows, width)
    ct_low = cotangent.reshape(rows, width)
    swap_now = swaps_in_kernels(width)
    out_first = gathered_rows(outproj[: inner // 2])
    ffn_pack = gathered_rows(
        jnp.concatenate([gateup[0], gateup[1], jnp.transpose(downproj)], 1)
    )
    conv_in, gate_mix, border, in_conv, in_gate = run_head(
        5, tokens_rows, gain_mix_row, inproj, seqs
    )
    hidden_in = tokens_rows.astype(jnp.float32)
    scale_one = inverse_rms(hidden_in)
    normed_one = (hidden_in * scale_one * gain_mix).astype(low)

    conv_seqs = conv_in.reshape(seqs, span, inner)
    rim_rows = border.reshape(seqs, BORDER, inner)[:, BORDER - (taps - 1) :]
    padded_in = jnp.concatenate([rim_rows, conv_seqs], 1).astype(jnp.float32)
    conv_out = kernel_bias[None, None]
    for offset in range(taps):
        conv_out = conv_out + kernel[offset][None, None] * padded_in[:, offset : offset + span]
    conv_out = conv_out.reshape(rows, inner)
    scan_in = jax.nn.silu(conv_out).astype(low)
    scan_float = scan_in.astype(jnp.float32)
    columns = selproj.shape[1]
    select_width = -(-columns // LANE) * LANE
    select_weights = jnp.pad(selproj, ((0, 0), (0, select_width - columns)))
    select_cols = run_select(0, matmul(scan_in, select_weights))

    def columns_of(swapped, array):
        if not swapped:
            return swapped_columns(array)
        return swapped[0].reshape(-1, swapped[0].shape[-1])

    step_low = select_cols[:, :rank].astype(low)
    b_rows = select_cols[:, rank : rank + n_state].reshape(-1)
    c_rows = select_cols[:, rank + n_state : columns].reshape(-1)
    step_pre = matmul(step_low, stepproj) + step_bias[None]
    step_size = jax.nn.softplus(step_pre)
    in_pairs = lax.axis_size("ctx") == 2
    if in_pairs:
        prior, scan_out, out_last = scan_forward_pair(
            6,
            step_size,
            scan_float,
            b_rows,
            c_rows,
            rate,
            seqs,
            outproj[inner // 2 :],
        )
    else:
        span_decay = jnp.exp(
            decay_rate[None] * jnp.sum(step_size.reshape(seqs, span, inner), 1)[:, None]
        ).reshape(seqs, n_state, tiles, LANE)
        ends = scan_ends(step_size, scan_float, b_rows, rate, seqs, False)
        start = from_earlier(ends, span_decay, 1)
        prior, scan_out = scan_forward(start, step_size, scan_float, b_rows, c_rows, rate, seqs)
        out_last = gathered_rows(outproj[inner // 2 :])
    mixer_core = scan_out + skip_weight[None] * scan_float
    gate_sig = jax.nn.silu(gate_mix)
    gated = (mixer_core * gate_sig).astype(low)
    normed_two, middle, gated_all, *swapped = mixer_out(
        1,
        gated,
        out_first,
        out_last,
        tokens_rows,
        gain_ffn_row,
        [normed_one] if swap_now else [],
    )
    normed_one_cols = columns_of(swapped, normed_one)
    made, *swapped = run_ffn(8, normed_two, ct_low, ffn_pack, swap_now)
    ct_cols = columns_of(swapped, ct_low)
    ffn_all = gathered_rows(made)
    middle_low, middle_grad, ffngain_part, gated_grad, ffn_part, *swapped = ffn_back(
        2,
        made,
        ct_low,
        middle,
        gain_ffn_row,
        out_first,
        out_last,
        ffn_pack,
        [normed_two] if swap_now else [],
    )
    normed_two_cols = columns_of(swapped, normed_two)
    core_grad = gated_grad * gate_sig
    gate_mix_grad = (gated_grad * mixer_core * silu_slope(gate_mix)).astype(low)
    grad_skipgain = jnp.sum(core_grad * scan_float, 0)
    if in_pairs:
        step_grad, input_grad, rate_grad, parts, *layer_rows = scan_backward_pair(
            7,
            prior,
            step_size,
            scan_float,
            core_grad,
            b_rows,
            c_rows,
            rate,
            seqs,
            ffn_part,
            middle,
            [],
        )
    else:
        back_ends = scan_ends(step_size, core_grad, c_rows, rate, seqs, True)
        end_grad = from_earlier(back_ends, span_decay, -1)
        step_grad, input_grad, rate_grad, parts = scan_backward(
            end_grad, prior, step_size, scan_float, core_grad, b_rows, c_rows, rate, seqs
        )
        ffn_sum = lax.psum_scatter(ffn_part, "tp", scatter_dimension=0, tiled=True)
        layer_rows = jnp.split((middle + ffn_sum.astype(jnp.float32)).astype(low), 2, 1)
    grad_decaylog = rate_grad.reshape(n_state, inner) * decay_rate
    pre_grad = step_grad * jax.nn.sigmoid(step_pre)
    grad_stepbias = jnp.sum(pre_grad, 0)
    pre_low = pre_grad.astype(low)
    select_part = jnp.concatenate(
        [
            matmul_nt(pre_low, stepproj),
            jnp.sum(parts, -1),
            jnp.zeros((rows, select_width - columns), jnp.float32),
        ],
        1,
    ).astype(low)
    select_low, layer_first = sum_over_tp(3, select_part, layer_rows[0])
    scan_in_grad = (
        core_grad * skip_weight[None]
        + input_grad
        + matmul_nt(select_low, select_weights)
    )
    conv_grad = scan_in_grad * silu_slope(conv_out)
    grad_convbias = jnp.sum(conv_grad, 0)
    conv_grad_seqs = conv_grad.reshape(seqs, span, inner)
    padded_grad = jnp.zeros(padded_in.shape, jnp.float32)
    kernel_rows = []
    for offset in range(taps):
        kernel_rows.append(jnp.sum(conv_grad_seqs * padded_in[:, offset : offset + span], (0, 1)))
        padded_grad = padded_grad + jnp.pad(
            kernel[offset][None, None] * conv_grad_seqs,
            ((0, 0), (offset, taps - 1 - offset), (0, 0)),
        )
    grad_convkern = jnp.stack(kernel_rows)
    returned = passed_along(padded_grad[:, : taps - 1], "ctx", -1)
    conv_in_grad = (
        (padded_grad[:, taps - 1 :] + jnp.pad(returned, ((0, 0), (span - taps + 1, 0), (0, 0))))
        .astype(low)
        .reshape(rows, inner)
    )
    vectors = [
        grad_convkern,
        grad_convbias[None],
        grad_stepbias[None],
        grad_decaylog,
        grad_skipgain[None],
        ffngain_part,
    ]
    (
        tokens_grad,
        layer_out,
        vectors,
        grad_stepproj,
        grad_selproj,
        gains,
        _,
        grad_inproj,
        grad_outproj,
        grad_gateup,
        grad_downproj,
    ) = run_tail(
        4,
        columns,
        swap_now,
        conv_in_grad,
        gate_mix_grad,
        vectors,
        layer_first,
        layer_rows[1],
        middle_low,
        step_low,
        pre_low,
        select_low,
        scan_in,
        tokens_rows,
        middle_grad,
        gain_mix_row,
        in_conv,
        in_gate,
        normed_one_cols,
        normed_two_cols,
        ct_cols,
        normed_two_cols if swap_now else swapped_columns(middle_low),
        ffn_all,
        gated_all,
    )
    at = taps + 2
    return (
        layer_out.reshape(tokens.shape),
        tokens_grad.reshape(tokens.shape),
        gains[8:10].reshape(width),
        grad_inproj,
        vectors[:taps],
        vectors[taps],
        jnp.transpose(grad_selproj),
        grad_stepproj,
        vectors[taps + 1],
        jnp.transpose(vectors[at : at + n_state]),
        vectors[at + n_state],
        grad_outproj,
        gains[10:12].reshape(width),
        grad_gateup,
        grad_downproj,
    )


def solution(mesh):
    in_specs = (
        P("dp", "ctx", None),
        P(),
        P(None, ("dp", "ctx"), "tp"),
        P(None, "tp"),
        P("tp"),
        P("tp", None),
        P(None, "tp"),
        P("tp"),
        P("tp", None),
        P("tp"),
        P("tp", ("dp", "ctx")),
        P(),
        P(None, ("dp", "ctx"), "tp"),
        P("tp", ("dp", "ctx")),
        P("dp", "ctx", None),
    )
    out_specs = (
        P("dp", "ctx", None),
        P("dp", "ctx", None),
        P(),
        P(None, ("dp", "ctx"), "tp"),
        P(None, "tp"),
        P("tp"),
        P("tp", None),
        P(None, "tp"),
        P("tp"),
        P("tp", None),
        P("tp"),
        P("tp", ("dp", "ctx")),
        P(),
        P(None, ("dp", "ctx"), "tp"),
        P("tp", ("dp", "ctx")),
    )
    return jax.shard_map(
        per_device, mesh=mesh, in_specs=in_specs, out_specs=out_specs, check_vma=False
    )
```
